32 devices in a mesh: dp: 8 (over z, x), seq: 4 (over y, core).
Axes of the slice: x: 2, y: 2, z: 4, core: 2. Of those that a mesh axis runs over, the one named last changes fastest.
Arguments:
- tokens: bfloat16 [16, 1024, 768], P('dp', 'seq'), may hold values from -6 to 6
- cotangent: bfloat16 [16, 1024, 768], P('dp', 'seq'), may hold values from -6 to 6
- segments: int32 [16, 1024], P('dp'), may hold values from 0 to 4, as said below
- valid: int32 [16], P('dp'), may hold values from 0 to 1, as said below
- w_qkv: float32 [768, 2304], P('seq'), may hold values from -0.21875 to 0.21875
- w_out: float32 [768, 768], P('seq'), may hold values from -4 to 4
- w_in: float32 [768, 2304], P('seq'), may hold values from -0.21875 to 0.21875
- w_down: float32 [1152, 768], P('seq'), may hold values from -0.1875 to 0.1875
- gains: float32 [2, 768], P(None, 'seq'), may hold values from 0.7 to 2.95
- m_qkv: float32 [768, 2304], P('seq'), may hold values from -0.0048828125 to 0.0048828125
- m_out: float32 [768, 768], P('seq'), may hold values from -0.00018310547 to 0.00018310547
- m_in: float32 [768, 2304], P('seq'), may hold values from -0.0007324219 to 0.0007324219
- m_down: float32 [1152, 768], P('seq'), may hold values from -0.0008544922 to 0.0008544922
- m_gains: float32 [2, 768], P(None, 'seq'), may hold values from -0.0043825276 to 0.0043825276
- v_qkv: float32 [768, 2304], P('seq'), may hold values from 5.544937e-07 to 2.2219497e-06
- v_out: float32 [768, 768], P('seq'), may hold values from 8.5203405e-10 to 3.4042547e-09
- v_in: float32 [768, 2304], P('seq'), may hold values from 1.2163087e-08 to 4.8692097e-08
- v_down: float32 [1152, 768], P('seq'), may hold values from 1.621745e-08 to 6.47903e-08
- v_gains: float32 [2, 768], P(None, 'seq'), may hold values from 2.0271812e-08 to 3.974865e-06
Outputs:
- mixed: bfloat16 [16, 1024, 768], P('dp', 'seq')
- input_grad: float32 [16, 1024, 768], P('dp', 'seq')
- grad_norm: float32 [], replicated
- new_qkv: float32 [768, 2304], P('seq')
- new_out: float32 [768, 768], P('seq')
- new_in: float32 [768, 2304], P('seq')
- new_down: float32 [1152, 768], P('seq')
- new_gains: float32 [2, 768], P(None, 'seq')
- first_qkv: float32 [768, 2304], P('seq')
- first_out: float32 [768, 768], P('seq')
- first_in: float32 [768, 2304], P('seq')
- first_down: float32 [1152, 768], P('seq')
- first_gains: float32 [2, 768], P(None, 'seq')
- second_qkv: float32 [768, 2304], P('seq')
- second_out: float32 [768, 768], P('seq')
- second_in: float32 [768, 2304], P('seq')
- second_down: float32 [1152, 768], P('seq')
- second_gains: float32 [2, 768], P(None, 'seq')
The draws below stay inside these ranges and needn't reach their ends.
Inputs may be any that keep to these rules, and one draw needn't show every extreme that they name: `segments`: segment numbers never fall along a slot. `valid`: on each index of dp the live slots come first, and on the last index of dp all 2 are live.
All inputs are finite; a program needn't handle non-finite values.
Results may differ from the reference program's by a relative error of at most 0.018.
The reference program's roundings to bfloat16 on the way count: a program that leaves them out, or rounds other values in their place, can miss the bound.
Values may be sent and summed in bfloat16 or wider, within the bound.
No kernel may reach another device: no remote copies, remote signals or barrier semaphores. Data moves between devices by JAX's collectives and lax.ppermute only.
A program may use at most 256 MiB of HBM per device.

```python
import math
import jax
import jax.numpy as jnp
from jax import lax

D = 768
HEADS = 12
HEAD_DIM = 64
FF = 1152
SLOTS = 2
LEN = 1024
STEP_COUNT = 10
SLOTS_ALL = 16
N_DP = 8


def draw_segments(key, part):
    key = jax.random.fold_in(key, 11)
    key_one, key_two, key_three, key_four = jax.random.split(key, 4)
    column_shape = (SLOTS_ALL, 1)
    cut_two = jax.random.randint(key_one, column_shape, 1, LEN // 4)
    cut_three = jax.random.randint(key_two, column_shape, 3 * LEN // 4 + 1, LEN)
    cut_one = jax.random.randint(key_three, column_shape, 0, cut_two)
    cut_four = jax.random.randint(key_four, column_shape, cut_three, LEN + 1)
    places = jnp.arange(LEN, dtype=jnp.int32)[None, :]
    total = (places >= cut_one).astype(jnp.int32) + (places >= cut_two).astype(jnp.int32)
    total = total + (places >= cut_three).astype(jnp.int32) + (places >= cut_four).astype(jnp.int32)
    return total


def draw_valid(key, part):
    key = jax.random.fold_in(key, 23)
    group_total = SLOTS_ALL // SLOTS
    extra_live = jax.random.randint(key, (group_total,), 0, 2)
    slot_index = jnp.arange(SLOTS_ALL, dtype=jnp.int32)
    group_index = slot_index // SLOTS
    live_count = jnp.minimum(SLOTS, 1 + group_index * SLOTS // group_total + extra_live[group_index])
    return (slot_index % SLOTS < live_count).astype(jnp.int32)


def draw_gains(key, part):
    key = jax.random.fold_in(key, 37)
    top_gain = 1.73
    low_end = 0.8
    high_end = 1.2
    ramp_up = 1.0 + (top_gain - 1.0) * jnp.arange(D, dtype=jnp.float32) / (D - 1)
    jitter_draw = jax.random.uniform(key, (2, D), jnp.float32, low_end, high_end)
    return ramp_up * jitter_draw


def weight_total():
    return 822.0 * D * D + 430.0 * D * D / LEN + 20.0 * D * FF + 500.0 * D


def draw_m_gains(key, part):
    key = jax.random.fold_in(key, 41)
    row_scale = jnp.sqrt(jnp.array([604.0, 12.3], jnp.float32) / weight_total())[:, None]
    normal_draw = jax.random.truncated_normal(key, -4.0, 4.0, (2, D), jnp.float32)
    return row_scale * normal_draw


def draw_v_gains(key, part):
    key = jax.random.fold_in(key, 43)
    row_low = (jnp.array([500.0, 10.2], jnp.float32) / weight_total())[:, None]
    spread_log = jax.random.uniform(key, (2, D), jnp.float32, 0.0, 1.3862943611198906)
    return row_low * jnp.exp(spread_log)


def level_of(stream_key, dims, shards, least, high):
    def one(position, parts):
        draws = jax.random.uniform(jax.random.fold_in(jax.random.fold_in(stream_key, 6), position), (parts,), jnp.float32, least / len(shards), high / len(shards))
        return jnp.repeat(jnp.exp(draws), dims[position] // parts).reshape((-1,) + (1,) * (len(dims) - position - 1))

    loudness = one(*shards[0])
    for cut in shards[1:]:
        loudness = loudness * one(*cut)
    return loudness


def noise(own_key, dims, scale, most, pieces=(), kind=jnp.bfloat16):
    drawn = scale * jax.random.normal(own_key, dims, jnp.float32)
    if pieces:
        drawn = drawn * level_of(own_key, dims, pieces, -0.22, 0.18)
    return jnp.clip(drawn, -most, most).astype(kind)


def setup_inputs(seed: int = 0) -> dict:
    seeds = jax.random.split(jax.random.key(seed), 20)
    tokens = noise(seeds[0], (SLOTS_ALL, LEN, D), 1.0, 6.0, ((0, 8), (1, 4)))
    cotangent = noise(seeds[1], (SLOTS_ALL, LEN, D), 1.0, 6.0, ((0, 8), (1, 4)))
    segments = draw_segments(jax.random.fold_in(seeds[19], 71), 0)
    valid = draw_valid(jax.random.fold_in(seeds[19], 71), 0)
    w_qkv = noise(seeds[4], (D, 3 * D), D ** -0.5, 0.21875, ((0, 4),), jnp.float32)
    w_out = noise(seeds[5], (D, D), (max(1, 3 * D // LEN)) ** -0.5, 4.0, ((0, 4),), jnp.float32)
    w_in = noise(seeds[6], (D, 2 * FF), D ** -0.5, 0.21875, ((0, 4),), jnp.float32)
    w_down = noise(seeds[7], (FF, D), FF ** -0.5, 0.1875, ((0, 4),), jnp.float32)
    gains = draw_gains(jax.random.fold_in(seeds[19], 71), 0)
    m_qkv = noise(seeds[9], (D, 3 * D), ((338 / (822 * D * D + 430 * D * D / LEN + 20 * D * FF + 500 * D)) ** 0.5), 0.0048828125, ((0, 4),), jnp.float32)
    m_out = noise(seeds[10], (D, D), ((530 / (LEN * (822 * D * D + 430 * D * D / LEN + 20 * D * FF + 500 * D))) ** 0.5), 0.00018310547, ((0, 4),), jnp.float32)
    m_in = noise(seeds[11], (D, 2 * FF), ((7.4 / (822 * D * D + 430 * D * D / LEN + 20 * D * FF + 500 * D)) ** 0.5), 0.0007324219, ((0, 4),), jnp.float32)
    m_down = noise(seeds[12], (FF, D), ((9.9 / (822 * D * D + 430 * D * D / LEN + 20 * D * FF + 500 * D)) ** 0.5), 0.0008544922, ((0, 4),), jnp.float32)
    m_gains = draw_m_gains(jax.random.fold_in(seeds[19], 71), 0)
    v_qkv = jnp.clip(jnp.exp(math.log(2.221949671366019e-06) - 1.3880849 * jax.random.uniform(seeds[14], (D, 3 * D), jnp.float32) ** level_of(seeds[14], (D, 3 * D), ((0, 4),), -0.2, 0.2)), 5.544936811929801e-07, 2.221949671366019e-06)
    v_out = jnp.clip(jnp.exp(math.log(3.404254655947625e-09) - 1.3851548 * jax.random.uniform(seeds[15], (D, D), jnp.float32) ** level_of(seeds[15], (D, D), ((0, 4),), -0.2, 0.2)), 8.520340544215799e-10, 3.404254655947625e-09)
    v_in = jnp.clip(jnp.exp(math.log(4.86920974651639e-08) - 1.387111 * jax.random.uniform(seeds[16], (D, 2 * FF), jnp.float32) ** level_of(seeds[16], (D, 2 * FF), ((0, 4),), -0.2, 0.2)), 1.216308742613137e-08, 4.86920974651639e-08)
    v_down = jnp.clip(jnp.exp(math.log(6.479029934780556e-08) - 1.385068 * jax.random.uniform(seeds[17], (FF, D), jnp.float32) ** level_of(seeds[17], (FF, D), ((0, 4),), -0.2, 0.2)), 1.621745049362744e-08, 6.479029934780556e-08)
    v_gains = draw_v_gains(jax.random.fold_in(seeds[19], 71), 0)
    return {"tokens": tokens, "cotangent": cotangent, "segments": segments, "valid": valid, "w_qkv": w_qkv, "w_out": w_out, "w_in": w_in, "w_down": w_down, "gains": gains, "m_qkv": m_qkv, "m_out": m_out, "m_in": m_in, "m_down": m_down, "m_gains": m_gains, "v_qkv": v_qkv, "v_out": v_out, "v_in": v_in, "v_down": v_down, "v_gains": v_gains}


@jax.custom_vjp
def low(v):
    return lax.optimization_barrier(v.astype(jnp.bfloat16)).astype(jnp.float32)

@jax.custom_vjp
def low_back(v):
    return v

def low_keep(v):
    return (low(v), None)

def low_pass(kept, grad):
    return (grad,)

def back_keep(v):
    return (v, None)

def back_low(kept, grad):
    return (low(grad),)
low.defvjp(low_keep, low_pass)
low_back.defvjp(back_keep, back_low)
EPS_NORM = 1e-05
ROPE_BASE = 160000.0
NEG_FILL = -1e+30
CLIP_LIMIT = 10.0
BETA_FIRST = 0.9
BETA_SECOND = 0.98
EPS_ADAM = 1e-06
STEP_RATES = (0.1, 0.5, 0.1, 0.1, 1.0)
DECAY_RATES = (0.01, 0.01, 0.01, 0.01, 0.0)

def doc_positions(segment_ids):
    seq_len = segment_ids.shape[-1]
    places = jnp.broadcast_to(jnp.arange(seq_len, dtype=jnp.int32), segment_ids.shape)
    first_mark = jnp.ones(segment_ids.shape[:-1] + (1,), jnp.bool_)
    change = jnp.concatenate([first_mark, segment_ids[..., 1:] != segment_ids[..., :-1]], axis=-1)
    starts = lax.cummax(jnp.where(change, places, 0), axis=segment_ids.ndim - 1)
    return places - starts

def rope_tables(positions, head_dim):
    half_dim = head_dim // 2
    exponents = jnp.arange(half_dim, dtype=jnp.float32) * (2.0 / head_dim)
    inv_freq = ROPE_BASE ** (-exponents)
    angles = positions.astype(jnp.float32)[..., None] * inv_freq
    return (jnp.cos(angles)[..., None, :], jnp.sin(angles)[..., None, :])

def rotate(values, cos_part, sin_part):
    half_dim = values.shape[-1] // 2
    first_half = values[..., :half_dim]
    second_half = values[..., half_dim:]
    return jnp.concatenate([first_half * cos_part - second_half * sin_part, second_half * cos_part + first_half * sin_part], axis=-1)

def layer_norm(inputs, gain_vec):
    centered = inputs - lax.optimization_barrier(jnp.mean(inputs, axis=-1, keepdims=True))
    spread = lax.optimization_barrier(jnp.mean(centered * centered, axis=-1, keepdims=True))
    return centered * lax.rsqrt(spread + EPS_NORM) * gain_vec

def matmul(left_side, right_side):
    return jnp.dot(left_side, right_side, precision=lax.Precision.HIGHEST)

def block_group(weights, inputs, segment_ids, live):
    w_qkv, w_out, w_in, w_down, gain_rows = weights
    slot_count, seq_len, model_width = inputs.shape
    head_shape = (slot_count, seq_len, HEADS, HEAD_DIM)
    live_rows = live.astype(jnp.float32)[:, None, None]
    normed = low(layer_norm(inputs, gain_rows[0]))
    projected = low_back(matmul(normed, w_qkv))
    query_raw, key_raw, value_raw = jnp.split(projected, 3, axis=-1)
    cos_part, sin_part = rope_tables(doc_positions(segment_ids), HEAD_DIM)
    queries = low(rotate(query_raw.reshape(head_shape), cos_part, sin_part))
    key_heads = low(rotate(key_raw.reshape(head_shape), cos_part, sin_part))
    value_heads = low(value_raw).reshape(head_shape)
    scale_factor = 1.0 / math.sqrt(HEAD_DIM)
    scores = jnp.einsum('bqhd,bkhd->bhqk', queries, key_heads, precision=lax.Precision.HIGHEST)
    scores = low_back(scores * scale_factor)
    same_doc = segment_ids[:, :, None] == segment_ids[:, None, :]
    scores = jnp.where(same_doc[:, None], scores, NEG_FILL)
    row_max = lax.optimization_barrier(jnp.max(scores, axis=-1, keepdims=True))
    exponentials = jnp.exp(scores - row_max)
    attn_probs = exponentials / lax.optimization_barrier(jnp.sum(exponentials, axis=-1, keepdims=True))
    attended = jnp.einsum('bhqk,bkhd->bqhd', low(attn_probs), value_heads, precision=lax.Precision.HIGHEST)
    attended = low(low_back(attended.reshape(slot_count, seq_len, model_width)))
    branch = low_back(matmul(attended, w_out))
    middle = inputs + live_rows * branch
    normed_two = low(layer_norm(middle, gain_rows[1]))
    gate_up = low_back(matmul(normed_two, w_in))
    hidden = low(jax.nn.gelu(gate_up[..., :FF], approximate=False) * gate_up[..., FF:])
    return middle + live_rows * low_back(matmul(hidden, w_down))

def adam_step(weight, first_old, second_old, gradient, factor, step_rate, decay_rate):
    clipped = gradient * factor
    first_new = BETA_FIRST * first_old + (1.0 - BETA_FIRST) * clipped
    second_new = BETA_SECOND * second_old + (1.0 - BETA_SECOND) * clipped * clipped
    first_hat = first_new / (1.0 - BETA_FIRST ** STEP_COUNT)
    second_hat = second_new / (1.0 - BETA_SECOND ** STEP_COUNT)
    weight_new = weight * (1.0 - step_rate * decay_rate) - step_rate * first_hat / (jnp.sqrt(second_hat) + EPS_ADAM)
    return (weight_new, first_new, second_new)

def reference(tokens, cotangent, segments, valid, w_qkv, w_out, w_in, w_down, gains, m_qkv, m_out, m_in, m_down, m_gains, v_qkv, v_out, v_in, v_down, v_gains):
    masters = (w_qkv, w_out, w_in, w_down, gains)
    seg_groups = segments.reshape(N_DP, SLOTS, LEN)
    live_groups = valid.reshape(N_DP, SLOTS)

    def whole(params, inputs):
        lowered = tuple((low(tensor) for tensor in params))

        def one_group(group_items):
            return block_group(lowered, group_items[0], group_items[1], group_items[2])
        grouped = inputs.reshape(N_DP, SLOTS, LEN, D)
        outputs = lax.map(jax.checkpoint(one_group), (grouped, seg_groups, live_groups))
        return outputs.reshape(SLOTS_ALL, LEN, D)
    mixed, pull_back = jax.vjp(whole, masters, tokens.astype(jnp.float32))
    grads, input_grad = pull_back(cotangent.astype(jnp.float32))
    squares = sum((jnp.sum(grad_part * grad_part) for grad_part in grads))
    grad_norm = jnp.sqrt(squares)
    factor = jnp.minimum(1.0, CLIP_LIMIT / (grad_norm + 1e-06))
    firsts = (m_qkv, m_out, m_in, m_down, m_gains)
    seconds = (v_qkv, v_out, v_in, v_down, v_gains)
    updates = [adam_step(masters[item_index], firsts[item_index], seconds[item_index], grads[item_index], factor, STEP_RATES[item_index], DECAY_RATES[item_index]) for item_index in range(5)]
    return (mixed.astype(jnp.bfloat16), input_grad, grad_norm, updates[0][0], updates[1][0], updates[2][0], updates[3][0], updates[4][0], updates[0][1], updates[1][1], updates[2][1], updates[3][1], updates[4][1], updates[0][2], updates[1][2], updates[2][2], updates[3][2], updates[4][2])
```

```python
import math

import jax
import jax.numpy as jnp
from jax import lax
from jax.sharding import PartitionSpec as P

HEADS = 12
HEAD_DIM = 64
STEP_COUNT = 10
EPS_NORM = 1e-05
ROPE_BASE = 160000.0
NEG_FILL = -1e30
CLIP_LIMIT = 10.0
BETA_FIRST = 0.9
BETA_SECOND = 0.98
EPS_ADAM = 1e-06
STEP_RATES = (0.1, 0.5, 0.1, 0.1, 1.0)
DECAY_RATES = (0.01, 0.01, 0.01, 0.01, 0.0)
LOW = jnp.bfloat16
FULL = jnp.float32


def doc_positions(segment_ids):
    seq_len = segment_ids.shape[-1]
    places = jnp.arange(seq_len, dtype=jnp.int32)
    first_mark = jnp.ones((1,), jnp.bool_)
    change = jnp.concatenate([first_mark, segment_ids[1:] != segment_ids[:-1]])
    starts = lax.cummax(jnp.where(change, places, 0), axis=0)
    return places - starts


def rope_tables(positions, head_dim):
    half_dim = head_dim // 2
    exponents = jnp.arange(half_dim, dtype=jnp.float32) * (2.0 / head_dim)
    inv_freq = ROPE_BASE ** (-exponents)
    angles = positions.astype(jnp.float32)[:, None] * inv_freq
    return jnp.cos(angles)[:, None, :], jnp.sin(angles)[:, None, :]


def rotate(values, cos_part, sin_part):
    half_dim = values.shape[-1] // 2
    first_half = values[..., :half_dim]
    second_half = values[..., half_dim:]
    return jnp.concatenate(
        [
            first_half * cos_part - second_half * sin_part,
            second_half * cos_part + first_half * sin_part,
        ],
        axis=-1,
    )


def norm_parts(inputs, gain_vec):
    centered = inputs - jnp.mean(inputs, axis=-1, keepdims=True)
    inv_root = lax.rsqrt(jnp.mean(centered * centered, axis=-1, keepdims=True) + EPS_NORM)
    scaled = centered * inv_root
    return (scaled * gain_vec, scaled, inv_root)


def norm_back(grad_normed, scaled, inv_root, gain_vec):
    grad_scaled = grad_normed * gain_vec
    mean_grad = jnp.mean(grad_scaled, axis=-1, keepdims=True)
    mean_cross = jnp.mean(grad_scaled * scaled, axis=-1, keepdims=True)
    grad_input = inv_root * (grad_scaled - mean_grad - scaled * mean_cross)
    return grad_input, jnp.sum(grad_normed * scaled, axis=0)


def geglu(gate_in, gate_up):
    return jax.nn.gelu(gate_in, approximate=False) * gate_up


def adam_step(weight, first_old, second_old, gradient, factor, step_rate, decay_rate):
    clipped = gradient * factor
    first_new = BETA_FIRST * first_old + (1.0 - BETA_FIRST) * clipped
    second_new = BETA_SECOND * second_old + (1.0 - BETA_SECOND) * clipped * clipped
    first_hat = first_new / (1.0 - BETA_FIRST**STEP_COUNT)
    second_hat = second_new / (1.0 - BETA_SECOND**STEP_COUNT)
    weight_new = weight * (1.0 - step_rate * decay_rate) - step_rate * first_hat / (
        jnp.sqrt(second_hat) + EPS_ADAM
    )
    return (weight_new, first_new, second_new)


def dot(left, right, dims):
    return lax.dot_general(left, right, ((dims[0], dims[1]), ((), ())), preferred_element_type=FULL)


def make(dp_count, seq_count):
    assert seq_count == 4 and dp_count & (dp_count - 1) == 0

    def trade(value, axis, bit):
        count = seq_count if axis == "seq" else dp_count
        return lax.ppermute(value, axis, [(i, i ^ bit) for i in range(count)])

    def gather_blocks(own):
        far = trade(own, "seq", 2)
        return (own, trade(own, "seq", 1), far, trade(far, "seq", 1))

    def in_order(blocks, place):
        stacked = jnp.stack(blocks)
        return jnp.concatenate(
            [lax.dynamic_index_in_dim(stacked, b ^ place, 0, keepdims=False) for b in range(4)]
        )

    def row_blocks(whole, place):
        cut = whole.reshape((4, whole.shape[0] // 4) + whole.shape[1:])
        return [lax.dynamic_index_in_dim(cut, place ^ j, 0, keepdims=False) for j in range(4)]

    def over_seq(blocks):
        one = trade(blocks[1].astype(LOW), "seq", 1).astype(FULL)
        three = trade(blocks[3].astype(LOW), "seq", 1).astype(FULL)
        far = trade((blocks[2] + three).astype(LOW), "seq", 2).astype(FULL)
        return blocks[0] + one + far

    def over_dp(share, group):
        bit = 1
        share = jnp.pad(share, ((0, -share.shape[0] % dp_count), (0, 0)))
        while bit < dp_count:
            half = share.shape[0] // 2
            mine = (group // bit) % 2
            keep = lax.dynamic_slice_in_dim(share, mine * half, half, 0)
            give = lax.dynamic_slice_in_dim(share, (1 - mine) * half, half, 0)
            share = keep + trade(give.astype(LOW), "dp", bit).astype(FULL)
            bit *= 2
        return share

    def spread_dp(piece, group):
        piece = piece.astype(LOW)
        bit = dp_count // 2
        while bit:
            mine = (group // bit) % 2
            other = trade(piece, "dp", bit)
            piece = jnp.where(
                mine == 0,
                jnp.concatenate([piece, other]),
                jnp.concatenate([other, piece]),
            )
            bit //= 2
        return piece.astype(FULL)

    def on_device(
        tokens, cotangent, segments, valid,
        w_qkv, w_out, w_in, w_down, gains,
        m_qkv, m_out, m_in, m_down, m_gains,
        v_qkv, v_out, v_in, v_down, v_gains,
    ):
        place = lax.axis_index("seq")
        group = lax.axis_index("dp")
        slot = place // 2
        local_len, width = tokens.shape[1:]
        rows = 2 * local_len

        def deal(value):
            mine = lax.dynamic_index_in_dim(value, slot, 0, keepdims=False)
            theirs = lax.dynamic_index_in_dim(value, 1 - slot, 0, keepdims=False)
            return jnp.concatenate([mine, trade(theirs, "seq", 2)])

        def undeal(value):
            mine = value[:local_len]
            theirs = trade(value[local_len:], "seq", 2)
            return jnp.where(slot == 0, jnp.stack([mine, theirs]), jnp.stack([theirs, mine]))

        source = deal(tokens).astype(FULL)
        blocks_qkv = gather_blocks(w_qkv.astype(LOW))
        blocks_out = gather_blocks(w_out.astype(LOW))
        blocks_in = gather_blocks(w_in.astype(LOW))
        blocks_down = gather_blocks(w_down.astype(LOW))
        gain_low = lax.all_gather(gains.astype(LOW), "seq", axis=1, tiled=True).astype(FULL)
        grad_out = deal(cotangent).astype(FULL)
        weight_qkv = in_order(blocks_qkv, place)
        weight_out = in_order(blocks_out, place)
        weight_in = in_order(blocks_in, place)
        weight_down = in_order(blocks_down, place)

        seg = lax.dynamic_index_in_dim(segments, slot, 0, keepdims=False)
        positions = doc_positions(seg).reshape(4, local_len)
        seg = seg.reshape(4, local_len)
        chunks = [place, place ^ 2, place ^ 1, place ^ 3]
        seg_keys = jnp.concatenate(
            [lax.dynamic_index_in_dim(seg, c, 0, keepdims=False) for c in chunks]
        )
        seg_query = seg_keys[:rows]
        pos = jnp.concatenate(
            [lax.dynamic_index_in_dim(positions, c, 0, keepdims=False) for c in chunks[:2]]
        )
        cos_part, sin_part = rope_tables(pos, HEAD_DIM)
        live = lax.dynamic_index_in_dim(valid, slot, 0, keepdims=False).astype(FULL)

        heads = lambda v: v.reshape(v.shape[0], HEADS, HEAD_DIM)
        flat = lambda v: v.reshape(v.shape[0], width)
        scale = 1.0 / math.sqrt(HEAD_DIM)

        normed, scaled_one, root_one = norm_parts(source, gain_low[0])
        a1 = normed.astype(LOW)
        projected = dot(a1, weight_qkv, ((1,), (0,)))
        query = (rotate(heads(projected[:, :width]), cos_part, sin_part).astype(LOW) * scale).astype(LOW)
        key_own = flat(rotate(heads(projected[:, width : 2 * width]), cos_part, sin_part)).astype(LOW)
        value_own = projected[:, 2 * width :].astype(LOW)
        keys = heads(jnp.concatenate([key_own, trade(key_own, "seq", 1)]))
        values = heads(jnp.concatenate([value_own, trade(value_own, "seq", 1)]))

        scores = jnp.einsum("qhd,khd->hqk", query, keys, preferred_element_type=FULL)
        scores = jnp.where((seg_query[:, None] == seg_keys[None, :])[None], scores, NEG_FILL)
        top = jnp.max(scores, axis=-1, keepdims=True)
        exps = jnp.exp(scores - top)
        total = jnp.sum(exps, axis=-1, keepdims=True)
        probs = exps / total
        o = flat(
            jnp.einsum("hqk,khd->qhd", probs.astype(LOW), values, preferred_element_type=FULL)
        ).astype(LOW)

        middle = source + live * dot(o, weight_out, ((1,), (0,)))
        normed_two, scaled_two, root_two = norm_parts(middle, gain_low[1])
        a2 = normed_two.astype(LOW)
        gate_up = dot(a2, weight_in, ((1,), (0,)))
        hidden_units = weight_down.shape[0]
        gate_in, gate_lin = gate_up[:, :hidden_units], gate_up[:, hidden_units:]
        geglu_out, pull_gate = jax.vjp(geglu, gate_in, gate_lin)
        hidden = geglu_out.astype(LOW)
        mixed = (middle + live * dot(hidden, weight_down, ((1,), (0,)))).astype(LOW)

        dm = (live * grad_out).astype(LOW)
        grad_down = dot(hidden, dm, ((0,), (0,)))
        duw = jnp.concatenate(pull_gate(dot(dm, weight_down, ((1,), (1,)))), axis=-1).astype(LOW)
        grad_in = dot(a2, duw, ((0,), (0,)))
        back_two, gain_two = norm_back(
            dot(duw, weight_in, ((1,), (1,))), scaled_two, root_two, gain_low[1]
        )
        dx1 = grad_out + back_two
        db = (live * dx1).astype(LOW)
        grad_outp = dot(o, db, ((0,), (0,)))
        do = heads(dot(db, weight_out, ((1,), (1,))).astype(LOW))

        grad_probs = jnp.einsum("qhd,khd->hqk", do, values, preferred_element_type=FULL)
        inner = jnp.sum(grad_probs * probs, axis=-1, keepdims=True)
        ds = (probs * (grad_probs - inner)).astype(LOW)
        dq = jnp.einsum("hqk,khd->qhd", ds, keys, preferred_element_type=FULL) * scale
        dk = flat(jnp.einsum("hqk,qhd->khd", ds, query, preferred_element_type=FULL))
        dv = flat(jnp.einsum("hqk,qhd->khd", probs.astype(LOW), do, preferred_element_type=FULL))
        dk = dk[:rows] + trade(dk[rows:].astype(LOW), "seq", 1).astype(FULL)
        dv = dv[:rows] + trade(dv[rows:].astype(LOW), "seq", 1).astype(FULL)
        dqkv = jnp.concatenate(
            [
                flat(rotate(dq, cos_part, -sin_part)),
                flat(rotate(heads(dk), cos_part, -sin_part)),
                dv,
            ],
            axis=-1,
        ).astype(LOW)
        grad_qkv = dot(a1, dqkv, ((0,), (0,)))
        back_one, gain_one = norm_back(
            dot(dqkv, weight_qkv, ((1,), (1,))), scaled_one, root_one, gain_low[0]
        )
        input_grad = dx1 + back_one

        pieces = [
            over_dp(over_seq(row_blocks(g, place)), group)
            for g in (grad_qkv, grad_outp, grad_in, grad_down)
        ]
        grad_gains = lax.psum(jnp.stack([gain_one, gain_two]), ("dp", "seq"))
        gain_share = lax.dynamic_slice_in_dim(grad_gains, place * gains.shape[1], gains.shape[1], 1)
        square = sum(jnp.sum(piece * piece) for piece in pieces)
        square = lax.psum(square, ("dp", "seq")) + jnp.sum(grad_gains * grad_gains)
        grad_norm = jnp.sqrt(square)
        factor = jnp.minimum(1.0, CLIP_LIMIT / (grad_norm + 1e-06))
        shares = [
            spread_dp(piece, group)[: w.shape[0]]
            for piece, w in zip(pieces, (w_qkv, w_out, w_in, w_down))
        ] + [gain_share]
        masters = (w_qkv, w_out, w_in, w_down, gains)
        firsts = (m_qkv, m_out, m_in, m_down, m_gains)
        seconds = (v_qkv, v_out, v_in, v_down, v_gains)
        updates = [
            adam_step(w, m, v, g, factor, rate, decay)
            for w, m, v, g, rate, decay in zip(
                masters, firsts, seconds, shares, STEP_RATES, DECAY_RATES
            )
        ]
        return (
            undeal(mixed),
            undeal(input_grad),
            grad_norm,
            *[u[0] for u in updates],
            *[u[1] for u in updates],
            *[u[2] for u in updates],
        )

    return on_device


def solution(mesh):
    rows, matrix, gain = P("dp", "seq", None), P("seq", None), P(None, "seq")
    weights = (matrix,) * 4 + (gain,)
    return jax.shard_map(
        make(mesh.shape["dp"], mesh.shape["seq"]),
        mesh=mesh,
        in_specs=(rows, rows, P("dp", None), P("dp")) + weights * 3,
        out_specs=(rows, rows, P()) + weights * 3,
        check_vma=False,
    )
```

```python
import math

import jax
import jax.numpy as jnp
from jax import lax
from jax.experimental import pallas as pl
from jax.experimental.pallas import tpu as pltpu
from jax.sharding import PartitionSpec as P

HEADS = 12
HEAD_DIM = 64
PAIR = 2 * HEAD_DIM
STEP_COUNT = 10
EPS_NORM = 1e-05
ROPE_BASE = 160000.0
NEG_FILL = -1e30
CLIP_LIMIT = 10.0
BETA_FIRST = 0.9
BETA_SECOND = 0.98
EPS_ADAM = 1e-06
STEP_RATES = (0.1, 0.5, 0.1, 0.1, 1.0)
DECAY_RATES = (0.01, 0.01, 0.01, 0.01, 0.0)
DOCS = 5
LOW = jnp.bfloat16
FULL = jnp.float32
SCALE = 1.0 / math.sqrt(HEAD_DIM)
MEMORY = 56 * 1024 * 1024


def doc_positions(segment_ids):
    seq_len = segment_ids.shape[-1]
    places = jnp.arange(seq_len, dtype=jnp.int32)
    first_mark = jnp.ones((1,), jnp.bool_)
    change = jnp.concatenate([first_mark, segment_ids[1:] != segment_ids[:-1]])
    starts = lax.cummax(jnp.where(change, places, 0), axis=0)
    return places - starts


def rope_tables(positions):
    half_dim = HEAD_DIM // 2
    exponents = jnp.arange(half_dim, dtype=jnp.float32) * (2.0 / HEAD_DIM)
    inv_freq = ROPE_BASE ** (-exponents)
    angles = positions.astype(jnp.float32)[:, None] * inv_freq
    cos_part, sin_part = jnp.cos(angles), jnp.sin(angles)
    return (
        jnp.concatenate([cos_part] * 4, axis=1),
        jnp.concatenate([-sin_part, sin_part] * 2, axis=1),
    )


def adam_step(weight, first_old, second_old, gradient, factor, step_rate, decay_rate):
    clipped = gradient * factor
    first_new = BETA_FIRST * first_old + (1.0 - BETA_FIRST) * clipped
    second_new = BETA_SECOND * second_old + (1.0 - BETA_SECOND) * clipped * clipped
    first_hat = first_new / (1.0 - BETA_FIRST**STEP_COUNT)
    second_hat = second_new / (1.0 - BETA_SECOND**STEP_COUNT)
    weight_new = weight * (1.0 - step_rate * decay_rate) - step_rate * first_hat / (
        jnp.sqrt(second_hat) + EPS_ADAM
    )
    return (weight_new, first_new, second_new)


def mul(left, right):
    return lax.dot_general(left, right, (((1,), (0,)), ((), ())), preferred_element_type=FULL)


def mul_t(left, right):
    return lax.dot_general(left, right, (((1,), (1,)), ((), ())), preferred_element_type=FULL)


def normalize(values):
    centered = values - jnp.mean(values, axis=-1, keepdims=True)
    root = lax.rsqrt(jnp.mean(centered * centered, axis=-1, keepdims=True) + EPS_NORM)
    return centered * root, root


def normalize_back(grad, gain, scaled, root):
    t = grad * gain
    back = root * (
        t
        - jnp.mean(t, axis=-1, keepdims=True)
        - scaled * jnp.mean(t * scaled, axis=-1, keepdims=True)
    )
    return back, jnp.sum(grad * scaled, axis=0, keepdims=True)


def turn(values, cos_part, sin_part):
    lane = lax.broadcasted_iota(jnp.int32, values.shape, 1)
    swapped = jnp.where(
        lane % HEAD_DIM < HEAD_DIM // 2,
        pltpu.roll(values, PAIR - HEAD_DIM // 2, 1),
        pltpu.roll(values, HEAD_DIM // 2, 1),
    )
    return values * cos_part + swapped * sin_part


def three_parts(values):
    high = values.astype(LOW).astype(FULL)
    rest = values - high
    mid = rest.astype(LOW).astype(FULL)
    return high, mid, rest - mid


def load_blocks(place, blocks, whole, sem):
    rows = blocks[0].shape[0]
    copies = []
    for j, block in enumerate(blocks):
        start = pl.multiple_of((place ^ j) * rows, rows)
        copies.append(pltpu.make_async_copy(block, whole.at[pl.ds(start, rows), :], sem.at[j]))
    for copy in copies:
        copy.start()
    return copies


def store_products(place, left_t, right, keep_ref, send_ref):
    rows = keep_ref.shape[1]
    for j in (1, 3, 0, 2):
        start = pl.multiple_of((place ^ j) * rows, rows)
        part = mul(left_t[pl.ds(start, rows), :], right)
        if j in (1, 3):
            send_ref[j // 2] = part.astype(LOW)
        else:
            keep_ref[j // 2] = part


def project_kernel(place_ref, own_ref, far_ref, gain_ref, cos_ref, sin_ref, w0, w1, w2, w3,
                   normed_ref, query_ref, kv_ref, weight, sem):
    copies = load_blocks(place_ref[0], (w0, w1, w2, w3), weight, sem)
    rows, width = own_ref.shape
    for part, ref in enumerate((own_ref, far_ref)):
        scaled, _ = normalize(ref[...].astype(FULL))
        normed_ref[pl.ds(part * rows, rows), :] = (scaled * gain_ref[...]).astype(LOW)
    for copy in copies:
        copy.wait()
    for part in range(2):
        span = pl.ds(part * rows, rows)
        normed = normed_ref[span, :]
        cos_part, sin_part = cos_ref[span, :], sin_ref[span, :]
        for pair in range(2 * width // PAIR):
            lanes = pl.ds(pair * PAIR, PAIR)
            if pair % 2 == 0:
                both = mul(normed, weight[:, pl.ds(pair * PAIR, 2 * PAIR)])
            raw = both[:, (pair % 2) * PAIR : (pair % 2 + 1) * PAIR]
            turned = turn(raw, cos_part, sin_part)
            if pair < width // PAIR:
                query_ref[span, lanes] = (turned * SCALE).astype(LOW)
            else:
                kv_ref[0, span, pl.ds(pair * PAIR - width, PAIR)] = turned.astype(LOW)
        kv_ref[1, span, :] = mul(normed, weight[:, 2 * width :]).astype(LOW)


def head_lanes(head, shape):
    lane = lax.broadcasted_iota(jnp.int32, shape, 1)
    return (lane < HEAD_DIM) if head == 0 else (lane >= HEAD_DIM)


def pick(head, inside, outside):
    return jnp.where(head_lanes(head, inside.shape), inside, outside)


def attend_kernel(query_ref, near_ref, far_ref, mark_query_ref, mark_key_ref, o_ref, extra_ref):
    rows = query_ref.shape[0]
    query = query_ref[...]
    mark_query = mark_query_ref[...]
    parts = [
        (near_ref[0], jnp.transpose(near_ref[1]), mark_key_ref[:rows, :]),
        (far_ref[0], jnp.transpose(far_ref[1]), mark_key_ref[rows:, :]),
    ]
    outs, logs = [], []
    for head in range(2):
        query_head = pick(head, query, mark_query)
        scores = [mul_t(pick(head, key, mark), query_head) for key, _, mark in parts]
        top = jnp.maximum(
            jnp.max(scores[0], axis=0, keepdims=True), jnp.max(scores[1], axis=0, keepdims=True)
        )
        exps = [jnp.exp(score - top) for score in scores]
        total = jnp.sum(exps[0], axis=0, keepdims=True) + jnp.sum(exps[1], axis=0, keepdims=True)
        span = slice(head * HEAD_DIM, (head + 1) * HEAD_DIM)
        out = sum(mul(value_t[span], e.astype(LOW)) for (_, value_t, _), e in zip(parts, exps))
        outs.append(out / total)
        logs.append(top + jnp.log(total))
    o_ref[...] = jnp.transpose(jnp.concatenate(outs)).astype(LOW)
    line = lax.broadcasted_iota(jnp.int32, (PAIR, rows), 0)
    extra = jnp.zeros((PAIR, rows), FULL)
    for head in range(2):
        base = DOCS + (HEAD_DIM if head == 0 else 0)
        for i, piece in enumerate(three_parts(-logs[head])):
            extra = jnp.where(line == base + i, piece, extra)
    extra_ref[...] = jnp.transpose(extra).astype(LOW) + mark_query


def attend_back_kernel(query_ref, near_ref, far_ref, extra_ref, mark_key_ref, o_ref, do_ref,
                       cos_ref, sin_ref, dq_ref, keep_ref, send_ref):
    rows = query_ref.shape[0]
    query, extra, do = query_ref[...], extra_ref[...], do_ref[...]
    inner_all = do.astype(FULL) * o_ref[...].astype(FULL)
    lane = lax.broadcasted_iota(jnp.int32, (rows, PAIR), 1)
    zero = jnp.zeros((rows, PAIR), LOW)
    grads_query = []
    sums = [[None, None], [None, None]]
    keys_t = [jnp.transpose(near_ref[0]), jnp.transpose(far_ref[0])]
    for head in range(2):
        inside = head_lanes(head, (rows, PAIR))
        inner = jnp.sum(jnp.where(inside, inner_all, 0.0), axis=1, keepdims=True)
        base = DOCS + (HEAD_DIM if head == 0 else 0)
        tail = jnp.zeros((rows, PAIR), FULL)
        for i, piece in enumerate(three_parts(-inner)):
            tail = jnp.where(lane == base + i, piece, tail)
        query_head = pick(head, query, extra)
        do_head = pick(head, do, tail.astype(LOW))
        query_only = pick(head, query, zero)
        do_only = pick(head, do, zero)
        span = slice(head * HEAD_DIM, (head + 1) * HEAD_DIM)
        grad_query = 0.0
        for part, ref in enumerate((near_ref, far_ref)):
            mark = mark_key_ref[pl.ds(part * rows, rows), :]
            probs = jnp.exp(mul_t(pick(head, ref[0], mark), query_head))
            grad_probs = mul_t(pick(head, ref[1], mark), do_head)
            grad_scores = (probs * grad_probs).astype(LOW)
            grad_value = mul(probs.astype(LOW), do_only)
            grad_key = mul(grad_scores, query_only)
            grad_query += mul(keys_t[part][span], grad_scores)
            if head == 0:
                sums[part] = [grad_key, grad_value]
            else:
                sums[part] = [sums[part][0] + grad_key, sums[part][1] + grad_value]
        grads_query.append(grad_query)
    turned = turn(
        jnp.transpose(jnp.concatenate(grads_query)) * SCALE, cos_ref[...], -sin_ref[...]
    )
    dq_ref[...] = turned.astype(LOW)
    for i in range(2):
        keep_ref[i] = sums[0][i]
        send_ref[i] = sums[1][i].astype(LOW)


def middle_kernel(place_ref, live_ref, own_ref, far_ref, cot_own_ref, cot_far_ref, o_ref, gain_ref,
                  o0, o1, o2, o3, i0, i1, i2, i3, d0, d1, d2, d3,
                  mixed_own_ref, mixed_far_ref, dx1_ref, do_ref, gain_grad_ref,
                  keep_out, send_out, keep_in, send_in, keep_down, send_down,
                  w_out, w_in, w_down, o_t, a2_t, h_t, dm_all, duw_all, db_all, sem):
    place, live = place_ref[0], live_ref[0]
    copies = load_blocks(place, (o0, o1, o2, o3), w_out, sem.at[0])
    copies += load_blocks(place, (i0, i1, i2, i3), w_in, sem.at[1])
    copies += load_blocks(place, (d0, d1, d2, d3), w_down, sem.at[2])
    for copy in copies:
        copy.wait()
    rows, width = own_ref.shape
    units = w_down.shape[0]
    gain = gain_ref[...]
    gain_grad = jnp.zeros((1, width), FULL)
    for part, (ref, cot_ref, mixed_ref) in enumerate(
        ((own_ref, cot_own_ref, mixed_own_ref), (far_ref, cot_far_ref, mixed_far_ref))
    ):
        span = pl.ds(part * rows, rows)
        o = o_ref[span, :]
        x1 = ref[...].astype(FULL) + live * mul(o, w_out[...])
        scaled, root = normalize(x1)
        a2 = (scaled * gain).astype(LOW)
        u = mul(a2, w_in[:, :units])
        w = mul(a2, w_in[:, units:])
        phi = 0.5 * (1.0 + lax.erf(u * math.sqrt(0.5)))
        gelu = u * phi
        h = (gelu * w).astype(LOW)
        mixed_ref[...] = (x1 + live * mul(h, w_down[...])).astype(LOW)
        cot = cot_ref[...].astype(FULL)
        dm = (live * cot).astype(LOW)
        dh = mul_t(dm, w_down[...])
        slope = phi + u * (jnp.exp(-0.5 * u * u) * (1.0 / math.sqrt(2.0 * math.pi)))
        duw_all[span, :units] = (dh * w * slope).astype(LOW)
        duw_all[span, units:] = (dh * gelu).astype(LOW)
        da2 = mul_t(duw_all[span, :], w_in[...])
        back, gain_part = normalize_back(da2, gain, scaled, root)
        gain_grad += gain_part
        dx1 = cot + back
        dx1_ref[span, :] = dx1
        db = (live * dx1).astype(LOW)
        do_ref[span, :] = mul_t(db, w_out[...]).astype(LOW)
        db_all[span, :] = db
        dm_all[span, :] = dm
        o_t[:, span] = jnp.transpose(o)
        a2_t[:, span] = jnp.transpose(a2)
        h_t[:, span] = jnp.transpose(h)
    gain_grad_ref[...] = gain_grad
    store_products(place, h_t, dm_all[...], keep_down, send_down)
    store_products(place, a2_t, duw_all[...], keep_in, send_in)
    store_products(place, o_t, db_all[...], keep_out, send_out)


def grads_kernel(place_ref, normed_ref, dq_ref, own_ref, got_ref, cos_ref, sin_ref,
                 dqkv_ref, keep_ref, send_ref, normed_t):
    rows, width = dq_ref.shape
    normed_t[...] = jnp.transpose(normed_ref[...])
    dqkv_ref[:, :width] = dq_ref[...]
    dqkv_ref[:, 2 * width :] = (own_ref[1] + got_ref[1].astype(FULL)).astype(LOW)
    cos_part, sin_part = cos_ref[...], -sin_ref[...]
    for pair in range(width // PAIR):
        lanes = pl.ds(pair * PAIR, PAIR)
        raw = own_ref[0, :, lanes] + got_ref[0, :, lanes].astype(FULL)
        dqkv_ref[:, pl.ds(width + pair * PAIR, PAIR)] = turn(raw, cos_part, sin_part).astype(LOW)
    store_products(place_ref[0], normed_t, dqkv_ref[...], keep_ref, send_ref)


def input_kernel(place_ref, own_ref, far_ref, gain_ref, dx1_ref, dqkv_ref, w0, w1, w2, w3,
                 grad_own_ref, grad_far_ref, gain_grad_ref, weight, sem):
    copies = load_blocks(place_ref[0], (w0, w1, w2, w3), weight, sem)
    for copy in copies:
        copy.wait()
    rows, width = own_ref.shape
    gain = gain_ref[...]
    gain_grad = jnp.zeros((1, width), FULL)
    for part, (ref, out_ref) in enumerate(((own_ref, grad_own_ref), (far_ref, grad_far_ref))):
        span = pl.ds(part * rows, rows)
        scaled, root = normalize(ref[...].astype(FULL))
        back, gain_part = normalize_back(mul_t(dqkv_ref[span, :], weight[...]), gain, scaled, root)
        gain_grad += gain_part
        out_ref[...] = (dx1_ref[span, :] + back).astype(out_ref.dtype)
    gain_grad_ref[...] = gain_grad


def shaped(*shape, kind=LOW):
    return jax.ShapeDtypeStruct(shape, kind)


IN_SMEM = pl.BlockSpec(memory_space=pltpu.SMEM)
IN_VMEM = pl.BlockSpec(memory_space=pltpu.VMEM)
IN_ANY = pl.BlockSpec(memory_space=pl.ANY)
PARAMS = pltpu.CompilerParams(vmem_limit_bytes=MEMORY)


def project(place, own, far, gain, cos_part, sin_part, blocks):
    rows, width = 2 * own.shape[0], own.shape[1]
    return pl.pallas_call(
        project_kernel,
        out_shape=(shaped(rows, width), shaped(rows, width), shaped(2, rows, width)),
        in_specs=[IN_SMEM] + [IN_VMEM] * 5 + [IN_ANY] * 4,
        out_specs=(IN_VMEM,) * 3,
        scratch_shapes=[pltpu.VMEM((width, 3 * width), LOW), pltpu.SemaphoreType.DMA((4,))],
        compiler_params=PARAMS,
        name="project",
    )(place, own, far, gain, cos_part, sin_part, *blocks)


def attend(query, near, far, mark_query, mark_key):
    rows, width = query.shape
    row_spec = pl.BlockSpec((rows, PAIR), lambda i: (0, i))
    kv_spec = pl.BlockSpec((2, rows, PAIR), lambda i: (0, 0, i))
    return pl.pallas_call(
        attend_kernel,
        grid=(width // PAIR,),
        out_shape=(shaped(rows, width), shaped(rows, width)),
        in_specs=[
            row_spec,
            kv_spec,
            kv_spec,
            pl.BlockSpec((rows, PAIR), lambda i: (0, 0)),
            pl.BlockSpec((2 * rows, PAIR), lambda i: (0, 0)),
        ],
        out_specs=(row_spec, row_spec),
        compiler_params=PARAMS,
        name="attend",
    )(query, near, far, mark_query, mark_key)


def attend_back(query, near, far, extra, mark_key, o, do, cos_part, sin_part):
    rows, width = query.shape
    row_spec = pl.BlockSpec((rows, PAIR), lambda i: (0, i))
    kv_spec = pl.BlockSpec((2, rows, PAIR), lambda i: (0, 0, i))
    fixed = pl.BlockSpec((rows, PAIR), lambda i: (0, 0))
    return pl.pallas_call(
        attend_back_kernel,
        grid=(width // PAIR,),
        out_shape=(
            shaped(rows, width),
            shaped(2, rows, width, kind=FULL),
            shaped(2, rows, width),
        ),
        in_specs=[
            row_spec,
            kv_spec,
            kv_spec,
            row_spec,
            pl.BlockSpec((2 * rows, PAIR), lambda i: (0, 0)),
            row_spec,
            row_spec,
            fixed,
            fixed,
        ],
        out_specs=(row_spec, kv_spec, kv_spec),
        compiler_params=PARAMS,
        name="attend_back",
    )(query, near, far, extra, mark_key, o, do, cos_part, sin_part)


def middle(place, live, own, far, cot_own, cot_far, o, gain, blocks_out, blocks_in, blocks_down):
    half, width = own.shape
    rows = 2 * half
    share = blocks_out[0].shape[0]
    share_down = blocks_down[0].shape[0]
    units = 4 * share_down
    return pl.pallas_call(
        middle_kernel,
        out_shape=(
            shaped(half, width),
            shaped(half, width),
            shaped(rows, width, kind=FULL),
            shaped(rows, width),
            shaped(1, width, kind=FULL),
            shaped(2, share, width, kind=FULL),
            shaped(2, share, width),
            shaped(2, share, 2 * units, kind=FULL),
            shaped(2, share, 2 * units),
            shaped(2, share_down, width, kind=FULL),
            shaped(2, share_down, width),
        ),
        in_specs=[IN_SMEM] * 2 + [IN_VMEM] * 6 + [IN_ANY] * 12,
        out_specs=(IN_VMEM,) * 11,
        scratch_shapes=[
            pltpu.VMEM((width, width), LOW),
            pltpu.VMEM((width, 2 * units), LOW),
            pltpu.VMEM((units, width), LOW),
            pltpu.VMEM((width, rows), LOW),
            pltpu.VMEM((width, rows), LOW),
            pltpu.VMEM((units, rows), LOW),
            pltpu.VMEM((rows, width), LOW),
            pltpu.VMEM((rows, 2 * units), LOW),
            pltpu.VMEM((rows, width), LOW),
            pltpu.SemaphoreType.DMA((3, 4)),
        ],
        compiler_params=PARAMS,
        name="middle",
    )(place, live, own, far, cot_own, cot_far, o, gain, *blocks_out, *blocks_in, *blocks_down)


def qkv_grads(place, normed, dq, own, got, cos_part, sin_part):
    rows, width = dq.shape
    share = width // 4
    return pl.pallas_call(
        grads_kernel,
        out_shape=(
            shaped(rows, 3 * width),
            shaped(2, share, 3 * width, kind=FULL),
            shaped(2, share, 3 * width),
        ),
        in_specs=[IN_SMEM] + [IN_VMEM] * 6,
        out_specs=(IN_VMEM,) * 3,
        scratch_shapes=[pltpu.VMEM((width, rows), LOW)],
        compiler_params=PARAMS,
        name="qkv_grads",
    )(place, normed, dq, own, got, cos_part, sin_part)


def input_back(place, own, far, gain, dx1, dqkv, blocks):
    half, width = own.shape
    return pl.pallas_call(
        input_kernel,
        out_shape=(
            shaped(half, width, kind=FULL),
            shaped(half, width),
            shaped(1, width, kind=FULL),
        ),
        in_specs=[IN_SMEM] + [IN_VMEM] * 5 + [IN_ANY] * 4,
        out_specs=(IN_VMEM,) * 3,
        scratch_shapes=[pltpu.VMEM((width, 3 * width), LOW), pltpu.SemaphoreType.DMA((4,))],
        compiler_params=PARAMS,
        name="input_back",
    )(place, own, far, gain, dx1, dqkv, *blocks)


def make(dp_count, seq_count):
    assert seq_count == 4 and dp_count & (dp_count - 1) == 0
    dp_bits = [1 << i for i in range(dp_count.bit_length() - 1)]

    def trade(value, axis, bit):
        count = seq_count if axis == "seq" else dp_count
        return lax.ppermute(value, axis, [(i, i ^ bit) for i in range(count)])

    def gather_blocks(own):
        far = trade(own, "seq", 2)
        near = trade(jnp.stack([own, far]), "seq", 1)
        return (own, near[0], far, near[1])

    def over_seq(keep, send):
        got = trade(send, "seq", 1)
        far = trade((keep[1] + got[1].astype(FULL)).astype(LOW), "seq", 2)
        return keep[0] + got[0].astype(FULL) + far.astype(FULL)

    def over_dp(share, group):
        share = jnp.pad(share, ((0, -share.shape[0] % dp_count), (0, 0)))
        for bit in dp_bits:
            half = share.shape[0] // 2
            mine = (group // bit) % 2
            keep = lax.dynamic_slice_in_dim(share, mine * half, half, 0)
            give = lax.dynamic_slice_in_dim(share, (1 - mine) * half, half, 0)
            share = keep + trade(give.astype(LOW), "dp", bit).astype(FULL)
        return share

    def spread_dp(piece, group):
        piece = piece.astype(LOW)
        for bit in dp_bits[::-1]:
            mine = (group // bit) % 2
            other = trade(piece, "dp", bit)
            piece = jnp.where(
                mine == 0,
                jnp.concatenate([piece, other]),
                jnp.concatenate([other, piece]),
            )
        return piece.astype(FULL)

    def sum_all(value):
        for bit in dp_bits[::-1]:
            value = value + trade(value, "dp", bit)
        for bit in (2, 1):
            value = value + trade(value, "seq", bit)
        return value

    def on_device(
        tokens, cotangent, segments, valid,
        w_qkv, w_out, w_in, w_down, gains,
        m_qkv, m_out, m_in, m_down, m_gains,
        v_qkv, v_out, v_in, v_down, v_gains,
    ):
        place = lax.axis_index("seq")
        group = lax.axis_index("dp")
        slot = place // 2
        local_len, width = tokens.shape[1:]
        rows = 2 * local_len
        at = place[None]

        def deal(value):
            mine = lax.dynamic_index_in_dim(value, slot, 0, keepdims=False)
            theirs = lax.dynamic_index_in_dim(value, 1 - slot, 0, keepdims=False)
            return mine, trade(theirs, "seq", 2)

        def undeal(mine, theirs):
            theirs = trade(theirs, "seq", 2).astype(mine.dtype)
            return jnp.where(slot == 0, jnp.stack([mine, theirs]), jnp.stack([theirs, mine]))

        own, far = deal(tokens)
        blocks_qkv = gather_blocks(w_qkv.astype(LOW))
        gain_blocks = gather_blocks(gains.astype(LOW))
        rest = (w_out.astype(LOW), w_in.astype(LOW), w_down.astype(LOW), cotangent)
        rest, _ = lax.optimization_barrier((rest, blocks_qkv[2]))
        blocks_out = gather_blocks(rest[0])
        blocks_in = gather_blocks(rest[1])
        blocks_down = gather_blocks(rest[2])
        cot_own, cot_far = deal(rest[3])
        gain_stack = jnp.stack(gain_blocks)
        gain_low = jnp.concatenate(
            [lax.dynamic_index_in_dim(gain_stack, b ^ place, 0, keepdims=False) for b in range(4)],
            axis=1,
        ).astype(FULL)

        seg = lax.dynamic_index_in_dim(segments, slot, 0, keepdims=False)
        positions = doc_positions(seg).reshape(4, local_len)
        seg = seg.reshape(4, local_len)
        chunks = [place, place ^ 2, place ^ 1, place ^ 3]
        seg_keys = jnp.concatenate(
            [lax.dynamic_index_in_dim(seg, c, 0, keepdims=False) for c in chunks]
        )
        pos = jnp.concatenate(
            [lax.dynamic_index_in_dim(positions, c, 0, keepdims=False) for c in chunks[:2]]
        )
        cos_part, sin_part = rope_tables(pos)
        lane = jnp.arange(PAIR, dtype=jnp.int32)[None] % HEAD_DIM
        same = seg_keys[:, None] == lane
        mark_key = jnp.where(lane < DOCS, 1.0 - same, (lane < DOCS + 3) * 1.0).astype(LOW)
        mark_query = jnp.where((lane < DOCS) & same[:rows], NEG_FILL, 0.0).astype(LOW)
        live = lax.dynamic_index_in_dim(valid, slot, 0, keepdims=True).astype(FULL)

        normed, query, kv = project(at, own, far, gain_low[:1], cos_part, sin_part, blocks_qkv)
        kv_far = trade(kv, "seq", 1)
        o, extra = attend(query, kv, kv_far, mark_query, mark_key)
        (mixed_own, mixed_far, dx1, do, gain_two, keep_out, send_out, keep_in, send_in,
         keep_down, send_down) = middle(
            at, live, own, far, cot_own, cot_far, o, gain_low[1:], blocks_out, blocks_in, blocks_down
        )
        pieces = [
            over_dp(over_seq(keep, send), group)
            for keep, send in ((keep_out, send_out), (keep_in, send_in), (keep_down, send_down))
        ]
        mixed = undeal(mixed_own, mixed_far)
        dq, dkv_keep, dkv_send = attend_back(
            query, kv, kv_far, extra, mark_key, o, do, cos_part, sin_part
        )
        dkv_got = trade(dkv_send, "seq", 1)
        dqkv, keep_qkv, send_qkv = qkv_grads(at, normed, dq, dkv_keep, dkv_got, cos_part, sin_part)
        pieces = [over_dp(over_seq(keep_qkv, send_qkv), group)] + pieces
        grad_own, grad_far, gain_one = input_back(
            at, own, far, gain_low[:1], dx1, dqkv, blocks_qkv
        )
        input_grad = undeal(grad_own, grad_far)

        grad_gains = sum_all(jnp.concatenate([gain_one, gain_two]))
        gain_share = lax.dynamic_slice_in_dim(grad_gains, place * gains.shape[1], gains.shape[1], 1)
        square = sum(jnp.sum(piece * piece) for piece in pieces)
        square = sum_all(square.reshape(1, 1))[0, 0] + jnp.sum(grad_gains * grad_gains)
        grad_norm = jnp.sqrt(square)
        factor = jnp.minimum(1.0, CLIP_LIMIT / (grad_norm + 1e-06))
        shares = [
            spread_dp(piece, group)[: w.shape[0]]
            for piece, w in zip(pieces, (w_qkv, w_out, w_in, w_down))
        ] + [gain_share]
        masters = (w_qkv, w_out, w_in, w_down, gains)
        firsts = (m_qkv, m_out, m_in, m_down, m_gains)
        seconds = (v_qkv, v_out, v_in, v_down, v_gains)
        updates = [
            adam_step(w, m, v, g, factor, rate, decay)
            for w, m, v, g, rate, decay in zip(
                masters, firsts, seconds, shares, STEP_RATES, DECAY_RATES
            )
        ]
        return (
            mixed,
            input_grad,
            grad_norm,
            *[u[0] for u in updates],
            *[u[1] for u in updates],
            *[u[2] for u in updates],
        )

    return on_device


def solution(mesh):
    rows, matrix, gain = P("dp", "seq", None), P("seq", None), P(None, "seq")
    weights = (matrix,) * 4 + (gain,)
    return jax.shard_map(
        make(mesh.shape["dp"], mesh.shape["seq"]),
        mesh=mesh,
        in_specs=(rows, rows, P("dp", None), P("dp")) + weights * 3,
        out_specs=(rows, rows, P()) + weights * 3,
        check_vma=False,
    )
```

```python
import functools
import math

import jax
import jax.numpy as jnp
from jax import lax
from jax.experimental import pallas as pl
from jax.experimental.pallas import tpu as pltpu
from jax.sharding import PartitionSpec as P

HEADS = 12
HEAD_DIM = 64
PAIR = 2 * HEAD_DIM
STEP_COUNT = 10
EPS_NORM = 1e-05
ROPE_BASE = 160000.0
NEG_FILL = -1e30
CLIP_LIMIT = 10.0
BETA_FIRST = 0.9
BETA_SECOND = 0.98
EPS_ADAM = 1e-06
STEP_RATES = (0.1, 0.5, 0.1, 0.1, 1.0)
DECAY_RATES = (0.01, 0.01, 0.01, 0.01, 0.0)
DOCS = 5
LOW = jnp.bfloat16
FULL = jnp.float32
SCALE = 1.0 / math.sqrt(HEAD_DIM)


def doc_positions(segment_ids):
    seq_len = segment_ids.shape[-1]
    places = jnp.arange(seq_len, dtype=jnp.int32)
    first_mark = jnp.ones((1,), jnp.bool_)
    change = jnp.concatenate([first_mark, segment_ids[1:] != segment_ids[:-1]])
    starts = lax.cummax(jnp.where(change, places, 0), axis=0)
    return places - starts


def rope_tables(positions):
    half_dim = HEAD_DIM // 2
    exponents = jnp.arange(half_dim, dtype=jnp.float32) * (2.0 / HEAD_DIM)
    inv_freq = ROPE_BASE ** (-exponents)
    angles = positions.astype(jnp.float32)[:, None] * inv_freq
    cos_part, sin_part = jnp.cos(angles), jnp.sin(angles)
    return (
        jnp.concatenate([cos_part] * 4, axis=1),
        jnp.concatenate([-sin_part, sin_part] * 2, axis=1),
    )


def adam_step(weight, first_old, second_old, gradient, factor, step_rate, decay_rate):
    clipped = gradient * factor
    first_new = BETA_FIRST * first_old + (1.0 - BETA_FIRST) * clipped
    second_new = BETA_SECOND * second_old + (1.0 - BETA_SECOND) * clipped * clipped
    first_hat = first_new / (1.0 - BETA_FIRST**STEP_COUNT)
    second_hat = second_new / (1.0 - BETA_SECOND**STEP_COUNT)
    weight_new = weight * (1.0 - step_rate * decay_rate) - step_rate * first_hat / (
        jnp.sqrt(second_hat) + EPS_ADAM
    )
    return (weight_new, first_new, second_new)


def mul(left, right):
    return lax.dot_general(left, right, (((1,), (0,)), ((), ())), preferred_element_type=FULL)


def mul_t(left, right):
    return lax.dot_general(left, right, (((1,), (1,)), ((), ())), preferred_element_type=FULL)


def normalize(values):
    centered = values - jnp.mean(values, axis=-1, keepdims=True)
    root = lax.rsqrt(jnp.mean(centered * centered, axis=-1, keepdims=True) + EPS_NORM)
    return centered * root, root


def normalize_back(grad, gain, scaled, root):
    t = grad * gain
    back = root * (
        t
        - jnp.mean(t, axis=-1, keepdims=True)
        - scaled * jnp.mean(t * scaled, axis=-1, keepdims=True)
    )
    return back


def turn(values, cos_part, sin_part):
    lane = lax.broadcasted_iota(jnp.int32, values.shape, 1)
    swapped = jnp.where(
        lane % HEAD_DIM < HEAD_DIM // 2,
        pltpu.roll(values, PAIR - HEAD_DIM // 2, 1),
        pltpu.roll(values, HEAD_DIM // 2, 1),
    )
    return values * cos_part + swapped * sin_part


def three_parts(values):
    high = values.astype(LOW).astype(FULL)
    rest = values - high
    mid = rest.astype(LOW).astype(FULL)
    return high, mid, rest - mid


def load_blocks(at_ref, blocks, whole, sem, first=0, rows=None):
    place, half = at_ref[0], at_ref[1]
    rows = rows or blocks[0].shape[0]
    short = rows // 2
    copies = []
    for i, (j, piece) in enumerate(((0, None), (1, None), (2, 0), (2, 1), (3, 0), (3, 1))):
        start = (place ^ j) * rows
        if piece is None:
            source = blocks[i].at[pl.ds(first, rows), :]
            target = whole.at[pl.ds(pl.multiple_of(start, rows), rows), :]
        else:
            source = blocks[i].at[pl.ds(first // 2, short), :]
            start = pl.multiple_of(start + (half ^ piece) * short, short)
            target = whole.at[pl.ds(start, short), :]
        copies.append(pltpu.make_async_copy(source, target, sem.at[i]))
    for copy in copies:
        copy.start()
    return copies


def wait_all(copies):
    for copy in copies:
        copy.wait()


def put(source, target, sem):
    copy = pltpu.make_async_copy(source, target, sem)
    copy.start()
    return copy


def project_kernel(at_ref, own_ref, far_ref, gain_ref, cos_ref, sin_ref, w0, w1, w2, w3, w4, w5,
                   normed_ref, query_ref, kv_ref, weight, sem):
    copies = load_blocks(at_ref, (w0, w1, w2, w3, w4, w5), weight, sem)
    rows, width = own_ref.shape
    for part, ref in enumerate((own_ref, far_ref)):
        scaled, _ = normalize(ref[...].astype(FULL))
        normed_ref[pl.ds(part * rows, rows), :] = (scaled * gain_ref[...]).astype(LOW)
    wait_all(copies)
    for part in range(2):
        span = pl.ds(part * rows, rows)
        normed = normed_ref[span, :]
        cos_part, sin_part = cos_ref[span, :], sin_ref[span, :]
        for pair in range(2 * width // PAIR):
            lanes = pl.ds(pair * PAIR, PAIR)
            if pair % 2 == 0:
                both = mul(normed, weight[:, pl.ds(pair * PAIR, 2 * PAIR)])
            raw = both[:, (pair % 2) * PAIR : (pair % 2 + 1) * PAIR]
            turned = turn(raw, cos_part, sin_part)
            if pair < width // PAIR:
                query_ref[span, lanes] = (turned * SCALE).astype(LOW)
            else:
                kv_ref[0, span, pl.ds(pair * PAIR - width, PAIR)] = turned.astype(LOW)
        kv_ref[1, span, :] = mul(normed, weight[:, 2 * width :]).astype(LOW)


def head_lanes(head, shape):
    lane = lax.broadcasted_iota(jnp.int32, shape, 1)
    return (lane < HEAD_DIM) if head == 0 else (lane >= HEAD_DIM)


def pick(head, inside, outside):
    return jnp.where(head_lanes(head, inside.shape), inside, outside)


def attend_kernel(query_ref, near_ref, far_ref, mark_query_ref, mark_key_ref, o_ref, extra_ref):
    rows = query_ref.shape[0]
    query = query_ref[...]
    mark_query = mark_query_ref[...]
    parts = [
        (near_ref[0], jnp.transpose(near_ref[1]), mark_key_ref[:rows, :]),
        (far_ref[0], jnp.transpose(far_ref[1]), mark_key_ref[rows:, :]),
    ]
    outs, logs = [], []
    for head in range(2):
        query_head = pick(head, query, mark_query)
        scores = [mul_t(pick(head, key, mark), query_head) for key, _, mark in parts]
        top = jnp.maximum(
            jnp.max(scores[0], axis=0, keepdims=True), jnp.max(scores[1], axis=0, keepdims=True)
        )
        exps = [jnp.exp(score - top) for score in scores]
        total = jnp.sum(exps[0], axis=0, keepdims=True) + jnp.sum(exps[1], axis=0, keepdims=True)
        span = slice(head * HEAD_DIM, (head + 1) * HEAD_DIM)
        out = sum(mul(value_t[span], e.astype(LOW)) for (_, value_t, _), e in zip(parts, exps))
        outs.append(out / total)
        logs.append(top + jnp.log(total))
    o_ref[...] = jnp.transpose(jnp.concatenate(outs)).astype(LOW)
    line = lax.broadcasted_iota(jnp.int32, (PAIR, rows), 0)
    extra = jnp.zeros((PAIR, rows), FULL)
    for head in range(2):
        base = DOCS + (HEAD_DIM if head == 0 else 0)
        for i, piece in enumerate(three_parts(-logs[head])):
            extra = jnp.where(line == base + i, piece, extra)
    extra_ref[...] = jnp.transpose(extra).astype(LOW) + mark_query


def attend_back_kernel(query_ref, near_ref, far_ref, extra_ref, mark_key_ref, o_ref, do_ref,
                       cos_ref, sin_ref, dq_ref, keep_ref, send_ref):
    rows = query_ref.shape[0]
    query, extra, do = query_ref[...], extra_ref[...], do_ref[...]
    inner_all = do.astype(FULL) * o_ref[...].astype(FULL)
    lane = lax.broadcasted_iota(jnp.int32, (rows, PAIR), 1)
    zero = jnp.zeros((rows, PAIR), LOW)
    grads_query = []
    sums = [[None, None], [None, None]]
    keys_t = [jnp.transpose(near_ref[0]), jnp.transpose(far_ref[0])]
    for head in range(2):
        inside = head_lanes(head, (rows, PAIR))
        inner = jnp.sum(jnp.where(inside, inner_all, 0.0), axis=1, keepdims=True)
        base = DOCS + (HEAD_DIM if head == 0 else 0)
        tail = jnp.zeros((rows, PAIR), FULL)
        for i, piece in enumerate(three_parts(-inner)):
            tail = jnp.where(lane == base + i, piece, tail)
        query_head = pick(head, query, extra)
        do_head = pick(head, do, tail.astype(LOW))
        query_only = pick(head, query, zero)
        do_only = pick(head, do, zero)
        span = slice(head * HEAD_DIM, (head + 1) * HEAD_DIM)
        grad_query = 0.0
        for part, ref in enumerate((near_ref, far_ref)):
            mark = mark_key_ref[pl.ds(part * rows, rows), :]
            probs = jnp.exp(mul_t(pick(head, ref[0], mark), query_head))
            grad_probs = mul_t(pick(head, ref[1], mark), do_head)
            grad_scores = (probs * grad_probs).astype(LOW)
            grad_value = mul(probs.astype(LOW), do_only)
            grad_key = mul(grad_scores, query_only)
            grad_query += mul(keys_t[part][span], grad_scores)
            if head == 0:
                sums[part] = [grad_key, grad_value]
            else:
                sums[part] = [sums[part][0] + grad_key, sums[part][1] + grad_value]
        grads_query.append(grad_query)
    turned = turn(
        jnp.transpose(jnp.concatenate(grads_query)) * SCALE, cos_ref[...], -sin_ref[...]
    )
    dq_ref[...] = turned.astype(LOW)
    for i in range(2):
        keep_ref[i] = sums[0][i].astype(LOW)
        send_ref[i] = sums[1][i].astype(LOW)


def products(place, left_t, right, out, target, sem, first, rows, copies, blocks):
    for j in blocks:
        start = pl.multiple_of((place ^ j) * rows, rows)
        span = pl.ds(first, rows)
        out[j // 2, span, :] = mul(left_t[pl.ds(start, rows), :], right).astype(LOW)
        copies.append(put(out.at[j // 2, span, :], target.at[j // 2, span, :], sem.at[len(copies)]))


def middle_kernel(at_ref, live_ref, own_ref, far_ref, cot_own_ref, cot_far_ref, o_ref, gain_ref,
                  i0, i1, i2, i3, i4, i5, d0, d1, d2, d3, d4, d5,
                  mixed_own_ref, mixed_far_ref, dx1_ref, do_ref,
                  keep_in, send_in, keep_od, send_od,
                  w_out, w_in, w_down, o_t, a2_t, h_t, dm_all, duw_all, db_all,
                  mixed, dx1_all, do_all, in_keep, in_send, od_keep, od_send, sem, out_sem):
    place, live = at_ref[0], live_ref[0]
    width = w_out.shape[1]
    share, units = w_out.shape[0] // 4, w_down.shape[0]
    share_down = units // 4
    wide = (d0, d1, d2, d3, d4, d5)
    copies_out = load_blocks(at_ref, wide, w_out, sem.at[0], 0, share)
    copies_in = load_blocks(at_ref, (i0, i1, i2, i3, i4, i5), w_in, sem.at[1])
    copies_down = load_blocks(at_ref, wide, w_down, sem.at[2], share, share_down)
    rows = own_ref.shape[0]
    gain = gain_ref[...]
    copies = []
    for part, (ref, cot_ref, mixed_ref) in enumerate(
        ((own_ref, cot_own_ref, mixed_own_ref), (far_ref, cot_far_ref, mixed_far_ref))
    ):
        span = pl.ds(part * rows, rows)
        o = o_ref[span, :]
        if part == 0:
            wait_all(copies_out)
        x1 = ref[...].astype(FULL) + live * mul(o, w_out[...])
        scaled, root = normalize(x1)
        a2 = (scaled * gain).astype(LOW)
        if part == 0:
            wait_all(copies_in)
        u = mul(a2, w_in[:, :units])
        w = mul(a2, w_in[:, units:])
        phi = 0.5 * (1.0 + lax.erf(u * math.sqrt(0.5)))
        gelu = u * phi
        h = (gelu * w).astype(LOW)
        if part == 0:
            wait_all(copies_down)
        mixed[span, :] = (x1 + live * mul(h, w_down[...])).astype(LOW)
        copies.append(put(mixed.at[span, :], mixed_ref, out_sem.at[len(copies)]))
        cot = cot_ref[...].astype(FULL)
        dm = (live * cot).astype(LOW)
        dh = mul_t(dm, w_down[...])
        slope = phi + u * (jnp.exp(-0.5 * u * u) * (1.0 / math.sqrt(2.0 * math.pi)))
        duw_all[span, :units] = (dh * w * slope).astype(LOW)
        duw_all[span, units:] = (dh * gelu).astype(LOW)
        da2 = mul_t(duw_all[span, :], w_in[...])
        dx1 = cot + normalize_back(da2, gain, scaled, root)
        dx1_all[span, :] = dx1
        copies.append(put(dx1_all.at[span, :], dx1_ref.at[span, :], out_sem.at[len(copies)]))
        db = (live * dx1).astype(LOW)
        do_all[span, :] = mul_t(db, w_out[...]).astype(LOW)
        copies.append(put(do_all.at[span, :], do_ref.at[span, :], out_sem.at[len(copies)]))
        db_all[span, :] = db
        dm_all[span, :] = dm
        o_t[:, span] = jnp.transpose(o)
        a2_t[:, span] = jnp.transpose(a2)
        h_t[:, span] = jnp.transpose(h)
    dm, duw, db = dm_all[...], duw_all[...], db_all[...]
    for blocks, out_od, od, out_in, in_ in (
        ((1, 3), od_send, send_od, in_send, send_in),
        ((0, 2), od_keep, keep_od, in_keep, keep_in),
    ):
        products(place, a2_t, duw, out_in, in_, out_sem, 0, share, copies, blocks)
        products(place, h_t, dm, out_od, od, out_sem, share, share_down, copies, blocks)
        products(place, o_t, db, out_od, od, out_sem, 0, share, copies, blocks)
    wait_all(copies)


def send_kernel(count, at_ref, normed_ref, *refs):
    groups = [refs[i * count : (i + 1) * count] for i in range(3)]
    cos_ref, sin_ref, dqkv_ref, normed_t_ref, send_ref, dqkv, normed_t, send, sem = refs[3 * count :]
    width = normed_ref.shape[1]
    part_width = width // count
    normed_t[...] = jnp.transpose(normed_ref[...])
    copies = [put(normed_t, normed_t_ref, sem.at[0])]
    cos_part, sin_part = cos_ref[...], -sin_ref[...]
    for part, (dq, own, got) in enumerate(zip(*groups)):
        base = part * part_width
        dqkv[:, pl.ds(base, part_width)] = dq[...]
        dqkv[:, pl.ds(2 * width + base, part_width)] = (
            own[1].astype(FULL) + got[1].astype(FULL)
        ).astype(LOW)
        for pair in range(part_width // PAIR):
            lanes = pl.ds(pair * PAIR, PAIR)
            raw = own[0, :, lanes].astype(FULL) + got[0, :, lanes].astype(FULL)
            dqkv[:, pl.ds(width + base + pair * PAIR, PAIR)] = turn(raw, cos_part, sin_part).astype(
                LOW
            )
    copies.append(put(dqkv, dqkv_ref, sem.at[1]))
    right = dqkv[...]
    share = send.shape[1]
    for j in (1, 3):
        start = pl.multiple_of((at_ref[0] ^ j) * share, share)
        send[j // 2] = mul(normed_t[pl.ds(start, share), :], right).astype(LOW)
        copies.append(put(send.at[j // 2], send_ref.at[j // 2], sem.at[len(copies)]))
    wait_all(copies)


def keep_kernel(at_ref, normed_t_ref, dqkv_ref, keep_ref, keep, sem):
    right = dqkv_ref[...]
    share = keep.shape[1]
    copies = []
    for j in (0, 2):
        start = pl.multiple_of((at_ref[0] ^ j) * share, share)
        keep[j // 2] = mul(normed_t_ref[pl.ds(start, share), :], right).astype(LOW)
        copies.append(put(keep.at[j // 2], keep_ref.at[j // 2], sem.at[len(copies)]))
    wait_all(copies)


def input_kernel(at_ref, own_ref, far_ref, gain_ref, dx1_ref, dqkv_ref, w0, w1, w2, w3, w4, w5,
                 grad_own_ref, grad_far_ref, weight, grad_own, sem, out_sem):
    wait_all(load_blocks(at_ref, (w0, w1, w2, w3, w4, w5), weight, sem))
    rows = own_ref.shape[0]
    gain = gain_ref[...]
    for part, ref in enumerate((far_ref, own_ref)):
        span = pl.ds((1 - part) * rows, rows)
        scaled, root = normalize(ref[...].astype(FULL))
        back = normalize_back(mul_t(dqkv_ref[span, :], weight[...]), gain, scaled, root)
        grad = dx1_ref[span, :] + back
        if part == 0:
            grad_far_ref[...] = grad.astype(LOW)
        else:
            grad_own[...] = grad
    put(grad_own, grad_own_ref, out_sem.at[0]).wait()


def shaped(*shape, kind=LOW):
    return jax.ShapeDtypeStruct(shape, kind)


IN_SMEM = pl.BlockSpec(memory_space=pltpu.SMEM)
IN_VMEM = pl.BlockSpec(memory_space=pltpu.VMEM)
IN_ANY = pl.BlockSpec(memory_space=pl.ANY)


def params(mebibytes):
    return pltpu.CompilerParams(vmem_limit_bytes=mebibytes * 1024 * 1024)


def call(kernel, args, in_specs, late=(), **options):
    count, skip = len(args), len(late)

    def body(*refs):
        return kernel(*refs[:count], *refs[count + skip :])

    return pl.pallas_call(body, in_specs=list(in_specs) + [IN_ANY] * skip, **options)(*args, *late)


def project(at, own, far, gain, cos_part, sin_part, blocks, late):
    rows, width = 2 * own.shape[0], own.shape[1]
    return call(
        project_kernel,
        (at, own, far, gain, cos_part, sin_part, *blocks),
        late=late,
        out_shape=(shaped(rows, width), shaped(rows, width), shaped(2, rows, width)),
        in_specs=[IN_SMEM] + [IN_VMEM] * 5 + [IN_ANY] * 6,
        out_specs=(IN_VMEM,) * 3,
        scratch_shapes=[pltpu.VMEM((width, 3 * width), LOW), pltpu.SemaphoreType.DMA((6,))],
        compiler_params=params(24),
        name="project",
    )


def attend(first, count, query, near, far, mark_query, mark_key, late=()):
    rows = query.shape[0]
    row_spec = pl.BlockSpec((rows, PAIR), lambda i: (0, i + first))
    kv_spec = pl.BlockSpec((2, rows, PAIR), lambda i: (0, 0, i + first))
    out_spec = pl.BlockSpec((rows, PAIR), lambda i: (0, i))
    return call(
        attend_kernel,
        (query, near, far, mark_query, mark_key),
        late=late,
        grid=(count,),
        out_shape=(shaped(rows, count * PAIR), shaped(rows, count * PAIR)),
        in_specs=[
            row_spec,
            kv_spec,
            kv_spec,
            pl.BlockSpec((rows, PAIR), lambda i: (0, 0)),
            pl.BlockSpec((2 * rows, PAIR), lambda i: (0, 0)),
        ],
        out_specs=(out_spec, out_spec),
        compiler_params=params(32),
        name="attend",
    )


def attend_back(first, count, query, near, far, extra, mark_key, o, do, cos_part, sin_part, late=()):
    rows = query.shape[0]
    row_spec = pl.BlockSpec((rows, PAIR), lambda i: (0, i + first))
    kv_spec = pl.BlockSpec((2, rows, PAIR), lambda i: (0, 0, i + first))
    fixed = pl.BlockSpec((rows, PAIR), lambda i: (0, 0))
    out_row = pl.BlockSpec((rows, PAIR), lambda i: (0, i))
    out_kv = pl.BlockSpec((2, rows, PAIR), lambda i: (0, 0, i))
    return call(
        attend_back_kernel,
        (query, near, far, extra, mark_key, o, do, cos_part, sin_part),
        late=late,
        grid=(count,),
        out_shape=(
            shaped(rows, count * PAIR),
            shaped(2, rows, count * PAIR),
            shaped(2, rows, count * PAIR),
        ),
        in_specs=[
            row_spec,
            kv_spec,
            kv_spec,
            row_spec,
            pl.BlockSpec((2 * rows, PAIR), lambda i: (0, 0)),
            row_spec,
            row_spec,
            fixed,
            fixed,
        ],
        out_specs=(out_row, out_kv, out_kv),
        compiler_params=params(32),
        name="attend_back",
    )


def middle(at, live, own, far, cot_own, cot_far, o, gain, blocks_in, blocks_od):
    half, width = own.shape
    rows = 2 * half
    share = width // 4
    share_down = blocks_od[0].shape[0] - share
    units = 4 * share_down
    both = share + share_down
    low = lambda *shape: pltpu.VMEM(shape, LOW)
    return pl.pallas_call(
        middle_kernel,
        out_shape=(
            shaped(half, width),
            shaped(half, width),
            shaped(rows, width, kind=FULL),
            shaped(rows, width),
            shaped(2, share, 2 * units),
            shaped(2, share, 2 * units),
            shaped(2, both, width),
            shaped(2, both, width),
        ),
        in_specs=[IN_SMEM] * 2 + [IN_VMEM] * 6 + [IN_ANY] * 12,
        out_specs=(IN_ANY,) * 8,
        scratch_shapes=[
            low(width, width),
            low(width, 2 * units),
            low(units, width),
            low(width, rows),
            low(width, rows),
            low(units, rows),
            low(rows, width),
            low(rows, 2 * units),
            low(rows, width),
            low(rows, width),
            pltpu.VMEM((rows, width), FULL),
            low(rows, width),
            low(2, share, 2 * units),
            low(2, share, 2 * units),
            low(2, both, width),
            low(2, both, width),
            pltpu.SemaphoreType.DMA((3, 6)),
            pltpu.SemaphoreType.DMA((18,)),
        ],
        compiler_params=params(56),
        name="middle",
    )(at, live, own, far, cot_own, cot_far, o, gain, *blocks_in, *blocks_od)


def qkv_send(at, normed, dq, own, got, cos_part, sin_part, late):
    rows, width = normed.shape
    share = width // 4
    return call(
        functools.partial(send_kernel, len(dq)),
        (at, normed, *dq, *own, *got, cos_part, sin_part),
        late=late,
        out_shape=(
            shaped(rows, 3 * width),
            shaped(width, rows),
            shaped(2, share, 3 * width),
        ),
        in_specs=[IN_SMEM] + [IN_VMEM] * (3 + 3 * len(dq)),
        out_specs=(IN_ANY,) * 3,
        scratch_shapes=[
            pltpu.VMEM((rows, 3 * width), LOW),
            pltpu.VMEM((width, rows), LOW),
            pltpu.VMEM((2, share, 3 * width), LOW),
            pltpu.SemaphoreType.DMA((4,)),
        ],
        compiler_params=params(32),
        name="qkv_send",
    )


def qkv_keep(at, normed_t, dqkv, late):
    width, rows = normed_t.shape
    share = width // 4
    return call(
        keep_kernel,
        (at, normed_t, dqkv),
        late=late,
        out_shape=shaped(2, share, 3 * width),
        in_specs=[IN_SMEM] + [IN_VMEM] * 2,
        out_specs=IN_ANY,
        scratch_shapes=[
            pltpu.VMEM((2, share, 3 * width), LOW),
            pltpu.SemaphoreType.DMA((2,)),
        ],
        compiler_params=params(24),
        name="qkv_keep",
    )


def input_back(at, own, far, gain, dx1, dqkv, blocks, late):
    half, width = own.shape
    return call(
        input_kernel,
        (at, own, far, gain, dx1, dqkv, *blocks),
        late=late,
        out_shape=(shaped(half, width, kind=FULL), shaped(half, width)),
        in_specs=[IN_SMEM] + [IN_VMEM] * 5 + [IN_ANY] * 6,
        out_specs=(IN_ANY, IN_VMEM),
        scratch_shapes=[
            pltpu.VMEM((width, 3 * width), LOW),
            pltpu.VMEM((half, width), FULL),
            pltpu.SemaphoreType.DMA((6,)),
            pltpu.SemaphoreType.DMA((1,)),
        ],
        compiler_params=params(32),
        name="input_back",
    )


def gate(values, late):
    return call(
        lambda *refs: None,
        values,
        late=late,
        out_shape=tuple(jax.ShapeDtypeStruct(v.shape, v.dtype) for v in values),
        in_specs=[IN_ANY] * len(values),
        out_specs=(IN_ANY,) * len(values),
        input_output_aliases={i: i for i in range(len(values))},
        name="gate",
    )


def first_sums_kernel(cuts, at_ref, *refs):
    count = len(cuts)
    sums = refs[: 2 * count]
    outs = refs[2 * count :]
    half = at_ref[1]
    for i, cut in enumerate(cuts):
        keep, got = sums[2 * i : 2 * i + 2]
        own_a, far_a, mine_b, give_b = outs[4 * i : 4 * i + 4]
        short = (keep.shape[1] - cut) // 2

        def add(block, start, size):
            span = pl.ds(start, size)
            return (keep[block, span, :].astype(FULL) + got[block, span, :].astype(FULL)).astype(LOW)

        far_a[...] = add(1, 0, cut)
        for block in range(2):
            give_b[block] = add(block, pl.multiple_of(cut + (1 - half) * short, 16), short)
            mine_b[block] = add(block, pl.multiple_of(cut + half * short, 16), short)
        own_a[...] = add(0, 0, cut)


def first_sums(at, cuts, pairs, late=()):
    shapes = []
    for cut, (keep, _) in zip(cuts, pairs):
        short, width = (keep.shape[1] - cut) // 2, keep.shape[2]
        shapes += [shaped(cut, width)] * 2 + [shaped(2, short, width)] * 2
    outs = call(
        functools.partial(first_sums_kernel, cuts),
        (at, *[value for pair in pairs for value in pair]),
        late=late,
        out_shape=tuple(shapes),
        in_specs=[IN_SMEM] + [IN_VMEM] * (2 * len(pairs)),
        out_specs=(IN_VMEM,) * len(shapes),
        compiler_params=params(40),
        name="first_sums",
    )
    return [outs[4 * i : 4 * i + 4] for i in range(len(cuts))]


def second_sums_kernel(count, at_ref, *refs):
    half = at_ref[1]
    ins, outs = refs[: 4 * count], refs[4 * count :]
    for i in range(count):
        own_a, got_a, mine_b, got_b = ins[4 * i : 4 * i + 4]
        mine_a, give_a, near_b, far_b = outs[4 * i : 4 * i + 4]
        short = own_a.shape[0] // 2
        for start, out in ((1 - half, give_a), (half, mine_a)):
            span = pl.ds(pl.multiple_of(start * short, 16), short)
            out[...] = (own_a[span, :].astype(FULL) + got_a[span, :].astype(FULL)).astype(LOW)
        for block, out in ((1, far_b), (0, near_b)):
            out[...] = (mine_b[block].astype(FULL) + got_b[block].astype(FULL)).astype(LOW)


def second_sums(at, items, late=()):
    shapes = []
    for own_a, _, mine_b, _ in items:
        rows, width = own_a.shape
        shapes += [shaped(rows // 2, width)] * 2 + [shaped(mine_b.shape[1], width)] * 2
    outs = call(
        functools.partial(second_sums_kernel, len(items)),
        (at, *[value for item in items for value in item]),
        late=late,
        out_shape=tuple(shapes),
        in_specs=[IN_SMEM] + [IN_VMEM] * (4 * len(items)),
        out_specs=(IN_VMEM,) * len(shapes),
        compiler_params=params(40),
        name="second_sums",
    )
    return [outs[4 * i : 4 * i + 4] for i in range(len(items))]


def third_sums_kernel(count, *refs):
    ins, outs = refs[: 4 * count], refs[4 * count :]
    for i, out in enumerate(outs):
        mine_a, got_a, near_b, got_b = ins[4 * i : 4 * i + 4]
        cut = mine_a.shape[0]
        out[:cut, :] = (mine_a[...].astype(FULL) + got_a[...].astype(FULL)).astype(LOW)
        out[cut:, :] = (near_b[...].astype(FULL) + got_b[...].astype(FULL)).astype(LOW)


def third_sums(items, late=()):
    shapes = [shaped(item[0].shape[0] + item[2].shape[0], item[0].shape[1]) for item in items]
    return call(
        functools.partial(third_sums_kernel, len(items)),
        [value for item in items for value in item],
        late=late,
        out_shape=tuple(shapes),
        in_specs=[IN_VMEM] * (4 * len(items)),
        out_specs=(IN_VMEM,) * len(shapes),
        compiler_params=params(40),
        name="third_sums",
    )


def low_sum(*values):
    return sum(value.astype(FULL) for value in values).astype(LOW)


def pick_part(value, index, count):
    size = value.shape[0] // count
    return lax.dynamic_slice_in_dim(value, index * size, size, 0)


def make(dp_count, seq_count):
    assert seq_count == 4 and dp_count % 4 == 0 and dp_count & (dp_count - 1) == 0
    bits = dp_count.bit_length() - 1
    steps = [(shift, min(2, bits - shift)) for shift in range(1, bits, 2)]
    upper = [1 << shift for shift in range(1, bits)]

    def trade(value, axis, bit):
        count = seq_count if axis == "seq" else dp_count
        return lax.ppermute(value, axis, [(i, i ^ bit) for i in range(count)])

    def split_steps(value, group, late=None):
        for shift, bit_count in steps:
            size = 1 << bit_count
            mine = (group >> shift) & (size - 1)
            value = jnp.pad(value, ((0, -value.shape[0] % size), (0, 0)))
            parts = [pick_part(value, mine ^ k, size) for k in range(1 if late is None else size)]
            got = [trade(parts[k], "dp", k << shift) for k in range(1, len(parts))]
            if late:
                got, late = gate(got, late), ()
            value = parts[0] if late is None else low_sum(parts[0], *got)
        return value

    def join_steps(value, group, rows, late=()):
        sizes = [rows]
        for _, bit_count in steps:
            sizes.append(-(-sizes[-1] >> bit_count))
        for (shift, bit_count), size_out in list(zip(steps, sizes))[::-1]:
            size = 1 << bit_count
            mine = (group >> shift) & (size - 1)
            got = [trade(value, "dp", k << shift) for k in range(1, size)]
            if late:
                got, late = gate(got, late), ()
            parts = jnp.stack([value, *got])
            ordered = [
                lax.dynamic_index_in_dim(parts, mine ^ k, 0, keepdims=False) for k in range(size)
            ]
            value = jnp.concatenate(ordered)[:size_out]
        return value

    def split_hops(value, group, lates=None):
        for i, bit in enumerate(upper):
            value = jnp.pad(value, ((0, value.shape[0] % 2), (0, 0)))
            mine = jnp.where(group & bit, 1, 0)
            keep = pick_part(value, mine, 2)
            if lates is not None:
                got = trade(pick_part(value, 1 - mine, 2), "dp", bit)
                if i < len(lates) and lates[i]:
                    (got,) = gate((got,), lates[i])
                keep = low_sum(keep, got)
            value = keep
        return value

    def join_hops(value, group, rows, lates):
        sizes = [rows]
        for _ in upper:
            sizes.append((sizes[-1] + 1) // 2)
        for i, bit in enumerate(upper[::-1]):
            got = trade(value, "dp", bit)
            if i < len(lates) and lates[i]:
                (got,) = gate((got,), lates[i])
            value = halves_join(value, got, jnp.where(group & bit, 1, 0))[: sizes[-2 - i]]
        return value

    def halves_join(mine, other, half):
        return jnp.where(
            half == 0, jnp.concatenate([mine, other]), jnp.concatenate([other, mine])
        )

    def sum_all(value, late):
        for bit in (2, 1):
            value = value + trade(value, "seq", bit)
        (value,) = gate((value,), late)
        for i in range(bits):
            value = value + trade(value, "dp", 1 << (bits - 1 - i))
        return value

    def on_device(
        tokens, cotangent, segments, valid,
        w_qkv, w_out, w_in, w_down, gains,
        m_qkv, m_out, m_in, m_down, m_gains,
        v_qkv, v_out, v_in, v_down, v_gains,
    ):
        place = lax.axis_index("seq")
        group = lax.axis_index("dp")
        slot = place >> 1
        half = group & 1
        local_len, width = tokens.shape[1:]
        rows = 2 * local_len
        at = jnp.stack([place, half])

        def mine_of(value):
            return lax.dynamic_index_in_dim(value, slot, 0, keepdims=False)

        def theirs_of(value):
            return lax.dynamic_index_in_dim(value, 1 - slot, 0, keepdims=False)

        def undeal(mine, theirs):
            theirs = trade(theirs, "seq", 2).astype(mine.dtype)
            return jnp.where(slot == 0, jnp.stack([mine, theirs]), jnp.stack([theirs, mine]))

        low_qkv = w_qkv.astype(LOW)
        near_q = trade(low_qkv, "seq", 1)
        far_qa = trade(pick_part(low_qkv, half, 2), "seq", 2)
        gain_far = trade(gains.astype(LOW), "seq", 2)
        gain_near = trade(jnp.stack([gains.astype(LOW), gain_far]), "seq", 1)
        gain_stack = jnp.stack([gains.astype(LOW), gain_near[0], gain_far, gain_near[1]])
        gain_low = jnp.concatenate(
            [lax.dynamic_index_in_dim(gain_stack, b ^ place, 0, keepdims=False) for b in range(4)],
            axis=1,
        ).astype(FULL)
        own = mine_of(tokens)
        far = trade(theirs_of(tokens), "seq", 2)
        far_qb = trade(far_qa, "dp", 1)
        near_qa = trade(far_qa, "seq", 1)
        near_qb = trade(far_qb, "seq", 1)
        blocks_qkv = (low_qkv, near_q, far_qa, far_qb, near_qa, near_qb)

        low_in = w_in.astype(LOW)
        low_od = jnp.concatenate([w_out.astype(LOW), w_down.astype(LOW)])
        half_od = jnp.concatenate(
            [pick_part(w_out, half, 2).astype(LOW), pick_part(w_down, half, 2).astype(LOW)]
        )
        far_ia = trade(pick_part(low_in, half, 2), "seq", 2)
        far_oa = trade(half_od, "seq", 2)

        seg = mine_of(segments)
        positions = doc_positions(seg).reshape(4, local_len)
        seg = seg.reshape(4, local_len)
        chunks = [place, place ^ 2, place ^ 1, place ^ 3]
        seg_keys = jnp.concatenate(
            [lax.dynamic_index_in_dim(seg, c, 0, keepdims=False) for c in chunks]
        )
        pos = jnp.concatenate(
            [lax.dynamic_index_in_dim(positions, c, 0, keepdims=False) for c in chunks[:2]]
        )
        cos_part, sin_part = rope_tables(pos)
        lane = jnp.arange(PAIR, dtype=jnp.int32)[None] % HEAD_DIM
        same = seg_keys[:, None] == lane
        mark_key = jnp.where(lane < DOCS, 1.0 - same, (lane < DOCS + 3) * 1.0).astype(LOW)
        mark_query = jnp.where((lane < DOCS) & same[:rows], NEG_FILL, 0.0).astype(LOW)
        live = lax.dynamic_index_in_dim(valid, slot, 0, keepdims=True).astype(FULL)

        normed, query, kv = project(
            at, own, far, gain_low[:1], cos_part, sin_part, blocks_qkv, (far_ia,)
        )
        kv_far = trade(kv, "seq", 1)
        far_ib = trade(far_ia, "dp", 1)
        near_i = trade(low_in, "seq", 1)
        near_o = trade(low_od, "seq", 1)
        near_ia = trade(far_ia, "seq", 1)
        cot_far = trade(theirs_of(cotangent), "seq", 2)
        pairs = width // PAIR
        args = (query, kv, kv_far, mark_query, mark_key)
        o_a, extra_a = attend(0, pairs // 2, *args)
        far_ib, far_oa = gate((far_ib, far_oa), (o_a,))
        far_ob = trade(far_oa, "dp", 1)
        o_b, extra_b = attend(pairs // 2, pairs - pairs // 2, *args, late=(far_oa, far_ib, o_a))
        (far_ob,) = gate((far_ob,), (o_b,))
        near_oa = trade(far_oa, "seq", 1)
        near_ib = trade(far_ib, "seq", 1)
        near_ob = trade(far_ob, "seq", 1)
        blocks_in = (low_in, near_i, far_ia, far_ib, near_ia, near_ib)
        blocks_od = (low_od, near_o, far_oa, far_ob, near_oa, near_ob)

        o = jnp.concatenate([o_a, o_b], axis=1)
        extra = jnp.concatenate([extra_a, extra_b], axis=1)
        mixed_own, mixed_far, dx1, do, keep_in, send_in, keep_od, send_od = middle(
            at, live, own, far, mine_of(cotangent), cot_far, o, gain_low[1:], blocks_in, blocks_od
        )
        got_in = trade(send_in, "seq", 1)
        got_od = trade(send_od, "seq", 1)
        mixed = undeal(mixed_own, mixed_far)
        back_args = (query, kv, kv_far, extra, mark_key, o, do, cos_part, sin_part)
        third = pairs // 3
        dq0, own0, give0 = attend_back(0, third, *back_args)
        cut_in = keep_in.shape[1] // 2
        cut_od = (keep_od.shape[1] // 2 + 31) // 32 * 32
        (in1, od1) = first_sums(
            at, (cut_in, cut_od), ((keep_in, got_in), (keep_od, got_od)), late=(own0,)
        )
        got_oa, got_ob = trade(od1[1], "seq", 2), trade(od1[3], "dp", 1)
        got0 = trade(give0, "seq", 1)
        dq1, own1, give1 = attend_back(third, third, *back_args, late=(od1[0],))
        (od2,) = second_sums(at, ((od1[0], got_oa, od1[2], got_ob),), late=(own1,))
        od_x, od_y = trade(od2[1], "dp", 1), trade(od2[3], "seq", 2)
        got1 = trade(give1, "seq", 1)
        dq2, own2, give2 = attend_back(
            2 * third, pairs - 2 * third, *back_args, late=(own1, od2[0])
        )
        (od_half,) = third_sums(((od2[0], od_x, od2[2], od_y),), late=(own2,))
        (give2,) = gate((give2,), (od_half,))
        got2 = trade(give2, "seq", 1)
        got_ia, got_ib = trade(in1[1], "seq", 2), trade(in1[3], "dp", 1)
        dqkv, normed_t, send_qkv = qkv_send(
            at, normed, (dq0, dq1, dq2), (own0, own1, own2), (got0, got1, got2),
            cos_part, sin_part, late=(od_half, got_ia, got_ib),
        )
        got_qkv = trade(send_qkv, "seq", 1)
        (in2,) = second_sums(at, ((in1[0], got_ia, in1[2], got_ib),), late=(dqkv,))
        in_x, in_y = trade(in2[1], "dp", 1), trade(in2[3], "seq", 2)
        keep_qkv = qkv_keep(at, normed_t, dqkv, late=(in2[0],))
        cut_qkv = keep_qkv.shape[1] // 2
        (q1,) = first_sums(at, (cut_qkv,), ((keep_qkv, got_qkv),))
        got_qa, got_qb = trade(q1[1], "seq", 2), trade(q1[3], "dp", 1)
        od_piece = split_hops(od_half, group, ((dqkv,), (keep_qkv,)))
        (in_half,) = third_sums(((in2[0], in_x, in2[2], in_y),), late=(q1[0],))
        grad_own, grad_far = input_back(
            at, own, far, gain_low[:1], dx1, dqkv, blocks_qkv, late=(in_half,)
        )
        (q2,) = second_sums(at, ((q1[0], got_qa, q1[2], got_qb),), late=(grad_own,))
        in_piece = split_hops(in_half, group, ((grad_own,), (q2[0],)))
        (qkv_half,) = third_sums(
            ((q2[0], trade(q2[1], "dp", 1), q2[2], trade(q2[3], "seq", 2)),)
        )
        od_mine = join_hops(od_piece, group, od_half.shape[0], ((grad_own,), (q2[0],)))
        qkv_piece = split_steps(qkv_half, group, (qkv_half,))
        in_mine = join_hops(in_piece, group, in_half.shape[0], ((qkv_half,), (qkv_piece,)))
        (grad_far,) = gate((grad_far,), (qkv_half,))
        input_grad = undeal(grad_own, grad_far)

        def half_of(value, cut):
            parts = [pick_part(value[:cut], half, 2), pick_part(value[cut:], half, 2)]
            return jnp.concatenate(parts)

        def qkv_rows(value):
            return split_steps(half_of(value, cut_qkv), group)

        def in_rows(value):
            return split_hops(half_of(value, cut_in), group)

        def gain_grad(weight, gradient, gain):
            total = jnp.sum(weight.astype(LOW).astype(FULL) * gradient.astype(FULL), axis=1)
            return total / gain

        gain_rows = gains.astype(LOW).astype(FULL)
        gain_one = gain_grad(qkv_rows(w_qkv), qkv_piece, 1.0)
        gain_two = gain_grad(in_rows(w_in), in_piece, 1.0)
        gain_at = [qkv_rows(gain_rows[0][:, None])[:, 0], in_rows(gain_rows[1][:, None])[:, 0]]
        gain_at = [jnp.where(g == 0.0, 1.0, g) for g in gain_at]
        square = sum(
            jnp.sum(jnp.square(piece.astype(FULL)))
            for piece in (qkv_piece, in_piece, od_piece, gain_one / gain_at[0], gain_two / gain_at[1])
        )
        qkv_mine = join_steps(qkv_piece, group, qkv_half.shape[0])
        grad_norm = jnp.sqrt(sum_all(square.reshape(1, 1), (qkv_mine,))[0, 0])
        factor = jnp.minimum(1.0, CLIP_LIMIT / (grad_norm + 1e-06))

        def whole(mine, cut):
            other = trade(mine, "dp", 1)
            part = cut // 2
            return jnp.concatenate(
                [
                    halves_join(mine[:part], other[:part], half),
                    halves_join(mine[part:], other[part:], half),
                ]
            )

        in_all = whole(in_mine, cut_in)
        od_all = whole(od_mine, cut_od)
        qkv_all = whole(qkv_mine, cut_qkv)
        share = w_out.shape[0]
        gain_all = jnp.stack(
            [
                gain_grad(w_qkv, qkv_all, gain_rows[0]),
                gain_grad(w_in, in_all, gain_rows[1]),
            ]
        )
        shares = (qkv_all, od_all[:share], in_all, od_all[share:], gain_all)
        masters = (w_qkv, w_out, w_in, w_down, gains)
        firsts = (m_qkv, m_out, m_in, m_down, m_gains)
        seconds = (v_qkv, v_out, v_in, v_down, v_gains)
        updates = [
            adam_step(w, m, v, g.astype(FULL), factor, rate, decay)
            for w, m, v, g, rate, decay in zip(
                masters, firsts, seconds, shares, STEP_RATES, DECAY_RATES
            )
        ]
        return (
            mixed,
            input_grad,
            grad_norm,
            *[u[0] for u in updates],
            *[u[1] for u in updates],
            *[u[2] for u in updates],
        )

    return on_device


def solution(mesh):
    rows, matrix, gain = P("dp", "seq", None), P("seq", None), P(None, "seq")
    weights = (matrix,) * 4 + (gain,)
    return jax.shard_map(
        make(mesh.shape["dp"], mesh.shape["seq"]),
        mesh=mesh,
        in_specs=(rows, rows, P("dp", None), P("dp")) + weights * 3,
        out_specs=(rows, rows, P()) + weights * 3,
        check_vma=False,
    )
```

```python
import functools
import math

import jax
import jax.numpy as jnp
from jax import lax
from jax.experimental import pallas as pl
from jax.experimental.pallas import tpu as pltpu
from jax.sharding import PartitionSpec as P

HEADS = 12
HEAD_DIM = 64
PAIR = 2 * HEAD_DIM
STEP_COUNT = 10
EPS_NORM = 1e-05
ROPE_BASE = 160000.0
NEG_FILL = -1e30
CLIP_LIMIT = 10.0
BETA_FIRST = 0.9
BETA_SECOND = 0.98
EPS_ADAM = 1e-06
STEP_RATES = (0.1, 0.5, 0.1, 0.1, 1.0)
DECAY_RATES = (0.01, 0.01, 0.01, 0.01, 0.0)
DOCS = 5
LOW = jnp.bfloat16
FULL = jnp.float32
SCALE = 1.0 / math.sqrt(HEAD_DIM)


def doc_positions(segment_ids):
    seq_len = segment_ids.shape[-1]
    places = jnp.arange(seq_len, dtype=jnp.int32)
    first_mark = jnp.ones((1,), jnp.bool_)
    change = jnp.concatenate([first_mark, segment_ids[1:] != segment_ids[:-1]])
    starts = lax.cummax(jnp.where(change, places, 0), axis=0)
    return places - starts


def rope_tables(positions):
    half_dim = HEAD_DIM // 2
    exponents = jnp.arange(half_dim, dtype=jnp.float32) * (2.0 / HEAD_DIM)
    inv_freq = ROPE_BASE ** (-exponents)
    angles = positions.astype(jnp.float32)[:, None] * inv_freq
    cos_part, sin_part = jnp.cos(angles), jnp.sin(angles)
    return (
        jnp.concatenate([cos_part] * 4, axis=1),
        jnp.concatenate([-sin_part, sin_part] * 2, axis=1),
    )


def adam_step(weight, first_old, second_old, gradient, factor, step_rate, decay_rate):
    clipped = gradient * factor
    first_new = BETA_FIRST * first_old + (1.0 - BETA_FIRST) * clipped
    second_new = BETA_SECOND * second_old + (1.0 - BETA_SECOND) * clipped * clipped
    first_hat = first_new / (1.0 - BETA_FIRST**STEP_COUNT)
    second_hat = second_new / (1.0 - BETA_SECOND**STEP_COUNT)
    weight_new = weight * (1.0 - step_rate * decay_rate) - step_rate * first_hat / (
        jnp.sqrt(second_hat) + EPS_ADAM
    )
    return (weight_new, first_new, second_new)


def mul(left, right):
    return lax.dot_general(left, right, (((1,), (0,)), ((), ())), preferred_element_type=FULL)


def mul_t(left, right):
    return lax.dot_general(left, right, (((1,), (1,)), ((), ())), preferred_element_type=FULL)


def normalize(values):
    centered = values - jnp.mean(values, axis=-1, keepdims=True)
    root = lax.rsqrt(jnp.mean(centered * centered, axis=-1, keepdims=True) + EPS_NORM)
    return centered * root, root


def normalize_back(grad, gain, scaled, root):
    t = grad * gain
    back = root * (
        t
        - jnp.mean(t, axis=-1, keepdims=True)
        - scaled * jnp.mean(t * scaled, axis=-1, keepdims=True)
    )
    return back


def turn(values, cos_part, sin_part):
    lane = lax.broadcasted_iota(jnp.int32, values.shape, 1)
    swapped = jnp.where(
        lane % HEAD_DIM < HEAD_DIM // 2,
        pltpu.roll(values, PAIR - HEAD_DIM // 2, 1),
        pltpu.roll(values, HEAD_DIM // 2, 1),
    )
    return values * cos_part + swapped * sin_part


def three_parts(values):
    high = values.astype(LOW).astype(FULL)
    rest = values - high
    mid = rest.astype(LOW).astype(FULL)
    return high, mid, rest - mid


def wait_all(copies):
    for copy in copies:
        copy.wait()


def put(source, target, sem):
    copy = pltpu.make_async_copy(source, target, sem)
    copy.start()
    return copy


PIECES = ((0, None), (1, None), (2, 0), (2, 1), (3, 0), (3, 1))


def load_blocks(at_ref, blocks, whole, sem):
    rows = blocks[0].shape[0]
    copies = []
    for i, (bits, part) in enumerate(PIECES):
        start = (at_ref[0] ^ bits) * rows
        size = rows
        if part is not None:
            size = rows // 2
            start += (at_ref[1] ^ part) * size
        target = whole.at[pl.ds(pl.multiple_of(start, size), size), :]
        copies.append(put(blocks[i], target, sem.at[i]))
    return copies


def load_folded(at_ref, blocks, w_out, w_down, sem):
    rows, width = blocks[0].shape[0], w_out.shape[1]
    short, last = rows // 2, width // 2
    copies = []

    def copy(source, target):
        copies.append(put(source, target, sem.at[len(copies)]))

    for i, (bits, part) in enumerate(PIECES):
        owner = at_ref[0] ^ bits
        base = owner * (rows + short)
        first = 0 if part is None else (at_ref[1] ^ part) * short
        size = rows if part is None else short
        for lanes, whole, start in ((0, w_out, owner * rows), (width, w_down, base)):
            span = pl.ds(pl.multiple_of(start + first, short), size)
            copy(blocks[i].at[:, pl.ds(lanes, width)], whole.at[span, :])
        span = pl.ds(pl.multiple_of(base + rows, short), short)
        if part is None:
            for fold in range(2):
                copy(
                    blocks[i].at[pl.ds(fold * short, short), pl.ds(2 * width, last)],
                    w_down.at[span, pl.ds(fold * last, last)],
                )
        else:
            lanes = pl.ds(pl.multiple_of((at_ref[1] ^ part) * last, last), last)
            copy(blocks[i].at[:, pl.ds(2 * width, last)], w_down.at[span, lanes])
    return copies


def fold(out, w_out, w_down, first):
    rows, width = w_out.shape
    short, last = rows // 2, width // 2
    out[:, first : first + width] = w_out[...].astype(LOW)
    out[:, first + width : first + 2 * width] = w_down[:rows, :].astype(LOW)
    for i in range(2):
        out[i * short : (i + 1) * short, first + 2 * width :] = w_down[
            rows:, i * last : (i + 1) * last
        ].astype(LOW)


def prepare_first_kernel(at_ref, w_ref, low_ref, half_ref):
    short = half_ref.shape[0]
    half_ref[...] = w_ref[pl.ds(pl.multiple_of(at_ref[1] * short, short), short), :].astype(LOW)
    low_ref[...] = w_ref[...].astype(LOW)


def prepare_rest_kernel(at_ref, in_ref, out_ref, down_ref, cot_ref,
                        low_in, half_in, low_od, half_od, their_cot):
    short = half_in.shape[0]
    span = pl.ds(pl.multiple_of(at_ref[1] * short, short), short)
    low_in[...] = in_ref[...].astype(LOW)
    half_in[...] = in_ref[span, :].astype(LOW)
    fold(low_od, out_ref, down_ref, 0)
    half_od[...] = low_od[span, :]
    their_cot[...] = cot_ref[1 - at_ref[2]]


def project_kernel(at_ref, tokens_ref, far_ref, gain_ref, cos_ref, sin_ref, w0, w1, w2, w3, w4, w5,
                   normed_ref, query_ref, kv_ref, weight, sem):
    copies = load_blocks(at_ref, (w0, w1, w2, w3, w4, w5), weight, sem)
    rows, width = far_ref.shape
    for part in range(2):
        values = tokens_ref[at_ref[2]] if part == 0 else far_ref[...]
        scaled, _ = normalize(values.astype(FULL))
        normed_ref[pl.ds(part * rows, rows), :] = (scaled * gain_ref[...]).astype(LOW)
    wait_all(copies)
    for part in range(2):
        span = pl.ds(part * rows, rows)
        normed = normed_ref[span, :]
        cos_part, sin_part = cos_ref[span, :], sin_ref[span, :]
        for pair in range(2 * width // PAIR):
            lanes = pl.ds(pair * PAIR, PAIR)
            if pair % 2 == 0:
                both = mul(normed, weight[:, pl.ds(pair * PAIR, 2 * PAIR)])
            raw = both[:, (pair % 2) * PAIR : (pair % 2 + 1) * PAIR]
            turned = turn(raw, cos_part, sin_part)
            if pair < width // PAIR:
                query_ref[span, lanes] = (turned * SCALE).astype(LOW)
            else:
                kv_ref[0, span, pl.ds(pair * PAIR - width, PAIR)] = turned.astype(LOW)
        kv_ref[1, span, :] = mul(normed, weight[:, 2 * width :]).astype(LOW)


def head_lanes(head, shape):
    lane = lax.broadcasted_iota(jnp.int32, shape, 1)
    return (lane < HEAD_DIM) if head == 0 else (lane >= HEAD_DIM)


def pick(head, inside, outside):
    return jnp.where(head_lanes(head, inside.shape), inside, outside)


def attend_kernel(query_ref, near_ref, far_ref, mark_query_ref, mark_key_ref, o_ref, extra_ref):
    rows = query_ref.shape[0]
    query = query_ref[...]
    mark_query = mark_query_ref[...]
    parts = [
        (near_ref[0], jnp.transpose(near_ref[1]), mark_key_ref[:rows, :]),
        (far_ref[0], jnp.transpose(far_ref[1]), mark_key_ref[rows:, :]),
    ]
    outs, logs = [], []
    for head in range(2):
        query_head = pick(head, query, mark_query)
        scores = [mul_t(pick(head, key, mark), query_head) for key, _, mark in parts]
        top = jnp.maximum(
            jnp.max(scores[0], axis=0, keepdims=True), jnp.max(scores[1], axis=0, keepdims=True)
        )
        exps = [jnp.exp(score - top) for score in scores]
        total = jnp.sum(exps[0], axis=0, keepdims=True) + jnp.sum(exps[1], axis=0, keepdims=True)
        span = slice(head * HEAD_DIM, (head + 1) * HEAD_DIM)
        out = sum(mul(value_t[span], e.astype(LOW)) for (_, value_t, _), e in zip(parts, exps))
        outs.append(out / total)
        logs.append(top + jnp.log(total))
    o_ref[...] = jnp.transpose(jnp.concatenate(outs)).astype(LOW)
    line = lax.broadcasted_iota(jnp.int32, (PAIR, rows), 0)
    extra = jnp.zeros((PAIR, rows), FULL)
    for head in range(2):
        base = DOCS + (HEAD_DIM if head == 0 else 0)
        for i, piece in enumerate(three_parts(-logs[head])):
            extra = jnp.where(line == base + i, piece, extra)
    extra_ref[...] = jnp.transpose(extra).astype(LOW) + mark_query


def attend_back_kernel(query_ref, near_ref, far_ref, extra_ref, mark_key_ref, o_ref, do_ref,
                       cos_ref, sin_ref, dq_ref, keep_ref, send_ref):
    rows = query_ref.shape[0]
    query, extra, do = query_ref[...], extra_ref[...], do_ref[...]
    inner_all = do.astype(FULL) * o_ref[...].astype(FULL)
    lane = lax.broadcasted_iota(jnp.int32, (rows, PAIR), 1)
    zero = jnp.zeros((rows, PAIR), LOW)
    grads_query = []
    sums = [[None, None], [None, None]]
    keys_t = [jnp.transpose(near_ref[0]), jnp.transpose(far_ref[0])]
    for head in range(2):
        inside = head_lanes(head, (rows, PAIR))
        inner = jnp.sum(jnp.where(inside, inner_all, 0.0), axis=1, keepdims=True)
        base = DOCS + (HEAD_DIM if head == 0 else 0)
        tail = jnp.zeros((rows, PAIR), FULL)
        for i, piece in enumerate(three_parts(-inner)):
            tail = jnp.where(lane == base + i, piece, tail)
        query_head = pick(head, query, extra)
        do_head = pick(head, do, tail.astype(LOW))
        query_only = pick(head, query, zero)
        do_only = pick(head, do, zero)
        span = slice(head * HEAD_DIM, (head + 1) * HEAD_DIM)
        grad_query = 0.0
        for part, ref in enumerate((near_ref, far_ref)):
            mark = mark_key_ref[pl.ds(part * rows, rows), :]
            probs = jnp.exp(mul_t(pick(head, ref[0], mark), query_head))
            grad_probs = mul_t(pick(head, ref[1], mark), do_head)
            grad_scores = (probs * grad_probs).astype(LOW)
            grad_value = mul(probs.astype(LOW), do_only)
            grad_key = mul(grad_scores, query_only)
            grad_query += mul(keys_t[part][span], grad_scores)
            if head == 0:
                sums[part] = [grad_key, grad_value]
            else:
                sums[part] = [sums[part][0] + grad_key, sums[part][1] + grad_value]
        grads_query.append(grad_query)
    turned = turn(
        jnp.transpose(jnp.concatenate(grads_query)) * SCALE, cos_ref[...], -sin_ref[...]
    )
    dq_ref[...] = turned.astype(LOW)
    for i in range(2):
        keep_ref[i] = sums[0][i].astype(LOW)
        send_ref[i] = sums[1][i].astype(LOW)


def middle_kernel(at_ref, live_ref, tokens_ref, far_ref, cot_ref, cot_far_ref, oa_ref, ob_ref,
                  gain_ref, i0, i1, i2, i3, i4, i5, d0, d1, d2, d3, d4, d5,
                  mixed_ref, mixed_far_ref, dx1_ref, do_ref, keep_ref, send_ref,
                  w_out, w_in, w_down, o_all, o_t, a2_t, h_t, dm_all, duw_all, db_all,
                  mixed, dx1_all, do_all, keep, send, sem, fold_sem, out_sem):
    place, slot, live = at_ref[0], at_ref[2], live_ref[0]
    copies_down = load_folded(at_ref, (d0, d1, d2, d3, d4, d5), w_out, w_down, fold_sem)
    copies_in = load_blocks(at_ref, (i0, i1, i2, i3, i4, i5), w_in, sem)
    rows, width = far_ref.shape
    share = width // 4
    short, units = share // 2, w_down.shape[0]
    gain = gain_ref[...]
    o_all[:, : oa_ref.shape[1]] = oa_ref[...]
    o_all[:, oa_ref.shape[1] :] = ob_ref[...]
    copies = []
    for part in range(2):
        span = pl.ds(part * rows, rows)
        o = o_all[span, :]
        values = tokens_ref[slot] if part == 0 else far_ref[...]
        if part == 0:
            wait_all(copies_down)
        x1 = values.astype(FULL) + live * mul(o, w_out[...])
        scaled, root = normalize(x1)
        a2 = (scaled * gain).astype(LOW)
        if part == 0:
            wait_all(copies_in)
        u = mul(a2, w_in[:, :units])
        w = mul(a2, w_in[:, units:])
        phi = 0.5 * (1.0 + lax.erf(u * math.sqrt(0.5)))
        gelu = u * phi
        h = (gelu * w).astype(LOW)
        mixed[span, :] = (x1 + live * mul(h, w_down[...])).astype(LOW)
        target = mixed_ref.at[slot] if part == 0 else mixed_far_ref
        copies.append(put(mixed.at[span, :], target, out_sem.at[len(copies)]))
        cot = (cot_ref[slot] if part == 0 else cot_far_ref[...]).astype(FULL)
        dm = (live * cot).astype(LOW)
        dh = mul_t(dm, w_down[...])
        slope = phi + u * (jnp.exp(-0.5 * u * u) * (1.0 / math.sqrt(2.0 * math.pi)))
        duw_all[span, :units] = (dh * w * slope).astype(LOW)
        duw_all[span, units:] = (dh * gelu).astype(LOW)
        da2 = mul_t(duw_all[span, :], w_in[...])
        dx1 = cot + normalize_back(da2, gain, scaled, root)
        dx1_all[span, :] = dx1
        copies.append(put(dx1_all.at[span, :], dx1_ref.at[span, :], out_sem.at[len(copies)]))
        db = (live * dx1).astype(LOW)
        do_all[span, :] = mul_t(db, w_out[...]).astype(LOW)
        copies.append(put(do_all.at[span, :], do_ref.at[span, :], out_sem.at[len(copies)]))
        db_all[span, :] = db
        dm_all[span, :] = dm
        o_t[:, span] = jnp.transpose(o)
        a2_t[:, span] = jnp.transpose(a2)
        h_t[:, span] = jnp.transpose(h)
    dm, duw, db = dm_all[...], duw_all[...], db_all[...]
    for j, out, target in ((1, send, send_ref), (3, send, send_ref), (0, keep, keep_ref), (2, keep, keep_ref)):
        span = pl.ds(pl.multiple_of((place ^ j) * share, share), share)
        base = (place ^ j) * (share + short)
        down = pl.ds(pl.multiple_of(base, short), share)
        down_last = pl.ds(pl.multiple_of(base + share, short), short)
        at = 2 * units
        out[j // 2, :, :at] = mul(a2_t[span, :], duw).astype(LOW)
        out[j // 2, :, at : at + width] = mul(o_t[span, :], db).astype(LOW)
        at += width
        out[j // 2, :, at : at + width] = mul(h_t[down, :], dm).astype(LOW)
        at += width
        last = mul(h_t[down_last, :], dm).astype(LOW)
        out[j // 2, :short, at:] = last[:, : width // 2]
        out[j // 2, short:, at:] = last[:, width // 2 :]
        copies.append(put(out.at[j // 2], target.at[j // 2], out_sem.at[len(copies)]))
    wait_all(copies)


def send_kernel(count, at_ref, normed_ref, *refs):
    groups = [refs[i * count : (i + 1) * count] for i in range(3)]
    cos_ref, sin_ref, dqkv_ref, normed_t_ref, send_ref, dqkv, normed_t, send, sem = refs[3 * count :]
    width = normed_ref.shape[1]
    part_width = width // count
    normed_t[...] = jnp.transpose(normed_ref[...])
    copies = [put(normed_t, normed_t_ref, sem.at[0])]
    cos_part, sin_part = cos_ref[...], -sin_ref[...]
    for part, (dq, own, got) in enumerate(zip(*groups)):
        base = part * part_width
        dqkv[:, pl.ds(base, part_width)] = dq[...]
        dqkv[:, pl.ds(2 * width + base, part_width)] = (
            own[1].astype(FULL) + got[1].astype(FULL)
        ).astype(LOW)
        for pair in range(part_width // PAIR):
            lanes = pl.ds(pair * PAIR, PAIR)
            raw = own[0, :, lanes].astype(FULL) + got[0, :, lanes].astype(FULL)
            dqkv[:, pl.ds(width + base + pair * PAIR, PAIR)] = turn(raw, cos_part, sin_part).astype(
                LOW
            )
    copies.append(put(dqkv, dqkv_ref, sem.at[1]))
    right = dqkv[...]
    share = send.shape[1]
    for j in (1, 3):
        start = pl.multiple_of((at_ref[0] ^ j) * share, share)
        send[j // 2] = mul(normed_t[pl.ds(start, share), :], right).astype(LOW)
        copies.append(put(send.at[j // 2], send_ref.at[j // 2], sem.at[len(copies)]))
    wait_all(copies)


def keep_kernel(at_ref, normed_t_ref, dqkv_ref, keep_ref, keep, sem):
    right = dqkv_ref[...]
    share = keep.shape[1]
    copies = []
    for j in (0, 2):
        start = pl.multiple_of((at_ref[0] ^ j) * share, share)
        keep[j // 2] = mul(normed_t_ref[pl.ds(start, share), :], right).astype(LOW)
        copies.append(put(keep.at[j // 2], keep_ref.at[j // 2], sem.at[len(copies)]))
    wait_all(copies)


def input_kernel(at_ref, tokens_ref, far_ref, gain_ref, dx1_ref, dqkv_ref, w0, w1, w2, w3, w4, w5,
                 grad_ref, grad_far_ref, weight, grad_own, sem, out_sem):
    wait_all(load_blocks(at_ref, (w0, w1, w2, w3, w4, w5), weight, sem))
    rows = far_ref.shape[0]
    gain = gain_ref[...]
    for part in (1, 0):
        span = pl.ds(part * rows, rows)
        values = tokens_ref[at_ref[2]] if part == 0 else far_ref[...]
        scaled, root = normalize(values.astype(FULL))
        back = normalize_back(mul_t(dqkv_ref[span, :], weight[...]), gain, scaled, root)
        grad = dx1_ref[span, :] + back
        if part == 1:
            grad_far_ref[...] = grad.astype(LOW)
        else:
            grad_own[...] = grad
    put(grad_own, grad_ref.at[at_ref[2]], out_sem.at[0]).wait()


def shaped(*shape, kind=LOW):
    return jax.ShapeDtypeStruct(shape, kind)


IN_SMEM = pl.BlockSpec(memory_space=pltpu.SMEM)
IN_VMEM = pl.BlockSpec(memory_space=pltpu.VMEM)
IN_ANY = pl.BlockSpec(memory_space=pl.ANY)


def params(mebibytes):
    return pltpu.CompilerParams(vmem_limit_bytes=int(mebibytes * 1024 * 1024))


def call(kernel, args, in_specs, late=(), **options):
    count, skip = len(args), len(late)

    def body(*refs):
        return kernel(*refs[:count], *refs[count + skip :])

    return pl.pallas_call(body, in_specs=list(in_specs) + [IN_ANY] * skip, **options)(*args, *late)


def gate(values, late):
    return call(
        lambda *refs: None,
        values,
        late=late,
        out_shape=tuple(jax.ShapeDtypeStruct(v.shape, v.dtype) for v in values),
        in_specs=[IN_ANY] * len(values),
        out_specs=(IN_ANY,) * len(values),
        input_output_aliases={i: i for i in range(len(values))},
        compiler_params=params(1),
        name="gate",
    )


def prepare_first(at, weight):
    rows, width = weight.shape
    return call(
        prepare_first_kernel,
        (at, weight),
        out_shape=(shaped(rows, width), shaped(rows // 2, width)),
        in_specs=[IN_SMEM, IN_VMEM],
        out_specs=(IN_VMEM,) * 2,
        compiler_params=params(8),
        name="prepare_first",
    )


def prepare_rest(at, w_in, w_out, w_down, cotangent):
    rows, width = w_out.shape
    folded = 2 * width + width // 2
    return call(
        prepare_rest_kernel,
        (at, w_in, w_out, w_down, cotangent),
        out_shape=(
            shaped(*w_in.shape),
            shaped(rows // 2, w_in.shape[1]),
            shaped(rows, folded),
            shaped(rows // 2, folded),
            shaped(*cotangent.shape[1:]),
        ),
        in_specs=[IN_SMEM] + [IN_VMEM] * 4,
        out_specs=(IN_VMEM,) * 5,
        compiler_params=params(12),
        name="prepare_rest",
    )


def project(at, tokens, far, gain, cos_part, sin_part, blocks, late):
    rows, width = 2 * far.shape[0], far.shape[1]
    return call(
        project_kernel,
        (at, tokens, far, gain, cos_part, sin_part, *blocks),
        late=late,
        out_shape=(shaped(rows, width), shaped(rows, width), shaped(2, rows, width)),
        in_specs=[IN_SMEM] + [IN_VMEM] * 5 + [IN_ANY] * 6,
        out_specs=(IN_VMEM,) * 3,
        scratch_shapes=[pltpu.VMEM((width, 3 * width), LOW), pltpu.SemaphoreType.DMA((6,))],
        compiler_params=params(16),
        name="project",
    )


def attend(first, count, query, near, far, mark_query, mark_key, late=()):
    rows = query.shape[0]
    row_spec = pl.BlockSpec((rows, PAIR), lambda i: (0, i + first))
    kv_spec = pl.BlockSpec((2, rows, PAIR), lambda i: (0, 0, i + first))
    out_spec = pl.BlockSpec((rows, PAIR), lambda i: (0, i))
    return call(
        attend_kernel,
        (query, near, far, mark_query, mark_key),
        late=late,
        grid=(count,),
        out_shape=(shaped(rows, count * PAIR), shaped(rows, count * PAIR)),
        in_specs=[
            row_spec,
            kv_spec,
            kv_spec,
            pl.BlockSpec((rows, PAIR), lambda i: (0, 0)),
            pl.BlockSpec((2 * rows, PAIR), lambda i: (0, 0)),
        ],
        out_specs=(out_spec, out_spec),
        compiler_params=params(16),
        name="attend",
    )


def attend_back(
    first, first_o, count, query, near, far, extra, o, mark_key, do, cos_part, sin_part, late=()
):
    rows = query.shape[0]
    row_spec = pl.BlockSpec((rows, PAIR), lambda i: (0, i + first))
    o_spec = pl.BlockSpec((rows, PAIR), lambda i: (0, i + first_o))
    kv_spec = pl.BlockSpec((2, rows, PAIR), lambda i: (0, 0, i + first))
    fixed = pl.BlockSpec((rows, PAIR), lambda i: (0, 0))
    out_row = pl.BlockSpec((rows, PAIR), lambda i: (0, i))
    out_kv = pl.BlockSpec((2, rows, PAIR), lambda i: (0, 0, i))
    return call(
        attend_back_kernel,
        (query, near, far, extra, mark_key, o, do, cos_part, sin_part),
        late=late,
        grid=(count,),
        out_shape=(
            shaped(rows, count * PAIR),
            shaped(2, rows, count * PAIR),
            shaped(2, rows, count * PAIR),
        ),
        in_specs=[
            row_spec,
            kv_spec,
            kv_spec,
            o_spec,
            pl.BlockSpec((2 * rows, PAIR), lambda i: (0, 0)),
            o_spec,
            row_spec,
            fixed,
            fixed,
        ],
        out_specs=(out_row, out_kv, out_kv),
        compiler_params=params(20),
        name="attend_back",
    )


def middle(at, live, tokens, far, cot, cot_far, o_a, o_b, gain, blocks_in, blocks_od):
    half, width = far.shape
    rows, share = 2 * half, width // 4
    units = blocks_in[0].shape[1] // 2
    total = 2 * units + blocks_od[0].shape[1]
    assert units == 4 * (share + share // 2)
    low = lambda *shape: pltpu.VMEM(shape, LOW)
    return call(
        middle_kernel,
        (at, live, tokens, far, cot, cot_far, o_a, o_b, gain, *blocks_in, *blocks_od),
        out_shape=(
            shaped(2, half, width),
            shaped(half, width),
            shaped(rows, width, kind=FULL),
            shaped(rows, width),
            shaped(2, share, total),
            shaped(2, share, total),
        ),
        in_specs=[IN_SMEM] * 2 + [IN_VMEM] * 7 + [IN_ANY] * 12,
        out_specs=(IN_ANY,) * 6,
        scratch_shapes=[
            low(width, width),
            low(width, 2 * units),
            low(units, width),
            low(rows, width),
            low(width, rows),
            low(width, rows),
            low(units, rows),
            low(rows, width),
            low(rows, 2 * units),
            low(rows, width),
            low(rows, width),
            pltpu.VMEM((rows, width), FULL),
            low(rows, width),
            low(2, share, total),
            low(2, share, total),
            pltpu.SemaphoreType.DMA((6,)),
            pltpu.SemaphoreType.DMA((20,)),
            pltpu.SemaphoreType.DMA((10,)),
        ],
        compiler_params=params(40),
        name="middle",
    )


def qkv_send(at, normed, dq, own, got, cos_part, sin_part, late):
    rows, width = normed.shape
    share = width // 4
    return call(
        functools.partial(send_kernel, len(dq)),
        (at, normed, *dq, *own, *got, cos_part, sin_part),
        late=late,
        out_shape=(
            shaped(rows, 3 * width),
            shaped(width, rows),
            shaped(2, share, 3 * width),
        ),
        in_specs=[IN_SMEM] + [IN_VMEM] * (3 + 3 * len(dq)),
        out_specs=(IN_ANY,) * 3,
        scratch_shapes=[
            pltpu.VMEM((rows, 3 * width), LOW),
            pltpu.VMEM((width, rows), LOW),
            pltpu.VMEM((2, share, 3 * width), LOW),
            pltpu.SemaphoreType.DMA((4,)),
        ],
        compiler_params=params(20),
        name="qkv_send",
    )


def qkv_keep(at, normed_t, dqkv, late):
    width, rows = normed_t.shape
    share = width // 4
    return call(
        keep_kernel,
        (at, normed_t, dqkv),
        late=late,
        out_shape=shaped(2, share, 3 * width),
        in_specs=[IN_SMEM] + [IN_VMEM] * 2,
        out_specs=IN_ANY,
        scratch_shapes=[
            pltpu.VMEM((2, share, 3 * width), LOW),
            pltpu.SemaphoreType.DMA((2,)),
        ],
        compiler_params=params(16),
        name="qkv_keep",
    )


def input_back(at, tokens, far, gain, dx1, dqkv, blocks, late):
    half, width = far.shape
    return call(
        input_kernel,
        (at, tokens, far, gain, dx1, dqkv, *blocks),
        late=late,
        out_shape=(shaped(2, half, width, kind=FULL), shaped(half, width)),
        in_specs=[IN_SMEM] + [IN_VMEM] * 5 + [IN_ANY] * 6,
        out_specs=(IN_ANY, IN_VMEM),
        scratch_shapes=[
            pltpu.VMEM((width, 3 * width), LOW),
            pltpu.VMEM((half, width), FULL),
            pltpu.SemaphoreType.DMA((6,)),
            pltpu.SemaphoreType.DMA((1,)),
        ],
        compiler_params=params(20),
        name="input_back",
    )


def first_sums_kernel(at_ref, keep, got, own_a, far_a, mine_b, give_b):
    cut, short = far_a.shape[0], give_b.shape[1]

    def add(block, start, size):
        span = pl.ds(start, size)
        return (keep[block, span, :].astype(FULL) + got[block, span, :].astype(FULL)).astype(LOW)

    far_a[...] = add(1, 0, cut)
    for block in range(2):
        give_b[block] = add(block, pl.multiple_of(cut + (1 - at_ref[1]) * short, short), short)
        mine_b[block] = add(block, pl.multiple_of(cut + at_ref[1] * short, short), short)
    own_a[...] = add(0, 0, cut)


def first_sums(at, keep, got, late=()):
    _, rows, width = keep.shape
    cut, short = rows // 2, rows // 4
    return call(
        first_sums_kernel,
        (at, keep, got),
        late=late,
        out_shape=(shaped(cut, width),) * 2 + (shaped(2, short, width),) * 2,
        in_specs=[IN_SMEM] + [IN_VMEM] * 2,
        out_specs=(IN_VMEM,) * 4,
        compiler_params=params(20),
        name="first_sums",
    )


def second_sums_kernel(at_ref, own_a, got_a, mine_b, got_b, mine_a, give_a, near_b, far_b):
    short = mine_a.shape[0]
    for start, out in ((1 - at_ref[1], give_a), (at_ref[1], mine_a)):
        span = pl.ds(pl.multiple_of(start * short, short), short)
        out[...] = (own_a[span, :].astype(FULL) + got_a[span, :].astype(FULL)).astype(LOW)
    for block, out in ((1, far_b), (0, near_b)):
        out[...] = (mine_b[block].astype(FULL) + got_b[block].astype(FULL)).astype(LOW)


def second_sums(at, own_a, got_a, mine_b, got_b, late=()):
    _, short, width = mine_b.shape
    return call(
        second_sums_kernel,
        (at, own_a, got_a, mine_b, got_b),
        late=late,
        out_shape=(shaped(short, width),) * 4,
        in_specs=[IN_SMEM] + [IN_VMEM] * 4,
        out_specs=(IN_VMEM,) * 4,
        compiler_params=params(12),
        name="second_sums",
    )


def third_sums_kernel(lanes, mine_a, got_a, near_b, got_b, *outs):
    upper = mine_a[...].astype(FULL) + got_a[...].astype(FULL)
    lower = near_b[...].astype(FULL) + got_b[...].astype(FULL)
    total = jnp.concatenate([upper, lower])
    first = 0
    for out, width in zip(outs, lanes):
        count, rows, _ = out.shape
        for i in range(count):
            out[i] = total[i * rows : (i + 1) * rows, first : first + width].astype(LOW)
        first += width


def third_sums(count, lanes, mine_a, got_a, near_b, got_b, late=()):
    rows = 2 * mine_a.shape[0] // count
    return call(
        functools.partial(third_sums_kernel, lanes),
        (mine_a, got_a, near_b, got_b),
        late=late,
        out_shape=tuple(shaped(count, rows, width) for width in lanes),
        in_specs=[IN_VMEM] * 4,
        out_specs=(IN_VMEM,) * len(lanes),
        compiler_params=params(12),
        name="third_sums",
    )


def squares_kernel(*refs):
    (qkv, w_qkv, gain_qkv, inner, w_in, gain_in, folded), out = refs[:-1], refs[-1]
    total = jnp.sum(jnp.square(folded[...].astype(FULL)), keepdims=True)
    for piece, weight, gain in ((qkv, w_qkv, gain_qkv), (inner, w_in, gain_in)):
        values = piece[...].astype(FULL)
        rows = jnp.sum(weight[...].astype(LOW).astype(FULL) * values, axis=1, keepdims=True)
        total += jnp.sum(jnp.square(values), keepdims=True)
        total += jnp.sum(jnp.square(rows / gain[...]), keepdims=True)
    out[...] = jnp.broadcast_to(total, out.shape)


def squares(*args):
    return call(
        squares_kernel,
        args,
        out_shape=shaped(8, 128, kind=FULL),
        in_specs=[IN_VMEM] * len(args),
        out_specs=IN_VMEM,
        compiler_params=params(6),
        name="squares",
    )


def adam_kernel(rates, at_ref, square_ref, w_ref, m_ref, v_ref, mine_ref, other_ref,
                w_out, m_out, v_out, row_out):
    own = (pl.program_id(0) & 1) == at_ref[1]
    gradient = jnp.where(own, mine_ref[...].astype(FULL), other_ref[...].astype(FULL))
    weight = w_ref[...]
    rows = jnp.sum(weight.astype(LOW).astype(FULL) * gradient, axis=1, keepdims=True)
    row_out[...] = jnp.broadcast_to(rows, row_out.shape)
    norm = jnp.sqrt(square_ref[:1, :1])
    factor = jnp.minimum(1.0, CLIP_LIMIT / (norm + 1e-06))
    w_out[...], m_out[...], v_out[...] = adam_step(
        weight, m_ref[...], v_ref[...], gradient, factor, *rates
    )


def adam(at, square, weight, first, second, mine, other, rates):
    rows, width = weight.shape
    quarter = rows // 4
    block = pl.BlockSpec((quarter, width), lambda i: (i, 0))
    part = pl.BlockSpec((quarter, width), lambda i: (i // 2, 0))
    return call(
        functools.partial(adam_kernel, rates),
        (at, square, weight, first, second, mine, other),
        grid=(4,),
        out_shape=(shaped(rows, width, kind=FULL),) * 3 + (shaped(rows, PAIR, kind=FULL),),
        in_specs=[IN_SMEM, pl.BlockSpec((8, 128), lambda i: (0, 0))] + [block] * 3 + [part] * 2,
        out_specs=(block,) * 3 + (pl.BlockSpec((quarter, PAIR), lambda i: (i, 0)),),
        compiler_params=params(16),
        name="adam",
    )


def low_sum(*values):
    return sum(value.astype(FULL) for value in values).astype(LOW)


def index(value, i):
    return lax.dynamic_index_in_dim(value, i, 0, keepdims=False)


def make(dp_count, seq_count):
    assert seq_count == 4 and dp_count % 4 == 0 and dp_count & (dp_count - 1) == 0
    bits = dp_count.bit_length() - 1
    ones = [(shift, 1) for shift in range(1, bits)]
    twos = [(shift, min(2, bits - shift)) for shift in range(1, bits, 2)]
    count = dp_count // 2

    def trade(value, axis, bit):
        size = seq_count if axis == "seq" else dp_count
        return lax.ppermute(value, axis, [(i, i ^ bit) for i in range(size)])

    def fields(group, steps):
        for shift, width in steps:
            yield shift, 1 << width, (group >> shift) & ((1 << width) - 1)

    def sum_steps(value, group, steps, lates=()):
        for i, (shift, size, mine) in enumerate(fields(group, steps)):
            parts = value.reshape((size, value.shape[0] // size) + value.shape[1:])
            got = [trade(index(parts, mine ^ k), "dp", k << shift) for k in range(1, size)]
            if i < len(lates) and lates[i]:
                got = gate(got, lates[i])
            value = low_sum(index(parts, mine), *got)
        return value[0]

    def pick_steps(value, group, steps):
        for _, size, mine in fields(group, steps):
            value = index(value.reshape((size, value.shape[0] // size) + value.shape[1:]), mine)
        return value[0]

    def join_steps(piece, group, steps, lates=()):
        value, came = piece[None], []
        for i, (shift, size, mine) in enumerate(list(fields(group, steps))[::-1]):
            got = [trade(value, "dp", k << shift) for k in range(1, size)]
            came.append(got)
            if i < len(lates) and lates[i]:
                got = gate(got, lates[i])
            stack = jnp.stack([value, *got])
            value = jnp.concatenate([index(stack, mine ^ k) for k in range(size)])
        return value, came

    def on_device(
        tokens, cotangent, segments, valid,
        w_qkv, w_out, w_in, w_down, gains,
        m_qkv, m_out, m_in, m_down, m_gains,
        v_qkv, v_out, v_in, v_down, v_gains,
    ):
        place = lax.axis_index("seq")
        group = lax.axis_index("dp")
        slot = place >> 1
        half = group & 1
        local_len, width = tokens.shape[1:]
        rows = 2 * local_len
        share = w_qkv.shape[0]
        at = jnp.stack([place, half, slot])

        low_qkv, half_qkv = prepare_first(at, w_qkv)
        far_qa = trade(half_qkv, "seq", 2)
        near_q = trade(low_qkv, "seq", 1)
        low_in, half_in, low_od, half_od, their_cot = prepare_rest(
            at, w_in, w_out, w_down, cotangent
        )
        low_gains = gains.astype(LOW)
        (their_tokens,) = gate((index(tokens, 1 - slot),), (far_qa,))
        far = trade(their_tokens, "seq", 2)
        gain_far = trade(low_gains, "seq", 2)
        far_qb = trade(far_qa, "dp", 1)
        near_qa = trade(far_qa, "seq", 1)
        near_qb = trade(far_qb, "seq", 1)
        gain_near = trade(jnp.stack([low_gains, gain_far]), "seq", 1)
        gain_stack = jnp.stack([low_gains, gain_near[0], gain_far, gain_near[1]])
        gain_low = jnp.concatenate(
            [index(gain_stack, b ^ place) for b in range(4)], axis=1
        ).astype(FULL)
        blocks_qkv = (low_qkv, near_q, far_qa, far_qb, near_qa, near_qb)
        near_i = trade(low_in, "seq", 1)
        near_o = trade(low_od, "seq", 1)
        (half_in,) = gate((half_in,), (near_qa,))
        far_ia = trade(half_in, "seq", 2)

        seg = index(segments, slot)
        positions = doc_positions(seg).reshape(4, local_len)
        seg = seg.reshape(4, local_len)
        chunks = [place, place ^ 2, place ^ 1, place ^ 3]
        seg_keys = jnp.concatenate([index(seg, c) for c in chunks])
        pos = jnp.concatenate([index(positions, c) for c in chunks[:2]])
        cos_part, sin_part = rope_tables(pos)
        lane = jnp.arange(PAIR, dtype=jnp.int32)[None] % HEAD_DIM
        same = seg_keys[:, None] == lane
        mark_key = jnp.where(lane < DOCS, 1.0 - same, (lane < DOCS + 3) * 1.0).astype(LOW)
        mark_query = jnp.where((lane < DOCS) & same[:rows], NEG_FILL, 0.0).astype(LOW)
        live = lax.dynamic_index_in_dim(valid, slot, 0, keepdims=True).astype(FULL)

        normed, query, kv = project(
            at, tokens, far, gain_low[:1], cos_part, sin_part, blocks_qkv,
            (far_ia, near_i, near_o, mark_key, mark_query),
        )
        kv_far = trade(kv, "seq", 1)
        far_oa = trade(half_od, "seq", 2)
        far_ib = trade(far_ia, "dp", 1)
        near_ia = trade(far_ia, "seq", 1)
        cot_far = trade(their_cot, "seq", 2)
        pairs = width // PAIR
        early = 2
        args = (query, kv, kv_far, mark_query, mark_key)
        o_a, extra_a = attend(0, early, *args)
        far_oa, far_ib = gate((far_oa, far_ib), (o_a,))
        far_ob = trade(far_oa, "dp", 1)
        near_oa = trade(far_oa, "seq", 1)
        near_ib = trade(far_ib, "seq", 1)
        o_b, extra_b = attend(early, pairs - early, *args, late=(o_a, far_oa, near_ia))
        (far_ob,) = gate((far_ob,), (o_b,))
        near_ob = trade(far_ob, "seq", 1)
        blocks_in = (low_in, near_i, far_ia, far_ib, near_ia, near_ib)
        blocks_od = (low_od, near_o, far_oa, far_ob, near_oa, near_ob)

        mixed, mixed_far, dx1, do, keep_rest, send_rest = middle(
            at, live, tokens, far, cotangent, cot_far, o_a, o_b, gain_low[1:], blocks_in, blocks_od
        )
        got_rest = trade(send_rest, "seq", 1)
        two = pairs // 3
        near_args = (query, kv, kv_far)
        back_args = (mark_key, do, cos_part, sin_part)
        dq0, own0, give0 = attend_back(0, 0, two, *near_args, extra_a, o_a, *back_args)
        r1 = first_sums(at, keep_rest, got_rest, late=(own0,))
        got_ra, got_rb = trade(r1[1], "seq", 2), trade(r1[3], "dp", 1)
        got0 = trade(give0, "seq", 1)
        dq1, own1, give1 = attend_back(
            two, two - early, two, *near_args, extra_b, o_b, *back_args, late=(r1[0],)
        )
        got1 = trade(give1, "seq", 1)
        dq2, own2, give2 = attend_back(
            2 * two, 2 * two - early, pairs - 2 * two, *near_args, extra_b, o_b, *back_args, late=(own1,)
        )
        got2 = trade(give2, "seq", 1)
        r2 = second_sums(at, r1[0], got_ra, r1[2], got_rb, late=(own2,))
        got_ra, got_rb = trade(r2[1], "dp", 1), trade(r2[3], "seq", 2)
        dqkv, normed_t, send_qkv = qkv_send(
            at, normed, (dq0, dq1, dq2), (own0, own1, own2), (got0, got1, got2),
            cos_part, sin_part, late=(r2[0],),
        )
        got_qkv = trade(send_qkv, "seq", 1)
        keep_qkv = qkv_keep(at, normed_t, dqkv, late=())
        q1 = first_sums(at, keep_qkv, got_qkv)
        got_qa, got_qb = trade(q1[1], "seq", 2), trade(q1[3], "dp", 1)
        inner_lanes = w_in.shape[1]
        lanes = (inner_lanes, keep_rest.shape[2] - inner_lanes)
        inner, folded = third_sums(count, lanes, r2[0], got_ra, r2[2], got_rb, late=(q1[0],))
        grad, grad_far = input_back(
            at, tokens, far, gain_low[:1], dx1, dqkv, blocks_qkv, late=(inner,)
        )
        q2 = second_sums(at, q1[0], got_qa, q1[2], got_qb, late=(grad_far,))
        got_qa, got_qb = trade(q2[1], "dp", 1), trade(q2[3], "seq", 2)
        (qkv,) = third_sums(count, (3 * width,), q2[0], got_qa, q2[2], got_qb)
        inner_piece = sum_steps(inner, group, ones, ((grad_far,), (qkv,)))
        folded_piece = sum_steps(folded, group, ones, ((grad_far,), (qkv,)))
        qkv_piece = sum_steps(qkv, group, twos)
        qkv_mine, came = join_steps(qkv_piece, group, twos)
        inner_mine, _ = join_steps(inner_piece, group, ones, ((came[0][0],), (qkv_mine,)))
        folded_mine, _ = join_steps(folded_piece, group, ones, ((came[0][0],), (qkv_mine,)))
        (mixed_far,) = gate((mixed_far,), (qkv,))
        mixed_far = trade(mixed_far, "seq", 2)
        (grad_far,) = gate((grad_far,), (qkv_piece,))
        grad_far = trade(grad_far, "seq", 2)

        w_rows, in_rows, gain_rows = gate(
            (w_qkv, w_in, jnp.transpose(gains.astype(LOW).astype(FULL))), (q2[0],)
        )

        def half_of(value):
            short = value.shape[0] // 4
            parts = index(jnp.swapaxes(value.reshape((2, 2, short) + value.shape[1:]), 0, 1), half)
            return parts.reshape((count, 2 * short // count) + value.shape[1:])

        square = squares(
            qkv_piece,
            pick_steps(half_of(w_rows), group, twos),
            pick_steps(half_of(gain_rows[:, :1]), group, twos),
            inner_piece,
            pick_steps(half_of(in_rows), group, ones),
            pick_steps(half_of(gain_rows[:, 1:]), group, ones),
            folded_piece,
        )
        (square,) = gate((square,), (came[0][0],))
        for bit in (2, 1):
            square = square + trade(square, "seq", bit)
        (square,) = gate((square,), (qkv_mine,))
        for bit in range(bits):
            square = square + trade(square, "dp", dp_count >> (bit + 1))
        grad_norm = jnp.sqrt(square[0, 0])
        factor = jnp.minimum(1.0, CLIP_LIMIT / (grad_norm + 1e-06))

        def both_halves(mine):
            mine = mine.reshape((-1,) + mine.shape[2:])
            return mine, trade(mine, "dp", 1)

        new_qkv, first_qkv, second_qkv, row_one = adam(
            at, square, w_qkv, m_qkv, v_qkv, *both_halves(qkv_mine), (STEP_RATES[0], DECAY_RATES[0])
        )
        new_in, first_in, second_in, row_two = adam(
            at, square, w_in, m_in, v_in, *both_halves(inner_mine), (STEP_RATES[2], DECAY_RATES[2])
        )
        mine, other = both_halves(folded_mine)
        short = share // 4
        lower = jnp.where(half == 0, mine, other)
        upper = jnp.where(half == 0, other, mine)
        folded_all = jnp.concatenate([lower[:short], upper[:short], lower[short:], upper[short:]])
        last = folded_all[:, 2 * width :]
        grad_down = jnp.concatenate(
            [
                folded_all[:, width : 2 * width],
                jnp.concatenate([last[: share // 2], last[share // 2 :]], axis=1),
            ]
        )
        gain_grads = jnp.stack([row_one[:, 0], row_two[:, 0]]) / gains.astype(LOW).astype(FULL)

        def step(weight, first, second, gradient, i):
            gradient = gradient.astype(FULL)
            return adam_step(
                weight, first, second, gradient, factor, STEP_RATES[i], DECAY_RATES[i]
            )

        new_out, first_out, second_out = step(w_out, m_out, v_out, folded_all[:, :width], 1)
        new_down, first_down, second_down = step(w_down, m_down, v_down, grad_down, 3)
        new_gains, first_gains, second_gains = step(gains, m_gains, v_gains, gain_grads, 4)

        def fill(whole, theirs):
            theirs = theirs.astype(whole.dtype)[None]
            return lax.dynamic_update_slice(whole, theirs, (1 - slot, 0, 0))

        return (
            fill(mixed, mixed_far),
            fill(grad, grad_far),
            grad_norm,
            new_qkv, new_out, new_in, new_down, new_gains,
            first_qkv, first_out, first_in, first_down, first_gains,
            second_qkv, second_out, second_in, second_down, second_gains,
        )

    return on_device


def solution(mesh):
    rows, matrix, gain = P("dp", "seq", None), P("seq", None), P(None, "seq")
    weights = (matrix,) * 4 + (gain,)
    return jax.shard_map(
        make(mesh.shape["dp"], mesh.shape["seq"]),
        mesh=mesh,
        in_specs=(rows, rows, P("dp", None), P("dp")) + weights * 3,
        out_specs=(rows, rows, P()) + weights * 3,
        check_vma=False,
    )
```

```python
import functools
import math

import jax
import jax.numpy as jnp
from jax import lax
from jax.experimental import pallas as pl
from jax.experimental.pallas import tpu as pltpu
from jax.sharding import PartitionSpec as P

HEADS = 12
HEAD_DIM = 64
PAIR = 2 * HEAD_DIM
STEP_COUNT = 10
EPS_NORM = 1e-05
ROPE_BASE = 160000.0
NEG_FILL = -1e30
CLIP_LIMIT = 10.0
BETA_FIRST = 0.9
BETA_SECOND = 0.98
EPS_ADAM = 1e-06
STEP_RATES = (0.1, 0.5, 0.1, 0.1, 1.0)
DECAY_RATES = (0.01, 0.01, 0.01, 0.01, 0.0)
DOCS = 5
LOW = jnp.bfloat16
FULL = jnp.float32
SCALE = 1.0 / math.sqrt(HEAD_DIM)
WEIGHT = 20_000_000_000


def doc_positions(segment_ids):
    seq_len = segment_ids.shape[-1]
    places = jnp.arange(seq_len, dtype=jnp.int32)
    first_mark = jnp.ones((1,), jnp.bool_)
    change = jnp.concatenate([first_mark, segment_ids[1:] != segment_ids[:-1]])
    starts = lax.cummax(jnp.where(change, places, 0), axis=0)
    return places - starts


def rope_tables(positions):
    half_dim = HEAD_DIM // 2
    exponents = jnp.arange(half_dim, dtype=jnp.float32) * (2.0 / HEAD_DIM)
    inv_freq = ROPE_BASE ** (-exponents)
    angles = positions.astype(jnp.float32)[:, None] * inv_freq
    cos_part, sin_part = jnp.cos(angles), jnp.sin(angles)
    return (
        jnp.concatenate([cos_part] * 4, axis=1),
        jnp.concatenate([-sin_part, sin_part] * 2, axis=1),
    )


def adam_step(weight, first_old, second_old, gradient, factor, step_rate, decay_rate):
    clipped = gradient * factor
    first_new = BETA_FIRST * first_old + (1.0 - BETA_FIRST) * clipped
    second_new = BETA_SECOND * second_old + (1.0 - BETA_SECOND) * clipped * clipped
    first_hat = first_new / (1.0 - BETA_FIRST**STEP_COUNT)
    second_hat = second_new / (1.0 - BETA_SECOND**STEP_COUNT)
    weight_new = weight * (1.0 - step_rate * decay_rate) - step_rate * first_hat / (
        jnp.sqrt(second_hat) + EPS_ADAM
    )
    return (weight_new, first_new, second_new)


def mul(left, right):
    return lax.dot_general(left, right, (((1,), (0,)), ((), ())), preferred_element_type=FULL)


def mul_t(left, right):
    return lax.dot_general(left, right, (((1,), (1,)), ((), ())), preferred_element_type=FULL)


def normalize(values):
    centered = values - jnp.mean(values, axis=-1, keepdims=True)
    root = lax.rsqrt(jnp.mean(centered * centered, axis=-1, keepdims=True) + EPS_NORM)
    return centered * root, root


def normalize_back(grad, gain, scaled, root):
    t = grad * gain
    back = root * (
        t
        - jnp.mean(t, axis=-1, keepdims=True)
        - scaled * jnp.mean(t * scaled, axis=-1, keepdims=True)
    )
    return back


def turn(values, cos_part, sin_part):
    lane = lax.broadcasted_iota(jnp.int32, values.shape, 1)
    swapped = jnp.where(
        lane % HEAD_DIM < HEAD_DIM // 2,
        pltpu.roll(values, PAIR - HEAD_DIM // 2, 1),
        pltpu.roll(values, HEAD_DIM // 2, 1),
    )
    return values * cos_part + swapped * sin_part


def three_parts(values):
    high = values.astype(LOW).astype(FULL)
    rest = values - high
    mid = rest.astype(LOW).astype(FULL)
    return high, mid, rest - mid


def wait_all(copies):
    for copy in copies:
        copy.wait()


def put(source, target, sem):
    copy = pltpu.make_async_copy(source, target, sem)
    copy.start()
    return copy


PIECES = ((0, None), (1, None), (2, 0), (2, 1), (3, 0), (3, 1))


def load_blocks(at_ref, blocks, whole, sem):
    rows = blocks[0].shape[0]
    copies = []
    for i, (bits, part) in enumerate(PIECES):
        start = (at_ref[0] ^ bits) * rows
        size = rows
        if part is not None:
            size = rows // 2
            start += (at_ref[1] ^ part) * size
        target = whole.at[pl.ds(pl.multiple_of(start, size), size), :]
        copies.append(put(blocks[i], target, sem.at[i]))
    return copies


def load_folded(at_ref, blocks, w_out, w_down, sem):
    rows, width = blocks[0].shape[0], w_out.shape[1]
    short, last = rows // 2, width // 2
    copies = []

    def copy(source, target):
        copies.append(put(source, target, sem.at[len(copies)]))

    for i, (bits, part) in enumerate(PIECES):
        owner = at_ref[0] ^ bits
        base = owner * (rows + short)
        first = 0 if part is None else (at_ref[1] ^ part) * short
        size = rows if part is None else short
        for lanes, whole, start in ((0, w_out, owner * rows), (width, w_down, base)):
            span = pl.ds(pl.multiple_of(start + first, short), size)
            copy(blocks[i].at[:, pl.ds(lanes, width)], whole.at[span, :])
        span = pl.ds(pl.multiple_of(base + rows, short), short)
        if part is None:
            for fold in range(2):
                copy(
                    blocks[i].at[pl.ds(fold * short, short), pl.ds(2 * width, last)],
                    w_down.at[span, pl.ds(fold * last, last)],
                )
        else:
            lanes = pl.ds(pl.multiple_of((at_ref[1] ^ part) * last, last), last)
            copy(blocks[i].at[:, pl.ds(2 * width, last)], w_down.at[span, lanes])
    return copies


def fold(out, w_out, w_down, first):
    rows, width = w_out.shape
    short, last = rows // 2, width // 2
    out[:, first : first + width] = w_out[...].astype(LOW)
    out[:, first + width : first + 2 * width] = w_down[:rows, :].astype(LOW)
    for i in range(2):
        out[i * short : (i + 1) * short, first + 2 * width :] = w_down[
            rows:, i * last : (i + 1) * last
        ].astype(LOW)


def prepare_first_kernel(at_ref, w_ref, low_ref, half_ref):
    short = half_ref.shape[0]
    half_ref[...] = w_ref[pl.ds(pl.multiple_of(at_ref[1] * short, short), short), :].astype(LOW)
    low_ref[...] = w_ref[...].astype(LOW)


def prepare_rest_kernel(at_ref, in_ref, out_ref, down_ref, cot_ref, tokens_ref,
                        low_in, half_in, low_od, half_od, their_cot, their_tokens):
    their_tokens[...] = tokens_ref[1 - at_ref[2]]
    short = half_in.shape[0]
    span = pl.ds(pl.multiple_of(at_ref[1] * short, short), short)
    low_in[...] = in_ref[...].astype(LOW)
    half_in[...] = in_ref[span, :].astype(LOW)
    fold(low_od, out_ref, down_ref, 0)
    half_od[...] = low_od[span, :]
    their_cot[...] = cot_ref[1 - at_ref[2]]


def project_kernel(at_ref, tokens_ref, far_ref, gain_ref, cos_ref, sin_ref, w0, w1, w2, w3, w4, w5,
                   normed_ref, query_ref, kv_ref, weight, sem):
    copies = load_blocks(at_ref, (w0, w1, w2, w3, w4, w5), weight, sem)
    rows, width = far_ref.shape
    for part in range(2):
        values = tokens_ref[at_ref[2]] if part == 0 else far_ref[...]
        scaled, _ = normalize(values.astype(FULL))
        normed_ref[pl.ds(part * rows, rows), :] = (scaled * gain_ref[...]).astype(LOW)
    wait_all(copies)
    for part in range(2):
        span = pl.ds(part * rows, rows)
        normed = normed_ref[span, :]
        cos_part, sin_part = cos_ref[span, :], sin_ref[span, :]
        for pair in range(2 * width // PAIR):
            lanes = pl.ds(pair * PAIR, PAIR)
            if pair % 2 == 0:
                both = mul(normed, weight[:, pl.ds(pair * PAIR, 2 * PAIR)])
            raw = both[:, (pair % 2) * PAIR : (pair % 2 + 1) * PAIR]
            turned = turn(raw, cos_part, sin_part)
            if pair < width // PAIR:
                query_ref[span, lanes] = (turned * SCALE).astype(LOW)
            else:
                kv_ref[0, span, pl.ds(pair * PAIR - width, PAIR)] = turned.astype(LOW)
        kv_ref[1, span, :] = mul(normed, weight[:, 2 * width :]).astype(LOW)


def head_lanes(head, shape):
    lane = lax.broadcasted_iota(jnp.int32, shape, 1)
    return (lane < HEAD_DIM) if head == 0 else (lane >= HEAD_DIM)


def pick(head, inside, outside):
    return jnp.where(head_lanes(head, inside.shape), inside, outside)


def attend_kernel(query_ref, near_ref, far_ref, mark_query_ref, mark_key_ref, o_ref, extra_ref):
    rows = query_ref.shape[0]
    query = query_ref[...]
    mark_query = mark_query_ref[...]
    parts = [
        (near_ref[0], jnp.transpose(near_ref[1]), mark_key_ref[:rows, :]),
        (far_ref[0], jnp.transpose(far_ref[1]), mark_key_ref[rows:, :]),
    ]
    outs, logs = [], []
    for head in range(2):
        query_head = pick(head, query, mark_query)
        scores = [mul_t(pick(head, key, mark), query_head) for key, _, mark in parts]
        top = jnp.maximum(
            jnp.max(scores[0], axis=0, keepdims=True), jnp.max(scores[1], axis=0, keepdims=True)
        )
        exps = [jnp.exp(score - top) for score in scores]
        total = jnp.sum(exps[0], axis=0, keepdims=True) + jnp.sum(exps[1], axis=0, keepdims=True)
        span = slice(head * HEAD_DIM, (head + 1) * HEAD_DIM)
        out = sum(mul(value_t[span], e.astype(LOW)) for (_, value_t, _), e in zip(parts, exps))
        outs.append(out / total)
        logs.append(top + jnp.log(total))
    o_ref[...] = jnp.transpose(jnp.concatenate(outs)).astype(LOW)
    line = lax.broadcasted_iota(jnp.int32, (PAIR, rows), 0)
    extra = jnp.zeros((PAIR, rows), FULL)
    for head in range(2):
        base = DOCS + (HEAD_DIM if head == 0 else 0)
        for i, piece in enumerate(three_parts(-logs[head])):
            extra = jnp.where(line == base + i, piece, extra)
    extra_ref[...] = jnp.transpose(extra).astype(LOW) + mark_query


def attend_back_kernel(query_ref, near_ref, far_ref, extra_ref, mark_key_ref, o_ref, do_ref,
                       cos_ref, sin_ref, dq_ref, keep_ref, send_ref):
    rows = query_ref.shape[0]
    query, extra, do = query_ref[...], extra_ref[...], do_ref[...]
    inner_all = do.astype(FULL) * o_ref[...].astype(FULL)
    lane = lax.broadcasted_iota(jnp.int32, (rows, PAIR), 1)
    zero = jnp.zeros((rows, PAIR), LOW)
    grads_query = []
    sums = [[None, None], [None, None]]
    keys_t = [jnp.transpose(near_ref[0]), jnp.transpose(far_ref[0])]
    for head in range(2):
        inside = head_lanes(head, (rows, PAIR))
        inner = jnp.sum(jnp.where(inside, inner_all, 0.0), axis=1, keepdims=True)
        base = DOCS + (HEAD_DIM if head == 0 else 0)
        tail = jnp.zeros((rows, PAIR), FULL)
        for i, piece in enumerate(three_parts(-inner)):
            tail = jnp.where(lane == base + i, piece, tail)
        query_head = pick(head, query, extra)
        do_head = pick(head, do, tail.astype(LOW))
        query_only = pick(head, query, zero)
        do_only = pick(head, do, zero)
        span = slice(head * HEAD_DIM, (head + 1) * HEAD_DIM)
        grad_query = 0.0
        for part, ref in enumerate((near_ref, far_ref)):
            mark = mark_key_ref[pl.ds(part * rows, rows), :]
            probs = jnp.exp(mul_t(pick(head, ref[0], mark), query_head))
            grad_probs = mul_t(pick(head, ref[1], mark), do_head)
            grad_scores = (probs * grad_probs).astype(LOW)
            grad_value = mul(probs.astype(LOW), do_only)
            grad_key = mul(grad_scores, query_only)
            grad_query += mul(keys_t[part][span], grad_scores)
            if head == 0:
                sums[part] = [grad_key, grad_value]
            else:
                sums[part] = [sums[part][0] + grad_key, sums[part][1] + grad_value]
        grads_query.append(grad_query)
    turned = turn(
        jnp.transpose(jnp.concatenate(grads_query)) * SCALE, cos_ref[...], -sin_ref[...]
    )
    dq_ref[...] = turned.astype(LOW)
    for i in range(2):
        keep_ref[i] = sums[0][i].astype(LOW)
        send_ref[i] = sums[1][i].astype(LOW)


def middle_kernel(at_ref, live_ref, tokens_ref, far_ref, cot_ref, cot_far_ref, oa_ref, ob_ref,
                  gain_ref, i0, i1, i2, i3, i4, i5, d0, d1, d2, d3, d4, d5,
                  mixed_ref, mixed_far_ref, dx1_ref, do_ref, keep_ref, send_ref,
                  w_out, w_in, w_down, o_all, o_t, a2_t, h_t, dm_all, duw_all, db_all,
                  mixed, dx1_all, do_all, keep, send, sem, fold_sem, out_sem):
    place, slot, live = at_ref[0], at_ref[2], live_ref[0]
    copies_down = load_folded(at_ref, (d0, d1, d2, d3, d4, d5), w_out, w_down, fold_sem)
    copies_in = load_blocks(at_ref, (i0, i1, i2, i3, i4, i5), w_in, sem)
    rows, width = far_ref.shape
    share = width // 4
    short, units = share // 2, w_down.shape[0]
    gain = gain_ref[...]
    o_all[:, : oa_ref.shape[1]] = oa_ref[...]
    o_all[:, oa_ref.shape[1] :] = ob_ref[...]
    copies = []
    for part in range(2):
        span = pl.ds(part * rows, rows)
        o = o_all[span, :]
        values = tokens_ref[slot] if part == 0 else far_ref[...]
        if part == 0:
            wait_all(copies_down)
        x1 = values.astype(FULL) + live * mul(o, w_out[...])
        scaled, root = normalize(x1)
        a2 = (scaled * gain).astype(LOW)
        if part == 0:
            wait_all(copies_in)
        u = mul(a2, w_in[:, :units])
        w = mul(a2, w_in[:, units:])
        phi = 0.5 * (1.0 + lax.erf(u * math.sqrt(0.5)))
        gelu = u * phi
        h = (gelu * w).astype(LOW)
        mixed[span, :] = (x1 + live * mul(h, w_down[...])).astype(LOW)
        target = mixed_ref.at[slot] if part == 0 else mixed_far_ref
        copies.append(put(mixed.at[span, :], target, out_sem.at[len(copies)]))
        cot = (cot_ref[slot] if part == 0 else cot_far_ref[...]).astype(FULL)
        dm = (live * cot).astype(LOW)
        dh = mul_t(dm, w_down[...])
        slope = phi + u * (jnp.exp(-0.5 * u * u) * (1.0 / math.sqrt(2.0 * math.pi)))
        duw_all[span, :units] = (dh * w * slope).astype(LOW)
        duw_all[span, units:] = (dh * gelu).astype(LOW)
        da2 = mul_t(duw_all[span, :], w_in[...])
        dx1 = cot + normalize_back(da2, gain, scaled, root)
        dx1_all[span, :] = dx1
        copies.append(put(dx1_all.at[span, :], dx1_ref.at[span, :], out_sem.at[len(copies)]))
        db = (live * dx1).astype(LOW)
        do_all[span, :] = mul_t(db, w_out[...]).astype(LOW)
        copies.append(put(do_all.at[span, :], do_ref.at[span, :], out_sem.at[len(copies)]))
        db_all[span, :] = db
        dm_all[span, :] = dm
        o_t[:, span] = jnp.transpose(o)
        a2_t[:, span] = jnp.transpose(a2)
        h_t[:, span] = jnp.transpose(h)
    dm, duw, db = dm_all[...], duw_all[...], db_all[...]
    for j, out, target in ((1, send, send_ref), (3, send, send_ref), (0, keep, keep_ref), (2, keep, keep_ref)):
        span = pl.ds(pl.multiple_of((place ^ j) * share, share), share)
        base = (place ^ j) * (share + short)
        down = pl.ds(pl.multiple_of(base, short), share)
        down_last = pl.ds(pl.multiple_of(base + share, short), short)
        at = 2 * units
        out[j // 2, :, :at] = mul(a2_t[span, :], duw).astype(LOW)
        out[j // 2, :, at : at + width] = mul(o_t[span, :], db).astype(LOW)
        at += width
        out[j // 2, :, at : at + width] = mul(h_t[down, :], dm).astype(LOW)
        at += width
        last = mul(h_t[down_last, :], dm).astype(LOW)
        out[j // 2, :short, at:] = last[:, : width // 2]
        out[j // 2, short:, at:] = last[:, width // 2 :]
        copies.append(put(out.at[j // 2], target.at[j // 2], out_sem.at[len(copies)]))
    wait_all(copies)


def send_kernel(count, at_ref, normed_ref, *refs):
    groups = [refs[i * count : (i + 1) * count] for i in range(3)]
    cos_ref, sin_ref, dqkv_ref, normed_t_ref, send_ref, dqkv, normed_t, send, sem = refs[3 * count :]
    width = normed_ref.shape[1]
    part_width = width // count
    normed_t[...] = jnp.transpose(normed_ref[...])
    copies = [put(normed_t, normed_t_ref, sem.at[0])]
    cos_part, sin_part = cos_ref[...], -sin_ref[...]
    for part, (dq, own, got) in enumerate(zip(*groups)):
        base = part * part_width
        dqkv[:, pl.ds(base, part_width)] = dq[...]
        dqkv[:, pl.ds(2 * width + base, part_width)] = (
            own[1].astype(FULL) + got[1].astype(FULL)
        ).astype(LOW)
        for pair in range(part_width // PAIR):
            lanes = pl.ds(pair * PAIR, PAIR)
            raw = own[0, :, lanes].astype(FULL) + got[0, :, lanes].astype(FULL)
            dqkv[:, pl.ds(width + base + pair * PAIR, PAIR)] = turn(raw, cos_part, sin_part).astype(
                LOW
            )
    copies.append(put(dqkv, dqkv_ref, sem.at[1]))
    right = dqkv[...]
    share = send.shape[1]
    for j in (1, 3):
        start = pl.multiple_of((at_ref[0] ^ j) * share, share)
        send[j // 2] = mul(normed_t[pl.ds(start, share), :], right).astype(LOW)
        copies.append(put(send.at[j // 2], send_ref.at[j // 2], sem.at[len(copies)]))
    wait_all(copies)


def keep_kernel(at_ref, normed_t_ref, dqkv_ref, keep_ref, keep, sem):
    right = dqkv_ref[...]
    share = keep.shape[1]
    copies = []
    for j in (0, 2):
        start = pl.multiple_of((at_ref[0] ^ j) * share, share)
        keep[j // 2] = mul(normed_t_ref[pl.ds(start, share), :], right).astype(LOW)
        copies.append(put(keep.at[j // 2], keep_ref.at[j // 2], sem.at[len(copies)]))
    wait_all(copies)


def input_kernel(at_ref, tokens_ref, far_ref, gain_ref, dx1_ref, dqkv_ref, w0, w1, w2, w3, w4, w5,
                 grad_ref, grad_far_ref, weight, grad_own, sem, out_sem):
    wait_all(load_blocks(at_ref, (w0, w1, w2, w3, w4, w5), weight, sem))
    rows = far_ref.shape[0]
    gain = gain_ref[...]
    for part in (1, 0):
        span = pl.ds(part * rows, rows)
        values = tokens_ref[at_ref[2]] if part == 0 else far_ref[...]
        scaled, root = normalize(values.astype(FULL))
        back = normalize_back(mul_t(dqkv_ref[span, :], weight[...]), gain, scaled, root)
        grad = dx1_ref[span, :] + back
        if part == 1:
            grad_far_ref[...] = grad.astype(LOW)
        else:
            grad_own[...] = grad
    put(grad_own, grad_ref.at[at_ref[2]], out_sem.at[0]).wait()


def shaped(*shape, kind=LOW):
    return jax.ShapeDtypeStruct(shape, kind)


IN_SMEM = pl.BlockSpec(memory_space=pltpu.SMEM)
IN_VMEM = pl.BlockSpec(memory_space=pltpu.VMEM)
IN_ANY = pl.BlockSpec(memory_space=pl.ANY)


def params(mebibytes):
    return pltpu.CompilerParams(vmem_limit_bytes=int(mebibytes * 1024 * 1024))


def call(kernel, args, in_specs, out_shape, out_specs, late=(), **options):
    if not isinstance(out_shape, tuple):
        out_shape, out_specs = (out_shape,), (out_specs,)
    count, skip, outs = len(args), len(late), len(out_shape)

    def body(*refs):
        outs_at = count + skip
        return kernel(*refs[:count], *refs[outs_at : outs_at + outs], *refs[outs_at + outs + 1 :])

    return pl.pallas_call(
        body,
        in_specs=list(in_specs) + [IN_ANY] * skip,
        out_shape=out_shape + (shaped(8, 128, kind=FULL),),
        out_specs=out_specs + (IN_ANY,),
        **options,
    )(*args, *late)


def gate(values, late=(), weight=0):
    hint = {}
    if weight:
        hint["cost_estimate"] = pl.CostEstimate(
            flops=weight, transcendentals=0, bytes_accessed=0
        )
    return call(
        lambda *refs: None,
        values,
        late=late,
        out_shape=tuple(jax.ShapeDtypeStruct(v.shape, v.dtype) for v in values),
        in_specs=[IN_ANY] * len(values),
        out_specs=(IN_ANY,) * len(values),
        input_output_aliases={i: i for i in range(len(values))},
        compiler_params=params(1),
        name="gate",
        **hint,
    )[: len(values)]


def prepare_first(at, weight):
    rows, width = weight.shape
    return call(
        prepare_first_kernel,
        (at, weight),
        out_shape=(shaped(rows, width), shaped(rows // 2, width)),
        in_specs=[IN_SMEM, IN_VMEM],
        out_specs=(IN_VMEM,) * 2,
        compiler_params=params(8),
        name="prepare_first",
    )


def prepare_rest(at, w_in, w_out, w_down, cotangent, tokens, late):
    rows, width = w_out.shape
    folded = 2 * width + width // 2
    return call(
        prepare_rest_kernel,
        (at, w_in, w_out, w_down, cotangent, tokens),
        late=late,
        out_shape=(
            shaped(*w_in.shape),
            shaped(rows // 2, w_in.shape[1]),
            shaped(rows, folded),
            shaped(rows // 2, folded),
            shaped(*cotangent.shape[1:]),
            shaped(*tokens.shape[1:]),
        ),
        in_specs=[IN_SMEM] + [IN_VMEM] * 5,
        out_specs=(IN_VMEM,) * 6,
        compiler_params=params(14),
        name="prepare_rest",
    )


def project(at, tokens, far, gain, cos_part, sin_part, blocks, late):
    rows, width = 2 * far.shape[0], far.shape[1]
    return call(
        project_kernel,
        (at, tokens, far, gain, cos_part, sin_part, *blocks),
        late=late,
        out_shape=(shaped(rows, width), shaped(rows, width), shaped(2, rows, width)),
        in_specs=[IN_SMEM] + [IN_VMEM] * 5 + [IN_ANY] * 6,
        out_specs=(IN_VMEM,) * 3,
        scratch_shapes=[pltpu.VMEM((width, 3 * width), LOW), pltpu.SemaphoreType.DMA((6,))],
        compiler_params=params(16),
        name="project",
    )


def attend(first, count, query, near, far, mark_query, mark_key, late=()):
    rows = query.shape[0]
    row_spec = pl.BlockSpec((rows, PAIR), lambda i: (0, i + first))
    kv_spec = pl.BlockSpec((2, rows, PAIR), lambda i: (0, 0, i + first))
    out_spec = pl.BlockSpec((rows, PAIR), lambda i: (0, i))
    return call(
        attend_kernel,
        (query, near, far, mark_query, mark_key),
        late=late,
        grid=(count,),
        out_shape=(shaped(rows, count * PAIR), shaped(rows, count * PAIR)),
        in_specs=[
            row_spec,
            kv_spec,
            kv_spec,
            pl.BlockSpec((rows, PAIR), lambda i: (0, 0)),
            pl.BlockSpec((2 * rows, PAIR), lambda i: (0, 0)),
        ],
        out_specs=(out_spec, out_spec),
        compiler_params=params(16),
        name="attend",
    )


def attend_back(
    first, first_o, count, query, near, far, extra, o, mark_key, do, cos_part, sin_part, late=()
):
    rows = query.shape[0]
    row_spec = pl.BlockSpec((rows, PAIR), lambda i: (0, i + first))
    o_spec = pl.BlockSpec((rows, PAIR), lambda i: (0, i + first_o))
    kv_spec = pl.BlockSpec((2, rows, PAIR), lambda i: (0, 0, i + first))
    fixed = pl.BlockSpec((rows, PAIR), lambda i: (0, 0))
    out_row = pl.BlockSpec((rows, PAIR), lambda i: (0, i))
    out_kv = pl.BlockSpec((2, rows, PAIR), lambda i: (0, 0, i))
    return call(
        attend_back_kernel,
        (query, near, far, extra, mark_key, o, do, cos_part, sin_part),
        late=late,
        grid=(count,),
        out_shape=(
            shaped(rows, count * PAIR),
            shaped(2, rows, count * PAIR),
            shaped(2, rows, count * PAIR),
        ),
        in_specs=[
            row_spec,
            kv_spec,
            kv_spec,
            o_spec,
            pl.BlockSpec((2 * rows, PAIR), lambda i: (0, 0)),
            o_spec,
            row_spec,
            fixed,
            fixed,
        ],
        out_specs=(out_row, out_kv, out_kv),
        compiler_params=params(20),
        name="attend_back",
    )


def middle(at, live, tokens, far, cot, cot_far, o_a, o_b, gain, blocks_in, blocks_od):
    half, width = far.shape
    rows, share = 2 * half, width // 4
    units = blocks_in[0].shape[1] // 2
    total = 2 * units + blocks_od[0].shape[1]
    assert units == 4 * (share + share // 2)
    low = lambda *shape: pltpu.VMEM(shape, LOW)
    return call(
        middle_kernel,
        (at, live, tokens, far, cot, cot_far, o_a, o_b, gain, *blocks_in, *blocks_od),
        out_shape=(
            shaped(2, half, width),
            shaped(half, width),
            shaped(rows, width, kind=FULL),
            shaped(rows, width),
            shaped(2, share, total),
            shaped(2, share, total),
        ),
        in_specs=[IN_SMEM] * 2 + [IN_VMEM] * 7 + [IN_ANY] * 12,
        out_specs=(IN_ANY,) * 6,
        scratch_shapes=[
            low(width, width),
            low(width, 2 * units),
            low(units, width),
            low(rows, width),
            low(width, rows),
            low(width, rows),
            low(units, rows),
            low(rows, width),
            low(rows, 2 * units),
            low(rows, width),
            low(rows, width),
            pltpu.VMEM((rows, width), FULL),
            low(rows, width),
            low(2, share, total),
            low(2, share, total),
            pltpu.SemaphoreType.DMA((6,)),
            pltpu.SemaphoreType.DMA((20,)),
            pltpu.SemaphoreType.DMA((10,)),
        ],
        compiler_params=params(40),
        name="middle",
    )


def qkv_send(at, normed, dq, own, got, cos_part, sin_part, late):
    rows, width = normed.shape
    share = width // 4
    return call(
        functools.partial(send_kernel, len(dq)),
        (at, normed, *dq, *own, *got, cos_part, sin_part),
        late=late,
        out_shape=(
            shaped(rows, 3 * width),
            shaped(width, rows),
            shaped(2, share, 3 * width),
        ),
        in_specs=[IN_SMEM] + [IN_VMEM] * (3 + 3 * len(dq)),
        out_specs=(IN_ANY,) * 3,
        scratch_shapes=[
            pltpu.VMEM((rows, 3 * width), LOW),
            pltpu.VMEM((width, rows), LOW),
            pltpu.VMEM((2, share, 3 * width), LOW),
            pltpu.SemaphoreType.DMA((4,)),
        ],
        compiler_params=params(20),
        name="qkv_send",
    )


def qkv_keep(at, normed_t, dqkv, late):
    width, rows = normed_t.shape
    share = width // 4
    return call(
        keep_kernel,
        (at, normed_t, dqkv),
        late=late,
        out_shape=shaped(2, share, 3 * width),
        in_specs=[IN_SMEM] + [IN_VMEM] * 2,
        out_specs=IN_ANY,
        scratch_shapes=[
            pltpu.VMEM((2, share, 3 * width), LOW),
            pltpu.SemaphoreType.DMA((2,)),
        ],
        compiler_params=params(16),
        name="qkv_keep",
    )


def input_back(at, tokens, far, gain, dx1, dqkv, blocks, late):
    half, width = far.shape
    return call(
        input_kernel,
        (at, tokens, far, gain, dx1, dqkv, *blocks),
        late=late,
        out_shape=(shaped(2, half, width, kind=FULL), shaped(half, width)),
        in_specs=[IN_SMEM] + [IN_VMEM] * 5 + [IN_ANY] * 6,
        out_specs=(IN_ANY, IN_VMEM),
        scratch_shapes=[
            pltpu.VMEM((width, 3 * width), LOW),
            pltpu.VMEM((half, width), FULL),
            pltpu.SemaphoreType.DMA((6,)),
            pltpu.SemaphoreType.DMA((1,)),
        ],
        compiler_params=params(20),
        name="input_back",
    )


def first_sums_kernel(at_ref, keep, got, own_a, far_a, mine_b, give_b):
    cut, short = far_a.shape[0], give_b.shape[1]

    def add(block, start, size):
        span = pl.ds(start, size)
        return (keep[block, span, :].astype(FULL) + got[block, span, :].astype(FULL)).astype(LOW)

    far_a[...] = add(1, 0, cut)
    for block in range(2):
        give_b[block] = add(block, pl.multiple_of(cut + (1 - at_ref[1]) * short, short), short)
        mine_b[block] = add(block, pl.multiple_of(cut + at_ref[1] * short, short), short)
    own_a[...] = add(0, 0, cut)


def first_sums(at, keep, got, late=()):
    _, rows, width = keep.shape
    cut, short = rows // 2, rows // 4
    return call(
        first_sums_kernel,
        (at, keep, got),
        late=late,
        out_shape=(shaped(cut, width),) * 2 + (shaped(2, short, width),) * 2,
        in_specs=[IN_SMEM] + [IN_VMEM] * 2,
        out_specs=(IN_VMEM,) * 4,
        compiler_params=params(20),
        name="first_sums",
    )


def second_sums_kernel(at_ref, own_a, got_a, mine_b, got_b, mine_a, give_a, near_b, far_b):
    short = mine_a.shape[0]
    for start, out in ((1 - at_ref[1], give_a), (at_ref[1], mine_a)):
        span = pl.ds(pl.multiple_of(start * short, short), short)
        out[...] = (own_a[span, :].astype(FULL) + got_a[span, :].astype(FULL)).astype(LOW)
    for block, out in ((1, far_b), (0, near_b)):
        out[...] = (mine_b[block].astype(FULL) + got_b[block].astype(FULL)).astype(LOW)


def second_sums(at, own_a, got_a, mine_b, got_b, late=()):
    _, short, width = mine_b.shape
    return call(
        second_sums_kernel,
        (at, own_a, got_a, mine_b, got_b),
        late=late,
        out_shape=(shaped(short, width),) * 4,
        in_specs=[IN_SMEM] + [IN_VMEM] * 4,
        out_specs=(IN_VMEM,) * 4,
        compiler_params=params(12),
        name="second_sums",
    )


def third_sums_kernel(lanes, mine_a, got_a, near_b, got_b, *outs):
    upper = mine_a[...].astype(FULL) + got_a[...].astype(FULL)
    lower = near_b[...].astype(FULL) + got_b[...].astype(FULL)
    total = jnp.concatenate([upper, lower])
    first = 0
    for out, width in zip(outs, lanes):
        count, rows, _ = out.shape
        for i in range(count):
            out[i] = total[i * rows : (i + 1) * rows, first : first + width].astype(LOW)
        first += width


def third_sums(count, lanes, mine_a, got_a, near_b, got_b, late=()):
    rows = 2 * mine_a.shape[0] // count
    return call(
        functools.partial(third_sums_kernel, lanes),
        (mine_a, got_a, near_b, got_b),
        late=late,
        out_shape=tuple(shaped(count, rows, width) for width in lanes),
        in_specs=[IN_VMEM] * 4,
        out_specs=(IN_VMEM,) * len(lanes),
        compiler_params=params(12),
        name="third_sums",
    )


def squares_kernel(at_ref, qkv, w_qkv, gain_one, inner, w_in, gain_two, folded, out):
    total = jnp.sum(jnp.square(folded[...].astype(FULL)), keepdims=True)
    rows = qkv.shape[0]
    for i, (piece, weight, gain) in enumerate(((qkv, w_qkv, gain_one), (inner, w_in, gain_two))):
        span = slice(0, rows)
        if weight.shape[0] != rows:
            span = pl.ds(pl.multiple_of(at_ref[3 + i], 8), rows)
        values = piece[...].astype(FULL)
        sums = jnp.sum(weight[span, :].astype(LOW).astype(FULL) * values, axis=1, keepdims=True)
        total += jnp.sum(jnp.square(values), keepdims=True)
        total += jnp.sum(jnp.square(sums / gain[span, :]), keepdims=True)
    out[...] = jnp.broadcast_to(total, out.shape)


def squares(*args):
    return call(
        squares_kernel,
        args,
        out_shape=shaped(8, 128, kind=FULL),
        in_specs=[IN_SMEM] + [IN_VMEM] * (len(args) - 1),
        out_specs=IN_VMEM,
        compiler_params=params(10),
        name="squares",
    )


def adam_kernel(rates, at_ref, square_ref, w_ref, m_ref, v_ref, mine_ref, other_ref,
                w_out, m_out, v_out, row_out):
    own = (pl.program_id(0) & 1) == at_ref[1]
    gradient = jnp.where(own, mine_ref[...].astype(FULL), other_ref[...].astype(FULL))
    weight = w_ref[...]
    rows = jnp.sum(weight.astype(LOW).astype(FULL) * gradient, axis=1, keepdims=True)
    row_out[...] = jnp.broadcast_to(rows, row_out.shape)
    norm = jnp.sqrt(square_ref[:1, :1])
    factor = jnp.minimum(1.0, CLIP_LIMIT / (norm + 1e-06))
    w_out[...], m_out[...], v_out[...] = adam_step(
        weight, m_ref[...], v_ref[...], gradient, factor, *rates
    )


def adam(at, square, weight, first, second, mine, other, rates):
    rows, width = weight.shape
    quarter = rows // 4
    block = pl.BlockSpec((quarter, width), lambda i: (i, 0))
    part = pl.BlockSpec((quarter, width), lambda i: (i // 2, 0))
    return call(
        functools.partial(adam_kernel, rates),
        (at, square, weight, first, second, mine, other),
        grid=(4,),
        out_shape=(shaped(rows, width, kind=FULL),) * 3 + (shaped(rows, PAIR, kind=FULL),),
        in_specs=[IN_SMEM, pl.BlockSpec((8, 128), lambda i: (0, 0))] + [block] * 3 + [part] * 2,
        out_specs=(block,) * 3 + (pl.BlockSpec((quarter, PAIR), lambda i: (i, 0)),),
        compiler_params=params(16),
        name="adam",
    )


def low_sum(*values):
    return sum(value.astype(FULL) for value in values).astype(LOW)


def index(value, i):
    return lax.dynamic_index_in_dim(value, i, 0, keepdims=False)


def make(dp_count, seq_count):
    assert seq_count == 4 and dp_count % 4 == 0 and dp_count & (dp_count - 1) == 0
    bits = dp_count.bit_length() - 1
    ones = [(shift, 1) for shift in range(1, bits)]
    twos = [(shift, min(2, bits - shift)) for shift in range(1, bits, 2)]
    count = dp_count // 2

    def trade(value, axis, bit):
        size = seq_count if axis == "seq" else dp_count
        return lax.ppermute(value, axis, [(i, i ^ bit) for i in range(size)])

    def fields(group, steps):
        for shift, width in steps:
            yield shift, 1 << width, (group >> shift) & ((1 << width) - 1)

    def sum_steps(value, group, steps, lates=()):
        for i, (shift, size, mine) in enumerate(fields(group, steps)):
            parts = value.reshape((size, value.shape[0] // size) + value.shape[1:])
            got = [trade(index(parts, mine ^ k), "dp", k << shift) for k in range(1, size)]
            if i < len(lates) and lates[i]:
                got = gate(got, lates[i])
            value = low_sum(index(parts, mine), *got)
        return value[0]

    def piece_row(group, steps, share):
        at = 0
        for _, size, mine in fields(group, steps):
            at = at * size + mine
        quarter, row = share // 4, at * (share // 2 // count)
        return (row // quarter) * 2 * quarter + (group & 1) * quarter + row % quarter

    def join_steps(piece, group, steps, lates=()):
        value, came = piece[None], []
        for i, (shift, size, mine) in enumerate(list(fields(group, steps))[::-1]):
            got = [trade(value, "dp", k << shift) for k in range(1, size)]
            came.append(got)
            if i < len(lates) and lates[i]:
                got = gate(got, lates[i])
            stack = jnp.stack([value, *got])
            value = jnp.concatenate([index(stack, mine ^ k) for k in range(size)])
        return value, came

    def on_device(
        tokens, cotangent, segments, valid,
        w_qkv, w_out, w_in, w_down, gains,
        m_qkv, m_out, m_in, m_down, m_gains,
        v_qkv, v_out, v_in, v_down, v_gains,
    ):
        place = lax.axis_index("seq")
        group = lax.axis_index("dp")
        slot = place >> 1
        half = group & 1
        local_len, width = tokens.shape[1:]
        rows = 2 * local_len
        share = w_qkv.shape[0]
        at = jnp.stack(
            [place, half, slot, piece_row(group, twos, share), piece_row(group, ones, share)]
        )
        gain_columns = jnp.transpose(gains.astype(LOW).astype(FULL))

        low_qkv, half_qkv, begun = prepare_first(at, w_qkv)
        far_qa = trade(half_qkv, "seq", 2)
        near_q = trade(low_qkv, "seq", 1)
        low_in, half_in, low_od, half_od, their_cot, their_tokens, _ = prepare_rest(
            at, w_in, w_out, w_down, cotangent, tokens, (begun,)
        )
        low_gains = gains.astype(LOW)
        far = trade(their_tokens, "seq", 2)
        gain_far = trade(low_gains, "seq", 2)
        far_qb = trade(far_qa, "dp", 1)
        near_qa = trade(far_qa, "seq", 1)
        near_qb = trade(far_qb, "seq", 1)
        gain_near = trade(jnp.stack([low_gains, gain_far]), "seq", 1)
        gain_stack = jnp.stack([low_gains, gain_near[0], gain_far, gain_near[1]])
        gain_low = jnp.concatenate(
            [index(gain_stack, b ^ place) for b in range(4)], axis=1
        ).astype(FULL)
        blocks_qkv = (low_qkv, near_q, far_qa, far_qb, near_qa, near_qb)
        near_i = trade(low_in, "seq", 1)
        near_o = trade(low_od, "seq", 1)
        (half_in,) = gate((half_in,), (far_qa,))
        far_ia = trade(half_in, "seq", 2)

        seg = index(segments, slot)
        positions = doc_positions(seg).reshape(4, local_len)
        seg = seg.reshape(4, local_len)
        chunks = [place, place ^ 2, place ^ 1, place ^ 3]
        seg_keys = jnp.concatenate([index(seg, c) for c in chunks])
        pos = jnp.concatenate([index(positions, c) for c in chunks[:2]])
        cos_part, sin_part = rope_tables(pos)
        lane = jnp.arange(PAIR, dtype=jnp.int32)[None] % HEAD_DIM
        same = seg_keys[:, None] == lane
        mark_key = jnp.where(lane < DOCS, 1.0 - same, (lane < DOCS + 3) * 1.0).astype(LOW)
        mark_query = jnp.where((lane < DOCS) & same[:rows], NEG_FILL, 0.0).astype(LOW)
        live = lax.dynamic_index_in_dim(valid, slot, 0, keepdims=True).astype(FULL)

        normed, query, kv, _ = project(
            at, tokens, far, gain_low[:1], cos_part, sin_part, blocks_qkv,
            (far_ia, near_i, near_o, mark_key, mark_query),
        )
        kv_far = trade(kv, "seq", 1)
        far_oa = trade(half_od, "seq", 2)
        far_ib = trade(far_ia, "dp", 1)
        near_ia = trade(far_ia, "seq", 1)
        (cot_far,) = gate((trade(their_cot, "seq", 2),), weight=WEIGHT)
        pairs = width // PAIR
        early = 2
        args = (query, kv, kv_far, mark_query, mark_key)
        o_a, extra_a, done_a = attend(0, early, *args)
        far_oa, far_ib = gate((far_oa, far_ib), (done_a,), weight=10 * WEIGHT)
        far_ob = trade(far_oa, "dp", 1)
        near_oa = trade(far_oa, "seq", 1)
        near_ib = trade(far_ib, "seq", 1)
        o_b, extra_b, done_b = attend(early, pairs - early, *args, late=(done_a, far_oa, near_ia))
        (far_ob,) = gate((far_ob,), (done_b,))
        near_ob = trade(far_ob, "seq", 1)
        blocks_in = (low_in, near_i, far_ia, far_ib, near_ia, near_ib)
        blocks_od = (low_od, near_o, far_oa, far_ob, near_oa, near_ob)

        mixed, mixed_far, dx1, do, keep_rest, send_rest, _ = middle(
            at, live, tokens, far, cotangent, cot_far, o_a, o_b, gain_low[1:], blocks_in, blocks_od
        )
        got_rest = trade(send_rest, "seq", 1)
        mixed_far = trade(mixed_far, "seq", 2)
        two = pairs // 3
        near_args = (query, kv, kv_far)
        back_args = (mark_key, do, cos_part, sin_part)
        dq0, own0, give0, back0 = attend_back(0, 0, two, *near_args, extra_a, o_a, *back_args)
        *r1, r1_done = first_sums(at, keep_rest, got_rest, late=(back0, mixed_far))
        got_ra, got_rb = trade(r1[1], "seq", 2), trade(r1[3], "dp", 1)
        got0 = trade(give0, "seq", 1)
        dq1, own1, give1, back1 = attend_back(
            two, two - early, two, *near_args, extra_b, o_b, *back_args, late=(r1_done,)
        )
        got1 = trade(give1, "seq", 1)
        dq2, own2, give2, back2 = attend_back(
            2 * two, 2 * two - early, pairs - 2 * two, *near_args, extra_b, o_b, *back_args,
            late=(back1,),
        )
        got2 = trade(give2, "seq", 1)
        *r2, r2_done = second_sums(at, r1[0], got_ra, r1[2], got_rb, late=(back2,))
        got_ra, got_rb = gate(
            (trade(r2[1], "dp", 1), trade(r2[3], "seq", 2)), weight=WEIGHT
        )
        dqkv, normed_t, send_qkv, _ = qkv_send(
            at, normed, (dq0, dq1, dq2), (own0, own1, own2), (got0, got1, got2),
            cos_part, sin_part, late=(r2_done,),
        )
        got_qkv = trade(send_qkv, "seq", 1)
        keep_qkv, _ = qkv_keep(at, normed_t, dqkv, late=())
        *q1, q1_done = first_sums(at, keep_qkv, got_qkv)
        got_qa, got_qb = trade(q1[1], "seq", 2), trade(q1[3], "dp", 1)
        inner_lanes = w_in.shape[1]
        lanes = (inner_lanes, keep_rest.shape[2] - inner_lanes)
        inner, folded, r3_done = third_sums(
            count, lanes, r2[0], got_ra, r2[2], got_rb, late=(q1_done,)
        )
        grad, grad_far, grad_done = input_back(
            at, tokens, far, gain_low[:1], dx1, dqkv, blocks_qkv, late=(r3_done,)
        )
        *q2, q2_done = second_sums(at, q1[0], got_qa, q1[2], got_qb, late=(grad_done,))
        got_qa, got_qb = gate(
            (trade(q2[1], "dp", 1), trade(q2[3], "seq", 2)), weight=10 * WEIGHT
        )
        qkv, q3_done = third_sums(count, (3 * width,), q2[0], got_qa, q2[2], got_qb)
        inner_piece = sum_steps(inner, group, ones, ((grad_done,), (q2_done,)))
        folded_piece = sum_steps(folded, group, ones, ((grad_done,), (q2_done,)))
        qkv_piece = sum_steps(qkv, group, twos)
        qkv_mine, came = join_steps(qkv_piece, group, twos)
        inner_mine, _ = join_steps(inner_piece, group, ones, ((q3_done,), (qkv_piece,)))
        folded_mine, _ = join_steps(folded_piece, group, ones, ((q3_done,), (qkv_piece,)))
        (grad_far,) = gate((grad_far,), tuple(came[0]))
        grad_far = trade(grad_far, "seq", 2)

        behind = [w_qkv, gain_columns[:, :1], w_in, gain_columns[:, 1:]]
        if qkv_piece.shape[0] % 8:
            behind = [
                lax.dynamic_slice_in_dim(value, at[3 + i // 2], qkv_piece.shape[0], 0)
                for i, value in enumerate(behind)
            ]
        square, _ = squares(at, qkv_piece, *behind[:2], inner_piece, *behind[2:], folded_piece)
        square = square + trade(square, "seq", 2)
        (square,) = gate((square,), tuple(came[0]))
        square = square + trade(square, "seq", 1)
        for bit in range(bits):
            square = square + trade(square, "dp", dp_count >> (bit + 1))
        grad_norm = jnp.sqrt(square[0, 0])
        factor = jnp.minimum(1.0, CLIP_LIMIT / (grad_norm + 1e-06))

        def both_halves(mine):
            mine = mine.reshape((-1,) + mine.shape[2:])
            return mine, gate((trade(mine, "dp", 1),), weight=WEIGHT)[0]

        new_qkv, first_qkv, second_qkv, row_one, _ = adam(
            at, square, w_qkv, m_qkv, v_qkv, *both_halves(qkv_mine), (STEP_RATES[0], DECAY_RATES[0])
        )
        new_in, first_in, second_in, row_two, _ = adam(
            at, square, w_in, m_in, v_in, *both_halves(inner_mine), (STEP_RATES[2], DECAY_RATES[2])
        )
        mine, other = both_halves(folded_mine)
        short = share // 4
        lower = jnp.where(half == 0, mine, other)
        upper = jnp.where(half == 0, other, mine)
        folded_all = jnp.concatenate([lower[:short], upper[:short], lower[short:], upper[short:]])
        last = folded_all[:, 2 * width :]
        grad_down = jnp.concatenate(
            [
                folded_all[:, width : 2 * width],
                jnp.concatenate([last[: share // 2], last[share // 2 :]], axis=1),
            ]
        )
        gain_grads = jnp.stack([row_one[:, 0], row_two[:, 0]]) / gains.astype(LOW).astype(FULL)

        def step(weight, first, second, gradient, i):
            gradient = gradient.astype(FULL)
            return adam_step(
                weight, first, second, gradient, factor, STEP_RATES[i], DECAY_RATES[i]
            )

        new_out, first_out, second_out = step(w_out, m_out, v_out, folded_all[:, :width], 1)
        new_down, first_down, second_down = step(w_down, m_down, v_down, grad_down, 3)
        new_gains, first_gains, second_gains = step(gains, m_gains, v_gains, gain_grads, 4)

        def fill(whole, theirs):
            theirs = theirs.astype(whole.dtype)[None]
            return lax.dynamic_update_slice(whole, theirs, (1 - slot, 0, 0))

        return (
            fill(mixed, mixed_far),
            fill(grad, grad_far),
            grad_norm,
            new_qkv, new_out, new_in, new_down, new_gains,
            first_qkv, first_out, first_in, first_down, first_gains,
            second_qkv, second_out, second_in, second_down, second_gains,
        )

    return on_device


def solution(mesh):
    rows, matrix, gain = P("dp", "seq", None), P("seq", None), P(None, "seq")
    weights = (matrix,) * 4 + (gain,)
    return jax.shard_map(
        make(mesh.shape["dp"], mesh.shape["seq"]),
        mesh=mesh,
        in_specs=(rows, rows, P("dp", None), P("dp")) + weights * 3,
        out_specs=(rows, rows, P()) + weights * 3,
        check_vma=False,
    )
```

```python
import functools
import math

import jax
import jax.numpy as jnp
from jax import lax
from jax.experimental import pallas as pl
from jax.experimental.pallas import tpu as pltpu
from jax.sharding import PartitionSpec as P

HEADS = 12
HEAD_DIM = 64
PAIR = 2 * HEAD_DIM
STEP_COUNT = 10
EPS_NORM = 1e-05
ROPE_BASE = 160000.0
NEG_FILL = -1e30
CLIP_LIMIT = 10.0
BETA_FIRST = 0.9
BETA_SECOND = 0.98
EPS_ADAM = 1e-06
STEP_RATES = (0.1, 0.5, 0.1, 0.1, 1.0)
DECAY_RATES = (0.01, 0.01, 0.01, 0.01, 0.0)
DOCS = 5
LOW = jnp.bfloat16
FULL = jnp.float32
SCALE = 1.0 / math.sqrt(HEAD_DIM)
WEIGHT = 20_000_000_000


def doc_positions(segment_ids):
    seq_len = segment_ids.shape[-1]
    places = jnp.arange(seq_len, dtype=jnp.int32)
    first_mark = jnp.ones((1,), jnp.bool_)
    change = jnp.concatenate([first_mark, segment_ids[1:] != segment_ids[:-1]])
    starts = lax.cummax(jnp.where(change, places, 0), axis=0)
    return places - starts


def rope_tables(positions):
    half_dim = HEAD_DIM // 2
    exponents = jnp.arange(half_dim, dtype=jnp.float32) * (2.0 / HEAD_DIM)
    inv_freq = ROPE_BASE ** (-exponents)
    angles = positions.astype(jnp.float32)[:, None] * inv_freq
    cos_part, sin_part = jnp.cos(angles), jnp.sin(angles)
    return (
        jnp.concatenate([cos_part] * 4, axis=1),
        jnp.concatenate([-sin_part, sin_part] * 2, axis=1),
    )


def adam_step(weight, first_old, second_old, gradient, factor, step_rate, decay_rate):
    clipped = gradient * factor
    first_new = BETA_FIRST * first_old + (1.0 - BETA_FIRST) * clipped
    second_new = BETA_SECOND * second_old + (1.0 - BETA_SECOND) * clipped * clipped
    first_hat = first_new / (1.0 - BETA_FIRST**STEP_COUNT)
    second_hat = second_new / (1.0 - BETA_SECOND**STEP_COUNT)
    weight_new = weight * (1.0 - step_rate * decay_rate) - step_rate * first_hat / (
        jnp.sqrt(second_hat) + EPS_ADAM
    )
    return (weight_new, first_new, second_new)


def mul(left, right):
    return lax.dot_general(left, right, (((1,), (0,)), ((), ())), preferred_element_type=FULL)


def mul_t(left, right):
    return lax.dot_general(left, right, (((1,), (1,)), ((), ())), preferred_element_type=FULL)


def normalize(values):
    centered = values - jnp.mean(values, axis=-1, keepdims=True)
    root = lax.rsqrt(jnp.mean(centered * centered, axis=-1, keepdims=True) + EPS_NORM)
    return centered * root, root


def normalize_back(grad, gain, scaled, root):
    t = grad * gain
    back = root * (
        t
        - jnp.mean(t, axis=-1, keepdims=True)
        - scaled * jnp.mean(t * scaled, axis=-1, keepdims=True)
    )
    return back


def turn(values, cos_part, sin_part):
    lane = lax.broadcasted_iota(jnp.int32, values.shape, 1)
    swapped = jnp.where(
        lane % HEAD_DIM < HEAD_DIM // 2,
        pltpu.roll(values, PAIR - HEAD_DIM // 2, 1),
        pltpu.roll(values, HEAD_DIM // 2, 1),
    )
    return values * cos_part + swapped * sin_part


def three_parts(values):
    high = values.astype(LOW).astype(FULL)
    rest = values - high
    mid = rest.astype(LOW).astype(FULL)
    return high, mid, rest - mid


def wait_all(copies):
    for copy in copies:
        copy.wait()


def put(source, target, sem):
    copy = pltpu.make_async_copy(source, target, sem)
    copy.start()
    return copy


PIECES = ((0, None), (1, None), (2, 0), (2, 1), (3, 0), (3, 1))


def load_blocks(at_ref, blocks, whole, sem):
    rows = blocks[0].shape[0]
    copies = []
    for i, (bits, part) in enumerate(PIECES):
        start = (at_ref[0] ^ bits) * rows
        size = rows
        if part is not None:
            size = rows // 2
            start += (at_ref[1] ^ part) * size
        target = whole.at[pl.ds(pl.multiple_of(start, size), size), :]
        copies.append(put(blocks[i], target, sem.at[i]))
    return copies


def load_folded(at_ref, blocks, w_out, w_down, sem):
    rows, width = blocks[0].shape[0], w_out.shape[1]
    short, last = rows // 2, width // 2
    copies = []

    def copy(source, target):
        copies.append(put(source, target, sem.at[len(copies)]))

    for i, (bits, part) in enumerate(PIECES):
        owner = at_ref[0] ^ bits
        base = owner * (rows + short)
        first = 0 if part is None else (at_ref[1] ^ part) * short
        size = rows if part is None else short
        for lanes, whole, start in ((0, w_out, owner * rows), (width, w_down, base)):
            span = pl.ds(pl.multiple_of(start + first, short), size)
            copy(blocks[i].at[:, pl.ds(lanes, width)], whole.at[span, :])
        span = pl.ds(pl.multiple_of(base + rows, short), short)
        if part is None:
            for fold in range(2):
                copy(
                    blocks[i].at[pl.ds(fold * short, short), pl.ds(2 * width, last)],
                    w_down.at[span, pl.ds(fold * last, last)],
                )
        else:
            lanes = pl.ds(pl.multiple_of((at_ref[1] ^ part) * last, last), last)
            copy(blocks[i].at[:, pl.ds(2 * width, last)], w_down.at[span, lanes])
    return copies


def fold(out, w_out, w_down, first):
    rows, width = w_out.shape
    short, last = rows // 2, width // 2
    out[:, first : first + width] = w_out[...].astype(LOW)
    out[:, first + width : first + 2 * width] = w_down[:rows, :].astype(LOW)
    for i in range(2):
        out[i * short : (i + 1) * short, first + 2 * width :] = w_down[
            rows:, i * last : (i + 1) * last
        ].astype(LOW)


def prepare_first_kernel(at_ref, w_ref, low_ref, half_ref):
    short = half_ref.shape[0]
    half_ref[...] = w_ref[pl.ds(pl.multiple_of(at_ref[1] * short, short), short), :].astype(LOW)
    low_ref[...] = w_ref[...].astype(LOW)


def prepare_rest_kernel(at_ref, in_ref, out_ref, down_ref, cot_ref, tokens_ref,
                        low_in, half_in, low_od, half_od, their_cot, their_tokens):
    their_tokens[...] = tokens_ref[1 - at_ref[2]]
    short = half_in.shape[0]
    span = pl.ds(pl.multiple_of(at_ref[1] * short, short), short)
    low_in[...] = in_ref[...].astype(LOW)
    half_in[...] = in_ref[span, :].astype(LOW)
    fold(low_od, out_ref, down_ref, 0)
    half_od[...] = low_od[span, :]
    their_cot[...] = cot_ref[1 - at_ref[2]]


def project_kernel(at_ref, tokens_ref, far_ref, gain_ref, cos_ref, sin_ref, w0, w1, w2, w3, w4, w5,
                   normed_ref, query_ref, kv_ref, weight, sem):
    copies = load_blocks(at_ref, (w0, w1, w2, w3, w4, w5), weight, sem)
    rows, width = far_ref.shape
    for part in range(2):
        values = tokens_ref[at_ref[2]] if part == 0 else far_ref[...]
        scaled, _ = normalize(values.astype(FULL))
        normed_ref[pl.ds(part * rows, rows), :] = (scaled * gain_ref[...]).astype(LOW)
    wait_all(copies)
    for part in range(2):
        span = pl.ds(part * rows, rows)
        normed = normed_ref[span, :]
        cos_part, sin_part = cos_ref[span, :], sin_ref[span, :]
        for pair in range(2 * width // PAIR):
            lanes = pl.ds(pair * PAIR, PAIR)
            if pair % 2 == 0:
                both = mul(normed, weight[:, pl.ds(pair * PAIR, 2 * PAIR)])
            raw = both[:, (pair % 2) * PAIR : (pair % 2 + 1) * PAIR]
            turned = turn(raw, cos_part, sin_part)
            if pair < width // PAIR:
                query_ref[span, lanes] = (turned * SCALE).astype(LOW)
            else:
                kv_ref[0, span, pl.ds(pair * PAIR - width, PAIR)] = turned.astype(LOW)
        kv_ref[1, span, :] = mul(normed, weight[:, 2 * width :]).astype(LOW)


def head_lanes(head, shape):
    lane = lax.broadcasted_iota(jnp.int32, shape, 1)
    return (lane < HEAD_DIM) if head == 0 else (lane >= HEAD_DIM)


def pick(head, inside, outside):
    return jnp.where(head_lanes(head, inside.shape), inside, outside)


def attend_kernel(query_ref, near_ref, far_ref, mark_query_ref, mark_key_ref, o_ref, extra_ref):
    rows = query_ref.shape[0]
    query = query_ref[...]
    mark_query = mark_query_ref[...]
    parts = [
        (near_ref[0], jnp.transpose(near_ref[1]), mark_key_ref[:rows, :]),
        (far_ref[0], jnp.transpose(far_ref[1]), mark_key_ref[rows:, :]),
    ]
    outs, logs = [], []
    for head in range(2):
        query_head = pick(head, query, mark_query)
        scores = [mul_t(pick(head, key, mark), query_head) for key, _, mark in parts]
        top = jnp.maximum(
            jnp.max(scores[0], axis=0, keepdims=True), jnp.max(scores[1], axis=0, keepdims=True)
        )
        exps = [jnp.exp(score - top) for score in scores]
        total = jnp.sum(exps[0], axis=0, keepdims=True) + jnp.sum(exps[1], axis=0, keepdims=True)
        span = slice(head * HEAD_DIM, (head + 1) * HEAD_DIM)
        out = sum(mul(value_t[span], e.astype(LOW)) for (_, value_t, _), e in zip(parts, exps))
        outs.append(out / total)
        logs.append(top + jnp.log(total))
    o_ref[...] = jnp.transpose(jnp.concatenate(outs)).astype(LOW)
    line = lax.broadcasted_iota(jnp.int32, (PAIR, rows), 0)
    extra = jnp.zeros((PAIR, rows), FULL)
    for head in range(2):
        base = DOCS + (HEAD_DIM if head == 0 else 0)
        for i, piece in enumerate(three_parts(-logs[head])):
            extra = jnp.where(line == base + i, piece, extra)
    extra_ref[...] = jnp.transpose(extra).astype(LOW) + mark_query


def attend_back_kernel(query_ref, near_ref, far_ref, extra_ref, mark_key_ref, o_ref, do_ref,
                       cos_ref, sin_ref, dq_ref, keep_ref, send_ref):
    rows = query_ref.shape[0]
    query, extra, do = query_ref[...], extra_ref[...], do_ref[...]
    inner_all = do.astype(FULL) * o_ref[...].astype(FULL)
    lane = lax.broadcasted_iota(jnp.int32, (rows, PAIR), 1)
    zero = jnp.zeros((rows, PAIR), LOW)
    grads_query = []
    sums = [[None, None], [None, None]]
    keys_t = [jnp.transpose(near_ref[0]), jnp.transpose(far_ref[0])]
    for head in range(2):
        inside = head_lanes(head, (rows, PAIR))
        inner = jnp.sum(jnp.where(inside, inner_all, 0.0), axis=1, keepdims=True)
        base = DOCS + (HEAD_DIM if head == 0 else 0)
        tail = jnp.zeros((rows, PAIR), FULL)
        for i, piece in enumerate(three_parts(-inner)):
            tail = jnp.where(lane == base + i, piece, tail)
        query_head = pick(head, query, extra)
        do_head = pick(head, do, tail.astype(LOW))
        query_only = pick(head, query, zero)
        do_only = pick(head, do, zero)
        span = slice(head * HEAD_DIM, (head + 1) * HEAD_DIM)
        grad_query = 0.0
        for part, ref in enumerate((near_ref, far_ref)):
            mark = mark_key_ref[pl.ds(part * rows, rows), :]
            probs = jnp.exp(mul_t(pick(head, ref[0], mark), query_head))
            grad_probs = mul_t(pick(head, ref[1], mark), do_head)
            grad_scores = (probs * grad_probs).astype(LOW)
            grad_value = mul(probs.astype(LOW), do_only)
            grad_key = mul(grad_scores, query_only)
            grad_query += mul(keys_t[part][span], grad_scores)
            if head == 0:
                sums[part] = [grad_key, grad_value]
            else:
                sums[part] = [sums[part][0] + grad_key, sums[part][1] + grad_value]
        grads_query.append(grad_query)
    turned = turn(
        jnp.transpose(jnp.concatenate(grads_query)) * SCALE, cos_ref[...], -sin_ref[...]
    )
    dq_ref[...] = turned.astype(LOW)
    for i in range(2):
        keep_ref[i] = sums[0][i].astype(LOW)
        send_ref[i] = sums[1][i].astype(LOW)


def middle_kernel(at_ref, live_ref, tokens_ref, far_ref, cot_ref, cot_far_ref, oa_ref, ob_ref,
                  gain_ref, i0, i1, i2, i3, i4, i5, d0, d1, d2, d3, d4, d5,
                  mixed_ref, mixed_far_ref, dx1_ref, do_ref, keep_ref, send_ref,
                  w_out, w_in, w_down, o_all, o_t, a2_t, h_t, dm_all, duw_all, db_all,
                  mixed, dx1_all, do_all, keep, send, sem, fold_sem, out_sem):
    place, slot, live = at_ref[0], at_ref[2], live_ref[0]
    copies_down = load_folded(at_ref, (d0, d1, d2, d3, d4, d5), w_out, w_down, fold_sem)
    copies_in = load_blocks(at_ref, (i0, i1, i2, i3, i4, i5), w_in, sem)
    rows, width = far_ref.shape
    share = width // 4
    short, units = share // 2, w_down.shape[0]
    gain = gain_ref[...]
    o_all[:, : oa_ref.shape[1]] = oa_ref[...]
    o_all[:, oa_ref.shape[1] :] = ob_ref[...]
    copies = []
    for part in range(2):
        span = pl.ds(part * rows, rows)
        o = o_all[span, :]
        values = tokens_ref[slot] if part == 0 else far_ref[...]
        if part == 0:
            wait_all(copies_down)
        x1 = values.astype(FULL) + live * mul(o, w_out[...])
        scaled, root = normalize(x1)
        a2 = (scaled * gain).astype(LOW)
        if part == 0:
            wait_all(copies_in)
        u = mul(a2, w_in[:, :units])
        w = mul(a2, w_in[:, units:])
        phi = 0.5 * (1.0 + lax.erf(u * math.sqrt(0.5)))
        gelu = u * phi
        h = (gelu * w).astype(LOW)
        mixed[span, :] = (x1 + live * mul(h, w_down[...])).astype(LOW)
        target = mixed_ref.at[slot] if part == 0 else mixed_far_ref
        copies.append(put(mixed.at[span, :], target, out_sem.at[len(copies)]))
        cot = (cot_ref[slot] if part == 0 else cot_far_ref[...]).astype(FULL)
        dm = (live * cot).astype(LOW)
        dh = mul_t(dm, w_down[...])
        slope = phi + u * (jnp.exp(-0.5 * u * u) * (1.0 / math.sqrt(2.0 * math.pi)))
        duw_all[span, :units] = (dh * w * slope).astype(LOW)
        duw_all[span, units:] = (dh * gelu).astype(LOW)
        da2 = mul_t(duw_all[span, :], w_in[...])
        dx1 = cot + normalize_back(da2, gain, scaled, root)
        dx1_all[span, :] = dx1
        copies.append(put(dx1_all.at[span, :], dx1_ref.at[span, :], out_sem.at[len(copies)]))
        db = (live * dx1).astype(LOW)
        do_all[span, :] = mul_t(db, w_out[...]).astype(LOW)
        copies.append(put(do_all.at[span, :], do_ref.at[span, :], out_sem.at[len(copies)]))
        db_all[span, :] = db
        dm_all[span, :] = dm
        o_t[:, span] = jnp.transpose(o)
        a2_t[:, span] = jnp.transpose(a2)
        h_t[:, span] = jnp.transpose(h)
    dm, duw, db = dm_all[...], duw_all[...], db_all[...]
    for j, out, target in ((1, send, send_ref), (3, send, send_ref), (0, keep, keep_ref), (2, keep, keep_ref)):
        span = pl.ds(pl.multiple_of((place ^ j) * share, share), share)
        base = (place ^ j) * (share + short)
        down = pl.ds(pl.multiple_of(base, short), share)
        down_last = pl.ds(pl.multiple_of(base + share, short), short)
        at = 2 * units
        out[j // 2, :, :at] = mul(a2_t[span, :], duw).astype(LOW)
        out[j // 2, :, at : at + width] = mul(o_t[span, :], db).astype(LOW)
        at += width
        out[j // 2, :, at : at + width] = mul(h_t[down, :], dm).astype(LOW)
        at += width
        last = mul(h_t[down_last, :], dm).astype(LOW)
        out[j // 2, :short, at:] = last[:, : width // 2]
        out[j // 2, short:, at:] = last[:, width // 2 :]
        copies.append(put(out.at[j // 2], target.at[j // 2], out_sem.at[len(copies)]))
    wait_all(copies)


def send_kernel(count, at_ref, normed_ref, *refs):
    groups = [refs[i * count : (i + 1) * count] for i in range(3)]
    cos_ref, sin_ref, dqkv_ref, normed_t_ref, send_ref, dqkv, normed_t, send, sem = refs[3 * count :]
    width = normed_ref.shape[1]
    part_width = width // count
    normed_t[...] = jnp.transpose(normed_ref[...])
    copies = [put(normed_t, normed_t_ref, sem.at[0])]
    cos_part, sin_part = cos_ref[...], -sin_ref[...]
    for part, (dq, own, got) in enumerate(zip(*groups)):
        base = part * part_width
        dqkv[:, pl.ds(base, part_width)] = dq[...]
        dqkv[:, pl.ds(2 * width + base, part_width)] = (
            own[1].astype(FULL) + got[1].astype(FULL)
        ).astype(LOW)
        for pair in range(part_width // PAIR):
            lanes = pl.ds(pair * PAIR, PAIR)
            raw = own[0, :, lanes].astype(FULL) + got[0, :, lanes].astype(FULL)
            dqkv[:, pl.ds(width + base + pair * PAIR, PAIR)] = turn(raw, cos_part, sin_part).astype(
                LOW
            )
    copies.append(put(dqkv, dqkv_ref, sem.at[1]))
    right = dqkv[...]
    share = send.shape[1]
    for j in (1, 3):
        start = pl.multiple_of((at_ref[0] ^ j) * share, share)
        send[j // 2] = mul(normed_t[pl.ds(start, share), :], right).astype(LOW)
        copies.append(put(send.at[j // 2], send_ref.at[j // 2], sem.at[len(copies)]))
    wait_all(copies)


def keep_kernel(at_ref, normed_t_ref, dqkv_ref, keep_ref, keep, sem):
    right = dqkv_ref[...]
    share = keep.shape[1]
    copies = []
    for j in (0, 2):
        start = pl.multiple_of((at_ref[0] ^ j) * share, share)
        keep[j // 2] = mul(normed_t_ref[pl.ds(start, share), :], right).astype(LOW)
        copies.append(put(keep.at[j // 2], keep_ref.at[j // 2], sem.at[len(copies)]))
    wait_all(copies)


def input_kernel(at_ref, tokens_ref, far_ref, gain_ref, dx1_ref, dqkv_ref, w0, w1, w2, w3, w4, w5,
                 grad_ref, grad_far_ref, weight, grad_own, sem, out_sem):
    wait_all(load_blocks(at_ref, (w0, w1, w2, w3, w4, w5), weight, sem))
    rows = far_ref.shape[0]
    gain = gain_ref[...]
    for part in (1, 0):
        span = pl.ds(part * rows, rows)
        values = tokens_ref[at_ref[2]] if part == 0 else far_ref[...]
        scaled, root = normalize(values.astype(FULL))
        back = normalize_back(mul_t(dqkv_ref[span, :], weight[...]), gain, scaled, root)
        grad = dx1_ref[span, :] + back
        if part == 1:
            grad_far_ref[...] = grad.astype(LOW)
        else:
            grad_own[...] = grad
    put(grad_own, grad_ref.at[at_ref[2]], out_sem.at[0]).wait()


def shaped(*shape, kind=LOW):
    return jax.ShapeDtypeStruct(shape, kind)


IN_SMEM = pl.BlockSpec(memory_space=pltpu.SMEM)
IN_VMEM = pl.BlockSpec(memory_space=pltpu.VMEM)
IN_ANY = pl.BlockSpec(memory_space=pl.ANY)


def params(mebibytes):
    return pltpu.CompilerParams(vmem_limit_bytes=int(mebibytes * 1024 * 1024))


def call(kernel, args, in_specs, out_shape, out_specs, late=(), **options):
    if not isinstance(out_shape, tuple):
        out_shape, out_specs = (out_shape,), (out_specs,)
    count, skip, outs = len(args), len(late), len(out_shape)

    def body(*refs):
        outs_at = count + skip
        return kernel(*refs[:count], *refs[outs_at : outs_at + outs], *refs[outs_at + outs + 1 :])

    return pl.pallas_call(
        body,
        in_specs=list(in_specs) + [IN_ANY] * skip,
        out_shape=out_shape + (shaped(8, 128, kind=FULL),),
        out_specs=out_specs + (IN_ANY,),
        **options,
    )(*args, *late)


def gate(values, late=(), weight=0):
    hint = {}
    if weight:
        hint["cost_estimate"] = pl.CostEstimate(
            flops=weight, transcendentals=0, bytes_accessed=0
        )
    return call(
        lambda *refs: None,
        values,
        late=late,
        out_shape=tuple(jax.ShapeDtypeStruct(v.shape, v.dtype) for v in values),
        in_specs=[IN_ANY] * len(values),
        out_specs=(IN_ANY,) * len(values),
        input_output_aliases={i: i for i in range(len(values))},
        compiler_params=params(1),
        name="gate",
        **hint,
    )[: len(values)]


def prepare_first(at, weight):
    rows, width = weight.shape
    return call(
        prepare_first_kernel,
        (at, weight),
        out_shape=(shaped(rows, width), shaped(rows // 2, width)),
        in_specs=[IN_SMEM, IN_VMEM],
        out_specs=(IN_VMEM,) * 2,
        compiler_params=params(8),
        name="prepare_first",
    )


def prepare_rest(at, w_in, w_out, w_down, cotangent, tokens, late):
    rows, width = w_out.shape
    folded = 2 * width + width // 2
    return call(
        prepare_rest_kernel,
        (at, w_in, w_out, w_down, cotangent, tokens),
        late=late,
        out_shape=(
            shaped(*w_in.shape),
            shaped(rows // 2, w_in.shape[1]),
            shaped(rows, folded),
            shaped(rows // 2, folded),
            shaped(*cotangent.shape[1:]),
            shaped(*tokens.shape[1:]),
        ),
        in_specs=[IN_SMEM] + [IN_VMEM] * 5,
        out_specs=(IN_VMEM,) * 6,
        compiler_params=params(14),
        name="prepare_rest",
    )


def project(at, tokens, far, gain, cos_part, sin_part, blocks, late):
    rows, width = 2 * far.shape[0], far.shape[1]
    return call(
        project_kernel,
        (at, tokens, far, gain, cos_part, sin_part, *blocks),
        late=late,
        out_shape=(shaped(rows, width), shaped(rows, width), shaped(2, rows, width)),
        in_specs=[IN_SMEM] + [IN_VMEM] * 5 + [IN_ANY] * 6,
        out_specs=(IN_VMEM,) * 3,
        scratch_shapes=[pltpu.VMEM((width, 3 * width), LOW), pltpu.SemaphoreType.DMA((6,))],
        compiler_params=params(16),
        name="project",
    )


def attend(first, count, query, near, far, mark_query, mark_key, late=()):
    rows = query.shape[0]
    row_spec = pl.BlockSpec((rows, PAIR), lambda i: (0, i + first))
    kv_spec = pl.BlockSpec((2, rows, PAIR), lambda i: (0, 0, i + first))
    out_spec = pl.BlockSpec((rows, PAIR), lambda i: (0, i))
    return call(
        attend_kernel,
        (query, near, far, mark_query, mark_key),
        late=late,
        grid=(count,),
        out_shape=(shaped(rows, count * PAIR), shaped(rows, count * PAIR)),
        in_specs=[
            row_spec,
            kv_spec,
            kv_spec,
            pl.BlockSpec((rows, PAIR), lambda i: (0, 0)),
            pl.BlockSpec((2 * rows, PAIR), lambda i: (0, 0)),
        ],
        out_specs=(out_spec, out_spec),
        compiler_params=params(16),
        name="attend",
    )


def attend_back(
    first, first_o, count, query, near, far, extra, o, mark_key, do, cos_part, sin_part, late=()
):
    rows = query.shape[0]
    row_spec = pl.BlockSpec((rows, PAIR), lambda i: (0, i + first))
    o_spec = pl.BlockSpec((rows, PAIR), lambda i: (0, i + first_o))
    kv_spec = pl.BlockSpec((2, rows, PAIR), lambda i: (0, 0, i + first))
    fixed = pl.BlockSpec((rows, PAIR), lambda i: (0, 0))
    out_row = pl.BlockSpec((rows, PAIR), lambda i: (0, i))
    out_kv = pl.BlockSpec((2, rows, PAIR), lambda i: (0, 0, i))
    return call(
        attend_back_kernel,
        (query, near, far, extra, mark_key, o, do, cos_part, sin_part),
        late=late,
        grid=(count,),
        out_shape=(
            shaped(rows, count * PAIR),
            shaped(2, rows, count * PAIR),
            shaped(2, rows, count * PAIR),
        ),
        in_specs=[
            row_spec,
            kv_spec,
            kv_spec,
            o_spec,
            pl.BlockSpec((2 * rows, PAIR), lambda i: (0, 0)),
            o_spec,
            row_spec,
            fixed,
            fixed,
        ],
        out_specs=(out_row, out_kv, out_kv),
        compiler_params=params(20),
        name="attend_back",
    )


def middle(at, live, tokens, far, cot, cot_far, o_a, o_b, gain, blocks_in, blocks_od):
    half, width = far.shape
    rows, share = 2 * half, width // 4
    units = blocks_in[0].shape[1] // 2
    total = 2 * units + blocks_od[0].shape[1]
    assert units == 4 * (share + share // 2)
    low = lambda *shape: pltpu.VMEM(shape, LOW)
    return call(
        middle_kernel,
        (at, live, tokens, far, cot, cot_far, o_a, o_b, gain, *blocks_in, *blocks_od),
        out_shape=(
            shaped(2, half, width),
            shaped(half, width),
            shaped(rows, width, kind=FULL),
            shaped(rows, width),
            shaped(2, share, total),
            shaped(2, share, total),
        ),
        in_specs=[IN_SMEM] * 2 + [IN_VMEM] * 7 + [IN_ANY] * 12,
        out_specs=(IN_ANY,) * 6,
        scratch_shapes=[
            low(width, width),
            low(width, 2 * units),
            low(units, width),
            low(rows, width),
            low(width, rows),
            low(width, rows),
            low(units, rows),
            low(rows, width),
            low(rows, 2 * units),
            low(rows, width),
            low(rows, width),
            pltpu.VMEM((rows, width), FULL),
            low(rows, width),
            low(2, share, total),
            low(2, share, total),
            pltpu.SemaphoreType.DMA((6,)),
            pltpu.SemaphoreType.DMA((20,)),
            pltpu.SemaphoreType.DMA((10,)),
        ],
        compiler_params=params(40),
        name="middle",
    )


def qkv_send(at, normed, dq, own, got, cos_part, sin_part, late):
    rows, width = normed.shape
    share = width // 4
    return call(
        functools.partial(send_kernel, len(dq)),
        (at, normed, *dq, *own, *got, cos_part, sin_part),
        late=late,
        out_shape=(
            shaped(rows, 3 * width),
            shaped(width, rows),
            shaped(2, share, 3 * width),
        ),
        in_specs=[IN_SMEM] + [IN_VMEM] * (3 + 3 * len(dq)),
        out_specs=(IN_ANY,) * 3,
        scratch_shapes=[
            pltpu.VMEM((rows, 3 * width), LOW),
            pltpu.VMEM((width, rows), LOW),
            pltpu.VMEM((2, share, 3 * width), LOW),
            pltpu.SemaphoreType.DMA((4,)),
        ],
        compiler_params=params(20),
        name="qkv_send",
    )


def qkv_keep(at, normed_t, dqkv, late):
    width, rows = normed_t.shape
    share = width // 4
    return call(
        keep_kernel,
        (at, normed_t, dqkv),
        late=late,
        out_shape=shaped(2, share, 3 * width),
        in_specs=[IN_SMEM] + [IN_VMEM] * 2,
        out_specs=IN_ANY,
        scratch_shapes=[
            pltpu.VMEM((2, share, 3 * width), LOW),
            pltpu.SemaphoreType.DMA((2,)),
        ],
        compiler_params=params(16),
        name="qkv_keep",
    )


def input_back(at, tokens, far, gain, dx1, dqkv, blocks, late):
    half, width = far.shape
    return call(
        input_kernel,
        (at, tokens, far, gain, dx1, dqkv, *blocks),
        late=late,
        out_shape=(shaped(2, half, width, kind=FULL), shaped(half, width)),
        in_specs=[IN_SMEM] + [IN_VMEM] * 5 + [IN_ANY] * 6,
        out_specs=(IN_ANY, IN_VMEM),
        scratch_shapes=[
            pltpu.VMEM((width, 3 * width), LOW),
            pltpu.VMEM((half, width), FULL),
            pltpu.SemaphoreType.DMA((6,)),
            pltpu.SemaphoreType.DMA((1,)),
        ],
        compiler_params=params(20),
        name="input_back",
    )


def first_sums_kernel(at_ref, keep, got, own_a, far_a, mine_b, give_b):
    cut, short = far_a.shape[0], give_b.shape[1]

    def add(block, start, size):
        span = pl.ds(start, size)
        return (keep[block, span, :].astype(FULL) + got[block, span, :].astype(FULL)).astype(LOW)

    far_a[...] = add(1, 0, cut)
    for block in range(2):
        give_b[block] = add(block, pl.multiple_of(cut + (1 - at_ref[1]) * short, short), short)
        mine_b[block] = add(block, pl.multiple_of(cut + at_ref[1] * short, short), short)
    own_a[...] = add(0, 0, cut)


def first_sums(at, keep, got, late=()):
    _, rows, width = keep.shape
    cut, short = rows // 2, rows // 4
    return call(
        first_sums_kernel,
        (at, keep, got),
        late=late,
        out_shape=(shaped(cut, width),) * 2 + (shaped(2, short, width),) * 2,
        in_specs=[IN_SMEM] + [IN_VMEM] * 2,
        out_specs=(IN_VMEM,) * 4,
        compiler_params=params(20),
        name="first_sums",
    )


def second_sums_kernel(at_ref, own_a, got_a, mine_b, got_b, mine_a, give_a, near_b, far_b):
    short = mine_a.shape[0]
    for start, out in ((1 - at_ref[1], give_a), (at_ref[1], mine_a)):
        span = pl.ds(pl.multiple_of(start * short, short), short)
        out[...] = (own_a[span, :].astype(FULL) + got_a[span, :].astype(FULL)).astype(LOW)
    for block, out in ((1, far_b), (0, near_b)):
        out[...] = (mine_b[block].astype(FULL) + got_b[block].astype(FULL)).astype(LOW)


def second_sums(at, own_a, got_a, mine_b, got_b, late=()):
    _, short, width = mine_b.shape
    return call(
        second_sums_kernel,
        (at, own_a, got_a, mine_b, got_b),
        late=late,
        out_shape=(shaped(short, width),) * 4,
        in_specs=[IN_SMEM] + [IN_VMEM] * 4,
        out_specs=(IN_VMEM,) * 4,
        compiler_params=params(12),
        name="second_sums",
    )


def third_sums_kernel(lanes, mine_a, got_a, near_b, got_b, *outs):
    upper = mine_a[...].astype(FULL) + got_a[...].astype(FULL)
    lower = near_b[...].astype(FULL) + got_b[...].astype(FULL)
    total = jnp.concatenate([upper, lower])
    first = 0
    for out, width in zip(outs, lanes):
        count, rows, _ = out.shape
        for i in range(count):
            out[i] = total[i * rows : (i + 1) * rows, first : first + width].astype(LOW)
        first += width


def third_sums(count, lanes, mine_a, got_a, near_b, got_b, late=()):
    rows = 2 * mine_a.shape[0] // count
    return call(
        functools.partial(third_sums_kernel, lanes),
        (mine_a, got_a, near_b, got_b),
        late=late,
        out_shape=tuple(shaped(count, rows, width) for width in lanes),
        in_specs=[IN_VMEM] * 4,
        out_specs=(IN_VMEM,) * len(lanes),
        compiler_params=params(12),
        name="third_sums",
    )


def squares_kernel(at_ref, qkv, w_qkv, inner, w_in, gains, folded, out):
    total = jnp.sum(jnp.square(folded[...].astype(FULL)), keepdims=True)
    rows = qkv.shape[0]
    shape = (rows, gains.shape[1])
    offset = lax.broadcasted_iota(jnp.int32, shape, 1) - lax.broadcasted_iota(jnp.int32, shape, 0)
    for i, (piece, weight) in enumerate(((qkv, w_qkv), (inner, w_in))):
        start = at_ref[3 + i]
        span = slice(0, rows)
        if weight.shape[0] != rows:
            span = pl.ds(pl.multiple_of(start, 8), rows)
        values = piece[...].astype(FULL)
        sums = jnp.sum(weight[span, :].astype(LOW).astype(FULL) * values, axis=1, keepdims=True)
        gain = gains[i : i + 1, :].astype(LOW).astype(FULL)
        gain = jnp.sum(jnp.where(offset == start, gain, 0.0), axis=1, keepdims=True)
        total += jnp.sum(jnp.square(values), keepdims=True)
        total += jnp.sum(jnp.square(sums / gain), keepdims=True)
    out[...] = jnp.broadcast_to(total, out.shape)


def squares(*args):
    return call(
        squares_kernel,
        args,
        out_shape=shaped(8, 128, kind=FULL),
        in_specs=[IN_SMEM] + [IN_VMEM] * (len(args) - 1),
        out_specs=IN_VMEM,
        compiler_params=params(10),
        name="squares",
    )


def clip_factor(square_ref):
    norm = jnp.sqrt(square_ref[:1, :1])
    return jnp.minimum(1.0, CLIP_LIMIT / (norm + 1e-06))


class Updates:
    def __init__(self, factor, sem):
        self.factor, self.sem, self.copies = factor, sem, []

    def block(self, index, weight, first, second, outs, targets, gradient, rows, lanes=None):
        span = (rows, lanes if lanes is not None else slice(None))
        results = adam_step(
            weight[span], first[span], second[span], gradient, self.factor,
            STEP_RATES[index], DECAY_RATES[index],
        )
        for result, out, target in zip(results, outs, targets):
            out[span] = result
            self.copies.append(put(out.at[span], target.at[span], self.sem.at[len(self.copies)]))


def quarters(at_ref, mine_ref, other_ref):
    short = mine_ref.shape[0] // 2
    for i in range(4):
        span = slice((i // 2) * short, (i // 2 + 1) * short)
        mine, other = mine_ref[span, :].astype(FULL), other_ref[span, :].astype(FULL)
        yield i, slice(i * short, (i + 1) * short), jnp.where(at_ref[1] == i % 2, mine, other)


def gain_row(weight, gradient, start, shape):
    sums = jnp.sum(weight.astype(LOW).astype(FULL) * gradient, axis=1, keepdims=True)
    shape = (weight.shape[0], shape[1])
    offset = lax.broadcasted_iota(jnp.int32, shape, 1) - lax.broadcasted_iota(jnp.int32, shape, 0)
    return jnp.sum(jnp.where(offset == start, sums, 0.0), axis=0, keepdims=True)


def update_first_kernel(at_ref, square_ref, q_w, q_m, q_v, q_mine, q_other,
                        o_w, o_m, o_v, d_w, d_m, d_v, f_mine, f_other,
                        q_w_out, q_m_out, q_v_out, o_w_out, o_m_out, o_v_out,
                        d_w_out, d_m_out, d_v_out, row_ref,
                        q_w_new, q_m_new, q_v_new, o_w_new, o_m_new, o_v_new,
                        d_w_new, d_m_new, d_v_new, sem):
    updates = Updates(clip_factor(square_ref), sem)
    rows, width = o_w.shape
    row = jnp.zeros(row_ref.shape, FULL)
    for i, span, gradient in quarters(at_ref, q_mine, q_other):
        updates.block(0, q_w, q_m, q_v, (q_w_new, q_m_new, q_v_new),
                      (q_w_out, q_m_out, q_v_out), gradient, span)
        row += gain_row(q_w[span, :], gradient, span.start, row_ref.shape)
    row_ref[...] = row
    for i, span, gradient in quarters(at_ref, f_mine, f_other):
        updates.block(1, o_w, o_m, o_v, (o_w_new, o_m_new, o_v_new),
                      (o_w_out, o_m_out, o_v_out), gradient[:, :width], span)
        down = (3, d_w, d_m, d_v, (d_w_new, d_m_new, d_v_new), (d_w_out, d_m_out, d_v_out))
        updates.block(*down, gradient[:, width : 2 * width], span)
        short = span.stop - span.start
        start = rows + (i % 2) * short
        lanes = slice((i // 2) * (width // 2), (i // 2 + 1) * (width // 2))
        updates.block(*down, gradient[:, 2 * width :], slice(start, start + short), lanes)
    wait_all(updates.copies)


def update_first(at, square, qkv, qkv_parts, out, down, folded_parts):
    like = [jax.ShapeDtypeStruct(v.shape, FULL) for v in (*qkv, *out, *down)]
    return call(
        update_first_kernel,
        (at, square, *qkv, *qkv_parts, *out, *down, *folded_parts),
        out_shape=(*like, shaped(1, qkv[0].shape[0], kind=FULL)),
        in_specs=[IN_SMEM] + [IN_VMEM] * 14,
        out_specs=(IN_ANY,) * 9 + (IN_VMEM,),
        scratch_shapes=[pltpu.VMEM(v.shape, FULL) for v in like]
        + [pltpu.SemaphoreType.DMA((48,))],
        compiler_params=params(28),
        name="update_first",
    )


def update_second_kernel(at_ref, square_ref, i_w, i_m, i_v, i_mine, i_other, row_ref,
                         g_w, g_m, g_v, i_w_out, i_m_out, i_v_out, g_w_out, g_m_out, g_v_out,
                         i_w_new, i_m_new, i_v_new, sem):
    updates = Updates(clip_factor(square_ref), sem)
    row = jnp.zeros(row_ref.shape, FULL)
    for i, span, gradient in quarters(at_ref, i_mine, i_other):
        updates.block(2, i_w, i_m, i_v, (i_w_new, i_m_new, i_v_new),
                      (i_w_out, i_m_out, i_v_out), gradient, span)
        row += gain_row(i_w[span, :], gradient, span.start, row_ref.shape)
    for i, values in enumerate((row_ref[...], row)):
        line = slice(i, i + 1)
        gradient = values / g_w[line, :].astype(LOW).astype(FULL)
        g_w_out[line, :], g_m_out[line, :], g_v_out[line, :] = adam_step(
            g_w[line, :], g_m[line, :], g_v[line, :], gradient, updates.factor,
            STEP_RATES[4], DECAY_RATES[4],
        )
    wait_all(updates.copies)


def update_second(at, square, inner, inner_parts, row, gains):
    like = [jax.ShapeDtypeStruct(v.shape, FULL) for v in inner]
    return call(
        update_second_kernel,
        (at, square, *inner, *inner_parts, row, *gains),
        out_shape=(*like, *[jax.ShapeDtypeStruct(v.shape, FULL) for v in gains]),
        in_specs=[IN_SMEM] + [IN_VMEM] * 10,
        out_specs=(IN_ANY,) * 3 + (IN_VMEM,) * 3,
        scratch_shapes=[pltpu.VMEM(v.shape, FULL) for v in like]
        + [pltpu.SemaphoreType.DMA((12,))],
        compiler_params=params(18),
        name="update_second",
    )


def low_sum(*values):
    return sum(value.astype(FULL) for value in values).astype(LOW)


def index(value, i):
    return lax.dynamic_index_in_dim(value, i, 0, keepdims=False)


def make(dp_count, seq_count):
    assert seq_count == 4 and dp_count % 4 == 0 and dp_count & (dp_count - 1) == 0
    bits = dp_count.bit_length() - 1
    ones = [(shift, 1) for shift in range(1, bits)]
    twos = [(shift, min(2, bits - shift)) for shift in range(1, bits, 2)]
    count = dp_count // 2

    def trade(value, axis, bit):
        size = seq_count if axis == "seq" else dp_count
        return lax.ppermute(value, axis, [(i, i ^ bit) for i in range(size)])

    def fields(group, steps):
        for shift, width in steps:
            yield shift, 1 << width, (group >> shift) & ((1 << width) - 1)

    def sum_steps(value, group, steps, lates=()):
        for i, (shift, size, mine) in enumerate(fields(group, steps)):
            parts = value.reshape((size, value.shape[0] // size) + value.shape[1:])
            got = [trade(index(parts, mine ^ k), "dp", k << shift) for k in range(1, size)]
            if i < len(lates) and lates[i]:
                got = gate(got, lates[i])
            value = low_sum(index(parts, mine), *got)
        return value[0]

    def piece_row(group, steps, share):
        at = 0
        for _, size, mine in fields(group, steps):
            at = at * size + mine
        quarter, row = share // 4, at * (share // 2 // count)
        return (row // quarter) * 2 * quarter + (group & 1) * quarter + row % quarter

    def join_steps(piece, group, steps, lates=()):
        value, came = piece[None], []
        for i, (shift, size, mine) in enumerate(list(fields(group, steps))[::-1]):
            got = [trade(value, "dp", k << shift) for k in range(1, size)]
            came.append(got)
            if i < len(lates) and lates[i]:
                got = gate(got, lates[i])
            stack = jnp.stack([value, *got])
            value = jnp.concatenate([index(stack, mine ^ k) for k in range(size)])
        return value, came

    def on_device(
        tokens, cotangent, segments, valid,
        w_qkv, w_out, w_in, w_down, gains,
        m_qkv, m_out, m_in, m_down, m_gains,
        v_qkv, v_out, v_in, v_down, v_gains,
    ):
        place = lax.axis_index("seq")
        group = lax.axis_index("dp")
        slot = place >> 1
        half = group & 1
        local_len, width = tokens.shape[1:]
        rows = 2 * local_len
        share = w_qkv.shape[0]
        at = jnp.stack(
            [place, half, slot, piece_row(group, twos, share), piece_row(group, ones, share)]
        )

        low_qkv, half_qkv, begun = prepare_first(at, w_qkv)
        (far_qa,) = gate((trade(half_qkv, "seq", 2),), weight=10 * WEIGHT)
        near_q = trade(low_qkv, "seq", 1)
        low_in, half_in, low_od, half_od, their_cot, their_tokens, _ = prepare_rest(
            at, w_in, w_out, w_down, cotangent, tokens, (begun,)
        )
        low_gains = gains.astype(LOW)
        far = trade(their_tokens, "seq", 2)
        (gain_far,) = gate((trade(low_gains, "seq", 2),), weight=20 * WEIGHT)
        far_qb = trade(far_qa, "dp", 1)
        near_qa = trade(far_qa, "seq", 1)
        near_qb = trade(far_qb, "seq", 1)
        (gain_far,) = gate((gain_far,), (far_qb,))
        gain_near = trade(jnp.stack([low_gains, gain_far]), "seq", 1)
        gain_stack = jnp.stack([low_gains, gain_near[0], gain_far, gain_near[1]])
        gain_low = jnp.concatenate(
            [index(gain_stack, b ^ place) for b in range(4)], axis=1
        ).astype(FULL)
        blocks_qkv = (low_qkv, near_q, far_qa, far_qb, near_qa, near_qb)
        low_in, low_od, half_in = gate((low_in, low_od, half_in), (far_qa,))
        near_i = trade(low_in, "seq", 1)
        near_o = trade(low_od, "seq", 1)
        (far_ia,) = gate((trade(half_in, "seq", 2),), weight=10 * WEIGHT)
        (half_od,) = gate((half_od,), (far,))

        seg = index(segments, slot)
        positions = doc_positions(seg).reshape(4, local_len)
        seg = seg.reshape(4, local_len)
        chunks = [place, place ^ 2, place ^ 1, place ^ 3]
        seg_keys = jnp.concatenate([index(seg, c) for c in chunks])
        pos = jnp.concatenate([index(positions, c) for c in chunks[:2]])
        cos_part, sin_part = rope_tables(pos)
        lane = jnp.arange(PAIR, dtype=jnp.int32)[None] % HEAD_DIM
        same = seg_keys[:, None] == lane
        mark_key = jnp.where(lane < DOCS, 1.0 - same, (lane < DOCS + 3) * 1.0).astype(LOW)
        mark_query = jnp.where((lane < DOCS) & same[:rows], NEG_FILL, 0.0).astype(LOW)
        live = lax.dynamic_index_in_dim(valid, slot, 0, keepdims=True).astype(FULL)

        normed, query, kv, _ = project(
            at, tokens, far, gain_low[:1], cos_part, sin_part, blocks_qkv,
            (far_ia, mark_key, mark_query),
        )
        kv_far = trade(kv, "seq", 1)
        far_oa = trade(half_od, "seq", 2)
        far_ib = trade(far_ia, "dp", 1)
        near_ia = trade(far_ia, "seq", 1)
        (cot_far,) = gate((trade(their_cot, "seq", 2),), weight=WEIGHT)
        pairs = width // PAIR
        early = 2
        args = (query, kv, kv_far, mark_query, mark_key)
        o_a, extra_a, done_a = attend(0, early, *args)
        far_oa, far_ib = gate((far_oa, far_ib), (done_a,), weight=10 * WEIGHT)
        far_ob = trade(far_oa, "dp", 1)
        near_oa = trade(far_oa, "seq", 1)
        near_ib = trade(far_ib, "seq", 1)
        o_b, extra_b, done_b = attend(early, pairs - early, *args, late=(done_a, far_oa, near_ia))
        (far_ob,) = gate((far_ob,), (done_b,))
        near_ob = trade(far_ob, "seq", 1)
        blocks_in = (low_in, near_i, far_ia, far_ib, near_ia, near_ib)
        blocks_od = (low_od, near_o, far_oa, far_ob, near_oa, near_ob)

        mixed, mixed_far, dx1, do, keep_rest, send_rest, _ = middle(
            at, live, tokens, far, cotangent, cot_far, o_a, o_b, gain_low[1:], blocks_in, blocks_od
        )
        got_rest = trade(send_rest, "seq", 1)
        two = pairs // 3
        near_args = (query, kv, kv_far)
        back_args = (mark_key, do, cos_part, sin_part)
        dq0, own0, give0, back0 = attend_back(0, 0, two, *near_args, extra_a, o_a, *back_args)
        *r1, r1_done = first_sums(at, keep_rest, got_rest, late=(back0,))
        got_ra, got_rb = trade(r1[1], "seq", 2), trade(r1[3], "dp", 1)
        got0 = trade(give0, "seq", 1)
        dq1, own1, give1, back1 = attend_back(
            two, two - early, two, *near_args, extra_b, o_b, *back_args, late=(r1_done,)
        )
        got1 = trade(give1, "seq", 1)
        (mixed_far,) = gate((mixed_far,), (back1,))
        mixed_far = trade(mixed_far, "seq", 2)
        dq2, own2, give2, back2 = attend_back(
            2 * two, 2 * two - early, pairs - 2 * two, *near_args, extra_b, o_b, *back_args,
            late=(back1,),
        )
        got2 = trade(give2, "seq", 1)
        *r2, r2_done = second_sums(at, r1[0], got_ra, r1[2], got_rb, late=(back2,))
        got_ra, got_rb = gate(
            (trade(r2[1], "dp", 1), trade(r2[3], "seq", 2)), weight=WEIGHT
        )
        dqkv, normed_t, send_qkv, _ = qkv_send(
            at, normed, (dq0, dq1, dq2), (own0, own1, own2), (got0, got1, got2),
            cos_part, sin_part, late=(r2_done,),
        )
        got_qkv = trade(send_qkv, "seq", 1)
        keep_qkv, _ = qkv_keep(at, normed_t, dqkv, late=(mixed_far,))
        *q1, q1_done = first_sums(at, keep_qkv, got_qkv)
        got_qa, got_qb = trade(q1[1], "seq", 2), trade(q1[3], "dp", 1)
        inner_lanes = w_in.shape[1]
        lanes = (inner_lanes, keep_rest.shape[2] - inner_lanes)
        inner, folded, r3_done = third_sums(
            count, lanes, r2[0], got_ra, r2[2], got_rb, late=(q1_done,)
        )
        grad, grad_far, grad_done = input_back(
            at, tokens, far, gain_low[:1], dx1, dqkv, blocks_qkv, late=(r3_done,)
        )
        *q2, q2_done = second_sums(at, q1[0], got_qa, q1[2], got_qb, late=(grad_done,))
        got_qa, got_qb = gate(
            (trade(q2[1], "dp", 1), trade(q2[3], "seq", 2)), weight=10 * WEIGHT
        )
        qkv, q3_done = third_sums(count, (3 * width,), q2[0], got_qa, q2[2], got_qb)
        inner_piece = sum_steps(inner, group, ones, ((grad_done,), (q2_done,)))
        folded_piece = sum_steps(folded, group, ones, ((grad_done,), (q2_done,)))
        qkv_piece = sum_steps(qkv, group, twos)
        qkv_mine, came = join_steps(qkv_piece, group, twos)
        inner_mine, _ = join_steps(inner_piece, group, ones, ((q3_done,), (qkv_piece,)))
        folded_mine, _ = join_steps(folded_piece, group, ones, ((q3_done,), (qkv_piece,)))
        (grad_far,) = gate((grad_far,), tuple(came[0]))
        grad_far = trade(grad_far, "seq", 2)

        behind = [w_qkv, w_in]
        if qkv_piece.shape[0] % 8:
            behind = [
                lax.dynamic_slice_in_dim(value, at[3 + i], qkv_piece.shape[0], 0)
                for i, value in enumerate(behind)
            ]
        square, _ = squares(
            at, qkv_piece, behind[0], inner_piece, behind[1], gains, folded_piece
        )
        square = square + trade(square, "seq", 2)
        (square,) = gate((square,), tuple(came[0]))
        square = square + trade(square, "seq", 1)
        for bit in range(bits):
            square = square + trade(square, "dp", dp_count >> (bit + 1))
        grad_norm = jnp.sqrt(square[0, 0])
        def both_halves(mine):
            mine = mine.reshape((-1,) + mine.shape[2:])
            return mine, gate((trade(mine, "dp", 1),), weight=WEIGHT)[0]

        (new_qkv, first_qkv, second_qkv, new_out, first_out, second_out,
         new_down, first_down, second_down, row, _) = update_first(
            at, square, (w_qkv, m_qkv, v_qkv), both_halves(qkv_mine),
            (w_out, m_out, v_out), (w_down, m_down, v_down), both_halves(folded_mine),
        )
        (new_in, first_in, second_in, new_gains, first_gains, second_gains, _) = update_second(
            at, square, (w_in, m_in, v_in), both_halves(inner_mine), row,
            (gains, m_gains, v_gains),
        )

        def fill(whole, theirs):
            theirs = theirs.astype(whole.dtype)[None]
            return lax.dynamic_update_slice(whole, theirs, (1 - slot, 0, 0))

        return (
            fill(mixed, mixed_far),
            fill(grad, grad_far),
            grad_norm,
            new_qkv, new_out, new_in, new_down, new_gains,
            first_qkv, first_out, first_in, first_down, first_gains,
            second_qkv, second_out, second_in, second_down, second_gains,
        )

    return on_device


def solution(mesh):
    rows, matrix, gain = P("dp", "seq", None), P("seq", None), P(None, "seq")
    weights = (matrix,) * 4 + (gain,)
    return jax.shard_map(
        make(mesh.shape["dp"], mesh.shape["seq"]),
        mesh=mesh,
        in_specs=(rows, rows, P("dp", None), P("dp")) + weights * 3,
        out_specs=(rows, rows, P()) + weights * 3,
        check_vma=False,
    )
```

```python
import functools
import math

import jax
import jax.numpy as jnp
from jax import lax
from jax.experimental import pallas as pl
from jax.experimental.pallas import tpu as pltpu
from jax.sharding import PartitionSpec as P

HEADS = 12
HEAD_DIM = 64
PAIR = 2 * HEAD_DIM
STEP_COUNT = 10
EPS_NORM = 1e-05
ROPE_BASE = 160000.0
NEG_FILL = -1e30
CLIP_LIMIT = 10.0
BETA_FIRST = 0.9
BETA_SECOND = 0.98
EPS_ADAM = 1e-06
STEP_RATES = (0.1, 0.5, 0.1, 0.1, 1.0)
DECAY_RATES = (0.01, 0.01, 0.01, 0.01, 0.0)
DOCS = 5
LOW = jnp.bfloat16
FULL = jnp.float32
SCALE = 1.0 / math.sqrt(HEAD_DIM)
WEIGHT = 20_000_000_000


def doc_positions(segment_ids):
    seq_len = segment_ids.shape[-1]
    places = jnp.arange(seq_len, dtype=jnp.int32)
    first_mark = jnp.ones((1,), jnp.bool_)
    change = jnp.concatenate([first_mark, segment_ids[1:] != segment_ids[:-1]])
    starts = lax.cummax(jnp.where(change, places, 0), axis=0)
    return places - starts


def rope_tables(positions):
    half_dim = HEAD_DIM // 2
    exponents = jnp.arange(half_dim, dtype=jnp.float32) * (2.0 / HEAD_DIM)
    inv_freq = ROPE_BASE ** (-exponents)
    angles = positions.astype(jnp.float32)[:, None] * inv_freq
    cos_part, sin_part = jnp.cos(angles), jnp.sin(angles)
    return (
        jnp.concatenate([cos_part] * 4, axis=1),
        jnp.concatenate([-sin_part, sin_part] * 2, axis=1),
    )


def adam_step(weight, first_old, second_old, gradient, factor, step_rate, decay_rate):
    clipped = gradient * factor
    first_new = BETA_FIRST * first_old + (1.0 - BETA_FIRST) * clipped
    second_new = BETA_SECOND * second_old + (1.0 - BETA_SECOND) * clipped * clipped
    root = second_new * lax.rsqrt(second_new) * (1.0 - BETA_SECOND**STEP_COUNT) ** -0.5
    step = first_new * (step_rate / (1.0 - BETA_FIRST**STEP_COUNT)) / (root + EPS_ADAM)
    return (weight * (1.0 - step_rate * decay_rate) - step, first_new, second_new)


def mul(left, right):
    return lax.dot_general(left, right, (((1,), (0,)), ((), ())), preferred_element_type=FULL)


def mul_t(left, right):
    return lax.dot_general(left, right, (((1,), (1,)), ((), ())), preferred_element_type=FULL)


def normalize(values):
    centered = values - jnp.mean(values, axis=-1, keepdims=True)
    root = lax.rsqrt(jnp.mean(centered * centered, axis=-1, keepdims=True) + EPS_NORM)
    return centered * root, root


def normalize_back(grad, gain, scaled, root):
    t = grad * gain
    back = root * (
        t
        - jnp.mean(t, axis=-1, keepdims=True)
        - scaled * jnp.mean(t * scaled, axis=-1, keepdims=True)
    )
    return back


def turn(values, cos_part, sin_part):
    lane = lax.broadcasted_iota(jnp.int32, values.shape, 1)
    swapped = jnp.where(
        lane % HEAD_DIM < HEAD_DIM // 2,
        pltpu.roll(values, PAIR - HEAD_DIM // 2, 1),
        pltpu.roll(values, HEAD_DIM // 2, 1),
    )
    return values * cos_part + swapped * sin_part


def three_parts(values):
    high = values.astype(LOW).astype(FULL)
    rest = values - high
    mid = rest.astype(LOW).astype(FULL)
    return high, mid, rest - mid


def wait_all(copies):
    for copy in copies:
        copy.wait()


def put(source, target, sem):
    copy = pltpu.make_async_copy(source, target, sem)
    copy.start()
    return copy


PIECES = ((0, None), (1, None), (2, 0), (2, 1), (3, 0), (3, 1))


def load_blocks(at_ref, blocks, whole, sem):
    rows = blocks[0].shape[0]
    copies = []
    for i, (bits, part) in enumerate(PIECES):
        start = (at_ref[0] ^ bits) * rows
        size = rows
        if part is not None:
            size = rows // 2
            start += (at_ref[1] ^ part) * size
        target = whole.at[pl.ds(pl.multiple_of(start, size), size), :]
        copies.append(put(blocks[i], target, sem.at[i]))
    return copies


def load_folded(at_ref, blocks, w_out, w_down, sem):
    rows, width = blocks[0].shape[0], w_out.shape[1]
    short, last = rows // 2, width // 2
    copies = []

    def copy(source, target):
        copies.append(put(source, target, sem.at[len(copies)]))

    for i, (bits, part) in enumerate(PIECES):
        owner = at_ref[0] ^ bits
        base = owner * (rows + short)
        first = 0 if part is None else (at_ref[1] ^ part) * short
        size = rows if part is None else short
        for lanes, whole, start in ((0, w_out, owner * rows), (width, w_down, base)):
            span = pl.ds(pl.multiple_of(start + first, short), size)
            copy(blocks[i].at[:, pl.ds(lanes, width)], whole.at[span, :])
        span = pl.ds(pl.multiple_of(base + rows, short), short)
        if part is None:
            for fold in range(2):
                copy(
                    blocks[i].at[pl.ds(fold * short, short), pl.ds(2 * width, last)],
                    w_down.at[span, pl.ds(fold * last, last)],
                )
        else:
            lanes = pl.ds(pl.multiple_of((at_ref[1] ^ part) * last, last), last)
            copy(blocks[i].at[:, pl.ds(2 * width, last)], w_down.at[span, lanes])
    return copies


def fold(out, w_out, w_down, first):
    rows, width = w_out.shape
    short, last = rows // 2, width // 2
    out[:, first : first + width] = w_out[...].astype(LOW)
    out[:, first + width : first + 2 * width] = w_down[:rows, :].astype(LOW)
    for i in range(2):
        out[i * short : (i + 1) * short, first + 2 * width :] = w_down[
            rows:, i * last : (i + 1) * last
        ].astype(LOW)


def prepare_first_kernel(at_ref, w_ref, low_ref, half_ref):
    short = half_ref.shape[0]
    half_ref[...] = w_ref[pl.ds(pl.multiple_of(at_ref[1] * short, short), short), :].astype(LOW)
    low_ref[...] = w_ref[...].astype(LOW)


def prepare_rest_kernel(at_ref, in_ref, out_ref, down_ref, cot_ref, tokens_ref,
                        low_in, half_in, low_od, half_od, their_cot, their_tokens):
    their_tokens[...] = tokens_ref[1 - at_ref[2]]
    short = half_in.shape[0]
    span = pl.ds(pl.multiple_of(at_ref[1] * short, short), short)
    low_in[...] = in_ref[...].astype(LOW)
    half_in[...] = in_ref[span, :].astype(LOW)
    fold(low_od, out_ref, down_ref, 0)
    half_od[...] = low_od[span, :]
    their_cot[...] = cot_ref[1 - at_ref[2]]


def project_kernel(at_ref, tokens_ref, far_ref, gain_ref, cos_ref, sin_ref, w0, w1, w2, w3, w4, w5,
                   normed_ref, query_ref, kv_ref, weight, sem):
    copies = load_blocks(at_ref, (w0, w1, w2, w3, w4, w5), weight, sem)
    rows, width = far_ref.shape
    for part in range(2):
        values = tokens_ref[at_ref[2]] if part == 0 else far_ref[...]
        scaled, _ = normalize(values.astype(FULL))
        normed_ref[pl.ds(part * rows, rows), :] = (scaled * gain_ref[...]).astype(LOW)
    wait_all(copies)
    for part in range(2):
        span = pl.ds(part * rows, rows)
        normed = normed_ref[span, :]
        cos_part, sin_part = cos_ref[span, :], sin_ref[span, :]
        for pair in range(2 * width // PAIR):
            lanes = pl.ds(pair * PAIR, PAIR)
            if pair % 2 == 0:
                both = mul(normed, weight[:, pl.ds(pair * PAIR, 2 * PAIR)])
            raw = both[:, (pair % 2) * PAIR : (pair % 2 + 1) * PAIR]
            turned = turn(raw, cos_part, sin_part)
            if pair < width // PAIR:
                query_ref[span, lanes] = (turned * SCALE).astype(LOW)
            else:
                kv_ref[0, span, pl.ds(pair * PAIR - width, PAIR)] = turned.astype(LOW)
        kv_ref[1, span, :] = mul(normed, weight[:, 2 * width :]).astype(LOW)


def head_lanes(head, shape):
    lane = lax.broadcasted_iota(jnp.int32, shape, 1)
    return (lane < HEAD_DIM) if head == 0 else (lane >= HEAD_DIM)


def pick(head, inside, outside):
    return jnp.where(head_lanes(head, inside.shape), inside, outside)


def attend_kernel(query_ref, near_ref, far_ref, mark_query_ref, mark_key_ref, o_ref, extra_ref):
    rows = query_ref.shape[0]
    query = query_ref[...]
    mark_query = mark_query_ref[...]
    parts = [
        (near_ref[0], jnp.transpose(near_ref[1]), mark_key_ref[:rows, :]),
        (far_ref[0], jnp.transpose(far_ref[1]), mark_key_ref[rows:, :]),
    ]
    outs, logs = [], []
    for head in range(2):
        query_head = pick(head, query, mark_query)
        scores = [mul_t(pick(head, key, mark), query_head) for key, _, mark in parts]
        top = jnp.maximum(
            jnp.max(scores[0], axis=0, keepdims=True), jnp.max(scores[1], axis=0, keepdims=True)
        )
        exps = [jnp.exp(score - top) for score in scores]
        total = jnp.sum(exps[0], axis=0, keepdims=True) + jnp.sum(exps[1], axis=0, keepdims=True)
        span = slice(head * HEAD_DIM, (head + 1) * HEAD_DIM)
        out = sum(mul(value_t[span], e.astype(LOW)) for (_, value_t, _), e in zip(parts, exps))
        outs.append(out / total)
        logs.append(top + jnp.log(total))
    o_ref[...] = jnp.transpose(jnp.concatenate(outs)).astype(LOW)
    line = lax.broadcasted_iota(jnp.int32, (PAIR, rows), 0)
    extra = jnp.zeros((PAIR, rows), FULL)
    for head in range(2):
        base = DOCS + (HEAD_DIM if head == 0 else 0)
        for i, piece in enumerate(three_parts(-logs[head])):
            extra = jnp.where(line == base + i, piece, extra)
    extra_ref[...] = jnp.transpose(extra).astype(LOW) + mark_query


def attend_back_kernel(query_ref, near_ref, far_ref, extra_ref, mark_key_ref, o_ref, do_ref,
                       cos_ref, sin_ref, dq_ref, keep_ref, send_ref):
    rows = query_ref.shape[0]
    query, extra, do = query_ref[...], extra_ref[...], do_ref[...]
    inner_all = do.astype(FULL) * o_ref[...].astype(FULL)
    lane = lax.broadcasted_iota(jnp.int32, (rows, PAIR), 1)
    zero = jnp.zeros((rows, PAIR), LOW)
    grads_query = []
    sums = [[None, None], [None, None]]
    keys_t = [jnp.transpose(near_ref[0]), jnp.transpose(far_ref[0])]
    for head in range(2):
        inside = head_lanes(head, (rows, PAIR))
        inner = jnp.sum(jnp.where(inside, inner_all, 0.0), axis=1, keepdims=True)
        base = DOCS + (HEAD_DIM if head == 0 else 0)
        tail = jnp.zeros((rows, PAIR), FULL)
        for i, piece in enumerate(three_parts(-inner)):
            tail = jnp.where(lane == base + i, piece, tail)
        query_head = pick(head, query, extra)
        do_head = pick(head, do, tail.astype(LOW))
        query_only = pick(head, query, zero)
        do_only = pick(head, do, zero)
        span = slice(head * HEAD_DIM, (head + 1) * HEAD_DIM)
        grad_query = 0.0
        for part, ref in enumerate((near_ref, far_ref)):
            mark = mark_key_ref[pl.ds(part * rows, rows), :]
            probs = jnp.exp(mul_t(pick(head, ref[0], mark), query_head))
            grad_probs = mul_t(pick(head, ref[1], mark), do_head)
            grad_scores = (probs * grad_probs).astype(LOW)
            grad_value = mul(probs.astype(LOW), do_only)
            grad_key = mul(grad_scores, query_only)
            grad_query += mul(keys_t[part][span], grad_scores)
            if head == 0:
                sums[part] = [grad_key, grad_value]
            else:
                sums[part] = [sums[part][0] + grad_key, sums[part][1] + grad_value]
        grads_query.append(grad_query)
    turned = turn(
        jnp.transpose(jnp.concatenate(grads_query)) * SCALE, cos_ref[...], -sin_ref[...]
    )
    dq_ref[...] = turned.astype(LOW)
    for i in range(2):
        keep_ref[i] = sums[0][i].astype(LOW)
        send_ref[i] = sums[1][i].astype(LOW)


def middle_kernel(at_ref, live_ref, tokens_ref, far_ref, cot_ref, cot_far_ref, oa_ref, ob_ref,
                  gain_ref, i0, i1, i2, i3, i4, i5, d0, d1, d2, d3, d4, d5,
                  mixed_ref, mixed_far_ref, dx1_ref, do_ref, keep_ref, send_ref,
                  w_out, w_in, w_down, o_all, o_t, a2_t, h_t, dm_all, duw_all, db_all,
                  mixed, dx1_all, do_all, keep, send, sem, fold_sem, out_sem):
    place, slot, live = at_ref[0], at_ref[2], live_ref[0]
    copies_down = load_folded(at_ref, (d0, d1, d2, d3, d4, d5), w_out, w_down, fold_sem)
    copies_in = load_blocks(at_ref, (i0, i1, i2, i3, i4, i5), w_in, sem)
    rows, width = far_ref.shape
    share = width // 4
    short, units = share // 2, w_down.shape[0]
    gain = gain_ref[...]
    o_all[:, : oa_ref.shape[1]] = oa_ref[...]
    o_all[:, oa_ref.shape[1] :] = ob_ref[...]
    copies = []
    for part in range(2):
        span = pl.ds(part * rows, rows)
        o = o_all[span, :]
        values = tokens_ref[slot] if part == 0 else far_ref[...]
        if part == 0:
            wait_all(copies_down)
        x1 = values.astype(FULL) + live * mul(o, w_out[...])
        scaled, root = normalize(x1)
        a2 = (scaled * gain).astype(LOW)
        if part == 0:
            wait_all(copies_in)
        u = mul(a2, w_in[:, :units])
        w = mul(a2, w_in[:, units:])
        phi = 0.5 * (1.0 + lax.erf(u * math.sqrt(0.5)))
        gelu = u * phi
        h = (gelu * w).astype(LOW)
        mixed[span, :] = (x1 + live * mul(h, w_down[...])).astype(LOW)
        target = mixed_ref.at[slot] if part == 0 else mixed_far_ref
        copies.append(put(mixed.at[span, :], target, out_sem.at[len(copies)]))
        cot = (cot_ref[slot] if part == 0 else cot_far_ref[...]).astype(FULL)
        dm = (live * cot).astype(LOW)
        dh = mul_t(dm, w_down[...])
        slope = phi + u * (jnp.exp(-0.5 * u * u) * (1.0 / math.sqrt(2.0 * math.pi)))
        duw_all[span, :units] = (dh * w * slope).astype(LOW)
        duw_all[span, units:] = (dh * gelu).astype(LOW)
        da2 = mul_t(duw_all[span, :], w_in[...])
        dx1 = cot + normalize_back(da2, gain, scaled, root)
        dx1_all[span, :] = dx1
        copies.append(put(dx1_all.at[span, :], dx1_ref.at[span, :], out_sem.at[len(copies)]))
        db = (live * dx1).astype(LOW)
        do_all[span, :] = mul_t(db, w_out[...]).astype(LOW)
        copies.append(put(do_all.at[span, :], do_ref.at[span, :], out_sem.at[len(copies)]))
        db_all[span, :] = db
        dm_all[span, :] = dm
        o_t[:, span] = jnp.transpose(o)
        a2_t[:, span] = jnp.transpose(a2)
        h_t[:, span] = jnp.transpose(h)
    dm, duw, db = dm_all[...], duw_all[...], db_all[...]
    for j, out, target in ((1, send, send_ref), (3, send, send_ref), (0, keep, keep_ref), (2, keep, keep_ref)):
        span = pl.ds(pl.multiple_of((place ^ j) * share, share), share)
        base = (place ^ j) * (share + short)
        down = pl.ds(pl.multiple_of(base, short), share)
        down_last = pl.ds(pl.multiple_of(base + share, short), short)
        at = 2 * units
        out[j // 2, :, :at] = mul(a2_t[span, :], duw).astype(LOW)
        out[j // 2, :, at : at + width] = mul(o_t[span, :], db).astype(LOW)
        at += width
        out[j // 2, :, at : at + width] = mul(h_t[down, :], dm).astype(LOW)
        at += width
        last = mul(h_t[down_last, :], dm).astype(LOW)
        out[j // 2, :short, at:] = last[:, : width // 2]
        out[j // 2, short:, at:] = last[:, width // 2 :]
        copies.append(put(out.at[j // 2], target.at[j // 2], out_sem.at[len(copies)]))
    wait_all(copies)


def send_kernel(count, at_ref, *refs):
    normed_ref = refs[0]
    dqs, owns, gots = (refs[1 + i * count : 1 + (i + 1) * count] for i in range(3))
    (cos_ref, sin_ref, dqkv_ref, normed_t_ref, send_ref,
     dqkv, normed_t, send, normed, own, got, in_sem, sem) = refs[1 + 3 * count :]
    width = normed.shape[1]
    part_width = width // count
    first = put(normed_ref, normed, in_sem.at[0])
    came = []
    for part in range(count):
        span = pl.ds(part * part_width, part_width)
        came.append([
            put(source, target, in_sem.at[1 + 3 * part + i])
            for i, (source, target) in enumerate((
                (owns[part], own.at[:, :, span]),
                (gots[part], got.at[:, :, span]),
                (dqs[part], dqkv.at[:, span]),
            ))
        ])
    first.wait()
    normed_t[...] = jnp.transpose(normed[...])
    copies = [put(normed_t, normed_t_ref, sem.at[0])]
    cos_part, sin_part = cos_ref[...], -sin_ref[...]
    for part in range(count):
        wait_all(came[part])
        for pair in range(part * part_width // PAIR, (part + 1) * part_width // PAIR):
            lanes = pl.ds(pair * PAIR, PAIR)
            raw = own[0, :, lanes].astype(FULL) + got[0, :, lanes].astype(FULL)
            dqkv[:, pl.ds(width + pair * PAIR, PAIR)] = turn(raw, cos_part, sin_part).astype(LOW)
            dqkv[:, pl.ds(2 * width + pair * PAIR, PAIR)] = (
                own[1, :, lanes].astype(FULL) + got[1, :, lanes].astype(FULL)
            ).astype(LOW)
    copies.append(put(dqkv, dqkv_ref, sem.at[1]))
    right = dqkv[...]
    share = send.shape[1]
    for j in (1, 3):
        start = pl.multiple_of((at_ref[0] ^ j) * share, share)
        send[j // 2] = mul(normed_t[pl.ds(start, share), :], right).astype(LOW)
        copies.append(put(send.at[j // 2], send_ref.at[j // 2], sem.at[len(copies)]))
    wait_all(copies)


def keep_kernel(at_ref, normed_t_ref, dqkv_ref, keep_ref, keep, sem):
    right = dqkv_ref[...]
    share = keep.shape[1]
    copies = []
    for j in (0, 2):
        start = pl.multiple_of((at_ref[0] ^ j) * share, share)
        keep[j // 2] = mul(normed_t_ref[pl.ds(start, share), :], right).astype(LOW)
        copies.append(put(keep.at[j // 2], keep_ref.at[j // 2], sem.at[len(copies)]))
    wait_all(copies)


def input_kernel(at_ref, tokens_ref, far_ref, gain_ref, dx1_ref, dqkv_ref, w0, w1, w2, w3, w4, w5,
                 grad_ref, grad_far_ref, weight, grad_own, sem, out_sem):
    wait_all(load_blocks(at_ref, (w0, w1, w2, w3, w4, w5), weight, sem))
    rows = far_ref.shape[0]
    gain = gain_ref[...]
    for part in (1, 0):
        span = pl.ds(part * rows, rows)
        values = tokens_ref[at_ref[2]] if part == 0 else far_ref[...]
        scaled, root = normalize(values.astype(FULL))
        back = normalize_back(mul_t(dqkv_ref[span, :], weight[...]), gain, scaled, root)
        grad = dx1_ref[span, :] + back
        if part == 1:
            grad_far_ref[...] = grad.astype(LOW)
        else:
            grad_own[...] = grad
    put(grad_own, grad_ref.at[at_ref[2]], out_sem.at[0]).wait()


def shaped(*shape, kind=LOW):
    return jax.ShapeDtypeStruct(shape, kind)


IN_SMEM = pl.BlockSpec(memory_space=pltpu.SMEM)
IN_VMEM = pl.BlockSpec(memory_space=pltpu.VMEM)
IN_ANY = pl.BlockSpec(memory_space=pl.ANY)


def params(mebibytes):
    return pltpu.CompilerParams(vmem_limit_bytes=int(mebibytes * 1024 * 1024))


def call(kernel, args, in_specs, out_shape, out_specs, late=(), **options):
    if not isinstance(out_shape, tuple):
        out_shape, out_specs = (out_shape,), (out_specs,)
    count, skip, outs = len(args), len(late), len(out_shape)

    def body(*refs):
        outs_at = count + skip
        return kernel(*refs[:count], *refs[outs_at : outs_at + outs], *refs[outs_at + outs + 1 :])

    return pl.pallas_call(
        body,
        in_specs=list(in_specs) + [IN_ANY] * skip,
        out_shape=out_shape + (shaped(8, 128, kind=FULL),),
        out_specs=out_specs + (IN_ANY,),
        **options,
    )(*args, *late)


def gate(values, late=(), weight=0):
    hint = {}
    if weight:
        hint["cost_estimate"] = pl.CostEstimate(
            flops=weight, transcendentals=0, bytes_accessed=0
        )
    return call(
        lambda *refs: None,
        values,
        late=late,
        out_shape=tuple(jax.ShapeDtypeStruct(v.shape, v.dtype) for v in values),
        in_specs=[IN_ANY] * len(values),
        out_specs=(IN_ANY,) * len(values),
        input_output_aliases={i: i for i in range(len(values))},
        compiler_params=params(1),
        name="gate",
        **hint,
    )[: len(values)]


def prepare_first(at, weight):
    rows, width = weight.shape
    return call(
        prepare_first_kernel,
        (at, weight),
        out_shape=(shaped(rows, width), shaped(rows // 2, width)),
        in_specs=[IN_SMEM, IN_VMEM],
        out_specs=(IN_VMEM,) * 2,
        compiler_params=params(8),
        name="prepare_first",
    )


def prepare_rest(at, w_in, w_out, w_down, cotangent, tokens, late):
    rows, width = w_out.shape
    folded = 2 * width + width // 2
    return call(
        prepare_rest_kernel,
        (at, w_in, w_out, w_down, cotangent, tokens),
        late=late,
        out_shape=(
            shaped(*w_in.shape),
            shaped(rows // 2, w_in.shape[1]),
            shaped(rows, folded),
            shaped(rows // 2, folded),
            shaped(*cotangent.shape[1:]),
            shaped(*tokens.shape[1:]),
        ),
        in_specs=[IN_SMEM] + [IN_VMEM] * 5,
        out_specs=(IN_VMEM,) * 6,
        compiler_params=params(14),
        name="prepare_rest",
    )


def project(at, tokens, far, gain, cos_part, sin_part, blocks, late):
    rows, width = 2 * far.shape[0], far.shape[1]
    return call(
        project_kernel,
        (at, tokens, far, gain, cos_part, sin_part, *blocks),
        late=late,
        out_shape=(shaped(rows, width), shaped(rows, width), shaped(2, rows, width)),
        in_specs=[IN_SMEM] + [IN_VMEM] * 5 + [IN_ANY] * 6,
        out_specs=(IN_VMEM,) * 3,
        scratch_shapes=[pltpu.VMEM((width, 3 * width), LOW), pltpu.SemaphoreType.DMA((6,))],
        compiler_params=params(16),
        name="project",
    )


def attend(first, count, query, near, far, mark_query, mark_key, late=()):
    rows = query.shape[0]
    row_spec = pl.BlockSpec((rows, PAIR), lambda i: (0, i + first))
    kv_spec = pl.BlockSpec((2, rows, PAIR), lambda i: (0, 0, i + first))
    out_spec = pl.BlockSpec((rows, PAIR), lambda i: (0, i))
    return call(
        attend_kernel,
        (query, near, far, mark_query, mark_key),
        late=late,
        grid=(count,),
        out_shape=(shaped(rows, count * PAIR), shaped(rows, count * PAIR)),
        in_specs=[
            row_spec,
            kv_spec,
            kv_spec,
            pl.BlockSpec((rows, PAIR), lambda i: (0, 0)),
            pl.BlockSpec((2 * rows, PAIR), lambda i: (0, 0)),
        ],
        out_specs=(out_spec, out_spec),
        compiler_params=params(16),
        name="attend",
    )


def attend_back(
    first, first_o, count, query, near, far, extra, o, mark_key, do, cos_part, sin_part, late=()
):
    rows = query.shape[0]
    row_spec = pl.BlockSpec((rows, PAIR), lambda i: (0, i + first))
    o_spec = pl.BlockSpec((rows, PAIR), lambda i: (0, i + first_o))
    kv_spec = pl.BlockSpec((2, rows, PAIR), lambda i: (0, 0, i + first))
    fixed = pl.BlockSpec((rows, PAIR), lambda i: (0, 0))
    out_row = pl.BlockSpec((rows, PAIR), lambda i: (0, i))
    out_kv = pl.BlockSpec((2, rows, PAIR), lambda i: (0, 0, i))
    return call(
        attend_back_kernel,
        (query, near, far, extra, mark_key, o, do, cos_part, sin_part),
        late=late,
        grid=(count,),
        out_shape=(
            shaped(rows, count * PAIR),
            shaped(2, rows, count * PAIR),
            shaped(2, rows, count * PAIR),
        ),
        in_specs=[
            row_spec,
            kv_spec,
            kv_spec,
            o_spec,
            pl.BlockSpec((2 * rows, PAIR), lambda i: (0, 0)),
            o_spec,
            row_spec,
            fixed,
            fixed,
        ],
        out_specs=(out_row, out_kv, out_kv),
        compiler_params=params(20),
        name="attend_back",
    )


def middle(at, live, tokens, far, cot, cot_far, o_a, o_b, gain, blocks_in, blocks_od):
    half, width = far.shape
    rows, share = 2 * half, width // 4
    units = blocks_in[0].shape[1] // 2
    total = 2 * units + blocks_od[0].shape[1]
    assert units == 4 * (share + share // 2)
    low = lambda *shape: pltpu.VMEM(shape, LOW)
    return call(
        middle_kernel,
        (at, live, tokens, far, cot, cot_far, o_a, o_b, gain, *blocks_in, *blocks_od),
        out_shape=(
            shaped(2, half, width),
            shaped(half, width),
            shaped(rows, width, kind=FULL),
            shaped(rows, width),
            shaped(2, share, total),
            shaped(2, share, total),
        ),
        in_specs=[IN_SMEM] * 2 + [IN_VMEM] * 7 + [IN_ANY] * 12,
        out_specs=(IN_ANY,) * 6,
        scratch_shapes=[
            low(width, width),
            low(width, 2 * units),
            low(units, width),
            low(rows, width),
            low(width, rows),
            low(width, rows),
            low(units, rows),
            low(rows, width),
            low(rows, 2 * units),
            low(rows, width),
            low(rows, width),
            pltpu.VMEM((rows, width), FULL),
            low(rows, width),
            low(2, share, total),
            low(2, share, total),
            pltpu.SemaphoreType.DMA((6,)),
            pltpu.SemaphoreType.DMA((20,)),
            pltpu.SemaphoreType.DMA((10,)),
        ],
        compiler_params=params(40),
        name="middle",
    )


def qkv_send(at, normed, dq, own, got, cos_part, sin_part, late):
    rows, width = normed.shape
    share = width // 4
    return call(
        functools.partial(send_kernel, len(dq)),
        (at, normed, *dq, *own, *got, cos_part, sin_part),
        late=late,
        out_shape=(
            shaped(rows, 3 * width),
            shaped(width, rows),
            shaped(2, share, 3 * width),
        ),
        in_specs=[IN_SMEM] + [IN_ANY] * (1 + 3 * len(dq)) + [IN_VMEM] * 2,
        out_specs=(IN_ANY,) * 3,
        scratch_shapes=[
            pltpu.VMEM((rows, 3 * width), LOW),
            pltpu.VMEM((width, rows), LOW),
            pltpu.VMEM((2, share, 3 * width), LOW),
            pltpu.VMEM((rows, width), LOW),
            pltpu.VMEM((2, rows, width), LOW),
            pltpu.VMEM((2, rows, width), LOW),
            pltpu.SemaphoreType.DMA((1 + 3 * len(dq),)),
            pltpu.SemaphoreType.DMA((4,)),
        ],
        compiler_params=params(20),
        name="qkv_send",
    )


def qkv_keep(at, normed_t, dqkv, late):
    width, rows = normed_t.shape
    share = width // 4
    return call(
        keep_kernel,
        (at, normed_t, dqkv),
        late=late,
        out_shape=shaped(2, share, 3 * width),
        in_specs=[IN_SMEM] + [IN_VMEM] * 2,
        out_specs=IN_ANY,
        scratch_shapes=[
            pltpu.VMEM((2, share, 3 * width), LOW),
            pltpu.SemaphoreType.DMA((2,)),
        ],
        compiler_params=params(16),
        name="qkv_keep",
    )


def input_back(at, tokens, far, gain, dx1, dqkv, blocks, late):
    half, width = far.shape
    return call(
        input_kernel,
        (at, tokens, far, gain, dx1, dqkv, *blocks),
        late=late,
        out_shape=(shaped(2, half, width, kind=FULL), shaped(half, width)),
        in_specs=[IN_SMEM] + [IN_VMEM] * 5 + [IN_ANY] * 6,
        out_specs=(IN_ANY, IN_VMEM),
        scratch_shapes=[
            pltpu.VMEM((width, 3 * width), LOW),
            pltpu.VMEM((half, width), FULL),
            pltpu.SemaphoreType.DMA((6,)),
            pltpu.SemaphoreType.DMA((1,)),
        ],
        compiler_params=params(20),
        name="input_back",
    )


def first_sums_kernel(at_ref, keep, got, own_a, far_a, mine_b, give_b):
    cut, short = far_a.shape[0], give_b.shape[1]

    def add(block, start, size):
        span = pl.ds(start, size)
        return (keep[block, span, :].astype(FULL) + got[block, span, :].astype(FULL)).astype(LOW)

    far_a[...] = add(1, 0, cut)
    for block in range(2):
        give_b[block] = add(block, pl.multiple_of(cut + (1 - at_ref[1]) * short, short), short)
        mine_b[block] = add(block, pl.multiple_of(cut + at_ref[1] * short, short), short)
    own_a[...] = add(0, 0, cut)


def first_sums(at, keep, got, late=()):
    _, rows, width = keep.shape
    cut, short = rows // 2, rows // 4
    return call(
        first_sums_kernel,
        (at, keep, got),
        late=late,
        out_shape=(shaped(cut, width),) * 2 + (shaped(2, short, width),) * 2,
        in_specs=[IN_SMEM] + [IN_VMEM] * 2,
        out_specs=(IN_VMEM,) * 4,
        compiler_params=params(20),
        name="first_sums",
    )


def second_sums_kernel(at_ref, own_a, got_a, mine_b, got_b, mine_a, give_a, near_b, far_b):
    short = mine_a.shape[0]
    for start, out in ((1 - at_ref[1], give_a), (at_ref[1], mine_a)):
        span = pl.ds(pl.multiple_of(start * short, short), short)
        out[...] = (own_a[span, :].astype(FULL) + got_a[span, :].astype(FULL)).astype(LOW)
    for block, out in ((1, far_b), (0, near_b)):
        out[...] = (mine_b[block].astype(FULL) + got_b[block].astype(FULL)).astype(LOW)


def second_sums(at, own_a, got_a, mine_b, got_b, late=()):
    _, short, width = mine_b.shape
    return call(
        second_sums_kernel,
        (at, own_a, got_a, mine_b, got_b),
        late=late,
        out_shape=(shaped(short, width),) * 4,
        in_specs=[IN_SMEM] + [IN_VMEM] * 4,
        out_specs=(IN_VMEM,) * 4,
        compiler_params=params(12),
        name="second_sums",
    )


def third_sums_kernel(lanes, mine_a, got_a, near_b, got_b, *outs):
    upper = mine_a[...].astype(FULL) + got_a[...].astype(FULL)
    lower = near_b[...].astype(FULL) + got_b[...].astype(FULL)
    total = jnp.concatenate([upper, lower])
    first = 0
    for out, width in zip(outs, lanes):
        count, rows, _ = out.shape
        for i in range(count):
            out[i] = total[i * rows : (i + 1) * rows, first : first + width].astype(LOW)
        first += width


def third_sums(count, lanes, mine_a, got_a, near_b, got_b, late=()):
    rows = 2 * mine_a.shape[0] // count
    return call(
        functools.partial(third_sums_kernel, lanes),
        (mine_a, got_a, near_b, got_b),
        late=late,
        out_shape=tuple(shaped(count, rows, width) for width in lanes),
        in_specs=[IN_VMEM] * 4,
        out_specs=(IN_VMEM,) * len(lanes),
        compiler_params=params(12),
        name="third_sums",
    )


def squares_kernel(at_ref, qkv, w_qkv, inner, w_in, gains, folded, out):
    total = jnp.sum(jnp.square(folded[...].astype(FULL)), keepdims=True)
    rows = qkv.shape[0]
    shape = (rows, gains.shape[1])
    offset = lax.broadcasted_iota(jnp.int32, shape, 1) - lax.broadcasted_iota(jnp.int32, shape, 0)
    for i, (piece, weight) in enumerate(((qkv, w_qkv), (inner, w_in))):
        start = at_ref[3 + i]
        span = slice(0, rows)
        if weight.shape[0] != rows:
            span = pl.ds(pl.multiple_of(start, 8), rows)
        values = piece[...].astype(FULL)
        sums = jnp.sum(weight[span, :].astype(LOW).astype(FULL) * values, axis=1, keepdims=True)
        gain = gains[i : i + 1, :].astype(LOW).astype(FULL)
        gain = jnp.sum(jnp.where(offset == start, gain, 0.0), axis=1, keepdims=True)
        total += jnp.sum(jnp.square(values), keepdims=True)
        total += jnp.sum(jnp.square(sums / gain), keepdims=True)
    width = qkv.shape[1]
    out[:, :width] = qkv[...]
    shape = (rows, 128)
    lane = lax.broadcasted_iota(jnp.int32, shape, 1)
    tile = jnp.zeros(shape, FULL)
    for i, part in enumerate(three_parts(total)):
        tile = jnp.where(lane == i, part, tile)
    out[:, width:] = tile.astype(LOW)


def squares(at, qkv, *args):
    return call(
        squares_kernel,
        (at, qkv, *args),
        out_shape=shaped(qkv.shape[0], qkv.shape[1] + 128),
        in_specs=[IN_SMEM] + [IN_VMEM] * (1 + len(args)),
        out_specs=IN_VMEM,
        compiler_params=params(10),
        name="squares",
    )


def square_sum_kernel(pieces, mine, other, out):
    rows = mine.shape[0] // pieces
    total = jnp.zeros((1, 1), FULL)
    for part in (mine, other):
        tile = part[:, part.shape[1] - 128 :].astype(FULL)
        line = lax.broadcasted_iota(jnp.int32, tile.shape, 0)
        for i in range(pieces):
            total += jnp.sum(jnp.where(line == i * rows, tile, 0.0), keepdims=True)
    out[...] = jnp.broadcast_to(total, out.shape)


def square_sum(pieces, mine, other):
    return call(
        functools.partial(square_sum_kernel, pieces),
        (mine, other),
        out_shape=shaped(8, 128, kind=FULL),
        in_specs=[IN_VMEM] * 2,
        out_specs=IN_VMEM,
        compiler_params=params(4),
        name="square_sum",
    )


def clip_factor(square_ref):
    norm = jnp.sqrt(square_ref[:1, :1])
    return jnp.minimum(1.0, CLIP_LIMIT / (norm + 1e-06))


def quarters(at_ref, mine, other):
    short = mine.shape[0] // 2
    for i in range(4):
        span = slice((i // 2) * short, (i // 2 + 1) * short)
        own = at_ref[1] == i % 2
        yield jnp.where(own, mine[span, :].astype(FULL), other[span, :].astype(FULL))


def gain_row(weight, gradient, start, shape):
    sums = jnp.sum(weight.astype(LOW).astype(FULL) * gradient, axis=1, keepdims=True)
    shape = (weight.shape[0], shape[1])
    offset = lax.broadcasted_iota(jnp.int32, shape, 1) - lax.broadcasted_iota(jnp.int32, shape, 0)
    return jnp.sum(jnp.where(offset == start, sums, 0.0), axis=0, keepdims=True)


class Update:
    def __init__(self, number, sources, held, targets, spans, in_sem, out_sem):
        self.number, self.held, self.targets = number, held, targets
        self.spans, self.out_sem, self.out = spans, out_sem, []
        self.come = [
            [
                put(source.at[span], here.at[span], in_sem.at[3 * i + k])
                for k, (source, here) in enumerate(zip(sources, held))
            ]
            for i, span in enumerate(spans)
        ]

    def step(self, i, gradient, factor):
        wait_all(self.come[i])
        span = self.spans[i]
        weight = self.held[0][span]
        results = adam_step(
            weight, self.held[1][span], self.held[2][span], gradient, factor,
            STEP_RATES[self.number], DECAY_RATES[self.number],
        )
        for k, (result, here, target) in enumerate(zip(results, self.held, self.targets)):
            here[span] = result
            self.out.append(put(here.at[span], target.at[span], self.out_sem.at[3 * i + k]))
        return weight


def row_spans(rows):
    short = rows // 4
    return [(slice(i * short, (i + 1) * short), slice(None)) for i in range(4)]


def update_first_kernel(at_ref, square_ref, q_mine, q_other, f_mine, f_other, *refs):
    sources, targets = refs[:9], refs[9:18]
    row_ref, qm, qo, fm, fo = refs[18:23]
    held = refs[23:32]
    part_sem, in_sem, out_sem = refs[32:]
    parts = [
        put(source, here, part_sem.at[i])
        for i, (source, here) in enumerate(
            ((q_mine, qm), (q_other, qo), (f_mine, fm), (f_other, fo))
        )
    ]
    rows, width = held[3].shape
    short, last = rows // 4, width // 2
    quarter_spans = row_spans(rows)
    down_last = [
        (slice(rows + (i % 2) * short, rows + (i % 2 + 1) * short),
         slice((i // 2) * last, (i // 2 + 1) * last))
        for i in range(4)
    ]
    qkv, out, down = (
        Update(
            number, sources[3 * k : 3 * k + 3], held[3 * k : 3 * k + 3],
            targets[3 * k : 3 * k + 3], spans, in_sem.at[k], out_sem.at[k],
        )
        for k, (number, spans) in enumerate(
            ((0, quarter_spans), (1, quarter_spans), (3, quarter_spans + down_last))
        )
    )
    factor = clip_factor(square_ref)
    wait_all(parts[:2])
    row = jnp.zeros(row_ref.shape, FULL)
    for i, gradient in enumerate(quarters(at_ref, qm, qo)):
        gradient = gradient[:, : held[0].shape[1]]
        row += gain_row(qkv.step(i, gradient, factor), gradient, i * short, row_ref.shape)
    row_ref[...] = row
    wait_all(parts[2:])
    for i, gradient in enumerate(quarters(at_ref, fm, fo)):
        out.step(i, gradient[:, :width], factor)
        down.step(i, gradient[:, width : 2 * width], factor)
        down.step(4 + i, gradient[:, 2 * width :], factor)
    wait_all(qkv.out + out.out + down.out)


def update_first(at, square, qkv, qkv_parts, out, down, folded_parts):
    like = [jax.ShapeDtypeStruct(v.shape, FULL) for v in (*qkv, *out, *down)]
    parts = (*qkv_parts, *folded_parts)
    return call(
        update_first_kernel,
        (at, square, *parts, *qkv, *out, *down),
        out_shape=(*like, shaped(1, qkv[0].shape[0], kind=FULL)),
        in_specs=[IN_SMEM, IN_VMEM] + [IN_ANY] * 13,
        out_specs=(IN_ANY,) * 9 + (IN_VMEM,),
        scratch_shapes=[pltpu.VMEM(v.shape, LOW) for v in parts]
        + [pltpu.VMEM(v.shape, FULL) for v in like]
        + [
            pltpu.SemaphoreType.DMA((4,)),
            pltpu.SemaphoreType.DMA((3, 24)),
            pltpu.SemaphoreType.DMA((3, 24)),
        ],
        compiler_params=params(20),
        name="update_first",
    )


def update_second_kernel(at_ref, square_ref, row_ref, g_w, g_m, g_v, i_mine, i_other, *refs):
    sources, targets = refs[:3], refs[3:6]
    g_w_out, g_m_out, g_v_out, im, io = refs[6:11]
    held = refs[11:14]
    part_sem, in_sem, out_sem = refs[14:]
    parts = [put(i_mine, im, part_sem.at[0]), put(i_other, io, part_sem.at[1])]
    rows = held[0].shape[0]
    inner = Update(2, sources, held, targets, row_spans(rows), in_sem, out_sem)
    factor = clip_factor(square_ref)
    wait_all(parts)
    row = jnp.zeros(row_ref.shape, FULL)
    for i, gradient in enumerate(quarters(at_ref, im, io)):
        row += gain_row(inner.step(i, gradient, factor), gradient, i * (rows // 4), row_ref.shape)
    for i, values in enumerate((row_ref[...], row)):
        line = slice(i, i + 1)
        gradient = values / g_w[line, :].astype(LOW).astype(FULL)
        g_w_out[line, :], g_m_out[line, :], g_v_out[line, :] = adam_step(
            g_w[line, :], g_m[line, :], g_v[line, :], gradient, factor,
            STEP_RATES[4], DECAY_RATES[4],
        )
    wait_all(inner.out)


def update_second(at, square, inner, inner_parts, row, gains):
    like = [jax.ShapeDtypeStruct(v.shape, FULL) for v in inner]
    return call(
        update_second_kernel,
        (at, square, row, *gains, *inner_parts, *inner),
        out_shape=(*like, *[jax.ShapeDtypeStruct(v.shape, FULL) for v in gains]),
        in_specs=[IN_SMEM] + [IN_VMEM] * 5 + [IN_ANY] * 5,
        out_specs=(IN_ANY,) * 3 + (IN_VMEM,) * 3,
        scratch_shapes=[pltpu.VMEM(v.shape, LOW) for v in inner_parts]
        + [pltpu.VMEM(v.shape, FULL) for v in like]
        + [
            pltpu.SemaphoreType.DMA((2,)),
            pltpu.SemaphoreType.DMA((12,)),
            pltpu.SemaphoreType.DMA((12,)),
        ],
        compiler_params=params(12),
        name="update_second",
    )


def low_sum(*values):
    return sum(value.astype(FULL) for value in values).astype(LOW)


def index(value, i):
    return lax.dynamic_index_in_dim(value, i, 0, keepdims=False)


def make(dp_count, seq_count):
    assert seq_count == 4 and dp_count % 4 == 0 and dp_count & (dp_count - 1) == 0
    bits = dp_count.bit_length() - 1
    ones = [(shift, 1) for shift in range(1, bits)]
    twos = [(shift, min(2, bits - shift)) for shift in range(1, bits, 2)]
    count = dp_count // 2

    def trade(value, axis, bit):
        size = seq_count if axis == "seq" else dp_count
        return lax.ppermute(value, axis, [(i, i ^ bit) for i in range(size)])

    def fields(group, steps):
        for shift, width in steps:
            yield shift, 1 << width, (group >> shift) & ((1 << width) - 1)

    def sum_steps(value, group, steps, lates=()):
        came = []
        for i, (shift, size, mine) in enumerate(fields(group, steps)):
            parts = value.reshape((size, value.shape[0] // size) + value.shape[1:])
            got = [trade(index(parts, mine ^ k), "dp", k << shift) for k in range(1, size)]
            came.append(got[0])
            if i < len(lates) and lates[i]:
                got = gate(got, lates[i])
            value = low_sum(index(parts, mine), *got)
        return value[0], came

    def piece_row(group, steps, share):
        at = 0
        for _, size, mine in fields(group, steps):
            at = at * size + mine
        quarter, row = share // 4, at * (share // 2 // count)
        return (row // quarter) * 2 * quarter + (group & 1) * quarter + row % quarter

    def join_steps(piece, group, steps, lates=()):
        value, came = piece[None], []
        for i, (shift, size, mine) in enumerate(list(fields(group, steps))[::-1]):
            got = [trade(value, "dp", k << shift) for k in range(1, size)]
            came.append(got)
            if i < len(lates) and lates[i]:
                got = gate(got, lates[i])
            stack = jnp.stack([value, *got])
            value = jnp.concatenate([index(stack, mine ^ k) for k in range(size)])
        return value, came

    def on_device(
        tokens, cotangent, segments, valid,
        w_qkv, w_out, w_in, w_down, gains,
        m_qkv, m_out, m_in, m_down, m_gains,
        v_qkv, v_out, v_in, v_down, v_gains,
    ):
        place = lax.axis_index("seq")
        group = lax.axis_index("dp")
        slot = place >> 1
        half = group & 1
        local_len, width = tokens.shape[1:]
        rows = 2 * local_len
        share = w_qkv.shape[0]
        at = jnp.stack(
            [place, half, slot, piece_row(group, twos, share), piece_row(group, ones, share)]
        )

        low_qkv, half_qkv, begun = prepare_first(at, w_qkv)
        (far_qa,) = gate((trade(half_qkv, "seq", 2),), weight=10 * WEIGHT)
        near_q = trade(low_qkv, "seq", 1)
        low_in, half_in, low_od, half_od, their_cot, their_tokens, _ = prepare_rest(
            at, w_in, w_out, w_down, cotangent, tokens, (begun,)
        )
        low_gains = gains.astype(LOW)
        far = trade(their_tokens, "seq", 2)
        (gain_far,) = gate((trade(low_gains, "seq", 2),), weight=20 * WEIGHT)
        far_qb = trade(far_qa, "dp", 1)
        near_qa = trade(far_qa, "seq", 1)
        near_qb = trade(far_qb, "seq", 1)
        (gain_far,) = gate((gain_far,), (far_qb,))
        gain_near = trade(jnp.stack([low_gains, gain_far]), "seq", 1)
        gain_stack = jnp.stack([low_gains, gain_near[0], gain_far, gain_near[1]])
        gain_low = jnp.concatenate(
            [index(gain_stack, b ^ place) for b in range(4)], axis=1
        ).astype(FULL)
        blocks_qkv = (low_qkv, near_q, far_qa, far_qb, near_qa, near_qb)
        low_in, low_od, half_in = gate((low_in, low_od, half_in), (far_qa,))
        near_i = trade(low_in, "seq", 1)
        near_o = trade(low_od, "seq", 1)
        (far_ia,) = gate((trade(half_in, "seq", 2),), weight=10 * WEIGHT)
        (half_od,) = gate((half_od,), (far,))

        seg = index(segments, slot)
        positions = doc_positions(seg).reshape(4, local_len)
        seg = seg.reshape(4, local_len)
        chunks = [place, place ^ 2, place ^ 1, place ^ 3]
        seg_keys = jnp.concatenate([index(seg, c) for c in chunks])
        pos = jnp.concatenate([index(positions, c) for c in chunks[:2]])
        cos_part, sin_part = rope_tables(pos)
        lane = jnp.arange(PAIR, dtype=jnp.int32)[None] % HEAD_DIM
        same = seg_keys[:, None] == lane
        mark_key = jnp.where(lane < DOCS, 1.0 - same, (lane < DOCS + 3) * 1.0).astype(LOW)
        mark_query = jnp.where((lane < DOCS) & same[:rows], NEG_FILL, 0.0).astype(LOW)
        live = lax.dynamic_index_in_dim(valid, slot, 0, keepdims=True).astype(FULL)

        normed, query, kv, _ = project(
            at, tokens, far, gain_low[:1], cos_part, sin_part, blocks_qkv,
            (far_ia, mark_key, mark_query),
        )
        kv_far = trade(kv, "seq", 1)
        far_oa = trade(half_od, "seq", 2)
        far_ib = trade(far_ia, "dp", 1)
        near_ia = trade(far_ia, "seq", 1)
        (cot_far,) = gate((trade(their_cot, "seq", 2),), weight=WEIGHT)
        pairs = width // PAIR
        early = 2
        args = (query, kv, kv_far, mark_query, mark_key)
        o_a, extra_a, done_a = attend(0, early, *args)
        far_oa, far_ib = gate((far_oa, far_ib), (done_a,), weight=10 * WEIGHT)
        far_ob = trade(far_oa, "dp", 1)
        near_oa = trade(far_oa, "seq", 1)
        near_ib = trade(far_ib, "seq", 1)
        o_b, extra_b, done_b = attend(early, pairs - early, *args, late=(done_a, far_oa, near_ia))
        (far_ob,) = gate((far_ob,), (done_b,))
        near_ob = trade(far_ob, "seq", 1)
        blocks_in = (low_in, near_i, far_ia, far_ib, near_ia, near_ib)
        blocks_od = (low_od, near_o, far_oa, far_ob, near_oa, near_ob)

        mixed, mixed_far, dx1, do, keep_rest, send_rest, _ = middle(
            at, live, tokens, far, cotangent, cot_far, o_a, o_b, gain_low[1:], blocks_in, blocks_od
        )
        got_rest = trade(send_rest, "seq", 1)
        two = pairs // 3
        near_args = (query, kv, kv_far)
        back_args = (mark_key, do, cos_part, sin_part)
        dq0, own0, give0, back0 = attend_back(0, 0, two, *near_args, extra_a, o_a, *back_args)
        *r1, r1_done = first_sums(at, keep_rest, got_rest, late=(back0,))
        got_ra, got_rb = trade(r1[1], "seq", 2), trade(r1[3], "dp", 1)
        got0 = trade(give0, "seq", 1)
        dq1, own1, give1, back1 = attend_back(
            two, two - early, two, *near_args, extra_b, o_b, *back_args, late=(r1_done,)
        )
        got1 = trade(give1, "seq", 1)
        (mixed_far,) = gate((mixed_far,), (back1,))
        mixed_far = trade(mixed_far, "seq", 2)
        dq2, own2, give2, back2 = attend_back(
            2 * two, 2 * two - early, pairs - 2 * two, *near_args, extra_b, o_b, *back_args,
            late=(back1, got0),
        )
        got2 = trade(give2, "seq", 1)
        *r2, r2_done = second_sums(at, r1[0], got_ra, r1[2], got_rb, late=(back2, got1))
        got_ra, got_rb = gate(
            (trade(r2[1], "dp", 1), trade(r2[3], "seq", 2)), weight=WEIGHT
        )
        dqkv, normed_t, send_qkv, send_done = qkv_send(
            at, normed, (dq0, dq1, dq2), (own0, own1, own2), (got0, got1, got2),
            cos_part, sin_part, late=(r2_done,),
        )
        got_qkv = trade(send_qkv, "seq", 1)
        inner_lanes = w_in.shape[1]
        lanes = (inner_lanes, keep_rest.shape[2] - inner_lanes)
        inner, folded, r3_done = third_sums(
            count, lanes, r2[0], got_ra, r2[2], got_rb, late=(send_done,)
        )
        keep_qkv, _ = qkv_keep(at, normed_t, dqkv, late=(r3_done,))
        *q1, q1_done = first_sums(at, keep_qkv, got_qkv)
        got_qa, got_qb = trade(q1[1], "seq", 2), trade(q1[3], "dp", 1)
        grad, grad_far, grad_done = input_back(
            at, tokens, far, gain_low[:1], dx1, dqkv, blocks_qkv, late=(q1_done, mixed_far)
        )
        *q2, q2_done = second_sums(at, q1[0], got_qa, q1[2], got_qb, late=(grad_done,))
        got_qa, got_qb = gate(
            (trade(q2[1], "dp", 1), trade(q2[3], "seq", 2)), weight=10 * WEIGHT
        )
        qkv, q3_done = third_sums(count, (3 * width,), q2[0], got_qa, q2[2], got_qb)
        qkv_piece, came_first = sum_steps(qkv, group, twos)
        lates = ((grad_done,), (came_first[0],))
        inner_piece, _ = sum_steps(inner, group, ones, lates)
        folded_piece, _ = sum_steps(folded, group, ones, lates)
        behind = [w_qkv, w_in]
        if qkv_piece.shape[0] % 8:
            behind = [
                lax.dynamic_slice_in_dim(value, at[3 + i], qkv_piece.shape[0], 0)
                for i, value in enumerate(behind)
            ]
        qkv_piece, _ = squares(
            at, qkv_piece, behind[0], inner_piece, behind[1], gains, folded_piece
        )
        qkv_mine, came = join_steps(qkv_piece, group, twos)
        lates = ((came[0][0],), (qkv_mine,))
        inner_mine, _ = join_steps(inner_piece, group, ones, lates)
        folded_mine, _ = join_steps(folded_piece, group, ones, lates)
        (grad_far,) = gate((grad_far,), tuple(came[0]))
        grad_far = trade(grad_far, "seq", 2)

        def both_halves(mine, weight=WEIGHT):
            mine = mine.reshape((-1,) + mine.shape[2:])
            return mine, gate((trade(mine, "dp", 1),), weight=weight)[0]

        qkv_parts = both_halves(qkv_mine)
        square, _ = square_sum(count, *qkv_parts)
        for bit in (2, 1):
            square = square + trade(square, "seq", bit)
        grad_norm = jnp.sqrt(square[0, 0])
        (new_qkv, first_qkv, second_qkv, new_out, first_out, second_out,
         new_down, first_down, second_down, row, _) = update_first(
            at, square, (w_qkv, m_qkv, v_qkv), qkv_parts,
            (w_out, m_out, v_out), (w_down, m_down, v_down), both_halves(folded_mine),
        )
        (new_in, first_in, second_in, new_gains, first_gains, second_gains, _) = update_second(
            at, square, (w_in, m_in, v_in), both_halves(inner_mine), row,
            (gains, m_gains, v_gains),
        )

        def fill(whole, theirs):
            theirs = theirs.astype(whole.dtype)[None]
            return lax.dynamic_update_slice(whole, theirs, (1 - slot, 0, 0))

        return (
            fill(mixed, mixed_far),
            fill(grad, grad_far),
            grad_norm,
            new_qkv, new_out, new_in, new_down, new_gains,
            first_qkv, first_out, first_in, first_down, first_gains,
            second_qkv, second_out, second_in, second_down, second_gains,
        )

    return on_device


def solution(mesh):
    rows, matrix, gain = P("dp", "seq", None), P("seq", None), P(None, "seq")
    weights = (matrix,) * 4 + (gain,)
    return jax.shard_map(
        make(mesh.shape["dp"], mesh.shape["seq"]),
        mesh=mesh,
        in_specs=(rows, rows, P("dp", None), P("dp")) + weights * 3,
        out_specs=(rows, rows, P()) + weights * 3,
        check_vma=False,
    )
```

```python
import functools
import math

import jax
import jax.numpy as jnp
from jax import lax
from jax.experimental import pallas as pl
from jax.experimental.pallas import tpu as pltpu
from jax.sharding import PartitionSpec as P

HEADS = 12
HEAD_DIM = 64
PAIR = 2 * HEAD_DIM
STEP_COUNT = 10
EPS_NORM = 1e-05
ROPE_BASE = 160000.0
NEG_FILL = -1e30
CLIP_LIMIT = 10.0
BETA_FIRST = 0.9
BETA_SECOND = 0.98
EPS_ADAM = 1e-06
STEP_RATES = (0.1, 0.5, 0.1, 0.1, 1.0)
DECAY_RATES = (0.01, 0.01, 0.01, 0.01, 0.0)
DOCS = 5
LOW = jnp.bfloat16
FULL = jnp.float32
SCALE = 1.0 / math.sqrt(HEAD_DIM)
WEIGHT = 20_000_000_000


def doc_positions(segment_ids):
    seq_len = segment_ids.shape[-1]
    places = jnp.arange(seq_len, dtype=jnp.int32)
    first_mark = jnp.ones((1,), jnp.bool_)
    change = jnp.concatenate([first_mark, segment_ids[1:] != segment_ids[:-1]])
    starts = lax.cummax(jnp.where(change, places, 0), axis=0)
    return places - starts


def rope_tables(positions):
    half_dim = HEAD_DIM // 2
    exponents = jnp.arange(half_dim, dtype=jnp.float32) * (2.0 / HEAD_DIM)
    inv_freq = ROPE_BASE ** (-exponents)
    angles = positions.astype(jnp.float32)[:, None] * inv_freq
    cos_part, sin_part = jnp.cos(angles), jnp.sin(angles)
    return (
        jnp.concatenate([cos_part] * 4, axis=1),
        jnp.concatenate([-sin_part, sin_part] * 2, axis=1),
    )


def adam_step(weight, first_old, second_old, gradient, factor, step_rate, decay_rate):
    clipped = gradient * factor
    first_new = BETA_FIRST * first_old + (1.0 - BETA_FIRST) * clipped
    second_new = BETA_SECOND * second_old + (1.0 - BETA_SECOND) * clipped * clipped
    root = second_new * lax.rsqrt(second_new) * (1.0 - BETA_SECOND**STEP_COUNT) ** -0.5
    step = first_new * (step_rate / (1.0 - BETA_FIRST**STEP_COUNT)) / (root + EPS_ADAM)
    return (weight * (1.0 - step_rate * decay_rate) - step, first_new, second_new)


def mul(left, right):
    return lax.dot_general(left, right, (((1,), (0,)), ((), ())), preferred_element_type=FULL)


def mul_t(left, right):
    return lax.dot_general(left, right, (((1,), (1,)), ((), ())), preferred_element_type=FULL)


def normalize(values):
    centered = values - jnp.mean(values, axis=-1, keepdims=True)
    root = lax.rsqrt(jnp.mean(centered * centered, axis=-1, keepdims=True) + EPS_NORM)
    return centered * root, root


def normalize_back(grad, gain, scaled, root):
    t = grad * gain
    back = root * (
        t
        - jnp.mean(t, axis=-1, keepdims=True)
        - scaled * jnp.mean(t * scaled, axis=-1, keepdims=True)
    )
    return back


def turn(values, cos_part, sin_part):
    lane = lax.broadcasted_iota(jnp.int32, values.shape, 1)
    swapped = jnp.where(
        lane % HEAD_DIM < HEAD_DIM // 2,
        pltpu.roll(values, PAIR - HEAD_DIM // 2, 1),
        pltpu.roll(values, HEAD_DIM // 2, 1),
    )
    return values * cos_part + swapped * sin_part


def three_parts(values):
    high = values.astype(LOW).astype(FULL)
    rest = values - high
    mid = rest.astype(LOW).astype(FULL)
    return high, mid, rest - mid


def wait_all(copies):
    for copy in copies:
        copy.wait()


def put(source, target, sem):
    copy = pltpu.make_async_copy(source, target, sem)
    copy.start()
    return copy


PIECES = ((0, None), (1, None), (2, 0), (2, 1), (3, 0), (3, 1))


def load_blocks(at_ref, blocks, whole, sem):
    rows = blocks[0].shape[0]
    copies = []
    for i, (bits, part) in enumerate(PIECES):
        start = (at_ref[0] ^ bits) * rows
        size = rows
        if part is not None:
            size = rows // 2
            start += (at_ref[1] ^ part) * size
        target = whole.at[pl.ds(pl.multiple_of(start, size), size), :]
        copies.append(put(blocks[i], target, sem.at[i]))
    return copies


def load_folded(at_ref, blocks, w_out, w_down, sem):
    rows, width = blocks[0].shape[0], w_out.shape[1]
    short, last = rows // 2, width // 2
    copies = []

    def copy(source, target):
        copies.append(put(source, target, sem.at[len(copies)]))

    for i, (bits, part) in enumerate(PIECES):
        owner = at_ref[0] ^ bits
        base = owner * (rows + short)
        first = 0 if part is None else (at_ref[1] ^ part) * short
        size = rows if part is None else short
        for lanes, whole, start in ((0, w_out, owner * rows), (width, w_down, base)):
            span = pl.ds(pl.multiple_of(start + first, short), size)
            copy(blocks[i].at[:, pl.ds(lanes, width)], whole.at[span, :])
        span = pl.ds(pl.multiple_of(base + rows, short), short)
        if part is None:
            for fold in range(2):
                copy(
                    blocks[i].at[pl.ds(fold * short, short), pl.ds(2 * width, last)],
                    w_down.at[span, pl.ds(fold * last, last)],
                )
        else:
            lanes = pl.ds(pl.multiple_of((at_ref[1] ^ part) * last, last), last)
            copy(blocks[i].at[:, pl.ds(2 * width, last)], w_down.at[span, lanes])
    return copies


def fold(out, w_out, w_down, first):
    rows, width = w_out.shape
    short, last = rows // 2, width // 2
    out[:, first : first + width] = w_out[...].astype(LOW)
    out[:, first + width : first + 2 * width] = w_down[:rows, :].astype(LOW)
    for i in range(2):
        out[i * short : (i + 1) * short, first + 2 * width :] = w_down[
            rows:, i * last : (i + 1) * last
        ].astype(LOW)


def prepare_first_kernel(at_ref, w_ref, low_ref, half_ref):
    short = half_ref.shape[0]
    half_ref[...] = w_ref[pl.ds(pl.multiple_of(at_ref[1] * short, short), short), :].astype(LOW)
    low_ref[...] = w_ref[...].astype(LOW)


def prepare_rest_kernel(at_ref, in_ref, out_ref, down_ref, cot_ref, tokens_ref,
                        low_in, half_in, low_od, half_od, their_cot, their_tokens):
    their_tokens[...] = tokens_ref[1 - at_ref[2]]
    short = half_in.shape[0]
    span = pl.ds(pl.multiple_of(at_ref[1] * short, short), short)
    low_in[...] = in_ref[...].astype(LOW)
    half_in[...] = in_ref[span, :].astype(LOW)
    fold(low_od, out_ref, down_ref, 0)
    half_od[...] = low_od[span, :]
    their_cot[...] = cot_ref[1 - at_ref[2]]


def project_kernel(at_ref, tokens_ref, far_ref, gain_ref, cos_ref, sin_ref, w0, w1, w2, w3, w4, w5,
                   normed_ref, query_ref, kv_ref, weight, sem):
    copies = load_blocks(at_ref, (w0, w1, w2, w3, w4, w5), weight, sem)
    rows, width = far_ref.shape
    for part in range(2):
        values = tokens_ref[at_ref[2]] if part == 0 else far_ref[...]
        scaled, _ = normalize(values.astype(FULL))
        normed_ref[pl.ds(part * rows, rows), :] = (scaled * gain_ref[...]).astype(LOW)
    wait_all(copies)
    for part in range(2):
        span = pl.ds(part * rows, rows)
        normed = normed_ref[span, :]
        cos_part, sin_part = cos_ref[span, :], sin_ref[span, :]
        for pair in range(2 * width // PAIR):
            lanes = pl.ds(pair * PAIR, PAIR)
            if pair % 2 == 0:
                both = mul(normed, weight[:, pl.ds(pair * PAIR, 2 * PAIR)])
            raw = both[:, (pair % 2) * PAIR : (pair % 2 + 1) * PAIR]
            turned = turn(raw, cos_part, sin_part)
            if pair < width // PAIR:
                query_ref[span, lanes] = (turned * SCALE).astype(LOW)
            else:
                kv_ref[0, span, pl.ds(pair * PAIR - width, PAIR)] = turned.astype(LOW)
        kv_ref[1, span, :] = mul(normed, weight[:, 2 * width :]).astype(LOW)


def head_lanes(head, shape):
    lane = lax.broadcasted_iota(jnp.int32, shape, 1)
    return (lane < HEAD_DIM) if head == 0 else (lane >= HEAD_DIM)


def pick(head, inside, outside):
    return jnp.where(head_lanes(head, inside.shape), inside, outside)


def attend_kernel(query_ref, near_ref, far_ref, mark_query_ref, mark_key_ref, o_ref, extra_ref):
    rows = query_ref.shape[0]
    query = query_ref[...]
    mark_query = mark_query_ref[...]
    parts = [
        (near_ref[0], jnp.transpose(near_ref[1]), mark_key_ref[:rows, :]),
        (far_ref[0], jnp.transpose(far_ref[1]), mark_key_ref[rows:, :]),
    ]
    outs, logs = [], []
    for head in range(2):
        query_head = pick(head, query, mark_query)
        scores = [mul_t(pick(head, key, mark), query_head) for key, _, mark in parts]
        top = jnp.maximum(
            jnp.max(scores[0], axis=0, keepdims=True), jnp.max(scores[1], axis=0, keepdims=True)
        )
        exps = [jnp.exp(score - top) for score in scores]
        total = jnp.sum(exps[0], axis=0, keepdims=True) + jnp.sum(exps[1], axis=0, keepdims=True)
        span = slice(head * HEAD_DIM, (head + 1) * HEAD_DIM)
        out = sum(mul(value_t[span], e.astype(LOW)) for (_, value_t, _), e in zip(parts, exps))
        outs.append(out / total)
        logs.append(top + jnp.log(total))
    o_ref[...] = jnp.transpose(jnp.concatenate(outs)).astype(LOW)
    line = lax.broadcasted_iota(jnp.int32, (PAIR, rows), 0)
    extra = jnp.zeros((PAIR, rows), FULL)
    for head in range(2):
        base = DOCS + (HEAD_DIM if head == 0 else 0)
        for i, piece in enumerate(three_parts(-logs[head])):
            extra = jnp.where(line == base + i, piece, extra)
    extra_ref[...] = jnp.transpose(extra).astype(LOW) + mark_query


def attend_back_kernel(query_ref, near_ref, far_ref, extra_ref, mark_key_ref, o_ref, do_ref,
                       cos_ref, sin_ref, dq_ref, keep_ref, send_ref):
    rows = query_ref.shape[0]
    query, extra, do = query_ref[...], extra_ref[...], do_ref[...]
    inner_all = do.astype(FULL) * o_ref[...].astype(FULL)
    lane = lax.broadcasted_iota(jnp.int32, (rows, PAIR), 1)
    zero = jnp.zeros((rows, PAIR), LOW)
    grads_query = []
    sums = [[None, None], [None, None]]
    keys_t = [jnp.transpose(near_ref[0]), jnp.transpose(far_ref[0])]
    for head in range(2):
        inside = head_lanes(head, (rows, PAIR))
        inner = jnp.sum(jnp.where(inside, inner_all, 0.0), axis=1, keepdims=True)
        base = DOCS + (HEAD_DIM if head == 0 else 0)
        tail = jnp.zeros((rows, PAIR), FULL)
        for i, piece in enumerate(three_parts(-inner)):
            tail = jnp.where(lane == base + i, piece, tail)
        query_head = pick(head, query, extra)
        do_head = pick(head, do, tail.astype(LOW))
        query_only = pick(head, query, zero)
        do_only = pick(head, do, zero)
        span = slice(head * HEAD_DIM, (head + 1) * HEAD_DIM)
        grad_query = 0.0
        for part, ref in enumerate((near_ref, far_ref)):
            mark = mark_key_ref[pl.ds(part * rows, rows), :]
            probs = jnp.exp(mul_t(pick(head, ref[0], mark), query_head))
            grad_probs = mul_t(pick(head, ref[1], mark), do_head)
            grad_scores = (probs * grad_probs).astype(LOW)
            grad_value = mul(probs.astype(LOW), do_only)
            grad_key = mul(grad_scores, query_only)
            grad_query += mul(keys_t[part][span], grad_scores)
            if head == 0:
                sums[part] = [grad_key, grad_value]
            else:
                sums[part] = [sums[part][0] + grad_key, sums[part][1] + grad_value]
        grads_query.append(grad_query)
    turned = turn(
        jnp.transpose(jnp.concatenate(grads_query)) * SCALE, cos_ref[...], -sin_ref[...]
    )
    dq_ref[...] = turned.astype(LOW)
    for i in range(2):
        keep_ref[i] = sums[0][i].astype(LOW)
        send_ref[i] = sums[1][i].astype(LOW)


def middle_kernel(at_ref, live_ref, tokens_ref, far_ref, cot_ref, cot_far_ref, oa_ref, ob_ref,
                  gain_ref, i0, i1, i2, i3, i4, i5, d0, d1, d2, d3, d4, d5,
                  mixed_ref, mixed_far_ref, dx1_ref, do_ref, keep_ref, send_ref,
                  w_out, w_in, w_down, o_all, o_t, a2_t, h_t, dm_all, duw_all, db_all,
                  mixed, dx1_all, do_all, keep, send, sem, fold_sem, out_sem):
    place, slot, live = at_ref[0], at_ref[2], live_ref[0]
    copies_down = load_folded(at_ref, (d0, d1, d2, d3, d4, d5), w_out, w_down, fold_sem)
    copies_in = load_blocks(at_ref, (i0, i1, i2, i3, i4, i5), w_in, sem)
    rows, width = far_ref.shape
    share = width // 4
    short, units = share // 2, w_down.shape[0]
    gain = gain_ref[...]
    o_all[:, : oa_ref.shape[1]] = oa_ref[...]
    o_all[:, oa_ref.shape[1] :] = ob_ref[...]
    copies = []
    for part in range(2):
        span = pl.ds(part * rows, rows)
        o = o_all[span, :]
        values = tokens_ref[slot] if part == 0 else far_ref[...]
        if part == 0:
            wait_all(copies_down)
        x1 = values.astype(FULL) + live * mul(o, w_out[...])
        scaled, root = normalize(x1)
        a2 = (scaled * gain).astype(LOW)
        if part == 0:
            wait_all(copies_in)
        u = mul(a2, w_in[:, :units])
        w = mul(a2, w_in[:, units:])
        phi = 0.5 * (1.0 + lax.erf(u * math.sqrt(0.5)))
        gelu = u * phi
        h = (gelu * w).astype(LOW)
        mixed[span, :] = (x1 + live * mul(h, w_down[...])).astype(LOW)
        target = mixed_ref.at[slot] if part == 0 else mixed_far_ref
        copies.append(put(mixed.at[span, :], target, out_sem.at[len(copies)]))
        cot = (cot_ref[slot] if part == 0 else cot_far_ref[...]).astype(FULL)
        dm = (live * cot).astype(LOW)
        dh = mul_t(dm, w_down[...])
        slope = phi + u * (jnp.exp(-0.5 * u * u) * (1.0 / math.sqrt(2.0 * math.pi)))
        duw_all[span, :units] = (dh * w * slope).astype(LOW)
        duw_all[span, units:] = (dh * gelu).astype(LOW)
        da2 = mul_t(duw_all[span, :], w_in[...])
        dx1 = cot + normalize_back(da2, gain, scaled, root)
        dx1_all[span, :] = dx1
        copies.append(put(dx1_all.at[span, :], dx1_ref.at[span, :], out_sem.at[len(copies)]))
        db = (live * dx1).astype(LOW)
        do_all[span, :] = mul_t(db, w_out[...]).astype(LOW)
        copies.append(put(do_all.at[span, :], do_ref.at[span, :], out_sem.at[len(copies)]))
        db_all[span, :] = db
        dm_all[span, :] = dm
        o_t[:, span] = jnp.transpose(o)
        a2_t[:, span] = jnp.transpose(a2)
        h_t[:, span] = jnp.transpose(h)
    dm, duw, db = dm_all[...], duw_all[...], db_all[...]
    for j, out, target in ((1, send, send_ref), (3, send, send_ref), (0, keep, keep_ref), (2, keep, keep_ref)):
        span = pl.ds(pl.multiple_of((place ^ j) * share, share), share)
        base = (place ^ j) * (share + short)
        down = pl.ds(pl.multiple_of(base, short), share)
        down_last = pl.ds(pl.multiple_of(base + share, short), short)
        at = 2 * units
        out[j // 2, :, :at] = mul(a2_t[span, :], duw).astype(LOW)
        out[j // 2, :, at : at + width] = mul(o_t[span, :], db).astype(LOW)
        at += width
        out[j // 2, :, at : at + width] = mul(h_t[down, :], dm).astype(LOW)
        at += width
        last = mul(h_t[down_last, :], dm).astype(LOW)
        out[j // 2, :short, at:] = last[:, : width // 2]
        out[j // 2, short:, at:] = last[:, width // 2 :]
        copies.append(put(out.at[j // 2], target.at[j // 2], out_sem.at[len(copies)]))
    wait_all(copies)


def send_kernel(count, at_ref, *refs):
    normed_ref = refs[0]
    dqs, owns, gots = (refs[1 + i * count : 1 + (i + 1) * count] for i in range(3))
    (cos_ref, sin_ref, dqkv_ref, normed_t_ref, send_ref,
     dqkv, normed_t, send, sem) = refs[1 + 3 * count :]
    width = normed_ref.shape[1]
    part_width = width // count
    normed_t[...] = jnp.transpose(normed_ref[...])
    copies = [put(normed_t, normed_t_ref, sem.at[0])]
    cos_part, sin_part = cos_ref[...], -sin_ref[...]
    for part, (dq, own, got) in enumerate(zip(dqs, owns, gots)):
        base = part * part_width
        dqkv[:, pl.ds(base, part_width)] = dq[...]
        dqkv[:, pl.ds(2 * width + base, part_width)] = (
            own[1].astype(FULL) + got[1].astype(FULL)
        ).astype(LOW)
        for pair in range(part_width // PAIR):
            lanes = pl.ds(pair * PAIR, PAIR)
            raw = own[0, :, lanes].astype(FULL) + got[0, :, lanes].astype(FULL)
            dqkv[:, pl.ds(width + base + pair * PAIR, PAIR)] = turn(raw, cos_part, sin_part).astype(
                LOW
            )
    copies.append(put(dqkv, dqkv_ref, sem.at[1]))
    right = dqkv[...]
    share = send.shape[1]
    for j in (1, 3):
        start = pl.multiple_of((at_ref[0] ^ j) * share, share)
        send[j // 2] = mul(normed_t[pl.ds(start, share), :], right).astype(LOW)
        copies.append(put(send.at[j // 2], send_ref.at[j // 2], sem.at[len(copies)]))
    wait_all(copies)


def keep_kernel(at_ref, normed_t_ref, dqkv_ref, keep_ref, keep, sem):
    right = dqkv_ref[...]
    share = keep.shape[1]
    copies = []
    for j in (0, 2):
        start = pl.multiple_of((at_ref[0] ^ j) * share, share)
        keep[j // 2] = mul(normed_t_ref[pl.ds(start, share), :], right).astype(LOW)
        copies.append(put(keep.at[j // 2], keep_ref.at[j // 2], sem.at[len(copies)]))
    wait_all(copies)


def input_kernel(at_ref, tokens_ref, far_ref, gain_ref, dx1_ref, dqkv_ref, w0, w1, w2, w3, w4, w5,
                 grad_ref, grad_far_ref, weight, grad_own, sem, out_sem):
    wait_all(load_blocks(at_ref, (w0, w1, w2, w3, w4, w5), weight, sem))
    rows = far_ref.shape[0]
    gain = gain_ref[...]
    for part in (1, 0):
        span = pl.ds(part * rows, rows)
        values = tokens_ref[at_ref[2]] if part == 0 else far_ref[...]
        scaled, root = normalize(values.astype(FULL))
        back = normalize_back(mul_t(dqkv_ref[span, :], weight[...]), gain, scaled, root)
        grad = dx1_ref[span, :] + back
        if part == 1:
            grad_far_ref[...] = grad.astype(LOW)
        else:
            grad_own[...] = grad
    put(grad_own, grad_ref.at[at_ref[2]], out_sem.at[0]).wait()


def shaped(*shape, kind=LOW):
    return jax.ShapeDtypeStruct(shape, kind)


IN_SMEM = pl.BlockSpec(memory_space=pltpu.SMEM)
IN_VMEM = pl.BlockSpec(memory_space=pltpu.VMEM)
IN_ANY = pl.BlockSpec(memory_space=pl.ANY)


def params(mebibytes):
    return pltpu.CompilerParams(vmem_limit_bytes=int(mebibytes * 1024 * 1024))


def call(kernel, args, in_specs, out_shape, out_specs, late=(), **options):
    if not isinstance(out_shape, tuple):
        out_shape, out_specs = (out_shape,), (out_specs,)
    count, skip, outs = len(args), len(late), len(out_shape)

    def body(*refs):
        outs_at = count + skip
        return kernel(*refs[:count], *refs[outs_at : outs_at + outs], *refs[outs_at + outs + 1 :])

    return pl.pallas_call(
        body,
        in_specs=list(in_specs) + [IN_ANY] * skip,
        out_shape=out_shape + (shaped(8, 128, kind=FULL),),
        out_specs=out_specs + (IN_ANY,),
        **options,
    )(*args, *late)


def gate(values, late=(), weight=0):
    hint = {}
    if weight:
        hint["cost_estimate"] = pl.CostEstimate(
            flops=weight, transcendentals=0, bytes_accessed=0
        )
    return call(
        lambda *refs: None,
        values,
        late=late,
        out_shape=tuple(jax.ShapeDtypeStruct(v.shape, v.dtype) for v in values),
        in_specs=[IN_ANY] * len(values),
        out_specs=(IN_ANY,) * len(values),
        input_output_aliases={i: i for i in range(len(values))},
        compiler_params=params(1),
        name="gate",
        **hint,
    )[: len(values)]


def prepare_first(at, weight):
    rows, width = weight.shape
    return call(
        prepare_first_kernel,
        (at, weight),
        out_shape=(shaped(rows, width), shaped(rows // 2, width)),
        in_specs=[IN_SMEM, IN_VMEM],
        out_specs=(IN_VMEM,) * 2,
        compiler_params=params(8),
        name="prepare_first",
    )


def prepare_rest(at, w_in, w_out, w_down, cotangent, tokens, late):
    rows, width = w_out.shape
    folded = 2 * width + width // 2
    return call(
        prepare_rest_kernel,
        (at, w_in, w_out, w_down, cotangent, tokens),
        late=late,
        out_shape=(
            shaped(*w_in.shape),
            shaped(rows // 2, w_in.shape[1]),
            shaped(rows, folded),
            shaped(rows // 2, folded),
            shaped(*cotangent.shape[1:]),
            shaped(*tokens.shape[1:]),
        ),
        in_specs=[IN_SMEM] + [IN_VMEM] * 5,
        out_specs=(IN_VMEM,) * 6,
        compiler_params=params(14),
        name="prepare_rest",
    )


def project(at, tokens, far, gain, cos_part, sin_part, blocks, late):
    rows, width = 2 * far.shape[0], far.shape[1]
    return call(
        project_kernel,
        (at, tokens, far, gain, cos_part, sin_part, *blocks),
        late=late,
        out_shape=(shaped(rows, width), shaped(rows, width), shaped(2, rows, width)),
        in_specs=[IN_SMEM] + [IN_VMEM] * 5 + [IN_ANY] * 6,
        out_specs=(IN_VMEM,) * 3,
        scratch_shapes=[pltpu.VMEM((width, 3 * width), LOW), pltpu.SemaphoreType.DMA((6,))],
        compiler_params=params(16),
        name="project",
    )


def attend(first, count, query, near, far, mark_query, mark_key, late=()):
    rows = query.shape[0]
    row_spec = pl.BlockSpec((rows, PAIR), lambda i: (0, i + first))
    kv_spec = pl.BlockSpec((2, rows, PAIR), lambda i: (0, 0, i + first))
    out_spec = pl.BlockSpec((rows, PAIR), lambda i: (0, i))
    return call(
        attend_kernel,
        (query, near, far, mark_query, mark_key),
        late=late,
        grid=(count,),
        out_shape=(shaped(rows, count * PAIR), shaped(rows, count * PAIR)),
        in_specs=[
            row_spec,
            kv_spec,
            kv_spec,
            pl.BlockSpec((rows, PAIR), lambda i: (0, 0)),
            pl.BlockSpec((2 * rows, PAIR), lambda i: (0, 0)),
        ],
        out_specs=(out_spec, out_spec),
        compiler_params=params(16),
        name="attend",
    )


def attend_back(
    first, first_o, count, query, near, far, extra, o, mark_key, do, cos_part, sin_part, late=()
):
    rows = query.shape[0]
    row_spec = pl.BlockSpec((rows, PAIR), lambda i: (0, i + first))
    o_spec = pl.BlockSpec((rows, PAIR), lambda i: (0, i + first_o))
    kv_spec = pl.BlockSpec((2, rows, PAIR), lambda i: (0, 0, i + first))
    fixed = pl.BlockSpec((rows, PAIR), lambda i: (0, 0))
    out_row = pl.BlockSpec((rows, PAIR), lambda i: (0, i))
    out_kv = pl.BlockSpec((2, rows, PAIR), lambda i: (0, 0, i))
    return call(
        attend_back_kernel,
        (query, near, far, extra, mark_key, o, do, cos_part, sin_part),
        late=late,
        grid=(count,),
        out_shape=(
            pltpu.VMEM((rows, count * PAIR), LOW),
            pltpu.VMEM((2, rows, count * PAIR), LOW),
            shaped(2, rows, count * PAIR),
        ),
        in_specs=[
            row_spec,
            kv_spec,
            kv_spec,
            o_spec,
            pl.BlockSpec((2 * rows, PAIR), lambda i: (0, 0)),
            o_spec,
            row_spec,
            fixed,
            fixed,
        ],
        out_specs=(out_row, out_kv, out_kv),
        compiler_params=params(20),
        name="attend_back",
    )


def middle(at, live, tokens, far, cot, cot_far, o_a, o_b, gain, blocks_in, blocks_od):
    half, width = far.shape
    rows, share = 2 * half, width // 4
    units = blocks_in[0].shape[1] // 2
    total = 2 * units + blocks_od[0].shape[1]
    assert units == 4 * (share + share // 2)
    low = lambda *shape: pltpu.VMEM(shape, LOW)
    return call(
        middle_kernel,
        (at, live, tokens, far, cot, cot_far, o_a, o_b, gain, *blocks_in, *blocks_od),
        out_shape=(
            shaped(2, half, width),
            shaped(half, width),
            shaped(rows, width, kind=FULL),
            shaped(rows, width),
            shaped(2, share, total),
            shaped(2, share, total),
        ),
        in_specs=[IN_SMEM] * 2 + [IN_VMEM] * 7 + [IN_ANY] * 12,
        out_specs=(IN_ANY,) * 6,
        scratch_shapes=[
            low(width, width),
            low(width, 2 * units),
            low(units, width),
            low(rows, width),
            low(width, rows),
            low(width, rows),
            low(units, rows),
            low(rows, width),
            low(rows, 2 * units),
            low(rows, width),
            low(rows, width),
            pltpu.VMEM((rows, width), FULL),
            low(rows, width),
            low(2, share, total),
            low(2, share, total),
            pltpu.SemaphoreType.DMA((6,)),
            pltpu.SemaphoreType.DMA((20,)),
            pltpu.SemaphoreType.DMA((10,)),
        ],
        compiler_params=params(40),
        name="middle",
    )


def qkv_send(at, normed, dq, own, got, cos_part, sin_part, late):
    rows, width = normed.shape
    share = width // 4
    return call(
        functools.partial(send_kernel, len(dq)),
        (at, normed, *dq, *own, *got, cos_part, sin_part),
        late=late,
        out_shape=(
            shaped(rows, 3 * width),
            shaped(width, rows),
            shaped(2, share, 3 * width),
        ),
        in_specs=[IN_SMEM] + [IN_VMEM] * (3 + 3 * len(dq)),
        out_specs=(IN_ANY,) * 3,
        scratch_shapes=[
            pltpu.VMEM((rows, 3 * width), LOW),
            pltpu.VMEM((width, rows), LOW),
            pltpu.VMEM((2, share, 3 * width), LOW),
            pltpu.SemaphoreType.DMA((4,)),
        ],
        compiler_params=params(20),
        name="qkv_send",
    )


def qkv_keep(at, normed_t, dqkv, late):
    width, rows = normed_t.shape
    share = width // 4
    return call(
        keep_kernel,
        (at, normed_t, dqkv),
        late=late,
        out_shape=shaped(2, share, 3 * width),
        in_specs=[IN_SMEM] + [IN_VMEM] * 2,
        out_specs=IN_ANY,
        scratch_shapes=[
            pltpu.VMEM((2, share, 3 * width), LOW),
            pltpu.SemaphoreType.DMA((2,)),
        ],
        compiler_params=params(16),
        name="qkv_keep",
    )


def input_back(at, tokens, far, gain, dx1, dqkv, blocks, late):
    half, width = far.shape
    return call(
        input_kernel,
        (at, tokens, far, gain, dx1, dqkv, *blocks),
        late=late,
        out_shape=(shaped(2, half, width, kind=FULL), shaped(half, width)),
        in_specs=[IN_SMEM] + [IN_VMEM] * 5 + [IN_ANY] * 6,
        out_specs=(IN_ANY, IN_VMEM),
        scratch_shapes=[
            pltpu.VMEM((width, 3 * width), LOW),
            pltpu.VMEM((half, width), FULL),
            pltpu.SemaphoreType.DMA((6,)),
            pltpu.SemaphoreType.DMA((1,)),
        ],
        compiler_params=params(20),
        name="input_back",
    )


def first_sums_kernel(at_ref, keep, got, own_a, far_a, mine_b, give_b):
    cut, short = far_a.shape[0], give_b.shape[1]

    def add(block, start, size):
        span = pl.ds(start, size)
        return (keep[block, span, :].astype(FULL) + got[block, span, :].astype(FULL)).astype(LOW)

    far_a[...] = add(1, 0, cut)
    for block in range(2):
        give_b[block] = add(block, pl.multiple_of(cut + (1 - at_ref[1]) * short, short), short)
        mine_b[block] = add(block, pl.multiple_of(cut + at_ref[1] * short, short), short)
    own_a[...] = add(0, 0, cut)


def first_sums(at, keep, got, late=()):
    _, rows, width = keep.shape
    cut, short = rows // 2, rows // 4
    return call(
        first_sums_kernel,
        (at, keep, got),
        late=late,
        out_shape=(shaped(cut, width),) * 2 + (shaped(2, short, width),) * 2,
        in_specs=[IN_SMEM] + [IN_VMEM] * 2,
        out_specs=(IN_VMEM,) * 4,
        compiler_params=params(20),
        name="first_sums",
    )


def second_sums_kernel(at_ref, own_a, got_a, mine_b, got_b, mine_a, give_a, near_b, far_b):
    short = mine_a.shape[0]
    for start, out in ((1 - at_ref[1], give_a), (at_ref[1], mine_a)):
        span = pl.ds(pl.multiple_of(start * short, short), short)
        out[...] = (own_a[span, :].astype(FULL) + got_a[span, :].astype(FULL)).astype(LOW)
    for block, out in ((1, far_b), (0, near_b)):
        out[...] = (mine_b[block].astype(FULL) + got_b[block].astype(FULL)).astype(LOW)


def second_sums(at, own_a, got_a, mine_b, got_b, late=()):
    _, short, width = mine_b.shape
    return call(
        second_sums_kernel,
        (at, own_a, got_a, mine_b, got_b),
        late=late,
        out_shape=(shaped(short, width),) * 4,
        in_specs=[IN_SMEM] + [IN_VMEM] * 4,
        out_specs=(IN_VMEM,) * 4,
        compiler_params=params(12),
        name="second_sums",
    )


def third_sums_kernel(lanes, mine_a, got_a, near_b, got_b, *outs):
    upper = mine_a[...].astype(FULL) + got_a[...].astype(FULL)
    lower = near_b[...].astype(FULL) + got_b[...].astype(FULL)
    total = jnp.concatenate([upper, lower])
    first = 0
    for out, width in zip(outs, lanes):
        count, rows, _ = out.shape
        for i in range(count):
            out[i] = total[i * rows : (i + 1) * rows, first : first + width].astype(LOW)
        first += width


def third_sums(count, lanes, mine_a, got_a, near_b, got_b, late=()):
    rows = 2 * mine_a.shape[0] // count
    return call(
        functools.partial(third_sums_kernel, lanes),
        (mine_a, got_a, near_b, got_b),
        late=late,
        out_shape=tuple(shaped(count, rows, width) for width in lanes),
        in_specs=[IN_VMEM] * 4,
        out_specs=(IN_VMEM,) * len(lanes),
        compiler_params=params(12),
        name="third_sums",
    )


def squares_kernel(at_ref, qkv, w_qkv, inner, w_in, gains, folded, out):
    total = jnp.sum(jnp.square(folded[...].astype(FULL)), keepdims=True)
    rows = qkv.shape[0]
    shape = (rows, gains.shape[1])
    offset = lax.broadcasted_iota(jnp.int32, shape, 1) - lax.broadcasted_iota(jnp.int32, shape, 0)
    for i, (piece, weight) in enumerate(((qkv, w_qkv), (inner, w_in))):
        start = at_ref[3]
        span = pl.ds(pl.multiple_of(start, 8), rows)
        values = piece[...].astype(FULL)
        sums = jnp.sum(weight[span, :].astype(LOW).astype(FULL) * values, axis=1, keepdims=True)
        gain = gains[i : i + 1, :].astype(LOW).astype(FULL)
        gain = jnp.sum(jnp.where(offset == start, gain, 0.0), axis=1, keepdims=True)
        total += jnp.sum(jnp.square(values), keepdims=True)
        total += jnp.sum(jnp.square(sums / gain), keepdims=True)
    out[...] = jnp.broadcast_to(total, out.shape)


def squares(*args):
    return call(
        squares_kernel,
        args,
        out_shape=shaped(8, 128, kind=FULL),
        in_specs=[IN_SMEM] + [IN_VMEM] * (len(args) - 1),
        out_specs=IN_VMEM,
        compiler_params=params(10),
        name="squares",
    )


def add_kernel(count, *refs):
    for i in range(count):
        total = refs[i][...].astype(FULL) + refs[count + i][...].astype(FULL)
        refs[2 * count + i][...] = total.astype(LOW)


def add(first, second, late=()):
    count = len(first)
    return call(
        functools.partial(add_kernel, count),
        (*first, *second),
        late=late,
        out_shape=tuple(shaped(*v.shape) for v in first),
        in_specs=[IN_VMEM] * (2 * count),
        out_specs=(IN_VMEM,) * count,
        compiler_params=params(8),
        name="add",
    )


def clip_factor(square_ref):
    norm = jnp.sqrt(square_ref[:1, :1])
    return jnp.minimum(1.0, CLIP_LIMIT / (norm + 1e-06))


def quarters(at_ref, parts):
    own, beside, other, other_beside = parts
    for i in range(4):
        same = at_ref[4] == i // 2
        near = jnp.where(same, own[...], beside[...])
        far = jnp.where(same, other[...], other_beside[...])
        yield jnp.where(at_ref[1] == i % 2, near, far).astype(FULL)


def gain_row(weight, gradient, start, shape):
    sums = jnp.sum(weight.astype(LOW).astype(FULL) * gradient, axis=1, keepdims=True)
    shape = (weight.shape[0], shape[1])
    offset = lax.broadcasted_iota(jnp.int32, shape, 1) - lax.broadcasted_iota(jnp.int32, shape, 0)
    return jnp.sum(jnp.where(offset == start, sums, 0.0), axis=0, keepdims=True)


class Update:
    def __init__(self, number, sources, news, targets, sem):
        self.number, self.sources, self.news, self.targets = number, sources, news, targets
        self.sem, self.out = sem, []

    def step(self, span, gradient, factor):
        weight = self.sources[0][span]
        results = adam_step(
            weight, self.sources[1][span], self.sources[2][span], gradient, factor,
            STEP_RATES[self.number], DECAY_RATES[self.number],
        )
        for result, new, target in zip(results, self.news, self.targets):
            new[span] = result
            self.out.append(put(new.at[span], target.at[span], self.sem.at[len(self.out)]))
        return weight


def update_rest_kernel(at_ref, square_ref, *refs):
    inner_parts, folded_parts, refs = refs[:4], refs[4:8], refs[8:]
    sources, targets, row_ref, news, sem = refs[:9], refs[9:18], refs[18], refs[19:28], refs[28]
    inner, out, down = (
        Update(number, *(group[3 * k : 3 * k + 3] for group in (sources, news, targets)), sem.at[k])
        for k, number in enumerate((2, 1, 3))
    )
    factor = clip_factor(square_ref)
    rows, width = sources[3].shape
    short, last = rows // 4, width // 2
    row = jnp.zeros(row_ref.shape, FULL)
    for i, gradient in enumerate(quarters(at_ref, inner_parts)):
        span = (slice(i * short, (i + 1) * short), slice(None))
        row += gain_row(inner.step(span, gradient, factor), gradient, i * short, row_ref.shape)
    row_ref[...] = row
    for i, gradient in enumerate(quarters(at_ref, folded_parts)):
        span = (slice(i * short, (i + 1) * short), slice(None))
        out.step(span, gradient[:, :width], factor)
        down.step(span, gradient[:, width : 2 * width], factor)
        start = rows + (i % 2) * short
        span = (slice(start, start + short), slice((i // 2) * last, (i // 2 + 1) * last))
        down.step(span, gradient[:, 2 * width :], factor)
    wait_all(inner.out + out.out + down.out)


def update_rest(at, square, inner, inner_parts, out, down, folded_parts, late):
    like = [jax.ShapeDtypeStruct(v.shape, FULL) for v in (*inner, *out, *down)]
    return call(
        update_rest_kernel,
        (at, square, *inner_parts, *folded_parts, *inner, *out, *down),
        late=late,
        out_shape=(*like, shaped(1, inner[0].shape[0], kind=FULL)),
        in_specs=[IN_SMEM] + [IN_VMEM] * 18,
        out_specs=(IN_ANY,) * 9 + (IN_VMEM,),
        scratch_shapes=[pltpu.VMEM(v.shape, FULL) for v in like]
        + [pltpu.SemaphoreType.DMA((3, 24))],
        compiler_params=params(28),
        name="update_rest",
    )


def update_last_kernel(at_ref, square_ref, row_ref, g_w, g_m, g_v, *refs):
    parts, refs = refs[:4], refs[4:]
    sources, targets = refs[:3], refs[3:6]
    g_w_out, g_m_out, g_v_out = refs[6:9]
    news, sem = refs[9:12], refs[12]
    qkv = Update(0, sources, news, targets, sem)
    factor = clip_factor(square_ref)
    short = sources[0].shape[0] // 4
    row = jnp.zeros(row_ref.shape, FULL)
    for i, gradient in enumerate(quarters(at_ref, parts)):
        span = (slice(i * short, (i + 1) * short), slice(None))
        row += gain_row(qkv.step(span, gradient, factor), gradient, i * short, row_ref.shape)
    for i, values in enumerate((row, row_ref[...])):
        line = slice(i, i + 1)
        gradient = values / g_w[line, :].astype(LOW).astype(FULL)
        g_w_out[line, :], g_m_out[line, :], g_v_out[line, :] = adam_step(
            g_w[line, :], g_m[line, :], g_v[line, :], gradient, factor,
            STEP_RATES[4], DECAY_RATES[4],
        )
    wait_all(qkv.out)


def update_last(at, square, qkv, qkv_parts, row, gains):
    like = [jax.ShapeDtypeStruct(v.shape, FULL) for v in qkv]
    return call(
        update_last_kernel,
        (at, square, row, *gains, *qkv_parts, *qkv),
        out_shape=(*like, *[jax.ShapeDtypeStruct(v.shape, FULL) for v in gains]),
        in_specs=[IN_SMEM] + [IN_VMEM] * 12,
        out_specs=(IN_ANY,) * 3 + (IN_VMEM,) * 3,
        scratch_shapes=[pltpu.VMEM(v.shape, FULL) for v in like]
        + [pltpu.SemaphoreType.DMA((12,))],
        compiler_params=params(18),
        name="update_last",
    )


def low_sum(*values):
    return sum(value.astype(FULL) for value in values).astype(LOW)


def index(value, i):
    return lax.dynamic_index_in_dim(value, i, 0, keepdims=False)


def make(dp_count, seq_count):
    assert seq_count == 4 and dp_count >= 8 and dp_count & (dp_count - 1) == 0
    far_bits = [1 << i for i in range(2, dp_count.bit_length() - 1)]

    def trade(value, axis, bit):
        size = seq_count if axis == "seq" else dp_count
        return lax.ppermute(value, axis, [(i, i ^ bit) for i in range(size)])

    def on_device(
        tokens, cotangent, segments, valid,
        w_qkv, w_out, w_in, w_down, gains,
        m_qkv, m_out, m_in, m_down, m_gains,
        v_qkv, v_out, v_in, v_down, v_gains,
    ):
        place = lax.axis_index("seq")
        group = lax.axis_index("dp")
        slot = place >> 1
        half = group & 1
        local_len, width = tokens.shape[1:]
        rows = 2 * local_len
        share = w_qkv.shape[0]
        side = (group >> 1) & 1
        quarter = share // 4
        at = jnp.stack([place, half, slot, side * 2 * quarter + half * quarter, side])

        low_qkv, half_qkv, begun = prepare_first(at, w_qkv)
        (far_qa,) = gate((trade(half_qkv, "seq", 2),), weight=10 * WEIGHT)
        near_q = trade(low_qkv, "seq", 1)
        low_in, half_in, low_od, half_od, their_cot, their_tokens, _ = prepare_rest(
            at, w_in, w_out, w_down, cotangent, tokens, (begun,)
        )
        low_gains = gains.astype(LOW)
        far = trade(their_tokens, "seq", 2)
        (gain_far,) = gate((trade(low_gains, "seq", 2),), weight=20 * WEIGHT)
        far_qb = trade(far_qa, "dp", 1)
        near_qa = trade(far_qa, "seq", 1)
        near_qb = trade(far_qb, "seq", 1)
        (gain_far,) = gate((gain_far,), (far_qb,))
        gain_near = trade(jnp.stack([low_gains, gain_far]), "seq", 1)
        gain_stack = jnp.stack([low_gains, gain_near[0], gain_far, gain_near[1]])
        gain_low = jnp.concatenate(
            [index(gain_stack, b ^ place) for b in range(4)], axis=1
        ).astype(FULL)
        blocks_qkv = (low_qkv, near_q, far_qa, far_qb, near_qa, near_qb)
        low_in, low_od, half_in = gate((low_in, low_od, half_in), (far_qa,))
        near_i = trade(low_in, "seq", 1)
        near_o = trade(low_od, "seq", 1)
        (far_ia,) = gate((trade(half_in, "seq", 2),), weight=10 * WEIGHT)
        (half_od,) = gate((half_od,), (far,))

        seg = index(segments, slot)
        positions = doc_positions(seg).reshape(4, local_len)
        seg = seg.reshape(4, local_len)
        chunks = [place, place ^ 2, place ^ 1, place ^ 3]
        seg_keys = jnp.concatenate([index(seg, c) for c in chunks])
        pos = jnp.concatenate([index(positions, c) for c in chunks[:2]])
        cos_part, sin_part = rope_tables(pos)
        lane = jnp.arange(PAIR, dtype=jnp.int32)[None] % HEAD_DIM
        same = seg_keys[:, None] == lane
        mark_key = jnp.where(lane < DOCS, 1.0 - same, (lane < DOCS + 3) * 1.0).astype(LOW)
        mark_query = jnp.where((lane < DOCS) & same[:rows], NEG_FILL, 0.0).astype(LOW)
        live = lax.dynamic_index_in_dim(valid, slot, 0, keepdims=True).astype(FULL)

        normed, query, kv, _ = project(
            at, tokens, far, gain_low[:1], cos_part, sin_part, blocks_qkv,
            (far_ia, mark_key, mark_query),
        )
        kv_far = trade(kv, "seq", 1)
        far_oa = trade(half_od, "seq", 2)
        far_ib = trade(far_ia, "dp", 1)
        near_ia = trade(far_ia, "seq", 1)
        (cot_far,) = gate((trade(their_cot, "seq", 2),), weight=WEIGHT)
        pairs = width // PAIR
        early = 2
        args = (query, kv, kv_far, mark_query, mark_key)
        o_a, extra_a, done_a = attend(0, early, *args)
        far_oa, far_ib = gate((far_oa, far_ib), (done_a,), weight=10 * WEIGHT)
        far_ob = trade(far_oa, "dp", 1)
        near_oa = trade(far_oa, "seq", 1)
        near_ib = trade(far_ib, "seq", 1)
        o_b, extra_b, done_b = attend(early, pairs - early, *args, late=(done_a, far_oa, near_ia))
        (far_ob,) = gate((far_ob,), (done_b,))
        near_ob = trade(far_ob, "seq", 1)
        blocks_in = (low_in, near_i, far_ia, far_ib, near_ia, near_ib)
        blocks_od = (low_od, near_o, far_oa, far_ob, near_oa, near_ob)

        mixed, mixed_far, dx1, do, keep_rest, send_rest, _ = middle(
            at, live, tokens, far, cotangent, cot_far, o_a, o_b, gain_low[1:], blocks_in, blocks_od
        )
        got_rest = trade(send_rest, "seq", 1)
        two = pairs // 3
        near_args = (query, kv, kv_far)
        back_args = (mark_key, do, cos_part, sin_part)
        dq0, own0, give0, back0 = attend_back(0, 0, two, *near_args, extra_a, o_a, *back_args)
        *r1, r1_done = first_sums(at, keep_rest, got_rest, late=(back0,))
        got_ra, got_rb = trade(r1[1], "seq", 2), trade(r1[3], "dp", 1)
        got0 = trade(give0, "seq", 1)
        dq1, own1, give1, back1 = attend_back(
            two, two - early, two, *near_args, extra_b, o_b, *back_args, late=(r1_done,)
        )
        got1 = trade(give1, "seq", 1)
        dq2, own2, give2, back2 = attend_back(
            2 * two, 2 * two - early, pairs - 2 * two, *near_args, extra_b, o_b, *back_args,
            late=(back1, got0),
        )
        got2 = trade(give2, "seq", 1)
        *r2, r2_done = second_sums(at, r1[0], got_ra, r1[2], got_rb, late=(back2, got1))
        got_ra, got_rb = gate(
            (trade(r2[1], "dp", 1), trade(r2[3], "seq", 2)), weight=WEIGHT
        )
        dqkv, normed_t, send_qkv, send_done = qkv_send(
            at, normed, (dq0, dq1, dq2), (own0, own1, own2), (got0, got1, got2),
            cos_part, sin_part, late=(r2_done,),
        )
        got_qkv = trade(send_qkv, "seq", 1)
        inner_lanes = w_in.shape[1]
        lanes = (inner_lanes, keep_rest.shape[2] - inner_lanes)
        inner, folded, r3_done = third_sums(
            2, lanes, r2[0], got_ra, r2[2], got_rb, late=(send_done,)
        )
        got_inner = trade(index(inner, 1 - side), "dp", 2)
        got_folded = trade(index(folded, 1 - side), "dp", 2)
        keep_qkv, _ = qkv_keep(at, normed_t, dqkv, late=(r3_done,))
        *q1, q1_done = first_sums(at, keep_qkv, got_qkv)
        got_qa, got_qb = trade(q1[1], "seq", 2), trade(q1[3], "dp", 1)
        grad, grad_far, grad_done = input_back(
            at, tokens, far, gain_low[:1], dx1, dqkv, blocks_qkv, late=(q1_done,)
        )
        *rest, rest_done = add(
            (index(inner, side), index(folded, side)), (got_inner, got_folded), late=(grad_done,)
        )
        rest_got = [trade(v, "dp", far_bits[0]) for v in rest]
        *q2, q2_done = second_sums(at, q1[0], got_qa, q1[2], got_qb, late=(rest_done,))
        got_qa, got_qb = gate(
            (trade(q2[1], "dp", 1), trade(q2[3], "seq", 2)), weight=10 * WEIGHT
        )
        qkv, q3_done = third_sums(
            2, (3 * width,), q2[0], got_qa, q2[2], got_qb, late=(rest_got[0],)
        )
        (mixed_far,) = gate((mixed_far,), (q2_done,))
        mixed_far = trade(mixed_far, "seq", 2)
        qkv, qkv_done = add(
            (index(qkv, side),), (trade(index(qkv, 1 - side), "dp", 2),),
            late=(rest_got[1], mixed_far),
        )
        for bit in far_bits[1:]:
            *rest, rest_done = add(rest, rest_got)
            rest_got = [trade(v, "dp", bit) for v in rest]
        *rest, rest_done = add(rest, rest_got, late=(qkv_done,))

        beside = [trade(v, "dp", 2) for v in rest]
        other = [trade(v, "dp", 1) for v in rest]
        late = (rest_done, *beside, *other)
        for bit in far_bits:
            qkv, qkv_done = add((qkv,), (trade(qkv, "dp", bit),), late=late)
            late = ()
        square, _ = squares(at, qkv, w_qkv, rest[0], w_in, gains, rest[1])
        qkv_beside, qkv_other = trade(qkv, "dp", 2), trade(qkv, "dp", 1)
        rest_parts = [(v, b, o, trade(b, "dp", 1)) for v, b, o in zip(rest, beside, other)]
        qkv_parts = (qkv, qkv_beside, qkv_other, trade(qkv_beside, "dp", 1))
        for bit in (2, 1):
            square = square + trade(square, "seq", bit)
        (square,) = gate((square,), (qkv_beside, qkv_other))
        square = square + trade(square, "dp", 2)
        (square,) = gate((square,), [parts[3] for parts in rest_parts])
        square = square + trade(square, "dp", 1)
        grad_norm = jnp.sqrt(square[0, 0])
        (grad_far,) = gate((grad_far,), (square,))
        grad_far = trade(grad_far, "seq", 2)

        (new_in, first_in, second_in, new_out, first_out, second_out,
         new_down, first_down, second_down, row, _) = update_rest(
            at, square, (w_in, m_in, v_in), rest_parts[0],
            (w_out, m_out, v_out), (w_down, m_down, v_down), rest_parts[1], (),
        )
        (new_qkv, first_qkv, second_qkv, new_gains, first_gains, second_gains, _) = update_last(
            at, square, (w_qkv, m_qkv, v_qkv), qkv_parts, row, (gains, m_gains, v_gains),
        )

        def fill(whole, theirs):
            theirs = theirs.astype(whole.dtype)[None]
            return lax.dynamic_update_slice(whole, theirs, (1 - slot, 0, 0))

        return (
            fill(mixed, mixed_far),
            fill(grad, grad_far),
            grad_norm,
            new_qkv, new_out, new_in, new_down, new_gains,
            first_qkv, first_out, first_in, first_down, first_gains,
            second_qkv, second_out, second_in, second_down, second_gains,
        )

    return on_device


def solution(mesh):
    rows, matrix, gain = P("dp", "seq", None), P("seq", None), P(None, "seq")
    weights = (matrix,) * 4 + (gain,)
    return jax.shard_map(
        make(mesh.shape["dp"], mesh.shape["seq"]),
        mesh=mesh,
        in_specs=(rows, rows, P("dp", None), P("dp")) + weights * 3,
        out_specs=(rows, rows, P()) + weights * 3,
        check_vma=False,
    )
```

```python
import functools
import math

import jax
import jax.numpy as jnp
from jax import lax
from jax.experimental import pallas as pl
from jax.experimental.pallas import tpu as pltpu
from jax.sharding import PartitionSpec as P

HEADS = 12
HEAD_DIM = 64
PAIR = 2 * HEAD_DIM
STEP_COUNT = 10
EPS_NORM = 1e-05
ROPE_BASE = 160000.0
NEG_FILL = -1e30
CLIP_LIMIT = 10.0
BETA_FIRST = 0.9
BETA_SECOND = 0.98
EPS_ADAM = 1e-06
STEP_RATES = (0.1, 0.5, 0.1, 0.1, 1.0)
DECAY_RATES = (0.01, 0.01, 0.01, 0.01, 0.0)
DOCS = 5
LOW = jnp.bfloat16
FULL = jnp.float32
SCALE = 1.0 / math.sqrt(HEAD_DIM)
WEIGHT = 20_000_000_000


def doc_positions(segment_ids):
    seq_len = segment_ids.shape[-1]
    places = jnp.arange(seq_len, dtype=jnp.int32)
    first_mark = jnp.ones((1,), jnp.bool_)
    change = jnp.concatenate([first_mark, segment_ids[1:] != segment_ids[:-1]])
    starts = lax.cummax(jnp.where(change, places, 0), axis=0)
    return places - starts


def rope_tables(positions):
    half_dim = HEAD_DIM // 2
    exponents = jnp.arange(half_dim, dtype=jnp.float32) * (2.0 / HEAD_DIM)
    inv_freq = ROPE_BASE ** (-exponents)
    angles = positions.astype(jnp.float32)[:, None] * inv_freq
    cos_part, sin_part = jnp.cos(angles), jnp.sin(angles)
    return (
        jnp.concatenate([cos_part] * 4, axis=1),
        jnp.concatenate([-sin_part, sin_part] * 2, axis=1),
    )


def adam_step(weight, first_old, second_old, gradient, factor, step_rate, decay_rate):
    clipped = gradient * factor
    first_new = BETA_FIRST * first_old + (1.0 - BETA_FIRST) * clipped
    second_new = BETA_SECOND * second_old + (1.0 - BETA_SECOND) * clipped * clipped
    root = second_new * lax.rsqrt(second_new) * (1.0 - BETA_SECOND**STEP_COUNT) ** -0.5
    step = first_new * (step_rate / (1.0 - BETA_FIRST**STEP_COUNT)) / (root + EPS_ADAM)
    return (weight * (1.0 - step_rate * decay_rate) - step, first_new, second_new)


def mul(left, right):
    return lax.dot_general(left, right, (((1,), (0,)), ((), ())), preferred_element_type=FULL)


def mul_t(left, right):
    return lax.dot_general(left, right, (((1,), (1,)), ((), ())), preferred_element_type=FULL)


def normalize(values):
    centered = values - jnp.mean(values, axis=-1, keepdims=True)
    root = lax.rsqrt(jnp.mean(centered * centered, axis=-1, keepdims=True) + EPS_NORM)
    return centered * root, root


def normalize_back(grad, gain, scaled, root):
    t = grad * gain
    back = root * (
        t
        - jnp.mean(t, axis=-1, keepdims=True)
        - scaled * jnp.mean(t * scaled, axis=-1, keepdims=True)
    )
    return back


def turn(values, cos_part, sin_part):
    lane = lax.broadcasted_iota(jnp.int32, values.shape, 1)
    swapped = jnp.where(
        lane % HEAD_DIM < HEAD_DIM // 2,
        pltpu.roll(values, PAIR - HEAD_DIM // 2, 1),
        pltpu.roll(values, HEAD_DIM // 2, 1),
    )
    return values * cos_part + swapped * sin_part


def three_parts(values):
    high = values.astype(LOW).astype(FULL)
    rest = values - high
    mid = rest.astype(LOW).astype(FULL)
    return high, mid, rest - mid


def wait_all(copies):
    for copy in copies:
        copy.wait()


def put(source, target, sem):
    copy = pltpu.make_async_copy(source, target, sem)
    copy.start()
    return copy


PIECES = ((0, None), (1, None), (2, 0), (2, 1), (3, 0), (3, 1))


def load_blocks(at_ref, blocks, whole, sem):
    rows = blocks[0].shape[0]
    copies = []
    for i, (bits, part) in enumerate(PIECES):
        start = (at_ref[0] ^ bits) * rows
        size = rows
        if part is not None:
            size = rows // 2
            start += (at_ref[1] ^ part) * size
        target = whole.at[pl.ds(pl.multiple_of(start, size), size), :]
        copies.append(put(blocks[i], target, sem.at[i]))
    return copies


def load_folded(at_ref, blocks, w_out, w_down, sem):
    rows, width = blocks[0].shape[0], w_out.shape[1]
    short, last = rows // 2, width // 2
    copies = []

    def copy(source, target):
        copies.append(put(source, target, sem.at[len(copies)]))

    for i, (bits, part) in enumerate(PIECES):
        owner = at_ref[0] ^ bits
        base = owner * (rows + short)
        first = 0 if part is None else (at_ref[1] ^ part) * short
        size = rows if part is None else short
        for lanes, whole, start in ((0, w_out, owner * rows), (width, w_down, base)):
            span = pl.ds(pl.multiple_of(start + first, short), size)
            copy(blocks[i].at[:, pl.ds(lanes, width)], whole.at[span, :])
        span = pl.ds(pl.multiple_of(base + rows, short), short)
        if part is None:
            for fold in range(2):
                copy(
                    blocks[i].at[pl.ds(fold * short, short), pl.ds(2 * width, last)],
                    w_down.at[span, pl.ds(fold * last, last)],
                )
        else:
            lanes = pl.ds(pl.multiple_of((at_ref[1] ^ part) * last, last), last)
            copy(blocks[i].at[:, pl.ds(2 * width, last)], w_down.at[span, lanes])
    return copies


def fold(out, w_out, w_down, first):
    rows, width = w_out.shape
    short, last = rows // 2, width // 2
    out[:, first : first + width] = w_out[...].astype(LOW)
    out[:, first + width : first + 2 * width] = w_down[:rows, :].astype(LOW)
    for i in range(2):
        out[i * short : (i + 1) * short, first + 2 * width :] = w_down[
            rows:, i * last : (i + 1) * last
        ].astype(LOW)


def prepare_first_kernel(at_ref, w_ref, low_ref, half_ref):
    short = half_ref.shape[0]
    half_ref[...] = w_ref[pl.ds(pl.multiple_of(at_ref[1] * short, short), short), :].astype(LOW)
    low_ref[...] = w_ref[...].astype(LOW)


def prepare_rest_kernel(at_ref, in_ref, out_ref, down_ref, cot_ref, tokens_ref,
                        low_in, half_in, low_od, half_od, their_cot, their_tokens):
    their_tokens[...] = tokens_ref[1 - at_ref[2]]
    short = half_in.shape[0]
    span = pl.ds(pl.multiple_of(at_ref[1] * short, short), short)
    low_in[...] = in_ref[...].astype(LOW)
    half_in[...] = in_ref[span, :].astype(LOW)
    fold(low_od, out_ref, down_ref, 0)
    half_od[...] = low_od[span, :]
    their_cot[...] = cot_ref[1 - at_ref[2]]


def project_kernel(at_ref, tokens_ref, far_ref, gain_ref, cos_ref, sin_ref, w0, w1, w2, w3, w4, w5,
                   normed_ref, query_ref, kv_ref, weight, sem):
    copies = load_blocks(at_ref, (w0, w1, w2, w3, w4, w5), weight, sem)
    rows, width = far_ref.shape
    for part in range(2):
        values = tokens_ref[at_ref[2]] if part == 0 else far_ref[...]
        scaled, _ = normalize(values.astype(FULL))
        normed_ref[pl.ds(part * rows, rows), :] = (scaled * gain_ref[...]).astype(LOW)
    wait_all(copies)
    for part in range(2):
        span = pl.ds(part * rows, rows)
        normed = normed_ref[span, :]
        cos_part, sin_part = cos_ref[span, :], sin_ref[span, :]
        for pair in range(2 * width // PAIR):
            lanes = pl.ds(pair * PAIR, PAIR)
            if pair % 2 == 0:
                both = mul(normed, weight[:, pl.ds(pair * PAIR, 2 * PAIR)])
            raw = both[:, (pair % 2) * PAIR : (pair % 2 + 1) * PAIR]
            turned = turn(raw, cos_part, sin_part)
            if pair < width // PAIR:
                query_ref[span, lanes] = (turned * SCALE).astype(LOW)
            else:
                kv_ref[0, span, pl.ds(pair * PAIR - width, PAIR)] = turned.astype(LOW)
        kv_ref[1, span, :] = mul(normed, weight[:, 2 * width :]).astype(LOW)


def head_lanes(head, shape):
    lane = lax.broadcasted_iota(jnp.int32, shape, 1)
    return (lane < HEAD_DIM) if head == 0 else (lane >= HEAD_DIM)


def pick(head, inside, outside):
    return jnp.where(head_lanes(head, inside.shape), inside, outside)


def attend_kernel(query_ref, near_ref, far_ref, mark_query_ref, mark_key_ref, o_ref, extra_ref):
    rows = query_ref.shape[0]
    query = query_ref[...]
    mark_query = mark_query_ref[...]
    parts = [
        (near_ref[0], jnp.transpose(near_ref[1]), mark_key_ref[:rows, :]),
        (far_ref[0], jnp.transpose(far_ref[1]), mark_key_ref[rows:, :]),
    ]
    outs, logs = [], []
    for head in range(2):
        query_head = pick(head, query, mark_query)
        scores = [mul_t(pick(head, key, mark), query_head) for key, _, mark in parts]
        top = jnp.maximum(
            jnp.max(scores[0], axis=0, keepdims=True), jnp.max(scores[1], axis=0, keepdims=True)
        )
        exps = [jnp.exp(score - top) for score in scores]
        total = jnp.sum(exps[0], axis=0, keepdims=True) + jnp.sum(exps[1], axis=0, keepdims=True)
        span = slice(head * HEAD_DIM, (head + 1) * HEAD_DIM)
        out = sum(mul(value_t[span], e.astype(LOW)) for (_, value_t, _), e in zip(parts, exps))
        outs.append(out / total)
        logs.append(top + jnp.log(total))
    o_ref[...] = jnp.transpose(jnp.concatenate(outs)).astype(LOW)
    line = lax.broadcasted_iota(jnp.int32, (PAIR, rows), 0)
    extra = jnp.zeros((PAIR, rows), FULL)
    for head in range(2):
        base = DOCS + (HEAD_DIM if head == 0 else 0)
        for i, piece in enumerate(three_parts(-logs[head])):
            extra = jnp.where(line == base + i, piece, extra)
    extra_ref[...] = jnp.transpose(extra).astype(LOW) + mark_query


def attend_back_kernel(query_ref, near_ref, far_ref, extra_ref, mark_key_ref, o_ref, do_ref,
                       cos_ref, sin_ref, dq_ref, keep_ref, send_ref):
    rows = query_ref.shape[0]
    query, extra, do = query_ref[...], extra_ref[...], do_ref[...]
    inner_all = do.astype(FULL) * o_ref[...].astype(FULL)
    lane = lax.broadcasted_iota(jnp.int32, (rows, PAIR), 1)
    zero = jnp.zeros((rows, PAIR), LOW)
    grads_query = []
    sums = [[None, None], [None, None]]
    keys_t = [jnp.transpose(near_ref[0]), jnp.transpose(far_ref[0])]
    for head in range(2):
        inside = head_lanes(head, (rows, PAIR))
        inner = jnp.sum(jnp.where(inside, inner_all, 0.0), axis=1, keepdims=True)
        base = DOCS + (HEAD_DIM if head == 0 else 0)
        tail = jnp.zeros((rows, PAIR), FULL)
        for i, piece in enumerate(three_parts(-inner)):
            tail = jnp.where(lane == base + i, piece, tail)
        query_head = pick(head, query, extra)
        do_head = pick(head, do, tail.astype(LOW))
        query_only = pick(head, query, zero)
        do_only = pick(head, do, zero)
        span = slice(head * HEAD_DIM, (head + 1) * HEAD_DIM)
        grad_query = 0.0
        for part, ref in enumerate((near_ref, far_ref)):
            mark = mark_key_ref[pl.ds(part * rows, rows), :]
            probs = jnp.exp(mul_t(pick(head, ref[0], mark), query_head))
            grad_probs = mul_t(pick(head, ref[1], mark), do_head)
            grad_scores = (probs * grad_probs).astype(LOW)
            grad_value = mul(probs.astype(LOW), do_only)
            grad_key = mul(grad_scores, query_only)
            grad_query += mul(keys_t[part][span], grad_scores)
            if head == 0:
                sums[part] = [grad_key, grad_value]
            else:
                sums[part] = [sums[part][0] + grad_key, sums[part][1] + grad_value]
        grads_query.append(grad_query)
    turned = turn(
        jnp.transpose(jnp.concatenate(grads_query)) * SCALE, cos_ref[...], -sin_ref[...]
    )
    dq_ref[...] = turned.astype(LOW)
    for i in range(2):
        keep_ref[i] = sums[0][i].astype(LOW)
        send_ref[i] = sums[1][i].astype(LOW)


def middle_kernel(at_ref, live_ref, tokens_ref, far_ref, cot_ref, cot_far_ref, oa_ref, ob_ref,
                  gain_ref, i0, i1, i2, i3, i4, i5, d0, d1, d2, d3, d4, d5,
                  mixed_ref, mixed_far_ref, dx1_ref, do_ref, keep_ref, send_ref,
                  w_out, w_in, w_down, o_all, o_t, a2_t, h_t, dm_all, duw_all, db_all,
                  mixed, dx1_all, do_all, keep, send, sem, fold_sem, out_sem):
    place, slot = at_ref[0], at_ref[2]
    live = live_ref[slot].astype(FULL)
    copies_down = load_folded(at_ref, (d0, d1, d2, d3, d4, d5), w_out, w_down, fold_sem)
    copies_in = load_blocks(at_ref, (i0, i1, i2, i3, i4, i5), w_in, sem)
    rows, width = far_ref.shape
    share = width // 4
    short, units = share // 2, w_down.shape[0]
    gain = gain_ref[...]
    o_all[:, : oa_ref.shape[1]] = oa_ref[...]
    o_all[:, oa_ref.shape[1] :] = ob_ref[...]
    copies = []
    for part in range(2):
        span = pl.ds(part * rows, rows)
        o = o_all[span, :]
        values = tokens_ref[slot] if part == 0 else far_ref[...]
        if part == 0:
            wait_all(copies_down)
        x1 = values.astype(FULL) + live * mul(o, w_out[...])
        scaled, root = normalize(x1)
        a2 = (scaled * gain).astype(LOW)
        if part == 0:
            wait_all(copies_in)
        u = mul(a2, w_in[:, :units])
        w = mul(a2, w_in[:, units:])
        phi = 0.5 * (1.0 + lax.erf(u * math.sqrt(0.5)))
        gelu = u * phi
        h = (gelu * w).astype(LOW)
        mixed[span, :] = (x1 + live * mul(h, w_down[...])).astype(LOW)
        target = mixed_ref.at[slot] if part == 0 else mixed_far_ref
        copies.append(put(mixed.at[span, :], target, out_sem.at[len(copies)]))
        cot = (cot_ref[slot] if part == 0 else cot_far_ref[...]).astype(FULL)
        dm = (live * cot).astype(LOW)
        dh = mul_t(dm, w_down[...])
        slope = phi + u * (jnp.exp(-0.5 * u * u) * (1.0 / math.sqrt(2.0 * math.pi)))
        duw_all[span, :units] = (dh * w * slope).astype(LOW)
        duw_all[span, units:] = (dh * gelu).astype(LOW)
        da2 = mul_t(duw_all[span, :], w_in[...])
        dx1 = cot + normalize_back(da2, gain, scaled, root)
        dx1_all[span, :] = dx1
        copies.append(put(dx1_all.at[span, :], dx1_ref.at[span, :], out_sem.at[len(copies)]))
        db = (live * dx1).astype(LOW)
        do_all[span, :] = mul_t(db, w_out[...]).astype(LOW)
        copies.append(put(do_all.at[span, :], do_ref.at[span, :], out_sem.at[len(copies)]))
        db_all[span, :] = db
        dm_all[span, :] = dm
        o_t[:, span] = jnp.transpose(o)
        a2_t[:, span] = jnp.transpose(a2)
        h_t[:, span] = jnp.transpose(h)
    dm, duw, db = dm_all[...], duw_all[...], db_all[...]
    for j, out, target in ((1, send, send_ref), (3, send, send_ref), (0, keep, keep_ref), (2, keep, keep_ref)):
        span = pl.ds(pl.multiple_of((place ^ j) * share, share), share)
        base = (place ^ j) * (share + short)
        down = pl.ds(pl.multiple_of(base, short), share)
        down_last = pl.ds(pl.multiple_of(base + share, short), short)
        at = 2 * units
        out[j // 2, :, :at] = mul(a2_t[span, :], duw).astype(LOW)
        out[j // 2, :, at : at + width] = mul(o_t[span, :], db).astype(LOW)
        at += width
        out[j // 2, :, at : at + width] = mul(h_t[down, :], dm).astype(LOW)
        at += width
        last = mul(h_t[down_last, :], dm).astype(LOW)
        out[j // 2, :short, at:] = last[:, : width // 2]
        out[j // 2, short:, at:] = last[:, width // 2 :]
        copies.append(put(out.at[j // 2], target.at[j // 2], out_sem.at[len(copies)]))
    wait_all(copies)


def send_kernel(count, at_ref, *refs):
    normed_ref = refs[0]
    dqs, owns, gots = (refs[1 + i * count : 1 + (i + 1) * count] for i in range(3))
    (cos_ref, sin_ref, dqkv_ref, normed_t_ref, send_ref,
     dqkv, normed_t, send, sem) = refs[1 + 3 * count :]
    width = normed_ref.shape[1]
    part_width = width // count
    normed_t[...] = jnp.transpose(normed_ref[...])
    copies = [put(normed_t, normed_t_ref, sem.at[0])]
    cos_part, sin_part = cos_ref[...], -sin_ref[...]
    for part, (dq, own, got) in enumerate(zip(dqs, owns, gots)):
        base = part * part_width
        dqkv[:, pl.ds(base, part_width)] = dq[...]
        dqkv[:, pl.ds(2 * width + base, part_width)] = (
            own[1].astype(FULL) + got[1].astype(FULL)
        ).astype(LOW)
        for pair in range(part_width // PAIR):
            lanes = pl.ds(pair * PAIR, PAIR)
            raw = own[0, :, lanes].astype(FULL) + got[0, :, lanes].astype(FULL)
            dqkv[:, pl.ds(width + base + pair * PAIR, PAIR)] = turn(raw, cos_part, sin_part).astype(
                LOW
            )
    copies.append(put(dqkv, dqkv_ref, sem.at[1]))
    right = dqkv[...]
    share = send.shape[1]
    for j in (1, 3):
        start = pl.multiple_of((at_ref[0] ^ j) * share, share)
        send[j // 2] = mul(normed_t[pl.ds(start, share), :], right).astype(LOW)
        copies.append(put(send.at[j // 2], send_ref.at[j // 2], sem.at[len(copies)]))
    wait_all(copies)


def keep_kernel(at_ref, normed_t_ref, dqkv_ref, keep_ref, keep, sem):
    right = dqkv_ref[...]
    share = keep.shape[1]
    copies = []
    for j in (0, 2):
        start = pl.multiple_of((at_ref[0] ^ j) * share, share)
        keep[j // 2] = mul(normed_t_ref[pl.ds(start, share), :], right).astype(LOW)
        copies.append(put(keep.at[j // 2], keep_ref.at[j // 2], sem.at[len(copies)]))
    wait_all(copies)


def input_kernel(at_ref, tokens_ref, far_ref, gain_ref, dx1_ref, dqkv_ref, w0, w1, w2, w3, w4, w5,
                 grad_ref, grad_far_ref, weight, grad_own, sem, out_sem):
    wait_all(load_blocks(at_ref, (w0, w1, w2, w3, w4, w5), weight, sem))
    rows = far_ref.shape[0]
    gain = gain_ref[...]
    for part in (1, 0):
        span = pl.ds(part * rows, rows)
        values = tokens_ref[at_ref[2]] if part == 0 else far_ref[...]
        scaled, root = normalize(values.astype(FULL))
        back = normalize_back(mul_t(dqkv_ref[span, :], weight[...]), gain, scaled, root)
        grad = dx1_ref[span, :] + back
        if part == 1:
            grad_far_ref[...] = grad.astype(LOW)
        else:
            grad_own[...] = grad
    put(grad_own, grad_ref.at[at_ref[2]], out_sem.at[0]).wait()


def shaped(*shape, kind=LOW):
    return jax.ShapeDtypeStruct(shape, kind)


IN_SMEM = pl.BlockSpec(memory_space=pltpu.SMEM)
IN_VMEM = pl.BlockSpec(memory_space=pltpu.VMEM)
IN_ANY = pl.BlockSpec(memory_space=pl.ANY)


def params(mebibytes):
    return pltpu.CompilerParams(vmem_limit_bytes=int(mebibytes * 1024 * 1024))


def call(kernel, args, in_specs, out_shape, out_specs, late=(), **options):
    if not isinstance(out_shape, tuple):
        out_shape, out_specs = (out_shape,), (out_specs,)
    count, skip, outs = len(args), len(late), len(out_shape)

    def body(*refs):
        outs_at = count + skip
        return kernel(*refs[:count], *refs[outs_at : outs_at + outs], *refs[outs_at + outs + 1 :])

    return pl.pallas_call(
        body,
        in_specs=list(in_specs) + [IN_ANY] * skip,
        out_shape=out_shape + (shaped(8, 128, kind=FULL),),
        out_specs=out_specs + (IN_ANY,),
        **options,
    )(*args, *late)


def gate(values, late=(), weight=0):
    hint = {}
    if weight:
        hint["cost_estimate"] = pl.CostEstimate(
            flops=weight, transcendentals=0, bytes_accessed=0
        )
    return call(
        lambda *refs: None,
        values,
        late=late,
        out_shape=tuple(jax.ShapeDtypeStruct(v.shape, v.dtype) for v in values),
        in_specs=[IN_ANY] * len(values),
        out_specs=(IN_ANY,) * len(values),
        input_output_aliases={i: i for i in range(len(values))},
        compiler_params=params(1),
        name="gate",
        **hint,
    )[: len(values)]


def prepare_first(at, weight):
    rows, width = weight.shape
    return call(
        prepare_first_kernel,
        (at, weight),
        out_shape=(shaped(rows, width), shaped(rows // 2, width)),
        in_specs=[IN_SMEM, IN_VMEM],
        out_specs=(IN_VMEM,) * 2,
        compiler_params=params(8),
        name="prepare_first",
    )


def prepare_rest(at, w_in, w_out, w_down, cotangent, tokens, late):
    rows, width = w_out.shape
    folded = 2 * width + width // 2
    return call(
        prepare_rest_kernel,
        (at, w_in, w_out, w_down, cotangent, tokens),
        late=late,
        out_shape=(
            shaped(*w_in.shape),
            shaped(rows // 2, w_in.shape[1]),
            shaped(rows, folded),
            shaped(rows // 2, folded),
            shaped(*cotangent.shape[1:]),
            shaped(*tokens.shape[1:]),
        ),
        in_specs=[IN_SMEM] + [IN_VMEM] * 5,
        out_specs=(IN_VMEM,) * 6,
        compiler_params=params(14),
        name="prepare_rest",
    )


def project(at, tokens, far, gain, cos_part, sin_part, blocks, late):
    rows, width = 2 * far.shape[0], far.shape[1]
    return call(
        project_kernel,
        (at, tokens, far, gain, cos_part, sin_part, *blocks),
        late=late,
        out_shape=(shaped(rows, width), shaped(rows, width), shaped(2, rows, width)),
        in_specs=[IN_SMEM] + [IN_VMEM] * 5 + [IN_ANY] * 6,
        out_specs=(IN_VMEM,) * 3,
        scratch_shapes=[pltpu.VMEM((width, 3 * width), LOW), pltpu.SemaphoreType.DMA((6,))],
        compiler_params=params(16),
        name="project",
    )


def attend(first, count, query, near, far, mark_query, mark_key, late=()):
    rows = query.shape[0]
    row_spec = pl.BlockSpec((rows, PAIR), lambda i: (0, i + first))
    kv_spec = pl.BlockSpec((2, rows, PAIR), lambda i: (0, 0, i + first))
    out_spec = pl.BlockSpec((rows, PAIR), lambda i: (0, i))
    return call(
        attend_kernel,
        (query, near, far, mark_query, mark_key),
        late=late,
        grid=(count,),
        out_shape=(shaped(rows, count * PAIR), shaped(rows, count * PAIR)),
        in_specs=[
            row_spec,
            kv_spec,
            kv_spec,
            pl.BlockSpec((rows, PAIR), lambda i: (0, 0)),
            pl.BlockSpec((2 * rows, PAIR), lambda i: (0, 0)),
        ],
        out_specs=(out_spec, out_spec),
        compiler_params=params(16),
        name="attend",
    )


def attend_back(
    first, first_o, count, query, near, far, extra, o, mark_key, do, cos_part, sin_part, late=()
):
    rows = query.shape[0]
    row_spec = pl.BlockSpec((rows, PAIR), lambda i: (0, i + first))
    o_spec = pl.BlockSpec((rows, PAIR), lambda i: (0, i + first_o))
    kv_spec = pl.BlockSpec((2, rows, PAIR), lambda i: (0, 0, i + first))
    fixed = pl.BlockSpec((rows, PAIR), lambda i: (0, 0))
    out_row = pl.BlockSpec((rows, PAIR), lambda i: (0, i))
    out_kv = pl.BlockSpec((2, rows, PAIR), lambda i: (0, 0, i))
    return call(
        attend_back_kernel,
        (query, near, far, extra, mark_key, o, do, cos_part, sin_part),
        late=late,
        grid=(count,),
        out_shape=(
            shaped(rows, count * PAIR),
            shaped(2, rows, count * PAIR),
            shaped(2, rows, count * PAIR),
        ),
        in_specs=[
            row_spec,
            kv_spec,
            kv_spec,
            o_spec,
            pl.BlockSpec((2 * rows, PAIR), lambda i: (0, 0)),
            o_spec,
            row_spec,
            fixed,
            fixed,
        ],
        out_specs=(out_row, out_kv, out_kv),
        compiler_params=params(20),
        name="attend_back",
    )


def middle(at, live, tokens, far, cot, cot_far, o_a, o_b, gain, blocks_in, blocks_od):
    half, width = far.shape
    rows, share = 2 * half, width // 4
    units = blocks_in[0].shape[1] // 2
    total = 2 * units + blocks_od[0].shape[1]
    assert units == 4 * (share + share // 2)
    low = lambda *shape: pltpu.VMEM(shape, LOW)
    return call(
        middle_kernel,
        (at, live, tokens, far, cot, cot_far, o_a, o_b, gain, *blocks_in, *blocks_od),
        out_shape=(
            shaped(2, half, width),
            shaped(half, width),
            shaped(rows, width, kind=FULL),
            shaped(rows, width),
            shaped(2, share, total),
            shaped(2, share, total),
        ),
        in_specs=[IN_SMEM] * 2 + [IN_VMEM] * 7 + [IN_ANY] * 12,
        out_specs=(IN_ANY,) * 6,
        scratch_shapes=[
            low(width, width),
            low(width, 2 * units),
            low(units, width),
            low(rows, width),
            low(width, rows),
            low(width, rows),
            low(units, rows),
            low(rows, width),
            low(rows, 2 * units),
            low(rows, width),
            low(rows, width),
            pltpu.VMEM((rows, width), FULL),
            low(rows, width),
            low(2, share, total),
            low(2, share, total),
            pltpu.SemaphoreType.DMA((6,)),
            pltpu.SemaphoreType.DMA((20,)),
            pltpu.SemaphoreType.DMA((10,)),
        ],
        compiler_params=params(40),
        name="middle",
    )


def qkv_send(at, normed, dq, own, got, cos_part, sin_part, late):
    rows, width = normed.shape
    share = width // 4
    return call(
        functools.partial(send_kernel, len(dq)),
        (at, normed, *dq, *own, *got, cos_part, sin_part),
        late=late,
        out_shape=(
            shaped(rows, 3 * width),
            shaped(width, rows),
            shaped(2, share, 3 * width),
        ),
        in_specs=[IN_SMEM] + [IN_VMEM] * (3 + 3 * len(dq)),
        out_specs=(IN_ANY,) * 3,
        scratch_shapes=[
            pltpu.VMEM((rows, 3 * width), LOW),
            pltpu.VMEM((width, rows), LOW),
            pltpu.VMEM((2, share, 3 * width), LOW),
            pltpu.SemaphoreType.DMA((4,)),
        ],
        compiler_params=params(20),
        name="qkv_send",
    )


def qkv_keep(at, normed_t, dqkv, late):
    width, rows = normed_t.shape
    share = width // 4
    return call(
        keep_kernel,
        (at, normed_t, dqkv),
        late=late,
        out_shape=shaped(2, share, 3 * width),
        in_specs=[IN_SMEM] + [IN_VMEM] * 2,
        out_specs=IN_ANY,
        scratch_shapes=[
            pltpu.VMEM((2, share, 3 * width), LOW),
            pltpu.SemaphoreType.DMA((2,)),
        ],
        compiler_params=params(16),
        name="qkv_keep",
    )


def input_back(at, tokens, far, gain, dx1, dqkv, blocks, late):
    half, width = far.shape
    return call(
        input_kernel,
        (at, tokens, far, gain, dx1, dqkv, *blocks),
        late=late,
        out_shape=(shaped(2, half, width, kind=FULL), shaped(half, width)),
        in_specs=[IN_SMEM] + [IN_VMEM] * 5 + [IN_ANY] * 6,
        out_specs=(IN_ANY, IN_VMEM),
        scratch_shapes=[
            pltpu.VMEM((width, 3 * width), LOW),
            pltpu.VMEM((half, width), FULL),
            pltpu.SemaphoreType.DMA((6,)),
            pltpu.SemaphoreType.DMA((1,)),
        ],
        compiler_params=params(20),
        name="input_back",
    )


def first_sums_kernel(at_ref, keep, got, own_a, far_a, mine_b, give_b):
    cut, short = far_a.shape[0], give_b.shape[1]

    def add(block, start, size):
        span = pl.ds(start, size)
        return (keep[block, span, :].astype(FULL) + got[block, span, :].astype(FULL)).astype(LOW)

    far_a[...] = add(1, 0, cut)
    for block in range(2):
        give_b[block] = add(block, pl.multiple_of(cut + (1 - at_ref[1]) * short, short), short)
        mine_b[block] = add(block, pl.multiple_of(cut + at_ref[1] * short, short), short)
    own_a[...] = add(0, 0, cut)


def first_sums(at, keep, got, late=()):
    _, rows, width = keep.shape
    cut, short = rows // 2, rows // 4
    return call(
        first_sums_kernel,
        (at, keep, got),
        late=late,
        out_shape=(shaped(cut, width),) * 2 + (shaped(2, short, width),) * 2,
        in_specs=[IN_SMEM] + [IN_VMEM] * 2,
        out_specs=(IN_VMEM,) * 4,
        compiler_params=params(20),
        name="first_sums",
    )


def second_sums_kernel(at_ref, own_a, got_a, mine_b, got_b, mine_a, give_a, near_b, far_b):
    short = mine_a.shape[0]
    for start, out in ((1 - at_ref[1], give_a), (at_ref[1], mine_a)):
        span = pl.ds(pl.multiple_of(start * short, short), short)
        out[...] = (own_a[span, :].astype(FULL) + got_a[span, :].astype(FULL)).astype(LOW)
    for block, out in ((1, far_b), (0, near_b)):
        out[...] = (mine_b[block].astype(FULL) + got_b[block].astype(FULL)).astype(LOW)


def second_sums(at, own_a, got_a, mine_b, got_b, late=()):
    _, short, width = mine_b.shape
    return call(
        second_sums_kernel,
        (at, own_a, got_a, mine_b, got_b),
        late=late,
        out_shape=(shaped(short, width),) * 4,
        in_specs=[IN_SMEM] + [IN_VMEM] * 4,
        out_specs=(IN_VMEM,) * 4,
        compiler_params=params(12),
        name="second_sums",
    )


def third_sums_kernel(lanes, at_ref, mine_a, got_a, near_b, got_b, *outs):
    upper = mine_a[...].astype(FULL) + got_a[...].astype(FULL)
    lower = near_b[...].astype(FULL) + got_b[...].astype(FULL)
    keep = jnp.where(at_ref[4] == 0, upper, lower).astype(LOW)
    give = jnp.where(at_ref[4] == 0, lower, upper).astype(LOW)
    first = 0
    for i, width in enumerate(lanes):
        outs[2 * i][...] = keep[:, first : first + width]
        outs[2 * i + 1][...] = give[:, first : first + width]
        first += width


def third_sums(at, lanes, mine_a, got_a, near_b, got_b, late=()):
    rows = mine_a.shape[0]
    return call(
        functools.partial(third_sums_kernel, lanes),
        (at, mine_a, got_a, near_b, got_b),
        late=late,
        out_shape=tuple(shaped(rows, width) for width in lanes for _ in range(2)),
        in_specs=[IN_SMEM] + [IN_VMEM] * 4,
        out_specs=(IN_VMEM,) * (2 * len(lanes)),
        compiler_params=params(12),
        name="third_sums",
    )


def squares_kernel(at_ref, qkv, w_qkv, inner, w_in, gains, folded, out):
    total = jnp.sum(jnp.square(folded[...].astype(FULL)), keepdims=True)
    rows = qkv.shape[0]
    shape = (rows, gains.shape[1])
    offset = lax.broadcasted_iota(jnp.int32, shape, 1) - lax.broadcasted_iota(jnp.int32, shape, 0)
    for i, (piece, weight) in enumerate(((qkv, w_qkv), (inner, w_in))):
        start = at_ref[3]
        span = pl.ds(pl.multiple_of(start, 8), rows)
        values = piece[...].astype(FULL)
        sums = jnp.sum(weight[span, :].astype(LOW).astype(FULL) * values, axis=1, keepdims=True)
        gain = gains[i : i + 1, :].astype(LOW).astype(FULL)
        gain = jnp.sum(jnp.where(offset == start, gain, 0.0), axis=1, keepdims=True)
        total += jnp.sum(jnp.square(values), keepdims=True)
        total += jnp.sum(jnp.square(sums / gain), keepdims=True)
    out[...] = jnp.broadcast_to(total, out.shape)


def squares(*args):
    return call(
        squares_kernel,
        args,
        out_shape=shaped(8, 128, kind=FULL),
        in_specs=[IN_SMEM] + [IN_VMEM] * (len(args) - 1),
        out_specs=IN_VMEM,
        compiler_params=params(10),
        name="squares",
    )


def add_kernel(count, *refs):
    for i in range(count):
        out = refs[2 * count + i]
        out[...] = (refs[i][...].astype(FULL) + refs[count + i][...].astype(FULL)).astype(out.dtype)


def add(first, second, late=()):
    count = len(first)
    return call(
        functools.partial(add_kernel, count),
        (*first, *second),
        late=late,
        out_shape=tuple(jax.ShapeDtypeStruct(v.shape, v.dtype) for v in first),
        in_specs=[IN_VMEM] * (2 * count),
        out_specs=(IN_VMEM,) * count,
        compiler_params=params(8),
        name="add",
    )


def fill_kernel(at_ref, mixed_far, grad_far, mixed_in, grad_in, mixed, grad, wide, sem):
    first = put(mixed_far, mixed.at[1 - at_ref[2]], sem.at[0])
    wide[...] = grad_far[...].astype(FULL)
    put(wide, grad.at[1 - at_ref[2]], sem.at[1]).wait()
    first.wait()


def fill(at, mixed, mixed_far, grad, grad_far):
    return call(
        fill_kernel,
        (at, mixed_far, grad_far, mixed, grad),
        out_shape=(shaped(*mixed.shape), shaped(*grad.shape, kind=FULL)),
        in_specs=[IN_SMEM, IN_ANY, IN_VMEM, IN_ANY, IN_ANY],
        out_specs=(IN_ANY,) * 2,
        input_output_aliases={3: 0, 4: 1},
        scratch_shapes=[pltpu.VMEM(grad_far.shape, FULL), pltpu.SemaphoreType.DMA((2,))],
        compiler_params=params(4),
        name="fill",
    )


def clip_factor(square_ref):
    norm = jnp.sqrt(square_ref[:1, :1])
    return jnp.minimum(1.0, CLIP_LIMIT / (norm + 1e-06))


def quarters(at_ref, parts):
    own, beside, other, other_beside = parts
    for i in range(4):
        same = at_ref[4] == i // 2
        near = jnp.where(same, own[...], beside[...])
        far = jnp.where(same, other[...], other_beside[...])
        yield jnp.where(at_ref[1] == i % 2, near, far).astype(FULL)


def gain_row(weight, gradient, start, shape):
    sums = jnp.sum(weight.astype(LOW).astype(FULL) * gradient, axis=1, keepdims=True)
    shape = (weight.shape[0], shape[1])
    offset = lax.broadcasted_iota(jnp.int32, shape, 1) - lax.broadcasted_iota(jnp.int32, shape, 0)
    return jnp.sum(jnp.where(offset == start, sums, 0.0), axis=0, keepdims=True)


class Update:
    def __init__(self, number, sources, news, targets, sem):
        self.number, self.sources, self.news, self.targets = number, sources, news, targets
        self.sem, self.out = sem, []

    def step(self, span, gradient, factor):
        weight = self.sources[0][span]
        results = adam_step(
            weight, self.sources[1][span], self.sources[2][span], gradient, factor,
            STEP_RATES[self.number], DECAY_RATES[self.number],
        )
        for result, new, target in zip(results, self.news, self.targets):
            new[span] = result
            self.out.append(put(new.at[span], target.at[span], self.sem.at[len(self.out)]))
        return weight


def update_rest_kernel(at_ref, square_ref, *refs):
    inner_parts, folded_parts, refs = refs[:4], refs[4:8], refs[8:]
    sources, targets, row_ref, news, sem = refs[:9], refs[9:18], refs[18], refs[19:28], refs[28]
    inner, out, down = (
        Update(number, *(group[3 * k : 3 * k + 3] for group in (sources, news, targets)), sem.at[k])
        for k, number in enumerate((2, 1, 3))
    )
    factor = clip_factor(square_ref)
    rows, width = sources[3].shape
    short, last = rows // 4, width // 2
    row = jnp.zeros(row_ref.shape, FULL)
    for i, gradient in enumerate(quarters(at_ref, inner_parts)):
        span = (slice(i * short, (i + 1) * short), slice(None))
        row += gain_row(inner.step(span, gradient, factor), gradient, i * short, row_ref.shape)
    row_ref[...] = row
    for i, gradient in enumerate(quarters(at_ref, folded_parts)):
        span = (slice(i * short, (i + 1) * short), slice(None))
        out.step(span, gradient[:, :width], factor)
        down.step(span, gradient[:, width : 2 * width], factor)
        start = rows + (i % 2) * short
        span = (slice(start, start + short), slice((i // 2) * last, (i // 2 + 1) * last))
        down.step(span, gradient[:, 2 * width :], factor)
    wait_all(inner.out + out.out + down.out)


def update_rest(at, square, inner, inner_parts, out, down, folded_parts, late):
    like = [jax.ShapeDtypeStruct(v.shape, FULL) for v in (*inner, *out, *down)]
    return call(
        update_rest_kernel,
        (at, square, *inner_parts, *folded_parts, *inner, *out, *down),
        late=late,
        out_shape=(*like, shaped(1, inner[0].shape[0], kind=FULL)),
        in_specs=[IN_SMEM] + [IN_VMEM] * 18,
        out_specs=(IN_ANY,) * 9 + (IN_VMEM,),
        scratch_shapes=[pltpu.VMEM(v.shape, FULL) for v in like]
        + [pltpu.SemaphoreType.DMA((3, 24))],
        compiler_params=params(28),
        name="update_rest",
    )


def update_last_kernel(at_ref, square_ref, row_ref, g_w, g_m, g_v, *refs):
    parts, refs = refs[:4], refs[4:]
    sources, targets = refs[:3], refs[3:6]
    g_w_out, g_m_out, g_v_out, norm_out = refs[6:10]
    news, sem = refs[10:13], refs[13]
    qkv = Update(0, sources, news, targets, sem)
    factor = clip_factor(square_ref)
    norm_out[...] = jnp.sqrt(square_ref[...])
    short = sources[0].shape[0] // 4
    row = jnp.zeros(row_ref.shape, FULL)
    for i, gradient in enumerate(quarters(at_ref, parts)):
        span = (slice(i * short, (i + 1) * short), slice(None))
        row += gain_row(qkv.step(span, gradient, factor), gradient, i * short, row_ref.shape)
    for i, values in enumerate((row, row_ref[...])):
        line = slice(i, i + 1)
        gradient = values / g_w[line, :].astype(LOW).astype(FULL)
        g_w_out[line, :], g_m_out[line, :], g_v_out[line, :] = adam_step(
            g_w[line, :], g_m[line, :], g_v[line, :], gradient, factor,
            STEP_RATES[4], DECAY_RATES[4],
        )
    wait_all(qkv.out)


def update_last(at, square, qkv, qkv_parts, row, gains):
    like = [jax.ShapeDtypeStruct(v.shape, FULL) for v in qkv]
    return call(
        update_last_kernel,
        (at, square, row, *gains, *qkv_parts, *qkv),
        out_shape=(
            *like,
            *[jax.ShapeDtypeStruct(v.shape, FULL) for v in gains],
            jax.ShapeDtypeStruct(square.shape, FULL),
        ),
        in_specs=[IN_SMEM] + [IN_VMEM] * 12,
        out_specs=(IN_ANY,) * 3 + (IN_VMEM,) * 4,
        scratch_shapes=[pltpu.VMEM(v.shape, FULL) for v in like]
        + [pltpu.SemaphoreType.DMA((12,))],
        compiler_params=params(18),
        name="update_last",
    )


def low_sum(*values):
    return sum(value.astype(FULL) for value in values).astype(LOW)


def index(value, i):
    return lax.dynamic_index_in_dim(value, i, 0, keepdims=False)


def make(dp_count, seq_count):
    assert seq_count == 4 and dp_count >= 8 and dp_count & (dp_count - 1) == 0
    far_bits = [1 << i for i in range(2, dp_count.bit_length() - 1)]

    def trade(value, axis, bit):
        size = seq_count if axis == "seq" else dp_count
        return lax.ppermute(value, axis, [(i, i ^ bit) for i in range(size)])

    def on_device(
        tokens, cotangent, segments, valid,
        w_qkv, w_out, w_in, w_down, gains,
        m_qkv, m_out, m_in, m_down, m_gains,
        v_qkv, v_out, v_in, v_down, v_gains,
    ):
        place = lax.axis_index("seq")
        group = lax.axis_index("dp")
        slot = place >> 1
        half = group & 1
        local_len, width = tokens.shape[1:]
        rows = 2 * local_len
        share = w_qkv.shape[0]
        side = (group >> 1) & 1
        quarter = share // 4
        at = jnp.stack([place, half, slot, side * 2 * quarter + half * quarter, side])

        low_qkv, half_qkv, begun = prepare_first(at, w_qkv)
        (far_qa,) = gate((trade(half_qkv, "seq", 2),), weight=10 * WEIGHT)
        near_q = trade(low_qkv, "seq", 1)
        low_in, half_in, low_od, half_od, their_cot, their_tokens, _ = prepare_rest(
            at, w_in, w_out, w_down, cotangent, tokens, (begun,)
        )
        low_gains = gains.astype(LOW)
        far = trade(their_tokens, "seq", 2)
        (gain_far,) = gate((trade(low_gains, "seq", 2),), weight=20 * WEIGHT)
        far_qb = trade(far_qa, "dp", 1)
        near_qa = trade(far_qa, "seq", 1)
        near_qb = trade(far_qb, "seq", 1)
        (gain_far,) = gate((gain_far,), (far_qb,))
        gain_near = trade(jnp.stack([low_gains, gain_far]), "seq", 1)
        gain_stack = jnp.stack([low_gains, gain_near[0], gain_far, gain_near[1]])
        gain_low = jnp.concatenate(
            [index(gain_stack, b ^ place) for b in range(4)], axis=1
        ).astype(FULL)
        blocks_qkv = (low_qkv, near_q, far_qa, far_qb, near_qa, near_qb)
        low_in, low_od, half_in = gate((low_in, low_od, half_in), (far_qa,))
        near_i = trade(low_in, "seq", 1)
        near_o = trade(low_od, "seq", 1)
        (far_ia,) = gate((trade(half_in, "seq", 2),), weight=10 * WEIGHT)
        (half_od,) = gate((half_od,), (far,))

        seg = index(segments, slot)
        positions = doc_positions(seg).reshape(4, local_len)
        seg = seg.reshape(4, local_len)
        chunks = [place, place ^ 2, place ^ 1, place ^ 3]
        seg_keys = jnp.concatenate([index(seg, c) for c in chunks])
        pos = jnp.concatenate([index(positions, c) for c in chunks[:2]])
        cos_part, sin_part = rope_tables(pos)
        lane = jnp.arange(PAIR, dtype=jnp.int32)[None] % HEAD_DIM
        same = seg_keys[:, None] == lane
        mark_key = jnp.where(lane < DOCS, 1.0 - same, (lane < DOCS + 3) * 1.0).astype(LOW)
        mark_query = jnp.where((lane < DOCS) & same[:rows], NEG_FILL, 0.0).astype(LOW)

        normed, query, kv, _ = project(
            at, tokens, far, gain_low[:1], cos_part, sin_part, blocks_qkv,
            (far_ia, mark_key, mark_query),
        )
        kv_far = trade(kv, "seq", 1)
        far_oa = trade(half_od, "seq", 2)
        far_ib = trade(far_ia, "dp", 1)
        near_ia = trade(far_ia, "seq", 1)
        (cot_far,) = gate((trade(their_cot, "seq", 2),), weight=WEIGHT)
        pairs = width // PAIR
        early = 2
        args = (query, kv, kv_far, mark_query, mark_key)
        o_a, extra_a, done_a = attend(0, early, *args)
        far_oa, far_ib = gate((far_oa, far_ib), (done_a,), weight=10 * WEIGHT)
        far_ob = trade(far_oa, "dp", 1)
        near_oa = trade(far_oa, "seq", 1)
        near_ib = trade(far_ib, "seq", 1)
        o_b, extra_b, done_b = attend(early, pairs - early, *args, late=(done_a, far_oa, near_ia))
        (far_ob,) = gate((far_ob,), (done_b,))
        near_ob = trade(far_ob, "seq", 1)
        blocks_in = (low_in, near_i, far_ia, far_ib, near_ia, near_ib)
        blocks_od = (low_od, near_o, far_oa, far_ob, near_oa, near_ob)

        mixed, mixed_far, dx1, do, keep_rest, send_rest, _ = middle(
            at, valid, tokens, far, cotangent, cot_far, o_a, o_b, gain_low[1:], blocks_in, blocks_od
        )
        got_rest = trade(send_rest, "seq", 1)
        two = pairs // 3
        near_args = (query, kv, kv_far)
        back_args = (mark_key, do, cos_part, sin_part)
        dq0, own0, give0, back0 = attend_back(0, 0, two, *near_args, extra_a, o_a, *back_args)
        *r1, r1_done = first_sums(at, keep_rest, got_rest, late=(back0,))
        got_ra, got_rb = trade(r1[1], "seq", 2), trade(r1[3], "dp", 1)
        got0 = trade(give0, "seq", 1)
        dq1, own1, give1, back1 = attend_back(
            two, two - early, two, *near_args, extra_b, o_b, *back_args, late=(r1_done,)
        )
        got1 = trade(give1, "seq", 1)
        dq2, own2, give2, back2 = attend_back(
            2 * two, 2 * two - early, pairs - 2 * two, *near_args, extra_b, o_b, *back_args,
            late=(back1, got0),
        )
        got2 = trade(give2, "seq", 1)
        *r2, r2_done = second_sums(at, r1[0], got_ra, r1[2], got_rb, late=(back2, got1))
        got_ra, got_rb = gate(
            (trade(r2[1], "dp", 1), trade(r2[3], "seq", 2)), weight=WEIGHT
        )
        dqkv, normed_t, send_qkv, send_done = qkv_send(
            at, normed, (dq0, dq1, dq2), (own0, own1, own2), (got0, got1, got2),
            cos_part, sin_part, late=(r2_done,),
        )
        got_qkv = trade(send_qkv, "seq", 1)
        inner_lanes = w_in.shape[1]
        lanes = (inner_lanes, keep_rest.shape[2] - inner_lanes)
        inner, give_inner, folded, give_folded, r3_done = third_sums(
            at, lanes, r2[0], got_ra, r2[2], got_rb, late=(send_done,)
        )
        got_inner, got_folded = trade(give_inner, "dp", 2), trade(give_folded, "dp", 2)
        keep_qkv, _ = qkv_keep(at, normed_t, dqkv, late=(r3_done,))
        *q1, q1_done = first_sums(at, keep_qkv, got_qkv)
        got_qa, got_qb = trade(q1[1], "seq", 2), trade(q1[3], "dp", 1)
        grad, grad_far, grad_done = input_back(
            at, tokens, far, gain_low[:1], dx1, dqkv, blocks_qkv, late=(q1_done,)
        )
        *rest, rest_done = add((inner, folded), (got_inner, got_folded), late=(grad_done,))
        rest_got = [trade(v, "dp", far_bits[0]) for v in rest]
        *q2, q2_done = second_sums(at, q1[0], got_qa, q1[2], got_qb, late=(rest_done,))
        got_qa, got_qb = gate(
            (trade(q2[1], "dp", 1), trade(q2[3], "seq", 2)), weight=10 * WEIGHT
        )
        qkv, give_qkv, q3_done = third_sums(
            at, (3 * width,), q2[0], got_qa, q2[2], got_qb, late=(rest_got[0],)
        )
        (mixed_far,) = gate((mixed_far,), (q2_done,))
        mixed_far = trade(mixed_far, "seq", 2)
        (grad_far,) = gate((grad_far,), (q3_done,))
        grad_far = trade(grad_far, "seq", 2)
        qkv, qkv_done = add(
            (qkv,), (trade(give_qkv, "dp", 2),), late=(rest_got[1], mixed_far)
        )
        for bit in far_bits[1:]:
            *rest, rest_done = add(rest, rest_got)
            rest_got = [trade(v, "dp", bit) for v in rest]
        *rest, rest_done = add(rest, rest_got, late=(qkv_done,))

        beside = [trade(v, "dp", 2) for v in rest]
        other = [trade(v, "dp", 1) for v in rest]
        mixed, grad, fill_done = fill(at, mixed, mixed_far, grad, grad_far)
        late = (rest_done, fill_done, *beside, *other)
        for bit in far_bits:
            qkv, qkv_done = add((qkv,), (trade(qkv, "dp", bit),), late=late)
            late = ()
        square, _ = squares(at, qkv, w_qkv, rest[0], w_in, gains, rest[1])
        qkv_beside, qkv_other = trade(qkv, "dp", 2), trade(qkv, "dp", 1)
        rest_parts = [(v, b, o, trade(b, "dp", 1)) for v, b, o in zip(rest, beside, other)]
        qkv_parts = (qkv, qkv_beside, qkv_other, trade(qkv_beside, "dp", 1))
        for axis, bit, late in (
            ("seq", 2, ()),
            ("seq", 1, (qkv_beside, qkv_other)),
            ("dp", 2, [parts[3] for parts in rest_parts]),
            ("dp", 1, ()),
        ):
            square, _ = add((square,), (trade(square, axis, bit),), late=late)

        (new_in, first_in, second_in, new_out, first_out, second_out,
         new_down, first_down, second_down, row, _) = update_rest(
            at, square, (w_in, m_in, v_in), rest_parts[0],
            (w_out, m_out, v_out), (w_down, m_down, v_down), rest_parts[1], (),
        )
        (new_qkv, first_qkv, second_qkv, new_gains, first_gains, second_gains, norm, _) = (
            update_last(
                at, square, (w_qkv, m_qkv, v_qkv), qkv_parts, row, (gains, m_gains, v_gains)
            )
        )
        return (
            mixed,
            grad,
            norm[0, 0],
            new_qkv, new_out, new_in, new_down, new_gains,
            first_qkv, first_out, first_in, first_down, first_gains,
            second_qkv, second_out, second_in, second_down, second_gains,
        )

    return on_device


def solution(mesh):
    rows, matrix, gain = P("dp", "seq", None), P("seq", None), P(None, "seq")
    weights = (matrix,) * 4 + (gain,)
    return jax.shard_map(
        make(mesh.shape["dp"], mesh.shape["seq"]),
        mesh=mesh,
        in_specs=(rows, rows, P("dp", None), P("dp")) + weights * 3,
        out_specs=(rows, rows, P()) + weights * 3,
        check_vma=False,
    )
```

```python
import functools
import math

import jax
import jax.numpy as jnp
from jax import lax
from jax.experimental import pallas as pl
from jax.experimental.pallas import tpu as pltpu
from jax.sharding import PartitionSpec as P

HEADS = 12
HEAD_DIM = 64
PAIR = 2 * HEAD_DIM
STEP_COUNT = 10
EPS_NORM = 1e-05
ROPE_BASE = 160000.0
NEG_FILL = -1e30
CLIP_LIMIT = 10.0
BETA_FIRST = 0.9
BETA_SECOND = 0.98
EPS_ADAM = 1e-06
STEP_RATES = (0.1, 0.5, 0.1, 0.1, 1.0)
DECAY_RATES = (0.01, 0.01, 0.01, 0.01, 0.0)
DOCS = 5
LOW = jnp.bfloat16
FULL = jnp.float32
SCALE = 1.0 / math.sqrt(HEAD_DIM)
WEIGHT = 20_000_000_000


def doc_positions(segment_ids):
    seq_len = segment_ids.shape[-1]
    places = jnp.arange(seq_len, dtype=jnp.int32)
    first_mark = jnp.ones((1,), jnp.bool_)
    change = jnp.concatenate([first_mark, segment_ids[1:] != segment_ids[:-1]])
    starts = lax.cummax(jnp.where(change, places, 0), axis=0)
    return places - starts


def rope_tables(positions):
    half_dim = HEAD_DIM // 2
    exponents = jnp.arange(half_dim, dtype=jnp.float32) * (2.0 / HEAD_DIM)
    inv_freq = ROPE_BASE ** (-exponents)
    angles = positions.astype(jnp.float32)[:, None] * inv_freq
    cos_part, sin_part = jnp.cos(angles), jnp.sin(angles)
    return (
        jnp.concatenate([cos_part] * 4, axis=1),
        jnp.concatenate([-sin_part, sin_part] * 2, axis=1),
    )


def adam_step(weight, first_old, second_old, gradient, factor, step_rate, decay_rate):
    clipped = gradient * factor
    first_new = BETA_FIRST * first_old + (1.0 - BETA_FIRST) * clipped
    second_new = BETA_SECOND * second_old + (1.0 - BETA_SECOND) * clipped * clipped
    root = second_new * lax.rsqrt(second_new) * (1.0 - BETA_SECOND**STEP_COUNT) ** -0.5
    step = first_new * (step_rate / (1.0 - BETA_FIRST**STEP_COUNT)) / (root + EPS_ADAM)
    return (weight * (1.0 - step_rate * decay_rate) - step, first_new, second_new)


def mul(left, right):
    return lax.dot_general(left, right, (((1,), (0,)), ((), ())), preferred_element_type=FULL)


def mul_t(left, right):
    return lax.dot_general(left, right, (((1,), (1,)), ((), ())), preferred_element_type=FULL)


def normalize(values):
    centered = values - jnp.mean(values, axis=-1, keepdims=True)
    root = lax.rsqrt(jnp.mean(centered * centered, axis=-1, keepdims=True) + EPS_NORM)
    return centered * root, root


def normalize_back(grad, gain, scaled, root):
    t = grad * gain
    back = root * (
        t
        - jnp.mean(t, axis=-1, keepdims=True)
        - scaled * jnp.mean(t * scaled, axis=-1, keepdims=True)
    )
    return back


def turn(values, cos_part, sin_part):
    lane = lax.broadcasted_iota(jnp.int32, values.shape, 1)
    swapped = jnp.where(
        lane % HEAD_DIM < HEAD_DIM // 2,
        pltpu.roll(values, PAIR - HEAD_DIM // 2, 1),
        pltpu.roll(values, HEAD_DIM // 2, 1),
    )
    return values * cos_part + swapped * sin_part


def three_parts(values):
    high = values.astype(LOW).astype(FULL)
    rest = values - high
    mid = rest.astype(LOW).astype(FULL)
    return high, mid, rest - mid


def wait_all(copies):
    for copy in copies:
        copy.wait()


def put(source, target, sem):
    copy = pltpu.make_async_copy(source, target, sem)
    copy.start()
    return copy


PIECES = ((0, None), (1, None), (2, 0), (2, 1), (3, 0), (3, 1))


def load_blocks(at_ref, blocks, whole, sem):
    rows = blocks[0].shape[0]
    copies = []
    for i, (bits, part) in enumerate(PIECES):
        start = (at_ref[0] ^ bits) * rows
        size = rows
        if part is not None:
            size = rows // 2
            start += (at_ref[1] ^ part) * size
        target = whole.at[pl.ds(pl.multiple_of(start, size), size), :]
        copies.append(put(blocks[i], target, sem.at[i]))
    return copies


def load_folded(at_ref, blocks, w_out, w_down, sem):
    rows, width = blocks[0].shape[0], w_out.shape[1]
    short, last = rows // 2, width // 2
    copies = []

    def copy(source, target):
        copies.append(put(source, target, sem.at[len(copies)]))

    for i, (bits, part) in enumerate(PIECES):
        owner = at_ref[0] ^ bits
        base = owner * (rows + short)
        first = 0 if part is None else (at_ref[1] ^ part) * short
        size = rows if part is None else short
        for lanes, whole, start in ((0, w_out, owner * rows), (width, w_down, base)):
            span = pl.ds(pl.multiple_of(start + first, short), size)
            copy(blocks[i].at[:, pl.ds(lanes, width)], whole.at[span, :])
        span = pl.ds(pl.multiple_of(base + rows, short), short)
        if part is None:
            for fold in range(2):
                copy(
                    blocks[i].at[pl.ds(fold * short, short), pl.ds(2 * width, last)],
                    w_down.at[span, pl.ds(fold * last, last)],
                )
        else:
            lanes = pl.ds(pl.multiple_of((at_ref[1] ^ part) * last, last), last)
            copy(blocks[i].at[:, pl.ds(2 * width, last)], w_down.at[span, lanes])
    return copies


def fold(out, w_out, w_down, first):
    rows, width = w_out.shape
    short, last = rows // 2, width // 2
    out[:, first : first + width] = w_out[...].astype(LOW)
    out[:, first + width : first + 2 * width] = w_down[:rows, :].astype(LOW)
    for i in range(2):
        out[i * short : (i + 1) * short, first + 2 * width :] = w_down[
            rows:, i * last : (i + 1) * last
        ].astype(LOW)


def prepare_first_kernel(at_ref, w_ref, gains_ref, half_ref, gains_out, wide, sem):
    short = half_ref.shape[0]
    span = pl.ds(pl.multiple_of(at_ref[1] * short, short), short)
    copy = put(w_ref.at[span, :], wide, sem.at[0])
    gains_out[...] = gains_ref[...].astype(LOW)
    copy.wait()
    half_ref[...] = wide[...].astype(LOW)


def prepare_rest_kernel(at_ref, tokens_ref, in_ref, out_ref, down_ref, qkv_ref, cot_ref,
                        their_tokens, low_in, half_in, low_od, half_od, low_qkv, their_cot,
                        in_wide, out_wide, down_wide, qkv_wide, sem):
    slot = 1 - at_ref[2]
    copies = [
        put(source, target, sem.at[i])
        for i, (source, target) in enumerate((
            (tokens_ref.at[slot], their_tokens), (in_ref, in_wide), (out_ref, out_wide),
            (down_ref, down_wide), (qkv_ref, qkv_wide), (cot_ref.at[slot], their_cot),
        ))
    ]
    short = half_in.shape[0]
    span = pl.ds(pl.multiple_of(at_ref[1] * short, short), short)
    copies[1].wait()
    low_in[...] = in_wide[...].astype(LOW)
    half_in[...] = in_wide[span, :].astype(LOW)
    copies[2].wait()
    copies[3].wait()
    fold(low_od, out_wide, down_wide, 0)
    half_od[...] = low_od[span, :]
    copies[4].wait()
    low_qkv[...] = qkv_wide[...].astype(LOW)
    copies[0].wait()
    copies[5].wait()


def project_kernel(at_ref, tokens_ref, far_ref, gain_ref, cos_ref, sin_ref, w0, w1, w2, w3, w4, w5,
                   normed_ref, query_ref, kv_ref, weight, sem):
    copies = load_blocks(at_ref, (w0, w1, w2, w3, w4, w5), weight, sem)
    rows, width = far_ref.shape
    for part in range(2):
        values = tokens_ref[at_ref[2]] if part == 0 else far_ref[...]
        scaled, _ = normalize(values.astype(FULL))
        normed_ref[pl.ds(part * rows, rows), :] = (scaled * gain_ref[...]).astype(LOW)
    wait_all(copies)
    for part in range(2):
        span = pl.ds(part * rows, rows)
        normed = normed_ref[span, :]
        cos_part, sin_part = cos_ref[span, :], sin_ref[span, :]
        for pair in range(2 * width // PAIR):
            lanes = pl.ds(pair * PAIR, PAIR)
            if pair % 2 == 0:
                both = mul(normed, weight[:, pl.ds(pair * PAIR, 2 * PAIR)])
            raw = both[:, (pair % 2) * PAIR : (pair % 2 + 1) * PAIR]
            turned = turn(raw, cos_part, sin_part)
            if pair < width // PAIR:
                query_ref[span, lanes] = (turned * SCALE).astype(LOW)
            else:
                kv_ref[0, span, pl.ds(pair * PAIR - width, PAIR)] = turned.astype(LOW)
        kv_ref[1, span, :] = mul(normed, weight[:, 2 * width :]).astype(LOW)


def head_lanes(head, shape):
    lane = lax.broadcasted_iota(jnp.int32, shape, 1)
    return (lane < HEAD_DIM) if head == 0 else (lane >= HEAD_DIM)


def pick(head, inside, outside):
    return jnp.where(head_lanes(head, inside.shape), inside, outside)


def attend_kernel(query_ref, near_ref, far_ref, mark_query_ref, mark_key_ref, o_ref, extra_ref):
    rows = query_ref.shape[0]
    query = query_ref[...]
    mark_query = mark_query_ref[...]
    parts = [
        (near_ref[0], jnp.transpose(near_ref[1]), mark_key_ref[:rows, :]),
        (far_ref[0], jnp.transpose(far_ref[1]), mark_key_ref[rows:, :]),
    ]
    outs, logs = [], []
    for head in range(2):
        query_head = pick(head, query, mark_query)
        scores = [mul_t(pick(head, key, mark), query_head) for key, _, mark in parts]
        top = jnp.maximum(
            jnp.max(scores[0], axis=0, keepdims=True), jnp.max(scores[1], axis=0, keepdims=True)
        )
        exps = [jnp.exp(score - top) for score in scores]
        total = jnp.sum(exps[0], axis=0, keepdims=True) + jnp.sum(exps[1], axis=0, keepdims=True)
        span = slice(head * HEAD_DIM, (head + 1) * HEAD_DIM)
        out = sum(mul(value_t[span], e.astype(LOW)) for (_, value_t, _), e in zip(parts, exps))
        outs.append(out / total)
        logs.append(top + jnp.log(total))
    o_ref[...] = jnp.transpose(jnp.concatenate(outs)).astype(LOW)
    line = lax.broadcasted_iota(jnp.int32, (PAIR, rows), 0)
    extra = jnp.zeros((PAIR, rows), FULL)
    for head in range(2):
        base = DOCS + (HEAD_DIM if head == 0 else 0)
        for i, piece in enumerate(three_parts(-logs[head])):
            extra = jnp.where(line == base + i, piece, extra)
    extra_ref[...] = jnp.transpose(extra).astype(LOW) + mark_query


def attend_back_kernel(query_ref, near_ref, far_ref, extra_ref, mark_key_ref, o_ref, do_ref,
                       cos_ref, sin_ref, dq_ref, keep_ref, send_ref):
    rows = query_ref.shape[0]
    query, extra, do = query_ref[...], extra_ref[...], do_ref[...]
    inner_all = do.astype(FULL) * o_ref[...].astype(FULL)
    lane = lax.broadcasted_iota(jnp.int32, (rows, PAIR), 1)
    zero = jnp.zeros((rows, PAIR), LOW)
    grads_query = []
    sums = [[None, None], [None, None]]
    keys_t = [jnp.transpose(near_ref[0]), jnp.transpose(far_ref[0])]
    for head in range(2):
        inside = head_lanes(head, (rows, PAIR))
        inner = jnp.sum(jnp.where(inside, inner_all, 0.0), axis=1, keepdims=True)
        base = DOCS + (HEAD_DIM if head == 0 else 0)
        tail = jnp.zeros((rows, PAIR), FULL)
        for i, piece in enumerate(three_parts(-inner)):
            tail = jnp.where(lane == base + i, piece, tail)
        query_head = pick(head, query, extra)
        do_head = pick(head, do, tail.astype(LOW))
        query_only = pick(head, query, zero)
        do_only = pick(head, do, zero)
        span = slice(head * HEAD_DIM, (head + 1) * HEAD_DIM)
        grad_query = 0.0
        for part, ref in enumerate((near_ref, far_ref)):
            mark = mark_key_ref[pl.ds(part * rows, rows), :]
            probs = jnp.exp(mul_t(pick(head, ref[0], mark), query_head))
            grad_probs = mul_t(pick(head, ref[1], mark), do_head)
            grad_scores = (probs * grad_probs).astype(LOW)
            grad_value = mul(probs.astype(LOW), do_only)
            grad_key = mul(grad_scores, query_only)
            grad_query += mul(keys_t[part][span], grad_scores)
            if head == 0:
                sums[part] = [grad_key, grad_value]
            else:
                sums[part] = [sums[part][0] + grad_key, sums[part][1] + grad_value]
        grads_query.append(grad_query)
    turned = turn(
        jnp.transpose(jnp.concatenate(grads_query)) * SCALE, cos_ref[...], -sin_ref[...]
    )
    dq_ref[...] = turned.astype(LOW)
    for i in range(2):
        keep_ref[i] = sums[0][i].astype(LOW)
        send_ref[i] = sums[1][i].astype(LOW)


def middle_kernel(at_ref, live_ref, tokens_ref, far_ref, cot_ref, cot_far_ref, oa_ref, ob_ref,
                  gain_ref, i0, i1, i2, i3, i4, i5, d0, d1, d2, d3, d4, d5,
                  mixed_ref, mixed_far_ref, dx1_ref, do_ref, keep_ref, send_ref,
                  w_out, w_in, w_down, o_all, o_t, a2_t, h_t, dm_all, duw_all, db_all,
                  mixed, dx1_all, do_all, keep, send, sem, fold_sem, out_sem):
    place, slot = at_ref[0], at_ref[2]
    live = live_ref[slot].astype(FULL)
    copies_down = load_folded(at_ref, (d0, d1, d2, d3, d4, d5), w_out, w_down, fold_sem)
    copies_in = load_blocks(at_ref, (i0, i1, i2, i3, i4, i5), w_in, sem)
    rows, width = far_ref.shape
    share = width // 4
    short, units = share // 2, w_down.shape[0]
    gain = gain_ref[...]
    o_all[:, : oa_ref.shape[1]] = oa_ref[...]
    o_all[:, oa_ref.shape[1] :] = ob_ref[...]
    copies = []
    for part in range(2):
        span = pl.ds(part * rows, rows)
        o = o_all[span, :]
        values = tokens_ref[slot] if part == 0 else far_ref[...]
        if part == 0:
            wait_all(copies_down)
        x1 = values.astype(FULL) + live * mul(o, w_out[...])
        scaled, root = normalize(x1)
        a2 = (scaled * gain).astype(LOW)
        if part == 0:
            wait_all(copies_in)
        u = mul(a2, w_in[:, :units])
        w = mul(a2, w_in[:, units:])
        phi = 0.5 * (1.0 + lax.erf(u * math.sqrt(0.5)))
        gelu = u * phi
        h = (gelu * w).astype(LOW)
        mixed[span, :] = (x1 + live * mul(h, w_down[...])).astype(LOW)
        target = mixed_ref.at[slot] if part == 0 else mixed_far_ref
        copies.append(put(mixed.at[span, :], target, out_sem.at[len(copies)]))
        cot = (cot_ref[slot] if part == 0 else cot_far_ref[...]).astype(FULL)
        dm = (live * cot).astype(LOW)
        dh = mul_t(dm, w_down[...])
        slope = phi + u * (jnp.exp(-0.5 * u * u) * (1.0 / math.sqrt(2.0 * math.pi)))
        duw_all[span, :units] = (dh * w * slope).astype(LOW)
        duw_all[span, units:] = (dh * gelu).astype(LOW)
        da2 = mul_t(duw_all[span, :], w_in[...])
        dx1 = cot + normalize_back(da2, gain, scaled, root)
        dx1_all[span, :] = dx1
        copies.append(put(dx1_all.at[span, :], dx1_ref.at[span, :], out_sem.at[len(copies)]))
        db = (live * dx1).astype(LOW)
        do_all[span, :] = mul_t(db, w_out[...]).astype(LOW)
        copies.append(put(do_all.at[span, :], do_ref.at[span, :], out_sem.at[len(copies)]))
        db_all[span, :] = db
        dm_all[span, :] = dm
        o_t[:, span] = jnp.transpose(o)
        a2_t[:, span] = jnp.transpose(a2)
        h_t[:, span] = jnp.transpose(h)
    dm, duw, db = dm_all[...], duw_all[...], db_all[...]
    for j, out, target in ((1, send, send_ref), (3, send, send_ref), (0, keep, keep_ref), (2, keep, keep_ref)):
        span = pl.ds(pl.multiple_of((place ^ j) * share, share), share)
        base = (place ^ j) * (share + short)
        down = pl.ds(pl.multiple_of(base, short), share)
        down_last = pl.ds(pl.multiple_of(base + share, short), short)
        at = 2 * units
        out[j // 2, :, :at] = mul(a2_t[span, :], duw).astype(LOW)
        out[j // 2, :, at : at + width] = mul(o_t[span, :], db).astype(LOW)
        at += width
        out[j // 2, :, at : at + width] = mul(h_t[down, :], dm).astype(LOW)
        at += width
        last = mul(h_t[down_last, :], dm).astype(LOW)
        out[j // 2, :short, at:] = last[:, : width // 2]
        out[j // 2, short:, at:] = last[:, width // 2 :]
        copies.append(put(out.at[j // 2], target.at[j // 2], out_sem.at[len(copies)]))
    wait_all(copies)


def send_kernel(count, at_ref, *refs):
    normed_ref = refs[0]
    dqs, owns, gots = (refs[1 + i * count : 1 + (i + 1) * count] for i in range(3))
    (cos_ref, sin_ref, dqkv_ref, normed_t_ref, send_ref,
     dqkv, normed_t, send, sem) = refs[1 + 3 * count :]
    width = normed_ref.shape[1]
    part_width = width // count
    normed_t[...] = jnp.transpose(normed_ref[...])
    copies = [put(normed_t, normed_t_ref, sem.at[0])]
    cos_part, sin_part = cos_ref[...], -sin_ref[...]
    for part, (dq, own, got) in enumerate(zip(dqs, owns, gots)):
        base = part * part_width
        dqkv[:, pl.ds(base, part_width)] = dq[...]
        dqkv[:, pl.ds(2 * width + base, part_width)] = (
            own[1].astype(FULL) + got[1].astype(FULL)
        ).astype(LOW)
        for pair in range(part_width // PAIR):
            lanes = pl.ds(pair * PAIR, PAIR)
            raw = own[0, :, lanes].astype(FULL) + got[0, :, lanes].astype(FULL)
            dqkv[:, pl.ds(width + base + pair * PAIR, PAIR)] = turn(raw, cos_part, sin_part).astype(
                LOW
            )
    copies.append(put(dqkv, dqkv_ref, sem.at[1]))
    right = dqkv[...]
    share = send.shape[1]
    for j in (1, 3):
        start = pl.multiple_of((at_ref[0] ^ j) * share, share)
        send[j // 2] = mul(normed_t[pl.ds(start, share), :], right).astype(LOW)
        copies.append(put(send.at[j // 2], send_ref.at[j // 2], sem.at[len(copies)]))
    wait_all(copies)


def keep_kernel(at_ref, normed_t_ref, dqkv_ref, keep_ref, keep, sem):
    right = dqkv_ref[...]
    share = keep.shape[1]
    copies = []
    for j in (0, 2):
        start = pl.multiple_of((at_ref[0] ^ j) * share, share)
        keep[j // 2] = mul(normed_t_ref[pl.ds(start, share), :], right).astype(LOW)
        copies.append(put(keep.at[j // 2], keep_ref.at[j // 2], sem.at[len(copies)]))
    wait_all(copies)


def input_kernel(at_ref, tokens_ref, far_ref, gain_ref, dx1_ref, dqkv_ref, w0, w1, w2, w3, w4, w5,
                 grad_ref, grad_far_ref, weight, grad_own, sem, out_sem):
    wait_all(load_blocks(at_ref, (w0, w1, w2, w3, w4, w5), weight, sem))
    rows = far_ref.shape[0]
    gain = gain_ref[...]
    for part in (1, 0):
        span = pl.ds(part * rows, rows)
        values = tokens_ref[at_ref[2]] if part == 0 else far_ref[...]
        scaled, root = normalize(values.astype(FULL))
        back = normalize_back(mul_t(dqkv_ref[span, :], weight[...]), gain, scaled, root)
        grad = dx1_ref[span, :] + back
        if part == 1:
            grad_far_ref[...] = grad.astype(LOW)
        else:
            grad_own[...] = grad
    put(grad_own, grad_ref.at[at_ref[2]], out_sem.at[0]).wait()


def shaped(*shape, kind=LOW):
    return jax.ShapeDtypeStruct(shape, kind)


IN_SMEM = pl.BlockSpec(memory_space=pltpu.SMEM)
IN_VMEM = pl.BlockSpec(memory_space=pltpu.VMEM)
IN_ANY = pl.BlockSpec(memory_space=pl.ANY)


def params(mebibytes):
    return pltpu.CompilerParams(vmem_limit_bytes=int(mebibytes * 1024 * 1024))


def call(kernel, args, in_specs, out_shape, out_specs, late=(), **options):
    if not isinstance(out_shape, tuple):
        out_shape, out_specs = (out_shape,), (out_specs,)
    count, skip, outs = len(args), len(late), len(out_shape)

    def body(*refs):
        outs_at = count + skip
        return kernel(*refs[:count], *refs[outs_at : outs_at + outs], *refs[outs_at + outs + 1 :])

    return pl.pallas_call(
        body,
        in_specs=list(in_specs) + [IN_ANY] * skip,
        out_shape=out_shape + (shaped(8, 128, kind=FULL),),
        out_specs=out_specs + (IN_ANY,),
        **options,
    )(*args, *late)


def gate(values, late=(), weight=0):
    hint = {}
    if weight:
        hint["cost_estimate"] = pl.CostEstimate(
            flops=weight, transcendentals=0, bytes_accessed=0
        )
    return call(
        lambda *refs: None,
        values,
        late=late,
        out_shape=tuple(jax.ShapeDtypeStruct(v.shape, v.dtype) for v in values),
        in_specs=[IN_ANY] * len(values),
        out_specs=(IN_ANY,) * len(values),
        input_output_aliases={i: i for i in range(len(values))},
        compiler_params=params(1),
        name="gate",
        **hint,
    )[: len(values)]


def in_hbm(value):
    return pltpu.with_memory_space_constraint(value, pltpu.HBM)


def prepare_first(at, weight, gains):
    rows, width = weight.shape
    return call(
        prepare_first_kernel,
        (at, in_hbm(weight), gains),
        out_shape=(shaped(rows // 2, width), shaped(*gains.shape)),
        in_specs=[IN_SMEM, IN_ANY, IN_VMEM],
        out_specs=(IN_VMEM,) * 2,
        scratch_shapes=[pltpu.VMEM((rows // 2, width), FULL), pltpu.SemaphoreType.DMA((1,))],
        compiler_params=params(6),
        name="prepare_first",
    )


def prepare_rest(at, tokens, w_in, w_out, w_down, w_qkv, cotangent, late):
    rows, width = w_out.shape
    folded = 2 * width + width // 2
    return call(
        prepare_rest_kernel,
        (at, *[in_hbm(v) for v in (tokens, w_in, w_out, w_down, w_qkv, cotangent)]),
        late=late,
        out_shape=(
            shaped(*tokens.shape[1:]),
            shaped(*w_in.shape),
            shaped(rows // 2, w_in.shape[1]),
            shaped(rows, folded),
            shaped(rows // 2, folded),
            shaped(*w_qkv.shape),
            shaped(*cotangent.shape[1:]),
        ),
        in_specs=[IN_SMEM] + [IN_ANY] * 6,
        out_specs=(IN_ANY,) + (IN_VMEM,) * 5 + (IN_ANY,),
        scratch_shapes=[
            pltpu.VMEM(v.shape, FULL) for v in (w_in, w_out, w_down, w_qkv)
        ] + [pltpu.SemaphoreType.DMA((6,))],
        compiler_params=params(16),
        name="prepare_rest",
    )


def project(at, tokens, far, gain, cos_part, sin_part, blocks, late):
    rows, width = 2 * far.shape[0], far.shape[1]
    return call(
        project_kernel,
        (at, tokens, far, gain, cos_part, sin_part, *blocks),
        late=late,
        out_shape=(shaped(rows, width), shaped(rows, width), shaped(2, rows, width)),
        in_specs=[IN_SMEM] + [IN_VMEM] * 5 + [IN_ANY] * 6,
        out_specs=(IN_VMEM,) * 3,
        scratch_shapes=[pltpu.VMEM((width, 3 * width), LOW), pltpu.SemaphoreType.DMA((6,))],
        compiler_params=params(16),
        name="project",
    )


def attend(first, count, query, near, far, mark_query, mark_key, late=()):
    rows = query.shape[0]
    row_spec = pl.BlockSpec((rows, PAIR), lambda i: (0, i + first))
    kv_spec = pl.BlockSpec((2, rows, PAIR), lambda i: (0, 0, i + first))
    out_spec = pl.BlockSpec((rows, PAIR), lambda i: (0, i))
    return call(
        attend_kernel,
        (query, near, far, mark_query, mark_key),
        late=late,
        grid=(count,),
        out_shape=(shaped(rows, count * PAIR), shaped(rows, count * PAIR)),
        in_specs=[
            row_spec,
            kv_spec,
            kv_spec,
            pl.BlockSpec((rows, PAIR), lambda i: (0, 0)),
            pl.BlockSpec((2 * rows, PAIR), lambda i: (0, 0)),
        ],
        out_specs=(out_spec, out_spec),
        compiler_params=params(16),
        name="attend",
    )


def attend_back(
    first, first_o, count, query, near, far, extra, o, mark_key, do, cos_part, sin_part, late=()
):
    rows = query.shape[0]
    row_spec = pl.BlockSpec((rows, PAIR), lambda i: (0, i + first))
    o_spec = pl.BlockSpec((rows, PAIR), lambda i: (0, i + first_o))
    kv_spec = pl.BlockSpec((2, rows, PAIR), lambda i: (0, 0, i + first))
    fixed = pl.BlockSpec((rows, PAIR), lambda i: (0, 0))
    out_row = pl.BlockSpec((rows, PAIR), lambda i: (0, i))
    out_kv = pl.BlockSpec((2, rows, PAIR), lambda i: (0, 0, i))
    return call(
        attend_back_kernel,
        (query, near, far, extra, mark_key, o, do, cos_part, sin_part),
        late=late,
        grid=(count,),
        out_shape=(
            shaped(rows, count * PAIR),
            shaped(2, rows, count * PAIR),
            shaped(2, rows, count * PAIR),
        ),
        in_specs=[
            row_spec,
            kv_spec,
            kv_spec,
            o_spec,
            pl.BlockSpec((2 * rows, PAIR), lambda i: (0, 0)),
            o_spec,
            row_spec,
            fixed,
            fixed,
        ],
        out_specs=(out_row, out_kv, out_kv),
        compiler_params=params(20),
        name="attend_back",
    )


def middle(at, live, tokens, far, cot, cot_far, o_a, o_b, gain, blocks_in, blocks_od):
    half, width = far.shape
    rows, share = 2 * half, width // 4
    units = blocks_in[0].shape[1] // 2
    total = 2 * units + blocks_od[0].shape[1]
    assert units == 4 * (share + share // 2)
    low = lambda *shape: pltpu.VMEM(shape, LOW)
    return call(
        middle_kernel,
        (at, live, tokens, far, cot, cot_far, o_a, o_b, gain, *blocks_in, *blocks_od),
        out_shape=(
            shaped(2, half, width),
            shaped(half, width),
            shaped(rows, width, kind=FULL),
            shaped(rows, width),
            shaped(2, share, total),
            shaped(2, share, total),
        ),
        in_specs=[IN_SMEM] * 2 + [IN_VMEM] * 7 + [IN_ANY] * 12,
        out_specs=(IN_ANY,) * 6,
        scratch_shapes=[
            low(width, width),
            low(width, 2 * units),
            low(units, width),
            low(rows, width),
            low(width, rows),
            low(width, rows),
            low(units, rows),
            low(rows, width),
            low(rows, 2 * units),
            low(rows, width),
            low(rows, width),
            pltpu.VMEM((rows, width), FULL),
            low(rows, width),
            low(2, share, total),
            low(2, share, total),
            pltpu.SemaphoreType.DMA((6,)),
            pltpu.SemaphoreType.DMA((20,)),
            pltpu.SemaphoreType.DMA((10,)),
        ],
        compiler_params=params(40),
        name="middle",
    )


def qkv_send(at, normed, dq, own, got, cos_part, sin_part, late):
    rows, width = normed.shape
    share = width // 4
    return call(
        functools.partial(send_kernel, len(dq)),
        (at, normed, *dq, *own, *got, cos_part, sin_part),
        late=late,
        out_shape=(
            shaped(rows, 3 * width),
            shaped(width, rows),
            shaped(2, share, 3 * width),
        ),
        in_specs=[IN_SMEM] + [IN_VMEM] * (3 + 3 * len(dq)),
        out_specs=(IN_ANY,) * 3,
        scratch_shapes=[
            pltpu.VMEM((rows, 3 * width), LOW),
            pltpu.VMEM((width, rows), LOW),
            pltpu.VMEM((2, share, 3 * width), LOW),
            pltpu.SemaphoreType.DMA((4,)),
        ],
        compiler_params=params(20),
        name="qkv_send",
    )


def qkv_keep(at, normed_t, dqkv, late):
    width, rows = normed_t.shape
    share = width // 4
    return call(
        keep_kernel,
        (at, normed_t, dqkv),
        late=late,
        out_shape=shaped(2, share, 3 * width),
        in_specs=[IN_SMEM] + [IN_VMEM] * 2,
        out_specs=IN_ANY,
        scratch_shapes=[
            pltpu.VMEM((2, share, 3 * width), LOW),
            pltpu.SemaphoreType.DMA((2,)),
        ],
        compiler_params=params(16),
        name="qkv_keep",
    )


def input_back(at, tokens, far, gain, dx1, dqkv, blocks, late):
    half, width = far.shape
    return call(
        input_kernel,
        (at, tokens, far, gain, dx1, dqkv, *blocks),
        late=late,
        out_shape=(shaped(2, half, width, kind=FULL), shaped(half, width)),
        in_specs=[IN_SMEM] + [IN_VMEM] * 5 + [IN_ANY] * 6,
        out_specs=(IN_ANY, IN_VMEM),
        scratch_shapes=[
            pltpu.VMEM((width, 3 * width), LOW),
            pltpu.VMEM((half, width), FULL),
            pltpu.SemaphoreType.DMA((6,)),
            pltpu.SemaphoreType.DMA((1,)),
        ],
        compiler_params=params(20),
        name="input_back",
    )


def first_sums_kernel(at_ref, keep, got, own_a, far_a, mine_b, give_b):
    cut, short = far_a.shape[0], give_b.shape[1]

    def add(block, start, size):
        span = pl.ds(start, size)
        return (keep[block, span, :].astype(FULL) + got[block, span, :].astype(FULL)).astype(LOW)

    far_a[...] = add(1, 0, cut)
    for block in range(2):
        give_b[block] = add(block, pl.multiple_of(cut + (1 - at_ref[1]) * short, short), short)
        mine_b[block] = add(block, pl.multiple_of(cut + at_ref[1] * short, short), short)
    own_a[...] = add(0, 0, cut)


def first_sums(at, keep, got, late=()):
    _, rows, width = keep.shape
    cut, short = rows // 2, rows // 4
    return call(
        first_sums_kernel,
        (at, keep, got),
        late=late,
        out_shape=(shaped(cut, width),) * 2 + (shaped(2, short, width),) * 2,
        in_specs=[IN_SMEM] + [IN_VMEM] * 2,
        out_specs=(IN_VMEM,) * 4,
        compiler_params=params(20),
        name="first_sums",
    )


def second_sums_kernel(at_ref, own_a, got_a, mine_b, got_b, mine_a, give_a, near_b, far_b):
    short = mine_a.shape[0]
    for start, out in ((1 - at_ref[1], give_a), (at_ref[1], mine_a)):
        span = pl.ds(pl.multiple_of(start * short, short), short)
        out[...] = (own_a[span, :].astype(FULL) + got_a[span, :].astype(FULL)).astype(LOW)
    for block, out in ((1, far_b), (0, near_b)):
        out[...] = (mine_b[block].astype(FULL) + got_b[block].astype(FULL)).astype(LOW)


def second_sums(at, own_a, got_a, mine_b, got_b, late=()):
    _, short, width = mine_b.shape
    return call(
        second_sums_kernel,
        (at, own_a, got_a, mine_b, got_b),
        late=late,
        out_shape=(shaped(short, width),) * 4,
        in_specs=[IN_SMEM] + [IN_VMEM] * 4,
        out_specs=(IN_VMEM,) * 4,
        compiler_params=params(12),
        name="second_sums",
    )


def third_sums_kernel(at_ref, mine_a, got_a, near_b, got_b, keep, give):
    upper = mine_a[...].astype(FULL) + got_a[...].astype(FULL)
    lower = near_b[...].astype(FULL) + got_b[...].astype(FULL)
    keep[...] = jnp.where(at_ref[4] == 0, upper, lower).astype(LOW)
    give[...] = jnp.where(at_ref[4] == 0, lower, upper).astype(LOW)


def third_sums(at, mine_a, got_a, near_b, got_b, late=()):
    return call(
        third_sums_kernel,
        (at, mine_a, got_a, near_b, got_b),
        late=late,
        out_shape=(shaped(*mine_a.shape),) * 2,
        in_specs=[IN_SMEM] + [IN_VMEM] * 4,
        out_specs=(IN_VMEM,) * 2,
        compiler_params=params(12),
        name="third_sums",
    )


def squares_kernel(at_ref, qkv, w_qkv, rest, w_in, gains, out):
    inner = w_in.shape[1]
    total = jnp.sum(jnp.square(rest[:, inner:].astype(FULL)), keepdims=True)
    rows = qkv.shape[0]
    shape = (rows, gains.shape[1])
    offset = lax.broadcasted_iota(jnp.int32, shape, 1) - lax.broadcasted_iota(jnp.int32, shape, 0)
    for i, (piece, weight) in enumerate(((qkv, w_qkv), (rest, w_in))):
        start = at_ref[3]
        span = pl.ds(pl.multiple_of(start, 8), rows)
        values = piece[:, : weight.shape[1]].astype(FULL)
        sums = jnp.sum(weight[span, :].astype(LOW).astype(FULL) * values, axis=1, keepdims=True)
        gain = gains[i : i + 1, :].astype(LOW).astype(FULL)
        gain = jnp.sum(jnp.where(offset == start, gain, 0.0), axis=1, keepdims=True)
        total += jnp.sum(jnp.square(values), keepdims=True)
        total += jnp.sum(jnp.square(sums / gain), keepdims=True)
    out[...] = jnp.broadcast_to(total, out.shape)


def squares(*args):
    return call(
        squares_kernel,
        args,
        out_shape=shaped(8, 128, kind=FULL),
        in_specs=[IN_SMEM] + [IN_VMEM] * (len(args) - 1),
        out_specs=IN_VMEM,
        compiler_params=params(10),
        name="squares",
    )


def add_kernel(count, *refs):
    for i in range(count):
        out = refs[2 * count + i]
        out[...] = (refs[i][...].astype(FULL) + refs[count + i][...].astype(FULL)).astype(out.dtype)


def add(first, second, late=()):
    count = len(first)
    return call(
        functools.partial(add_kernel, count),
        (*first, *second),
        late=late,
        out_shape=tuple(jax.ShapeDtypeStruct(v.shape, v.dtype) for v in first),
        in_specs=[IN_VMEM] * (2 * count),
        out_specs=(IN_VMEM,) * count,
        compiler_params=params(8),
        name="add",
    )


def fill_kernel(at_ref, mixed_far, grad_far, mixed_in, grad_in, mixed, grad, wide, sem):
    first = put(mixed_far, mixed.at[1 - at_ref[2]], sem.at[0])
    wide[...] = grad_far[...].astype(FULL)
    put(wide, grad.at[1 - at_ref[2]], sem.at[1]).wait()
    first.wait()


def fill(at, mixed, mixed_far, grad, grad_far):
    return call(
        fill_kernel,
        (at, mixed_far, grad_far, mixed, grad),
        out_shape=(shaped(*mixed.shape), shaped(*grad.shape, kind=FULL)),
        in_specs=[IN_SMEM, IN_VMEM, IN_VMEM, IN_ANY, IN_ANY],
        out_specs=(IN_ANY,) * 2,
        input_output_aliases={3: 0, 4: 1},
        scratch_shapes=[pltpu.VMEM(grad_far.shape, FULL), pltpu.SemaphoreType.DMA((2,))],
        compiler_params=params(4),
        name="fill",
    )


def clip_factor(square_ref):
    norm = jnp.sqrt(square_ref[:1, :1])
    return jnp.minimum(1.0, CLIP_LIMIT / (norm + 1e-06))


def quarters(at_ref, parts):
    own, beside, other, other_beside = parts
    for i in range(4):
        same = at_ref[4] == i // 2
        near = jnp.where(same, own[...], beside[...])
        far = jnp.where(same, other[...], other_beside[...])
        yield jnp.where(at_ref[1] == i % 2, near, far).astype(FULL)


def gain_row(weight, gradient, start, shape):
    sums = jnp.sum(weight.astype(LOW).astype(FULL) * gradient, axis=1, keepdims=True)
    shape = (weight.shape[0], shape[1])
    offset = lax.broadcasted_iota(jnp.int32, shape, 1) - lax.broadcasted_iota(jnp.int32, shape, 0)
    return jnp.sum(jnp.where(offset == start, sums, 0.0), axis=0, keepdims=True)


class Update:
    def __init__(self, number, sources, news, targets, sem):
        self.number, self.sources, self.news, self.targets = number, sources, news, targets
        self.sem, self.out = sem, []

    def step(self, span, gradient, factor):
        weight = self.sources[0][span]
        results = adam_step(
            weight, self.sources[1][span], self.sources[2][span], gradient, factor,
            STEP_RATES[self.number], DECAY_RATES[self.number],
        )
        for result, new, target in zip(results, self.news, self.targets):
            new[span] = result
            self.out.append(put(new.at[span], target.at[span], self.sem.at[len(self.out)]))
        return weight


def update_rest_kernel(at_ref, square_ref, *refs):
    parts, refs = refs[:4], refs[4:]
    sources, targets, row_ref, news, sem = refs[:9], refs[9:18], refs[18], refs[19:28], refs[28]
    inner, out, down = (
        Update(number, *(group[3 * k : 3 * k + 3] for group in (sources, news, targets)), sem.at[k])
        for k, number in enumerate((2, 1, 3))
    )
    factor = clip_factor(square_ref)
    rows, width = sources[3].shape
    lanes = sources[0].shape[1]
    short, last = rows // 4, width // 2
    row = jnp.zeros(row_ref.shape, FULL)
    for i, gradient in enumerate(quarters(at_ref, parts)):
        span = (slice(i * short, (i + 1) * short), slice(None))
        part = gradient[:, :lanes]
        row += gain_row(inner.step(span, part, factor), part, i * short, row_ref.shape)
        out.step(span, gradient[:, lanes : lanes + width], factor)
        down.step(span, gradient[:, lanes + width : lanes + 2 * width], factor)
        start = rows + (i % 2) * short
        span = (slice(start, start + short), slice((i // 2) * last, (i // 2 + 1) * last))
        down.step(span, gradient[:, lanes + 2 * width :], factor)
    row_ref[...] = row
    wait_all(inner.out + out.out + down.out)


def update_rest(at, square, parts, inner, out, down):
    like = [jax.ShapeDtypeStruct(v.shape, FULL) for v in (*inner, *out, *down)]
    return call(
        update_rest_kernel,
        (at, square, *parts, *inner, *out, *down),
        out_shape=(*like, shaped(1, inner[0].shape[0], kind=FULL)),
        in_specs=[IN_SMEM] + [IN_VMEM] * 14,
        out_specs=(IN_ANY,) * 9 + (IN_VMEM,),
        scratch_shapes=[pltpu.VMEM(v.shape, FULL) for v in like]
        + [pltpu.SemaphoreType.DMA((3, 24))],
        compiler_params=params(28),
        name="update_rest",
    )


def update_last_kernel(at_ref, square_ref, row_ref, g_w, g_m, g_v, *refs):
    parts, refs = refs[:4], refs[4:]
    sources, targets = refs[:3], refs[3:6]
    g_w_out, g_m_out, g_v_out, norm_out = refs[6:10]
    news, sem = refs[10:13], refs[13]
    qkv = Update(0, sources, news, targets, sem)
    factor = clip_factor(square_ref)
    norm_out[...] = jnp.sqrt(square_ref[...])
    short = sources[0].shape[0] // 4
    row = jnp.zeros(row_ref.shape, FULL)
    for i, gradient in enumerate(quarters(at_ref, parts)):
        span = (slice(i * short, (i + 1) * short), slice(None))
        row += gain_row(qkv.step(span, gradient, factor), gradient, i * short, row_ref.shape)
    for i, values in enumerate((row, row_ref[...])):
        line = slice(i, i + 1)
        gradient = values / g_w[line, :].astype(LOW).astype(FULL)
        g_w_out[line, :], g_m_out[line, :], g_v_out[line, :] = adam_step(
            g_w[line, :], g_m[line, :], g_v[line, :], gradient, factor,
            STEP_RATES[4], DECAY_RATES[4],
        )
    wait_all(qkv.out)


def update_last(at, square, qkv, qkv_parts, row, gains):
    like = [jax.ShapeDtypeStruct(v.shape, FULL) for v in qkv]
    return call(
        update_last_kernel,
        (at, square, row, *gains, *qkv_parts, *qkv),
        out_shape=(
            *like,
            *[jax.ShapeDtypeStruct(v.shape, FULL) for v in gains],
            jax.ShapeDtypeStruct(square.shape, FULL),
        ),
        in_specs=[IN_SMEM] + [IN_VMEM] * 12,
        out_specs=(IN_ANY,) * 3 + (IN_VMEM,) * 4,
        scratch_shapes=[pltpu.VMEM(v.shape, FULL) for v in like]
        + [pltpu.SemaphoreType.DMA((12,))],
        compiler_params=params(18),
        name="update_last",
    )


def low_sum(*values):
    return sum(value.astype(FULL) for value in values).astype(LOW)


def index(value, i):
    return lax.dynamic_index_in_dim(value, i, 0, keepdims=False)


def make(dp_count, seq_count):
    assert seq_count == 4 and dp_count >= 8 and dp_count & (dp_count - 1) == 0
    far_bits = [1 << i for i in range(2, dp_count.bit_length() - 1)]

    def trade(value, axis, bit):
        size = seq_count if axis == "seq" else dp_count
        return lax.ppermute(value, axis, [(i, i ^ bit) for i in range(size)])

    def on_device(
        tokens, cotangent, segments, valid,
        w_qkv, w_out, w_in, w_down, gains,
        m_qkv, m_out, m_in, m_down, m_gains,
        v_qkv, v_out, v_in, v_down, v_gains,
    ):
        place = lax.axis_index("seq")
        group = lax.axis_index("dp")
        slot = place >> 1
        half = group & 1
        local_len, width = tokens.shape[1:]
        rows = 2 * local_len
        share = w_qkv.shape[0]
        side = (group >> 1) & 1
        quarter = share // 4
        at = jnp.stack([place, half, slot, side * 2 * quarter + half * quarter, side])

        half_qkv, low_gains, begun = prepare_first(at, w_qkv, gains)
        (far_qa,) = gate((trade(half_qkv, "seq", 2),), weight=10 * WEIGHT)
        (gain_far,) = gate((trade(low_gains, "seq", 2),), weight=20 * WEIGHT)
        their_tokens, low_in, half_in, low_od, half_od, low_qkv, their_cot, _ = prepare_rest(
            at, tokens, w_in, w_out, w_down, w_qkv, cotangent, (begun,)
        )
        near_q = trade(low_qkv, "seq", 1)
        far = trade(their_tokens, "seq", 2)
        far_qb = trade(far_qa, "dp", 1)
        near_qa = trade(far_qa, "seq", 1)
        near_qb = trade(far_qb, "seq", 1)
        (gain_far,) = gate((gain_far,), (far_qb,))
        gain_near = trade(jnp.stack([low_gains, gain_far]), "seq", 1)
        gain_stack = jnp.stack([low_gains, gain_near[0], gain_far, gain_near[1]])
        gain_low = jnp.concatenate(
            [index(gain_stack, b ^ place) for b in range(4)], axis=1
        ).astype(FULL)
        blocks_qkv = (low_qkv, near_q, far_qa, far_qb, near_qa, near_qb)
        low_in, low_od, half_in = gate((low_in, low_od, half_in), (far_qa,))
        near_i = trade(low_in, "seq", 1)
        near_o = trade(low_od, "seq", 1)
        (far_ia,) = gate((trade(half_in, "seq", 2),), weight=10 * WEIGHT)
        (half_od,) = gate((half_od,), (far,))

        seg = index(segments, slot)
        positions = doc_positions(seg).reshape(4, local_len)
        seg = seg.reshape(4, local_len)
        chunks = [place, place ^ 2, place ^ 1, place ^ 3]
        seg_keys = jnp.concatenate([index(seg, c) for c in chunks])
        pos = jnp.concatenate([index(positions, c) for c in chunks[:2]])
        cos_part, sin_part = rope_tables(pos)
        lane = jnp.arange(PAIR, dtype=jnp.int32)[None] % HEAD_DIM
        same = seg_keys[:, None] == lane
        mark_key = jnp.where(lane < DOCS, 1.0 - same, (lane < DOCS + 3) * 1.0).astype(LOW)
        mark_query = jnp.where((lane < DOCS) & same[:rows], NEG_FILL, 0.0).astype(LOW)

        normed, query, kv, _ = project(
            at, tokens, far, gain_low[:1], cos_part, sin_part, blocks_qkv,
            (far_ia, mark_key, mark_query),
        )
        kv_far = trade(kv, "seq", 1)
        far_oa = trade(half_od, "seq", 2)
        far_ib = trade(far_ia, "dp", 1)
        near_ia = trade(far_ia, "seq", 1)
        (cot_far,) = gate((trade(their_cot, "seq", 2),), weight=WEIGHT)
        pairs = width // PAIR
        early = 2
        args = (query, kv, kv_far, mark_query, mark_key)
        o_a, extra_a, done_a = attend(0, early, *args, late=(far_oa,))
        (far_ib,) = gate((far_ib,), (done_a,), weight=10 * WEIGHT)
        far_ob = trade(far_oa, "dp", 1)
        near_oa = trade(far_oa, "seq", 1)
        near_ib = trade(far_ib, "seq", 1)
        o_b, extra_b, done_b = attend(early, pairs - early, *args, late=(done_a, near_ia))
        (far_ob,) = gate((far_ob,), (done_b,))
        near_ob = trade(far_ob, "seq", 1)
        blocks_in = (low_in, near_i, far_ia, far_ib, near_ia, near_ib)
        blocks_od = (low_od, near_o, far_oa, far_ob, near_oa, near_ob)

        mixed, mixed_far, dx1, do, keep_rest, send_rest, _ = middle(
            at, valid, tokens, far, cotangent, cot_far, o_a, o_b, gain_low[1:], blocks_in, blocks_od
        )
        got_rest = trade(send_rest, "seq", 1)
        two = pairs // 3
        near_args = (query, kv, kv_far)
        back_args = (mark_key, do, cos_part, sin_part)
        dq0, own0, give0, back0 = attend_back(0, 0, two, *near_args, extra_a, o_a, *back_args)
        *r1, r1_done = first_sums(at, keep_rest, got_rest, late=(back0,))
        got_ra, got_rb = trade(r1[1], "seq", 2), trade(r1[3], "dp", 1)
        got0 = trade(give0, "seq", 1)
        dq1, own1, give1, back1 = attend_back(
            two, two - early, two, *near_args, extra_b, o_b, *back_args, late=(r1_done,)
        )
        got1 = trade(give1, "seq", 1)
        dq2, own2, give2, back2 = attend_back(
            2 * two, 2 * two - early, pairs - 2 * two, *near_args, extra_b, o_b, *back_args,
            late=(back1, got0),
        )
        got2 = trade(give2, "seq", 1)
        dqkv, normed_t, send_qkv, send_done = qkv_send(
            at, normed, (dq0, dq1, dq2), (own0, own1, own2), (got0, got1, got2),
            cos_part, sin_part, late=(got_ra, got_rb),
        )
        got_qkv = trade(send_qkv, "seq", 1)
        *r2, r2_done = second_sums(at, r1[0], got_ra, r1[2], got_rb, late=(send_done,))
        got_ra, got_rb = trade(r2[1], "dp", 1), trade(r2[3], "seq", 2)
        keep_qkv, _ = qkv_keep(at, normed_t, dqkv, late=(r2_done,))
        *q1, q1_done = first_sums(at, keep_qkv, got_qkv)
        got_qa, got_qb = trade(q1[1], "seq", 2), trade(q1[3], "dp", 1)
        grad, grad_far, grad_done = input_back(
            at, tokens, far, gain_low[:1], dx1, dqkv, blocks_qkv, late=(q1_done,)
        )
        rest, give_rest, r3_done = third_sums(
            at, r2[0], got_ra, r2[2], got_rb, late=(grad_done,)
        )
        got_rest = trade(give_rest, "dp", 2)
        *q2, q2_done = second_sums(at, q1[0], got_qa, q1[2], got_qb, late=(r3_done,))
        got_qa, got_qb = gate(
            (trade(q2[1], "dp", 1), trade(q2[3], "seq", 2)), weight=10 * WEIGHT
        )
        rest, rest_done = add((rest,), (got_rest,), late=(q2_done,))
        got_rest = trade(rest, "dp", far_bits[0])
        qkv, give_qkv, q3_done = third_sums(
            at, q2[0], got_qa, q2[2], got_qb, late=(rest_done,)
        )
        (mixed_far,) = gate((mixed_far,), (q2_done,))
        mixed_far = trade(mixed_far, "seq", 2)
        (grad_far,) = gate((grad_far,), (q3_done,))
        grad_far = trade(grad_far, "seq", 2)
        qkv, qkv_done = add((qkv,), (trade(give_qkv, "dp", 2),), late=(mixed_far,))
        got_qkv = trade(qkv, "dp", far_bits[0])
        rest, rest_done = add((rest,), (got_rest,), late=(qkv_done,))
        for bit in far_bits[1:]:
            rest, rest_done = add((rest,), (trade(rest, "dp", bit),))

        beside, other = trade(rest, "dp", 2), trade(rest, "dp", 1)
        mixed, grad, fill_done = fill(at, mixed, mixed_far, grad, grad_far)
        qkv, qkv_done = add((qkv,), (got_qkv,), late=(rest_done, fill_done))
        for bit in far_bits[1:]:
            qkv, qkv_done = add((qkv,), (trade(qkv, "dp", bit),))
        square, _ = squares(at, qkv, w_qkv, rest, w_in, gains)
        qkv_beside, qkv_other = trade(qkv, "dp", 2), trade(qkv, "dp", 1)
        rest_parts = (rest, beside, other, trade(beside, "dp", 1))
        qkv_parts = (qkv, qkv_beside, qkv_other, trade(qkv_beside, "dp", 1))
        for axis, bit, late in (
            ("seq", 2, (beside, other)),
            ("seq", 1, (qkv_beside, qkv_other)),
            ("dp", 2, (rest_parts[3],)),
            ("dp", 1, ()),
        ):
            square, _ = add((square,), (trade(square, axis, bit),), late=late)

        (new_in, first_in, second_in, new_out, first_out, second_out,
         new_down, first_down, second_down, row, _) = update_rest(
            at, square, rest_parts,
            (w_in, m_in, v_in), (w_out, m_out, v_out), (w_down, m_down, v_down),
        )
        (new_qkv, first_qkv, second_qkv, new_gains, first_gains, second_gains, norm, _) = (
            update_last(
                at, square, (w_qkv, m_qkv, v_qkv), qkv_parts, row, (gains, m_gains, v_gains)
            )
        )
        return (
            mixed,
            grad,
            norm[0, 0],
            new_qkv, new_out, new_in, new_down, new_gains,
            first_qkv, first_out, first_in, first_down, first_gains,
            second_qkv, second_out, second_in, second_down, second_gains,
        )

    return on_device


def solution(mesh):
    rows, matrix, gain = P("dp", "seq", None), P("seq", None), P(None, "seq")
    weights = (matrix,) * 4 + (gain,)
    return jax.shard_map(
        make(mesh.shape["dp"], mesh.shape["seq"]),
        mesh=mesh,
        in_specs=(rows, rows, P("dp", None), P("dp")) + weights * 3,
        out_specs=(rows, rows, P()) + weights * 3,
        check_vma=False,
    )
```

```python
import functools
import math

import jax
import jax.numpy as jnp
from jax import lax
from jax.experimental import pallas as pl
from jax.experimental.pallas import tpu as pltpu
from jax.sharding import PartitionSpec as P

HEADS = 12
HEAD_DIM = 64
PAIR = 2 * HEAD_DIM
STEP_COUNT = 10
EPS_NORM = 1e-05
ROPE_BASE = 160000.0
NEG_FILL = -1e30
CLIP_LIMIT = 10.0
BETA_FIRST = 0.9
BETA_SECOND = 0.98
EPS_ADAM = 1e-06
STEP_RATES = (0.1, 0.5, 0.1, 0.1, 1.0)
DECAY_RATES = (0.01, 0.01, 0.01, 0.01, 0.0)
DOCS = 5
LOW = jnp.bfloat16
FULL = jnp.float32
SCALE = 1.0 / math.sqrt(HEAD_DIM)
WEIGHT = 20_000_000_000


def doc_positions(segment_ids):
    seq_len = segment_ids.shape[-1]
    places = jnp.arange(seq_len, dtype=jnp.int32)
    first_mark = jnp.ones((1,), jnp.bool_)
    change = jnp.concatenate([first_mark, segment_ids[1:] != segment_ids[:-1]])
    starts = lax.cummax(jnp.where(change, places, 0), axis=0)
    return places - starts


def rope_tables(positions):
    half_dim = HEAD_DIM // 2
    exponents = jnp.arange(half_dim, dtype=jnp.float32) * (2.0 / HEAD_DIM)
    inv_freq = ROPE_BASE ** (-exponents)
    angles = positions.astype(jnp.float32)[:, None] * inv_freq
    cos_part, sin_part = jnp.cos(angles), jnp.sin(angles)
    return (
        jnp.concatenate([cos_part] * 4, axis=1),
        jnp.concatenate([-sin_part, sin_part] * 2, axis=1),
    )


def adam_step(weight, first_old, second_old, gradient, factor, step_rate, decay_rate):
    clipped = gradient * factor
    first_new = BETA_FIRST * first_old + (1.0 - BETA_FIRST) * clipped
    second_new = BETA_SECOND * second_old + (1.0 - BETA_SECOND) * clipped * clipped
    root = second_new * lax.rsqrt(second_new) * (1.0 - BETA_SECOND**STEP_COUNT) ** -0.5
    step = first_new * (step_rate / (1.0 - BETA_FIRST**STEP_COUNT)) / (root + EPS_ADAM)
    return (weight * (1.0 - step_rate * decay_rate) - step, first_new, second_new)


def mul(left, right):
    return lax.dot_general(left, right, (((1,), (0,)), ((), ())), preferred_element_type=FULL)


def mul_t(left, right):
    return lax.dot_general(left, right, (((1,), (1,)), ((), ())), preferred_element_type=FULL)


def normalize(values):
    centered = values - jnp.mean(values, axis=-1, keepdims=True)
    root = lax.rsqrt(jnp.mean(centered * centered, axis=-1, keepdims=True) + EPS_NORM)
    return centered * root, root


def normalize_back(grad, gain, scaled, root):
    t = grad * gain
    back = root * (
        t
        - jnp.mean(t, axis=-1, keepdims=True)
        - scaled * jnp.mean(t * scaled, axis=-1, keepdims=True)
    )
    return back


def turn(values, cos_part, sin_part):
    lane = lax.broadcasted_iota(jnp.int32, values.shape, 1)
    swapped = jnp.where(
        lane % HEAD_DIM < HEAD_DIM // 2,
        pltpu.roll(values, PAIR - HEAD_DIM // 2, 1),
        pltpu.roll(values, HEAD_DIM // 2, 1),
    )
    return values * cos_part + swapped * sin_part


def three_parts(values):
    high = values.astype(LOW).astype(FULL)
    rest = values - high
    mid = rest.astype(LOW).astype(FULL)
    return high, mid, rest - mid


def wait_all(copies):
    for copy in copies:
        copy.wait()


def put(source, target, sem):
    copy = pltpu.make_async_copy(source, target, sem)
    copy.start()
    return copy


PIECES = ((0, None), (1, None), (2, 0), (2, 1), (3, 0), (3, 1))


def load_blocks(at_ref, blocks, whole, sem):
    rows = blocks[0].shape[0]
    copies = []
    for i, (bits, part) in enumerate(PIECES):
        start = (at_ref[0] ^ bits) * rows
        size = rows
        if part is not None:
            size = rows // 2
            start += (at_ref[1] ^ part) * size
        target = whole.at[pl.ds(pl.multiple_of(start, size), size), :]
        copies.append(put(blocks[i], target, sem.at[i]))
    return copies


def load_folded(at_ref, blocks, w_out, w_down, sem):
    rows, width = blocks[0].shape[0], w_out.shape[1]
    short, last = rows // 2, width // 2
    copies = []

    def copy(source, target):
        copies.append(put(source, target, sem.at[len(copies)]))

    for i, (bits, part) in enumerate(PIECES):
        owner = at_ref[0] ^ bits
        base = owner * (rows + short)
        first = 0 if part is None else (at_ref[1] ^ part) * short
        size = rows if part is None else short
        for lanes, whole, start in ((0, w_out, owner * rows), (width, w_down, base)):
            span = pl.ds(pl.multiple_of(start + first, short), size)
            copy(blocks[i].at[:, pl.ds(lanes, width)], whole.at[span, :])
        span = pl.ds(pl.multiple_of(base + rows, short), short)
        if part is None:
            for fold in range(2):
                copy(
                    blocks[i].at[pl.ds(fold * short, short), pl.ds(2 * width, last)],
                    w_down.at[span, pl.ds(fold * last, last)],
                )
        else:
            lanes = pl.ds(pl.multiple_of((at_ref[1] ^ part) * last, last), last)
            copy(blocks[i].at[:, pl.ds(2 * width, last)], w_down.at[span, lanes])
    return copies


def fold(out, w_out, w_down, first):
    rows, width = w_out.shape
    short, last = rows // 2, width // 2
    out[:, first : first + width] = w_out[...].astype(LOW)
    out[:, first + width : first + 2 * width] = w_down[:rows, :].astype(LOW)
    for i in range(2):
        out[i * short : (i + 1) * short, first + 2 * width :] = w_down[
            rows:, i * last : (i + 1) * last
        ].astype(LOW)


def prepare_first_kernel(at_ref, w_ref, gains_ref, half_ref, gains_out, wide, sem):
    short = half_ref.shape[0]
    span = pl.ds(pl.multiple_of(at_ref[1] * short, short), short)
    copy = put(w_ref.at[span, :], wide, sem.at[0])
    gains_out[...] = gains_ref[...].astype(LOW)
    copy.wait()
    half_ref[...] = wide[...].astype(LOW)


def prepare_rest_kernel(at_ref, tokens_ref, in_ref, out_ref, down_ref, qkv_ref, cot_ref,
                        their_tokens, low_in, half_in, low_od, half_od, low_qkv, their_cot,
                        in_wide, out_wide, down_wide, qkv_wide, sem):
    slot = 1 - at_ref[2]
    copies = [
        put(source, target, sem.at[i])
        for i, (source, target) in enumerate((
            (tokens_ref.at[slot], their_tokens), (in_ref, in_wide), (out_ref, out_wide),
            (down_ref, down_wide), (qkv_ref, qkv_wide), (cot_ref.at[slot], their_cot),
        ))
    ]
    short = half_in.shape[0]
    span = pl.ds(pl.multiple_of(at_ref[1] * short, short), short)
    copies[1].wait()
    low_in[...] = in_wide[...].astype(LOW)
    half_in[...] = in_wide[span, :].astype(LOW)
    copies[2].wait()
    copies[3].wait()
    fold(low_od, out_wide, down_wide, 0)
    half_od[...] = low_od[span, :]
    copies[4].wait()
    low_qkv[...] = qkv_wide[...].astype(LOW)
    copies[0].wait()
    copies[5].wait()


def project_kernel(at_ref, tokens_ref, far_ref, gain_ref, cos_ref, sin_ref, w0, w1, w2, w3, w4, w5,
                   normed_ref, query_ref, kv_ref, weight, sem):
    copies = load_blocks(at_ref, (w0, w1, w2, w3, w4, w5), weight, sem)
    rows, width = far_ref.shape
    for part in range(2):
        values = tokens_ref[at_ref[2]] if part == 0 else far_ref[...]
        scaled, _ = normalize(values.astype(FULL))
        normed_ref[pl.ds(part * rows, rows), :] = (scaled * gain_ref[...]).astype(LOW)
    wait_all(copies)
    for part in range(2):
        span = pl.ds(part * rows, rows)
        normed = normed_ref[span, :]
        cos_part, sin_part = cos_ref[span, :], sin_ref[span, :]
        for pair in range(2 * width // PAIR):
            lanes = pl.ds(pair * PAIR, PAIR)
            if pair % 2 == 0:
                both = mul(normed, weight[:, pl.ds(pair * PAIR, 2 * PAIR)])
            raw = both[:, (pair % 2) * PAIR : (pair % 2 + 1) * PAIR]
            turned = turn(raw, cos_part, sin_part)
            if pair < width // PAIR:
                query_ref[span, lanes] = (turned * SCALE).astype(LOW)
            else:
                kv_ref[0, span, pl.ds(pair * PAIR - width, PAIR)] = turned.astype(LOW)
        kv_ref[1, span, :] = mul(normed, weight[:, 2 * width :]).astype(LOW)


def head_lanes(head, shape):
    lane = lax.broadcasted_iota(jnp.int32, shape, 1)
    return (lane < HEAD_DIM) if head == 0 else (lane >= HEAD_DIM)


def pick(head, inside, outside):
    return jnp.where(head_lanes(head, inside.shape), inside, outside)


def attend_kernel(query_ref, near_ref, far_ref, mark_query_ref, mark_key_ref, o_ref, extra_ref):
    rows = query_ref.shape[0]
    query = query_ref[...]
    mark_query = mark_query_ref[...]
    parts = [
        (near_ref[0], jnp.transpose(near_ref[1]), mark_key_ref[:rows, :]),
        (far_ref[0], jnp.transpose(far_ref[1]), mark_key_ref[rows:, :]),
    ]
    outs, logs = [], []
    for head in range(2):
        query_head = pick(head, query, mark_query)
        scores = [mul_t(pick(head, key, mark), query_head) for key, _, mark in parts]
        top = jnp.maximum(
            jnp.max(scores[0], axis=0, keepdims=True), jnp.max(scores[1], axis=0, keepdims=True)
        )
        exps = [jnp.exp(score - top) for score in scores]
        total = jnp.sum(exps[0], axis=0, keepdims=True) + jnp.sum(exps[1], axis=0, keepdims=True)
        span = slice(head * HEAD_DIM, (head + 1) * HEAD_DIM)
        out = sum(mul(value_t[span], e.astype(LOW)) for (_, value_t, _), e in zip(parts, exps))
        outs.append(out / total)
        logs.append(top + jnp.log(total))
    o_ref[...] = jnp.transpose(jnp.concatenate(outs)).astype(LOW)
    line = lax.broadcasted_iota(jnp.int32, (PAIR, rows), 0)
    extra = jnp.zeros((PAIR, rows), FULL)
    for head in range(2):
        base = DOCS + (HEAD_DIM if head == 0 else 0)
        for i, piece in enumerate(three_parts(-logs[head])):
            extra = jnp.where(line == base + i, piece, extra)
    extra_ref[...] = jnp.transpose(extra).astype(LOW) + mark_query


def attend_back_kernel(query_ref, near_ref, far_ref, extra_ref, mark_key_ref, o_ref, do_ref,
                       cos_ref, sin_ref, dq_ref, keep_ref, send_ref):
    rows = query_ref.shape[0]
    query, extra, do = query_ref[...], extra_ref[...], do_ref[...]
    inner_all = do.astype(FULL) * o_ref[...].astype(FULL)
    lane = lax.broadcasted_iota(jnp.int32, (rows, PAIR), 1)
    zero = jnp.zeros((rows, PAIR), LOW)
    grads_query = []
    sums = [[None, None], [None, None]]
    keys_t = [jnp.transpose(near_ref[0]), jnp.transpose(far_ref[0])]
    for head in range(2):
        inside = head_lanes(head, (rows, PAIR))
        inner = jnp.sum(jnp.where(inside, inner_all, 0.0), axis=1, keepdims=True)
        base = DOCS + (HEAD_DIM if head == 0 else 0)
        tail = jnp.zeros((rows, PAIR), FULL)
        for i, piece in enumerate(three_parts(-inner)):
            tail = jnp.where(lane == base + i, piece, tail)
        query_head = pick(head, query, extra)
        do_head = pick(head, do, tail.astype(LOW))
        query_only = pick(head, query, zero)
        do_only = pick(head, do, zero)
        span = slice(head * HEAD_DIM, (head + 1) * HEAD_DIM)
        grad_query = 0.0
        for part, ref in enumerate((near_ref, far_ref)):
            mark = mark_key_ref[pl.ds(part * rows, rows), :]
            probs = jnp.exp(mul_t(pick(head, ref[0], mark), query_head))
            grad_probs = mul_t(pick(head, ref[1], mark), do_head)
            grad_scores = (probs * grad_probs).astype(LOW)
            grad_value = mul(probs.astype(LOW), do_only)
            grad_key = mul(grad_scores, query_only)
            grad_query += mul(keys_t[part][span], grad_scores)
            if head == 0:
                sums[part] = [grad_key, grad_value]
            else:
                sums[part] = [sums[part][0] + grad_key, sums[part][1] + grad_value]
        grads_query.append(grad_query)
    turned = turn(
        jnp.transpose(jnp.concatenate(grads_query)) * SCALE, cos_ref[...], -sin_ref[...]
    )
    dq_ref[...] = turned.astype(LOW)
    for i in range(2):
        keep_ref[i] = sums[0][i].astype(LOW)
        send_ref[i] = sums[1][i].astype(LOW)


def middle_kernel(at_ref, live_ref, tokens_ref, far_ref, cot_ref, cot_far_ref, oa_ref, ob_ref,
                  gain_ref, i0, i1, i2, i3, i4, i5, d0, d1, d2, d3, d4, d5,
                  mixed_ref, mixed_far_ref, dx1_ref, do_ref, keep_ref, send_ref,
                  w_out, w_in, w_down, o_all, o_t, a2_t, h_t, dm_all, duw_all, db_all,
                  mixed, dx1_all, do_all, keep, send, sem, fold_sem, out_sem):
    place, slot = at_ref[0], at_ref[2]
    live = live_ref[slot].astype(FULL)
    copies_down = load_folded(at_ref, (d0, d1, d2, d3, d4, d5), w_out, w_down, fold_sem)
    copies_in = load_blocks(at_ref, (i0, i1, i2, i3, i4, i5), w_in, sem)
    rows, width = far_ref.shape
    share = width // 4
    short, units = share // 2, w_down.shape[0]
    gain = gain_ref[...]
    o_all[:, : oa_ref.shape[1]] = oa_ref[...]
    o_all[:, oa_ref.shape[1] :] = ob_ref[...]
    copies = []
    for part in range(2):
        span = pl.ds(part * rows, rows)
        o = o_all[span, :]
        values = tokens_ref[slot] if part == 0 else far_ref[...]
        if part == 0:
            wait_all(copies_down)
        x1 = values.astype(FULL) + live * mul(o, w_out[...])
        scaled, root = normalize(x1)
        a2 = (scaled * gain).astype(LOW)
        if part == 0:
            wait_all(copies_in)
        u = mul(a2, w_in[:, :units])
        w = mul(a2, w_in[:, units:])
        phi = 0.5 * (1.0 + lax.erf(u * math.sqrt(0.5)))
        gelu = u * phi
        h = (gelu * w).astype(LOW)
        mixed[span, :] = (x1 + live * mul(h, w_down[...])).astype(LOW)
        target = mixed_ref.at[slot] if part == 0 else mixed_far_ref
        copies.append(put(mixed.at[span, :], target, out_sem.at[len(copies)]))
        cot = (cot_ref[slot] if part == 0 else cot_far_ref[...]).astype(FULL)
        dm = (live * cot).astype(LOW)
        dh = mul_t(dm, w_down[...])
        slope = phi + u * (jnp.exp(-0.5 * u * u) * (1.0 / math.sqrt(2.0 * math.pi)))
        duw_all[span, :units] = (dh * w * slope).astype(LOW)
        duw_all[span, units:] = (dh * gelu).astype(LOW)
        da2 = mul_t(duw_all[span, :], w_in[...])
        dx1 = cot + normalize_back(da2, gain, scaled, root)
        dx1_all[span, :] = dx1
        copies.append(put(dx1_all.at[span, :], dx1_ref.at[span, :], out_sem.at[len(copies)]))
        db = (live * dx1).astype(LOW)
        do_all[span, :] = mul_t(db, w_out[...]).astype(LOW)
        copies.append(put(do_all.at[span, :], do_ref.at[span, :], out_sem.at[len(copies)]))
        db_all[span, :] = db
        dm_all[span, :] = dm
        o_t[:, span] = jnp.transpose(o)
        a2_t[:, span] = jnp.transpose(a2)
        h_t[:, span] = jnp.transpose(h)
    dm, duw, db = dm_all[...], duw_all[...], db_all[...]
    for j, out, target in ((1, send, send_ref), (3, send, send_ref), (0, keep, keep_ref), (2, keep, keep_ref)):
        span = pl.ds(pl.multiple_of((place ^ j) * share, share), share)
        base = (place ^ j) * (share + short)
        down = pl.ds(pl.multiple_of(base, short), share)
        down_last = pl.ds(pl.multiple_of(base + share, short), short)
        at = 2 * units
        out[j // 2, :, :at] = mul(a2_t[span, :], duw).astype(LOW)
        out[j // 2, :, at : at + width] = mul(o_t[span, :], db).astype(LOW)
        at += width
        out[j // 2, :, at : at + width] = mul(h_t[down, :], dm).astype(LOW)
        at += width
        last = mul(h_t[down_last, :], dm).astype(LOW)
        out[j // 2, :short, at:] = last[:, : width // 2]
        out[j // 2, short:, at:] = last[:, width // 2 :]
        copies.append(put(out.at[j // 2], target.at[j // 2], out_sem.at[len(copies)]))
    wait_all(copies)


def send_kernel(count, at_ref, *refs):
    normed_ref = refs[0]
    dqs, owns, gots = (refs[1 + i * count : 1 + (i + 1) * count] for i in range(3))
    (cos_ref, sin_ref, dqkv_ref, normed_t_ref, send_ref,
     dqkv, normed_t, send, sem) = refs[1 + 3 * count :]
    width = normed_ref.shape[1]
    part_width = width // count
    normed_t[...] = jnp.transpose(normed_ref[...])
    copies = [put(normed_t, normed_t_ref, sem.at[0])]
    cos_part, sin_part = cos_ref[...], -sin_ref[...]
    for part, (dq, own, got) in enumerate(zip(dqs, owns, gots)):
        base = part * part_width
        dqkv[:, pl.ds(base, part_width)] = dq[...]
        dqkv[:, pl.ds(2 * width + base, part_width)] = (
            own[1].astype(FULL) + got[1].astype(FULL)
        ).astype(LOW)
        for pair in range(part_width // PAIR):
            lanes = pl.ds(pair * PAIR, PAIR)
            raw = own[0, :, lanes].astype(FULL) + got[0, :, lanes].astype(FULL)
            dqkv[:, pl.ds(width + base + pair * PAIR, PAIR)] = turn(raw, cos_part, sin_part).astype(
                LOW
            )
    copies.append(put(dqkv, dqkv_ref, sem.at[1]))
    right = dqkv[...]
    share = send.shape[1]
    for j in (1, 3):
        start = pl.multiple_of((at_ref[0] ^ j) * share, share)
        send[j // 2] = mul(normed_t[pl.ds(start, share), :], right).astype(LOW)
        copies.append(put(send.at[j // 2], send_ref.at[j // 2], sem.at[len(copies)]))
    wait_all(copies)


def keep_kernel(at_ref, normed_t_ref, dqkv_ref, keep_ref, keep, sem):
    right = dqkv_ref[...]
    share = keep.shape[1]
    copies = []
    for j in (0, 2):
        start = pl.multiple_of((at_ref[0] ^ j) * share, share)
        keep[j // 2] = mul(normed_t_ref[pl.ds(start, share), :], right).astype(LOW)
        copies.append(put(keep.at[j // 2], keep_ref.at[j // 2], sem.at[len(copies)]))
    wait_all(copies)


def input_kernel(at_ref, tokens_ref, far_ref, gain_ref, dx1_ref, dqkv_ref, w0, w1, w2, w3, w4, w5,
                 grad_ref, grad_far_ref, weight, grad_own, sem, out_sem):
    wait_all(load_blocks(at_ref, (w0, w1, w2, w3, w4, w5), weight, sem))
    rows = far_ref.shape[0]
    gain = gain_ref[...]
    for part in (1, 0):
        span = pl.ds(part * rows, rows)
        values = tokens_ref[at_ref[2]] if part == 0 else far_ref[...]
        scaled, root = normalize(values.astype(FULL))
        back = normalize_back(mul_t(dqkv_ref[span, :], weight[...]), gain, scaled, root)
        grad = dx1_ref[span, :] + back
        if part == 1:
            grad_far_ref[...] = grad.astype(LOW)
        else:
            grad_own[...] = grad
    put(grad_own, grad_ref.at[at_ref[2]], out_sem.at[0]).wait()


def shaped(*shape, kind=LOW):
    return jax.ShapeDtypeStruct(shape, kind)


IN_SMEM = pl.BlockSpec(memory_space=pltpu.SMEM)
IN_VMEM = pl.BlockSpec(memory_space=pltpu.VMEM)
IN_ANY = pl.BlockSpec(memory_space=pl.ANY)


def params(mebibytes):
    return pltpu.CompilerParams(vmem_limit_bytes=int(mebibytes * 1024 * 1024))


def call(kernel, args, in_specs, out_shape, out_specs, late=(), **options):
    if not isinstance(out_shape, tuple):
        out_shape, out_specs = (out_shape,), (out_specs,)
    count, skip, outs = len(args), len(late), len(out_shape)

    def body(*refs):
        outs_at = count + skip
        return kernel(*refs[:count], *refs[outs_at : outs_at + outs], *refs[outs_at + outs + 1 :])

    return pl.pallas_call(
        body,
        in_specs=list(in_specs) + [IN_ANY] * skip,
        out_shape=out_shape + (shaped(8, 128, kind=FULL),),
        out_specs=out_specs + (IN_ANY,),
        **options,
    )(*args, *late)


def gate(values, late=(), weight=0):
    hint = {}
    if weight:
        hint["cost_estimate"] = pl.CostEstimate(
            flops=weight, transcendentals=0, bytes_accessed=0
        )
    return call(
        lambda *refs: None,
        values,
        late=late,
        out_shape=tuple(jax.ShapeDtypeStruct(v.shape, v.dtype) for v in values),
        in_specs=[IN_ANY] * len(values),
        out_specs=(IN_ANY,) * len(values),
        input_output_aliases={i: i for i in range(len(values))},
        compiler_params=params(1),
        name="gate",
        **hint,
    )[: len(values)]


def in_hbm(value):
    return pltpu.with_memory_space_constraint(value, pltpu.HBM)


def prepare_first(at, weight, gains):
    rows, width = weight.shape
    return call(
        prepare_first_kernel,
        (at, in_hbm(weight), gains),
        out_shape=(shaped(rows // 2, width), shaped(*gains.shape)),
        in_specs=[IN_SMEM, IN_ANY, IN_VMEM],
        out_specs=(IN_VMEM,) * 2,
        scratch_shapes=[pltpu.VMEM((rows // 2, width), FULL), pltpu.SemaphoreType.DMA((1,))],
        compiler_params=params(6),
        name="prepare_first",
    )


def prepare_rest(at, tokens, w_in, w_out, w_down, w_qkv, cotangent, late):
    rows, width = w_out.shape
    folded = 2 * width + width // 2
    return call(
        prepare_rest_kernel,
        (at, *[in_hbm(v) for v in (tokens, w_in, w_out, w_down, w_qkv, cotangent)]),
        late=late,
        out_shape=(
            shaped(*tokens.shape[1:]),
            shaped(*w_in.shape),
            shaped(rows // 2, w_in.shape[1]),
            shaped(rows, folded),
            shaped(rows // 2, folded),
            shaped(*w_qkv.shape),
            shaped(*cotangent.shape[1:]),
        ),
        in_specs=[IN_SMEM] + [IN_ANY] * 6,
        out_specs=(IN_VMEM,) * 7,
        scratch_shapes=[
            pltpu.VMEM(v.shape, FULL) for v in (w_in, w_out, w_down, w_qkv)
        ] + [pltpu.SemaphoreType.DMA((6,))],
        compiler_params=params(18),
        name="prepare_rest",
    )


def project(at, tokens, far, gain, cos_part, sin_part, blocks, late):
    rows, width = 2 * far.shape[0], far.shape[1]
    return call(
        project_kernel,
        (at, tokens, far, gain, cos_part, sin_part, *blocks),
        late=late,
        out_shape=(shaped(rows, width), shaped(rows, width), shaped(2, rows, width)),
        in_specs=[IN_SMEM] + [IN_VMEM] * 5 + [IN_ANY] * 6,
        out_specs=(IN_VMEM,) * 3,
        scratch_shapes=[pltpu.VMEM((width, 3 * width), LOW), pltpu.SemaphoreType.DMA((6,))],
        compiler_params=params(16),
        name="project",
    )


def attend(first, count, query, near, far, mark_query, mark_key, late=()):
    rows = query.shape[0]
    row_spec = pl.BlockSpec((rows, PAIR), lambda i: (0, i + first))
    kv_spec = pl.BlockSpec((2, rows, PAIR), lambda i: (0, 0, i + first))
    out_spec = pl.BlockSpec((rows, PAIR), lambda i: (0, i))
    return call(
        attend_kernel,
        (query, near, far, mark_query, mark_key),
        late=late,
        grid=(count,),
        out_shape=(shaped(rows, count * PAIR), shaped(rows, count * PAIR)),
        in_specs=[
            row_spec,
            kv_spec,
            kv_spec,
            pl.BlockSpec((rows, PAIR), lambda i: (0, 0)),
            pl.BlockSpec((2 * rows, PAIR), lambda i: (0, 0)),
        ],
        out_specs=(out_spec, out_spec),
        compiler_params=params(16),
        name="attend",
    )


def attend_back(
    first, first_o, count, query, near, far, extra, o, mark_key, do, cos_part, sin_part, late=()
):
    rows = query.shape[0]
    row_spec = pl.BlockSpec((rows, PAIR), lambda i: (0, i + first))
    o_spec = pl.BlockSpec((rows, PAIR), lambda i: (0, i + first_o))
    kv_spec = pl.BlockSpec((2, rows, PAIR), lambda i: (0, 0, i + first))
    fixed = pl.BlockSpec((rows, PAIR), lambda i: (0, 0))
    out_row = pl.BlockSpec((rows, PAIR), lambda i: (0, i))
    out_kv = pl.BlockSpec((2, rows, PAIR), lambda i: (0, 0, i))
    return call(
        attend_back_kernel,
        (query, near, far, extra, mark_key, o, do, cos_part, sin_part),
        late=late,
        grid=(count,),
        out_shape=(
            shaped(rows, count * PAIR),
            shaped(2, rows, count * PAIR),
            shaped(2, rows, count * PAIR),
        ),
        in_specs=[
            row_spec,
            kv_spec,
            kv_spec,
            o_spec,
            pl.BlockSpec((2 * rows, PAIR), lambda i: (0, 0)),
            o_spec,
            row_spec,
            fixed,
            fixed,
        ],
        out_specs=(out_row, out_kv, out_kv),
        compiler_params=params(20),
        name="attend_back",
    )


def middle(at, live, tokens, far, cot, cot_far, o_a, o_b, gain, blocks_in, blocks_od):
    half, width = far.shape
    rows, share = 2 * half, width // 4
    units = blocks_in[0].shape[1] // 2
    total = 2 * units + blocks_od[0].shape[1]
    assert units == 4 * (share + share // 2)
    low = lambda *shape: pltpu.VMEM(shape, LOW)
    return call(
        middle_kernel,
        (at, live, tokens, far, cot, cot_far, o_a, o_b, gain, *blocks_in, *blocks_od),
        out_shape=(
            shaped(2, half, width),
            shaped(half, width),
            shaped(rows, width, kind=FULL),
            shaped(rows, width),
            shaped(2, share, total),
            shaped(2, share, total),
        ),
        in_specs=[IN_SMEM] * 2 + [IN_VMEM] * 7 + [IN_ANY] * 12,
        out_specs=(IN_ANY,) * 6,
        scratch_shapes=[
            low(width, width),
            low(width, 2 * units),
            low(units, width),
            low(rows, width),
            low(width, rows),
            low(width, rows),
            low(units, rows),
            low(rows, width),
            low(rows, 2 * units),
            low(rows, width),
            low(rows, width),
            pltpu.VMEM((rows, width), FULL),
            low(rows, width),
            low(2, share, total),
            low(2, share, total),
            pltpu.SemaphoreType.DMA((6,)),
            pltpu.SemaphoreType.DMA((20,)),
            pltpu.SemaphoreType.DMA((10,)),
        ],
        compiler_params=params(40),
        name="middle",
    )


def qkv_send(at, normed, dq, own, got, cos_part, sin_part, late):
    rows, width = normed.shape
    share = width // 4
    return call(
        functools.partial(send_kernel, len(dq)),
        (at, normed, *dq, *own, *got, cos_part, sin_part),
        late=late,
        out_shape=(
            shaped(rows, 3 * width),
            shaped(width, rows),
            shaped(2, share, 3 * width),
        ),
        in_specs=[IN_SMEM] + [IN_VMEM] * (3 + 3 * len(dq)),
        out_specs=(IN_ANY,) * 3,
        scratch_shapes=[
            pltpu.VMEM((rows, 3 * width), LOW),
            pltpu.VMEM((width, rows), LOW),
            pltpu.VMEM((2, share, 3 * width), LOW),
            pltpu.SemaphoreType.DMA((4,)),
        ],
        compiler_params=params(20),
        name="qkv_send",
    )


def qkv_keep(at, normed_t, dqkv, late):
    width, rows = normed_t.shape
    share = width // 4
    return call(
        keep_kernel,
        (at, normed_t, dqkv),
        late=late,
        out_shape=shaped(2, share, 3 * width),
        in_specs=[IN_SMEM] + [IN_VMEM] * 2,
        out_specs=IN_ANY,
        scratch_shapes=[
            pltpu.VMEM((2, share, 3 * width), LOW),
            pltpu.SemaphoreType.DMA((2,)),
        ],
        compiler_params=params(16),
        name="qkv_keep",
    )


def input_back(at, tokens, far, gain, dx1, dqkv, blocks, late):
    half, width = far.shape
    return call(
        input_kernel,
        (at, tokens, far, gain, dx1, dqkv, *blocks),
        late=late,
        out_shape=(shaped(2, half, width, kind=FULL), shaped(half, width)),
        in_specs=[IN_SMEM] + [IN_VMEM] * 5 + [IN_ANY] * 6,
        out_specs=(IN_ANY, IN_VMEM),
        scratch_shapes=[
            pltpu.VMEM((width, 3 * width), LOW),
            pltpu.VMEM((half, width), FULL),
            pltpu.SemaphoreType.DMA((6,)),
            pltpu.SemaphoreType.DMA((1,)),
        ],
        compiler_params=params(20),
        name="input_back",
    )


def first_sums_kernel(at_ref, keep, got, own_a, far_a, mine_b, give_b):
    cut, short = far_a.shape[0], give_b.shape[1]

    def add(block, start, size):
        span = pl.ds(start, size)
        return (keep[block, span, :].astype(FULL) + got[block, span, :].astype(FULL)).astype(LOW)

    far_a[...] = add(1, 0, cut)
    for block in range(2):
        give_b[block] = add(block, pl.multiple_of(cut + (1 - at_ref[1]) * short, short), short)
        mine_b[block] = add(block, pl.multiple_of(cut + at_ref[1] * short, short), short)
    own_a[...] = add(0, 0, cut)


def first_sums(at, keep, got, late=()):
    _, rows, width = keep.shape
    cut, short = rows // 2, rows // 4
    return call(
        first_sums_kernel,
        (at, keep, got),
        late=late,
        out_shape=(shaped(cut, width),) * 2 + (shaped(2, short, width),) * 2,
        in_specs=[IN_SMEM] + [IN_VMEM] * 2,
        out_specs=(IN_VMEM,) * 4,
        compiler_params=params(20),
        name="first_sums",
    )


def second_sums_kernel(at_ref, own_a, got_a, mine_b, got_b, mine_a, give_a, near_b, far_b):
    short = mine_a.shape[0]
    for start, out in ((1 - at_ref[1], give_a), (at_ref[1], mine_a)):
        span = pl.ds(pl.multiple_of(start * short, short), short)
        out[...] = (own_a[span, :].astype(FULL) + got_a[span, :].astype(FULL)).astype(LOW)
    for block, out in ((1, far_b), (0, near_b)):
        out[...] = (mine_b[block].astype(FULL) + got_b[block].astype(FULL)).astype(LOW)


def second_sums(at, own_a, got_a, mine_b, got_b, late=()):
    _, short, width = mine_b.shape
    return call(
        second_sums_kernel,
        (at, own_a, got_a, mine_b, got_b),
        late=late,
        out_shape=(shaped(short, width),) * 4,
        in_specs=[IN_SMEM] + [IN_VMEM] * 4,
        out_specs=(IN_VMEM,) * 4,
        compiler_params=params(12),
        name="second_sums",
    )


def third_sums_kernel(at_ref, mine_a, got_a, near_b, got_b, keep, give):
    upper = mine_a[...].astype(FULL) + got_a[...].astype(FULL)
    lower = near_b[...].astype(FULL) + got_b[...].astype(FULL)
    keep[...] = jnp.where(at_ref[4] == 0, upper, lower).astype(LOW)
    give[...] = jnp.where(at_ref[4] == 0, lower, upper).astype(LOW)


def third_sums(at, mine_a, got_a, near_b, got_b, late=()):
    return call(
        third_sums_kernel,
        (at, mine_a, got_a, near_b, got_b),
        late=late,
        out_shape=(shaped(*mine_a.shape),) * 2,
        in_specs=[IN_SMEM] + [IN_VMEM] * 4,
        out_specs=(IN_VMEM,) * 2,
        compiler_params=params(12),
        name="third_sums",
    )


def squares_kernel(at_ref, qkv, w_qkv, rest, w_in, gains, out):
    inner = w_in.shape[1]
    total = jnp.sum(jnp.square(rest[:, inner:].astype(FULL)), keepdims=True)
    rows = qkv.shape[0]
    shape = (rows, gains.shape[1])
    offset = lax.broadcasted_iota(jnp.int32, shape, 1) - lax.broadcasted_iota(jnp.int32, shape, 0)
    for i, (piece, weight) in enumerate(((qkv, w_qkv), (rest, w_in))):
        start = at_ref[3]
        span = pl.ds(pl.multiple_of(start, 8), rows)
        values = piece[:, : weight.shape[1]].astype(FULL)
        sums = jnp.sum(weight[span, :].astype(LOW).astype(FULL) * values, axis=1, keepdims=True)
        gain = gains[i : i + 1, :].astype(LOW).astype(FULL)
        gain = jnp.sum(jnp.where(offset == start, gain, 0.0), axis=1, keepdims=True)
        total += jnp.sum(jnp.square(values), keepdims=True)
        total += jnp.sum(jnp.square(sums / gain), keepdims=True)
    out[...] = jnp.broadcast_to(total, out.shape)


def squares(*args):
    return call(
        squares_kernel,
        args,
        out_shape=shaped(8, 128, kind=FULL),
        in_specs=[IN_SMEM] + [IN_VMEM] * (len(args) - 1),
        out_specs=IN_VMEM,
        compiler_params=params(10),
        name="squares",
    )


def add_kernel(count, *refs):
    for i in range(count):
        out = refs[2 * count + i]
        out[...] = (refs[i][...].astype(FULL) + refs[count + i][...].astype(FULL)).astype(out.dtype)


def add(first, second, late=()):
    count = len(first)
    return call(
        functools.partial(add_kernel, count),
        (*first, *second),
        late=late,
        out_shape=tuple(jax.ShapeDtypeStruct(v.shape, v.dtype) for v in first),
        in_specs=[IN_VMEM] * (2 * count),
        out_specs=(IN_VMEM,) * count,
        compiler_params=params(8),
        name="add",
    )


def fill_kernel(at_ref, mixed_far, grad_far, mixed_in, grad_in, mixed, grad, wide, sem):
    first = put(mixed_far, mixed.at[1 - at_ref[2]], sem.at[0])
    wide[...] = grad_far[...].astype(FULL)
    put(wide, grad.at[1 - at_ref[2]], sem.at[1]).wait()
    first.wait()


def fill(at, mixed, mixed_far, grad, grad_far):
    return call(
        fill_kernel,
        (at, mixed_far, grad_far, mixed, grad),
        out_shape=(shaped(*mixed.shape), shaped(*grad.shape, kind=FULL)),
        in_specs=[IN_SMEM, IN_VMEM, IN_VMEM, IN_ANY, IN_ANY],
        out_specs=(IN_ANY,) * 2,
        input_output_aliases={3: 0, 4: 1},
        scratch_shapes=[pltpu.VMEM(grad_far.shape, FULL), pltpu.SemaphoreType.DMA((2,))],
        compiler_params=params(4),
        name="fill",
    )


def clip_factor(square_ref):
    norm = jnp.sqrt(square_ref[:1, :1])
    return jnp.minimum(1.0, CLIP_LIMIT / (norm + 1e-06))


def quarters(at_ref, parts):
    own, beside, other, other_beside = parts
    for i in range(4):
        same = at_ref[4] == i // 2
        near = jnp.where(same, own[...], beside[...])
        far = jnp.where(same, other[...], other_beside[...])
        yield jnp.where(at_ref[1] == i % 2, near, far).astype(FULL)


def gain_row(weight, gradient, start, shape):
    sums = jnp.sum(weight.astype(LOW).astype(FULL) * gradient, axis=1, keepdims=True)
    shape = (weight.shape[0], shape[1])
    offset = lax.broadcasted_iota(jnp.int32, shape, 1) - lax.broadcasted_iota(jnp.int32, shape, 0)
    return jnp.sum(jnp.where(offset == start, sums, 0.0), axis=0, keepdims=True)


class Update:
    def __init__(self, number, sources, news, targets, sem):
        self.number, self.sources, self.news, self.targets = number, sources, news, targets
        self.sem, self.out = sem, []

    def step(self, span, gradient, factor):
        weight = self.sources[0][span]
        results = adam_step(
            weight, self.sources[1][span], self.sources[2][span], gradient, factor,
            STEP_RATES[self.number], DECAY_RATES[self.number],
        )
        for result, new, target in zip(results, self.news, self.targets):
            new[span] = result
            self.out.append(put(new.at[span], target.at[span], self.sem.at[len(self.out)]))
        return weight


def update_rest_kernel(at_ref, square_ref, *refs):
    parts, refs = refs[:4], refs[4:]
    sources, targets, row_ref, news, sem = refs[:9], refs[9:18], refs[18], refs[19:28], refs[28]
    inner, out, down = (
        Update(number, *(group[3 * k : 3 * k + 3] for group in (sources, news, targets)), sem.at[k])
        for k, number in enumerate((2, 1, 3))
    )
    factor = clip_factor(square_ref)
    rows, width = sources[3].shape
    lanes = sources[0].shape[1]
    short, last = rows // 4, width // 2
    row = jnp.zeros(row_ref.shape, FULL)
    for i, gradient in enumerate(quarters(at_ref, parts)):
        span = (slice(i * short, (i + 1) * short), slice(None))
        part = gradient[:, :lanes]
        row += gain_row(inner.step(span, part, factor), part, i * short, row_ref.shape)
        out.step(span, gradient[:, lanes : lanes + width], factor)
        down.step(span, gradient[:, lanes + width : lanes + 2 * width], factor)
        start = rows + (i % 2) * short
        span = (slice(start, start + short), slice((i // 2) * last, (i // 2 + 1) * last))
        down.step(span, gradient[:, lanes + 2 * width :], factor)
    row_ref[...] = row
    wait_all(inner.out + out.out + down.out)


def update_rest(at, square, parts, inner, out, down, late):
    like = [jax.ShapeDtypeStruct(v.shape, FULL) for v in (*inner, *out, *down)]
    return call(
        update_rest_kernel,
        (at, square, *parts, *inner, *out, *down),
        late=late,
        out_shape=(*like, shaped(1, inner[0].shape[0], kind=FULL)),
        in_specs=[IN_SMEM] + [IN_VMEM] * 14,
        out_specs=(IN_ANY,) * 9 + (IN_VMEM,),
        scratch_shapes=[pltpu.VMEM(v.shape, FULL) for v in like]
        + [pltpu.SemaphoreType.DMA((3, 24))],
        compiler_params=params(28),
        name="update_rest",
    )


def update_last_kernel(at_ref, square_ref, row_ref, g_w, g_m, g_v, *refs):
    parts, refs = refs[:4], refs[4:]
    sources, targets = refs[:3], refs[3:6]
    g_w_out, g_m_out, g_v_out, norm_out = refs[6:10]
    news, sem = refs[10:13], refs[13]
    qkv = Update(0, sources, news, targets, sem)
    factor = clip_factor(square_ref)
    norm_out[...] = jnp.sqrt(square_ref[...])
    short = sources[0].shape[0] // 4
    row = jnp.zeros(row_ref.shape, FULL)
    for i, gradient in enumerate(quarters(at_ref, parts)):
        span = (slice(i * short, (i + 1) * short), slice(None))
        row += gain_row(qkv.step(span, gradient, factor), gradient, i * short, row_ref.shape)
    for i, values in enumerate((row, row_ref[...])):
        line = slice(i, i + 1)
        gradient = values / g_w[line, :].astype(LOW).astype(FULL)
        g_w_out[line, :], g_m_out[line, :], g_v_out[line, :] = adam_step(
            g_w[line, :], g_m[line, :], g_v[line, :], gradient, factor,
            STEP_RATES[4], DECAY_RATES[4],
        )
    wait_all(qkv.out)


def update_last(at, square, qkv, qkv_parts, row, gains):
    like = [jax.ShapeDtypeStruct(v.shape, FULL) for v in qkv]
    return call(
        update_last_kernel,
        (at, square, row, *gains, *qkv_parts, *qkv),
        out_shape=(
            *like,
            *[jax.ShapeDtypeStruct(v.shape, FULL) for v in gains],
            jax.ShapeDtypeStruct(square.shape, FULL),
        ),
        in_specs=[IN_SMEM] + [IN_VMEM] * 12,
        out_specs=(IN_ANY,) * 3 + (IN_VMEM,) * 4,
        scratch_shapes=[pltpu.VMEM(v.shape, FULL) for v in like]
        + [pltpu.SemaphoreType.DMA((12,))],
        compiler_params=params(18),
        name="update_last",
    )


def low_sum(*values):
    return sum(value.astype(FULL) for value in values).astype(LOW)


def index(value, i):
    return lax.dynamic_index_in_dim(value, i, 0, keepdims=False)


def make(dp_count, seq_count):
    assert seq_count == 4 and dp_count >= 8 and dp_count & (dp_count - 1) == 0
    far_bits = [1 << i for i in range(2, dp_count.bit_length() - 1)]

    def trade(value, axis, bit):
        size = seq_count if axis == "seq" else dp_count
        return lax.ppermute(value, axis, [(i, i ^ bit) for i in range(size)])

    def on_device(
        tokens, cotangent, segments, valid,
        w_qkv, w_out, w_in, w_down, gains,
        m_qkv, m_out, m_in, m_down, m_gains,
        v_qkv, v_out, v_in, v_down, v_gains,
    ):
        place = lax.axis_index("seq")
        group = lax.axis_index("dp")
        slot = place >> 1
        half = group & 1
        local_len, width = tokens.shape[1:]
        rows = 2 * local_len
        share = w_qkv.shape[0]
        side = (group >> 1) & 1
        quarter = share // 4
        at = jnp.stack([place, half, slot, side * 2 * quarter + half * quarter, side])

        half_qkv, low_gains, begun = prepare_first(at, w_qkv, gains)
        (far_qa,) = gate((trade(half_qkv, "seq", 2),), weight=10 * WEIGHT)
        (gain_far,) = gate((trade(low_gains, "seq", 2),), weight=20 * WEIGHT)
        their_tokens, low_in, half_in, low_od, half_od, low_qkv, their_cot, _ = prepare_rest(
            at, tokens, w_in, w_out, w_down, w_qkv, cotangent, (begun,)
        )
        near_q = trade(low_qkv, "seq", 1)
        far = trade(their_tokens, "seq", 2)
        far_qb = trade(far_qa, "dp", 1)
        near_qa = trade(far_qa, "seq", 1)
        near_qb = trade(far_qb, "seq", 1)
        (gain_far,) = gate((gain_far,), (far_qb,))
        gain_near = trade(jnp.stack([low_gains, gain_far]), "seq", 1)
        gain_stack = jnp.stack([low_gains, gain_near[0], gain_far, gain_near[1]])
        gain_low = jnp.concatenate(
            [index(gain_stack, b ^ place) for b in range(4)], axis=1
        ).astype(FULL)
        blocks_qkv = (low_qkv, near_q, far_qa, far_qb, near_qa, near_qb)
        low_in, low_od, half_in = gate((low_in, low_od, half_in), (far_qa,))
        near_i = trade(low_in, "seq", 1)
        near_o = trade(low_od, "seq", 1)
        (far_ia,) = gate((trade(half_in, "seq", 2),), weight=10 * WEIGHT)
        (half_od,) = gate((half_od,), (far,))

        seg = index(segments, slot)
        positions = doc_positions(seg).reshape(4, local_len)
        seg = seg.reshape(4, local_len)
        chunks = [place, place ^ 2, place ^ 1, place ^ 3]
        seg_keys = jnp.concatenate([index(seg, c) for c in chunks])
        pos = jnp.concatenate([index(positions, c) for c in chunks[:2]])
        cos_part, sin_part = rope_tables(pos)
        lane = jnp.arange(PAIR, dtype=jnp.int32)[None] % HEAD_DIM
        same = seg_keys[:, None] == lane
        mark_key = jnp.where(lane < DOCS, 1.0 - same, (lane < DOCS + 3) * 1.0).astype(LOW)
        mark_query = jnp.where((lane < DOCS) & same[:rows], NEG_FILL, 0.0).astype(LOW)

        normed, query, kv, _ = project(
            at, tokens, far, gain_low[:1], cos_part, sin_part, blocks_qkv,
            (far_ia, mark_key, mark_query),
        )
        kv_far = trade(kv, "seq", 1)
        far_oa = trade(half_od, "seq", 2)
        far_ib = trade(far_ia, "dp", 1)
        near_ia = trade(far_ia, "seq", 1)
        (cot_far,) = gate((trade(their_cot, "seq", 2),), weight=WEIGHT)
        pairs = width // PAIR
        early = 2
        args = (query, kv, kv_far, mark_query, mark_key)
        o_a, extra_a, done_a = attend(0, early, *args, late=(far_oa,))
        (far_ib,) = gate((far_ib,), (done_a,), weight=10 * WEIGHT)
        far_ob = trade(far_oa, "dp", 1)
        near_oa = trade(far_oa, "seq", 1)
        near_ib = trade(far_ib, "seq", 1)
        o_b, extra_b, done_b = attend(early, pairs - early, *args, late=(done_a, near_ia))
        (far_ob,) = gate((far_ob,), (done_b,))
        near_ob = trade(far_ob, "seq", 1)
        blocks_in = (low_in, near_i, far_ia, far_ib, near_ia, near_ib)
        blocks_od = (low_od, near_o, far_oa, far_ob, near_oa, near_ob)

        mixed, mixed_far, dx1, do, keep_rest, send_rest, _ = middle(
            at, valid, tokens, far, cotangent, cot_far, o_a, o_b, gain_low[1:], blocks_in, blocks_od
        )
        got_rest = trade(send_rest, "seq", 1)
        two = pairs // 3
        near_args = (query, kv, kv_far)
        back_args = (mark_key, do, cos_part, sin_part)
        dq0, own0, give0, back0 = attend_back(0, 0, two, *near_args, extra_a, o_a, *back_args)
        *r1, r1_done = first_sums(at, keep_rest, got_rest, late=(back0,))
        got_ra, got_rb = trade(r1[1], "seq", 2), trade(r1[3], "dp", 1)
        got0 = trade(give0, "seq", 1)
        dq1, own1, give1, back1 = attend_back(
            two, two - early, two, *near_args, extra_b, o_b, *back_args, late=(r1_done,)
        )
        got1 = trade(give1, "seq", 1)
        dq2, own2, give2, back2 = attend_back(
            2 * two, 2 * two - early, pairs - 2 * two, *near_args, extra_b, o_b, *back_args,
            late=(back1, got0),
        )
        got2 = trade(give2, "seq", 1)
        *r2, r2_done = second_sums(at, r1[0], got_ra, r1[2], got_rb, late=(back2,))
        got_ra, got_rb = gate(
            (trade(r2[1], "dp", 1), trade(r2[3], "seq", 2)), weight=WEIGHT
        )
        dqkv, normed_t, send_qkv, send_done = qkv_send(
            at, normed, (dq0, dq1, dq2), (own0, own1, own2), (got0, got1, got2),
            cos_part, sin_part, late=(r2_done,),
        )
        got_qkv = trade(send_qkv, "seq", 1)
        keep_qkv, _ = qkv_keep(at, normed_t, dqkv, late=(got_ra, got_rb))
        *q1, q1_done = first_sums(at, keep_qkv, got_qkv)
        got_qa, got_qb = trade(q1[1], "seq", 2), trade(q1[3], "dp", 1)
        rest, give_rest, r3_done = third_sums(
            at, r2[0], got_ra, r2[2], got_rb, late=(q1_done,)
        )
        got_rest = trade(give_rest, "dp", 2)
        grad, grad_far, grad_done = input_back(
            at, tokens, far, gain_low[:1], dx1, dqkv, blocks_qkv, late=(r3_done,)
        )
        *q2, q2_done = second_sums(at, q1[0], got_qa, q1[2], got_qb, late=(grad_done,))
        got_qa, got_qb = gate(
            (trade(q2[1], "dp", 1), trade(q2[3], "seq", 2)), weight=10 * WEIGHT
        )
        rest, rest_done = add((rest,), (got_rest,), late=(q2_done,))
        got_rest = trade(rest, "dp", far_bits[0])
        qkv, give_qkv, q3_done = third_sums(
            at, q2[0], got_qa, q2[2], got_qb, late=(rest_done,)
        )
        (mixed_far,) = gate((mixed_far,), (q2_done,))
        mixed_far = trade(mixed_far, "seq", 2)
        (grad_far,) = gate((grad_far,), (q3_done,))
        grad_far = trade(grad_far, "seq", 2)
        qkv, qkv_done = add((qkv,), (trade(give_qkv, "dp", 2),), late=(mixed_far,))
        got_qkv = trade(qkv, "dp", far_bits[0])
        rest, rest_done = add((rest,), (got_rest,), late=(qkv_done,))
        for bit in far_bits[1:]:
            rest, rest_done = add((rest,), (trade(rest, "dp", bit),))

        beside, other = trade(rest, "dp", 2), trade(rest, "dp", 1)
        mixed, grad, fill_done = fill(at, mixed, mixed_far, grad, grad_far)
        qkv, qkv_done = add((qkv,), (got_qkv,), late=(rest_done, beside, other))
        for bit in far_bits[1:]:
            qkv, qkv_done = add((qkv,), (trade(qkv, "dp", bit),))
        square, _ = squares(at, qkv, w_qkv, rest, w_in, gains)
        qkv_beside, qkv_other = trade(qkv, "dp", 2), trade(qkv, "dp", 1)
        rest_parts = (rest, beside, other, trade(beside, "dp", 1))
        qkv_parts = (qkv, qkv_beside, qkv_other, trade(qkv_beside, "dp", 1))
        for axis, bit, late in (
            ("seq", 2, ()),
            ("seq", 1, (qkv_beside, qkv_other)),
            ("dp", 2, (rest_parts[3],)),
            ("dp", 1, ()),
        ):
            square, _ = add((square,), (trade(square, axis, bit),), late=late)

        (new_in, first_in, second_in, new_out, first_out, second_out,
         new_down, first_down, second_down, row, _) = update_rest(
            at, square, rest_parts,
            (w_in, m_in, v_in), (w_out, m_out, v_out), (w_down, m_down, v_down), (fill_done,),
        )
        (new_qkv, first_qkv, second_qkv, new_gains, first_gains, second_gains, norm, _) = (
            update_last(
                at, square, (w_qkv, m_qkv, v_qkv), qkv_parts, row, (gains, m_gains, v_gains)
            )
        )
        return (
            mixed,
            grad,
            norm[0, 0],
            new_qkv, new_out, new_in, new_down, new_gains,
            first_qkv, first_out, first_in, first_down, first_gains,
            second_qkv, second_out, second_in, second_down, second_gains,
        )

    return on_device


def solution(mesh):
    rows, matrix, gain = P("dp", "seq", None), P("seq", None), P(None, "seq")
    weights = (matrix,) * 4 + (gain,)
    return jax.shard_map(
        make(mesh.shape["dp"], mesh.shape["seq"]),
        mesh=mesh,
        in_specs=(rows, rows, P("dp", None), P("dp")) + weights * 3,
        out_specs=(rows, rows, P()) + weights * 3,
        check_vma=False,
    )
```

```python
import functools
import math

import jax
import jax.numpy as jnp
from jax import lax
from jax.experimental import pallas as pl
from jax.experimental.pallas import tpu as pltpu
from jax.sharding import PartitionSpec as P

HEADS = 12
HEAD_DIM = 64
PAIR = 2 * HEAD_DIM
STEP_COUNT = 10
EPS_NORM = 1e-05
ROPE_BASE = 160000.0
NEG_FILL = -1e30
CLIP_LIMIT = 10.0
BETA_FIRST = 0.9
BETA_SECOND = 0.98
EPS_ADAM = 1e-06
STEP_RATES = (0.1, 0.5, 0.1, 0.1, 1.0)
DECAY_RATES = (0.01, 0.01, 0.01, 0.01, 0.0)
DOCS = 5
LOW = jnp.bfloat16
FULL = jnp.float32
SCALE = 1.0 / math.sqrt(HEAD_DIM)
WEIGHT = 20_000_000_000


def doc_positions(segment_ids):
    seq_len = segment_ids.shape[-1]
    places = jnp.arange(seq_len, dtype=jnp.int32)
    first_mark = jnp.ones((1,), jnp.bool_)
    change = jnp.concatenate([first_mark, segment_ids[1:] != segment_ids[:-1]])
    starts = lax.cummax(jnp.where(change, places, 0), axis=0)
    return places - starts


def rope_tables(positions):
    half_dim = HEAD_DIM // 2
    exponents = jnp.arange(half_dim, dtype=jnp.float32) * (2.0 / HEAD_DIM)
    inv_freq = ROPE_BASE ** (-exponents)
    angles = positions.astype(jnp.float32)[:, None] * inv_freq
    cos_part, sin_part = jnp.cos(angles), jnp.sin(angles)
    return (
        jnp.concatenate([cos_part] * 4, axis=1),
        jnp.concatenate([-sin_part, sin_part] * 2, axis=1),
    )


def adam_step(weight, first_old, second_old, gradient, factor, step_rate, decay_rate):
    clipped = gradient * factor
    first_new = BETA_FIRST * first_old + (1.0 - BETA_FIRST) * clipped
    second_new = BETA_SECOND * second_old + (1.0 - BETA_SECOND) * clipped * clipped
    root = second_new * lax.rsqrt(second_new) * (1.0 - BETA_SECOND**STEP_COUNT) ** -0.5
    step = first_new * (step_rate / (1.0 - BETA_FIRST**STEP_COUNT)) / (root + EPS_ADAM)
    return (weight * (1.0 - step_rate * decay_rate) - step, first_new, second_new)


def mul(left, right):
    return lax.dot_general(left, right, (((1,), (0,)), ((), ())), preferred_element_type=FULL)


def mul_t(left, right):
    return lax.dot_general(left, right, (((1,), (1,)), ((), ())), preferred_element_type=FULL)


def normalize(values):
    centered = values - jnp.mean(values, axis=-1, keepdims=True)
    root = lax.rsqrt(jnp.mean(centered * centered, axis=-1, keepdims=True) + EPS_NORM)
    return centered * root, root


def normalize_back(grad, gain, scaled, root):
    t = grad * gain
    back = root * (
        t
        - jnp.mean(t, axis=-1, keepdims=True)
        - scaled * jnp.mean(t * scaled, axis=-1, keepdims=True)
    )
    return back


def turn(values, cos_part, sin_part):
    lane = lax.broadcasted_iota(jnp.int32, values.shape, 1)
    swapped = jnp.where(
        lane % HEAD_DIM < HEAD_DIM // 2,
        pltpu.roll(values, PAIR - HEAD_DIM // 2, 1),
        pltpu.roll(values, HEAD_DIM // 2, 1),
    )
    return values * cos_part + swapped * sin_part


def three_parts(values):
    high = values.astype(LOW).astype(FULL)
    rest = values - high
    mid = rest.astype(LOW).astype(FULL)
    return high, mid, rest - mid


def wait_all(copies):
    for copy in copies:
        copy.wait()


def put(source, target, sem):
    copy = pltpu.make_async_copy(source, target, sem)
    copy.start()
    return copy


PIECES = ((0, None), (1, None), (2, 0), (2, 1), (3, 0), (3, 1))


def join_blocks(at_ref, blocks, whole):
    rows = blocks[0].shape[0]
    for block, (bits, part) in zip(blocks, PIECES):
        start = (at_ref[0] ^ bits) * rows
        size = rows
        if part is not None:
            size = rows // 2
            start += (at_ref[1] ^ part) * size
        whole[pl.ds(pl.multiple_of(start, size), size), :] = block[...]


def join_folded(at_ref, blocks, w_out, w_down):
    rows, width = blocks[0].shape[0], w_out.shape[1]
    short, last = rows // 2, width // 2
    for block, (bits, part) in zip(blocks, PIECES):
        owner = at_ref[0] ^ bits
        base = owner * (rows + short)
        first = 0 if part is None else (at_ref[1] ^ part) * short
        size = rows if part is None else short
        span = pl.ds(pl.multiple_of(owner * rows + first, short), size)
        w_out[span, :] = block[:, :width]
        span = pl.ds(pl.multiple_of(base + first, short), size)
        w_down[span, :] = block[:, width : 2 * width]
        span = pl.ds(pl.multiple_of(base + rows, short), short)
        if part is None:
            for i in range(2):
                w_down[span, i * last : (i + 1) * last] = block[
                    i * short : (i + 1) * short, 2 * width :
                ]
        else:
            lanes = pl.ds(pl.multiple_of((at_ref[1] ^ part) * last, last), last)
            w_down[span, lanes] = block[:, 2 * width :]


def fold(out, w_out, w_down, first):
    rows, width = w_out.shape
    short, last = rows // 2, width // 2
    out[:, first : first + width] = w_out[...].astype(LOW)
    out[:, first + width : first + 2 * width] = w_down[:rows, :].astype(LOW)
    for i in range(2):
        out[i * short : (i + 1) * short, first + 2 * width :] = w_down[
            rows:, i * last : (i + 1) * last
        ].astype(LOW)


def prepare_first_kernel(at_ref, w_ref, gains_ref, half_ref, gains_out, wide, sem):
    short = half_ref.shape[0]
    span = pl.ds(pl.multiple_of(at_ref[1] * short, short), short)
    copy = put(w_ref.at[span, :], wide, sem.at[0])
    gains_out[...] = gains_ref[...].astype(LOW)
    copy.wait()
    half_ref[...] = wide[...].astype(LOW)


def prepare_rest_kernel(at_ref, tokens_ref, in_ref, out_ref, down_ref, qkv_ref, cot_ref,
                        their_tokens, low_in, half_in, low_od, half_od, low_qkv, their_cot,
                        in_wide, out_wide, down_wide, qkv_wide, sem):
    slot = 1 - at_ref[2]
    copies = [
        put(source, target, sem.at[i])
        for i, (source, target) in enumerate((
            (tokens_ref.at[slot], their_tokens), (in_ref, in_wide), (out_ref, out_wide),
            (down_ref, down_wide), (qkv_ref, qkv_wide), (cot_ref.at[slot], their_cot),
        ))
    ]
    short = half_in.shape[0]
    span = pl.ds(pl.multiple_of(at_ref[1] * short, short), short)
    copies[1].wait()
    low_in[...] = in_wide[...].astype(LOW)
    half_in[...] = in_wide[span, :].astype(LOW)
    copies[2].wait()
    copies[3].wait()
    fold(low_od, out_wide, down_wide, 0)
    half_od[...] = low_od[span, :]
    copies[4].wait()
    low_qkv[...] = qkv_wide[...].astype(LOW)
    copies[0].wait()
    copies[5].wait()


def project_kernel(at_ref, tokens_ref, far_ref, gain_ref, cos_ref, sin_ref, w0, w1, w2, w3, w4, w5,
                   normed_ref, query_ref, kv_ref, weight):
    join_blocks(at_ref, (w0, w1, w2, w3, w4, w5), weight)
    rows, width = far_ref.shape
    for part in range(2):
        values = tokens_ref[at_ref[2]] if part == 0 else far_ref[...]
        scaled, _ = normalize(values.astype(FULL))
        normed_ref[pl.ds(part * rows, rows), :] = (scaled * gain_ref[...]).astype(LOW)
    for part in range(2):
        span = pl.ds(part * rows, rows)
        normed = normed_ref[span, :]
        cos_part, sin_part = cos_ref[span, :], sin_ref[span, :]
        for pair in range(2 * width // PAIR):
            lanes = pl.ds(pair * PAIR, PAIR)
            if pair % 2 == 0:
                both = mul(normed, weight[:, pl.ds(pair * PAIR, 2 * PAIR)])
            raw = both[:, (pair % 2) * PAIR : (pair % 2 + 1) * PAIR]
            turned = turn(raw, cos_part, sin_part)
            if pair < width // PAIR:
                query_ref[span, lanes] = (turned * SCALE).astype(LOW)
            else:
                kv_ref[0, span, pl.ds(pair * PAIR - width, PAIR)] = turned.astype(LOW)
        kv_ref[1, span, :] = mul(normed, weight[:, 2 * width :]).astype(LOW)


def head_lanes(head, shape):
    lane = lax.broadcasted_iota(jnp.int32, shape, 1)
    return (lane < HEAD_DIM) if head == 0 else (lane >= HEAD_DIM)


def pick(head, inside, outside):
    return jnp.where(head_lanes(head, inside.shape), inside, outside)


def attend_kernel(query_ref, near_ref, far_ref, mark_query_ref, mark_key_ref, o_ref, extra_ref):
    rows = query_ref.shape[0]
    query = query_ref[...]
    mark_query = mark_query_ref[...]
    parts = [
        (near_ref[0], jnp.transpose(near_ref[1]), mark_key_ref[:rows, :]),
        (far_ref[0], jnp.transpose(far_ref[1]), mark_key_ref[rows:, :]),
    ]
    outs, logs = [], []
    for head in range(2):
        query_head = pick(head, query, mark_query)
        scores = [mul_t(pick(head, key, mark), query_head) for key, _, mark in parts]
        top = jnp.maximum(
            jnp.max(scores[0], axis=0, keepdims=True), jnp.max(scores[1], axis=0, keepdims=True)
        )
        exps = [jnp.exp(score - top) for score in scores]
        total = jnp.sum(exps[0], axis=0, keepdims=True) + jnp.sum(exps[1], axis=0, keepdims=True)
        span = slice(head * HEAD_DIM, (head + 1) * HEAD_DIM)
        out = sum(mul(value_t[span], e.astype(LOW)) for (_, value_t, _), e in zip(parts, exps))
        outs.append(out / total)
        logs.append(top + jnp.log(total))
    o_ref[...] = jnp.transpose(jnp.concatenate(outs)).astype(LOW)
    line = lax.broadcasted_iota(jnp.int32, (PAIR, rows), 0)
    extra = jnp.zeros((PAIR, rows), FULL)
    for head in range(2):
        base = DOCS + (HEAD_DIM if head == 0 else 0)
        for i, piece in enumerate(three_parts(-logs[head])):
            extra = jnp.where(line == base + i, piece, extra)
    extra_ref[...] = jnp.transpose(extra).astype(LOW) + mark_query


def attend_back_kernel(query_ref, near_ref, far_ref, extra_ref, mark_key_ref, o_ref, do_ref,
                       cos_ref, sin_ref, dq_ref, keep_ref, send_ref):
    rows = query_ref.shape[0]
    query, extra, do = query_ref[...], extra_ref[...], do_ref[...]
    inner_all = do.astype(FULL) * o_ref[...].astype(FULL)
    lane = lax.broadcasted_iota(jnp.int32, (rows, PAIR), 1)
    zero = jnp.zeros((rows, PAIR), LOW)
    grads_query = []
    sums = [[None, None], [None, None]]
    keys_t = [jnp.transpose(near_ref[0]), jnp.transpose(far_ref[0])]
    for head in range(2):
        inside = head_lanes(head, (rows, PAIR))
        inner = jnp.sum(jnp.where(inside, inner_all, 0.0), axis=1, keepdims=True)
        base = DOCS + (HEAD_DIM if head == 0 else 0)
        tail = jnp.zeros((rows, PAIR), FULL)
        for i, piece in enumerate(three_parts(-inner)):
            tail = jnp.where(lane == base + i, piece, tail)
        query_head = pick(head, query, extra)
        do_head = pick(head, do, tail.astype(LOW))
        query_only = pick(head, query, zero)
        do_only = pick(head, do, zero)
        span = slice(head * HEAD_DIM, (head + 1) * HEAD_DIM)
        grad_query = 0.0
        for part, ref in enumerate((near_ref, far_ref)):
            mark = mark_key_ref[pl.ds(part * rows, rows), :]
            probs = jnp.exp(mul_t(pick(head, ref[0], mark), query_head))
            grad_probs = mul_t(pick(head, ref[1], mark), do_head)
            grad_scores = (probs * grad_probs).astype(LOW)
            grad_value = mul(probs.astype(LOW), do_only)
            grad_key = mul(grad_scores, query_only)
            grad_query += mul(keys_t[part][span], grad_scores)
            if head == 0:
                sums[part] = [grad_key, grad_value]
            else:
                sums[part] = [sums[part][0] + grad_key, sums[part][1] + grad_value]
        grads_query.append(grad_query)
    turned = turn(
        jnp.transpose(jnp.concatenate(grads_query)) * SCALE, cos_ref[...], -sin_ref[...]
    )
    dq_ref[...] = turned.astype(LOW)
    for i in range(2):
        keep_ref[i] = sums[0][i].astype(LOW)
        send_ref[i] = sums[1][i].astype(LOW)


def middle_kernel(at_ref, live_ref, tokens_ref, far_ref, cot_ref, cot_far_ref, oa_ref, ob_ref,
                  gain_ref, i0, i1, i2, i3, i4, i5, d0, d1, d2, d3, d4, d5,
                  mixed_ref, mixed_far_ref, dx1_ref, do_ref, keep_ref, send_ref,
                  w_out, w_in, w_down, o_all, o_t, a2_t, h_t, dm_all, duw_all, db_all,
                  mixed, dx1_all, do_all, keep, send, out_sem):
    place, slot = at_ref[0], at_ref[2]
    live = live_ref[slot].astype(FULL)
    join_folded(at_ref, (d0, d1, d2, d3, d4, d5), w_out, w_down)
    join_blocks(at_ref, (i0, i1, i2, i3, i4, i5), w_in)
    rows, width = far_ref.shape
    share = width // 4
    short, units = share // 2, w_down.shape[0]
    gain = gain_ref[...]
    o_all[:, : oa_ref.shape[1]] = oa_ref[...]
    o_all[:, oa_ref.shape[1] :] = ob_ref[...]
    copies = []
    for part in range(2):
        span = pl.ds(part * rows, rows)
        o = o_all[span, :]
        values = tokens_ref[slot] if part == 0 else far_ref[...]
        x1 = values.astype(FULL) + live * mul(o, w_out[...])
        scaled, root = normalize(x1)
        a2 = (scaled * gain).astype(LOW)
        u = mul(a2, w_in[:, :units])
        w = mul(a2, w_in[:, units:])
        phi = 0.5 * (1.0 + lax.erf(u * math.sqrt(0.5)))
        gelu = u * phi
        h = (gelu * w).astype(LOW)
        mixed[span, :] = (x1 + live * mul(h, w_down[...])).astype(LOW)
        target = mixed_ref.at[slot] if part == 0 else mixed_far_ref
        copies.append(put(mixed.at[span, :], target, out_sem.at[len(copies)]))
        cot = (cot_ref[slot] if part == 0 else cot_far_ref[...]).astype(FULL)
        dm = (live * cot).astype(LOW)
        dh = mul_t(dm, w_down[...])
        slope = phi + u * (jnp.exp(-0.5 * u * u) * (1.0 / math.sqrt(2.0 * math.pi)))
        duw_all[span, :units] = (dh * w * slope).astype(LOW)
        duw_all[span, units:] = (dh * gelu).astype(LOW)
        da2 = mul_t(duw_all[span, :], w_in[...])
        dx1 = cot + normalize_back(da2, gain, scaled, root)
        dx1_all[span, :] = dx1
        copies.append(put(dx1_all.at[span, :], dx1_ref.at[span, :], out_sem.at[len(copies)]))
        db = (live * dx1).astype(LOW)
        do_all[span, :] = mul_t(db, w_out[...]).astype(LOW)
        copies.append(put(do_all.at[span, :], do_ref.at[span, :], out_sem.at[len(copies)]))
        db_all[span, :] = db
        dm_all[span, :] = dm
        o_t[:, span] = jnp.transpose(o)
        a2_t[:, span] = jnp.transpose(a2)
        h_t[:, span] = jnp.transpose(h)
    dm, duw, db = dm_all[...], duw_all[...], db_all[...]
    for j, out, target in ((1, send, send_ref), (3, send, send_ref), (0, keep, keep_ref), (2, keep, keep_ref)):
        span = pl.ds(pl.multiple_of((place ^ j) * share, share), share)
        base = (place ^ j) * (share + short)
        down = pl.ds(pl.multiple_of(base, short), share)
        down_last = pl.ds(pl.multiple_of(base + share, short), short)
        at = 2 * units
        out[j // 2, :, :at] = mul(a2_t[span, :], duw).astype(LOW)
        out[j // 2, :, at : at + width] = mul(o_t[span, :], db).astype(LOW)
        at += width
        out[j // 2, :, at : at + width] = mul(h_t[down, :], dm).astype(LOW)
        at += width
        last = mul(h_t[down_last, :], dm).astype(LOW)
        out[j // 2, :short, at:] = last[:, : width // 2]
        out[j // 2, short:, at:] = last[:, width // 2 :]
        copies.append(put(out.at[j // 2], target.at[j // 2], out_sem.at[len(copies)]))
    wait_all(copies)


def send_kernel(count, at_ref, *refs):
    normed_ref = refs[0]
    dqs, owns, gots = (refs[1 + i * count : 1 + (i + 1) * count] for i in range(3))
    (cos_ref, sin_ref, dqkv_ref, normed_t_ref, send_ref,
     dqkv, normed_t, send, sem) = refs[1 + 3 * count :]
    width = normed_ref.shape[1]
    part_width = width // count
    normed_t[...] = jnp.transpose(normed_ref[...])
    copies = [put(normed_t, normed_t_ref, sem.at[0])]
    cos_part, sin_part = cos_ref[...], -sin_ref[...]
    for part, (dq, own, got) in enumerate(zip(dqs, owns, gots)):
        base = part * part_width
        dqkv[:, pl.ds(base, part_width)] = dq[...]
        dqkv[:, pl.ds(2 * width + base, part_width)] = (
            own[1].astype(FULL) + got[1].astype(FULL)
        ).astype(LOW)
        for pair in range(part_width // PAIR):
            lanes = pl.ds(pair * PAIR, PAIR)
            raw = own[0, :, lanes].astype(FULL) + got[0, :, lanes].astype(FULL)
            dqkv[:, pl.ds(width + base + pair * PAIR, PAIR)] = turn(raw, cos_part, sin_part).astype(
                LOW
            )
    copies.append(put(dqkv, dqkv_ref, sem.at[1]))
    right = dqkv[...]
    share = send.shape[1]
    for j in (1, 3):
        start = pl.multiple_of((at_ref[0] ^ j) * share, share)
        send[j // 2] = mul(normed_t[pl.ds(start, share), :], right).astype(LOW)
        copies.append(put(send.at[j // 2], send_ref.at[j // 2], sem.at[len(copies)]))
    wait_all(copies)


def keep_kernel(at_ref, normed_t_ref, dqkv_ref, keep_ref, keep, sem):
    right = dqkv_ref[...]
    share = keep.shape[1]
    copies = []
    for j in (0, 2):
        start = pl.multiple_of((at_ref[0] ^ j) * share, share)
        keep[j // 2] = mul(normed_t_ref[pl.ds(start, share), :], right).astype(LOW)
        copies.append(put(keep.at[j // 2], keep_ref.at[j // 2], sem.at[len(copies)]))
    wait_all(copies)


def input_kernel(at_ref, tokens_ref, far_ref, gain_ref, dx1_ref, dqkv_ref, w0, w1, w2, w3, w4, w5,
                 grad_ref, grad_far_ref, weight, grad_own, out_sem):
    join_blocks(at_ref, (w0, w1, w2, w3, w4, w5), weight)
    rows = far_ref.shape[0]
    gain = gain_ref[...]
    for part in (1, 0):
        span = pl.ds(part * rows, rows)
        values = tokens_ref[at_ref[2]] if part == 0 else far_ref[...]
        scaled, root = normalize(values.astype(FULL))
        back = normalize_back(mul_t(dqkv_ref[span, :], weight[...]), gain, scaled, root)
        grad = dx1_ref[span, :] + back
        if part == 1:
            grad_far_ref[...] = grad.astype(LOW)
        else:
            grad_own[...] = grad
    put(grad_own, grad_ref.at[at_ref[2]], out_sem.at[0]).wait()


def shaped(*shape, kind=LOW):
    return jax.ShapeDtypeStruct(shape, kind)


IN_SMEM = pl.BlockSpec(memory_space=pltpu.SMEM)
IN_VMEM = pl.BlockSpec(memory_space=pltpu.VMEM)
IN_ANY = pl.BlockSpec(memory_space=pl.ANY)


def params(mebibytes):
    return pltpu.CompilerParams(vmem_limit_bytes=int(mebibytes * 1024 * 1024))


def call(kernel, args, in_specs, out_shape, out_specs, late=(), **options):
    if not isinstance(out_shape, tuple):
        out_shape, out_specs = (out_shape,), (out_specs,)
    count, skip, outs = len(args), len(late), len(out_shape)

    def body(*refs):
        outs_at = count + skip
        return kernel(*refs[:count], *refs[outs_at : outs_at + outs], *refs[outs_at + outs + 1 :])

    return pl.pallas_call(
        body,
        in_specs=list(in_specs) + [IN_ANY] * skip,
        out_shape=out_shape + (shaped(8, 128, kind=FULL),),
        out_specs=out_specs + (IN_ANY,),
        **options,
    )(*args, *late)


def gate(values, late=(), weight=0):
    hint = {}
    if weight:
        hint["cost_estimate"] = pl.CostEstimate(
            flops=weight, transcendentals=0, bytes_accessed=0
        )
    return call(
        lambda *refs: None,
        values,
        late=late,
        out_shape=tuple(jax.ShapeDtypeStruct(v.shape, v.dtype) for v in values),
        in_specs=[IN_ANY] * len(values),
        out_specs=(IN_ANY,) * len(values),
        input_output_aliases={i: i for i in range(len(values))},
        compiler_params=params(1),
        name="gate",
        **hint,
    )[: len(values)]


def in_hbm(value):
    return pltpu.with_memory_space_constraint(value, pltpu.HBM)


def prepare_first(at, weight, gains):
    rows, width = weight.shape
    return call(
        prepare_first_kernel,
        (at, in_hbm(weight), gains),
        out_shape=(shaped(rows // 2, width), shaped(*gains.shape)),
        in_specs=[IN_SMEM, IN_ANY, IN_VMEM],
        out_specs=(IN_VMEM,) * 2,
        scratch_shapes=[pltpu.VMEM((rows // 2, width), FULL), pltpu.SemaphoreType.DMA((1,))],
        compiler_params=params(6),
        name="prepare_first",
    )


def prepare_rest(at, tokens, w_in, w_out, w_down, w_qkv, cotangent, late):
    rows, width = w_out.shape
    folded = 2 * width + width // 2
    return call(
        prepare_rest_kernel,
        (at, *[in_hbm(v) for v in (tokens, w_in, w_out, w_down, w_qkv, cotangent)]),
        late=late,
        out_shape=(
            shaped(*tokens.shape[1:]),
            shaped(*w_in.shape),
            shaped(rows // 2, w_in.shape[1]),
            shaped(rows, folded),
            shaped(rows // 2, folded),
            shaped(*w_qkv.shape),
            shaped(*cotangent.shape[1:]),
        ),
        in_specs=[IN_SMEM] + [IN_ANY] * 6,
        out_specs=(IN_VMEM,) * 7,
        scratch_shapes=[
            pltpu.VMEM(v.shape, FULL) for v in (w_in, w_out, w_down, w_qkv)
        ] + [pltpu.SemaphoreType.DMA((6,))],
        compiler_params=params(18),
        name="prepare_rest",
    )


def project(at, tokens, far, gain, cos_part, sin_part, blocks, late):
    rows, width = 2 * far.shape[0], far.shape[1]
    return call(
        project_kernel,
        (at, tokens, far, gain, cos_part, sin_part, *blocks),
        late=late,
        out_shape=(shaped(rows, width), shaped(rows, width), shaped(2, rows, width)),
        in_specs=[IN_SMEM] + [IN_VMEM] * 11,
        out_specs=(IN_VMEM,) * 3,
        scratch_shapes=[pltpu.VMEM((width, 3 * width), LOW)],
        compiler_params=params(18),
        name="project",
    )


def attend(first, count, query, near, far, mark_query, mark_key, late=()):
    rows = query.shape[0]
    row_spec = pl.BlockSpec((rows, PAIR), lambda i: (0, i + first))
    kv_spec = pl.BlockSpec((2, rows, PAIR), lambda i: (0, 0, i + first))
    out_spec = pl.BlockSpec((rows, PAIR), lambda i: (0, i))
    return call(
        attend_kernel,
        (query, near, far, mark_query, mark_key),
        late=late,
        grid=(count,),
        out_shape=(shaped(rows, count * PAIR), shaped(rows, count * PAIR)),
        in_specs=[
            row_spec,
            kv_spec,
            kv_spec,
            pl.BlockSpec((rows, PAIR), lambda i: (0, 0)),
            pl.BlockSpec((2 * rows, PAIR), lambda i: (0, 0)),
        ],
        out_specs=(out_spec, out_spec),
        compiler_params=params(16),
        name="attend",
    )


def attend_back(
    first, first_o, count, query, near, far, extra, o, mark_key, do, cos_part, sin_part, late=()
):
    rows = query.shape[0]
    row_spec = pl.BlockSpec((rows, PAIR), lambda i: (0, i + first))
    o_spec = pl.BlockSpec((rows, PAIR), lambda i: (0, i + first_o))
    kv_spec = pl.BlockSpec((2, rows, PAIR), lambda i: (0, 0, i + first))
    fixed = pl.BlockSpec((rows, PAIR), lambda i: (0, 0))
    out_row = pl.BlockSpec((rows, PAIR), lambda i: (0, i))
    out_kv = pl.BlockSpec((2, rows, PAIR), lambda i: (0, 0, i))
    return call(
        attend_back_kernel,
        (query, near, far, extra, mark_key, o, do, cos_part, sin_part),
        late=late,
        grid=(count,),
        out_shape=(
            shaped(rows, count * PAIR),
            shaped(2, rows, count * PAIR),
            shaped(2, rows, count * PAIR),
        ),
        in_specs=[
            row_spec,
            kv_spec,
            kv_spec,
            o_spec,
            pl.BlockSpec((2 * rows, PAIR), lambda i: (0, 0)),
            o_spec,
            row_spec,
            fixed,
            fixed,
        ],
        out_specs=(out_row, out_kv, out_kv),
        compiler_params=params(20),
        name="attend_back",
    )


def middle(at, live, tokens, far, cot, cot_far, o_a, o_b, gain, blocks_in, blocks_od):
    half, width = far.shape
    rows, share = 2 * half, width // 4
    units = blocks_in[0].shape[1] // 2
    total = 2 * units + blocks_od[0].shape[1]
    assert units == 4 * (share + share // 2)
    low = lambda *shape: pltpu.VMEM(shape, LOW)
    return call(
        middle_kernel,
        (at, live, tokens, far, cot, cot_far, o_a, o_b, gain, *blocks_in, *blocks_od),
        out_shape=(
            shaped(2, half, width),
            shaped(half, width),
            shaped(rows, width, kind=FULL),
            shaped(rows, width),
            shaped(2, share, total),
            shaped(2, share, total),
        ),
        in_specs=[IN_SMEM] * 2 + [IN_VMEM] * 19,
        out_specs=(IN_ANY,) * 6,
        scratch_shapes=[
            low(width, width),
            low(width, 2 * units),
            low(units, width),
            low(rows, width),
            low(width, rows),
            low(width, rows),
            low(units, rows),
            low(rows, width),
            low(rows, 2 * units),
            low(rows, width),
            low(rows, width),
            pltpu.VMEM((rows, width), FULL),
            low(rows, width),
            low(2, share, total),
            low(2, share, total),
            pltpu.SemaphoreType.DMA((10,)),
        ],
        compiler_params=params(44),
        name="middle",
    )


def qkv_send(at, normed, dq, own, got, cos_part, sin_part, late):
    rows, width = normed.shape
    share = width // 4
    return call(
        functools.partial(send_kernel, len(dq)),
        (at, normed, *dq, *own, *got, cos_part, sin_part),
        late=late,
        out_shape=(
            shaped(rows, 3 * width),
            shaped(width, rows),
            shaped(2, share, 3 * width),
        ),
        in_specs=[IN_SMEM] + [IN_VMEM] * (3 + 3 * len(dq)),
        out_specs=(IN_ANY,) * 3,
        scratch_shapes=[
            pltpu.VMEM((rows, 3 * width), LOW),
            pltpu.VMEM((width, rows), LOW),
            pltpu.VMEM((2, share, 3 * width), LOW),
            pltpu.SemaphoreType.DMA((4,)),
        ],
        compiler_params=params(20),
        name="qkv_send",
    )


def qkv_keep(at, normed_t, dqkv, late):
    width, rows = normed_t.shape
    share = width // 4
    return call(
        keep_kernel,
        (at, normed_t, dqkv),
        late=late,
        out_shape=shaped(2, share, 3 * width),
        in_specs=[IN_SMEM] + [IN_VMEM] * 2,
        out_specs=IN_ANY,
        scratch_shapes=[
            pltpu.VMEM((2, share, 3 * width), LOW),
            pltpu.SemaphoreType.DMA((2,)),
        ],
        compiler_params=params(16),
        name="qkv_keep",
    )


def input_back(at, tokens, far, gain, dx1, dqkv, blocks, late):
    half, width = far.shape
    return call(
        input_kernel,
        (at, tokens, far, gain, dx1, dqkv, *blocks),
        late=late,
        out_shape=(shaped(2, half, width, kind=FULL), shaped(half, width)),
        in_specs=[IN_SMEM] + [IN_VMEM] * 11,
        out_specs=(IN_ANY, IN_VMEM),
        scratch_shapes=[
            pltpu.VMEM((width, 3 * width), LOW),
            pltpu.VMEM((half, width), FULL),
            pltpu.SemaphoreType.DMA((1,)),
        ],
        compiler_params=params(20),
        name="input_back",
    )


def first_sums_kernel(at_ref, keep, got, own_a, far_a, mine_b, give_b):
    cut, short = far_a.shape[0], give_b.shape[1]

    def add(block, start, size):
        span = pl.ds(start, size)
        return (keep[block, span, :].astype(FULL) + got[block, span, :].astype(FULL)).astype(LOW)

    far_a[...] = add(1, 0, cut)
    for block in range(2):
        give_b[block] = add(block, pl.multiple_of(cut + (1 - at_ref[1]) * short, short), short)
        mine_b[block] = add(block, pl.multiple_of(cut + at_ref[1] * short, short), short)
    own_a[...] = add(0, 0, cut)


def first_sums(at, keep, got, late=()):
    _, rows, width = keep.shape
    cut, short = rows // 2, rows // 4
    return call(
        first_sums_kernel,
        (at, keep, got),
        late=late,
        out_shape=(shaped(cut, width),) * 2 + (shaped(2, short, width),) * 2,
        in_specs=[IN_SMEM] + [IN_VMEM] * 2,
        out_specs=(IN_VMEM,) * 4,
        compiler_params=params(20),
        name="first_sums",
    )


def second_sums_kernel(at_ref, own_a, got_a, mine_b, got_b, mine_a, give_a, near_b, far_b):
    short = mine_a.shape[0]
    for start, out in ((1 - at_ref[1], give_a), (at_ref[1], mine_a)):
        span = pl.ds(pl.multiple_of(start * short, short), short)
        out[...] = (own_a[span, :].astype(FULL) + got_a[span, :].astype(FULL)).astype(LOW)
    for block, out in ((1, far_b), (0, near_b)):
        out[...] = (mine_b[block].astype(FULL) + got_b[block].astype(FULL)).astype(LOW)


def second_sums(at, own_a, got_a, mine_b, got_b, late=()):
    _, short, width = mine_b.shape
    return call(
        second_sums_kernel,
        (at, own_a, got_a, mine_b, got_b),
        late=late,
        out_shape=(shaped(short, width),) * 4,
        in_specs=[IN_SMEM] + [IN_VMEM] * 4,
        out_specs=(IN_VMEM,) * 4,
        compiler_params=params(12),
        name="second_sums",
    )


def third_sums_kernel(at_ref, mine_a, got_a, near_b, got_b, keep, give):
    upper = mine_a[...].astype(FULL) + got_a[...].astype(FULL)
    lower = near_b[...].astype(FULL) + got_b[...].astype(FULL)
    keep[...] = jnp.where(at_ref[4] == 0, upper, lower).astype(LOW)
    give[...] = jnp.where(at_ref[4] == 0, lower, upper).astype(LOW)


def third_sums(at, mine_a, got_a, near_b, got_b, late=()):
    return call(
        third_sums_kernel,
        (at, mine_a, got_a, near_b, got_b),
        late=late,
        out_shape=(shaped(*mine_a.shape),) * 2,
        in_specs=[IN_SMEM] + [IN_VMEM] * 4,
        out_specs=(IN_VMEM,) * 2,
        compiler_params=params(12),
        name="third_sums",
    )


def squares_kernel(at_ref, qkv, w_qkv, rest, w_in, gains, out):
    inner = w_in.shape[1]
    total = jnp.sum(jnp.square(rest[:, inner:].astype(FULL)), keepdims=True)
    rows = qkv.shape[0]
    shape = (rows, gains.shape[1])
    offset = lax.broadcasted_iota(jnp.int32, shape, 1) - lax.broadcasted_iota(jnp.int32, shape, 0)
    for i, (piece, weight) in enumerate(((qkv, w_qkv), (rest, w_in))):
        start = at_ref[3]
        span = pl.ds(pl.multiple_of(start, 8), rows)
        values = piece[:, : weight.shape[1]].astype(FULL)
        sums = jnp.sum(weight[span, :].astype(LOW).astype(FULL) * values, axis=1, keepdims=True)
        gain = gains[i : i + 1, :].astype(LOW).astype(FULL)
        gain = jnp.sum(jnp.where(offset == start, gain, 0.0), axis=1, keepdims=True)
        total += jnp.sum(jnp.square(values), keepdims=True)
        total += jnp.sum(jnp.square(sums / gain), keepdims=True)
    out[...] = jnp.broadcast_to(total, out.shape)


def squares(*args):
    return call(
        squares_kernel,
        args,
        out_shape=shaped(8, 128, kind=FULL),
        in_specs=[IN_SMEM] + [IN_VMEM] * (len(args) - 1),
        out_specs=IN_VMEM,
        compiler_params=params(10),
        name="squares",
    )


def add_kernel(count, *refs):
    for i in range(count):
        out = refs[2 * count + i]
        out[...] = (refs[i][...].astype(FULL) + refs[count + i][...].astype(FULL)).astype(out.dtype)


def add(first, second, late=()):
    count = len(first)
    return call(
        functools.partial(add_kernel, count),
        (*first, *second),
        late=late,
        out_shape=tuple(jax.ShapeDtypeStruct(v.shape, v.dtype) for v in first),
        in_specs=[IN_VMEM] * (2 * count),
        out_specs=(IN_VMEM,) * count,
        compiler_params=params(8),
        name="add",
    )


def fill_kernel(at_ref, mixed_far, grad_far, mixed_in, grad_in, mixed, grad, wide, sem):
    first = put(mixed_far, mixed.at[1 - at_ref[2]], sem.at[0])
    wide[...] = grad_far[...].astype(FULL)
    put(wide, grad.at[1 - at_ref[2]], sem.at[1]).wait()
    first.wait()


def fill(at, mixed, mixed_far, grad, grad_far):
    return call(
        fill_kernel,
        (at, mixed_far, grad_far, mixed, grad),
        out_shape=(shaped(*mixed.shape), shaped(*grad.shape, kind=FULL)),
        in_specs=[IN_SMEM, IN_VMEM, IN_VMEM, IN_ANY, IN_ANY],
        out_specs=(IN_ANY,) * 2,
        input_output_aliases={3: 0, 4: 1},
        scratch_shapes=[pltpu.VMEM(grad_far.shape, FULL), pltpu.SemaphoreType.DMA((2,))],
        compiler_params=params(4),
        name="fill",
    )


def clip_factor(square_ref):
    norm = jnp.sqrt(square_ref[:1, :1])
    return jnp.minimum(1.0, CLIP_LIMIT / (norm + 1e-06))


def quarters(at_ref, parts):
    own, beside, other, other_beside = parts
    for i in range(4):
        same = at_ref[4] == i // 2
        near = jnp.where(same, own[...], beside[...])
        far = jnp.where(same, other[...], other_beside[...])
        yield jnp.where(at_ref[1] == i % 2, near, far).astype(FULL)


def gain_row(weight, gradient, start, shape):
    sums = jnp.sum(weight.astype(LOW).astype(FULL) * gradient, axis=1, keepdims=True)
    shape = (weight.shape[0], shape[1])
    offset = lax.broadcasted_iota(jnp.int32, shape, 1) - lax.broadcasted_iota(jnp.int32, shape, 0)
    return jnp.sum(jnp.where(offset == start, sums, 0.0), axis=0, keepdims=True)


class Update:
    def __init__(self, number, sources, news, targets, sem):
        self.number, self.sources, self.news, self.targets = number, sources, news, targets
        self.sem, self.out = sem, []

    def step(self, span, gradient, factor):
        weight = self.sources[0][span]
        results = adam_step(
            weight, self.sources[1][span], self.sources[2][span], gradient, factor,
            STEP_RATES[self.number], DECAY_RATES[self.number],
        )
        for result, new, target in zip(results, self.news, self.targets):
            new[span] = result
            self.out.append(put(new.at[span], target.at[span], self.sem.at[len(self.out)]))
        return weight


def update_rest_kernel(at_ref, square_ref, *refs):
    parts, refs = refs[:4], refs[4:]
    sources, targets, row_ref, news, sem = refs[:9], refs[9:18], refs[18], refs[19:28], refs[28]
    inner, out, down = (
        Update(number, *(group[3 * k : 3 * k + 3] for group in (sources, news, targets)), sem.at[k])
        for k, number in enumerate((2, 1, 3))
    )
    factor = clip_factor(square_ref)
    rows, width = sources[3].shape
    lanes = sources[0].shape[1]
    short, last = rows // 4, width // 2
    row = jnp.zeros(row_ref.shape, FULL)
    for i, gradient in enumerate(quarters(at_ref, parts)):
        span = (slice(i * short, (i + 1) * short), slice(None))
        part = gradient[:, :lanes]
        row += gain_row(inner.step(span, part, factor), part, i * short, row_ref.shape)
        out.step(span, gradient[:, lanes : lanes + width], factor)
        down.step(span, gradient[:, lanes + width : lanes + 2 * width], factor)
        start = rows + (i % 2) * short
        span = (slice(start, start + short), slice((i // 2) * last, (i // 2 + 1) * last))
        down.step(span, gradient[:, lanes + 2 * width :], factor)
    row_ref[...] = row
    wait_all(inner.out + out.out + down.out)


def update_rest(at, square, parts, inner, out, down, late):
    like = [jax.ShapeDtypeStruct(v.shape, FULL) for v in (*inner, *out, *down)]
    return call(
        update_rest_kernel,
        (at, square, *parts, *inner, *out, *down),
        late=late,
        out_shape=(*like, shaped(1, inner[0].shape[0], kind=FULL)),
        in_specs=[IN_SMEM] + [IN_VMEM] * 14,
        out_specs=(IN_ANY,) * 9 + (IN_VMEM,),
        scratch_shapes=[pltpu.VMEM(v.shape, FULL) for v in like]
        + [pltpu.SemaphoreType.DMA((3, 24))],
        compiler_params=params(28),
        name="update_rest",
    )


def update_last_kernel(at_ref, square_ref, row_ref, g_w, g_m, g_v, *refs):
    parts, refs = refs[:4], refs[4:]
    sources, targets = refs[:3], refs[3:6]
    g_w_out, g_m_out, g_v_out, norm_out = refs[6:10]
    news, sem = refs[10:13], refs[13]
    qkv = Update(0, sources, news, targets, sem)
    factor = clip_factor(square_ref)
    norm_out[...] = jnp.sqrt(square_ref[...])
    short = sources[0].shape[0] // 4
    row = jnp.zeros(row_ref.shape, FULL)
    for i, gradient in enumerate(quarters(at_ref, parts)):
        span = (slice(i * short, (i + 1) * short), slice(None))
        row += gain_row(qkv.step(span, gradient, factor), gradient, i * short, row_ref.shape)
    for i, values in enumerate((row, row_ref[...])):
        line = slice(i, i + 1)
        gradient = values / g_w[line, :].astype(LOW).astype(FULL)
        g_w_out[line, :], g_m_out[line, :], g_v_out[line, :] = adam_step(
            g_w[line, :], g_m[line, :], g_v[line, :], gradient, factor,
            STEP_RATES[4], DECAY_RATES[4],
        )
    wait_all(qkv.out)


def update_last(at, square, qkv, qkv_parts, row, gains):
    like = [jax.ShapeDtypeStruct(v.shape, FULL) for v in qkv]
    return call(
        update_last_kernel,
        (at, square, row, *gains, *qkv_parts, *qkv),
        out_shape=(
            *like,
            *[jax.ShapeDtypeStruct(v.shape, FULL) for v in gains],
            jax.ShapeDtypeStruct(square.shape, FULL),
        ),
        in_specs=[IN_SMEM] + [IN_VMEM] * 12,
        out_specs=(IN_ANY,) * 3 + (IN_VMEM,) * 4,
        scratch_shapes=[pltpu.VMEM(v.shape, FULL) for v in like]
        + [pltpu.SemaphoreType.DMA((12,))],
        compiler_params=params(18),
        name="update_last",
    )


def low_sum(*values):
    return sum(value.astype(FULL) for value in values).astype(LOW)


def index(value, i):
    return lax.dynamic_index_in_dim(value, i, 0, keepdims=False)


def make(dp_count, seq_count):
    assert seq_count == 4 and dp_count >= 8 and dp_count & (dp_count - 1) == 0
    far_bits = [1 << i for i in range(2, dp_count.bit_length() - 1)]

    def trade(value, axis, bit):
        size = seq_count if axis == "seq" else dp_count
        return lax.ppermute(value, axis, [(i, i ^ bit) for i in range(size)])

    def on_device(
        tokens, cotangent, segments, valid,
        w_qkv, w_out, w_in, w_down, gains,
        m_qkv, m_out, m_in, m_down, m_gains,
        v_qkv, v_out, v_in, v_down, v_gains,
    ):
        place = lax.axis_index("seq")
        group = lax.axis_index("dp")
        slot = place >> 1
        half = group & 1
        local_len, width = tokens.shape[1:]
        rows = 2 * local_len
        share = w_qkv.shape[0]
        side = (group >> 1) & 1
        quarter = share // 4
        at = jnp.stack([place, half, slot, side * 2 * quarter + half * quarter, side])

        half_qkv, low_gains, begun = prepare_first(at, w_qkv, gains)
        (far_qa,) = gate((trade(half_qkv, "seq", 2),), weight=10 * WEIGHT)
        (gain_far,) = gate((trade(low_gains, "seq", 2),), weight=20 * WEIGHT)
        their_tokens, low_in, half_in, low_od, half_od, low_qkv, their_cot, _ = prepare_rest(
            at, tokens, w_in, w_out, w_down, w_qkv, cotangent, (begun,)
        )
        near_q = trade(low_qkv, "seq", 1)
        far = trade(their_tokens, "seq", 2)
        far_qb = trade(far_qa, "dp", 1)
        near_qa = trade(far_qa, "seq", 1)
        near_qb = trade(far_qb, "seq", 1)
        (gain_far,) = gate((gain_far,), (far_qb,))
        gain_near = trade(jnp.stack([low_gains, gain_far]), "seq", 1)
        gain_stack = jnp.stack([low_gains, gain_near[0], gain_far, gain_near[1]])
        gain_low = jnp.concatenate(
            [index(gain_stack, b ^ place) for b in range(4)], axis=1
        ).astype(FULL)
        blocks_qkv = (low_qkv, near_q, far_qa, far_qb, near_qa, near_qb)
        low_in, low_od, half_in = gate((low_in, low_od, half_in), (far_qa,))
        near_i = trade(low_in, "seq", 1)
        near_o = trade(low_od, "seq", 1)
        (far_ia,) = gate((trade(half_in, "seq", 2),), weight=10 * WEIGHT)

        seg = index(segments, slot)
        positions = doc_positions(seg).reshape(4, local_len)
        seg = seg.reshape(4, local_len)
        chunks = [place, place ^ 2, place ^ 1, place ^ 3]
        seg_keys = jnp.concatenate([index(seg, c) for c in chunks])
        pos = jnp.concatenate([index(positions, c) for c in chunks[:2]])
        cos_part, sin_part = rope_tables(pos)
        lane = jnp.arange(PAIR, dtype=jnp.int32)[None] % HEAD_DIM
        same = seg_keys[:, None] == lane
        mark_key = jnp.where(lane < DOCS, 1.0 - same, (lane < DOCS + 3) * 1.0).astype(LOW)
        mark_query = jnp.where((lane < DOCS) & same[:rows], NEG_FILL, 0.0).astype(LOW)

        normed, query, kv, _ = project(
            at, tokens, far, gain_low[:1], cos_part, sin_part, blocks_qkv,
            (far_ia, mark_key, mark_query),
        )
        kv_far = trade(kv, "seq", 1)
        far_oa = trade(half_od, "seq", 2)
        far_ib = trade(far_ia, "dp", 1)
        near_ia = trade(far_ia, "seq", 1)
        (cot_far,) = gate((trade(their_cot, "seq", 2),), weight=WEIGHT)
        pairs = width // PAIR
        early = 2
        args = (query, kv, kv_far, mark_query, mark_key)
        o_a, extra_a, done_a = attend(0, early, *args)
        far_oa, far_ib = gate((far_oa, far_ib), (done_a,), weight=10 * WEIGHT)
        far_ob = trade(far_oa, "dp", 1)
        near_oa = trade(far_oa, "seq", 1)
        near_ib = trade(far_ib, "seq", 1)
        o_b, extra_b, done_b = attend(early, pairs - early, *args, late=(done_a, far_oa, near_ia))
        (far_ob,) = gate((far_ob,), (done_b,))
        near_ob = trade(far_ob, "seq", 1)
        blocks_in = (low_in, near_i, far_ia, far_ib, near_ia, near_ib)
        blocks_od = (low_od, near_o, far_oa, far_ob, near_oa, near_ob)

        mixed, mixed_far, dx1, do, keep_rest, send_rest, _ = middle(
            at, valid, tokens, far, cotangent, cot_far, o_a, o_b, gain_low[1:], blocks_in, blocks_od
        )
        got_rest = trade(send_rest, "seq", 1)
        two = pairs // 3
        near_args = (query, kv, kv_far)
        back_args = (mark_key, do, cos_part, sin_part)
        dq0, own0, give0, back0 = attend_back(0, 0, two, *near_args, extra_a, o_a, *back_args)
        *r1, r1_done = first_sums(at, keep_rest, got_rest, late=(back0,))
        got_ra, got_rb = gate(
            (trade(r1[1], "seq", 2), trade(r1[3], "dp", 1)), weight=10 * WEIGHT
        )
        got0 = trade(give0, "seq", 1)
        dq1, own1, give1, back1 = attend_back(
            two, two - early, two, *near_args, extra_b, o_b, *back_args, late=(r1_done,)
        )
        got1 = trade(give1, "seq", 1)
        dq2, own2, give2, back2 = attend_back(
            2 * two, 2 * two - early, pairs - 2 * two, *near_args, extra_b, o_b, *back_args,
            late=(back1, got0),
        )
        got2 = trade(give2, "seq", 1)
        dqkv, normed_t, send_qkv, send_done = qkv_send(
            at, normed, (dq0, dq1, dq2), (own0, own1, own2), (got0, got1, got2),
            cos_part, sin_part, late=(),
        )
        got_qkv = trade(send_qkv, "seq", 1)
        *r2, r2_done = second_sums(at, r1[0], got_ra, r1[2], got_rb, late=(send_done,))
        got_ra, got_rb = trade(r2[1], "dp", 1), trade(r2[3], "seq", 2)
        keep_qkv, _ = qkv_keep(at, normed_t, dqkv, late=(r2_done,))
        *q1, q1_done = first_sums(at, keep_qkv, got_qkv)
        got_qa, got_qb = trade(q1[1], "seq", 2), trade(q1[3], "dp", 1)
        grad, grad_far, grad_done = input_back(
            at, tokens, far, gain_low[:1], dx1, dqkv, blocks_qkv, late=(q1_done,)
        )
        rest, give_rest, r3_done = third_sums(
            at, r2[0], got_ra, r2[2], got_rb, late=(grad_done,)
        )
        got_rest = trade(give_rest, "dp", 2)
        *q2, q2_done = second_sums(at, q1[0], got_qa, q1[2], got_qb, late=(r3_done,))
        got_qa, got_qb = gate(
            (trade(q2[1], "dp", 1), trade(q2[3], "seq", 2)), weight=10 * WEIGHT
        )
        rest, rest_done = add((rest,), (got_rest,), late=(q2_done,))
        got_rest = trade(rest, "dp", far_bits[0])
        qkv, give_qkv, q3_done = third_sums(
            at, q2[0], got_qa, q2[2], got_qb, late=(rest_done,)
        )
        (mixed_far,) = gate((mixed_far,), (q2_done,))
        mixed_far = trade(mixed_far, "seq", 2)
        (grad_far,) = gate((grad_far,), (q2_done,))
        grad_far = trade(grad_far, "seq", 2)
        qkv, qkv_done = add((qkv,), (trade(give_qkv, "dp", 2),), late=(mixed_far,))
        got_qkv = trade(qkv, "dp", far_bits[0])
        rest, rest_done = add((rest,), (got_rest,), late=(qkv_done, grad_far))
        for bit in far_bits[1:]:
            rest, rest_done = add((rest,), (trade(rest, "dp", bit),))

        beside, other = trade(rest, "dp", 2), trade(rest, "dp", 1)
        mixed, grad, fill_done = fill(at, mixed, mixed_far, grad, grad_far)
        qkv, qkv_done = add((qkv,), (got_qkv,), late=(rest_done, fill_done, beside, other))
        for bit in far_bits[1:]:
            qkv, qkv_done = add((qkv,), (trade(qkv, "dp", bit),))
        square, _ = squares(at, qkv, w_qkv, rest, w_in, gains)
        qkv_beside, qkv_other = trade(qkv, "dp", 2), trade(qkv, "dp", 1)
        rest_parts = (rest, beside, other, trade(beside, "dp", 1))
        qkv_parts = (qkv, qkv_beside, qkv_other, trade(qkv_beside, "dp", 1))
        for axis, bit, late in (
            ("seq", 2, ()),
            ("seq", 1, (qkv_beside, qkv_other)),
            ("dp", 2, (rest_parts[3],)),
            ("dp", 1, ()),
        ):
            square, _ = add((square,), (trade(square, axis, bit),), late=late)

        (new_in, first_in, second_in, new_out, first_out, second_out,
         new_down, first_down, second_down, row, _) = update_rest(
            at, square, rest_parts,
            (w_in, m_in, v_in), (w_out, m_out, v_out), (w_down, m_down, v_down), (),
        )
        (new_qkv, first_qkv, second_qkv, new_gains, first_gains, second_gains, norm, _) = (
            update_last(
                at, square, (w_qkv, m_qkv, v_qkv), qkv_parts, row, (gains, m_gains, v_gains)
            )
        )
        return (
            mixed,
            grad,
            norm[0, 0],
            new_qkv, new_out, new_in, new_down, new_gains,
            first_qkv, first_out, first_in, first_down, first_gains,
            second_qkv, second_out, second_in, second_down, second_gains,
        )

    return on_device


def solution(mesh):
    rows, matrix, gain = P("dp", "seq", None), P("seq", None), P(None, "seq")
    weights = (matrix,) * 4 + (gain,)
    return jax.shard_map(
        make(mesh.shape["dp"], mesh.shape["seq"]),
        mesh=mesh,
        in_specs=(rows, rows, P("dp", None), P("dp")) + weights * 3,
        out_specs=(rows, rows, P()) + weights * 3,
        check_vma=False,
    )
```

```python
import functools
import math

import jax
import jax.numpy as jnp
from jax import lax
from jax.experimental import pallas as pl
from jax.experimental.pallas import tpu as pltpu
from jax.sharding import PartitionSpec as P

HEADS = 12
HEAD_DIM = 64
PAIR = 2 * HEAD_DIM
STEP_COUNT = 10
EPS_NORM = 1e-05
ROPE_BASE = 160000.0
NEG_FILL = -1e30
CLIP_LIMIT = 10.0
BETA_FIRST = 0.9
BETA_SECOND = 0.98
EPS_ADAM = 1e-06
STEP_RATES = (0.1, 0.5, 0.1, 0.1, 1.0)
DECAY_RATES = (0.01, 0.01, 0.01, 0.01, 0.0)
DOCS = 5
LOW = jnp.bfloat16
FULL = jnp.float32
SCALE = 1.0 / math.sqrt(HEAD_DIM)
WEIGHT = 20_000_000_000


def doc_positions(segment_ids):
    seq_len = segment_ids.shape[-1]
    places = jnp.arange(seq_len, dtype=jnp.int32)
    first_mark = jnp.ones((1,), jnp.bool_)
    change = jnp.concatenate([first_mark, segment_ids[1:] != segment_ids[:-1]])
    starts = lax.cummax(jnp.where(change, places, 0), axis=0)
    return places - starts


def rope_tables(positions):
    half_dim = HEAD_DIM // 2
    exponents = jnp.arange(half_dim, dtype=jnp.float32) * (2.0 / HEAD_DIM)
    inv_freq = ROPE_BASE ** (-exponents)
    angles = positions.astype(jnp.float32)[:, None] * inv_freq
    cos_part, sin_part = jnp.cos(angles), jnp.sin(angles)
    return (
        jnp.concatenate([cos_part] * 4, axis=1),
        jnp.concatenate([-sin_part, sin_part] * 2, axis=1),
    )


def adam_step(weight, first_old, second_old, gradient, factor, step_rate, decay_rate):
    clipped = gradient * factor
    first_new = BETA_FIRST * first_old + (1.0 - BETA_FIRST) * clipped
    second_new = BETA_SECOND * second_old + (1.0 - BETA_SECOND) * clipped * clipped
    root = second_new * lax.rsqrt(second_new) * (1.0 - BETA_SECOND**STEP_COUNT) ** -0.5
    step = first_new * (step_rate / (1.0 - BETA_FIRST**STEP_COUNT)) / (root + EPS_ADAM)
    return (weight * (1.0 - step_rate * decay_rate) - step, first_new, second_new)


def mul(left, right):
    return lax.dot_general(left, right, (((1,), (0,)), ((), ())), preferred_element_type=FULL)


def mul_t(left, right):
    return lax.dot_general(left, right, (((1,), (1,)), ((), ())), preferred_element_type=FULL)


def normalize(values):
    centered = values - jnp.mean(values, axis=-1, keepdims=True)
    root = lax.rsqrt(jnp.mean(centered * centered, axis=-1, keepdims=True) + EPS_NORM)
    return centered * root, root


def normalize_back(grad, gain, scaled, root):
    t = grad * gain
    back = root * (
        t
        - jnp.mean(t, axis=-1, keepdims=True)
        - scaled * jnp.mean(t * scaled, axis=-1, keepdims=True)
    )
    return back


def turn(values, cos_part, sin_part):
    lane = lax.broadcasted_iota(jnp.int32, values.shape, 1)
    swapped = jnp.where(
        lane % HEAD_DIM < HEAD_DIM // 2,
        pltpu.roll(values, PAIR - HEAD_DIM // 2, 1),
        pltpu.roll(values, HEAD_DIM // 2, 1),
    )
    return values * cos_part + swapped * sin_part


def three_parts(values):
    high = values.astype(LOW).astype(FULL)
    rest = values - high
    mid = rest.astype(LOW).astype(FULL)
    return high, mid, rest - mid


def wait_all(copies):
    for copy in copies:
        copy.wait()


def put(source, target, sem):
    copy = pltpu.make_async_copy(source, target, sem)
    copy.start()
    return copy


PIECES = ((0, None), (1, None), (2, 0), (2, 1), (3, 0), (3, 1))


def join_blocks(at_ref, blocks, whole, first=0):
    rows = blocks[0].shape[0]
    lanes = slice(first, first + whole.shape[1])
    for block, (bits, part) in zip(blocks, PIECES):
        start = (at_ref[0] ^ bits) * rows
        size = rows
        if part is not None:
            size = rows // 2
            start += (at_ref[1] ^ part) * size
        whole[pl.ds(pl.multiple_of(start, size), size), :] = block[:, lanes]


def join_folded(at_ref, blocks, w_out, w_down):
    rows, width = blocks[0].shape[0], w_out.shape[1]
    short, last = rows // 2, width // 2
    for block, (bits, part) in zip(blocks, PIECES):
        owner = at_ref[0] ^ bits
        base = owner * (rows + short)
        first = 0 if part is None else (at_ref[1] ^ part) * short
        size = rows if part is None else short
        span = pl.ds(pl.multiple_of(owner * rows + first, short), size)
        w_out[span, :] = block[:, :width]
        span = pl.ds(pl.multiple_of(base + first, short), size)
        w_down[span, :] = block[:, width : 2 * width]
        span = pl.ds(pl.multiple_of(base + rows, short), short)
        if part is None:
            for i in range(2):
                w_down[span, i * last : (i + 1) * last] = block[
                    i * short : (i + 1) * short, 2 * width :
                ]
        else:
            lanes = pl.ds(pl.multiple_of((at_ref[1] ^ part) * last, last), last)
            w_down[span, lanes] = block[:, 2 * width :]


def fold(out, w_out, w_down, first):
    rows, width = w_out.shape
    short, last = rows // 2, width // 2
    out[:, first : first + width] = w_out[...].astype(LOW)
    out[:, first + width : first + 2 * width] = w_down[:rows, :].astype(LOW)
    for i in range(2):
        out[i * short : (i + 1) * short, first + 2 * width :] = w_down[
            rows:, i * last : (i + 1) * last
        ].astype(LOW)


def prepare_first_kernel(at_ref, w_ref, gains_ref, half_ref, gains_out, wide, sem):
    short = half_ref.shape[0]
    span = pl.ds(pl.multiple_of(at_ref[1] * short, short), short)
    copy = put(w_ref.at[span, :], wide, sem.at[0])
    gains_out[...] = gains_ref[...].astype(LOW)
    copy.wait()
    half_ref[...] = wide[...].astype(LOW)


def prepare_rest_kernel(at_ref, tokens_ref, in_ref, out_ref, down_ref, qkv_ref, cot_ref,
                        their_tokens, low_in, upper_in, lower_in, low_od, half_od, low_qkv, their_cot,
                        in_wide, out_wide, down_wide, qkv_wide, sem):
    slot = 1 - at_ref[2]
    copies = [
        put(source, target, sem.at[i])
        for i, (source, target) in enumerate((
            (tokens_ref.at[slot], their_tokens), (in_ref, in_wide), (out_ref, out_wide),
            (down_ref, down_wide), (qkv_ref, qkv_wide), (cot_ref.at[slot], their_cot),
        ))
    ]
    short = half_od.shape[0]
    start = pl.multiple_of(at_ref[1] * short, short)
    span = pl.ds(start, short)
    copies[1].wait()
    upper_in[...] = in_wide[pl.ds(start, short // 2), :].astype(LOW)
    lower_in[...] = in_wide[pl.ds(start + short // 2, short // 2), :].astype(LOW)
    low_in[...] = in_wide[...].astype(LOW)
    copies[2].wait()
    copies[3].wait()
    fold(low_od, out_wide, down_wide, 0)
    half_od[...] = low_od[span, :]
    copies[4].wait()
    low_qkv[...] = qkv_wide[...].astype(LOW)
    copies[0].wait()
    copies[5].wait()


def keys_values_kernel(at_ref, tokens_ref, far_ref, gain_ref, cos_ref, sin_ref,
                       w0, w1, w2, w3, w4, w5, normed_ref, kv_ref, weight):
    rows, width = far_ref.shape
    join_blocks(at_ref, (w0, w1, w2, w3, w4, w5), weight, width)
    for part in range(2):
        span = pl.ds(part * rows, rows)
        values = tokens_ref[at_ref[2]] if part == 0 else far_ref[...]
        scaled, _ = normalize(values.astype(FULL))
        normed = (scaled * gain_ref[...]).astype(LOW)
        normed_ref[span, :] = normed
        cos_part, sin_part = cos_ref[span, :], sin_ref[span, :]
        for lane in range(0, width, 2 * PAIR):
            both = mul(normed, weight[:, lane : lane + 2 * PAIR])
            for i in range(2):
                turned = turn(both[:, i * PAIR : (i + 1) * PAIR], cos_part, sin_part)
                kv_ref[0, span, lane + i * PAIR : lane + (i + 1) * PAIR] = turned.astype(LOW)
        kv_ref[1, span, :] = mul(normed, weight[:, width:]).astype(LOW)


def queries_kernel(at_ref, normed_ref, cos_ref, sin_ref, w0, w1, w2, w3, w4, w5,
                   upper, lower, query_ref, both_ref, weight):
    rows, width = normed_ref.shape
    both_ref[: upper.shape[0], :] = upper[...]
    both_ref[upper.shape[0] :, :] = lower[...]
    join_blocks(at_ref, (w0, w1, w2, w3, w4, w5), weight)
    for part in range(2):
        span = pl.ds(part * (rows // 2), rows // 2)
        normed = normed_ref[span, :]
        cos_part, sin_part = cos_ref[span, :], sin_ref[span, :]
        for lane in range(0, width, 2 * PAIR):
            both = mul(normed, weight[:, lane : lane + 2 * PAIR])
            for i in range(2):
                turned = turn(both[:, i * PAIR : (i + 1) * PAIR], cos_part, sin_part)
                query_ref[span, lane + i * PAIR : lane + (i + 1) * PAIR] = (turned * SCALE).astype(
                    LOW
                )


def head_lanes(head, shape):
    lane = lax.broadcasted_iota(jnp.int32, shape, 1)
    return (lane < HEAD_DIM) if head == 0 else (lane >= HEAD_DIM)


def pick(head, inside, outside):
    return jnp.where(head_lanes(head, inside.shape), inside, outside)


def attend_kernel(query_ref, near_ref, far_ref, mark_query_ref, mark_key_ref, o_ref, extra_ref):
    rows = query_ref.shape[0]
    query = query_ref[...]
    mark_query = mark_query_ref[...]
    parts = [
        (near_ref[0], jnp.transpose(near_ref[1]), mark_key_ref[:rows, :]),
        (far_ref[0], jnp.transpose(far_ref[1]), mark_key_ref[rows:, :]),
    ]
    outs, logs = [], []
    for head in range(2):
        query_head = pick(head, query, mark_query)
        scores = [mul_t(pick(head, key, mark), query_head) for key, _, mark in parts]
        top = jnp.maximum(
            jnp.max(scores[0], axis=0, keepdims=True), jnp.max(scores[1], axis=0, keepdims=True)
        )
        exps = [jnp.exp(score - top) for score in scores]
        total = jnp.sum(exps[0], axis=0, keepdims=True) + jnp.sum(exps[1], axis=0, keepdims=True)
        span = slice(head * HEAD_DIM, (head + 1) * HEAD_DIM)
        out = sum(mul(value_t[span], e.astype(LOW)) for (_, value_t, _), e in zip(parts, exps))
        outs.append(out / total)
        logs.append(top + jnp.log(total))
    o_ref[...] = jnp.transpose(jnp.concatenate(outs)).astype(LOW)
    line = lax.broadcasted_iota(jnp.int32, (PAIR, rows), 0)
    extra = jnp.zeros((PAIR, rows), FULL)
    for head in range(2):
        base = DOCS + (HEAD_DIM if head == 0 else 0)
        for i, piece in enumerate(three_parts(-logs[head])):
            extra = jnp.where(line == base + i, piece, extra)
    extra_ref[...] = jnp.transpose(extra).astype(LOW) + mark_query


def attend_back_kernel(query_ref, near_ref, far_ref, extra_ref, mark_key_ref, o_ref, do_ref,
                       cos_ref, sin_ref, dq_ref, keep_ref, send_ref):
    rows = query_ref.shape[0]
    query, extra, do = query_ref[...], extra_ref[...], do_ref[...]
    inner_all = do.astype(FULL) * o_ref[...].astype(FULL)
    lane = lax.broadcasted_iota(jnp.int32, (rows, PAIR), 1)
    zero = jnp.zeros((rows, PAIR), LOW)
    grads_query = []
    sums = [[None, None], [None, None]]
    keys_t = [jnp.transpose(near_ref[0]), jnp.transpose(far_ref[0])]
    for head in range(2):
        inside = head_lanes(head, (rows, PAIR))
        inner = jnp.sum(jnp.where(inside, inner_all, 0.0), axis=1, keepdims=True)
        base = DOCS + (HEAD_DIM if head == 0 else 0)
        tail = jnp.zeros((rows, PAIR), FULL)
        for i, piece in enumerate(three_parts(-inner)):
            tail = jnp.where(lane == base + i, piece, tail)
        query_head = pick(head, query, extra)
        do_head = pick(head, do, tail.astype(LOW))
        query_only = pick(head, query, zero)
        do_only = pick(head, do, zero)
        span = slice(head * HEAD_DIM, (head + 1) * HEAD_DIM)
        grad_query = 0.0
        for part, ref in enumerate((near_ref, far_ref)):
            mark = mark_key_ref[pl.ds(part * rows, rows), :]
            probs = jnp.exp(mul_t(pick(head, ref[0], mark), query_head))
            grad_probs = mul_t(pick(head, ref[1], mark), do_head)
            grad_scores = (probs * grad_probs).astype(LOW)
            grad_value = mul(probs.astype(LOW), do_only)
            grad_key = mul(grad_scores, query_only)
            grad_query += mul(keys_t[part][span], grad_scores)
            if head == 0:
                sums[part] = [grad_key, grad_value]
            else:
                sums[part] = [sums[part][0] + grad_key, sums[part][1] + grad_value]
        grads_query.append(grad_query)
    turned = turn(
        jnp.transpose(jnp.concatenate(grads_query)) * SCALE, cos_ref[...], -sin_ref[...]
    )
    dq_ref[...] = turned.astype(LOW)
    for i in range(2):
        keep_ref[i] = sums[0][i].astype(LOW)
        send_ref[i] = sums[1][i].astype(LOW)


def middle_kernel(at_ref, live_ref, tokens_ref, far_ref, cot_ref, cot_far_ref, oa_ref, ob_ref,
                  gain_ref, i0, i1, i2, i3, i4, i5, d0, d1, d2, d3, d4, d5,
                  mixed_ref, mixed_far_ref, dx1_ref, do_ref, keep_ref, send_ref,
                  w_out, w_in, w_down, o_all, o_t, a2_t, h_t, dm_all, duw_all, db_all,
                  mixed, dx1_all, do_all, keep, send, out_sem):
    place, slot = at_ref[0], at_ref[2]
    live = live_ref[slot].astype(FULL)
    join_folded(at_ref, (d0, d1, d2, d3, d4, d5), w_out, w_down)
    join_blocks(at_ref, (i0, i1, i2, i3, i4, i5), w_in)
    rows, width = far_ref.shape
    share = width // 4
    short, units = share // 2, w_down.shape[0]
    gain = gain_ref[...]
    o_all[:, : oa_ref.shape[1]] = oa_ref[...]
    o_all[:, oa_ref.shape[1] :] = ob_ref[...]
    copies = []
    for part in range(2):
        span = pl.ds(part * rows, rows)
        o = o_all[span, :]
        values = tokens_ref[slot] if part == 0 else far_ref[...]
        x1 = values.astype(FULL) + live * mul(o, w_out[...])
        scaled, root = normalize(x1)
        a2 = (scaled * gain).astype(LOW)
        u = mul(a2, w_in[:, :units])
        w = mul(a2, w_in[:, units:])
        phi = 0.5 * (1.0 + lax.erf(u * math.sqrt(0.5)))
        gelu = u * phi
        h = (gelu * w).astype(LOW)
        mixed[span, :] = (x1 + live * mul(h, w_down[...])).astype(LOW)
        target = mixed_ref.at[slot] if part == 0 else mixed_far_ref
        copies.append(put(mixed.at[span, :], target, out_sem.at[len(copies)]))
        cot = (cot_ref[slot] if part == 0 else cot_far_ref[...]).astype(FULL)
        dm = (live * cot).astype(LOW)
        dh = mul_t(dm, w_down[...])
        slope = phi + u * (jnp.exp(-0.5 * u * u) * (1.0 / math.sqrt(2.0 * math.pi)))
        duw_all[span, :units] = (dh * w * slope).astype(LOW)
        duw_all[span, units:] = (dh * gelu).astype(LOW)
        da2 = mul_t(duw_all[span, :], w_in[...])
        dx1 = cot + normalize_back(da2, gain, scaled, root)
        dx1_all[span, :] = dx1
        copies.append(put(dx1_all.at[span, :], dx1_ref.at[span, :], out_sem.at[len(copies)]))
        db = (live * dx1).astype(LOW)
        do_all[span, :] = mul_t(db, w_out[...]).astype(LOW)
        copies.append(put(do_all.at[span, :], do_ref.at[span, :], out_sem.at[len(copies)]))
        db_all[span, :] = db
        dm_all[span, :] = dm
        o_t[:, span] = jnp.transpose(o)
        a2_t[:, span] = jnp.transpose(a2)
        h_t[:, span] = jnp.transpose(h)
    dm, duw, db = dm_all[...], duw_all[...], db_all[...]
    for j, out, target in ((1, send, send_ref), (3, send, send_ref), (0, keep, keep_ref), (2, keep, keep_ref)):
        span = pl.ds(pl.multiple_of((place ^ j) * share, share), share)
        base = (place ^ j) * (share + short)
        down = pl.ds(pl.multiple_of(base, short), share)
        down_last = pl.ds(pl.multiple_of(base + share, short), short)
        at = 2 * units
        out[j // 2, :, :at] = mul(a2_t[span, :], duw).astype(LOW)
        out[j // 2, :, at : at + width] = mul(o_t[span, :], db).astype(LOW)
        at += width
        out[j // 2, :, at : at + width] = mul(h_t[down, :], dm).astype(LOW)
        at += width
        last = mul(h_t[down_last, :], dm).astype(LOW)
        out[j // 2, :short, at:] = last[:, : width // 2]
        out[j // 2, short:, at:] = last[:, width // 2 :]
        copies.append(put(out.at[j // 2], target.at[j // 2], out_sem.at[len(copies)]))
    wait_all(copies)


def send_kernel(count, at_ref, *refs):
    normed_ref = refs[0]
    dqs, owns, gots = (refs[1 + i * count : 1 + (i + 1) * count] for i in range(3))
    (cos_ref, sin_ref, dqkv_ref, normed_t_ref, send_ref,
     dqkv, normed_t, send, sem) = refs[1 + 3 * count :]
    width = normed_ref.shape[1]
    part_width = width // count
    normed_t[...] = jnp.transpose(normed_ref[...])
    copies = [put(normed_t, normed_t_ref, sem.at[0])]
    cos_part, sin_part = cos_ref[...], -sin_ref[...]
    for part, (dq, own, got) in enumerate(zip(dqs, owns, gots)):
        base = part * part_width
        dqkv[:, pl.ds(base, part_width)] = dq[...]
        dqkv[:, pl.ds(2 * width + base, part_width)] = (
            own[1].astype(FULL) + got[1].astype(FULL)
        ).astype(LOW)
        for pair in range(part_width // PAIR):
            lanes = pl.ds(pair * PAIR, PAIR)
            raw = own[0, :, lanes].astype(FULL) + got[0, :, lanes].astype(FULL)
            dqkv[:, pl.ds(width + base + pair * PAIR, PAIR)] = turn(raw, cos_part, sin_part).astype(
                LOW
            )
    copies.append(put(dqkv, dqkv_ref, sem.at[1]))
    right = dqkv[...]
    share = send.shape[1]
    for j in (1, 3):
        start = pl.multiple_of((at_ref[0] ^ j) * share, share)
        send[j // 2] = mul(normed_t[pl.ds(start, share), :], right).astype(LOW)
        copies.append(put(send.at[j // 2], send_ref.at[j // 2], sem.at[len(copies)]))
    wait_all(copies)


def keep_kernel(at_ref, normed_t_ref, dqkv_ref, keep_ref, keep, sem):
    right = dqkv_ref[...]
    share = keep.shape[1]
    copies = []
    for j in (0, 2):
        start = pl.multiple_of((at_ref[0] ^ j) * share, share)
        keep[j // 2] = mul(normed_t_ref[pl.ds(start, share), :], right).astype(LOW)
        copies.append(put(keep.at[j // 2], keep_ref.at[j // 2], sem.at[len(copies)]))
    wait_all(copies)


def input_kernel(at_ref, tokens_ref, far_ref, gain_ref, dx1_ref, dqkv_ref, w0, w1, w2, w3, w4, w5,
                 grad_ref, grad_far_ref, weight, grad_own, out_sem):
    join_blocks(at_ref, (w0, w1, w2, w3, w4, w5), weight)
    rows = far_ref.shape[0]
    gain = gain_ref[...]
    for part in (1, 0):
        span = pl.ds(part * rows, rows)
        values = tokens_ref[at_ref[2]] if part == 0 else far_ref[...]
        scaled, root = normalize(values.astype(FULL))
        back = normalize_back(mul_t(dqkv_ref[span, :], weight[...]), gain, scaled, root)
        grad = dx1_ref[span, :] + back
        if part == 1:
            grad_far_ref[...] = grad.astype(LOW)
        else:
            grad_own[...] = grad
    put(grad_own, grad_ref.at[at_ref[2]], out_sem.at[0]).wait()


def shaped(*shape, kind=LOW):
    return jax.ShapeDtypeStruct(shape, kind)


IN_SMEM = pl.BlockSpec(memory_space=pltpu.SMEM)
IN_VMEM = pl.BlockSpec(memory_space=pltpu.VMEM)
IN_ANY = pl.BlockSpec(memory_space=pl.ANY)


def params(mebibytes):
    return pltpu.CompilerParams(vmem_limit_bytes=int(mebibytes * 1024 * 1024))


def call(kernel, args, in_specs, out_shape, out_specs, late=(), **options):
    if not isinstance(out_shape, tuple):
        out_shape, out_specs = (out_shape,), (out_specs,)
    count, skip, outs = len(args), len(late), len(out_shape)

    def body(*refs):
        outs_at = count + skip
        return kernel(*refs[:count], *refs[outs_at : outs_at + outs], *refs[outs_at + outs + 1 :])

    return pl.pallas_call(
        body,
        in_specs=list(in_specs) + [IN_ANY] * skip,
        out_shape=out_shape + (shaped(8, 128, kind=FULL),),
        out_specs=out_specs + (IN_ANY,),
        **options,
    )(*args, *late)


def gate(values, late=(), weight=0):
    hint = {}
    if weight:
        hint["cost_estimate"] = pl.CostEstimate(
            flops=weight, transcendentals=0, bytes_accessed=0
        )
    return call(
        lambda *refs: None,
        values,
        late=late,
        out_shape=tuple(jax.ShapeDtypeStruct(v.shape, v.dtype) for v in values),
        in_specs=[IN_ANY] * len(values),
        out_specs=(IN_ANY,) * len(values),
        input_output_aliases={i: i for i in range(len(values))},
        compiler_params=params(1),
        name="gate",
        **hint,
    )[: len(values)]


def in_hbm(value):
    return pltpu.with_memory_space_constraint(value, pltpu.HBM)


def prepare_first(at, weight, gains):
    rows, width = weight.shape
    return call(
        prepare_first_kernel,
        (at, in_hbm(weight), gains),
        out_shape=(shaped(rows // 2, width), shaped(*gains.shape)),
        in_specs=[IN_SMEM, IN_ANY, IN_VMEM],
        out_specs=(IN_VMEM,) * 2,
        scratch_shapes=[pltpu.VMEM((rows // 2, width), FULL), pltpu.SemaphoreType.DMA((1,))],
        compiler_params=params(6),
        name="prepare_first",
    )


def prepare_rest(at, tokens, w_in, w_out, w_down, w_qkv, cotangent, late):
    rows, width = w_out.shape
    folded = 2 * width + width // 2
    return call(
        prepare_rest_kernel,
        (at, *[in_hbm(v) for v in (tokens, w_in, w_out, w_down, w_qkv, cotangent)]),
        late=late,
        out_shape=(
            shaped(*tokens.shape[1:]),
            shaped(*w_in.shape),
            shaped(rows // 4, w_in.shape[1]),
            shaped(rows // 4, w_in.shape[1]),
            shaped(rows, folded),
            shaped(rows // 2, folded),
            shaped(*w_qkv.shape),
            shaped(*cotangent.shape[1:]),
        ),
        in_specs=[IN_SMEM] + [IN_ANY] * 6,
        out_specs=(IN_VMEM,) * 8,
        scratch_shapes=[
            pltpu.VMEM(v.shape, FULL) for v in (w_in, w_out, w_down, w_qkv)
        ] + [pltpu.SemaphoreType.DMA((6,))],
        compiler_params=params(18),
        name="prepare_rest",
    )


def keys_values(at, tokens, far, gain, cos_part, sin_part, blocks, late):
    rows, width = 2 * far.shape[0], far.shape[1]
    return call(
        keys_values_kernel,
        (at, tokens, far, gain, cos_part, sin_part, *blocks),
        late=late,
        out_shape=(shaped(rows, width), shaped(2, rows, width)),
        in_specs=[IN_SMEM] + [IN_VMEM] * 11,
        out_specs=(IN_VMEM,) * 2,
        scratch_shapes=[pltpu.VMEM((width, 2 * width), LOW)],
        compiler_params=params(16),
        name="keys_values",
    )


def queries(at, normed, cos_part, sin_part, blocks, come):
    rows, width = normed.shape
    return call(
        queries_kernel,
        (at, normed, cos_part, sin_part, *blocks, *come),
        out_shape=(shaped(rows, width), shaped(2 * come[0].shape[0], come[0].shape[1])),
        in_specs=[IN_SMEM] + [IN_VMEM] * 11,
        out_specs=(IN_VMEM,) * 2,
        scratch_shapes=[pltpu.VMEM((width, width), LOW)],
        compiler_params=params(12),
        name="queries",
    )


def attend(first, count, query, near, far, mark_query, mark_key, late=()):
    rows = query.shape[0]
    row_spec = pl.BlockSpec((rows, PAIR), lambda i: (0, i + first))
    kv_spec = pl.BlockSpec((2, rows, PAIR), lambda i: (0, 0, i + first))
    out_spec = pl.BlockSpec((rows, PAIR), lambda i: (0, i))
    return call(
        attend_kernel,
        (query, near, far, mark_query, mark_key),
        late=late,
        grid=(count,),
        out_shape=(shaped(rows, count * PAIR), shaped(rows, count * PAIR)),
        in_specs=[
            row_spec,
            kv_spec,
            kv_spec,
            pl.BlockSpec((rows, PAIR), lambda i: (0, 0)),
            pl.BlockSpec((2 * rows, PAIR), lambda i: (0, 0)),
        ],
        out_specs=(out_spec, out_spec),
        compiler_params=params(16),
        name="attend",
    )


def attend_back(
    first, first_o, count, query, near, far, extra, o, mark_key, do, cos_part, sin_part, late=()
):
    rows = query.shape[0]
    row_spec = pl.BlockSpec((rows, PAIR), lambda i: (0, i + first))
    o_spec = pl.BlockSpec((rows, PAIR), lambda i: (0, i + first_o))
    kv_spec = pl.BlockSpec((2, rows, PAIR), lambda i: (0, 0, i + first))
    fixed = pl.BlockSpec((rows, PAIR), lambda i: (0, 0))
    out_row = pl.BlockSpec((rows, PAIR), lambda i: (0, i))
    out_kv = pl.BlockSpec((2, rows, PAIR), lambda i: (0, 0, i))
    return call(
        attend_back_kernel,
        (query, near, far, extra, mark_key, o, do, cos_part, sin_part),
        late=late,
        grid=(count,),
        out_shape=(
            shaped(rows, count * PAIR),
            shaped(2, rows, count * PAIR),
            shaped(2, rows, count * PAIR),
        ),
        in_specs=[
            row_spec,
            kv_spec,
            kv_spec,
            o_spec,
            pl.BlockSpec((2 * rows, PAIR), lambda i: (0, 0)),
            o_spec,
            row_spec,
            fixed,
            fixed,
        ],
        out_specs=(out_row, out_kv, out_kv),
        compiler_params=params(20),
        name="attend_back",
    )


def middle(at, live, tokens, far, cot, cot_far, o_a, o_b, gain, blocks_in, blocks_od):
    half, width = far.shape
    rows, share = 2 * half, width // 4
    units = blocks_in[0].shape[1] // 2
    total = 2 * units + blocks_od[0].shape[1]
    assert units == 4 * (share + share // 2)
    low = lambda *shape: pltpu.VMEM(shape, LOW)
    return call(
        middle_kernel,
        (at, live, tokens, far, cot, cot_far, o_a, o_b, gain, *blocks_in, *blocks_od),
        out_shape=(
            shaped(2, half, width),
            shaped(half, width),
            shaped(rows, width, kind=FULL),
            shaped(rows, width),
            shaped(2, share, total),
            shaped(2, share, total),
        ),
        in_specs=[IN_SMEM] * 2 + [IN_VMEM] * 19,
        out_specs=(IN_ANY,) * 6,
        scratch_shapes=[
            low(width, width),
            low(width, 2 * units),
            low(units, width),
            low(rows, width),
            low(width, rows),
            low(width, rows),
            low(units, rows),
            low(rows, width),
            low(rows, 2 * units),
            low(rows, width),
            low(rows, width),
            pltpu.VMEM((rows, width), FULL),
            low(rows, width),
            low(2, share, total),
            low(2, share, total),
            pltpu.SemaphoreType.DMA((10,)),
        ],
        compiler_params=params(44),
        name="middle",
    )


def qkv_send(at, normed, dq, own, got, cos_part, sin_part, late):
    rows, width = normed.shape
    share = width // 4
    return call(
        functools.partial(send_kernel, len(dq)),
        (at, normed, *dq, *own, *got, cos_part, sin_part),
        late=late,
        out_shape=(
            shaped(rows, 3 * width),
            shaped(width, rows),
            shaped(2, share, 3 * width),
        ),
        in_specs=[IN_SMEM] + [IN_VMEM] * (3 + 3 * len(dq)),
        out_specs=(IN_ANY,) * 3,
        scratch_shapes=[
            pltpu.VMEM((rows, 3 * width), LOW),
            pltpu.VMEM((width, rows), LOW),
            pltpu.VMEM((2, share, 3 * width), LOW),
            pltpu.SemaphoreType.DMA((4,)),
        ],
        compiler_params=params(20),
        name="qkv_send",
    )


def qkv_keep(at, normed_t, dqkv, late):
    width, rows = normed_t.shape
    share = width // 4
    return call(
        keep_kernel,
        (at, normed_t, dqkv),
        late=late,
        out_shape=shaped(2, share, 3 * width),
        in_specs=[IN_SMEM] + [IN_VMEM] * 2,
        out_specs=IN_ANY,
        scratch_shapes=[
            pltpu.VMEM((2, share, 3 * width), LOW),
            pltpu.SemaphoreType.DMA((2,)),
        ],
        compiler_params=params(16),
        name="qkv_keep",
    )


def input_back(at, tokens, far, gain, dx1, dqkv, blocks, late):
    half, width = far.shape
    return call(
        input_kernel,
        (at, tokens, far, gain, dx1, dqkv, *blocks),
        late=late,
        out_shape=(shaped(2, half, width, kind=FULL), shaped(half, width)),
        in_specs=[IN_SMEM] + [IN_VMEM] * 11,
        out_specs=(IN_ANY, IN_VMEM),
        scratch_shapes=[
            pltpu.VMEM((width, 3 * width), LOW),
            pltpu.VMEM((half, width), FULL),
            pltpu.SemaphoreType.DMA((1,)),
        ],
        compiler_params=params(20),
        name="input_back",
    )


def first_sums_kernel(at_ref, keep, got, own_a, far_a, mine_b, give_b):
    cut, short = far_a.shape[0], give_b.shape[1]

    def add(block, start, size):
        span = pl.ds(start, size)
        return (keep[block, span, :].astype(FULL) + got[block, span, :].astype(FULL)).astype(LOW)

    far_a[...] = add(1, 0, cut)
    for block in range(2):
        give_b[block] = add(block, pl.multiple_of(cut + (1 - at_ref[1]) * short, short), short)
        mine_b[block] = add(block, pl.multiple_of(cut + at_ref[1] * short, short), short)
    own_a[...] = add(0, 0, cut)


def first_sums(at, keep, got, late=()):
    _, rows, width = keep.shape
    cut, short = rows // 2, rows // 4
    return call(
        first_sums_kernel,
        (at, keep, got),
        late=late,
        out_shape=(shaped(cut, width),) * 2 + (shaped(2, short, width),) * 2,
        in_specs=[IN_SMEM] + [IN_VMEM] * 2,
        out_specs=(IN_VMEM,) * 4,
        compiler_params=params(20),
        name="first_sums",
    )


def second_sums_kernel(at_ref, own_a, got_a, mine_b, got_b, mine_a, give_a, near_b, far_b):
    short = mine_a.shape[0]
    for start, out in ((1 - at_ref[1], give_a), (at_ref[1], mine_a)):
        span = pl.ds(pl.multiple_of(start * short, short), short)
        out[...] = (own_a[span, :].astype(FULL) + got_a[span, :].astype(FULL)).astype(LOW)
    for block, out in ((1, far_b), (0, near_b)):
        out[...] = (mine_b[block].astype(FULL) + got_b[block].astype(FULL)).astype(LOW)


def second_sums(at, own_a, got_a, mine_b, got_b, late=()):
    _, short, width = mine_b.shape
    return call(
        second_sums_kernel,
        (at, own_a, got_a, mine_b, got_b),
        late=late,
        out_shape=(shaped(short, width),) * 4,
        in_specs=[IN_SMEM] + [IN_VMEM] * 4,
        out_specs=(IN_VMEM,) * 4,
        compiler_params=params(12),
        name="second_sums",
    )


def third_sums_kernel(at_ref, mine_a, got_a, near_b, got_b, keep, give):
    upper = mine_a[...].astype(FULL) + got_a[...].astype(FULL)
    lower = near_b[...].astype(FULL) + got_b[...].astype(FULL)
    keep[...] = jnp.where(at_ref[4] == 0, upper, lower).astype(LOW)
    give[...] = jnp.where(at_ref[4] == 0, lower, upper).astype(LOW)


def third_sums(at, mine_a, got_a, near_b, got_b, late=()):
    return call(
        third_sums_kernel,
        (at, mine_a, got_a, near_b, got_b),
        late=late,
        out_shape=(shaped(*mine_a.shape),) * 2,
        in_specs=[IN_SMEM] + [IN_VMEM] * 4,
        out_specs=(IN_VMEM,) * 2,
        compiler_params=params(12),
        name="third_sums",
    )


def squares_kernel(at_ref, qkv, w_qkv, rest, w_in, gains, out):
    inner = w_in.shape[1]
    total = jnp.sum(jnp.square(rest[:, inner:].astype(FULL)), keepdims=True)
    rows = qkv.shape[0]
    shape = (rows, gains.shape[1])
    offset = lax.broadcasted_iota(jnp.int32, shape, 1) - lax.broadcasted_iota(jnp.int32, shape, 0)
    for i, (piece, weight) in enumerate(((qkv, w_qkv), (rest, w_in))):
        start = at_ref[3]
        span = pl.ds(pl.multiple_of(start, 8), rows)
        values = piece[:, : weight.shape[1]].astype(FULL)
        sums = jnp.sum(weight[span, :].astype(LOW).astype(FULL) * values, axis=1, keepdims=True)
        gain = gains[i : i + 1, :].astype(LOW).astype(FULL)
        gain = jnp.sum(jnp.where(offset == start, gain, 0.0), axis=1, keepdims=True)
        total += jnp.sum(jnp.square(values), keepdims=True)
        total += jnp.sum(jnp.square(sums / gain), keepdims=True)
    out[...] = jnp.broadcast_to(total, out.shape)


def squares(*args):
    return call(
        squares_kernel,
        args,
        out_shape=shaped(8, 128, kind=FULL),
        in_specs=[IN_SMEM] + [IN_VMEM] * (len(args) - 1),
        out_specs=IN_VMEM,
        compiler_params=params(10),
        name="squares",
    )


def add_kernel(count, *refs):
    for i in range(count):
        out = refs[2 * count + i]
        out[...] = (refs[i][...].astype(FULL) + refs[count + i][...].astype(FULL)).astype(out.dtype)


def add(first, second, late=()):
    count = len(first)
    return call(
        functools.partial(add_kernel, count),
        (*first, *second),
        late=late,
        out_shape=tuple(jax.ShapeDtypeStruct(v.shape, v.dtype) for v in first),
        in_specs=[IN_VMEM] * (2 * count),
        out_specs=(IN_VMEM,) * count,
        compiler_params=params(8),
        name="add",
    )


def fill_kernel(at_ref, mixed_far, grad_far, mixed_in, grad_in, mixed, grad, wide, sem):
    first = put(mixed_far, mixed.at[1 - at_ref[2]], sem.at[0])
    wide[...] = grad_far[...].astype(FULL)
    put(wide, grad.at[1 - at_ref[2]], sem.at[1]).wait()
    first.wait()


def fill(at, mixed, mixed_far, grad, grad_far):
    return call(
        fill_kernel,
        (at, mixed_far, grad_far, mixed, grad),
        out_shape=(shaped(*mixed.shape), shaped(*grad.shape, kind=FULL)),
        in_specs=[IN_SMEM, IN_VMEM, IN_VMEM, IN_ANY, IN_ANY],
        out_specs=(IN_ANY,) * 2,
        input_output_aliases={3: 0, 4: 1},
        scratch_shapes=[pltpu.VMEM(grad_far.shape, FULL), pltpu.SemaphoreType.DMA((2,))],
        compiler_params=params(4),
        name="fill",
    )


def clip_factor(square_ref):
    norm = jnp.sqrt(square_ref[:1, :1])
    return jnp.minimum(1.0, CLIP_LIMIT / (norm + 1e-06))


def quarters(at_ref, parts):
    own, beside, other, other_beside = parts
    for i in range(4):
        same = at_ref[4] == i // 2
        near = jnp.where(same, own[...], beside[...])
        far = jnp.where(same, other[...], other_beside[...])
        yield jnp.where(at_ref[1] == i % 2, near, far).astype(FULL)


def gain_row(weight, gradient, start, shape):
    sums = jnp.sum(weight.astype(LOW).astype(FULL) * gradient, axis=1, keepdims=True)
    shape = (weight.shape[0], shape[1])
    offset = lax.broadcasted_iota(jnp.int32, shape, 1) - lax.broadcasted_iota(jnp.int32, shape, 0)
    return jnp.sum(jnp.where(offset == start, sums, 0.0), axis=0, keepdims=True)


class Update:
    def __init__(self, number, sources, news, targets, sem):
        self.number, self.sources, self.news, self.targets = number, sources, news, targets
        self.sem, self.out = sem, []

    def step(self, span, gradient, factor):
        weight = self.sources[0][span]
        results = adam_step(
            weight, self.sources[1][span], self.sources[2][span], gradient, factor,
            STEP_RATES[self.number], DECAY_RATES[self.number],
        )
        for result, new, target in zip(results, self.news, self.targets):
            new[span] = result
            self.out.append(put(new.at[span], target.at[span], self.sem.at[len(self.out)]))
        return weight


def update_rest_kernel(at_ref, square_ref, *refs):
    parts, refs = refs[:4], refs[4:]
    sources, targets, row_ref, news, sem = refs[:9], refs[9:18], refs[18], refs[19:28], refs[28]
    inner, out, down = (
        Update(number, *(group[3 * k : 3 * k + 3] for group in (sources, news, targets)), sem.at[k])
        for k, number in enumerate((2, 1, 3))
    )
    factor = clip_factor(square_ref)
    rows, width = sources[3].shape
    lanes = sources[0].shape[1]
    short, last = rows // 4, width // 2
    row = jnp.zeros(row_ref.shape, FULL)
    for i, gradient in enumerate(quarters(at_ref, parts)):
        span = (slice(i * short, (i + 1) * short), slice(None))
        part = gradient[:, :lanes]
        row += gain_row(inner.step(span, part, factor), part, i * short, row_ref.shape)
        out.step(span, gradient[:, lanes : lanes + width], factor)
        down.step(span, gradient[:, lanes + width : lanes + 2 * width], factor)
        start = rows + (i % 2) * short
        span = (slice(start, start + short), slice((i // 2) * last, (i // 2 + 1) * last))
        down.step(span, gradient[:, lanes + 2 * width :], factor)
    row_ref[...] = row
    wait_all(inner.out + out.out + down.out)


def update_rest(at, square, parts, inner, out, down, late):
    like = [jax.ShapeDtypeStruct(v.shape, FULL) for v in (*inner, *out, *down)]
    return call(
        update_rest_kernel,
        (at, square, *parts, *inner, *out, *down),
        late=late,
        out_shape=(*like, shaped(1, inner[0].shape[0], kind=FULL)),
        in_specs=[IN_SMEM] + [IN_VMEM] * 14,
        out_specs=(IN_ANY,) * 9 + (IN_VMEM,),
        scratch_shapes=[pltpu.VMEM(v.shape, FULL) for v in like]
        + [pltpu.SemaphoreType.DMA((3, 24))],
        compiler_params=params(28),
        name="update_rest",
    )


def update_last_kernel(at_ref, square_ref, row_ref, g_w, g_m, g_v, *refs):
    parts, refs = refs[:4], refs[4:]
    sources, targets = refs[:3], refs[3:6]
    g_w_out, g_m_out, g_v_out, norm_out = refs[6:10]
    news, sem = refs[10:13], refs[13]
    qkv = Update(0, sources, news, targets, sem)
    factor = clip_factor(square_ref)
    norm_out[...] = jnp.sqrt(square_ref[...])
    short = sources[0].shape[0] // 4
    row = jnp.zeros(row_ref.shape, FULL)
    for i, gradient in enumerate(quarters(at_ref, parts)):
        span = (slice(i * short, (i + 1) * short), slice(None))
        row += gain_row(qkv.step(span, gradient, factor), gradient, i * short, row_ref.shape)
    for i, values in enumerate((row, row_ref[...])):
        line = slice(i, i + 1)
        gradient = values / g_w[line, :].astype(LOW).astype(FULL)
        g_w_out[line, :], g_m_out[line, :], g_v_out[line, :] = adam_step(
            g_w[line, :], g_m[line, :], g_v[line, :], gradient, factor,
            STEP_RATES[4], DECAY_RATES[4],
        )
    wait_all(qkv.out)


def update_last(at, square, qkv, qkv_parts, row, gains):
    like = [jax.ShapeDtypeStruct(v.shape, FULL) for v in qkv]
    return call(
        update_last_kernel,
        (at, square, row, *gains, *qkv_parts, *qkv),
        out_shape=(
            *like,
            *[jax.ShapeDtypeStruct(v.shape, FULL) for v in gains],
            jax.ShapeDtypeStruct(square.shape, FULL),
        ),
        in_specs=[IN_SMEM] + [IN_VMEM] * 12,
        out_specs=(IN_ANY,) * 3 + (IN_VMEM,) * 4,
        scratch_shapes=[pltpu.VMEM(v.shape, FULL) for v in like]
        + [pltpu.SemaphoreType.DMA((12,))],
        compiler_params=params(18),
        name="update_last",
    )


def low_sum(*values):
    return sum(value.astype(FULL) for value in values).astype(LOW)


def index(value, i):
    return lax.dynamic_index_in_dim(value, i, 0, keepdims=False)


def make(dp_count, seq_count):
    assert seq_count == 4 and dp_count >= 8 and dp_count & (dp_count - 1) == 0
    far_bits = [1 << i for i in range(2, dp_count.bit_length() - 1)]

    def trade(value, axis, bit):
        size = seq_count if axis == "seq" else dp_count
        return lax.ppermute(value, axis, [(i, i ^ bit) for i in range(size)])

    def on_device(
        tokens, cotangent, segments, valid,
        w_qkv, w_out, w_in, w_down, gains,
        m_qkv, m_out, m_in, m_down, m_gains,
        v_qkv, v_out, v_in, v_down, v_gains,
    ):
        place = lax.axis_index("seq")
        group = lax.axis_index("dp")
        slot = place >> 1
        half = group & 1
        local_len, width = tokens.shape[1:]
        rows = 2 * local_len
        share = w_qkv.shape[0]
        side = (group >> 1) & 1
        quarter = share // 4
        at = jnp.stack([place, half, slot, side * 2 * quarter + half * quarter, side])

        half_qkv, low_gains, begun = prepare_first(at, w_qkv, gains)
        (far_qa,) = gate((trade(half_qkv, "seq", 2),), weight=10 * WEIGHT)
        (gain_far,) = gate((trade(low_gains, "seq", 2),), weight=20 * WEIGHT)
        (their_tokens, low_in, upper_in, lower_in, low_od, half_od, low_qkv, their_cot, _) = (
            prepare_rest(at, tokens, w_in, w_out, w_down, w_qkv, cotangent, (begun,))
        )
        near_q = trade(low_qkv, "seq", 1)
        far = trade(their_tokens, "seq", 2)
        far_qb = trade(far_qa, "dp", 1)
        near_qa = trade(far_qa, "seq", 1)
        near_qb = trade(far_qb, "seq", 1)
        (gain_far,) = gate((gain_far,), (far_qb,))
        gain_near = trade(jnp.stack([low_gains, gain_far]), "seq", 1)
        gain_stack = jnp.stack([low_gains, gain_near[0], gain_far, gain_near[1]])
        gain_low = jnp.concatenate(
            [index(gain_stack, b ^ place) for b in range(4)], axis=1
        ).astype(FULL)
        blocks_qkv = (low_qkv, near_q, far_qa, far_qb, near_qa, near_qb)
        low_in, low_od, upper_in, lower_in = gate((low_in, low_od, upper_in, lower_in), (far_qa,))
        near_i = trade(low_in, "seq", 1)
        near_o = trade(low_od, "seq", 1)
        (far_iu,) = gate((trade(upper_in, "seq", 2),), weight=10 * WEIGHT)
        (far_il,) = gate((trade(lower_in, "seq", 2),), weight=10 * WEIGHT)

        seg = index(segments, slot)
        positions = doc_positions(seg).reshape(4, local_len)
        seg = seg.reshape(4, local_len)
        chunks = [place, place ^ 2, place ^ 1, place ^ 3]
        seg_keys = jnp.concatenate([index(seg, c) for c in chunks])
        pos = jnp.concatenate([index(positions, c) for c in chunks[:2]])
        cos_part, sin_part = rope_tables(pos)
        lane = jnp.arange(PAIR, dtype=jnp.int32)[None] % HEAD_DIM
        same = seg_keys[:, None] == lane
        mark_key = jnp.where(lane < DOCS, 1.0 - same, (lane < DOCS + 3) * 1.0).astype(LOW)
        mark_query = jnp.where((lane < DOCS) & same[:rows], NEG_FILL, 0.0).astype(LOW)

        normed, kv, _ = keys_values(
            at, tokens, far, gain_low[:1], cos_part, sin_part, blocks_qkv,
            (mark_key, mark_query, far_iu),
        )
        query, far_ia, _ = queries(at, normed, cos_part, sin_part, blocks_qkv, (far_iu, far_il))
        kv_far = trade(kv, "seq", 1)
        far_oa = trade(half_od, "seq", 2)
        far_ib = trade(far_ia, "dp", 1)
        near_ia = trade(far_ia, "seq", 1)
        (cot_far,) = gate((trade(their_cot, "seq", 2),), weight=WEIGHT)
        pairs = width // PAIR
        early = 2
        args = (query, kv, kv_far, mark_query, mark_key)
        o_a, extra_a, done_a = attend(0, early, *args)
        far_oa, far_ib = gate((far_oa, far_ib), (done_a,), weight=10 * WEIGHT)
        far_ob = trade(far_oa, "dp", 1)
        near_oa = trade(far_oa, "seq", 1)
        near_ib = trade(far_ib, "seq", 1)
        o_b, extra_b, done_b = attend(early, pairs - early, *args, late=(done_a, far_oa, near_ia))
        (far_ob,) = gate((far_ob,), (done_b,))
        near_ob = trade(far_ob, "seq", 1)
        blocks_in = (low_in, near_i, far_ia, far_ib, near_ia, near_ib)
        blocks_od = (low_od, near_o, far_oa, far_ob, near_oa, near_ob)

        mixed, mixed_far, dx1, do, keep_rest, send_rest, _ = middle(
            at, valid, tokens, far, cotangent, cot_far, o_a, o_b, gain_low[1:], blocks_in, blocks_od
        )
        got_rest = trade(send_rest, "seq", 1)
        two = pairs // 3
        near_args = (query, kv, kv_far)
        back_args = (mark_key, do, cos_part, sin_part)
        dq0, own0, give0, back0 = attend_back(0, 0, two, *near_args, extra_a, o_a, *back_args)
        *r1, r1_done = first_sums(at, keep_rest, got_rest, late=(back0,))
        got_ra, got_rb = gate(
            (trade(r1[1], "seq", 2), trade(r1[3], "dp", 1)), weight=10 * WEIGHT
        )
        got0 = trade(give0, "seq", 1)
        dq1, own1, give1, back1 = attend_back(
            two, two - early, two, *near_args, extra_b, o_b, *back_args, late=(r1_done,)
        )
        got1 = trade(give1, "seq", 1)
        dq2, own2, give2, back2 = attend_back(
            2 * two, 2 * two - early, pairs - 2 * two, *near_args, extra_b, o_b, *back_args,
            late=(back1, got0),
        )
        got2 = trade(give2, "seq", 1)
        dqkv, normed_t, send_qkv, send_done = qkv_send(
            at, normed, (dq0, dq1, dq2), (own0, own1, own2), (got0, got1, got2),
            cos_part, sin_part, late=(),
        )
        got_qkv = trade(send_qkv, "seq", 1)
        *r2, r2_done = second_sums(at, r1[0], got_ra, r1[2], got_rb, late=(send_done,))
        got_ra, got_rb = trade(r2[1], "dp", 1), trade(r2[3], "seq", 2)
        keep_qkv, _ = qkv_keep(at, normed_t, dqkv, late=(r2_done,))
        *q1, q1_done = first_sums(at, keep_qkv, got_qkv)
        got_qa, got_qb = trade(q1[1], "seq", 2), trade(q1[3], "dp", 1)
        grad, grad_far, grad_done = input_back(
            at, tokens, far, gain_low[:1], dx1, dqkv, blocks_qkv, late=(q1_done,)
        )
        rest, give_rest, r3_done = third_sums(
            at, r2[0], got_ra, r2[2], got_rb, late=(grad_done,)
        )
        got_rest = trade(give_rest, "dp", 2)
        *q2, q2_done = second_sums(at, q1[0], got_qa, q1[2], got_qb, late=(r3_done,))
        got_qa, got_qb = gate(
            (trade(q2[1], "dp", 1), trade(q2[3], "seq", 2)), weight=10 * WEIGHT
        )
        rest, rest_done = add((rest,), (got_rest,), late=(q2_done,))
        got_rest = trade(rest, "dp", far_bits[0])
        qkv, give_qkv, q3_done = third_sums(
            at, q2[0], got_qa, q2[2], got_qb, late=(rest_done,)
        )
        (mixed_far,) = gate((mixed_far,), (q2_done,))
        mixed_far = trade(mixed_far, "seq", 2)
        (grad_far,) = gate((grad_far,), (q2_done,))
        grad_far = trade(grad_far, "seq", 2)
        qkv, qkv_done = add((qkv,), (trade(give_qkv, "dp", 2),))
        got_qkv = trade(qkv, "dp", far_bits[0])
        rest, rest_done = add((rest,), (got_rest,), late=(qkv_done, grad_far, mixed_far))
        for bit in far_bits[1:]:
            rest, rest_done = add((rest,), (trade(rest, "dp", bit),))

        beside, other = trade(rest, "dp", 2), trade(rest, "dp", 1)
        mixed, grad, fill_done = fill(at, mixed, mixed_far, grad, grad_far)
        qkv, qkv_done = add((qkv,), (got_qkv,), late=(rest_done, fill_done, beside, other))
        for bit in far_bits[1:]:
            qkv, qkv_done = add((qkv,), (trade(qkv, "dp", bit),))
        square, _ = squares(at, qkv, w_qkv, rest, w_in, gains)
        qkv_beside, qkv_other = trade(qkv, "dp", 2), trade(qkv, "dp", 1)
        (beside,) = gate((beside,), (square,))
        rest_parts = (rest, beside, other, trade(beside, "dp", 1))
        qkv_parts = (qkv, qkv_beside, qkv_other, trade(qkv_beside, "dp", 1))
        for axis, bit, late in (
            ("seq", 2, ()),
            ("seq", 1, (qkv_beside, qkv_other)),
            ("dp", 2, (rest_parts[3],)),
            ("dp", 1, ()),
        ):
            square, _ = add((square,), (trade(square, axis, bit),), late=late)

        (new_in, first_in, second_in, new_out, first_out, second_out,
         new_down, first_down, second_down, row, _) = update_rest(
            at, square, rest_parts,
            (w_in, m_in, v_in), (w_out, m_out, v_out), (w_down, m_down, v_down), (),
        )
        (new_qkv, first_qkv, second_qkv, new_gains, first_gains, second_gains, norm, _) = (
            update_last(
                at, square, (w_qkv, m_qkv, v_qkv), qkv_parts, row, (gains, m_gains, v_gains)
            )
        )
        return (
            mixed,
            grad,
            norm[0, 0],
            new_qkv, new_out, new_in, new_down, new_gains,
            first_qkv, first_out, first_in, first_down, first_gains,
            second_qkv, second_out, second_in, second_down, second_gains,
        )

    return on_device


def solution(mesh):
    rows, matrix, gain = P("dp", "seq", None), P("seq", None), P(None, "seq")
    weights = (matrix,) * 4 + (gain,)
    return jax.shard_map(
        make(mesh.shape["dp"], mesh.shape["seq"]),
        mesh=mesh,
        in_specs=(rows, rows, P("dp", None), P("dp")) + weights * 3,
        out_specs=(rows, rows, P()) + weights * 3,
        check_vma=False,
    )
```

```python
import functools
import math

import jax
import jax.numpy as jnp
from jax import lax
from jax.experimental import pallas as pl
from jax.experimental.pallas import tpu as pltpu
from jax.sharding import PartitionSpec as P

HEADS = 12
HEAD_DIM = 64
PAIR = 2 * HEAD_DIM
STEP_COUNT = 10
EPS_NORM = 1e-05
ROPE_BASE = 160000.0
NEG_FILL = -1e30
CLIP_LIMIT = 10.0
BETA_FIRST = 0.9
BETA_SECOND = 0.98
EPS_ADAM = 1e-06
STEP_RATES = (0.1, 0.5, 0.1, 0.1, 1.0)
DECAY_RATES = (0.01, 0.01, 0.01, 0.01, 0.0)
DOCS = 5
LOW = jnp.bfloat16
FULL = jnp.float32
SCALE = 1.0 / math.sqrt(HEAD_DIM)
WEIGHT = 20_000_000_000


def doc_positions(segment_ids):
    seq_len = segment_ids.shape[-1]
    places = jnp.arange(seq_len, dtype=jnp.int32)
    first_mark = jnp.ones((1,), jnp.bool_)
    change = jnp.concatenate([first_mark, segment_ids[1:] != segment_ids[:-1]])
    starts = lax.cummax(jnp.where(change, places, 0), axis=0)
    return places - starts


def rope_tables(positions):
    half_dim = HEAD_DIM // 2
    exponents = jnp.arange(half_dim, dtype=jnp.float32) * (2.0 / HEAD_DIM)
    inv_freq = ROPE_BASE ** (-exponents)
    angles = positions.astype(jnp.float32)[:, None] * inv_freq
    cos_part, sin_part = jnp.cos(angles), jnp.sin(angles)
    return (
        jnp.concatenate([cos_part] * 4, axis=1),
        jnp.concatenate([-sin_part, sin_part] * 2, axis=1),
    )


def adam_step(weight, first_old, second_old, gradient, factor, step_rate, decay_rate):
    clipped = gradient * factor
    first_new = BETA_FIRST * first_old + (1.0 - BETA_FIRST) * clipped
    second_new = BETA_SECOND * second_old + (1.0 - BETA_SECOND) * clipped * clipped
    root = second_new * lax.rsqrt(second_new) * (1.0 - BETA_SECOND**STEP_COUNT) ** -0.5
    step = first_new * (step_rate / (1.0 - BETA_FIRST**STEP_COUNT)) / (root + EPS_ADAM)
    return (weight * (1.0 - step_rate * decay_rate) - step, first_new, second_new)


def mul(left, right):
    return lax.dot_general(left, right, (((1,), (0,)), ((), ())), preferred_element_type=FULL)


def mul_t(left, right):
    return lax.dot_general(left, right, (((1,), (1,)), ((), ())), preferred_element_type=FULL)


def normalize(values):
    centered = values - jnp.mean(values, axis=-1, keepdims=True)
    root = lax.rsqrt(jnp.mean(centered * centered, axis=-1, keepdims=True) + EPS_NORM)
    return centered * root, root


def normalize_back(grad, gain, scaled, root):
    t = grad * gain
    back = root * (
        t
        - jnp.mean(t, axis=-1, keepdims=True)
        - scaled * jnp.mean(t * scaled, axis=-1, keepdims=True)
    )
    return back


def turn(values, cos_part, sin_part):
    lane = lax.broadcasted_iota(jnp.int32, values.shape, 1)
    swapped = jnp.where(
        lane % HEAD_DIM < HEAD_DIM // 2,
        pltpu.roll(values, PAIR - HEAD_DIM // 2, 1),
        pltpu.roll(values, HEAD_DIM // 2, 1),
    )
    return values * cos_part + swapped * sin_part


def three_parts(values):
    high = values.astype(LOW).astype(FULL)
    rest = values - high
    mid = rest.astype(LOW).astype(FULL)
    return high, mid, rest - mid


def wait_all(copies):
    for copy in copies:
        copy.wait()


def put(source, target, sem):
    copy = pltpu.make_async_copy(source, target, sem)
    copy.start()
    return copy


PIECES = ((0, None), (1, None), (2, 0), (2, 1), (3, 0), (3, 1))


def join_blocks(at_ref, blocks, whole):
    rows = blocks[0].shape[0]
    for block, (bits, part) in zip(blocks, PIECES):
        start = (at_ref[0] ^ bits) * rows
        size = rows
        if part is not None:
            size = rows // 2
            start += (at_ref[1] ^ part) * size
        whole[pl.ds(pl.multiple_of(start, size), size), :] = block[...]


def join_folded(at_ref, blocks, w_out, w_down):
    rows, width = blocks[0].shape[0], w_out.shape[1]
    short, last = rows // 2, width // 2
    for block, (bits, part) in zip(blocks, PIECES):
        owner = at_ref[0] ^ bits
        base = owner * (rows + short)
        first = 0 if part is None else (at_ref[1] ^ part) * short
        size = rows if part is None else short
        span = pl.ds(pl.multiple_of(owner * rows + first, short), size)
        w_out[span, :] = block[:, :width]
        span = pl.ds(pl.multiple_of(base + first, short), size)
        w_down[span, :] = block[:, width : 2 * width]
        span = pl.ds(pl.multiple_of(base + rows, short), short)
        if part is None:
            for i in range(2):
                w_down[span, i * last : (i + 1) * last] = block[
                    i * short : (i + 1) * short, 2 * width :
                ]
        else:
            lanes = pl.ds(pl.multiple_of((at_ref[1] ^ part) * last, last), last)
            w_down[span, lanes] = block[:, 2 * width :]


def fold(out, w_out, w_down, first):
    rows, width = w_out.shape
    short, last = rows // 2, width // 2
    out[:, first : first + width] = w_out[...].astype(LOW)
    out[:, first + width : first + 2 * width] = w_down[:rows, :].astype(LOW)
    for i in range(2):
        out[i * short : (i + 1) * short, first + 2 * width :] = w_down[
            rows:, i * last : (i + 1) * last
        ].astype(LOW)


def prepare_first_kernel(at_ref, w_ref, gains_ref, half_ref, gains_out, wide, sem):
    short = half_ref.shape[0]
    span = pl.ds(pl.multiple_of(at_ref[1] * short, short), short)
    copy = put(w_ref.at[span, :], wide, sem.at[0])
    gains_out[...] = gains_ref[...].astype(LOW)
    copy.wait()
    half_ref[...] = wide[...].astype(LOW)


def prepare_rest_kernel(at_ref, tokens_ref, in_ref, out_ref, down_ref, qkv_ref, cot_ref,
                        their_tokens, low_in, half_in, low_od, half_od, low_qkv, their_cot,
                        in_wide, out_wide, down_wide, qkv_wide, sem):
    slot = 1 - at_ref[2]
    copies = [
        put(source, target, sem.at[i])
        for i, (source, target) in enumerate((
            (tokens_ref.at[slot], their_tokens), (in_ref, in_wide), (out_ref, out_wide),
            (down_ref, down_wide), (qkv_ref, qkv_wide), (cot_ref.at[slot], their_cot),
        ))
    ]
    short = half_in.shape[0]
    span = pl.ds(pl.multiple_of(at_ref[1] * short, short), short)
    copies[1].wait()
    low_in[...] = in_wide[...].astype(LOW)
    half_in[...] = in_wide[span, :].astype(LOW)
    copies[2].wait()
    copies[3].wait()
    fold(low_od, out_wide, down_wide, 0)
    half_od[...] = low_od[span, :]
    copies[4].wait()
    low_qkv[...] = qkv_wide[...].astype(LOW)
    copies[0].wait()
    copies[5].wait()


def project_kernel(at_ref, tokens_ref, far_ref, gain_ref, cos_ref, sin_ref, w0, w1, w2, w3, w4, w5,
                   normed_ref, query_ref, kv_ref, weight):
    join_blocks(at_ref, (w0, w1, w2, w3, w4, w5), weight)
    rows, width = far_ref.shape
    for part in range(2):
        values = tokens_ref[at_ref[2]] if part == 0 else far_ref[...]
        scaled, _ = normalize(values.astype(FULL))
        normed_ref[pl.ds(part * rows, rows), :] = (scaled * gain_ref[...]).astype(LOW)
    for part in range(2):
        span = pl.ds(part * rows, rows)
        normed = normed_ref[span, :]
        cos_part, sin_part = cos_ref[span, :], sin_ref[span, :]
        for pair in range(2 * width // PAIR):
            lanes = pl.ds(pair * PAIR, PAIR)
            if pair % 2 == 0:
                both = mul(normed, weight[:, pl.ds(pair * PAIR, 2 * PAIR)])
            raw = both[:, (pair % 2) * PAIR : (pair % 2 + 1) * PAIR]
            turned = turn(raw, cos_part, sin_part)
            if pair < width // PAIR:
                query_ref[span, lanes] = (turned * SCALE).astype(LOW)
            else:
                kv_ref[0, span, pl.ds(pair * PAIR - width, PAIR)] = turned.astype(LOW)
        kv_ref[1, span, :] = mul(normed, weight[:, 2 * width :]).astype(LOW)


def head_lanes(head, shape):
    lane = lax.broadcasted_iota(jnp.int32, shape, 1)
    return (lane < HEAD_DIM) if head == 0 else (lane >= HEAD_DIM)


def pick(head, inside, outside):
    return jnp.where(head_lanes(head, inside.shape), inside, outside)


def attend_kernel(query_ref, near_ref, far_ref, mark_query_ref, mark_key_ref, o_ref, extra_ref):
    rows = query_ref.shape[0]
    query = query_ref[...]
    mark_query = mark_query_ref[...]
    parts = [
        (near_ref[0], jnp.transpose(near_ref[1]), mark_key_ref[:rows, :]),
        (far_ref[0], jnp.transpose(far_ref[1]), mark_key_ref[rows:, :]),
    ]
    outs, logs = [], []
    for head in range(2):
        query_head = pick(head, query, mark_query)
        scores = [mul_t(pick(head, key, mark), query_head) for key, _, mark in parts]
        top = jnp.maximum(
            jnp.max(scores[0], axis=0, keepdims=True), jnp.max(scores[1], axis=0, keepdims=True)
        )
        exps = [jnp.exp(score - top) for score in scores]
        total = jnp.sum(exps[0], axis=0, keepdims=True) + jnp.sum(exps[1], axis=0, keepdims=True)
        span = slice(head * HEAD_DIM, (head + 1) * HEAD_DIM)
        out = sum(mul(value_t[span], e.astype(LOW)) for (_, value_t, _), e in zip(parts, exps))
        outs.append(out / total)
        logs.append(top + jnp.log(total))
    o_ref[...] = jnp.transpose(jnp.concatenate(outs)).astype(LOW)
    line = lax.broadcasted_iota(jnp.int32, (PAIR, rows), 0)
    extra = jnp.zeros((PAIR, rows), FULL)
    for head in range(2):
        base = DOCS + (HEAD_DIM if head == 0 else 0)
        for i, piece in enumerate(three_parts(-logs[head])):
            extra = jnp.where(line == base + i, piece, extra)
    extra_ref[...] = jnp.transpose(extra).astype(LOW) + mark_query


def attend_back_kernel(query_ref, near_ref, far_ref, extra_ref, mark_key_ref, o_ref, do_ref,
                       cos_ref, sin_ref, dq_ref, keep_ref, send_ref):
    rows = query_ref.shape[0]
    query, extra, do = query_ref[...], extra_ref[...], do_ref[...]
    inner_all = do.astype(FULL) * o_ref[...].astype(FULL)
    lane = lax.broadcasted_iota(jnp.int32, (rows, PAIR), 1)
    zero = jnp.zeros((rows, PAIR), LOW)
    grads_query = []
    sums = [[None, None], [None, None]]
    keys_t = [jnp.transpose(near_ref[0]), jnp.transpose(far_ref[0])]
    for head in range(2):
        inside = head_lanes(head, (rows, PAIR))
        inner = jnp.sum(jnp.where(inside, inner_all, 0.0), axis=1, keepdims=True)
        base = DOCS + (HEAD_DIM if head == 0 else 0)
        tail = jnp.zeros((rows, PAIR), FULL)
        for i, piece in enumerate(three_parts(-inner)):
            tail = jnp.where(lane == base + i, piece, tail)
        query_head = pick(head, query, extra)
        do_head = pick(head, do, tail.astype(LOW))
        query_only = pick(head, query, zero)
        do_only = pick(head, do, zero)
        span = slice(head * HEAD_DIM, (head + 1) * HEAD_DIM)
        grad_query = 0.0
        for part, ref in enumerate((near_ref, far_ref)):
            mark = mark_key_ref[pl.ds(part * rows, rows), :]
            probs = jnp.exp(mul_t(pick(head, ref[0], mark), query_head))
            grad_probs = mul_t(pick(head, ref[1], mark), do_head)
            grad_scores = (probs * grad_probs).astype(LOW)
            grad_value = mul(probs.astype(LOW), do_only)
            grad_key = mul(grad_scores, query_only)
            grad_query += mul(keys_t[part][span], grad_scores)
            if head == 0:
                sums[part] = [grad_key, grad_value]
            else:
                sums[part] = [sums[part][0] + grad_key, sums[part][1] + grad_value]
        grads_query.append(grad_query)
    turned = turn(
        jnp.transpose(jnp.concatenate(grads_query)) * SCALE, cos_ref[...], -sin_ref[...]
    )
    dq_ref[...] = turned.astype(LOW)
    for i in range(2):
        keep_ref[i] = sums[0][i].astype(LOW)
        send_ref[i] = sums[1][i].astype(LOW)


def middle_kernel(at_ref, live_ref, tokens_ref, far_ref, cot_ref, cot_far_ref, oa_ref, ob_ref,
                  gain_ref, i0, i1, i2, i3, i4, i5, d0, d1, d2, d3, d4, d5,
                  mixed_ref, mixed_far_ref, dx1_ref, do_ref, keep_ref, send_ref,
                  w_out, w_in, w_down, o_all, o_t, a2_t, h_t, dm_all, duw_all, db_all,
                  mixed, dx1_all, do_all, keep, send, out_sem):
    place, slot = at_ref[0], at_ref[2]
    live = live_ref[slot].astype(FULL)
    join_folded(at_ref, (d0, d1, d2, d3, d4, d5), w_out, w_down)
    join_blocks(at_ref, (i0, i1, i2, i3, i4, i5), w_in)
    rows, width = far_ref.shape
    share = width // 4
    short, units = share // 2, w_down.shape[0]
    gain = gain_ref[...]
    o_all[:, : oa_ref.shape[1]] = oa_ref[...]
    o_all[:, oa_ref.shape[1] :] = ob_ref[...]
    copies = []
    for part in range(2):
        span = pl.ds(part * rows, rows)
        o = o_all[span, :]
        values = tokens_ref[slot] if part == 0 else far_ref[...]
        x1 = values.astype(FULL) + live * mul(o, w_out[...])
        scaled, root = normalize(x1)
        a2 = (scaled * gain).astype(LOW)
        u = mul(a2, w_in[:, :units])
        w = mul(a2, w_in[:, units:])
        phi = 0.5 * (1.0 + lax.erf(u * math.sqrt(0.5)))
        gelu = u * phi
        h = (gelu * w).astype(LOW)
        mixed[span, :] = (x1 + live * mul(h, w_down[...])).astype(LOW)
        target = mixed_ref.at[slot] if part == 0 else mixed_far_ref
        copies.append(put(mixed.at[span, :], target, out_sem.at[len(copies)]))
        cot = (cot_ref[slot] if part == 0 else cot_far_ref[...]).astype(FULL)
        dm = (live * cot).astype(LOW)
        dh = mul_t(dm, w_down[...])
        slope = phi + u * (jnp.exp(-0.5 * u * u) * (1.0 / math.sqrt(2.0 * math.pi)))
        duw_all[span, :units] = (dh * w * slope).astype(LOW)
        duw_all[span, units:] = (dh * gelu).astype(LOW)
        da2 = mul_t(duw_all[span, :], w_in[...])
        dx1 = cot + normalize_back(da2, gain, scaled, root)
        dx1_all[span, :] = dx1
        copies.append(put(dx1_all.at[span, :], dx1_ref.at[span, :], out_sem.at[len(copies)]))
        db = (live * dx1).astype(LOW)
        do_all[span, :] = mul_t(db, w_out[...]).astype(LOW)
        copies.append(put(do_all.at[span, :], do_ref.at[span, :], out_sem.at[len(copies)]))
        db_all[span, :] = db
        dm_all[span, :] = dm
        o_t[:, span] = jnp.transpose(o)
        a2_t[:, span] = jnp.transpose(a2)
        h_t[:, span] = jnp.transpose(h)
    dm, duw, db = dm_all[...], duw_all[...], db_all[...]
    for j, out, target in ((1, send, send_ref), (3, send, send_ref), (0, keep, keep_ref), (2, keep, keep_ref)):
        span = pl.ds(pl.multiple_of((place ^ j) * share, share), share)
        base = (place ^ j) * (share + short)
        down = pl.ds(pl.multiple_of(base, short), share)
        down_last = pl.ds(pl.multiple_of(base + share, short), short)
        at = 2 * units
        out[j // 2, :, :at] = mul(a2_t[span, :], duw).astype(LOW)
        out[j // 2, :, at : at + width] = mul(o_t[span, :], db).astype(LOW)
        at += width
        out[j // 2, :, at : at + width] = mul(h_t[down, :], dm).astype(LOW)
        at += width
        last = mul(h_t[down_last, :], dm).astype(LOW)
        out[j // 2, :short, at:] = last[:, : width // 2]
        out[j // 2, short:, at:] = last[:, width // 2 :]
        copies.append(put(out.at[j // 2], target.at[j // 2], out_sem.at[len(copies)]))
    wait_all(copies)


def send_kernel(count, at_ref, *refs):
    normed_ref = refs[0]
    dqs, owns, gots = (refs[1 + i * count : 1 + (i + 1) * count] for i in range(3))
    (cos_ref, sin_ref, dqkv_ref, normed_t_ref, send_ref,
     dqkv, normed_t, send, sem) = refs[1 + 3 * count :]
    width = normed_ref.shape[1]
    part_width = width // count
    normed_t[...] = jnp.transpose(normed_ref[...])
    copies = [put(normed_t, normed_t_ref, sem.at[0])]
    cos_part, sin_part = cos_ref[...], -sin_ref[...]
    for part, (dq, own, got) in enumerate(zip(dqs, owns, gots)):
        base = part * part_width
        dqkv[:, pl.ds(base, part_width)] = dq[...]
        dqkv[:, pl.ds(2 * width + base, part_width)] = (
            own[1].astype(FULL) + got[1].astype(FULL)
        ).astype(LOW)
        for pair in range(part_width // PAIR):
            lanes = pl.ds(pair * PAIR, PAIR)
            raw = own[0, :, lanes].astype(FULL) + got[0, :, lanes].astype(FULL)
            dqkv[:, pl.ds(width + base + pair * PAIR, PAIR)] = turn(raw, cos_part, sin_part).astype(
                LOW
            )
    copies.append(put(dqkv, dqkv_ref, sem.at[1]))
    right = dqkv[...]
    share = send.shape[1]
    for j in (1, 3):
        start = pl.multiple_of((at_ref[0] ^ j) * share, share)
        send[j // 2] = mul(normed_t[pl.ds(start, share), :], right).astype(LOW)
        copies.append(put(send.at[j // 2], send_ref.at[j // 2], sem.at[len(copies)]))
    wait_all(copies)


def keep_kernel(at_ref, normed_t_ref, dqkv_ref, keep_ref, keep, sem):
    right = dqkv_ref[...]
    share = keep.shape[1]
    copies = []
    for j in (0, 2):
        start = pl.multiple_of((at_ref[0] ^ j) * share, share)
        keep[j // 2] = mul(normed_t_ref[pl.ds(start, share), :], right).astype(LOW)
        copies.append(put(keep.at[j // 2], keep_ref.at[j // 2], sem.at[len(copies)]))
    wait_all(copies)


def input_kernel(at_ref, tokens_ref, far_ref, gain_ref, dx1_ref, dqkv_ref, w0, w1, w2, w3, w4, w5,
                 grad_ref, grad_far_ref, weight, grad_own, out_sem):
    join_blocks(at_ref, (w0, w1, w2, w3, w4, w5), weight)
    rows = far_ref.shape[0]
    gain = gain_ref[...]
    for part in (1, 0):
        span = pl.ds(part * rows, rows)
        values = tokens_ref[at_ref[2]] if part == 0 else far_ref[...]
        scaled, root = normalize(values.astype(FULL))
        back = normalize_back(mul_t(dqkv_ref[span, :], weight[...]), gain, scaled, root)
        grad = dx1_ref[span, :] + back
        if part == 1:
            grad_far_ref[...] = grad.astype(LOW)
        else:
            grad_own[...] = grad
    put(grad_own, grad_ref.at[at_ref[2]], out_sem.at[0]).wait()


def shaped(*shape, kind=LOW):
    return jax.ShapeDtypeStruct(shape, kind)


IN_SMEM = pl.BlockSpec(memory_space=pltpu.SMEM)
IN_VMEM = pl.BlockSpec(memory_space=pltpu.VMEM)
IN_ANY = pl.BlockSpec(memory_space=pl.ANY)


def params(mebibytes):
    return pltpu.CompilerParams(vmem_limit_bytes=int(mebibytes * 1024 * 1024))


def call(kernel, args, in_specs, out_shape, out_specs, late=(), **options):
    if not isinstance(out_shape, tuple):
        out_shape, out_specs = (out_shape,), (out_specs,)
    count, skip, outs = len(args), len(late), len(out_shape)

    def body(*refs):
        outs_at = count + skip
        return kernel(*refs[:count], *refs[outs_at : outs_at + outs], *refs[outs_at + outs + 1 :])

    return pl.pallas_call(
        body,
        in_specs=list(in_specs) + [IN_ANY] * skip,
        out_shape=out_shape + (shaped(8, 128, kind=FULL),),
        out_specs=out_specs + (IN_ANY,),
        **options,
    )(*args, *late)


def gate(values, late=(), weight=0):
    hint = {}
    if weight:
        hint["cost_estimate"] = pl.CostEstimate(
            flops=weight, transcendentals=0, bytes_accessed=0
        )
    return call(
        lambda *refs: None,
        values,
        late=late,
        out_shape=tuple(jax.ShapeDtypeStruct(v.shape, v.dtype) for v in values),
        in_specs=[IN_ANY] * len(values),
        out_specs=(IN_ANY,) * len(values),
        input_output_aliases={i: i for i in range(len(values))},
        compiler_params=params(1),
        name="gate",
        **hint,
    )[: len(values)]


def in_hbm(value):
    return pltpu.with_memory_space_constraint(value, pltpu.HBM)


def prepare_first(at, weight, gains):
    rows, width = weight.shape
    return call(
        prepare_first_kernel,
        (at, in_hbm(weight), gains),
        out_shape=(shaped(rows // 2, width), shaped(*gains.shape)),
        in_specs=[IN_SMEM, IN_ANY, IN_VMEM],
        out_specs=(IN_VMEM,) * 2,
        scratch_shapes=[pltpu.VMEM((rows // 2, width), FULL), pltpu.SemaphoreType.DMA((1,))],
        compiler_params=params(6),
        name="prepare_first",
    )


def prepare_rest(at, tokens, w_in, w_out, w_down, w_qkv, cotangent, late):
    rows, width = w_out.shape
    folded = 2 * width + width // 2
    return call(
        prepare_rest_kernel,
        (at, *[in_hbm(v) for v in (tokens, w_in, w_out, w_down, w_qkv, cotangent)]),
        late=late,
        out_shape=(
            shaped(*tokens.shape[1:]),
            shaped(*w_in.shape),
            shaped(rows // 2, w_in.shape[1]),
            shaped(rows, folded),
            shaped(rows // 2, folded),
            shaped(*w_qkv.shape),
            shaped(*cotangent.shape[1:]),
        ),
        in_specs=[IN_SMEM] + [IN_ANY] * 6,
        out_specs=(IN_VMEM,) * 7,
        scratch_shapes=[
            pltpu.VMEM(v.shape, FULL) for v in (w_in, w_out, w_down, w_qkv)
        ] + [pltpu.SemaphoreType.DMA((6,))],
        compiler_params=params(18),
        name="prepare_rest",
    )


def project(at, tokens, far, gain, cos_part, sin_part, blocks, late):
    rows, width = 2 * far.shape[0], far.shape[1]
    return call(
        project_kernel,
        (at, tokens, far, gain, cos_part, sin_part, *blocks),
        late=late,
        out_shape=(shaped(rows, width), shaped(rows, width), shaped(2, rows, width)),
        in_specs=[IN_SMEM] + [IN_VMEM] * 11,
        out_specs=(IN_VMEM,) * 3,
        scratch_shapes=[pltpu.VMEM((width, 3 * width), LOW)],
        compiler_params=params(18),
        name="project",
    )


def attend(first, count, query, near, far, mark_query, mark_key, late=()):
    rows = query.shape[0]
    row_spec = pl.BlockSpec((rows, PAIR), lambda i: (0, i + first))
    kv_spec = pl.BlockSpec((2, rows, PAIR), lambda i: (0, 0, i + first))
    out_spec = pl.BlockSpec((rows, PAIR), lambda i: (0, i))
    return call(
        attend_kernel,
        (query, near, far, mark_query, mark_key),
        late=late,
        grid=(count,),
        out_shape=(shaped(rows, count * PAIR), shaped(rows, count * PAIR)),
        in_specs=[
            row_spec,
            kv_spec,
            kv_spec,
            pl.BlockSpec((rows, PAIR), lambda i: (0, 0)),
            pl.BlockSpec((2 * rows, PAIR), lambda i: (0, 0)),
        ],
        out_specs=(out_spec, out_spec),
        compiler_params=params(16),
        name="attend",
    )


def attend_back(
    first, first_o, count, query, near, far, extra, o, mark_key, do, cos_part, sin_part, late=()
):
    rows = query.shape[0]
    row_spec = pl.BlockSpec((rows, PAIR), lambda i: (0, i + first))
    o_spec = pl.BlockSpec((rows, PAIR), lambda i: (0, i + first_o))
    kv_spec = pl.BlockSpec((2, rows, PAIR), lambda i: (0, 0, i + first))
    fixed = pl.BlockSpec((rows, PAIR), lambda i: (0, 0))
    out_row = pl.BlockSpec((rows, PAIR), lambda i: (0, i))
    out_kv = pl.BlockSpec((2, rows, PAIR), lambda i: (0, 0, i))
    return call(
        attend_back_kernel,
        (query, near, far, extra, mark_key, o, do, cos_part, sin_part),
        late=late,
        grid=(count,),
        out_shape=(
            shaped(rows, count * PAIR),
            shaped(2, rows, count * PAIR),
            shaped(2, rows, count * PAIR),
        ),
        in_specs=[
            row_spec,
            kv_spec,
            kv_spec,
            o_spec,
            pl.BlockSpec((2 * rows, PAIR), lambda i: (0, 0)),
            o_spec,
            row_spec,
            fixed,
            fixed,
        ],
        out_specs=(out_row, out_kv, out_kv),
        compiler_params=params(20),
        name="attend_back",
    )


def middle(at, live, tokens, far, cot, cot_far, o_a, o_b, gain, blocks_in, blocks_od):
    half, width = far.shape
    rows, share = 2 * half, width // 4
    units = blocks_in[0].shape[1] // 2
    total = 2 * units + blocks_od[0].shape[1]
    assert units == 4 * (share + share // 2)
    low = lambda *shape: pltpu.VMEM(shape, LOW)
    return call(
        middle_kernel,
        (at, live, tokens, far, cot, cot_far, o_a, o_b, gain, *blocks_in, *blocks_od),
        out_shape=(
            shaped(2, half, width),
            shaped(half, width),
            shaped(rows, width, kind=FULL),
            shaped(rows, width),
            shaped(2, share, total),
            shaped(2, share, total),
        ),
        in_specs=[IN_SMEM] * 2 + [IN_VMEM] * 19,
        out_specs=(IN_ANY,) * 6,
        scratch_shapes=[
            low(width, width),
            low(width, 2 * units),
            low(units, width),
            low(rows, width),
            low(width, rows),
            low(width, rows),
            low(units, rows),
            low(rows, width),
            low(rows, 2 * units),
            low(rows, width),
            low(rows, width),
            pltpu.VMEM((rows, width), FULL),
            low(rows, width),
            low(2, share, total),
            low(2, share, total),
            pltpu.SemaphoreType.DMA((10,)),
        ],
        compiler_params=params(44),
        name="middle",
    )


def qkv_send(at, normed, dq, own, got, cos_part, sin_part, late):
    rows, width = normed.shape
    share = width // 4
    return call(
        functools.partial(send_kernel, len(dq)),
        (at, normed, *dq, *own, *got, cos_part, sin_part),
        late=late,
        out_shape=(
            shaped(rows, 3 * width),
            shaped(width, rows),
            shaped(2, share, 3 * width),
        ),
        in_specs=[IN_SMEM] + [IN_VMEM] * (3 + 3 * len(dq)),
        out_specs=(IN_ANY,) * 3,
        scratch_shapes=[
            pltpu.VMEM((rows, 3 * width), LOW),
            pltpu.VMEM((width, rows), LOW),
            pltpu.VMEM((2, share, 3 * width), LOW),
            pltpu.SemaphoreType.DMA((4,)),
        ],
        compiler_params=params(20),
        name="qkv_send",
    )


def qkv_keep(at, normed_t, dqkv, late):
    width, rows = normed_t.shape
    share = width // 4
    return call(
        keep_kernel,
        (at, normed_t, dqkv),
        late=late,
        out_shape=shaped(2, share, 3 * width),
        in_specs=[IN_SMEM] + [IN_VMEM] * 2,
        out_specs=IN_ANY,
        scratch_shapes=[
            pltpu.VMEM((2, share, 3 * width), LOW),
            pltpu.SemaphoreType.DMA((2,)),
        ],
        compiler_params=params(16),
        name="qkv_keep",
    )


def input_back(at, tokens, far, gain, dx1, dqkv, blocks, late):
    half, width = far.shape
    return call(
        input_kernel,
        (at, tokens, far, gain, dx1, dqkv, *blocks),
        late=late,
        out_shape=(shaped(2, half, width, kind=FULL), shaped(half, width)),
        in_specs=[IN_SMEM] + [IN_VMEM] * 11,
        out_specs=(IN_ANY, IN_VMEM),
        scratch_shapes=[
            pltpu.VMEM((width, 3 * width), LOW),
            pltpu.VMEM((half, width), FULL),
            pltpu.SemaphoreType.DMA((1,)),
        ],
        compiler_params=params(20),
        name="input_back",
    )


def first_sums_kernel(at_ref, keep, got, own_a, far_a, mine_b, give_b):
    cut, short = far_a.shape[0], give_b.shape[1]

    def add(block, start, size):
        span = pl.ds(start, size)
        return (keep[block, span, :].astype(FULL) + got[block, span, :].astype(FULL)).astype(LOW)

    far_a[...] = add(1, 0, cut)
    for block in range(2):
        give_b[block] = add(block, pl.multiple_of(cut + (1 - at_ref[1]) * short, short), short)
        mine_b[block] = add(block, pl.multiple_of(cut + at_ref[1] * short, short), short)
    own_a[...] = add(0, 0, cut)


def first_sums(at, keep, got, late=()):
    _, rows, width = keep.shape
    cut, short = rows // 2, rows // 4
    return call(
        first_sums_kernel,
        (at, keep, got),
        late=late,
        out_shape=(shaped(cut, width),) * 2 + (shaped(2, short, width),) * 2,
        in_specs=[IN_SMEM] + [IN_VMEM] * 2,
        out_specs=(IN_VMEM,) * 4,
        compiler_params=params(20),
        name="first_sums",
    )


def second_sums_kernel(at_ref, own_a, got_a, mine_b, got_b, mine_a, give_a, near_b, far_b):
    short = mine_a.shape[0]
    for start, out in ((1 - at_ref[1], give_a), (at_ref[1], mine_a)):
        span = pl.ds(pl.multiple_of(start * short, short), short)
        out[...] = (own_a[span, :].astype(FULL) + got_a[span, :].astype(FULL)).astype(LOW)
    for block, out in ((1, far_b), (0, near_b)):
        out[...] = (mine_b[block].astype(FULL) + got_b[block].astype(FULL)).astype(LOW)


def second_sums(at, own_a, got_a, mine_b, got_b, late=()):
    _, short, width = mine_b.shape
    return call(
        second_sums_kernel,
        (at, own_a, got_a, mine_b, got_b),
        late=late,
        out_shape=(shaped(short, width),) * 4,
        in_specs=[IN_SMEM] + [IN_VMEM] * 4,
        out_specs=(IN_VMEM,) * 4,
        compiler_params=params(12),
        name="second_sums",
    )


def third_sums_kernel(at_ref, mine_a, got_a, near_b, got_b, keep, give):
    upper = mine_a[...].astype(FULL) + got_a[...].astype(FULL)
    lower = near_b[...].astype(FULL) + got_b[...].astype(FULL)
    keep[...] = jnp.where(at_ref[4] == 0, upper, lower).astype(LOW)
    give[...] = jnp.where(at_ref[4] == 0, lower, upper).astype(LOW)


def third_sums(at, mine_a, got_a, near_b, got_b, late=()):
    return call(
        third_sums_kernel,
        (at, mine_a, got_a, near_b, got_b),
        late=late,
        out_shape=(shaped(*mine_a.shape),) * 2,
        in_specs=[IN_SMEM] + [IN_VMEM] * 4,
        out_specs=(IN_VMEM,) * 2,
        compiler_params=params(12),
        name="third_sums",
    )


def squares_kernel(at_ref, qkv, w_qkv, rest, w_in, gains, out):
    inner = w_in.shape[1]
    total = jnp.sum(jnp.square(rest[:, inner:].astype(FULL)), keepdims=True)
    rows = qkv.shape[0]
    shape = (rows, gains.shape[1])
    offset = lax.broadcasted_iota(jnp.int32, shape, 1) - lax.broadcasted_iota(jnp.int32, shape, 0)
    for i, (piece, weight) in enumerate(((qkv, w_qkv), (rest, w_in))):
        start = at_ref[3]
        span = pl.ds(pl.multiple_of(start, 8), rows)
        values = piece[:, : weight.shape[1]].astype(FULL)
        sums = jnp.sum(weight[span, :].astype(LOW).astype(FULL) * values, axis=1, keepdims=True)
        gain = gains[i : i + 1, :].astype(LOW).astype(FULL)
        gain = jnp.sum(jnp.where(offset == start, gain, 0.0), axis=1, keepdims=True)
        total += jnp.sum(jnp.square(values), keepdims=True)
        total += jnp.sum(jnp.square(sums / gain), keepdims=True)
    out[...] = jnp.broadcast_to(total, out.shape)


def squares(*args):
    return call(
        squares_kernel,
        args,
        out_shape=shaped(8, 128, kind=FULL),
        in_specs=[IN_SMEM] + [IN_VMEM] * (len(args) - 1),
        out_specs=IN_VMEM,
        compiler_params=params(10),
        name="squares",
    )


def add_kernel(count, *refs):
    for i in range(count):
        out = refs[2 * count + i]
        out[...] = (refs[i][...].astype(FULL) + refs[count + i][...].astype(FULL)).astype(out.dtype)


def add(first, second, late=()):
    count = len(first)
    return call(
        functools.partial(add_kernel, count),
        (*first, *second),
        late=late,
        out_shape=tuple(jax.ShapeDtypeStruct(v.shape, v.dtype) for v in first),
        in_specs=[IN_VMEM] * (2 * count),
        out_specs=(IN_VMEM,) * count,
        compiler_params=params(8),
        name="add",
    )


def fill_kernel(at_ref, mixed_far, grad_far, mixed_in, grad_in, mixed, grad, wide, sem):
    first = put(mixed_far, mixed.at[1 - at_ref[2]], sem.at[0])
    wide[...] = grad_far[...].astype(FULL)
    put(wide, grad.at[1 - at_ref[2]], sem.at[1]).wait()
    first.wait()


def fill(at, mixed, mixed_far, grad, grad_far):
    return call(
        fill_kernel,
        (at, mixed_far, grad_far, mixed, grad),
        out_shape=(shaped(*mixed.shape), shaped(*grad.shape, kind=FULL)),
        in_specs=[IN_SMEM, IN_VMEM, IN_VMEM, IN_ANY, IN_ANY],
        out_specs=(IN_ANY,) * 2,
        input_output_aliases={3: 0, 4: 1},
        scratch_shapes=[pltpu.VMEM(grad_far.shape, FULL), pltpu.SemaphoreType.DMA((2,))],
        compiler_params=params(4),
        name="fill",
    )


def clip_factor(square_ref):
    norm = jnp.sqrt(square_ref[:1, :1])
    return jnp.minimum(1.0, CLIP_LIMIT / (norm + 1e-06))


def quarters(at_ref, parts):
    own, beside, other, other_beside = parts
    for i in range(4):
        same = at_ref[4] == i // 2
        near = jnp.where(same, own[...], beside[...])
        far = jnp.where(same, other[...], other_beside[...])
        yield jnp.where(at_ref[1] == i % 2, near, far).astype(FULL)


def gain_row(weight, gradient, start, shape):
    sums = jnp.sum(weight.astype(LOW).astype(FULL) * gradient, axis=1, keepdims=True)
    shape = (weight.shape[0], shape[1])
    offset = lax.broadcasted_iota(jnp.int32, shape, 1) - lax.broadcasted_iota(jnp.int32, shape, 0)
    return jnp.sum(jnp.where(offset == start, sums, 0.0), axis=0, keepdims=True)


class Update:
    def __init__(self, number, sources, news, targets, sem):
        self.number, self.sources, self.news, self.targets = number, sources, news, targets
        self.sem, self.out = sem, []

    def step(self, span, gradient, factor):
        weight = self.sources[0][span]
        results = adam_step(
            weight, self.sources[1][span], self.sources[2][span], gradient, factor,
            STEP_RATES[self.number], DECAY_RATES[self.number],
        )
        for result, new, target in zip(results, self.news, self.targets):
            new[span] = result
            self.out.append(put(new.at[span], target.at[span], self.sem.at[len(self.out)]))
        return weight


def update_rest_kernel(at_ref, square_ref, *refs):
    parts, refs = refs[:4], refs[4:]
    sources, targets, row_ref, news, sem = refs[:9], refs[9:18], refs[18], refs[19:28], refs[28]
    inner, out, down = (
        Update(number, *(group[3 * k : 3 * k + 3] for group in (sources, news, targets)), sem.at[k])
        for k, number in enumerate((2, 1, 3))
    )
    factor = clip_factor(square_ref)
    rows, width = sources[3].shape
    lanes = sources[0].shape[1]
    short, last = rows // 4, width // 2
    row = jnp.zeros(row_ref.shape, FULL)
    for i, gradient in enumerate(quarters(at_ref, parts)):
        span = (slice(i * short, (i + 1) * short), slice(None))
        part = gradient[:, :lanes]
        row += gain_row(inner.step(span, part, factor), part, i * short, row_ref.shape)
        out.step(span, gradient[:, lanes : lanes + width], factor)
        down.step(span, gradient[:, lanes + width : lanes + 2 * width], factor)
        start = rows + (i % 2) * short
        span = (slice(start, start + short), slice((i // 2) * last, (i // 2 + 1) * last))
        down.step(span, gradient[:, lanes + 2 * width :], factor)
    row_ref[...] = row
    wait_all(inner.out + out.out + down.out)


def update_rest(at, square, parts, inner, out, down, late):
    like = [jax.ShapeDtypeStruct(v.shape, FULL) for v in (*inner, *out, *down)]
    return call(
        update_rest_kernel,
        (at, square, *parts, *inner, *out, *down),
        late=late,
        out_shape=(*like, shaped(1, inner[0].shape[0], kind=FULL)),
        in_specs=[IN_SMEM] + [IN_VMEM] * 14,
        out_specs=(IN_ANY,) * 9 + (IN_VMEM,),
        scratch_shapes=[pltpu.VMEM(v.shape, FULL) for v in like]
        + [pltpu.SemaphoreType.DMA((3, 24))],
        compiler_params=params(28),
        name="update_rest",
    )


def update_last_kernel(at_ref, square_ref, row_ref, g_w, g_m, g_v, *refs):
    parts, refs = refs[:4], refs[4:]
    sources, targets = refs[:3], refs[3:6]
    g_w_out, g_m_out, g_v_out, norm_out = refs[6:10]
    news, sem = refs[10:13], refs[13]
    qkv = Update(0, sources, news, targets, sem)
    factor = clip_factor(square_ref)
    norm_out[...] = jnp.sqrt(square_ref[...])
    short = sources[0].shape[0] // 4
    row = jnp.zeros(row_ref.shape, FULL)
    for i, gradient in enumerate(quarters(at_ref, parts)):
        span = (slice(i * short, (i + 1) * short), slice(None))
        row += gain_row(qkv.step(span, gradient, factor), gradient, i * short, row_ref.shape)
    for i, values in enumerate((row, row_ref[...])):
        line = slice(i, i + 1)
        gradient = values / g_w[line, :].astype(LOW).astype(FULL)
        g_w_out[line, :], g_m_out[line, :], g_v_out[line, :] = adam_step(
            g_w[line, :], g_m[line, :], g_v[line, :], gradient, factor,
            STEP_RATES[4], DECAY_RATES[4],
        )
    wait_all(qkv.out)


def update_last(at, square, qkv, qkv_parts, row, gains):
    like = [jax.ShapeDtypeStruct(v.shape, FULL) for v in qkv]
    return call(
        update_last_kernel,
        (at, square, row, *gains, *qkv_parts, *qkv),
        out_shape=(
            *like,
            *[jax.ShapeDtypeStruct(v.shape, FULL) for v in gains],
            jax.ShapeDtypeStruct(square.shape, FULL),
        ),
        in_specs=[IN_SMEM] + [IN_VMEM] * 12,
        out_specs=(IN_ANY,) * 3 + (IN_VMEM,) * 4,
        scratch_shapes=[pltpu.VMEM(v.shape, FULL) for v in like]
        + [pltpu.SemaphoreType.DMA((12,))],
        compiler_params=params(18),
        name="update_last",
    )


def low_sum(*values):
    return sum(value.astype(FULL) for value in values).astype(LOW)


def index(value, i):
    return lax.dynamic_index_in_dim(value, i, 0, keepdims=False)


def make(dp_count, seq_count):
    assert seq_count == 4 and dp_count >= 8 and dp_count & (dp_count - 1) == 0
    far_bits = [1 << i for i in range(2, dp_count.bit_length() - 1)]

    def trade(value, axis, bit):
        size = seq_count if axis == "seq" else dp_count
        return lax.ppermute(value, axis, [(i, i ^ bit) for i in range(size)])

    def on_device(
        tokens, cotangent, segments, valid,
        w_qkv, w_out, w_in, w_down, gains,
        m_qkv, m_out, m_in, m_down, m_gains,
        v_qkv, v_out, v_in, v_down, v_gains,
    ):
        place = lax.axis_index("seq")
        group = lax.axis_index("dp")
        slot = place >> 1
        half = group & 1
        local_len, width = tokens.shape[1:]
        rows = 2 * local_len
        share = w_qkv.shape[0]
        side = (group >> 1) & 1
        quarter = share // 4
        at = jnp.stack([place, half, slot, side * 2 * quarter + half * quarter, side])

        half_qkv, low_gains, begun = prepare_first(at, w_qkv, gains)
        (far_qa,) = gate((trade(half_qkv, "seq", 2),), weight=10 * WEIGHT)
        (gain_far,) = gate((trade(low_gains, "seq", 2),), weight=20 * WEIGHT)
        their_tokens, low_in, half_in, low_od, half_od, low_qkv, their_cot, _ = prepare_rest(
            at, tokens, w_in, w_out, w_down, w_qkv, cotangent, (begun,)
        )
        near_q = trade(low_qkv, "seq", 1)
        far = trade(their_tokens, "seq", 2)
        far_qb = trade(far_qa, "dp", 1)
        near_qa = trade(far_qa, "seq", 1)
        near_qb = trade(far_qb, "seq", 1)
        (gain_far,) = gate((gain_far,), (far_qb,))
        gain_near = trade(jnp.stack([low_gains, gain_far]), "seq", 1)
        gain_stack = jnp.stack([low_gains, gain_near[0], gain_far, gain_near[1]])
        gain_low = jnp.concatenate(
            [index(gain_stack, b ^ place) for b in range(4)], axis=1
        ).astype(FULL)
        blocks_qkv = (low_qkv, near_q, far_qa, far_qb, near_qa, near_qb)
        low_in, low_od, half_in = gate((low_in, low_od, half_in), (far_qa,))
        near_i = trade(low_in, "seq", 1)
        near_o = trade(low_od, "seq", 1)
        (far_ia,) = gate((trade(half_in, "seq", 2),), weight=10 * WEIGHT)

        seg = index(segments, slot)
        positions = doc_positions(seg).reshape(4, local_len)
        seg = seg.reshape(4, local_len)
        chunks = [place, place ^ 2, place ^ 1, place ^ 3]
        seg_keys = jnp.concatenate([index(seg, c) for c in chunks])
        pos = jnp.concatenate([index(positions, c) for c in chunks[:2]])
        cos_part, sin_part = rope_tables(pos)
        lane = jnp.arange(PAIR, dtype=jnp.int32)[None] % HEAD_DIM
        same = seg_keys[:, None] == lane
        mark_key = jnp.where(lane < DOCS, 1.0 - same, (lane < DOCS + 3) * 1.0).astype(LOW)
        mark_query = jnp.where((lane < DOCS) & same[:rows], NEG_FILL, 0.0).astype(LOW)

        normed, query, kv, _ = project(
            at, tokens, far, gain_low[:1], cos_part, sin_part, blocks_qkv,
            (mark_key, mark_query),
        )
        kv_far = trade(kv, "seq", 1)
        far_oa = trade(half_od, "seq", 2)
        far_ib = trade(far_ia, "dp", 1)
        near_ia = trade(far_ia, "seq", 1)
        (cot_far,) = gate((trade(their_cot, "seq", 2),), weight=WEIGHT)
        pairs = width // PAIR
        early = 2
        args = (query, kv, kv_far, mark_query, mark_key)
        o_a, extra_a, done_a = attend(0, early, *args, late=(far_ia,))
        far_oa, far_ib = gate((far_oa, far_ib), (done_a,), weight=10 * WEIGHT)
        far_ob = trade(far_oa, "dp", 1)
        near_oa = trade(far_oa, "seq", 1)
        near_ib = trade(far_ib, "seq", 1)
        o_b, extra_b, done_b = attend(early, pairs - early, *args, late=(done_a, far_oa, near_ia))
        (far_ob,) = gate((far_ob,), (done_b,))
        near_ob = trade(far_ob, "seq", 1)
        blocks_in = (low_in, near_i, far_ia, far_ib, near_ia, near_ib)
        blocks_od = (low_od, near_o, far_oa, far_ob, near_oa, near_ob)

        mixed, mixed_far, dx1, do, keep_rest, send_rest, _ = middle(
            at, valid, tokens, far, cotangent, cot_far, o_a, o_b, gain_low[1:], blocks_in, blocks_od
        )
        got_rest = trade(send_rest, "seq", 1)
        two = pairs // 3
        near_args = (query, kv, kv_far)
        back_args = (mark_key, do, cos_part, sin_part)
        dq0, own0, give0, back0 = attend_back(0, 0, two, *near_args, extra_a, o_a, *back_args)
        *r1, r1_done = first_sums(at, keep_rest, got_rest, late=(back0,))
        got_ra, got_rb = gate(
            (trade(r1[1], "seq", 2), trade(r1[3], "dp", 1)), weight=10 * WEIGHT
        )
        got0 = trade(give0, "seq", 1)
        dq1, own1, give1, back1 = attend_back(
            two, two - early, two, *near_args, extra_b, o_b, *back_args, late=(r1_done,)
        )
        got1 = trade(give1, "seq", 1)
        dq2, own2, give2, back2 = attend_back(
            2 * two, 2 * two - early, pairs - 2 * two, *near_args, extra_b, o_b, *back_args,
            late=(back1, got0),
        )
        got2 = trade(give2, "seq", 1)
        dqkv, normed_t, send_qkv, send_done = qkv_send(
            at, normed, (dq0, dq1, dq2), (own0, own1, own2), (got0, got1, got2),
            cos_part, sin_part, late=(),
        )
        got_qkv = trade(send_qkv, "seq", 1)
        *r2, r2_done = second_sums(at, r1[0], got_ra, r1[2], got_rb, late=(send_done,))
        got_ra, got_rb = trade(r2[1], "dp", 1), trade(r2[3], "seq", 2)
        keep_qkv, _ = qkv_keep(at, normed_t, dqkv, late=(r2_done,))
        *q1, q1_done = first_sums(at, keep_qkv, got_qkv)
        got_qa, got_qb = trade(q1[1], "seq", 2), trade(q1[3], "dp", 1)
        grad, grad_far, grad_done = input_back(
            at, tokens, far, gain_low[:1], dx1, dqkv, blocks_qkv, late=(q1_done,)
        )
        rest, give_rest, r3_done = third_sums(
            at, r2[0], got_ra, r2[2], got_rb, late=(grad_done,)
        )
        got_rest = trade(give_rest, "dp", 2)
        *q2, q2_done = second_sums(at, q1[0], got_qa, q1[2], got_qb, late=(r3_done,))
        got_qa, got_qb = gate(
            (trade(q2[1], "dp", 1), trade(q2[3], "seq", 2)), weight=10 * WEIGHT
        )
        rest, rest_done = add((rest,), (got_rest,), late=(q2_done,))
        got_rest = trade(rest, "dp", far_bits[0])
        qkv, give_qkv, q3_done = third_sums(
            at, q2[0], got_qa, q2[2], got_qb, late=(rest_done,)
        )
        (mixed_far,) = gate((mixed_far,), (q2_done,))
        mixed_far = trade(mixed_far, "seq", 2)
        (grad_far,) = gate((grad_far,), (q2_done,))
        grad_far = trade(grad_far, "seq", 2)
        qkv, qkv_done = add((qkv,), (trade(give_qkv, "dp", 2),))
        got_qkv = trade(qkv, "dp", far_bits[0])
        rest, rest_done = add((rest,), (got_rest,), late=(qkv_done, grad_far, mixed_far))
        for bit in far_bits[1:]:
            rest, rest_done = add((rest,), (trade(rest, "dp", bit),))

        beside, other = trade(rest, "dp", 2), trade(rest, "dp", 1)
        mixed, grad, fill_done = fill(at, mixed, mixed_far, grad, grad_far)
        qkv, qkv_done = add((qkv,), (got_qkv,), late=(rest_done, fill_done, beside, other))
        for bit in far_bits[1:]:
            qkv, qkv_done = add((qkv,), (trade(qkv, "dp", bit),))
        square, _ = squares(at, qkv, w_qkv, rest, w_in, gains)
        qkv_beside, qkv_other = trade(qkv, "dp", 2), trade(qkv, "dp", 1)
        qkv_parts = (qkv, qkv_beside, qkv_other, trade(qkv_beside, "dp", 1))
        square, _ = add((square,), (trade(square, "seq", 2),))
        square, square_done = add(
            (square,), (trade(square, "seq", 1),), late=(qkv_other, qkv_beside)
        )
        (beside,) = gate((beside,), (square_done,))
        rest_parts = (rest, beside, other, trade(beside, "dp", 1))
        square, _ = add((square,), (trade(square, "dp", 2),))
        square, _ = add((square,), (trade(square, "dp", 1),), late=(rest_parts[3],))

        (new_in, first_in, second_in, new_out, first_out, second_out,
         new_down, first_down, second_down, row, _) = update_rest(
            at, square, rest_parts,
            (w_in, m_in, v_in), (w_out, m_out, v_out), (w_down, m_down, v_down), (),
        )
        (new_qkv, first_qkv, second_qkv, new_gains, first_gains, second_gains, norm, _) = (
            update_last(
                at, square, (w_qkv, m_qkv, v_qkv), qkv_parts, row, (gains, m_gains, v_gains)
            )
        )
        return (
            mixed,
            grad,
            norm[0, 0],
            new_qkv, new_out, new_in, new_down, new_gains,
            first_qkv, first_out, first_in, first_down, first_gains,
            second_qkv, second_out, second_in, second_down, second_gains,
        )

    return on_device


def solution(mesh):
    rows, matrix, gain = P("dp", "seq", None), P("seq", None), P(None, "seq")
    weights = (matrix,) * 4 + (gain,)
    return jax.shard_map(
        make(mesh.shape["dp"], mesh.shape["seq"]),
        mesh=mesh,
        in_specs=(rows, rows, P("dp", None), P("dp")) + weights * 3,
        out_specs=(rows, rows, P()) + weights * 3,
        check_vma=False,
    )
```

```python
import functools
import math

import jax
import jax.numpy as jnp
from jax import lax
from jax.experimental import pallas as pl
from jax.experimental.pallas import tpu as pltpu
from jax.sharding import PartitionSpec as P

HEADS = 12
HEAD_DIM = 64
PAIR = 2 * HEAD_DIM
STEP_COUNT = 10
EPS_NORM = 1e-05
ROPE_BASE = 160000.0
NEG_FILL = -1e30
CLIP_LIMIT = 10.0
BETA_FIRST = 0.9
BETA_SECOND = 0.98
EPS_ADAM = 1e-06
STEP_RATES = (0.1, 0.5, 0.1, 0.1, 1.0)
DECAY_RATES = (0.01, 0.01, 0.01, 0.01, 0.0)
DOCS = 5
LOW = jnp.bfloat16
FULL = jnp.float32
SCALE = 1.0 / math.sqrt(HEAD_DIM)
WEIGHT = 20_000_000_000


def doc_positions(segment_ids):
    seq_len = segment_ids.shape[-1]
    places = jnp.arange(seq_len, dtype=jnp.int32)
    first_mark = jnp.ones((1,), jnp.bool_)
    change = jnp.concatenate([first_mark, segment_ids[1:] != segment_ids[:-1]])
    starts = lax.cummax(jnp.where(change, places, 0), axis=0)
    return places - starts


def rope_tables(positions):
    half_dim = HEAD_DIM // 2
    exponents = jnp.arange(half_dim, dtype=jnp.float32) * (2.0 / HEAD_DIM)
    inv_freq = ROPE_BASE ** (-exponents)
    angles = positions.astype(jnp.float32)[:, None] * inv_freq
    cos_part, sin_part = jnp.cos(angles), jnp.sin(angles)
    return (
        jnp.concatenate([cos_part] * 4, axis=1),
        jnp.concatenate([-sin_part, sin_part] * 2, axis=1),
    )


def adam_step(weight, first_old, second_old, gradient, factor, step_rate, decay_rate):
    clipped = gradient * factor
    first_new = BETA_FIRST * first_old + (1.0 - BETA_FIRST) * clipped
    second_new = BETA_SECOND * second_old + (1.0 - BETA_SECOND) * clipped * clipped
    root = second_new * lax.rsqrt(second_new) * (1.0 - BETA_SECOND**STEP_COUNT) ** -0.5
    step = first_new * (step_rate / (1.0 - BETA_FIRST**STEP_COUNT)) / (root + EPS_ADAM)
    return (weight * (1.0 - step_rate * decay_rate) - step, first_new, second_new)


def mul(left, right):
    return lax.dot_general(left, right, (((1,), (0,)), ((), ())), preferred_element_type=FULL)


def mul_t(left, right):
    return lax.dot_general(left, right, (((1,), (1,)), ((), ())), preferred_element_type=FULL)


def normalize(values):
    centered = values - jnp.mean(values, axis=-1, keepdims=True)
    root = lax.rsqrt(jnp.mean(centered * centered, axis=-1, keepdims=True) + EPS_NORM)
    return centered * root, root


def normalize_back(grad, gain, scaled, root):
    t = grad * gain
    back = root * (
        t
        - jnp.mean(t, axis=-1, keepdims=True)
        - scaled * jnp.mean(t * scaled, axis=-1, keepdims=True)
    )
    return back


def turn(values, cos_part, sin_part):
    lane = lax.broadcasted_iota(jnp.int32, values.shape, 1)
    swapped = jnp.where(
        lane % HEAD_DIM < HEAD_DIM // 2,
        pltpu.roll(values, PAIR - HEAD_DIM // 2, 1),
        pltpu.roll(values, HEAD_DIM // 2, 1),
    )
    return values * cos_part + swapped * sin_part


def three_parts(values):
    high = values.astype(LOW).astype(FULL)
    rest = values - high
    mid = rest.astype(LOW).astype(FULL)
    return high, mid, rest - mid


def wait_all(copies):
    for copy in copies:
        copy.wait()


def put(source, target, sem):
    copy = pltpu.make_async_copy(source, target, sem)
    copy.start()
    return copy


PIECES = ((0, None), (1, None), (2, 0), (2, 1), (3, 0), (3, 1))


def join_blocks(at_ref, blocks, whole):
    rows = blocks[0].shape[0]
    for block, (bits, part) in zip(blocks, PIECES):
        start = (at_ref[0] ^ bits) * rows
        size = rows
        if part is not None:
            size = rows // 2
            start += (at_ref[1] ^ part) * size
        whole[pl.ds(pl.multiple_of(start, size), size), :] = block[...]


def join_folded(at_ref, blocks, w_out, w_down):
    rows, width = blocks[0].shape[0], w_out.shape[1]
    short, last = rows // 2, width // 2
    for block, (bits, part) in zip(blocks, PIECES):
        owner = at_ref[0] ^ bits
        base = owner * (rows + short)
        first = 0 if part is None else (at_ref[1] ^ part) * short
        size = rows if part is None else short
        span = pl.ds(pl.multiple_of(owner * rows + first, short), size)
        w_out[span, :] = block[:, :width]
        span = pl.ds(pl.multiple_of(base + first, short), size)
        w_down[span, :] = block[:, width : 2 * width]
        span = pl.ds(pl.multiple_of(base + rows, short), short)
        if part is None:
            for i in range(2):
                w_down[span, i * last : (i + 1) * last] = block[
                    i * short : (i + 1) * short, 2 * width :
                ]
        else:
            lanes = pl.ds(pl.multiple_of((at_ref[1] ^ part) * last, last), last)
            w_down[span, lanes] = block[:, 2 * width :]


def fold(out, w_out, w_down, first):
    rows, width = w_out.shape
    short, last = rows // 2, width // 2
    out[:, first : first + width] = w_out[...].astype(LOW)
    out[:, first + width : first + 2 * width] = w_down[:rows, :].astype(LOW)
    for i in range(2):
        out[i * short : (i + 1) * short, first + 2 * width :] = w_down[
            rows:, i * last : (i + 1) * last
        ].astype(LOW)


def prepare_first_kernel(at_ref, w_ref, gains_ref, half_ref, gains_out, wide, sem):
    short = half_ref.shape[0]
    span = pl.ds(pl.multiple_of(at_ref[1] * short, short), short)
    copy = put(w_ref.at[span, :], wide, sem.at[0])
    gains_out[...] = gains_ref[...].astype(LOW)
    copy.wait()
    half_ref[...] = wide[...].astype(LOW)


def prepare_rest_kernel(at_ref, tokens_ref, in_ref, out_ref, down_ref, qkv_ref, cot_ref,
                        their_tokens, low_in, half_in, low_od, half_od, low_qkv, their_cot,
                        in_wide, out_wide, down_wide, qkv_wide, sem):
    slot = 1 - at_ref[2]
    copies = [
        put(source, target, sem.at[i])
        for i, (source, target) in enumerate((
            (tokens_ref.at[slot], their_tokens), (in_ref, in_wide), (out_ref, out_wide),
            (down_ref, down_wide), (qkv_ref, qkv_wide), (cot_ref.at[slot], their_cot),
        ))
    ]
    short = half_in.shape[0]
    span = pl.ds(pl.multiple_of(at_ref[1] * short, short), short)
    copies[1].wait()
    low_in[...] = in_wide[...].astype(LOW)
    half_in[...] = in_wide[span, :].astype(LOW)
    copies[2].wait()
    copies[3].wait()
    fold(low_od, out_wide, down_wide, 0)
    half_od[...] = low_od[span, :]
    copies[4].wait()
    low_qkv[...] = qkv_wide[...].astype(LOW)
    copies[0].wait()
    copies[5].wait()


def project_kernel(at_ref, tokens_ref, far_ref, gain_ref, cos_ref, sin_ref, w0, w1, w2, w3, w4, w5,
                   normed_ref, query_ref, kv_ref, weight):
    join_blocks(at_ref, (w0, w1, w2, w3, w4, w5), weight)
    rows, width = far_ref.shape
    for part in range(2):
        values = tokens_ref[at_ref[2]] if part == 0 else far_ref[...]
        scaled, _ = normalize(values.astype(FULL))
        normed_ref[pl.ds(part * rows, rows), :] = (scaled * gain_ref[...]).astype(LOW)
    for part in range(2):
        span = pl.ds(part * rows, rows)
        normed = normed_ref[span, :]
        cos_part, sin_part = cos_ref[span, :], sin_ref[span, :]
        for pair in range(2 * width // PAIR):
            lanes = pl.ds(pair * PAIR, PAIR)
            if pair % 2 == 0:
                both = mul(normed, weight[:, pl.ds(pair * PAIR, 2 * PAIR)])
            raw = both[:, (pair % 2) * PAIR : (pair % 2 + 1) * PAIR]
            turned = turn(raw, cos_part, sin_part)
            if pair < width // PAIR:
                query_ref[span, lanes] = (turned * SCALE).astype(LOW)
            else:
                kv_ref[0, span, pl.ds(pair * PAIR - width, PAIR)] = turned.astype(LOW)
        kv_ref[1, span, :] = mul(normed, weight[:, 2 * width :]).astype(LOW)


def head_lanes(head, shape):
    lane = lax.broadcasted_iota(jnp.int32, shape, 1)
    return (lane < HEAD_DIM) if head == 0 else (lane >= HEAD_DIM)


def pick(head, inside, outside):
    return jnp.where(head_lanes(head, inside.shape), inside, outside)


def attend_kernel(query_ref, near_ref, far_ref, mark_query_ref, mark_key_ref, o_ref, extra_ref):
    rows = query_ref.shape[0]
    query = query_ref[...]
    mark_query = mark_query_ref[...]
    parts = [
        (near_ref[0], jnp.transpose(near_ref[1]), mark_key_ref[:rows, :]),
        (far_ref[0], jnp.transpose(far_ref[1]), mark_key_ref[rows:, :]),
    ]
    outs, logs = [], []
    for head in range(2):
        query_head = pick(head, query, mark_query)
        scores = [mul_t(pick(head, key, mark), query_head) for key, _, mark in parts]
        top = jnp.maximum(
            jnp.max(scores[0], axis=0, keepdims=True), jnp.max(scores[1], axis=0, keepdims=True)
        )
        exps = [jnp.exp(score - top) for score in scores]
        total = jnp.sum(exps[0], axis=0, keepdims=True) + jnp.sum(exps[1], axis=0, keepdims=True)
        span = slice(head * HEAD_DIM, (head + 1) * HEAD_DIM)
        out = sum(mul(value_t[span], e.astype(LOW)) for (_, value_t, _), e in zip(parts, exps))
        outs.append(out / total)
        logs.append(top + jnp.log(total))
    o_ref[...] = jnp.transpose(jnp.concatenate(outs)).astype(LOW)
    line = lax.broadcasted_iota(jnp.int32, (PAIR, rows), 0)
    extra = jnp.zeros((PAIR, rows), FULL)
    for head in range(2):
        base = DOCS + (HEAD_DIM if head == 0 else 0)
        for i, piece in enumerate(three_parts(-logs[head])):
            extra = jnp.where(line == base + i, piece, extra)
    extra_ref[...] = jnp.transpose(extra).astype(LOW) + mark_query


def attend_back_kernel(query_ref, near_ref, far_ref, extra_ref, mark_key_ref, o_ref, do_ref,
                       cos_ref, sin_ref, dq_ref, keep_ref, send_ref):
    rows = query_ref.shape[0]
    query, extra, do = query_ref[...], extra_ref[...], do_ref[...]
    inner_all = do.astype(FULL) * o_ref[...].astype(FULL)
    lane = lax.broadcasted_iota(jnp.int32, (rows, PAIR), 1)
    zero = jnp.zeros((rows, PAIR), LOW)
    grads_query = []
    sums = [[None, None], [None, None]]
    keys_t = [jnp.transpose(near_ref[0]), jnp.transpose(far_ref[0])]
    for head in range(2):
        inside = head_lanes(head, (rows, PAIR))
        inner = jnp.sum(jnp.where(inside, inner_all, 0.0), axis=1, keepdims=True)
        base = DOCS + (HEAD_DIM if head == 0 else 0)
        tail = jnp.zeros((rows, PAIR), FULL)
        for i, piece in enumerate(three_parts(-inner)):
            tail = jnp.where(lane == base + i, piece, tail)
        query_head = pick(head, query, extra)
        do_head = pick(head, do, tail.astype(LOW))
        query_only = pick(head, query, zero)
        do_only = pick(head, do, zero)
        span = slice(head * HEAD_DIM, (head + 1) * HEAD_DIM)
        grad_query = 0.0
        for part, ref in enumerate((near_ref, far_ref)):
            mark = mark_key_ref[pl.ds(part * rows, rows), :]
            probs = jnp.exp(mul_t(pick(head, ref[0], mark), query_head))
            grad_probs = mul_t(pick(head, ref[1], mark), do_head)
            grad_scores = (probs * grad_probs).astype(LOW)
            grad_value = mul(probs.astype(LOW), do_only)
            grad_key = mul(grad_scores, query_only)
            grad_query += mul(keys_t[part][span], grad_scores)
            if head == 0:
                sums[part] = [grad_key, grad_value]
            else:
                sums[part] = [sums[part][0] + grad_key, sums[part][1] + grad_value]
        grads_query.append(grad_query)
    turned = turn(
        jnp.transpose(jnp.concatenate(grads_query)) * SCALE, cos_ref[...], -sin_ref[...]
    )
    dq_ref[...] = turned.astype(LOW)
    for i in range(2):
        keep_ref[i] = sums[0][i].astype(LOW)
        send_ref[i] = sums[1][i].astype(LOW)


def middle_kernel(at_ref, live_ref, tokens_ref, far_ref, cot_ref, cot_far_ref, oa_ref, ob_ref,
                  gain_ref, i0, i1, i2, i3, i4, i5, d0, d1, d2, d3, d4, d5,
                  mixed_ref, mixed_far_ref, dx1_ref, do_ref, keep_ref, send_ref,
                  w_out, w_in, w_down, o_all, o_t, a2_t, h_t, dm_all, duw_all, db_all,
                  mixed, dx1_all, do_all, keep, send, out_sem):
    place, slot = at_ref[0], at_ref[2]
    live = live_ref[slot].astype(FULL)
    join_folded(at_ref, (d0, d1, d2, d3, d4, d5), w_out, w_down)
    join_blocks(at_ref, (i0, i1, i2, i3, i4, i5), w_in)
    rows, width = far_ref.shape
    share = width // 4
    short, units = share // 2, w_down.shape[0]
    gain = gain_ref[...]
    o_all[:, : oa_ref.shape[1]] = oa_ref[...]
    o_all[:, oa_ref.shape[1] :] = ob_ref[...]
    copies = []
    for part in range(2):
        span = pl.ds(part * rows, rows)
        o = o_all[span, :]
        values = tokens_ref[slot] if part == 0 else far_ref[...]
        x1 = values.astype(FULL) + live * mul(o, w_out[...])
        scaled, root = normalize(x1)
        a2 = (scaled * gain).astype(LOW)
        u = mul(a2, w_in[:, :units])
        w = mul(a2, w_in[:, units:])
        phi = 0.5 * (1.0 + lax.erf(u * math.sqrt(0.5)))
        gelu = u * phi
        h = (gelu * w).astype(LOW)
        mixed[span, :] = (x1 + live * mul(h, w_down[...])).astype(LOW)
        target = mixed_ref.at[slot] if part == 0 else mixed_far_ref
        copies.append(put(mixed.at[span, :], target, out_sem.at[len(copies)]))
        cot = (cot_ref[slot] if part == 0 else cot_far_ref[...]).astype(FULL)
        dm = (live * cot).astype(LOW)
        dh = mul_t(dm, w_down[...])
        slope = phi + u * (jnp.exp(-0.5 * u * u) * (1.0 / math.sqrt(2.0 * math.pi)))
        duw_all[span, :units] = (dh * w * slope).astype(LOW)
        duw_all[span, units:] = (dh * gelu).astype(LOW)
        da2 = mul_t(duw_all[span, :], w_in[...])
        dx1 = cot + normalize_back(da2, gain, scaled, root)
        dx1_all[span, :] = dx1
        copies.append(put(dx1_all.at[span, :], dx1_ref.at[span, :], out_sem.at[len(copies)]))
        db = (live * dx1).astype(LOW)
        do_all[span, :] = mul_t(db, w_out[...]).astype(LOW)
        copies.append(put(do_all.at[span, :], do_ref.at[span, :], out_sem.at[len(copies)]))
        db_all[span, :] = db
        dm_all[span, :] = dm
        o_t[:, span] = jnp.transpose(o)
        a2_t[:, span] = jnp.transpose(a2)
        h_t[:, span] = jnp.transpose(h)
    dm, duw, db = dm_all[...], duw_all[...], db_all[...]
    for j, out, target in ((1, send, send_ref), (3, send, send_ref), (0, keep, keep_ref), (2, keep, keep_ref)):
        span = pl.ds(pl.multiple_of((place ^ j) * share, share), share)
        base = (place ^ j) * (share + short)
        down = pl.ds(pl.multiple_of(base, short), share)
        down_last = pl.ds(pl.multiple_of(base + share, short), short)
        at = 2 * units
        out[j // 2, :, :at] = mul(a2_t[span, :], duw).astype(LOW)
        out[j // 2, :, at : at + width] = mul(o_t[span, :], db).astype(LOW)
        at += width
        out[j // 2, :, at : at + width] = mul(h_t[down, :], dm).astype(LOW)
        at += width
        last = mul(h_t[down_last, :], dm).astype(LOW)
        out[j // 2, :short, at:] = last[:, : width // 2]
        out[j // 2, short:, at:] = last[:, width // 2 :]
        copies.append(put(out.at[j // 2], target.at[j // 2], out_sem.at[len(copies)]))
    wait_all(copies)


def send_kernel(count, at_ref, *refs):
    normed_ref = refs[0]
    dqs, owns, gots = (refs[1 + i * count : 1 + (i + 1) * count] for i in range(3))
    (cos_ref, sin_ref, dqkv_ref, normed_t_ref, send_ref,
     dqkv, normed_t, send, sem) = refs[1 + 3 * count :]
    width = normed_ref.shape[1]
    part_width = width // count
    normed_t[...] = jnp.transpose(normed_ref[...])
    copies = [put(normed_t, normed_t_ref, sem.at[0])]
    cos_part, sin_part = cos_ref[...], -sin_ref[...]
    for part, (dq, own, got) in enumerate(zip(dqs, owns, gots)):
        base = part * part_width
        dqkv[:, pl.ds(base, part_width)] = dq[...]
        dqkv[:, pl.ds(2 * width + base, part_width)] = (
            own[1].astype(FULL) + got[1].astype(FULL)
        ).astype(LOW)
        for pair in range(part_width // PAIR):
            lanes = pl.ds(pair * PAIR, PAIR)
            raw = own[0, :, lanes].astype(FULL) + got[0, :, lanes].astype(FULL)
            dqkv[:, pl.ds(width + base + pair * PAIR, PAIR)] = turn(raw, cos_part, sin_part).astype(
                LOW
            )
    copies.append(put(dqkv, dqkv_ref, sem.at[1]))
    right = dqkv[...]
    share = send.shape[1]
    for j in (1, 3):
        start = pl.multiple_of((at_ref[0] ^ j) * share, share)
        send[j // 2] = mul(normed_t[pl.ds(start, share), :], right).astype(LOW)
        copies.append(put(send.at[j // 2], send_ref.at[j // 2], sem.at[len(copies)]))
    wait_all(copies)


def keep_kernel(at_ref, normed_t_ref, dqkv_ref, keep_ref, keep, sem):
    right = dqkv_ref[...]
    share = keep.shape[1]
    copies = []
    for j in (0, 2):
        start = pl.multiple_of((at_ref[0] ^ j) * share, share)
        keep[j // 2] = mul(normed_t_ref[pl.ds(start, share), :], right).astype(LOW)
        copies.append(put(keep.at[j // 2], keep_ref.at[j // 2], sem.at[len(copies)]))
    wait_all(copies)


def input_kernel(at_ref, tokens_ref, far_ref, gain_ref, dx1_ref, dqkv_ref, w0, w1, w2, w3, w4, w5,
                 grad_ref, grad_far_ref, weight, grad_own, out_sem):
    join_blocks(at_ref, (w0, w1, w2, w3, w4, w5), weight)
    rows = far_ref.shape[0]
    gain = gain_ref[...]
    for part in (1, 0):
        span = pl.ds(part * rows, rows)
        values = tokens_ref[at_ref[2]] if part == 0 else far_ref[...]
        scaled, root = normalize(values.astype(FULL))
        back = normalize_back(mul_t(dqkv_ref[span, :], weight[...]), gain, scaled, root)
        grad = dx1_ref[span, :] + back
        if part == 1:
            grad_far_ref[...] = grad.astype(LOW)
        else:
            grad_own[...] = grad
    put(grad_own, grad_ref.at[at_ref[2]], out_sem.at[0]).wait()


def shaped(*shape, kind=LOW):
    return jax.ShapeDtypeStruct(shape, kind)


IN_SMEM = pl.BlockSpec(memory_space=pltpu.SMEM)
IN_VMEM = pl.BlockSpec(memory_space=pltpu.VMEM)
IN_ANY = pl.BlockSpec(memory_space=pl.ANY)


def params(mebibytes):
    return pltpu.CompilerParams(vmem_limit_bytes=int(mebibytes * 1024 * 1024))


def call(kernel, args, in_specs, out_shape, out_specs, late=(), **options):
    if not isinstance(out_shape, tuple):
        out_shape, out_specs = (out_shape,), (out_specs,)
    count, skip, outs = len(args), len(late), len(out_shape)

    def body(*refs):
        outs_at = count + skip
        return kernel(*refs[:count], *refs[outs_at : outs_at + outs], *refs[outs_at + outs + 1 :])

    return pl.pallas_call(
        body,
        in_specs=list(in_specs) + [IN_ANY] * skip,
        out_shape=out_shape + (shaped(8, 128, kind=FULL),),
        out_specs=out_specs + (IN_ANY,),
        **options,
    )(*args, *late)


def gate(values, late=(), weight=0):
    hint = {}
    if weight:
        hint["cost_estimate"] = pl.CostEstimate(
            flops=weight, transcendentals=0, bytes_accessed=0
        )
    return call(
        lambda *refs: None,
        values,
        late=late,
        out_shape=tuple(jax.ShapeDtypeStruct(v.shape, v.dtype) for v in values),
        in_specs=[IN_ANY] * len(values),
        out_specs=(IN_ANY,) * len(values),
        input_output_aliases={i: i for i in range(len(values))},
        compiler_params=params(1),
        name="gate",
        **hint,
    )[: len(values)]


def in_hbm(value):
    return pltpu.with_memory_space_constraint(value, pltpu.HBM)


def in_vmem(*values):
    return [pltpu.with_memory_space_constraint(value, pltpu.VMEM) for value in values]


def prepare_first(at, weight, gains):
    rows, width = weight.shape
    return call(
        prepare_first_kernel,
        (at, in_hbm(weight), gains),
        out_shape=(shaped(rows // 2, width), shaped(*gains.shape)),
        in_specs=[IN_SMEM, IN_ANY, IN_VMEM],
        out_specs=(IN_VMEM,) * 2,
        scratch_shapes=[pltpu.VMEM((rows // 2, width), FULL), pltpu.SemaphoreType.DMA((1,))],
        compiler_params=params(6),
        name="prepare_first",
    )


def prepare_rest(at, tokens, w_in, w_out, w_down, w_qkv, cotangent, late):
    rows, width = w_out.shape
    folded = 2 * width + width // 2
    return call(
        prepare_rest_kernel,
        (at, *[in_hbm(v) for v in (tokens, w_in, w_out, w_down, w_qkv, cotangent)]),
        late=late,
        out_shape=(
            shaped(*tokens.shape[1:]),
            shaped(*w_in.shape),
            shaped(rows // 2, w_in.shape[1]),
            shaped(rows, folded),
            shaped(rows // 2, folded),
            shaped(*w_qkv.shape),
            shaped(*cotangent.shape[1:]),
        ),
        in_specs=[IN_SMEM] + [IN_ANY] * 6,
        out_specs=(IN_VMEM,) * 7,
        scratch_shapes=[
            pltpu.VMEM(v.shape, FULL) for v in (w_in, w_out, w_down, w_qkv)
        ] + [pltpu.SemaphoreType.DMA((6,))],
        compiler_params=params(18),
        name="prepare_rest",
    )


def project(at, tokens, far, gain, cos_part, sin_part, blocks, late):
    rows, width = 2 * far.shape[0], far.shape[1]
    return call(
        project_kernel,
        (at, tokens, *in_vmem(far), gain, cos_part, sin_part, *in_vmem(*blocks)),
        late=late,
        out_shape=(shaped(rows, width), shaped(rows, width), shaped(2, rows, width)),
        in_specs=[IN_SMEM] + [IN_VMEM] * 11,
        out_specs=(IN_VMEM,) * 3,
        scratch_shapes=[pltpu.VMEM((width, 3 * width), LOW)],
        compiler_params=params(18),
        name="project",
    )


def attend(first, count, query, near, far, mark_query, mark_key, late=()):
    rows = query.shape[0]
    row_spec = pl.BlockSpec((rows, PAIR), lambda i: (0, i + first))
    kv_spec = pl.BlockSpec((2, rows, PAIR), lambda i: (0, 0, i + first))
    out_spec = pl.BlockSpec((rows, PAIR), lambda i: (0, i))
    return call(
        attend_kernel,
        (*in_vmem(query, near, far), mark_query, mark_key),
        late=late,
        grid=(count,),
        out_shape=(shaped(rows, count * PAIR), shaped(rows, count * PAIR)),
        in_specs=[
            row_spec,
            kv_spec,
            kv_spec,
            pl.BlockSpec((rows, PAIR), lambda i: (0, 0)),
            pl.BlockSpec((2 * rows, PAIR), lambda i: (0, 0)),
        ],
        out_specs=(out_spec, out_spec),
        compiler_params=params(16),
        name="attend",
    )


def attend_back(
    first, first_o, count, query, near, far, extra, o, mark_key, do, cos_part, sin_part, late=()
):
    rows = query.shape[0]
    row_spec = pl.BlockSpec((rows, PAIR), lambda i: (0, i + first))
    o_spec = pl.BlockSpec((rows, PAIR), lambda i: (0, i + first_o))
    kv_spec = pl.BlockSpec((2, rows, PAIR), lambda i: (0, 0, i + first))
    fixed = pl.BlockSpec((rows, PAIR), lambda i: (0, 0))
    out_row = pl.BlockSpec((rows, PAIR), lambda i: (0, i))
    out_kv = pl.BlockSpec((2, rows, PAIR), lambda i: (0, 0, i))
    return call(
        attend_back_kernel,
        (*in_vmem(query, near, far, extra), mark_key, *in_vmem(o, do), cos_part, sin_part),
        late=late,
        grid=(count,),
        out_shape=(
            shaped(rows, count * PAIR),
            shaped(2, rows, count * PAIR),
            shaped(2, rows, count * PAIR),
        ),
        in_specs=[
            row_spec,
            kv_spec,
            kv_spec,
            o_spec,
            pl.BlockSpec((2 * rows, PAIR), lambda i: (0, 0)),
            o_spec,
            row_spec,
            fixed,
            fixed,
        ],
        out_specs=(out_row, out_kv, out_kv),
        compiler_params=params(20),
        name="attend_back",
    )


def middle(at, live, tokens, far, cot, cot_far, o_a, o_b, gain, blocks_in, blocks_od):
    half, width = far.shape
    rows, share = 2 * half, width // 4
    units = blocks_in[0].shape[1] // 2
    total = 2 * units + blocks_od[0].shape[1]
    assert units == 4 * (share + share // 2)
    low = lambda *shape: pltpu.VMEM(shape, LOW)
    return call(
        middle_kernel,
        (at, live, tokens, *in_vmem(far), cot, *in_vmem(cot_far, o_a, o_b), gain,
         *in_vmem(*blocks_in, *blocks_od)),
        out_shape=(
            shaped(2, half, width),
            shaped(half, width),
            shaped(rows, width, kind=FULL),
            shaped(rows, width),
            shaped(2, share, total),
            shaped(2, share, total),
        ),
        in_specs=[IN_SMEM] * 2 + [IN_VMEM] * 19,
        out_specs=(IN_ANY,) * 6,
        scratch_shapes=[
            low(width, width),
            low(width, 2 * units),
            low(units, width),
            low(rows, width),
            low(width, rows),
            low(width, rows),
            low(units, rows),
            low(rows, width),
            low(rows, 2 * units),
            low(rows, width),
            low(rows, width),
            pltpu.VMEM((rows, width), FULL),
            low(rows, width),
            low(2, share, total),
            low(2, share, total),
            pltpu.SemaphoreType.DMA((10,)),
        ],
        compiler_params=params(44),
        name="middle",
    )


def qkv_send(at, normed, dq, own, got, cos_part, sin_part, late):
    rows, width = normed.shape
    share = width // 4
    return call(
        functools.partial(send_kernel, len(dq)),
        (at, normed, *dq, *own, *got, cos_part, sin_part),
        late=late,
        out_shape=(
            shaped(rows, 3 * width),
            shaped(width, rows),
            shaped(2, share, 3 * width),
        ),
        in_specs=[IN_SMEM] + [IN_VMEM] * (3 + 3 * len(dq)),
        out_specs=(IN_ANY,) * 3,
        scratch_shapes=[
            pltpu.VMEM((rows, 3 * width), LOW),
            pltpu.VMEM((width, rows), LOW),
            pltpu.VMEM((2, share, 3 * width), LOW),
            pltpu.SemaphoreType.DMA((4,)),
        ],
        compiler_params=params(20),
        name="qkv_send",
    )


def qkv_keep(at, normed_t, dqkv, late):
    width, rows = normed_t.shape
    share = width // 4
    return call(
        keep_kernel,
        (at, normed_t, dqkv),
        late=late,
        out_shape=shaped(2, share, 3 * width),
        in_specs=[IN_SMEM] + [IN_VMEM] * 2,
        out_specs=IN_ANY,
        scratch_shapes=[
            pltpu.VMEM((2, share, 3 * width), LOW),
            pltpu.SemaphoreType.DMA((2,)),
        ],
        compiler_params=params(16),
        name="qkv_keep",
    )


def input_back(at, tokens, far, gain, dx1, dqkv, blocks, late):
    half, width = far.shape
    return call(
        input_kernel,
        (at, tokens, far, gain, dx1, *in_vmem(dqkv, *blocks)),
        late=late,
        out_shape=(shaped(2, half, width, kind=FULL), shaped(half, width)),
        in_specs=[IN_SMEM] + [IN_VMEM] * 11,
        out_specs=(IN_ANY, IN_VMEM),
        scratch_shapes=[
            pltpu.VMEM((width, 3 * width), LOW),
            pltpu.VMEM((half, width), FULL),
            pltpu.SemaphoreType.DMA((1,)),
        ],
        compiler_params=params(20),
        name="input_back",
    )


def first_sums_kernel(at_ref, keep, got, own_a, far_a, mine_b, give_b):
    cut, short = far_a.shape[0], give_b.shape[1]

    def add(block, start, size):
        span = pl.ds(start, size)
        return (keep[block, span, :].astype(FULL) + got[block, span, :].astype(FULL)).astype(LOW)

    far_a[...] = add(1, 0, cut)
    for block in range(2):
        give_b[block] = add(block, pl.multiple_of(cut + (1 - at_ref[1]) * short, short), short)
        mine_b[block] = add(block, pl.multiple_of(cut + at_ref[1] * short, short), short)
    own_a[...] = add(0, 0, cut)


def first_sums(at, keep, got, late=()):
    _, rows, width = keep.shape
    cut, short = rows // 2, rows // 4
    return call(
        first_sums_kernel,
        (at, keep, got),
        late=late,
        out_shape=(shaped(cut, width),) * 2 + (shaped(2, short, width),) * 2,
        in_specs=[IN_SMEM] + [IN_VMEM] * 2,
        out_specs=(IN_VMEM,) * 4,
        compiler_params=params(20),
        name="first_sums",
    )


def second_sums_kernel(at_ref, own_a, got_a, mine_b, got_b, mine_a, give_a, near_b, far_b):
    short = mine_a.shape[0]
    for start, out in ((1 - at_ref[1], give_a), (at_ref[1], mine_a)):
        span = pl.ds(pl.multiple_of(start * short, short), short)
        out[...] = (own_a[span, :].astype(FULL) + got_a[span, :].astype(FULL)).astype(LOW)
    for block, out in ((1, far_b), (0, near_b)):
        out[...] = (mine_b[block].astype(FULL) + got_b[block].astype(FULL)).astype(LOW)


def second_sums(at, own_a, got_a, mine_b, got_b, late=()):
    _, short, width = mine_b.shape
    return call(
        second_sums_kernel,
        (at, own_a, got_a, mine_b, got_b),
        late=late,
        out_shape=(shaped(short, width),) * 4,
        in_specs=[IN_SMEM] + [IN_VMEM] * 4,
        out_specs=(IN_VMEM,) * 4,
        compiler_params=params(12),
        name="second_sums",
    )


def third_sums_kernel(at_ref, mine_a, got_a, near_b, got_b, keep, give):
    upper = mine_a[...].astype(FULL) + got_a[...].astype(FULL)
    lower = near_b[...].astype(FULL) + got_b[...].astype(FULL)
    keep[...] = jnp.where(at_ref[4] == 0, upper, lower).astype(LOW)
    give[...] = jnp.where(at_ref[4] == 0, lower, upper).astype(LOW)


def third_sums(at, mine_a, got_a, near_b, got_b, late=()):
    return call(
        third_sums_kernel,
        (at, mine_a, got_a, near_b, got_b),
        late=late,
        out_shape=(shaped(*mine_a.shape),) * 2,
        in_specs=[IN_SMEM] + [IN_VMEM] * 4,
        out_specs=(IN_VMEM,) * 2,
        compiler_params=params(12),
        name="third_sums",
    )


def squares_kernel(at_ref, qkv, w_qkv, rest, w_in, gains, out):
    inner = w_in.shape[1]
    total = jnp.sum(jnp.square(rest[:, inner:].astype(FULL)), keepdims=True)
    rows = qkv.shape[0]
    shape = (rows, gains.shape[1])
    offset = lax.broadcasted_iota(jnp.int32, shape, 1) - lax.broadcasted_iota(jnp.int32, shape, 0)
    for i, (piece, weight) in enumerate(((qkv, w_qkv), (rest, w_in))):
        start = at_ref[3]
        span = pl.ds(pl.multiple_of(start, 8), rows)
        values = piece[:, : weight.shape[1]].astype(FULL)
        sums = jnp.sum(weight[span, :].astype(LOW).astype(FULL) * values, axis=1, keepdims=True)
        gain = gains[i : i + 1, :].astype(LOW).astype(FULL)
        gain = jnp.sum(jnp.where(offset == start, gain, 0.0), axis=1, keepdims=True)
        total += jnp.sum(jnp.square(values), keepdims=True)
        total += jnp.sum(jnp.square(sums / gain), keepdims=True)
    out[...] = jnp.broadcast_to(total, out.shape)


def squares(*args):
    return call(
        squares_kernel,
        args,
        out_shape=shaped(8, 128, kind=FULL),
        in_specs=[IN_SMEM] + [IN_VMEM] * (len(args) - 1),
        out_specs=IN_VMEM,
        compiler_params=params(10),
        name="squares",
    )


def add_kernel(count, *refs):
    for i in range(count):
        out = refs[2 * count + i]
        out[...] = (refs[i][...].astype(FULL) + refs[count + i][...].astype(FULL)).astype(out.dtype)


def add(first, second, late=()):
    count = len(first)
    return call(
        functools.partial(add_kernel, count),
        (*first, *second),
        late=late,
        out_shape=tuple(jax.ShapeDtypeStruct(v.shape, v.dtype) for v in first),
        in_specs=[IN_VMEM] * (2 * count),
        out_specs=(IN_VMEM,) * count,
        compiler_params=params(8),
        name="add",
    )


def fill_kernel(at_ref, mixed_far, grad_far, mixed_in, grad_in, mixed, grad, wide, sem):
    first = put(mixed_far, mixed.at[1 - at_ref[2]], sem.at[0])
    wide[...] = grad_far[...].astype(FULL)
    put(wide, grad.at[1 - at_ref[2]], sem.at[1]).wait()
    first.wait()


def fill(at, mixed, mixed_far, grad, grad_far):
    return call(
        fill_kernel,
        (at, mixed_far, grad_far, mixed, grad),
        out_shape=(shaped(*mixed.shape), shaped(*grad.shape, kind=FULL)),
        in_specs=[IN_SMEM, IN_VMEM, IN_VMEM, IN_ANY, IN_ANY],
        out_specs=(IN_ANY,) * 2,
        input_output_aliases={3: 0, 4: 1},
        scratch_shapes=[pltpu.VMEM(grad_far.shape, FULL), pltpu.SemaphoreType.DMA((2,))],
        compiler_params=params(4),
        name="fill",
    )


def clip_factor(square_ref):
    norm = jnp.sqrt(square_ref[:1, :1])
    return jnp.minimum(1.0, CLIP_LIMIT / (norm + 1e-06))


def quarters(at_ref, parts):
    own, beside, other, other_beside = parts
    for i in range(4):
        same = at_ref[4] == i // 2
        near = jnp.where(same, own[...], beside[...])
        far = jnp.where(same, other[...], other_beside[...])
        yield jnp.where(at_ref[1] == i % 2, near, far).astype(FULL)


def gain_row(weight, gradient, start, shape):
    sums = jnp.sum(weight.astype(LOW).astype(FULL) * gradient, axis=1, keepdims=True)
    shape = (weight.shape[0], shape[1])
    offset = lax.broadcasted_iota(jnp.int32, shape, 1) - lax.broadcasted_iota(jnp.int32, shape, 0)
    return jnp.sum(jnp.where(offset == start, sums, 0.0), axis=0, keepdims=True)


class Update:
    def __init__(self, number, sources, news, targets, sem):
        self.number, self.sources, self.news, self.targets = number, sources, news, targets
        self.sem, self.out = sem, []

    def step(self, span, gradient, factor):
        weight = self.sources[0][span]
        results = adam_step(
            weight, self.sources[1][span], self.sources[2][span], gradient, factor,
            STEP_RATES[self.number], DECAY_RATES[self.number],
        )
        for result, new, target in zip(results, self.news, self.targets):
            new[span] = result
            self.out.append(put(new.at[span], target.at[span], self.sem.at[len(self.out)]))
        return weight


def update_rest_kernel(at_ref, square_ref, *refs):
    parts, refs = refs[:4], refs[4:]
    sources, targets, row_ref, news, sem = refs[:9], refs[9:18], refs[18], refs[19:28], refs[28]
    inner, out, down = (
        Update(number, *(group[3 * k : 3 * k + 3] for group in (sources, news, targets)), sem.at[k])
        for k, number in enumerate((2, 1, 3))
    )
    factor = clip_factor(square_ref)
    rows, width = sources[3].shape
    lanes = sources[0].shape[1]
    short, last = rows // 4, width // 2
    row = jnp.zeros(row_ref.shape, FULL)
    for i, gradient in enumerate(quarters(at_ref, parts)):
        span = (slice(i * short, (i + 1) * short), slice(None))
        part = gradient[:, :lanes]
        row += gain_row(inner.step(span, part, factor), part, i * short, row_ref.shape)
        out.step(span, gradient[:, lanes : lanes + width], factor)
        down.step(span, gradient[:, lanes + width : lanes + 2 * width], factor)
        start = rows + (i % 2) * short
        span = (slice(start, start + short), slice((i // 2) * last, (i // 2 + 1) * last))
        down.step(span, gradient[:, lanes + 2 * width :], factor)
    row_ref[...] = row
    wait_all(inner.out + out.out + down.out)


def update_rest(at, square, parts, inner, out, down, late):
    like = [jax.ShapeDtypeStruct(v.shape, FULL) for v in (*inner, *out, *down)]
    return call(
        update_rest_kernel,
        (at, square, *parts, *inner, *out, *down),
        late=late,
        out_shape=(*like, shaped(1, inner[0].shape[0], kind=FULL)),
        in_specs=[IN_SMEM] + [IN_VMEM] * 14,
        out_specs=(IN_ANY,) * 9 + (IN_VMEM,),
        scratch_shapes=[pltpu.VMEM(v.shape, FULL) for v in like]
        + [pltpu.SemaphoreType.DMA((3, 24))],
        compiler_params=params(28),
        name="update_rest",
    )


def update_last_kernel(at_ref, square_ref, row_ref, g_w, g_m, g_v, *refs):
    parts, refs = refs[:4], refs[4:]
    sources, targets = refs[:3], refs[3:6]
    g_w_out, g_m_out, g_v_out, norm_out = refs[6:10]
    news, sem = refs[10:13], refs[13]
    qkv = Update(0, sources, news, targets, sem)
    factor = clip_factor(square_ref)
    norm_out[...] = jnp.sqrt(square_ref[...])
    short = sources[0].shape[0] // 4
    row = jnp.zeros(row_ref.shape, FULL)
    for i, gradient in enumerate(quarters(at_ref, parts)):
        span = (slice(i * short, (i + 1) * short), slice(None))
        row += gain_row(qkv.step(span, gradient, factor), gradient, i * short, row_ref.shape)
    for i, values in enumerate((row, row_ref[...])):
        line = slice(i, i + 1)
        gradient = values / g_w[line, :].astype(LOW).astype(FULL)
        g_w_out[line, :], g_m_out[line, :], g_v_out[line, :] = adam_step(
            g_w[line, :], g_m[line, :], g_v[line, :], gradient, factor,
            STEP_RATES[4], DECAY_RATES[4],
        )
    wait_all(qkv.out)


def update_last(at, square, qkv, qkv_parts, row, gains):
    like = [jax.ShapeDtypeStruct(v.shape, FULL) for v in qkv]
    return call(
        update_last_kernel,
        (at, square, row, *gains, *qkv_parts, *qkv),
        out_shape=(
            *like,
            *[jax.ShapeDtypeStruct(v.shape, FULL) for v in gains],
            jax.ShapeDtypeStruct(square.shape, FULL),
        ),
        in_specs=[IN_SMEM] + [IN_VMEM] * 12,
        out_specs=(IN_ANY,) * 3 + (IN_VMEM,) * 4,
        scratch_shapes=[pltpu.VMEM(v.shape, FULL) for v in like]
        + [pltpu.SemaphoreType.DMA((12,))],
        compiler_params=params(18),
        name="update_last",
    )


def low_sum(*values):
    return sum(value.astype(FULL) for value in values).astype(LOW)


def index(value, i):
    return lax.dynamic_index_in_dim(value, i, 0, keepdims=False)


def make(dp_count, seq_count):
    assert seq_count == 4 and dp_count >= 8 and dp_count & (dp_count - 1) == 0
    far_bits = [1 << i for i in range(2, dp_count.bit_length() - 1)]

    def trade(value, axis, bit):
        size = seq_count if axis == "seq" else dp_count
        return lax.ppermute(value, axis, [(i, i ^ bit) for i in range(size)])

    def on_device(
        tokens, cotangent, segments, valid,
        w_qkv, w_out, w_in, w_down, gains,
        m_qkv, m_out, m_in, m_down, m_gains,
        v_qkv, v_out, v_in, v_down, v_gains,
    ):
        place = lax.axis_index("seq")
        group = lax.axis_index("dp")
        slot = place >> 1
        half = group & 1
        local_len, width = tokens.shape[1:]
        rows = 2 * local_len
        share = w_qkv.shape[0]
        side = (group >> 1) & 1
        quarter = share // 4
        at = jnp.stack([place, half, slot, side * 2 * quarter + half * quarter, side])

        half_qkv, low_gains, begun = prepare_first(at, w_qkv, gains)
        (far_qa,) = gate((trade(half_qkv, "seq", 2),), weight=10 * WEIGHT)
        (gain_far,) = gate((trade(low_gains, "seq", 2),), weight=20 * WEIGHT)
        their_tokens, low_in, half_in, low_od, half_od, low_qkv, their_cot, _ = prepare_rest(
            at, tokens, w_in, w_out, w_down, w_qkv, cotangent, (begun,)
        )
        near_q = trade(low_qkv, "seq", 1)
        far = trade(their_tokens, "seq", 2)
        far_qb = trade(far_qa, "dp", 1)
        near_qa = trade(far_qa, "seq", 1)
        near_qb = trade(far_qb, "seq", 1)
        (gain_far,) = gate((gain_far,), (far_qb,))
        gain_near = trade(jnp.stack([low_gains, gain_far]), "seq", 1)
        gain_stack = jnp.stack([low_gains, gain_near[0], gain_far, gain_near[1]])
        gain_low = jnp.concatenate(
            [index(gain_stack, b ^ place) for b in range(4)], axis=1
        ).astype(FULL)
        blocks_qkv = (low_qkv, near_q, far_qa, far_qb, near_qa, near_qb)
        low_in, low_od, half_in = gate((low_in, low_od, half_in), (far_qa,))
        near_i = trade(low_in, "seq", 1)
        near_o = trade(low_od, "seq", 1)
        (far_ia,) = gate((trade(half_in, "seq", 2),), weight=10 * WEIGHT)

        seg = index(segments, slot)
        positions = doc_positions(seg).reshape(4, local_len)
        seg = seg.reshape(4, local_len)
        chunks = [place, place ^ 2, place ^ 1, place ^ 3]
        seg_keys = jnp.concatenate([index(seg, c) for c in chunks])
        pos = jnp.concatenate([index(positions, c) for c in chunks[:2]])
        cos_part, sin_part = rope_tables(pos)
        lane = jnp.arange(PAIR, dtype=jnp.int32)[None] % HEAD_DIM
        same = seg_keys[:, None] == lane
        mark_key = jnp.where(lane < DOCS, 1.0 - same, (lane < DOCS + 3) * 1.0).astype(LOW)
        mark_query = jnp.where((lane < DOCS) & same[:rows], NEG_FILL, 0.0).astype(LOW)

        normed, query, kv, _ = project(
            at, tokens, far, gain_low[:1], cos_part, sin_part, blocks_qkv,
            (far_ia, mark_key, mark_query),
        )
        kv_far = trade(kv, "seq", 1)
        far_oa = trade(half_od, "seq", 2)
        far_ib = trade(far_ia, "dp", 1)
        near_ia = trade(far_ia, "seq", 1)
        pairs = width // PAIR
        early = 2
        args = (query, kv, kv_far, mark_query, mark_key)
        o_a, extra_a, done_a = attend(0, early, *args)
        far_oa, far_ib = gate((far_oa, far_ib), (done_a,), weight=10 * WEIGHT)
        (their_cot,) = gate((their_cot,), (far_oa,))
        (cot_far,) = gate((trade(their_cot, "seq", 2),), weight=WEIGHT)
        far_ob = trade(far_oa, "dp", 1)
        near_oa = trade(far_oa, "seq", 1)
        near_ib = trade(far_ib, "seq", 1)
        o_b, extra_b, done_b = attend(early, pairs - early, *args, late=(done_a, far_oa, near_ia))
        (far_ob,) = gate((far_ob,), (done_b,))
        near_ob = trade(far_ob, "seq", 1)
        blocks_in = (low_in, near_i, far_ia, far_ib, near_ia, near_ib)
        blocks_od = (low_od, near_o, far_oa, far_ob, near_oa, near_ob)

        mixed, mixed_far, dx1, do, keep_rest, send_rest, _ = middle(
            at, valid, tokens, far, cotangent, cot_far, o_a, o_b, gain_low[1:], blocks_in, blocks_od
        )
        got_rest = trade(send_rest, "seq", 1)
        two = pairs // 3
        near_args = (query, kv, kv_far)
        back_args = (mark_key, do, cos_part, sin_part)
        dq0, own0, give0, back0 = attend_back(0, 0, two, *near_args, extra_a, o_a, *back_args)
        *r1, r1_done = first_sums(at, keep_rest, got_rest, late=(back0,))
        got_ra, got_rb = gate(
            (trade(r1[1], "seq", 2), trade(r1[3], "dp", 1)), weight=10 * WEIGHT
        )
        got0 = trade(give0, "seq", 1)
        dq1, own1, give1, back1 = attend_back(
            two, two - early, two, *near_args, extra_b, o_b, *back_args, late=(r1_done,)
        )
        got1 = trade(give1, "seq", 1)
        dq2, own2, give2, back2 = attend_back(
            2 * two, 2 * two - early, pairs - 2 * two, *near_args, extra_b, o_b, *back_args,
            late=(back1, got0),
        )
        got2 = trade(give2, "seq", 1)
        dqkv, normed_t, send_qkv, send_done = qkv_send(
            at, normed, (dq0, dq1, dq2), (own0, own1, own2), (got0, got1, got2),
            cos_part, sin_part, late=(),
        )
        got_qkv = trade(send_qkv, "seq", 1)
        *r2, r2_done = second_sums(at, r1[0], got_ra, r1[2], got_rb, late=(send_done,))
        got_ra, got_rb = trade(r2[1], "dp", 1), trade(r2[3], "seq", 2)
        keep_qkv, _ = qkv_keep(at, normed_t, dqkv, late=(r2_done,))
        *q1, q1_done = first_sums(at, keep_qkv, got_qkv)
        got_qa, got_qb = trade(q1[1], "seq", 2), trade(q1[3], "dp", 1)
        grad, grad_far, grad_done = input_back(
            at, tokens, far, gain_low[:1], dx1, dqkv, blocks_qkv, late=(q1_done,)
        )
        rest, give_rest, r3_done = third_sums(
            at, r2[0], got_ra, r2[2], got_rb, late=(grad_done,)
        )
        got_rest = trade(give_rest, "dp", 2)
        *q2, q2_done = second_sums(at, q1[0], got_qa, q1[2], got_qb, late=(r3_done,))
        got_qa, got_qb = gate(
            (trade(q2[1], "dp", 1), trade(q2[3], "seq", 2)), weight=10 * WEIGHT
        )
        rest, rest_done = add((rest,), (got_rest,), late=(q2_done,))
        got_rest = trade(rest, "dp", far_bits[0])
        qkv, give_qkv, q3_done = third_sums(
            at, q2[0], got_qa, q2[2], got_qb, late=(rest_done,)
        )
        (mixed_far,) = gate((mixed_far,), (q3_done,))
        mixed_far = trade(mixed_far, "seq", 2)
        qkv, qkv_done = add((qkv,), (trade(give_qkv, "dp", 2),))
        got_qkv = trade(qkv, "dp", far_bits[0])
        rest, rest_done = add((rest,), (got_rest,), late=(qkv_done, mixed_far))
        for bit in far_bits[1:]:
            rest, rest_done = add((rest,), (trade(rest, "dp", bit),))
        (grad_far,) = gate((grad_far,), (rest_done,))
        grad_far = trade(grad_far, "seq", 2)

        beside, other = trade(rest, "dp", 2), trade(rest, "dp", 1)
        mixed, grad, fill_done = fill(at, mixed, mixed_far, grad, grad_far)
        qkv, qkv_done = add((qkv,), (got_qkv,), late=(rest_done, grad_far, beside, other))
        for bit in far_bits[1:]:
            qkv, qkv_done = add((qkv,), (trade(qkv, "dp", bit),))
        square, _ = squares(at, qkv, w_qkv, rest, w_in, gains)
        qkv_beside, qkv_other = trade(qkv, "dp", 2), trade(qkv, "dp", 1)
        rest_parts = (rest, beside, other, trade(beside, "dp", 1))
        qkv_parts = (qkv, qkv_beside, qkv_other, trade(qkv_beside, "dp", 1))
        for axis, bit, late in (
            ("seq", 2, ()),
            ("seq", 1, ()),
            ("dp", 2, (qkv_beside, rest_parts[3])),
            ("dp", 1, (qkv_other, fill_done)),
        ):
            square, _ = add((square,), (trade(square, axis, bit),), late=late)

        (new_in, first_in, second_in, new_out, first_out, second_out,
         new_down, first_down, second_down, row, _) = update_rest(
            at, square, rest_parts,
            (w_in, m_in, v_in), (w_out, m_out, v_out), (w_down, m_down, v_down), (),
        )
        (new_qkv, first_qkv, second_qkv, new_gains, first_gains, second_gains, norm, _) = (
            update_last(
                at, square, (w_qkv, m_qkv, v_qkv), qkv_parts, row, (gains, m_gains, v_gains)
            )
        )
        return (
            mixed,
            grad,
            norm[0, 0],
            new_qkv, new_out, new_in, new_down, new_gains,
            first_qkv, first_out, first_in, first_down, first_gains,
            second_qkv, second_out, second_in, second_down, second_gains,
        )

    return on_device


def solution(mesh):
    rows, matrix, gain = P("dp", "seq", None), P("seq", None), P(None, "seq")
    weights = (matrix,) * 4 + (gain,)
    return jax.shard_map(
        make(mesh.shape["dp"], mesh.shape["seq"]),
        mesh=mesh,
        in_specs=(rows, rows, P("dp", None), P("dp")) + weights * 3,
        out_specs=(rows, rows, P()) + weights * 3,
        check_vma=False,
    )
```

```python
import functools
import math

import jax
import jax.numpy as jnp
from jax import lax
from jax.experimental import pallas as pl
from jax.experimental.pallas import tpu as pltpu
from jax.sharding import PartitionSpec as P

HEADS = 12
HEAD_DIM = 64
PAIR = 2 * HEAD_DIM
STEP_COUNT = 10
EPS_NORM = 1e-05
ROPE_BASE = 160000.0
NEG_FILL = -1e30
CLIP_LIMIT = 10.0
BETA_FIRST = 0.9
BETA_SECOND = 0.98
EPS_ADAM = 1e-06
STEP_RATES = (0.1, 0.5, 0.1, 0.1, 1.0)
DECAY_RATES = (0.01, 0.01, 0.01, 0.01, 0.0)
DOCS = 5
LOW = jnp.bfloat16
FULL = jnp.float32
SCALE = 1.0 / math.sqrt(HEAD_DIM)
WEIGHT = 20_000_000_000


def doc_positions(segment_ids):
    seq_len = segment_ids.shape[-1]
    places = jnp.arange(seq_len, dtype=jnp.int32)
    first_mark = jnp.ones((1,), jnp.bool_)
    change = jnp.concatenate([first_mark, segment_ids[1:] != segment_ids[:-1]])
    starts = lax.cummax(jnp.where(change, places, 0), axis=0)
    return places - starts


def rope_tables(positions):
    half_dim = HEAD_DIM // 2
    exponents = jnp.arange(half_dim, dtype=jnp.float32) * (2.0 / HEAD_DIM)
    inv_freq = ROPE_BASE ** (-exponents)
    angles = positions.astype(jnp.float32)[:, None] * inv_freq
    cos_part, sin_part = jnp.cos(angles), jnp.sin(angles)
    return (
        jnp.concatenate([cos_part] * 4, axis=1),
        jnp.concatenate([-sin_part, sin_part] * 2, axis=1),
    )


def adam_step(weight, first_old, second_old, gradient, factor, step_rate, decay_rate):
    first_new = BETA_FIRST * first_old + ((1.0 - BETA_FIRST) * factor) * gradient
    second_new = BETA_SECOND * second_old + ((1.0 - BETA_SECOND) * factor * factor) * (
        gradient * gradient
    )
    unbias = math.sqrt(1.0 - BETA_SECOND**STEP_COUNT)
    rate = step_rate / (1.0 - BETA_FIRST**STEP_COUNT) * unbias
    step = first_new * rate / (second_new * lax.rsqrt(second_new) + EPS_ADAM * unbias)
    return (weight * (1.0 - step_rate * decay_rate) - step, first_new, second_new)


def mul(left, right):
    return lax.dot_general(left, right, (((1,), (0,)), ((), ())), preferred_element_type=FULL)


def mul_t(left, right):
    return lax.dot_general(left, right, (((1,), (1,)), ((), ())), preferred_element_type=FULL)


def normalize(values):
    centered = values - jnp.mean(values, axis=-1, keepdims=True)
    root = lax.rsqrt(jnp.mean(centered * centered, axis=-1, keepdims=True) + EPS_NORM)
    return centered * root, root


def normalize_back(grad, gain, scaled, root):
    t = grad * gain
    back = root * (
        t
        - jnp.mean(t, axis=-1, keepdims=True)
        - scaled * jnp.mean(t * scaled, axis=-1, keepdims=True)
    )
    return back


def turn(values, cos_part, sin_part):
    lane = lax.broadcasted_iota(jnp.int32, values.shape, 1)
    swapped = jnp.where(
        lane % HEAD_DIM < HEAD_DIM // 2,
        pltpu.roll(values, PAIR - HEAD_DIM // 2, 1),
        pltpu.roll(values, HEAD_DIM // 2, 1),
    )
    return values * cos_part + swapped * sin_part


def three_parts(values):
    high = values.astype(LOW).astype(FULL)
    rest = values - high
    mid = rest.astype(LOW).astype(FULL)
    return high, mid, rest - mid


def wait_all(copies):
    for copy in copies:
        copy.wait()


def put(source, target, sem):
    copy = pltpu.make_async_copy(source, target, sem)
    copy.start()
    return copy


PIECES = ((0, None), (1, None), (2, 0), (2, 1), (3, 0), (3, 1))


def join_blocks(at_ref, blocks, whole):
    rows = blocks[0].shape[0]
    for block, (bits, part) in zip(blocks, PIECES):
        start = (at_ref[0] ^ bits) * rows
        size = rows
        if part is not None:
            size = rows // 2
            start += (at_ref[1] ^ part) * size
        whole[pl.ds(pl.multiple_of(start, size), size), :] = block[...]


def join_folded(at_ref, blocks, w_out, w_down):
    rows, width = blocks[0].shape[0], w_out.shape[1]
    short, last = rows // 2, width // 2
    for block, (bits, part) in zip(blocks, PIECES):
        owner = at_ref[0] ^ bits
        base = owner * (rows + short)
        first = 0 if part is None else (at_ref[1] ^ part) * short
        size = rows if part is None else short
        span = pl.ds(pl.multiple_of(owner * rows + first, short), size)
        w_out[span, :] = block[:, :width]
        span = pl.ds(pl.multiple_of(base + first, short), size)
        w_down[span, :] = block[:, width : 2 * width]
        span = pl.ds(pl.multiple_of(base + rows, short), short)
        if part is None:
            for i in range(2):
                w_down[span, i * last : (i + 1) * last] = block[
                    i * short : (i + 1) * short, 2 * width :
                ]
        else:
            lanes = pl.ds(pl.multiple_of((at_ref[1] ^ part) * last, last), last)
            w_down[span, lanes] = block[:, 2 * width :]


def fold(out, w_out, w_down, first):
    rows, width = w_out.shape
    short, last = rows // 2, width // 2
    out[:, first : first + width] = w_out[...].astype(LOW)
    out[:, first + width : first + 2 * width] = w_down[:rows, :].astype(LOW)
    for i in range(2):
        out[i * short : (i + 1) * short, first + 2 * width :] = w_down[
            rows:, i * last : (i + 1) * last
        ].astype(LOW)


def prepare_first_kernel(at_ref, w_ref, gains_ref, half_ref, gains_out, wide, sem):
    short = half_ref.shape[0]
    span = pl.ds(pl.multiple_of(at_ref[1] * short, short), short)
    copy = put(w_ref.at[span, :], wide, sem.at[0])
    gains_out[...] = gains_ref[...].astype(LOW)
    copy.wait()
    half_ref[...] = wide[...].astype(LOW)


def prepare_rest_kernel(at_ref, tokens_ref, in_ref, out_ref, down_ref, qkv_ref, cot_ref,
                        their_tokens, low_in, part_in, low_od, part_od, low_qkv, their_cot,
                        in_wide, out_wide, down_wide, qkv_wide, sem):
    slot = 1 - at_ref[2]
    copies = [
        put(source, target, sem.at[i])
        for i, (source, target) in enumerate((
            (tokens_ref.at[slot], their_tokens), (in_ref, in_wide), (out_ref, out_wide),
            (down_ref, down_wide), (qkv_ref, qkv_wide), (cot_ref.at[slot], their_cot),
        ))
    ]
    short = part_in.shape[0]
    span = pl.ds(pl.multiple_of((2 * at_ref[1] + at_ref[4]) * short, short), short)
    copies[1].wait()
    part_in[...] = in_wide[span, :].astype(LOW)
    low_in[...] = in_wide[...].astype(LOW)
    copies[2].wait()
    copies[3].wait()
    fold(low_od, out_wide, down_wide, 0)
    part_od[...] = low_od[span, :]
    copies[4].wait()
    low_qkv[...] = qkv_wide[...].astype(LOW)
    copies[0].wait()
    copies[5].wait()


def project_kernel(at_ref, tokens_ref, far_ref, gain_ref, cos_ref, sin_ref, w0, w1, w2, w3, w4, w5,
                   normed_ref, query_ref, kv_ref, weight):
    join_blocks(at_ref, (w0, w1, w2, w3, w4, w5), weight)
    rows, width = far_ref.shape
    for part in range(2):
        values = tokens_ref[at_ref[2]] if part == 0 else far_ref[...]
        scaled, _ = normalize(values.astype(FULL))
        normed_ref[pl.ds(part * rows, rows), :] = (scaled * gain_ref[...]).astype(LOW)
    for part in range(2):
        span = pl.ds(part * rows, rows)
        normed = normed_ref[span, :]
        cos_part, sin_part = cos_ref[span, :], sin_ref[span, :]
        for pair in range(2 * width // PAIR):
            lanes = pl.ds(pair * PAIR, PAIR)
            if pair % 2 == 0:
                both = mul(normed, weight[:, pl.ds(pair * PAIR, 2 * PAIR)])
            raw = both[:, (pair % 2) * PAIR : (pair % 2 + 1) * PAIR]
            turned = turn(raw, cos_part, sin_part)
            if pair < width // PAIR:
                query_ref[span, lanes] = (turned * SCALE).astype(LOW)
            else:
                kv_ref[0, span, pl.ds(pair * PAIR - width, PAIR)] = turned.astype(LOW)
        kv_ref[1, span, :] = mul(normed, weight[:, 2 * width :]).astype(LOW)


def head_lanes(head, shape):
    lane = lax.broadcasted_iota(jnp.int32, shape, 1)
    return (lane < HEAD_DIM) if head == 0 else (lane >= HEAD_DIM)


def pick(head, inside, outside):
    return jnp.where(head_lanes(head, inside.shape), inside, outside)


def attend_kernel(query_ref, near_ref, far_ref, mark_query_ref, mark_key_ref, o_ref, extra_ref):
    rows = query_ref.shape[0]
    query = query_ref[...]
    mark_query = mark_query_ref[...]
    parts = [
        (near_ref[0], jnp.transpose(near_ref[1]), mark_key_ref[:rows, :]),
        (far_ref[0], jnp.transpose(far_ref[1]), mark_key_ref[rows:, :]),
    ]
    outs, logs = [], []
    for head in range(2):
        query_head = pick(head, query, mark_query)
        scores = [mul_t(pick(head, key, mark), query_head) for key, _, mark in parts]
        top = jnp.maximum(
            jnp.max(scores[0], axis=0, keepdims=True), jnp.max(scores[1], axis=0, keepdims=True)
        )
        exps = [jnp.exp(score - top) for score in scores]
        total = jnp.sum(exps[0], axis=0, keepdims=True) + jnp.sum(exps[1], axis=0, keepdims=True)
        span = slice(head * HEAD_DIM, (head + 1) * HEAD_DIM)
        out = sum(mul(value_t[span], e.astype(LOW)) for (_, value_t, _), e in zip(parts, exps))
        outs.append(out / total)
        logs.append(top + jnp.log(total))
    o_ref[...] = jnp.transpose(jnp.concatenate(outs)).astype(LOW)
    line = lax.broadcasted_iota(jnp.int32, (PAIR, rows), 0)
    extra = jnp.zeros((PAIR, rows), FULL)
    for head in range(2):
        base = DOCS + (HEAD_DIM if head == 0 else 0)
        for i, piece in enumerate(three_parts(-logs[head])):
            extra = jnp.where(line == base + i, piece, extra)
    extra_ref[...] = jnp.transpose(extra).astype(LOW) + mark_query


def attend_back_kernel(query_ref, near_ref, far_ref, extra_ref, mark_key_ref, o_ref, do_ref,
                       cos_ref, sin_ref, dq_ref, keep_ref, send_ref):
    rows = query_ref.shape[0]
    query, extra, do = query_ref[...], extra_ref[...], do_ref[...]
    inner_all = do.astype(FULL) * o_ref[...].astype(FULL)
    lane = lax.broadcasted_iota(jnp.int32, (rows, PAIR), 1)
    zero = jnp.zeros((rows, PAIR), LOW)
    grads_query = []
    sums = [[None, None], [None, None]]
    keys_t = [jnp.transpose(near_ref[0]), jnp.transpose(far_ref[0])]
    for head in range(2):
        inside = head_lanes(head, (rows, PAIR))
        inner = jnp.sum(jnp.where(inside, inner_all, 0.0), axis=1, keepdims=True)
        base = DOCS + (HEAD_DIM if head == 0 else 0)
        tail = jnp.zeros((rows, PAIR), FULL)
        for i, piece in enumerate(three_parts(-inner)):
            tail = jnp.where(lane == base + i, piece, tail)
        query_head = pick(head, query, extra)
        do_head = pick(head, do, tail.astype(LOW))
        query_only = pick(head, query, zero)
        do_only = pick(head, do, zero)
        span = slice(head * HEAD_DIM, (head + 1) * HEAD_DIM)
        grad_query = 0.0
        for part, ref in enumerate((near_ref, far_ref)):
            mark = mark_key_ref[pl.ds(part * rows, rows), :]
            probs = jnp.exp(mul_t(pick(head, ref[0], mark), query_head))
            grad_probs = mul_t(pick(head, ref[1], mark), do_head)
            grad_scores = (probs * grad_probs).astype(LOW)
            grad_value = mul(probs.astype(LOW), do_only)
            grad_key = mul(grad_scores, query_only)
            grad_query += mul(keys_t[part][span], grad_scores)
            if head == 0:
                sums[part] = [grad_key, grad_value]
            else:
                sums[part] = [sums[part][0] + grad_key, sums[part][1] + grad_value]
        grads_query.append(grad_query)
    turned = turn(
        jnp.transpose(jnp.concatenate(grads_query)) * SCALE, cos_ref[...], -sin_ref[...]
    )
    dq_ref[...] = turned.astype(LOW)
    for i in range(2):
        keep_ref[i] = sums[0][i].astype(LOW)
        send_ref[i] = sums[1][i].astype(LOW)


def middle_kernel(at_ref, live_ref, tokens_ref, far_ref, cot_ref, cot_far_ref,
                  oa_ref, ob_ref, oc_ref, gain_ref, i0, i1, i2, i3, i4, i5, d0, d1, d2, d3, d4, d5,
                  mixed_ref, mixed_far_ref, dx1_ref, do_ref, keep_ref, send_ref,
                  w_out, w_in, w_down, o_all, o_t, a2_t, h_t, dm_all, duw_all, db_all,
                  mixed, dx1_all, do_all, keep, send, out_sem):
    place, slot = at_ref[0], at_ref[2]
    live = live_ref[slot].astype(FULL)
    join_folded(at_ref, (d0, d1, d2, d3, d4, d5), w_out, w_down)
    join_blocks(at_ref, (i0, i1, i2, i3, i4, i5), w_in)
    rows, width = far_ref.shape
    share = width // 4
    short, units = share // 2, w_down.shape[0]
    gain = gain_ref[...]
    first = 0
    for ref in (oa_ref, ob_ref, oc_ref):
        o_all[:, first : first + ref.shape[1]] = ref[...]
        first += ref.shape[1]
    copies = []
    for part in range(2):
        span = pl.ds(part * rows, rows)
        o = o_all[span, :]
        values = tokens_ref[slot] if part == 0 else far_ref[...]
        x1 = values.astype(FULL) + live * mul(o, w_out[...])
        scaled, root = normalize(x1)
        a2 = (scaled * gain).astype(LOW)
        u = mul(a2, w_in[:, :units])
        w = mul(a2, w_in[:, units:])
        phi = 0.5 * (1.0 + lax.erf(u * math.sqrt(0.5)))
        gelu = u * phi
        h = (gelu * w).astype(LOW)
        mixed[span, :] = (x1 + live * mul(h, w_down[...])).astype(LOW)
        target = mixed_ref.at[slot] if part == 0 else mixed_far_ref
        copies.append(put(mixed.at[span, :], target, out_sem.at[len(copies)]))
        cot = (cot_ref[slot] if part == 0 else cot_far_ref[...]).astype(FULL)
        dm = (live * cot).astype(LOW)
        dh = mul_t(dm, w_down[...])
        slope = phi + u * (jnp.exp(-0.5 * u * u) * (1.0 / math.sqrt(2.0 * math.pi)))
        duw_all[span, :units] = (dh * w * slope).astype(LOW)
        duw_all[span, units:] = (dh * gelu).astype(LOW)
        da2 = mul_t(duw_all[span, :], w_in[...])
        dx1 = cot + normalize_back(da2, gain, scaled, root)
        dx1_all[span, :] = dx1
        copies.append(put(dx1_all.at[span, :], dx1_ref.at[span, :], out_sem.at[len(copies)]))
        db = (live * dx1).astype(LOW)
        do_all[span, :] = mul_t(db, w_out[...]).astype(LOW)
        copies.append(put(do_all.at[span, :], do_ref.at[span, :], out_sem.at[len(copies)]))
        db_all[span, :] = db
        dm_all[span, :] = dm
        o_t[:, span] = jnp.transpose(o)
        a2_t[:, span] = jnp.transpose(a2)
        h_t[:, span] = jnp.transpose(h)
    dm, duw, db = dm_all[...], duw_all[...], db_all[...]
    for j, out, target in ((1, send, send_ref), (3, send, send_ref), (0, keep, keep_ref), (2, keep, keep_ref)):
        span = pl.ds(pl.multiple_of((place ^ j) * share, share), share)
        base = (place ^ j) * (share + short)
        down = pl.ds(pl.multiple_of(base, short), share)
        down_last = pl.ds(pl.multiple_of(base + share, short), short)
        at = 2 * units
        out[j // 2, :, :at] = mul(a2_t[span, :], duw).astype(LOW)
        out[j // 2, :, at : at + width] = mul(o_t[span, :], db).astype(LOW)
        at += width
        out[j // 2, :, at : at + width] = mul(h_t[down, :], dm).astype(LOW)
        at += width
        last = mul(h_t[down_last, :], dm).astype(LOW)
        out[j // 2, :short, at:] = last[:, : width // 2]
        out[j // 2, short:, at:] = last[:, width // 2 :]
        copies.append(put(out.at[j // 2], target.at[j // 2], out_sem.at[len(copies)]))
    wait_all(copies)


def send_kernel(count, at_ref, *refs):
    normed_ref = refs[0]
    dqs, owns, gots = (refs[1 + i * count : 1 + (i + 1) * count] for i in range(3))
    (cos_ref, sin_ref, dqkv_ref, normed_t_ref, send_ref,
     dqkv, normed_t, send, sem) = refs[1 + 3 * count :]
    width = normed_ref.shape[1]
    part_width = width // count
    normed_t[...] = jnp.transpose(normed_ref[...])
    copies = [put(normed_t, normed_t_ref, sem.at[0])]
    cos_part, sin_part = cos_ref[...], -sin_ref[...]
    for part, (dq, own, got) in enumerate(zip(dqs, owns, gots)):
        base = part * part_width
        dqkv[:, pl.ds(base, part_width)] = dq[...]
        dqkv[:, pl.ds(2 * width + base, part_width)] = (
            own[1].astype(FULL) + got[1].astype(FULL)
        ).astype(LOW)
        for pair in range(part_width // PAIR):
            lanes = pl.ds(pair * PAIR, PAIR)
            raw = own[0, :, lanes].astype(FULL) + got[0, :, lanes].astype(FULL)
            dqkv[:, pl.ds(width + base + pair * PAIR, PAIR)] = turn(raw, cos_part, sin_part).astype(
                LOW
            )
    copies.append(put(dqkv, dqkv_ref, sem.at[1]))
    right = dqkv[...]
    share = send.shape[1]
    for j in (1, 3):
        start = pl.multiple_of((at_ref[0] ^ j) * share, share)
        send[j // 2] = mul(normed_t[pl.ds(start, share), :], right).astype(LOW)
        copies.append(put(send.at[j // 2], send_ref.at[j // 2], sem.at[len(copies)]))
    wait_all(copies)


def keep_kernel(at_ref, normed_t_ref, dqkv_ref, keep_ref, keep, sem):
    right = dqkv_ref[...]
    share = keep.shape[1]
    copies = []
    for j in (0, 2):
        start = pl.multiple_of((at_ref[0] ^ j) * share, share)
        keep[j // 2] = mul(normed_t_ref[pl.ds(start, share), :], right).astype(LOW)
        copies.append(put(keep.at[j // 2], keep_ref.at[j // 2], sem.at[len(copies)]))
    wait_all(copies)


def input_kernel(at_ref, tokens_ref, far_ref, gain_ref, dx1_ref, dqkv_ref, w0, w1, w2, w3, w4, w5,
                 grad_ref, grad_far_ref, weight, grad_own, out_sem):
    join_blocks(at_ref, (w0, w1, w2, w3, w4, w5), weight)
    rows = far_ref.shape[0]
    gain = gain_ref[...]
    for part in (1, 0):
        span = pl.ds(part * rows, rows)
        values = tokens_ref[at_ref[2]] if part == 0 else far_ref[...]
        scaled, root = normalize(values.astype(FULL))
        back = normalize_back(mul_t(dqkv_ref[span, :], weight[...]), gain, scaled, root)
        grad = dx1_ref[span, :] + back
        if part == 1:
            grad_far_ref[...] = grad.astype(LOW)
        else:
            grad_own[...] = grad
    put(grad_own, grad_ref.at[at_ref[2]], out_sem.at[0]).wait()


def shaped(*shape, kind=LOW):
    return jax.ShapeDtypeStruct(shape, kind)


IN_SMEM = pl.BlockSpec(memory_space=pltpu.SMEM)
IN_VMEM = pl.BlockSpec(memory_space=pltpu.VMEM)
IN_ANY = pl.BlockSpec(memory_space=pl.ANY)


def params(mebibytes):
    return pltpu.CompilerParams(vmem_limit_bytes=int(mebibytes * 1024 * 1024))


def call(kernel, args, in_specs, out_shape, out_specs, late=(), **options):
    if not isinstance(out_shape, tuple):
        out_shape, out_specs = (out_shape,), (out_specs,)
    count, skip, outs = len(args), len(late), len(out_shape)

    def body(*refs):
        outs_at = count + skip
        return kernel(*refs[:count], *refs[outs_at : outs_at + outs], *refs[outs_at + outs + 1 :])

    return pl.pallas_call(
        body,
        in_specs=list(in_specs) + [IN_ANY] * skip,
        out_shape=out_shape + (shaped(8, 128, kind=FULL),),
        out_specs=out_specs + (IN_ANY,),
        **options,
    )(*args, *late)


def gate(values, late=(), weight=0):
    hint = {}
    if weight:
        hint["cost_estimate"] = pl.CostEstimate(
            flops=weight, transcendentals=0, bytes_accessed=0
        )
    return call(
        lambda *refs: None,
        values,
        late=late,
        out_shape=tuple(jax.ShapeDtypeStruct(v.shape, v.dtype) for v in values),
        in_specs=[IN_ANY] * len(values),
        out_specs=(IN_ANY,) * len(values),
        input_output_aliases={i: i for i in range(len(values))},
        compiler_params=params(1),
        name="gate",
        **hint,
    )[: len(values)]


def join_two_kernel(at_ref, mine, other, out):
    short = mine.shape[0]
    out[pl.ds(pl.multiple_of(at_ref[4] * short, short), short), :] = mine[...]
    out[pl.ds(pl.multiple_of((1 - at_ref[4]) * short, short), short), :] = other[...]


def join_two(at, mine, other, late=()):
    rows, width = mine.shape
    return call(
        join_two_kernel,
        (at, mine, other),
        late=late,
        out_shape=shaped(2 * rows, width),
        in_specs=[IN_SMEM] + [IN_VMEM] * 2,
        out_specs=IN_VMEM,
        compiler_params=params(4),
        name="join_two",
    )


def in_hbm(value):
    return pltpu.with_memory_space_constraint(value, pltpu.HBM)


def in_vmem(*values):
    return [pltpu.with_memory_space_constraint(value, pltpu.VMEM) for value in values]


def prepare_first(at, weight, gains):
    rows, width = weight.shape
    return call(
        prepare_first_kernel,
        (at, in_hbm(weight), gains),
        out_shape=(shaped(rows // 2, width), shaped(*gains.shape)),
        in_specs=[IN_SMEM, IN_ANY, IN_VMEM],
        out_specs=(IN_VMEM,) * 2,
        scratch_shapes=[pltpu.VMEM((rows // 2, width), FULL), pltpu.SemaphoreType.DMA((1,))],
        compiler_params=params(6),
        name="prepare_first",
    )


def prepare_rest(at, tokens, w_in, w_out, w_down, w_qkv, cotangent, late):
    rows, width = w_out.shape
    folded = 2 * width + width // 2
    return call(
        prepare_rest_kernel,
        (at, *[in_hbm(v) for v in (tokens, w_in, w_out, w_down, w_qkv, cotangent)]),
        late=late,
        out_shape=(
            shaped(*tokens.shape[1:]),
            shaped(*w_in.shape),
            shaped(rows // 4, w_in.shape[1]),
            shaped(rows, folded),
            shaped(rows // 4, folded),
            shaped(*w_qkv.shape),
            shaped(*cotangent.shape[1:]),
        ),
        in_specs=[IN_SMEM] + [IN_ANY] * 6,
        out_specs=(IN_VMEM,) * 7,
        scratch_shapes=[
            pltpu.VMEM(v.shape, FULL) for v in (w_in, w_out, w_down, w_qkv)
        ] + [pltpu.SemaphoreType.DMA((6,))],
        compiler_params=params(18),
        name="prepare_rest",
    )


def project(at, tokens, far, gain, cos_part, sin_part, blocks, late):
    rows, width = 2 * far.shape[0], far.shape[1]
    return call(
        project_kernel,
        (at, tokens, *in_vmem(far), gain, cos_part, sin_part, *in_vmem(*blocks)),
        late=late,
        out_shape=(shaped(rows, width), shaped(rows, width), shaped(2, rows, width)),
        in_specs=[IN_SMEM] + [IN_VMEM] * 11,
        out_specs=(IN_VMEM,) * 3,
        scratch_shapes=[pltpu.VMEM((width, 3 * width), LOW)],
        compiler_params=params(18),
        name="project",
    )


def attend(first, count, query, near, far, mark_query, mark_key, late=()):
    rows = query.shape[0]
    row_spec = pl.BlockSpec((rows, PAIR), lambda i: (0, i + first))
    kv_spec = pl.BlockSpec((2, rows, PAIR), lambda i: (0, 0, i + first))
    out_spec = pl.BlockSpec((rows, PAIR), lambda i: (0, i))
    return call(
        attend_kernel,
        (*in_vmem(query, near, far), mark_query, mark_key),
        late=late,
        grid=(count,),
        out_shape=(shaped(rows, count * PAIR), shaped(rows, count * PAIR)),
        in_specs=[
            row_spec,
            kv_spec,
            kv_spec,
            pl.BlockSpec((rows, PAIR), lambda i: (0, 0)),
            pl.BlockSpec((2 * rows, PAIR), lambda i: (0, 0)),
        ],
        out_specs=(out_spec, out_spec),
        compiler_params=params(16),
        name="attend",
    )


def attend_back(
    first, first_o, count, query, near, far, extra, o, mark_key, do, cos_part, sin_part, late=()
):
    rows = query.shape[0]
    row_spec = pl.BlockSpec((rows, PAIR), lambda i: (0, i + first))
    o_spec = pl.BlockSpec((rows, PAIR), lambda i: (0, i + first_o))
    kv_spec = pl.BlockSpec((2, rows, PAIR), lambda i: (0, 0, i + first))
    fixed = pl.BlockSpec((rows, PAIR), lambda i: (0, 0))
    out_row = pl.BlockSpec((rows, PAIR), lambda i: (0, i))
    out_kv = pl.BlockSpec((2, rows, PAIR), lambda i: (0, 0, i))
    return call(
        attend_back_kernel,
        (*in_vmem(query, near, far, extra), mark_key, *in_vmem(o, do), cos_part, sin_part),
        late=late,
        grid=(count,),
        out_shape=(
            shaped(rows, count * PAIR),
            shaped(2, rows, count * PAIR),
            shaped(2, rows, count * PAIR),
        ),
        in_specs=[
            row_spec,
            kv_spec,
            kv_spec,
            o_spec,
            pl.BlockSpec((2 * rows, PAIR), lambda i: (0, 0)),
            o_spec,
            row_spec,
            fixed,
            fixed,
        ],
        out_specs=(out_row, out_kv, out_kv),
        compiler_params=params(20),
        name="attend_back",
    )


def middle(at, live, tokens, far, cot, cot_far, o_parts, gain, blocks_in, blocks_od):
    half, width = far.shape
    rows, share = 2 * half, width // 4
    units = blocks_in[0].shape[1] // 2
    total = 2 * units + blocks_od[0].shape[1]
    assert units == 4 * (share + share // 2)
    low = lambda *shape: pltpu.VMEM(shape, LOW)
    return call(
        middle_kernel,
        (at, live, tokens, *in_vmem(far), cot, *in_vmem(cot_far, *o_parts), gain,
         *in_vmem(*blocks_in, *blocks_od)),
        out_shape=(
            shaped(2, half, width),
            shaped(half, width),
            shaped(rows, width, kind=FULL),
            shaped(rows, width),
            shaped(2, share, total),
            shaped(2, share, total),
        ),
        in_specs=[IN_SMEM] * 2 + [IN_VMEM] * 20,
        out_specs=(IN_ANY,) * 6,
        scratch_shapes=[
            low(width, width),
            low(width, 2 * units),
            low(units, width),
            low(rows, width),
            low(width, rows),
            low(width, rows),
            low(units, rows),
            low(rows, width),
            low(rows, 2 * units),
            low(rows, width),
            low(rows, width),
            pltpu.VMEM((rows, width), FULL),
            low(rows, width),
            low(2, share, total),
            low(2, share, total),
            pltpu.SemaphoreType.DMA((10,)),
        ],
        compiler_params=params(44),
        name="middle",
    )


def qkv_send(at, normed, dq, own, got, cos_part, sin_part, late):
    rows, width = normed.shape
    share = width // 4
    return call(
        functools.partial(send_kernel, len(dq)),
        (at, normed, *dq, *own, *got, cos_part, sin_part),
        late=late,
        out_shape=(
            shaped(rows, 3 * width),
            shaped(width, rows),
            shaped(2, share, 3 * width),
        ),
        in_specs=[IN_SMEM] + [IN_VMEM] * (3 + 3 * len(dq)),
        out_specs=(IN_ANY,) * 3,
        scratch_shapes=[
            pltpu.VMEM((rows, 3 * width), LOW),
            pltpu.VMEM((width, rows), LOW),
            pltpu.VMEM((2, share, 3 * width), LOW),
            pltpu.SemaphoreType.DMA((4,)),
        ],
        compiler_params=params(20),
        name="qkv_send",
    )


def qkv_keep(at, normed_t, dqkv, late):
    width, rows = normed_t.shape
    share = width // 4
    return call(
        keep_kernel,
        (at, normed_t, dqkv),
        late=late,
        out_shape=shaped(2, share, 3 * width),
        in_specs=[IN_SMEM] + [IN_VMEM] * 2,
        out_specs=IN_ANY,
        scratch_shapes=[
            pltpu.VMEM((2, share, 3 * width), LOW),
            pltpu.SemaphoreType.DMA((2,)),
        ],
        compiler_params=params(16),
        name="qkv_keep",
    )


def input_back(at, tokens, far, gain, dx1, dqkv, blocks, late):
    half, width = far.shape
    return call(
        input_kernel,
        (at, tokens, far, gain, dx1, *in_vmem(dqkv, *blocks)),
        late=late,
        out_shape=(shaped(2, half, width, kind=FULL), shaped(half, width)),
        in_specs=[IN_SMEM] + [IN_VMEM] * 11,
        out_specs=(IN_ANY, IN_VMEM),
        scratch_shapes=[
            pltpu.VMEM((width, 3 * width), LOW),
            pltpu.VMEM((half, width), FULL),
            pltpu.SemaphoreType.DMA((1,)),
        ],
        compiler_params=params(20),
        name="input_back",
    )


def first_sums_kernel(at_ref, keep, got, own_a, far_a, mine_b, give_b):
    cut, short = far_a.shape[0], give_b.shape[1]

    def add(block, start, size):
        span = pl.ds(start, size)
        return (keep[block, span, :].astype(FULL) + got[block, span, :].astype(FULL)).astype(LOW)

    far_a[...] = add(1, 0, cut)
    for block in range(2):
        give_b[block] = add(block, pl.multiple_of(cut + (1 - at_ref[1]) * short, short), short)
        mine_b[block] = add(block, pl.multiple_of(cut + at_ref[1] * short, short), short)
    own_a[...] = add(0, 0, cut)


def first_sums(at, keep, got, late=()):
    _, rows, width = keep.shape
    cut, short = rows // 2, rows // 4
    return call(
        first_sums_kernel,
        (at, keep, got),
        late=late,
        out_shape=(shaped(cut, width),) * 2 + (shaped(2, short, width),) * 2,
        in_specs=[IN_SMEM] + [IN_VMEM] * 2,
        out_specs=(IN_VMEM,) * 4,
        compiler_params=params(20),
        name="first_sums",
    )


def second_sums_kernel(at_ref, own_a, got_a, mine_b, got_b, mine_a, give_a, near_b, far_b):
    short = mine_a.shape[0]
    for start, out in ((1 - at_ref[1], give_a), (at_ref[1], mine_a)):
        span = pl.ds(pl.multiple_of(start * short, short), short)
        out[...] = (own_a[span, :].astype(FULL) + got_a[span, :].astype(FULL)).astype(LOW)
    for block, out in ((1, far_b), (0, near_b)):
        out[...] = (mine_b[block].astype(FULL) + got_b[block].astype(FULL)).astype(LOW)


def second_sums(at, own_a, got_a, mine_b, got_b, late=()):
    _, short, width = mine_b.shape
    return call(
        second_sums_kernel,
        (at, own_a, got_a, mine_b, got_b),
        late=late,
        out_shape=(shaped(short, width),) * 4,
        in_specs=[IN_SMEM] + [IN_VMEM] * 4,
        out_specs=(IN_VMEM,) * 4,
        compiler_params=params(12),
        name="second_sums",
    )


def third_sums_kernel(at_ref, mine_a, got_a, near_b, got_b, keep, give):
    upper = mine_a[...].astype(FULL) + got_a[...].astype(FULL)
    lower = near_b[...].astype(FULL) + got_b[...].astype(FULL)
    keep[...] = jnp.where(at_ref[4] == 0, upper, lower).astype(LOW)
    give[...] = jnp.where(at_ref[4] == 0, lower, upper).astype(LOW)


def third_sums(at, mine_a, got_a, near_b, got_b, late=()):
    return call(
        third_sums_kernel,
        (at, mine_a, got_a, near_b, got_b),
        late=late,
        out_shape=(shaped(*mine_a.shape),) * 2,
        in_specs=[IN_SMEM] + [IN_VMEM] * 4,
        out_specs=(IN_VMEM,) * 2,
        compiler_params=params(12),
        name="third_sums",
    )


def squares_kernel(at_ref, qkv, w_qkv, rest, w_in, gains, out):
    inner = w_in.shape[1]
    total = jnp.sum(jnp.square(rest[:, inner:].astype(FULL)), keepdims=True)
    rows = qkv.shape[0]
    shape = (rows, gains.shape[1])
    offset = lax.broadcasted_iota(jnp.int32, shape, 1) - lax.broadcasted_iota(jnp.int32, shape, 0)
    for i, (piece, weight) in enumerate(((qkv, w_qkv), (rest, w_in))):
        start = at_ref[3]
        span = pl.ds(pl.multiple_of(start, 8), rows)
        values = piece[:, : weight.shape[1]].astype(FULL)
        sums = jnp.sum(weight[span, :].astype(LOW).astype(FULL) * values, axis=1, keepdims=True)
        gain = gains[i : i + 1, :].astype(LOW).astype(FULL)
        gain = jnp.sum(jnp.where(offset == start, gain, 0.0), axis=1, keepdims=True)
        total += jnp.sum(jnp.square(values), keepdims=True)
        total += jnp.sum(jnp.square(sums / gain), keepdims=True)
    out[...] = jnp.broadcast_to(total, out.shape)


def squares(*args):
    return call(
        squares_kernel,
        args,
        out_shape=shaped(8, 128, kind=FULL),
        in_specs=[IN_SMEM] + [IN_VMEM] * (len(args) - 1),
        out_specs=IN_VMEM,
        compiler_params=params(10),
        name="squares",
    )


def add_kernel(count, *refs):
    for i in range(count):
        out = refs[2 * count + i]
        out[...] = (refs[i][...].astype(FULL) + refs[count + i][...].astype(FULL)).astype(out.dtype)


def add(first, second, late=()):
    count = len(first)
    return call(
        functools.partial(add_kernel, count),
        (*first, *second),
        late=late,
        out_shape=tuple(jax.ShapeDtypeStruct(v.shape, v.dtype) for v in first),
        in_specs=[IN_VMEM] * (2 * count),
        out_specs=(IN_VMEM,) * count,
        compiler_params=params(8),
        name="add",
    )


def fill_kernel(at_ref, mixed_far, grad_far, mixed_in, grad_in, mixed, grad, wide, sem):
    first = put(mixed_far, mixed.at[1 - at_ref[2]], sem.at[0])
    wide[...] = grad_far[...].astype(FULL)
    put(wide, grad.at[1 - at_ref[2]], sem.at[1]).wait()
    first.wait()


def fill(at, mixed, mixed_far, grad, grad_far):
    return call(
        fill_kernel,
        (at, mixed_far, grad_far, mixed, grad),
        out_shape=(shaped(*mixed.shape), shaped(*grad.shape, kind=FULL)),
        in_specs=[IN_SMEM, IN_VMEM, IN_VMEM, IN_ANY, IN_ANY],
        out_specs=(IN_ANY,) * 2,
        input_output_aliases={3: 0, 4: 1},
        scratch_shapes=[pltpu.VMEM(grad_far.shape, FULL), pltpu.SemaphoreType.DMA((2,))],
        compiler_params=params(4),
        name="fill",
    )


def clip_factor(square_ref):
    norm = jnp.sqrt(square_ref[:1, :1])
    return jnp.minimum(1.0, CLIP_LIMIT / (norm + 1e-06))


def quarters(at_ref, parts):
    own, beside, other, other_beside = parts
    for i in range(4):
        same = at_ref[4] == i // 2
        near = jnp.where(same, own[...], beside[...])
        far = jnp.where(same, other[...], other_beside[...])
        yield jnp.where(at_ref[1] == i % 2, near, far).astype(FULL)


def gain_row(weight, gradient, start, shape):
    sums = jnp.sum(weight.astype(LOW).astype(FULL) * gradient, axis=1, keepdims=True)
    shape = (weight.shape[0], shape[1])
    offset = lax.broadcasted_iota(jnp.int32, shape, 1) - lax.broadcasted_iota(jnp.int32, shape, 0)
    return jnp.sum(jnp.where(offset == start, sums, 0.0), axis=0, keepdims=True)


class Update:
    def __init__(self, number, sources, news, targets, sem):
        self.number, self.sources, self.news, self.targets = number, sources, news, targets
        self.sem, self.out = sem, []

    def step(self, span, gradient, factor):
        weight = self.sources[0][span]
        results = adam_step(
            weight, self.sources[1][span], self.sources[2][span], gradient, factor,
            STEP_RATES[self.number], DECAY_RATES[self.number],
        )
        for result, new, target in zip(results, self.news, self.targets):
            new[span] = result
            self.out.append(put(new.at[span], target.at[span], self.sem.at[len(self.out)]))
        return weight


def update_rest_kernel(at_ref, square_ref, *refs):
    parts, refs = refs[:4], refs[4:]
    sources, targets, row_ref, news, sem = refs[:9], refs[9:18], refs[18], refs[19:28], refs[28]
    inner, out, down = (
        Update(number, *(group[3 * k : 3 * k + 3] for group in (sources, news, targets)), sem.at[k])
        for k, number in enumerate((2, 1, 3))
    )
    factor = clip_factor(square_ref)
    rows, width = sources[3].shape
    lanes = sources[0].shape[1]
    short, last = rows // 4, width // 2
    row = jnp.zeros(row_ref.shape, FULL)
    for i, gradient in enumerate(quarters(at_ref, parts)):
        span = (slice(i * short, (i + 1) * short), slice(None))
        part = gradient[:, :lanes]
        row += gain_row(inner.step(span, part, factor), part, i * short, row_ref.shape)
        out.step(span, gradient[:, lanes : lanes + width], factor)
        down.step(span, gradient[:, lanes + width : lanes + 2 * width], factor)
        start = rows + (i % 2) * short
        span = (slice(start, start + short), slice((i // 2) * last, (i // 2 + 1) * last))
        down.step(span, gradient[:, lanes + 2 * width :], factor)
    row_ref[...] = row
    wait_all(inner.out + out.out + down.out)


def update_rest(at, square, parts, inner, out, down, late):
    like = [jax.ShapeDtypeStruct(v.shape, FULL) for v in (*inner, *out, *down)]
    return call(
        update_rest_kernel,
        (at, square, *parts, *inner, *out, *down),
        late=late,
        out_shape=(*like, shaped(1, inner[0].shape[0], kind=FULL)),
        in_specs=[IN_SMEM] + [IN_VMEM] * 14,
        out_specs=(IN_ANY,) * 9 + (IN_VMEM,),
        scratch_shapes=[pltpu.VMEM(v.shape, FULL) for v in like]
        + [pltpu.SemaphoreType.DMA((3, 24))],
        compiler_params=params(28),
        name="update_rest",
    )


def update_last_kernel(at_ref, square_ref, row_ref, g_w, g_m, g_v, *refs):
    parts, refs = refs[:4], refs[4:]
    sources, targets = refs[:3], refs[3:6]
    g_w_out, g_m_out, g_v_out, norm_out = refs[6:10]
    news, sem = refs[10:13], refs[13]
    qkv = Update(0, sources, news, targets, sem)
    factor = clip_factor(square_ref)
    norm_out[...] = jnp.sqrt(square_ref[...])
    short = sources[0].shape[0] // 4
    row = jnp.zeros(row_ref.shape, FULL)
    for i, gradient in enumerate(quarters(at_ref, parts)):
        span = (slice(i * short, (i + 1) * short), slice(None))
        row += gain_row(qkv.step(span, gradient, factor), gradient, i * short, row_ref.shape)
    for i, values in enumerate((row, row_ref[...])):
        line = slice(i, i + 1)
        gradient = values / g_w[line, :].astype(LOW).astype(FULL)
        g_w_out[line, :], g_m_out[line, :], g_v_out[line, :] = adam_step(
            g_w[line, :], g_m[line, :], g_v[line, :], gradient, factor,
            STEP_RATES[4], DECAY_RATES[4],
        )
    wait_all(qkv.out)


def update_last(at, square, qkv, qkv_parts, row, gains):
    like = [jax.ShapeDtypeStruct(v.shape, FULL) for v in qkv]
    return call(
        update_last_kernel,
        (at, square, row, *gains, *qkv_parts, *qkv),
        out_shape=(
            *like,
            *[jax.ShapeDtypeStruct(v.shape, FULL) for v in gains],
            jax.ShapeDtypeStruct(square.shape, FULL),
        ),
        in_specs=[IN_SMEM] + [IN_VMEM] * 12,
        out_specs=(IN_ANY,) * 3 + (IN_VMEM,) * 4,
        scratch_shapes=[pltpu.VMEM(v.shape, FULL) for v in like]
        + [pltpu.SemaphoreType.DMA((12,))],
        compiler_params=params(18),
        name="update_last",
    )


def low_sum(*values):
    return sum(value.astype(FULL) for value in values).astype(LOW)


def index(value, i):
    return lax.dynamic_index_in_dim(value, i, 0, keepdims=False)


def make(dp_count, seq_count):
    assert seq_count == 4 and dp_count >= 8 and dp_count & (dp_count - 1) == 0
    far_bits = [1 << i for i in range(2, dp_count.bit_length() - 1)]

    def trade(value, axis, bit):
        size = seq_count if axis == "seq" else dp_count
        return lax.ppermute(value, axis, [(i, i ^ bit) for i in range(size)])

    def on_device(
        tokens, cotangent, segments, valid,
        w_qkv, w_out, w_in, w_down, gains,
        m_qkv, m_out, m_in, m_down, m_gains,
        v_qkv, v_out, v_in, v_down, v_gains,
    ):
        place = lax.axis_index("seq")
        group = lax.axis_index("dp")
        slot = place >> 1
        half = group & 1
        local_len, width = tokens.shape[1:]
        rows = 2 * local_len
        share = w_qkv.shape[0]
        side = (group >> 1) & 1
        quarter = share // 4
        at = jnp.stack([place, half, slot, side * 2 * quarter + half * quarter, side])

        half_qkv, low_gains, begun = prepare_first(at, w_qkv, gains)
        (far_qa,) = gate((trade(half_qkv, "seq", 2),), weight=10 * WEIGHT)
        (gain_far,) = gate((trade(low_gains, "seq", 2),), weight=20 * WEIGHT)
        their_tokens, low_in, part_in, low_od, part_od, low_qkv, their_cot, _ = prepare_rest(
            at, tokens, w_in, w_out, w_down, w_qkv, cotangent, (begun,)
        )
        near_q = trade(low_qkv, "seq", 1)
        far = trade(their_tokens, "seq", 2)
        far_qb = trade(far_qa, "dp", 1)
        near_qa = trade(far_qa, "seq", 1)
        near_qb = trade(far_qb, "seq", 1)
        (gain_far,) = gate((gain_far,), (far_qb,))
        gain_near = trade(jnp.stack([low_gains, gain_far]), "seq", 1)
        gain_stack = jnp.stack([low_gains, gain_near[0], gain_far, gain_near[1]])
        gain_low = jnp.concatenate(
            [index(gain_stack, b ^ place) for b in range(4)], axis=1
        ).astype(FULL)
        blocks_qkv = (low_qkv, near_q, far_qa, far_qb, near_qa, near_qb)
        low_in, low_od, part_in, part_od = gate((low_in, low_od, part_in, part_od), (far_qa,))
        near_i = trade(low_in, "seq", 1)
        near_o = trade(low_od, "seq", 1)
        (come_in,) = gate((trade(part_in, "seq", 2),), weight=10 * WEIGHT)

        seg = index(segments, slot)
        positions = doc_positions(seg).reshape(4, local_len)
        seg = seg.reshape(4, local_len)
        chunks = [place, place ^ 2, place ^ 1, place ^ 3]
        seg_keys = jnp.concatenate([index(seg, c) for c in chunks])
        pos = jnp.concatenate([index(positions, c) for c in chunks[:2]])
        cos_part, sin_part = rope_tables(pos)
        lane = jnp.arange(PAIR, dtype=jnp.int32)[None] % HEAD_DIM
        same = seg_keys[:, None] == lane
        mark_key = jnp.where(lane < DOCS, 1.0 - same, (lane < DOCS + 3) * 1.0).astype(LOW)
        mark_query = jnp.where((lane < DOCS) & same[:rows], NEG_FILL, 0.0).astype(LOW)

        normed, query, kv, _ = project(
            at, tokens, far, gain_low[:1], cos_part, sin_part, blocks_qkv,
            (come_in, mark_key, mark_query),
        )
        kv_far = trade(kv, "seq", 1)
        far_ia, _ = join_two(at, come_in, trade(come_in, "dp", 2))
        (come_od,) = gate((trade(part_od, "seq", 2),), weight=10 * WEIGHT)
        far_oa, oa_done = join_two(at, come_od, trade(come_od, "dp", 2))
        far_ib = trade(far_ia, "dp", 1)
        near_ia = trade(far_ia, "seq", 1)
        near_oa = trade(far_oa, "seq", 1)
        (their_cot,) = gate((their_cot,), (come_od,))
        (cot_far,) = gate((trade(their_cot, "seq", 2),), weight=WEIGHT)
        pairs = width // PAIR
        two = pairs // 3
        args = (query, kv, kv_far, mark_query, mark_key)
        o_a, extra_a, done_a = attend(0, two, *args, late=(come_od,))
        o_b, extra_b, done_b = attend(two, two, *args, late=(done_a, oa_done))
        far_ob = trade(far_oa, "dp", 1)
        o_c, extra_c, done_c = attend(2 * two, pairs - 2 * two, *args, late=(done_b, far_ib))
        near_ib = trade(far_ib, "seq", 1)
        (far_ob,) = gate((far_ob,), (done_c,))
        near_ob = trade(far_ob, "seq", 1)
        blocks_in = (low_in, near_i, far_ia, far_ib, near_ia, near_ib)
        blocks_od = (low_od, near_o, far_oa, far_ob, near_oa, near_ob)

        mixed, mixed_far, dx1, do, keep_rest, send_rest, _ = middle(
            at, valid, tokens, far, cotangent, cot_far, (o_a, o_b, o_c), gain_low[1:], blocks_in, blocks_od
        )
        got_rest = trade(send_rest, "seq", 1)
        near_args = (query, kv, kv_far)
        back_args = (mark_key, do, cos_part, sin_part)
        dq0, own0, give0, back0 = attend_back(0, 0, two, *near_args, extra_a, o_a, *back_args)
        *r1, r1_done = first_sums(at, keep_rest, got_rest, late=(back0,))
        got_ra, got_rb = gate(
            (trade(r1[1], "seq", 2), trade(r1[3], "dp", 1)), weight=10 * WEIGHT
        )
        got0 = trade(give0, "seq", 1)
        dq1, own1, give1, back1 = attend_back(
            two, 0, two, *near_args, extra_b, o_b, *back_args, late=(r1_done,)
        )
        got1 = trade(give1, "seq", 1)
        dq2, own2, give2, back2 = attend_back(
            2 * two, 0, pairs - 2 * two, *near_args, extra_c, o_c, *back_args,
            late=(back1, got0),
        )
        got2 = trade(give2, "seq", 1)
        dqkv, normed_t, send_qkv, send_done = qkv_send(
            at, normed, (dq0, dq1, dq2), (own0, own1, own2), (got0, got1, got2),
            cos_part, sin_part, late=(),
        )
        got_qkv = trade(send_qkv, "seq", 1)
        *r2, r2_done = second_sums(at, r1[0], got_ra, r1[2], got_rb, late=(send_done,))
        got_ra, got_rb = trade(r2[1], "dp", 1), trade(r2[3], "seq", 2)
        keep_qkv, _ = qkv_keep(at, normed_t, dqkv, late=(r2_done,))
        *q1, q1_done = first_sums(at, keep_qkv, got_qkv)
        got_qa, got_qb = trade(q1[1], "seq", 2), trade(q1[3], "dp", 1)
        grad, grad_far, grad_done = input_back(
            at, tokens, far, gain_low[:1], dx1, dqkv, blocks_qkv, late=(q1_done,)
        )
        rest, give_rest, r3_done = third_sums(
            at, r2[0], got_ra, r2[2], got_rb, late=(grad_done,)
        )
        got_rest = trade(give_rest, "dp", 2)
        *q2, q2_done = second_sums(at, q1[0], got_qa, q1[2], got_qb, late=(r3_done,))
        got_qa, got_qb = gate(
            (trade(q2[1], "dp", 1), trade(q2[3], "seq", 2)), weight=10 * WEIGHT
        )
        rest, rest_done = add((rest,), (got_rest,), late=(q2_done,))
        got_rest = trade(rest, "dp", far_bits[0])
        qkv, give_qkv, q3_done = third_sums(
            at, q2[0], got_qa, q2[2], got_qb, late=(rest_done,)
        )
        (mixed_far,) = gate((mixed_far,), (q3_done,))
        mixed_far = trade(mixed_far, "seq", 2)
        qkv, qkv_done = add((qkv,), (trade(give_qkv, "dp", 2),))
        got_qkv = trade(qkv, "dp", far_bits[0])
        rest, rest_done = add((rest,), (got_rest,), late=(qkv_done, mixed_far))
        for bit in far_bits[1:]:
            rest, rest_done = add((rest,), (trade(rest, "dp", bit),))
        (grad_far,) = gate((grad_far,), (rest_done,))
        grad_far = trade(grad_far, "seq", 2)

        beside, other = trade(rest, "dp", 2), trade(rest, "dp", 1)
        mixed, grad, fill_done = fill(at, mixed, mixed_far, grad, grad_far)
        qkv, qkv_done = add((qkv,), (got_qkv,), late=(rest_done, grad_far, beside, other))
        for bit in far_bits[1:]:
            qkv, qkv_done = add((qkv,), (trade(qkv, "dp", bit),))
        square, _ = squares(at, qkv, w_qkv, rest, w_in, gains)
        square, square_done = add((square,), (trade(square, "seq", 2),))
        (qkv,) = gate((qkv,), (square_done,))
        qkv_beside, qkv_other = trade(qkv, "dp", 2), trade(qkv, "dp", 1)
        rest_parts = (rest, beside, other, trade(beside, "dp", 1))
        qkv_parts = (qkv, qkv_beside, qkv_other, trade(qkv_beside, "dp", 1))
        for axis, bit, late in (
            ("seq", 1, ()),
            ("dp", 2, (qkv_beside, rest_parts[3])),
            ("dp", 1, (qkv_other, fill_done)),
        ):
            square, _ = add((square,), (trade(square, axis, bit),), late=late)

        (new_in, first_in, second_in, new_out, first_out, second_out,
         new_down, first_down, second_down, row, _) = update_rest(
            at, square, rest_parts,
            (w_in, m_in, v_in), (w_out, m_out, v_out), (w_down, m_down, v_down), (),
        )
        (new_qkv, first_qkv, second_qkv, new_gains, first_gains, second_gains, norm, _) = (
            update_last(
                at, square, (w_qkv, m_qkv, v_qkv), qkv_parts, row, (gains, m_gains, v_gains)
            )
        )
        return (
            mixed,
            grad,
            norm[0, 0],
            new_qkv, new_out, new_in, new_down, new_gains,
            first_qkv, first_out, first_in, first_down, first_gains,
            second_qkv, second_out, second_in, second_down, second_gains,
        )

    return on_device


def solution(mesh):
    rows, matrix, gain = P("dp", "seq", None), P("seq", None), P(None, "seq")
    weights = (matrix,) * 4 + (gain,)
    return jax.shard_map(
        make(mesh.shape["dp"], mesh.shape["seq"]),
        mesh=mesh,
        in_specs=(rows, rows, P("dp", None), P("dp")) + weights * 3,
        out_specs=(rows, rows, P()) + weights * 3,
        check_vma=False,
    )
```

```python
import functools
import math

import jax
import jax.numpy as jnp
from jax import lax
from jax.experimental import pallas as pl
from jax.experimental.pallas import tpu as pltpu
from jax.sharding import PartitionSpec as P

HEADS = 12
HEAD_DIM = 64
PAIR = 2 * HEAD_DIM
STEP_COUNT = 10
EPS_NORM = 1e-05
ROPE_BASE = 160000.0
NEG_FILL = -1e30
CLIP_LIMIT = 10.0
BETA_FIRST = 0.9
BETA_SECOND = 0.98
EPS_ADAM = 1e-06
STEP_RATES = (0.1, 0.5, 0.1, 0.1, 1.0)
DECAY_RATES = (0.01, 0.01, 0.01, 0.01, 0.0)
DOCS = 5
LOW = jnp.bfloat16
FULL = jnp.float32
SCALE = 1.0 / math.sqrt(HEAD_DIM)
WEIGHT = 20_000_000_000
EARLY = 20_000_000_000


def doc_positions(segment_ids):
    seq_len = segment_ids.shape[-1]
    places = jnp.arange(seq_len, dtype=jnp.int32)
    first_mark = jnp.ones((1,), jnp.bool_)
    change = jnp.concatenate([first_mark, segment_ids[1:] != segment_ids[:-1]])
    starts = lax.cummax(jnp.where(change, places, 0), axis=0)
    return places - starts


def rope_tables(positions):
    half_dim = HEAD_DIM // 2
    exponents = jnp.arange(half_dim, dtype=jnp.float32) * (2.0 / HEAD_DIM)
    inv_freq = ROPE_BASE ** (-exponents)
    angles = positions.astype(jnp.float32)[:, None] * inv_freq
    cos_part, sin_part = jnp.cos(angles), jnp.sin(angles)
    return (
        jnp.concatenate([cos_part] * 4, axis=1),
        jnp.concatenate([-sin_part, sin_part] * 2, axis=1),
    )


def adam_step(weight, first_old, second_old, gradient, factor, step_rate, decay_rate):
    first_new = BETA_FIRST * first_old + ((1.0 - BETA_FIRST) * factor) * gradient
    second_new = BETA_SECOND * second_old + ((1.0 - BETA_SECOND) * factor * factor) * (
        gradient * gradient
    )
    unbias = math.sqrt(1.0 - BETA_SECOND**STEP_COUNT)
    rate = step_rate / (1.0 - BETA_FIRST**STEP_COUNT) * unbias
    step = first_new * rate / (second_new * lax.rsqrt(second_new) + EPS_ADAM * unbias)
    return (weight * (1.0 - step_rate * decay_rate) - step, first_new, second_new)


def mul(left, right):
    return lax.dot_general(left, right, (((1,), (0,)), ((), ())), preferred_element_type=FULL)


def mul_t(left, right):
    return lax.dot_general(left, right, (((1,), (1,)), ((), ())), preferred_element_type=FULL)


def normalize(values):
    centered = values - jnp.mean(values, axis=-1, keepdims=True)
    root = lax.rsqrt(jnp.mean(centered * centered, axis=-1, keepdims=True) + EPS_NORM)
    return centered * root, root


def normalize_back(grad, gain, scaled, root):
    t = grad * gain
    back = root * (
        t
        - jnp.mean(t, axis=-1, keepdims=True)
        - scaled * jnp.mean(t * scaled, axis=-1, keepdims=True)
    )
    return back


def turn(values, cos_part, sin_part):
    lane = lax.broadcasted_iota(jnp.int32, values.shape, 1)
    swapped = jnp.where(
        lane % HEAD_DIM < HEAD_DIM // 2,
        pltpu.roll(values, PAIR - HEAD_DIM // 2, 1),
        pltpu.roll(values, HEAD_DIM // 2, 1),
    )
    return values * cos_part + swapped * sin_part


def three_parts(values):
    high = values.astype(LOW).astype(FULL)
    rest = values - high
    mid = rest.astype(LOW).astype(FULL)
    return high, mid, rest - mid


def wait_all(copies):
    for copy in copies:
        copy.wait()


def put(source, target, sem):
    copy = pltpu.make_async_copy(source, target, sem)
    copy.start()
    return copy


PIECES = ((0, None), (1, None), (2, 0), (2, 1), (3, 0), (3, 1))


def join_blocks(at_ref, blocks, whole):
    rows = blocks[0].shape[0]
    for block, (bits, part) in zip(blocks, PIECES):
        start = (at_ref[0] ^ bits) * rows
        size = rows
        if part is not None:
            size = rows // 2
            start += (at_ref[1] ^ part) * size
        whole[pl.ds(pl.multiple_of(start, size), size), :] = block[...]


def join_folded(at_ref, blocks, w_out, w_down):
    rows, width = blocks[0].shape[0], w_out.shape[1]
    short, last = rows // 2, width // 2
    for block, (bits, part) in zip(blocks, PIECES):
        owner = at_ref[0] ^ bits
        base = owner * (rows + short)
        first = 0 if part is None else (at_ref[1] ^ part) * short
        size = rows if part is None else short
        span = pl.ds(pl.multiple_of(owner * rows + first, short), size)
        w_out[span, :] = block[:, :width]
        span = pl.ds(pl.multiple_of(base + first, short), size)
        w_down[span, :] = block[:, width : 2 * width]
        span = pl.ds(pl.multiple_of(base + rows, short), short)
        if part is None:
            for i in range(2):
                w_down[span, i * last : (i + 1) * last] = block[
                    i * short : (i + 1) * short, 2 * width :
                ]
        else:
            lanes = pl.ds(pl.multiple_of((at_ref[1] ^ part) * last, last), last)
            w_down[span, lanes] = block[:, 2 * width :]


def fold(out, w_out, w_down, first):
    rows, width = w_out.shape
    short, last = rows // 2, width // 2
    out[:, first : first + width] = w_out[...].astype(LOW)
    out[:, first + width : first + 2 * width] = w_down[:rows, :].astype(LOW)
    for i in range(2):
        out[i * short : (i + 1) * short, first + 2 * width :] = w_down[
            rows:, i * last : (i + 1) * last
        ].astype(LOW)


def prepare_first_kernel(at_ref, w_ref, gains_ref, half_ref, gains_out, wide, sem):
    short = half_ref.shape[0]
    span = pl.ds(pl.multiple_of(at_ref[1] * short, short), short)
    copy = put(w_ref.at[span, :], wide, sem.at[0])
    gains_out[...] = gains_ref[...].astype(LOW)
    copy.wait()
    half_ref[...] = wide[...].astype(LOW)


def prepare_rest_kernel(at_ref, tokens_ref, in_ref, out_ref, down_ref, qkv_ref, cot_ref,
                        their_tokens, low_in, part_in, low_od, half_od, low_qkv, their_cot,
                        in_wide, out_wide, down_wide, qkv_wide, sem):
    slot = 1 - at_ref[2]
    copies = [
        put(source, target, sem.at[i])
        for i, (source, target) in enumerate((
            (tokens_ref.at[slot], their_tokens), (in_ref, in_wide), (out_ref, out_wide),
            (down_ref, down_wide), (qkv_ref, qkv_wide), (cot_ref.at[slot], their_cot),
        ))
    ]
    short = part_in.shape[0]
    span = pl.ds(pl.multiple_of((2 * at_ref[1] + at_ref[4]) * short, short), short)
    copies[1].wait()
    part_in[...] = in_wide[span, :].astype(LOW)
    low_in[...] = in_wide[...].astype(LOW)
    copies[2].wait()
    copies[3].wait()
    fold(low_od, out_wide, down_wide, 0)
    short = half_od.shape[0]
    half_od[...] = low_od[pl.ds(pl.multiple_of(at_ref[1] * short, short), short), :]
    copies[4].wait()
    low_qkv[...] = qkv_wide[...].astype(LOW)
    copies[0].wait()
    copies[5].wait()


def project_kernel(at_ref, tokens_ref, far_ref, gain_ref, cos_ref, sin_ref, w0, w1, w2, w3, w4, w5,
                   normed_ref, query_ref, kv_ref, weight):
    join_blocks(at_ref, (w0, w1, w2, w3, w4, w5), weight)
    rows, width = far_ref.shape
    for part in range(2):
        values = tokens_ref[at_ref[2]] if part == 0 else far_ref[...]
        scaled, _ = normalize(values.astype(FULL))
        normed_ref[pl.ds(part * rows, rows), :] = (scaled * gain_ref[...]).astype(LOW)
    for part in range(2):
        span = pl.ds(part * rows, rows)
        normed = normed_ref[span, :]
        cos_part, sin_part = cos_ref[span, :], sin_ref[span, :]
        for pair in range(2 * width // PAIR):
            lanes = pl.ds(pair * PAIR, PAIR)
            if pair % 2 == 0:
                both = mul(normed, weight[:, pl.ds(pair * PAIR, 2 * PAIR)])
            raw = both[:, (pair % 2) * PAIR : (pair % 2 + 1) * PAIR]
            turned = turn(raw, cos_part, sin_part)
            if pair < width // PAIR:
                query_ref[span, lanes] = (turned * SCALE).astype(LOW)
            else:
                kv_ref[0, span, pl.ds(pair * PAIR - width, PAIR)] = turned.astype(LOW)
        kv_ref[1, span, :] = mul(normed, weight[:, 2 * width :]).astype(LOW)


def head_lanes(head, shape):
    lane = lax.broadcasted_iota(jnp.int32, shape, 1)
    return (lane < HEAD_DIM) if head == 0 else (lane >= HEAD_DIM)


def pick(head, inside, outside):
    return jnp.where(head_lanes(head, inside.shape), inside, outside)


def attend_kernel(query_ref, near_ref, far_ref, mark_query_ref, mark_key_ref, o_ref, extra_ref):
    rows = query_ref.shape[0]
    query = query_ref[...]
    mark_query = mark_query_ref[...]
    parts = [
        (near_ref[0], jnp.transpose(near_ref[1]), mark_key_ref[:rows, :]),
        (far_ref[0], jnp.transpose(far_ref[1]), mark_key_ref[rows:, :]),
    ]
    outs, logs = [], []
    for head in range(2):
        query_head = pick(head, query, mark_query)
        scores = [mul_t(pick(head, key, mark), query_head) for key, _, mark in parts]
        top = jnp.maximum(
            jnp.max(scores[0], axis=0, keepdims=True), jnp.max(scores[1], axis=0, keepdims=True)
        )
        exps = [jnp.exp(score - top) for score in scores]
        total = jnp.sum(exps[0], axis=0, keepdims=True) + jnp.sum(exps[1], axis=0, keepdims=True)
        span = slice(head * HEAD_DIM, (head + 1) * HEAD_DIM)
        out = sum(mul(value_t[span], e.astype(LOW)) for (_, value_t, _), e in zip(parts, exps))
        outs.append(out / total)
        logs.append(top + jnp.log(total))
    o_ref[...] = jnp.transpose(jnp.concatenate(outs)).astype(LOW)
    line = lax.broadcasted_iota(jnp.int32, (PAIR, rows), 0)
    extra = jnp.zeros((PAIR, rows), FULL)
    for head in range(2):
        base = DOCS + (HEAD_DIM if head == 0 else 0)
        for i, piece in enumerate(three_parts(-logs[head])):
            extra = jnp.where(line == base + i, piece, extra)
    extra_ref[...] = jnp.transpose(extra).astype(LOW) + mark_query


def attend_back_kernel(query_ref, near_ref, far_ref, extra_ref, mark_key_ref, o_ref, do_ref,
                       cos_ref, sin_ref, dq_ref, keep_ref, send_ref):
    rows = query_ref.shape[0]
    query, extra, do = query_ref[...], extra_ref[...], do_ref[...]
    inner_all = do.astype(FULL) * o_ref[...].astype(FULL)
    lane = lax.broadcasted_iota(jnp.int32, (rows, PAIR), 1)
    zero = jnp.zeros((rows, PAIR), LOW)
    grads_query = []
    sums = [[None, None], [None, None]]
    keys_t = [jnp.transpose(near_ref[0]), jnp.transpose(far_ref[0])]
    for head in range(2):
        inside = head_lanes(head, (rows, PAIR))
        inner = jnp.sum(jnp.where(inside, inner_all, 0.0), axis=1, keepdims=True)
        base = DOCS + (HEAD_DIM if head == 0 else 0)
        tail = jnp.zeros((rows, PAIR), FULL)
        for i, piece in enumerate(three_parts(-inner)):
            tail = jnp.where(lane == base + i, piece, tail)
        query_head = pick(head, query, extra)
        do_head = pick(head, do, tail.astype(LOW))
        query_only = pick(head, query, zero)
        do_only = pick(head, do, zero)
        span = slice(head * HEAD_DIM, (head + 1) * HEAD_DIM)
        grad_query = 0.0
        for part, ref in enumerate((near_ref, far_ref)):
            mark = mark_key_ref[pl.ds(part * rows, rows), :]
            probs = jnp.exp(mul_t(pick(head, ref[0], mark), query_head))
            grad_probs = mul_t(pick(head, ref[1], mark), do_head)
            grad_scores = (probs * grad_probs).astype(LOW)
            grad_value = mul(probs.astype(LOW), do_only)
            grad_key = mul(grad_scores, query_only)
            grad_query += mul(keys_t[part][span], grad_scores)
            if head == 0:
                sums[part] = [grad_key, grad_value]
            else:
                sums[part] = [sums[part][0] + grad_key, sums[part][1] + grad_value]
        grads_query.append(grad_query)
    turned = turn(
        jnp.transpose(jnp.concatenate(grads_query)) * SCALE, cos_ref[...], -sin_ref[...]
    )
    dq_ref[...] = turned.astype(LOW)
    for i in range(2):
        keep_ref[i] = sums[0][i].astype(LOW)
        send_ref[i] = sums[1][i].astype(LOW)


def middle_kernel(at_ref, live_ref, tokens_ref, far_ref, cot_ref, cot_far_ref,
                  oa_ref, ob_ref, oc_ref, gain_ref, i0, i1, i2, i3, i4, i5, d0, d1, d2, d3, d4, d5,
                  mixed_ref, mixed_far_ref, dx1_ref, do_ref, keep_ref, send_ref,
                  w_out, w_in, w_down, o_all, o_t, a2_t, h_t, dm_all, duw_all, db_all,
                  mixed, dx1_all, do_all, keep, send, out_sem):
    place, slot = at_ref[0], at_ref[2]
    live = live_ref[slot].astype(FULL)
    join_folded(at_ref, (d0, d1, d2, d3, d4, d5), w_out, w_down)
    join_blocks(at_ref, (i0, i1, i2, i3, i4, i5), w_in)
    rows, width = far_ref.shape
    share = width // 4
    short, units = share // 2, w_down.shape[0]
    gain = gain_ref[...]
    first = 0
    for ref in (oa_ref, ob_ref, oc_ref):
        o_all[:, first : first + ref.shape[1]] = ref[...]
        first += ref.shape[1]
    copies = []
    for part in range(2):
        span = pl.ds(part * rows, rows)
        o = o_all[span, :]
        values = tokens_ref[slot] if part == 0 else far_ref[...]
        x1 = values.astype(FULL) + live * mul(o, w_out[...])
        scaled, root = normalize(x1)
        a2 = (scaled * gain).astype(LOW)
        u = mul(a2, w_in[:, :units])
        w = mul(a2, w_in[:, units:])
        phi = 0.5 * (1.0 + lax.erf(u * math.sqrt(0.5)))
        gelu = u * phi
        h = (gelu * w).astype(LOW)
        mixed[span, :] = (x1 + live * mul(h, w_down[...])).astype(LOW)
        target = mixed_ref.at[slot] if part == 0 else mixed_far_ref
        copies.append(put(mixed.at[span, :], target, out_sem.at[len(copies)]))
        cot = (cot_ref[slot] if part == 0 else cot_far_ref[...]).astype(FULL)
        dm = (live * cot).astype(LOW)
        dh = mul_t(dm, w_down[...])
        slope = phi + u * (jnp.exp(-0.5 * u * u) * (1.0 / math.sqrt(2.0 * math.pi)))
        duw_all[span, :units] = (dh * w * slope).astype(LOW)
        duw_all[span, units:] = (dh * gelu).astype(LOW)
        da2 = mul_t(duw_all[span, :], w_in[...])
        dx1 = cot + normalize_back(da2, gain, scaled, root)
        dx1_all[span, :] = dx1
        copies.append(put(dx1_all.at[span, :], dx1_ref.at[span, :], out_sem.at[len(copies)]))
        db = (live * dx1).astype(LOW)
        do_all[span, :] = mul_t(db, w_out[...]).astype(LOW)
        copies.append(put(do_all.at[span, :], do_ref.at[span, :], out_sem.at[len(copies)]))
        db_all[span, :] = db
        dm_all[span, :] = dm
        o_t[:, span] = jnp.transpose(o)
        a2_t[:, span] = jnp.transpose(a2)
        h_t[:, span] = jnp.transpose(h)
    dm, duw, db = dm_all[...], duw_all[...], db_all[...]
    for j, out, target in ((1, send, send_ref), (3, send, send_ref), (0, keep, keep_ref), (2, keep, keep_ref)):
        span = pl.ds(pl.multiple_of((place ^ j) * share, share), share)
        base = (place ^ j) * (share + short)
        down = pl.ds(pl.multiple_of(base, short), share)
        down_last = pl.ds(pl.multiple_of(base + share, short), short)
        at = 2 * units
        out[j // 2, :, :at] = mul(a2_t[span, :], duw).astype(LOW)
        out[j // 2, :, at : at + width] = mul(o_t[span, :], db).astype(LOW)
        at += width
        out[j // 2, :, at : at + width] = mul(h_t[down, :], dm).astype(LOW)
        at += width
        last = mul(h_t[down_last, :], dm).astype(LOW)
        out[j // 2, :short, at:] = last[:, : width // 2]
        out[j // 2, short:, at:] = last[:, width // 2 :]
        copies.append(put(out.at[j // 2], target.at[j // 2], out_sem.at[len(copies)]))
    wait_all(copies)


def send_kernel(count, at_ref, *refs):
    normed_ref = refs[0]
    dqs, owns, gots = (refs[1 + i * count : 1 + (i + 1) * count] for i in range(3))
    (cos_ref, sin_ref, dqkv_ref, normed_t_ref, send_ref,
     dqkv, normed_t, send, sem) = refs[1 + 3 * count :]
    width = normed_ref.shape[1]
    part_width = width // count
    normed_t[...] = jnp.transpose(normed_ref[...])
    copies = [put(normed_t, normed_t_ref, sem.at[0])]
    cos_part, sin_part = cos_ref[...], -sin_ref[...]
    for part, (dq, own, got) in enumerate(zip(dqs, owns, gots)):
        base = part * part_width
        dqkv[:, pl.ds(base, part_width)] = dq[...]
        dqkv[:, pl.ds(2 * width + base, part_width)] = (
            own[1].astype(FULL) + got[1].astype(FULL)
        ).astype(LOW)
        for pair in range(part_width // PAIR):
            lanes = pl.ds(pair * PAIR, PAIR)
            raw = own[0, :, lanes].astype(FULL) + got[0, :, lanes].astype(FULL)
            dqkv[:, pl.ds(width + base + pair * PAIR, PAIR)] = turn(raw, cos_part, sin_part).astype(
                LOW
            )
    copies.append(put(dqkv, dqkv_ref, sem.at[1]))
    right = dqkv[...]
    share = send.shape[1]
    for j in (1, 3):
        start = pl.multiple_of((at_ref[0] ^ j) * share, share)
        send[j // 2] = mul(normed_t[pl.ds(start, share), :], right).astype(LOW)
        copies.append(put(send.at[j // 2], send_ref.at[j // 2], sem.at[len(copies)]))
    wait_all(copies)


def keep_kernel(at_ref, normed_t_ref, dqkv_ref, keep_ref, keep, sem):
    right = dqkv_ref[...]
    share = keep.shape[1]
    copies = []
    for j in (0, 2):
        start = pl.multiple_of((at_ref[0] ^ j) * share, share)
        keep[j // 2] = mul(normed_t_ref[pl.ds(start, share), :], right).astype(LOW)
        copies.append(put(keep.at[j // 2], keep_ref.at[j // 2], sem.at[len(copies)]))
    wait_all(copies)


def input_kernel(at_ref, tokens_ref, far_ref, gain_ref, dx1_ref, dqkv_ref, w0, w1, w2, w3, w4, w5,
                 grad_ref, grad_far_ref, weight, grad_own, out_sem):
    join_blocks(at_ref, (w0, w1, w2, w3, w4, w5), weight)
    rows = far_ref.shape[0]
    gain = gain_ref[...]
    for part in (1, 0):
        span = pl.ds(part * rows, rows)
        values = tokens_ref[at_ref[2]] if part == 0 else far_ref[...]
        scaled, root = normalize(values.astype(FULL))
        back = normalize_back(mul_t(dqkv_ref[span, :], weight[...]), gain, scaled, root)
        grad = dx1_ref[span, :] + back
        if part == 1:
            grad_far_ref[...] = grad.astype(LOW)
        else:
            grad_own[...] = grad
    put(grad_own, grad_ref.at[at_ref[2]], out_sem.at[0]).wait()


def shaped(*shape, kind=LOW):
    return jax.ShapeDtypeStruct(shape, kind)


IN_SMEM = pl.BlockSpec(memory_space=pltpu.SMEM)
IN_VMEM = pl.BlockSpec(memory_space=pltpu.VMEM)
IN_ANY = pl.BlockSpec(memory_space=pl.ANY)


def params(mebibytes):
    return pltpu.CompilerParams(vmem_limit_bytes=int(mebibytes * 1024 * 1024))


def call(kernel, args, in_specs, out_shape, out_specs, late=(), **options):
    if not isinstance(out_shape, tuple):
        out_shape, out_specs = (out_shape,), (out_specs,)
    count, skip, outs = len(args), len(late), len(out_shape)

    def body(*refs):
        outs_at = count + skip
        return kernel(*refs[:count], *refs[outs_at : outs_at + outs], *refs[outs_at + outs + 1 :])

    return pl.pallas_call(
        body,
        in_specs=list(in_specs) + [IN_ANY] * skip,
        out_shape=out_shape + (shaped(8, 128, kind=FULL),),
        out_specs=out_specs + (IN_ANY,),
        **options,
    )(*args, *late)


def gate(values, late=(), weight=0):
    hint = {}
    if weight:
        hint["cost_estimate"] = pl.CostEstimate(
            flops=weight, transcendentals=0, bytes_accessed=0
        )
    return call(
        lambda *refs: None,
        values,
        late=late,
        out_shape=tuple(jax.ShapeDtypeStruct(v.shape, v.dtype) for v in values),
        in_specs=[IN_ANY] * len(values),
        out_specs=(IN_ANY,) * len(values),
        input_output_aliases={i: i for i in range(len(values))},
        compiler_params=params(1),
        name="gate",
        **hint,
    )[: len(values)]


def join_two_kernel(at_ref, mine, other, out):
    short = mine.shape[0]
    out[pl.ds(pl.multiple_of(at_ref[4] * short, short), short), :] = mine[...]
    out[pl.ds(pl.multiple_of((1 - at_ref[4]) * short, short), short), :] = other[...]


def join_two(at, mine, other, late=()):
    rows, width = mine.shape
    return call(
        join_two_kernel,
        (at, mine, other),
        late=late,
        out_shape=shaped(2 * rows, width),
        in_specs=[IN_SMEM] + [IN_VMEM] * 2,
        out_specs=IN_VMEM,
        compiler_params=params(4),
        name="join_two",
    )


def in_hbm(value):
    return pltpu.with_memory_space_constraint(value, pltpu.HBM)


def in_vmem(*values):
    return [pltpu.with_memory_space_constraint(value, pltpu.VMEM) for value in values]


def prepare_first(at, weight, gains):
    rows, width = weight.shape
    return call(
        prepare_first_kernel,
        (at, in_hbm(weight), gains),
        out_shape=(shaped(rows // 2, width), shaped(*gains.shape)),
        in_specs=[IN_SMEM, IN_ANY, IN_VMEM],
        out_specs=(IN_VMEM,) * 2,
        scratch_shapes=[pltpu.VMEM((rows // 2, width), FULL), pltpu.SemaphoreType.DMA((1,))],
        compiler_params=params(6),
        name="prepare_first",
    )


def prepare_rest(at, tokens, w_in, w_out, w_down, w_qkv, cotangent, late):
    rows, width = w_out.shape
    folded = 2 * width + width // 2
    return call(
        prepare_rest_kernel,
        (at, *[in_hbm(v) for v in (tokens, w_in, w_out, w_down, w_qkv, cotangent)]),
        late=late,
        out_shape=(
            shaped(*tokens.shape[1:]),
            shaped(*w_in.shape),
            shaped(rows // 4, w_in.shape[1]),
            shaped(rows, folded),
            shaped(rows // 2, folded),
            shaped(*w_qkv.shape),
            shaped(*cotangent.shape[1:]),
        ),
        in_specs=[IN_SMEM] + [IN_ANY] * 6,
        out_specs=(IN_VMEM,) * 7,
        scratch_shapes=[
            pltpu.VMEM(v.shape, FULL) for v in (w_in, w_out, w_down, w_qkv)
        ] + [pltpu.SemaphoreType.DMA((6,))],
        compiler_params=params(18),
        name="prepare_rest",
    )


def project(at, tokens, far, gain, cos_part, sin_part, blocks, late):
    rows, width = 2 * far.shape[0], far.shape[1]
    return call(
        project_kernel,
        (at, tokens, *in_vmem(far), gain, cos_part, sin_part, *in_vmem(*blocks)),
        late=late,
        out_shape=(shaped(rows, width), shaped(rows, width), shaped(2, rows, width)),
        in_specs=[IN_SMEM] + [IN_VMEM] * 11,
        out_specs=(IN_VMEM,) * 3,
        scratch_shapes=[pltpu.VMEM((width, 3 * width), LOW)],
        compiler_params=params(18),
        name="project",
    )


def attend(first, count, query, near, far, mark_query, mark_key, late=()):
    rows = query.shape[0]
    row_spec = pl.BlockSpec((rows, PAIR), lambda i: (0, i + first))
    kv_spec = pl.BlockSpec((2, rows, PAIR), lambda i: (0, 0, i + first))
    out_spec = pl.BlockSpec((rows, PAIR), lambda i: (0, i))
    return call(
        attend_kernel,
        (*in_vmem(query, near, far), mark_query, mark_key),
        late=late,
        grid=(count,),
        out_shape=(shaped(rows, count * PAIR), shaped(rows, count * PAIR)),
        in_specs=[
            row_spec,
            kv_spec,
            kv_spec,
            pl.BlockSpec((rows, PAIR), lambda i: (0, 0)),
            pl.BlockSpec((2 * rows, PAIR), lambda i: (0, 0)),
        ],
        out_specs=(out_spec, out_spec),
        compiler_params=params(16),
        name="attend",
    )


def attend_back(
    first, first_o, count, query, near, far, extra, o, mark_key, do, cos_part, sin_part, late=()
):
    rows = query.shape[0]
    row_spec = pl.BlockSpec((rows, PAIR), lambda i: (0, i + first))
    o_spec = pl.BlockSpec((rows, PAIR), lambda i: (0, i + first_o))
    kv_spec = pl.BlockSpec((2, rows, PAIR), lambda i: (0, 0, i + first))
    fixed = pl.BlockSpec((rows, PAIR), lambda i: (0, 0))
    out_row = pl.BlockSpec((rows, PAIR), lambda i: (0, i))
    out_kv = pl.BlockSpec((2, rows, PAIR), lambda i: (0, 0, i))
    return call(
        attend_back_kernel,
        (*in_vmem(query, near, far, extra), mark_key, *in_vmem(o, do), cos_part, sin_part),
        late=late,
        grid=(count,),
        out_shape=(
            shaped(rows, count * PAIR),
            shaped(2, rows, count * PAIR),
            shaped(2, rows, count * PAIR),
        ),
        in_specs=[
            row_spec,
            kv_spec,
            kv_spec,
            o_spec,
            pl.BlockSpec((2 * rows, PAIR), lambda i: (0, 0)),
            o_spec,
            row_spec,
            fixed,
            fixed,
        ],
        out_specs=(out_row, out_kv, out_kv),
        compiler_params=params(20),
        name="attend_back",
    )


def middle(at, live, tokens, far, cot, cot_far, o_parts, gain, blocks_in, blocks_od):
    half, width = far.shape
    rows, share = 2 * half, width // 4
    units = blocks_in[0].shape[1] // 2
    total = 2 * units + blocks_od[0].shape[1]
    assert units == 4 * (share + share // 2)
    low = lambda *shape: pltpu.VMEM(shape, LOW)
    return call(
        middle_kernel,
        (at, live, tokens, *in_vmem(far), cot, *in_vmem(cot_far, *o_parts), gain,
         *in_vmem(*blocks_in, *blocks_od)),
        out_shape=(
            shaped(2, half, width),
            shaped(half, width),
            shaped(rows, width, kind=FULL),
            shaped(rows, width),
            shaped(2, share, total),
            shaped(2, share, total),
        ),
        in_specs=[IN_SMEM] * 2 + [IN_VMEM] * 20,
        out_specs=(IN_ANY,) * 6,
        scratch_shapes=[
            low(width, width),
            low(width, 2 * units),
            low(units, width),
            low(rows, width),
            low(width, rows),
            low(width, rows),
            low(units, rows),
            low(rows, width),
            low(rows, 2 * units),
            low(rows, width),
            low(rows, width),
            pltpu.VMEM((rows, width), FULL),
            low(rows, width),
            low(2, share, total),
            low(2, share, total),
            pltpu.SemaphoreType.DMA((10,)),
        ],
        compiler_params=params(44),
        name="middle",
    )


def qkv_send(at, normed, dq, own, got, cos_part, sin_part, late):
    rows, width = normed.shape
    share = width // 4
    return call(
        functools.partial(send_kernel, len(dq)),
        (at, normed, *dq, *own, *got, cos_part, sin_part),
        late=late,
        out_shape=(
            shaped(rows, 3 * width),
            shaped(width, rows),
            shaped(2, share, 3 * width),
        ),
        in_specs=[IN_SMEM] + [IN_VMEM] * (3 + 3 * len(dq)),
        out_specs=(IN_ANY,) * 3,
        scratch_shapes=[
            pltpu.VMEM((rows, 3 * width), LOW),
            pltpu.VMEM((width, rows), LOW),
            pltpu.VMEM((2, share, 3 * width), LOW),
            pltpu.SemaphoreType.DMA((4,)),
        ],
        compiler_params=params(20),
        name="qkv_send",
    )


def qkv_keep(at, normed_t, dqkv, late):
    width, rows = normed_t.shape
    share = width // 4
    return call(
        keep_kernel,
        (at, normed_t, dqkv),
        late=late,
        out_shape=shaped(2, share, 3 * width),
        in_specs=[IN_SMEM] + [IN_VMEM] * 2,
        out_specs=IN_ANY,
        scratch_shapes=[
            pltpu.VMEM((2, share, 3 * width), LOW),
            pltpu.SemaphoreType.DMA((2,)),
        ],
        compiler_params=params(16),
        name="qkv_keep",
    )


def input_back(at, tokens, far, gain, dx1, dqkv, blocks, late):
    half, width = far.shape
    return call(
        input_kernel,
        (at, tokens, far, gain, dx1, *in_vmem(dqkv, *blocks)),
        late=late,
        out_shape=(shaped(2, half, width, kind=FULL), shaped(half, width)),
        in_specs=[IN_SMEM] + [IN_VMEM] * 11,
        out_specs=(IN_ANY, IN_VMEM),
        scratch_shapes=[
            pltpu.VMEM((width, 3 * width), LOW),
            pltpu.VMEM((half, width), FULL),
            pltpu.SemaphoreType.DMA((1,)),
        ],
        compiler_params=params(20),
        name="input_back",
    )


def first_sums_kernel(at_ref, keep, got, own_a, far_a, mine_b, give_b):
    cut, short = far_a.shape[0], give_b.shape[1]

    def add(block, start, size):
        span = pl.ds(start, size)
        return (keep[block, span, :].astype(FULL) + got[block, span, :].astype(FULL)).astype(LOW)

    far_a[...] = add(1, 0, cut)
    for block in range(2):
        give_b[block] = add(block, pl.multiple_of(cut + (1 - at_ref[1]) * short, short), short)
        mine_b[block] = add(block, pl.multiple_of(cut + at_ref[1] * short, short), short)
    own_a[...] = add(0, 0, cut)


def first_sums(at, keep, got, late=()):
    _, rows, width = keep.shape
    cut, short = rows // 2, rows // 4
    return call(
        first_sums_kernel,
        (at, keep, got),
        late=late,
        out_shape=(shaped(cut, width),) * 2 + (shaped(2, short, width),) * 2,
        in_specs=[IN_SMEM] + [IN_VMEM] * 2,
        out_specs=(IN_VMEM,) * 4,
        compiler_params=params(20),
        name="first_sums",
    )


def second_sums_kernel(at_ref, own_a, got_a, mine_b, got_b, mine_a, give_a, near_b, far_b):
    short = mine_a.shape[0]
    for start, out in ((1 - at_ref[1], give_a), (at_ref[1], mine_a)):
        span = pl.ds(pl.multiple_of(start * short, short), short)
        out[...] = (own_a[span, :].astype(FULL) + got_a[span, :].astype(FULL)).astype(LOW)
    for block, out in ((1, far_b), (0, near_b)):
        out[...] = (mine_b[block].astype(FULL) + got_b[block].astype(FULL)).astype(LOW)


def second_sums(at, own_a, got_a, mine_b, got_b, late=()):
    _, short, width = mine_b.shape
    return call(
        second_sums_kernel,
        (at, own_a, got_a, mine_b, got_b),
        late=late,
        out_shape=(shaped(short, width),) * 4,
        in_specs=[IN_SMEM] + [IN_VMEM] * 4,
        out_specs=(IN_VMEM,) * 4,
        compiler_params=params(12),
        name="second_sums",
    )


def third_sums_kernel(at_ref, mine_a, got_a, near_b, got_b, keep, give):
    upper = mine_a[...].astype(FULL) + got_a[...].astype(FULL)
    lower = near_b[...].astype(FULL) + got_b[...].astype(FULL)
    keep[...] = jnp.where(at_ref[4] == 0, upper, lower).astype(LOW)
    give[...] = jnp.where(at_ref[4] == 0, lower, upper).astype(LOW)


def third_sums(at, mine_a, got_a, near_b, got_b, late=()):
    return call(
        third_sums_kernel,
        (at, mine_a, got_a, near_b, got_b),
        late=late,
        out_shape=(shaped(*mine_a.shape),) * 2,
        in_specs=[IN_SMEM] + [IN_VMEM] * 4,
        out_specs=(IN_VMEM,) * 2,
        compiler_params=params(12),
        name="third_sums",
    )


def squares_kernel(at_ref, qkv, w_qkv, rest, w_in, gains, out):
    inner = w_in.shape[1]
    total = jnp.sum(jnp.square(rest[:, inner:].astype(FULL)), keepdims=True)
    rows = qkv.shape[0]
    shape = (rows, gains.shape[1])
    offset = lax.broadcasted_iota(jnp.int32, shape, 1) - lax.broadcasted_iota(jnp.int32, shape, 0)
    for i, (piece, weight) in enumerate(((qkv, w_qkv), (rest, w_in))):
        start = at_ref[3]
        span = pl.ds(pl.multiple_of(start, 8), rows)
        values = piece[:, : weight.shape[1]].astype(FULL)
        sums = jnp.sum(weight[span, :].astype(LOW).astype(FULL) * values, axis=1, keepdims=True)
        gain = gains[i : i + 1, :].astype(LOW).astype(FULL)
        gain = jnp.sum(jnp.where(offset == start, gain, 0.0), axis=1, keepdims=True)
        total += jnp.sum(jnp.square(values), keepdims=True)
        total += jnp.sum(jnp.square(sums / gain), keepdims=True)
    out[...] = jnp.broadcast_to(total, out.shape)


def squares(*args):
    return call(
        squares_kernel,
        args,
        out_shape=shaped(8, 128, kind=FULL),
        in_specs=[IN_SMEM] + [IN_VMEM] * (len(args) - 1),
        out_specs=IN_VMEM,
        compiler_params=params(10),
        name="squares",
    )


def add_kernel(count, *refs):
    for i in range(count):
        out = refs[2 * count + i]
        out[...] = (refs[i][...].astype(FULL) + refs[count + i][...].astype(FULL)).astype(out.dtype)


def add(first, second, late=()):
    count = len(first)
    return call(
        functools.partial(add_kernel, count),
        (*first, *second),
        late=late,
        out_shape=tuple(jax.ShapeDtypeStruct(v.shape, v.dtype) for v in first),
        in_specs=[IN_VMEM] * (2 * count),
        out_specs=(IN_VMEM,) * count,
        compiler_params=params(8),
        name="add",
    )


def fill_kernel(at_ref, mixed_far, grad_far, mixed_in, grad_in, mixed, grad, wide, sem):
    first = put(mixed_far, mixed.at[1 - at_ref[2]], sem.at[0])
    wide[...] = grad_far[...].astype(FULL)
    put(wide, grad.at[1 - at_ref[2]], sem.at[1]).wait()
    first.wait()


def fill(at, mixed, mixed_far, grad, grad_far):
    return call(
        fill_kernel,
        (at, mixed_far, grad_far, mixed, grad),
        out_shape=(shaped(*mixed.shape), shaped(*grad.shape, kind=FULL)),
        in_specs=[IN_SMEM, IN_VMEM, IN_VMEM, IN_ANY, IN_ANY],
        out_specs=(IN_ANY,) * 2,
        input_output_aliases={3: 0, 4: 1},
        scratch_shapes=[pltpu.VMEM(grad_far.shape, FULL), pltpu.SemaphoreType.DMA((2,))],
        compiler_params=params(4),
        name="fill",
    )


def clip_factor(square_ref):
    norm = jnp.sqrt(square_ref[:1, :1])
    return jnp.minimum(1.0, CLIP_LIMIT / (norm + 1e-06))


def quarters(at_ref, parts):
    own, beside, other, other_beside = parts
    for i in range(4):
        same = at_ref[4] == i // 2
        near = jnp.where(same, own[...], beside[...])
        far = jnp.where(same, other[...], other_beside[...])
        yield jnp.where(at_ref[1] == i % 2, near, far).astype(FULL)


def gain_row(weight, gradient, start, shape):
    sums = jnp.sum(weight.astype(LOW).astype(FULL) * gradient, axis=1, keepdims=True)
    shape = (weight.shape[0], shape[1])
    offset = lax.broadcasted_iota(jnp.int32, shape, 1) - lax.broadcasted_iota(jnp.int32, shape, 0)
    return jnp.sum(jnp.where(offset == start, sums, 0.0), axis=0, keepdims=True)


class Update:
    def __init__(self, number, sources, news, targets, sem):
        self.number, self.sources, self.news, self.targets = number, sources, news, targets
        self.sem, self.out = sem, []

    def step(self, span, gradient, factor):
        weight = self.sources[0][span]
        results = adam_step(
            weight, self.sources[1][span], self.sources[2][span], gradient, factor,
            STEP_RATES[self.number], DECAY_RATES[self.number],
        )
        for result, new, target in zip(results, self.news, self.targets):
            new[span] = result
            self.out.append(put(new.at[span], target.at[span], self.sem.at[len(self.out)]))
        return weight


def update_rest_kernel(at_ref, square_ref, *refs):
    parts, refs = refs[:4], refs[4:]
    sources, targets, row_ref, news, sem = refs[:9], refs[9:18], refs[18], refs[19:28], refs[28]
    inner, out, down = (
        Update(number, *(group[3 * k : 3 * k + 3] for group in (sources, news, targets)), sem.at[k])
        for k, number in enumerate((2, 1, 3))
    )
    factor = clip_factor(square_ref)
    rows, width = sources[3].shape
    lanes = sources[0].shape[1]
    short, last = rows // 4, width // 2
    row = jnp.zeros(row_ref.shape, FULL)
    for i, gradient in enumerate(quarters(at_ref, parts)):
        span = (slice(i * short, (i + 1) * short), slice(None))
        part = gradient[:, :lanes]
        row += gain_row(inner.step(span, part, factor), part, i * short, row_ref.shape)
        out.step(span, gradient[:, lanes : lanes + width], factor)
        down.step(span, gradient[:, lanes + width : lanes + 2 * width], factor)
        start = rows + (i % 2) * short
        span = (slice(start, start + short), slice((i // 2) * last, (i // 2 + 1) * last))
        down.step(span, gradient[:, lanes + 2 * width :], factor)
    row_ref[...] = row
    wait_all(inner.out + out.out + down.out)


def update_rest(at, square, parts, inner, out, down, late):
    like = [jax.ShapeDtypeStruct(v.shape, FULL) for v in (*inner, *out, *down)]
    return call(
        update_rest_kernel,
        (at, square, *parts, *inner, *out, *down),
        late=late,
        out_shape=(*like, shaped(1, inner[0].shape[0], kind=FULL)),
        in_specs=[IN_SMEM] + [IN_VMEM] * 14,
        out_specs=(IN_ANY,) * 9 + (IN_VMEM,),
        scratch_shapes=[pltpu.VMEM(v.shape, FULL) for v in like]
        + [pltpu.SemaphoreType.DMA((3, 24))],
        compiler_params=params(28),
        name="update_rest",
    )


def update_last_kernel(at_ref, square_ref, row_ref, g_w, g_m, g_v, *refs):
    parts, refs = refs[:4], refs[4:]
    sources, targets = refs[:3], refs[3:6]
    g_w_out, g_m_out, g_v_out, norm_out = refs[6:10]
    news, sem = refs[10:13], refs[13]
    qkv = Update(0, sources, news, targets, sem)
    factor = clip_factor(square_ref)
    norm_out[...] = jnp.sqrt(square_ref[...])
    short = sources[0].shape[0] // 4
    row = jnp.zeros(row_ref.shape, FULL)
    for i, gradient in enumerate(quarters(at_ref, parts)):
        span = (slice(i * short, (i + 1) * short), slice(None))
        row += gain_row(qkv.step(span, gradient, factor), gradient, i * short, row_ref.shape)
    for i, values in enumerate((row, row_ref[...])):
        line = slice(i, i + 1)
        gradient = values / g_w[line, :].astype(LOW).astype(FULL)
        g_w_out[line, :], g_m_out[line, :], g_v_out[line, :] = adam_step(
            g_w[line, :], g_m[line, :], g_v[line, :], gradient, factor,
            STEP_RATES[4], DECAY_RATES[4],
        )
    wait_all(qkv.out)


def update_last(at, square, qkv, qkv_parts, row, gains):
    like = [jax.ShapeDtypeStruct(v.shape, FULL) for v in qkv]
    return call(
        update_last_kernel,
        (at, square, row, *gains, *qkv_parts, *qkv),
        out_shape=(
            *like,
            *[jax.ShapeDtypeStruct(v.shape, FULL) for v in gains],
            jax.ShapeDtypeStruct(square.shape, FULL),
        ),
        in_specs=[IN_SMEM] + [IN_VMEM] * 12,
        out_specs=(IN_ANY,) * 3 + (IN_VMEM,) * 4,
        scratch_shapes=[pltpu.VMEM(v.shape, FULL) for v in like]
        + [pltpu.SemaphoreType.DMA((12,))],
        compiler_params=params(18),
        name="update_last",
    )


def low_sum(*values):
    return sum(value.astype(FULL) for value in values).astype(LOW)


def index(value, i):
    return lax.dynamic_index_in_dim(value, i, 0, keepdims=False)


def make(dp_count, seq_count):
    assert seq_count == 4 and dp_count >= 8 and dp_count & (dp_count - 1) == 0
    far_bits = [1 << i for i in range(2, dp_count.bit_length() - 1)]

    def trade(value, axis, bit):
        size = seq_count if axis == "seq" else dp_count
        return lax.ppermute(value, axis, [(i, i ^ bit) for i in range(size)])

    def on_device(
        tokens, cotangent, segments, valid,
        w_qkv, w_out, w_in, w_down, gains,
        m_qkv, m_out, m_in, m_down, m_gains,
        v_qkv, v_out, v_in, v_down, v_gains,
    ):
        place = lax.axis_index("seq")
        group = lax.axis_index("dp")
        slot = place >> 1
        half = group & 1
        local_len, width = tokens.shape[1:]
        rows = 2 * local_len
        share = w_qkv.shape[0]
        side = (group >> 1) & 1
        quarter = share // 4
        at = jnp.stack([place, half, slot, side * 2 * quarter + half * quarter, side])

        half_qkv, low_gains, begun = prepare_first(at, w_qkv, gains)
        (far_qa,) = gate((trade(half_qkv, "seq", 2),), weight=EARLY)
        (gain_far,) = gate((trade(low_gains, "seq", 2),), weight=2 * EARLY)
        their_tokens, low_in, part_in, low_od, half_od, low_qkv, their_cot, _ = prepare_rest(
            at, tokens, w_in, w_out, w_down, w_qkv, cotangent, (begun,)
        )
        near_q = trade(low_qkv, "seq", 1)
        far = trade(their_tokens, "seq", 2)
        far_qb = trade(far_qa, "dp", 1)
        near_qa = trade(far_qa, "seq", 1)
        near_qb = trade(far_qb, "seq", 1)
        gain_near = trade(jnp.stack([low_gains, gain_far]), "seq", 1)
        gain_stack = jnp.stack([low_gains, gain_near[0], gain_far, gain_near[1]])
        gain_low = jnp.concatenate(
            [index(gain_stack, b ^ place) for b in range(4)], axis=1
        ).astype(FULL)
        blocks_qkv = (low_qkv, near_q, far_qa, far_qb, near_qa, near_qb)
        low_in, low_od, part_in, half_od = gate((low_in, low_od, part_in, half_od), (far_qa,))
        near_i = trade(low_in, "seq", 1)
        near_o = trade(low_od, "seq", 1)
        (come_in,) = gate((trade(part_in, "seq", 2),), weight=EARLY)

        seg = index(segments, slot)
        positions = doc_positions(seg).reshape(4, local_len)
        seg = seg.reshape(4, local_len)
        chunks = [place, place ^ 2, place ^ 1, place ^ 3]
        seg_keys = jnp.concatenate([index(seg, c) for c in chunks])
        pos = jnp.concatenate([index(positions, c) for c in chunks[:2]])
        cos_part, sin_part = rope_tables(pos)
        lane = jnp.arange(PAIR, dtype=jnp.int32)[None] % HEAD_DIM
        same = seg_keys[:, None] == lane
        mark_key = jnp.where(lane < DOCS, 1.0 - same, (lane < DOCS + 3) * 1.0).astype(LOW)
        mark_query = jnp.where((lane < DOCS) & same[:rows], NEG_FILL, 0.0).astype(LOW)

        normed, query, kv, _ = project(
            at, tokens, far, gain_low[:1], cos_part, sin_part, blocks_qkv,
            (come_in, mark_key, mark_query),
        )
        kv_far = trade(kv, "seq", 1)
        (beside_in,) = gate((trade(come_in, "dp", 2),), weight=EARLY)
        far_ia, _ = join_two(at, come_in, beside_in)
        far_ib = trade(far_ia, "dp", 1)
        near_ia = trade(far_ia, "seq", 1)
        pairs = width // PAIR
        two = pairs // 3
        args = (query, kv, kv_far, mark_query, mark_key)
        o_a, extra_a, done_a = attend(0, two, *args)
        (far_oa,) = gate((trade(half_od, "seq", 2),), (done_a,), weight=EARLY)
        near_oa = trade(far_oa, "seq", 1)
        (their_cot,) = gate((their_cot,), (far_oa,))
        (cot_far,) = gate((trade(their_cot, "seq", 2),), weight=WEIGHT)
        far_ob = trade(far_oa, "dp", 1)
        o_b, extra_b, done_b = attend(two, two, *args, late=(done_a, far_oa))
        o_c, extra_c, done_c = attend(2 * two, pairs - 2 * two, *args, late=(done_b, far_ib))
        near_ib = trade(far_ib, "seq", 1)
        (far_ob,) = gate((far_ob,), (done_c,))
        near_ob = trade(far_ob, "seq", 1)
        blocks_in = (low_in, near_i, far_ia, far_ib, near_ia, near_ib)
        blocks_od = (low_od, near_o, far_oa, far_ob, near_oa, near_ob)

        mixed, mixed_far, dx1, do, keep_rest, send_rest, _ = middle(
            at, valid, tokens, far, cotangent, cot_far, (o_a, o_b, o_c), gain_low[1:], blocks_in, blocks_od
        )
        got_rest = trade(send_rest, "seq", 1)
        near_args = (query, kv, kv_far)
        back_args = (mark_key, do, cos_part, sin_part)
        dq0, own0, give0, back0 = attend_back(0, 0, two, *near_args, extra_a, o_a, *back_args)
        *r1, r1_done = first_sums(at, keep_rest, got_rest, late=(back0,))
        got_ra, got_rb = gate(
            (trade(r1[1], "seq", 2), trade(r1[3], "dp", 1)), weight=10 * WEIGHT
        )
        got0 = trade(give0, "seq", 1)
        dq1, own1, give1, back1 = attend_back(
            two, 0, two, *near_args, extra_b, o_b, *back_args, late=(r1_done,)
        )
        got1 = trade(give1, "seq", 1)
        dq2, own2, give2, back2 = attend_back(
            2 * two, 0, pairs - 2 * two, *near_args, extra_c, o_c, *back_args,
            late=(back1, got0),
        )
        got2 = trade(give2, "seq", 1)
        dqkv, normed_t, send_qkv, send_done = qkv_send(
            at, normed, (dq0, dq1, dq2), (own0, own1, own2), (got0, got1, got2),
            cos_part, sin_part, late=(),
        )
        got_qkv = trade(send_qkv, "seq", 1)
        *r2, r2_done = second_sums(at, r1[0], got_ra, r1[2], got_rb, late=(send_done,))
        got_ra, got_rb = trade(r2[1], "dp", 1), trade(r2[3], "seq", 2)
        keep_qkv, _ = qkv_keep(at, normed_t, dqkv, late=(r2_done,))
        *q1, q1_done = first_sums(at, keep_qkv, got_qkv)
        got_qa, got_qb = trade(q1[1], "seq", 2), trade(q1[3], "dp", 1)
        grad, grad_far, grad_done = input_back(
            at, tokens, far, gain_low[:1], dx1, dqkv, blocks_qkv, late=(q1_done,)
        )
        rest, give_rest, r3_done = third_sums(
            at, r2[0], got_ra, r2[2], got_rb, late=(grad_done,)
        )
        got_rest = trade(give_rest, "dp", 2)
        *q2, q2_done = second_sums(at, q1[0], got_qa, q1[2], got_qb, late=(r3_done,))
        got_qa, got_qb = gate(
            (trade(q2[1], "dp", 1), trade(q2[3], "seq", 2)), weight=10 * WEIGHT
        )
        rest, rest_done = add((rest,), (got_rest,), late=(q2_done,))
        got_rest = trade(rest, "dp", far_bits[0])
        qkv, give_qkv, q3_done = third_sums(
            at, q2[0], got_qa, q2[2], got_qb, late=(rest_done,)
        )
        (mixed_far,) = gate((mixed_far,), (q3_done,))
        mixed_far = trade(mixed_far, "seq", 2)
        qkv, qkv_done = add((qkv,), (trade(give_qkv, "dp", 2),))
        got_qkv = trade(qkv, "dp", far_bits[0])
        rest, rest_done = add((rest,), (got_rest,), late=(qkv_done, mixed_far))
        for bit in far_bits[1:]:
            rest, rest_done = add((rest,), (trade(rest, "dp", bit),))
        (grad_far,) = gate((grad_far,), (rest_done,))
        grad_far = trade(grad_far, "seq", 2)

        beside, other = trade(rest, "dp", 2), trade(rest, "dp", 1)
        mixed, grad, fill_done = fill(at, mixed, mixed_far, grad, grad_far)
        qkv, qkv_done = add((qkv,), (got_qkv,), late=(rest_done, grad_far, beside, other))
        for bit in far_bits[1:]:
            qkv, qkv_done = add((qkv,), (trade(qkv, "dp", bit),))
        square, _ = squares(at, qkv, w_qkv, rest, w_in, gains)
        square, square_done = add((square,), (trade(square, "seq", 2),))
        (qkv,) = gate((qkv,), (square_done,))
        qkv_beside, qkv_other = trade(qkv, "dp", 2), trade(qkv, "dp", 1)
        rest_parts = (rest, beside, other, trade(beside, "dp", 1))
        qkv_parts = (qkv, qkv_beside, qkv_other, trade(qkv_beside, "dp", 1))
        for axis, bit, late in (
            ("seq", 1, ()),
            ("dp", 2, (qkv_beside, rest_parts[3])),
            ("dp", 1, (qkv_other, fill_done)),
        ):
            square, _ = add((square,), (trade(square, axis, bit),), late=late)

        (new_in, first_in, second_in, new_out, first_out, second_out,
         new_down, first_down, second_down, row, _) = update_rest(
            at, square, rest_parts,
            (w_in, m_in, v_in), (w_out, m_out, v_out), (w_down, m_down, v_down), (),
        )
        (new_qkv, first_qkv, second_qkv, new_gains, first_gains, second_gains, norm, _) = (
            update_last(
                at, square, (w_qkv, m_qkv, v_qkv), qkv_parts, row, (gains, m_gains, v_gains)
            )
        )
        return (
            mixed,
            grad,
            norm[0, 0],
            new_qkv, new_out, new_in, new_down, new_gains,
            first_qkv, first_out, first_in, first_down, first_gains,
            second_qkv, second_out, second_in, second_down, second_gains,
        )

    return on_device


def solution(mesh):
    rows, matrix, gain = P("dp", "seq", None), P("seq", None), P(None, "seq")
    weights = (matrix,) * 4 + (gain,)
    return jax.shard_map(
        make(mesh.shape["dp"], mesh.shape["seq"]),
        mesh=mesh,
        in_specs=(rows, rows, P("dp", None), P("dp")) + weights * 3,
        out_specs=(rows, rows, P()) + weights * 3,
        check_vma=False,
    )
```

```python
import functools
import math

import jax
import jax.numpy as jnp
from jax import lax
from jax.experimental import pallas as pl
from jax.experimental.pallas import tpu as pltpu
from jax.sharding import PartitionSpec as P

HEADS = 12
HEAD_DIM = 64
PAIR = 2 * HEAD_DIM
STEP_COUNT = 10
EPS_NORM = 1e-05
ROPE_BASE = 160000.0
NEG_FILL = -1e30
CLIP_LIMIT = 10.0
BETA_FIRST = 0.9
BETA_SECOND = 0.98
EPS_ADAM = 1e-06
STEP_RATES = (0.1, 0.5, 0.1, 0.1, 1.0)
DECAY_RATES = (0.01, 0.01, 0.01, 0.01, 0.0)
DOCS = 5
LOW = jnp.bfloat16
FULL = jnp.float32
SCALE = 1.0 / math.sqrt(HEAD_DIM)
WEIGHT = 20_000_000_000
EARLY = 20_000_000_000


def doc_positions(segment_ids):
    seq_len = segment_ids.shape[-1]
    places = jnp.arange(seq_len, dtype=jnp.int32)
    first_mark = jnp.ones((1,), jnp.bool_)
    change = jnp.concatenate([first_mark, segment_ids[1:] != segment_ids[:-1]])
    starts = lax.cummax(jnp.where(change, places, 0), axis=0)
    return places - starts


def rope_tables(positions):
    half_dim = HEAD_DIM // 2
    exponents = jnp.arange(half_dim, dtype=jnp.float32) * (2.0 / HEAD_DIM)
    inv_freq = ROPE_BASE ** (-exponents)
    angles = positions.astype(jnp.float32)[:, None] * inv_freq
    cos_part, sin_part = jnp.cos(angles), jnp.sin(angles)
    return (
        jnp.concatenate([cos_part] * 4, axis=1),
        jnp.concatenate([-sin_part, sin_part] * 2, axis=1),
    )


def adam_step(weight, first_old, second_old, gradient, factor, step_rate, decay_rate):
    first_new = BETA_FIRST * first_old + ((1.0 - BETA_FIRST) * factor) * gradient
    second_new = BETA_SECOND * second_old + ((1.0 - BETA_SECOND) * factor * factor) * (
        gradient * gradient
    )
    unbias = math.sqrt(1.0 - BETA_SECOND**STEP_COUNT)
    rate = step_rate / (1.0 - BETA_FIRST**STEP_COUNT) * unbias
    step = first_new * rate / (second_new * lax.rsqrt(second_new) + EPS_ADAM * unbias)
    return (weight * (1.0 - step_rate * decay_rate) - step, first_new, second_new)


def mul(left, right):
    return lax.dot_general(left, right, (((1,), (0,)), ((), ())), preferred_element_type=FULL)


def mul_t(left, right):
    return lax.dot_general(left, right, (((1,), (1,)), ((), ())), preferred_element_type=FULL)


def normalize(values):
    centered = values - jnp.mean(values, axis=-1, keepdims=True)
    root = lax.rsqrt(jnp.mean(centered * centered, axis=-1, keepdims=True) + EPS_NORM)
    return centered * root, root


def normalize_back(grad, gain, scaled, root):
    t = grad * gain
    back = root * (
        t
        - jnp.mean(t, axis=-1, keepdims=True)
        - scaled * jnp.mean(t * scaled, axis=-1, keepdims=True)
    )
    return back


def turn(values, cos_part, sin_part):
    lane = lax.broadcasted_iota(jnp.int32, values.shape, 1)
    swapped = jnp.where(
        lane % HEAD_DIM < HEAD_DIM // 2,
        pltpu.roll(values, PAIR - HEAD_DIM // 2, 1),
        pltpu.roll(values, HEAD_DIM // 2, 1),
    )
    return values * cos_part + swapped * sin_part


def three_parts(values):
    high = values.astype(LOW).astype(FULL)
    rest = values - high
    mid = rest.astype(LOW).astype(FULL)
    return high, mid, rest - mid


def wait_all(copies):
    for copy in copies:
        copy.wait()


def put(source, target, sem):
    copy = pltpu.make_async_copy(source, target, sem)
    copy.start()
    return copy


PIECES = ((0, None), (1, None), (2, 0), (2, 1), (3, 0), (3, 1))


def join_blocks(at_ref, blocks, whole):
    rows = blocks[0].shape[0]
    for block, (bits, part) in zip(blocks, PIECES):
        start = (at_ref[0] ^ bits) * rows
        size = rows
        if part is not None:
            size = rows // 2
            start += (at_ref[1] ^ part) * size
        whole[pl.ds(pl.multiple_of(start, size), size), :] = block[...]


def join_folded(at_ref, blocks, w_out, w_down):
    rows, width = blocks[0].shape[0], w_out.shape[1]
    short, last = rows // 2, width // 2
    for block, (bits, part) in zip(blocks, PIECES):
        owner = at_ref[0] ^ bits
        base = owner * (rows + short)
        first = 0 if part is None else (at_ref[1] ^ part) * short
        size = rows if part is None else short
        span = pl.ds(pl.multiple_of(owner * rows + first, short), size)
        w_out[span, :] = block[:, :width]
        span = pl.ds(pl.multiple_of(base + first, short), size)
        w_down[span, :] = block[:, width : 2 * width]
        span = pl.ds(pl.multiple_of(base + rows, short), short)
        if part is None:
            for i in range(2):
                w_down[span, i * last : (i + 1) * last] = block[
                    i * short : (i + 1) * short, 2 * width :
                ]
        else:
            lanes = pl.ds(pl.multiple_of((at_ref[1] ^ part) * last, last), last)
            w_down[span, lanes] = block[:, 2 * width :]


def fold(out, w_out, w_down, first):
    rows, width = w_out.shape
    short, last = rows // 2, width // 2
    out[:, first : first + width] = w_out[...].astype(LOW)
    out[:, first + width : first + 2 * width] = w_down[:rows, :].astype(LOW)
    for i in range(2):
        out[i * short : (i + 1) * short, first + 2 * width :] = w_down[
            rows:, i * last : (i + 1) * last
        ].astype(LOW)


def prepare_first_kernel(at_ref, w_ref, gains_ref, half_ref, gains_out, wide, sem):
    short = half_ref.shape[0]
    span = pl.ds(pl.multiple_of(at_ref[1] * short, short), short)
    copy = put(w_ref.at[span, :], wide, sem.at[0])
    gains_out[...] = gains_ref[...].astype(LOW)
    copy.wait()
    half_ref[...] = wide[...].astype(LOW)


def prepare_rest_kernel(at_ref, tokens_ref, in_ref, out_ref, down_ref, qkv_ref, cot_ref,
                        their_tokens, low_in, part_in, low_od, half_od, low_qkv, their_cot,
                        in_wide, out_wide, down_wide, qkv_wide, sem):
    slot = 1 - at_ref[2]
    copies = [
        put(source, target, sem.at[i])
        for i, (source, target) in enumerate((
            (tokens_ref.at[slot], their_tokens), (in_ref, in_wide), (out_ref, out_wide),
            (down_ref, down_wide), (qkv_ref, qkv_wide), (cot_ref.at[slot], their_cot),
        ))
    ]
    short = part_in.shape[0]
    span = pl.ds(pl.multiple_of((2 * at_ref[1] + at_ref[4]) * short, short), short)
    copies[1].wait()
    part_in[...] = in_wide[span, :].astype(LOW)
    low_in[...] = in_wide[...].astype(LOW)
    copies[2].wait()
    copies[3].wait()
    fold(low_od, out_wide, down_wide, 0)
    short = half_od.shape[0]
    half_od[...] = low_od[pl.ds(pl.multiple_of(at_ref[1] * short, short), short), :]
    copies[4].wait()
    low_qkv[...] = qkv_wide[...].astype(LOW)
    copies[0].wait()
    copies[5].wait()


def project_kernel(at_ref, tokens_ref, far_ref, gain_ref, cos_ref, sin_ref, w0, w1, w2, w3, w4, w5,
                   normed_ref, query_ref, kv_ref, weight):
    join_blocks(at_ref, (w0, w1, w2, w3, w4, w5), weight)
    rows, width = far_ref.shape
    for part in range(2):
        values = tokens_ref[at_ref[2]] if part == 0 else far_ref[...]
        scaled, _ = normalize(values.astype(FULL))
        normed_ref[pl.ds(part * rows, rows), :] = (scaled * gain_ref[...]).astype(LOW)
    for part in range(2):
        span = pl.ds(part * rows, rows)
        normed = normed_ref[span, :]
        cos_part, sin_part = cos_ref[span, :], sin_ref[span, :]
        for pair in range(2 * width // PAIR):
            lanes = pl.ds(pair * PAIR, PAIR)
            if pair % 2 == 0:
                both = mul(normed, weight[:, pl.ds(pair * PAIR, 2 * PAIR)])
            raw = both[:, (pair % 2) * PAIR : (pair % 2 + 1) * PAIR]
            turned = turn(raw, cos_part, sin_part)
            if pair < width // PAIR:
                query_ref[span, lanes] = (turned * SCALE).astype(LOW)
            else:
                kv_ref[0, span, pl.ds(pair * PAIR - width, PAIR)] = turned.astype(LOW)
        kv_ref[1, span, :] = mul(normed, weight[:, 2 * width :]).astype(LOW)


def head_lanes(head, shape):
    lane = lax.broadcasted_iota(jnp.int32, shape, 1)
    return (lane < HEAD_DIM) if head == 0 else (lane >= HEAD_DIM)


def pick(head, inside, outside):
    return jnp.where(head_lanes(head, inside.shape), inside, outside)


def attend_kernel(query_ref, near_ref, far_ref, mark_query_ref, mark_key_ref, o_ref, extra_ref):
    rows = query_ref.shape[0]
    query = query_ref[...]
    mark_query = mark_query_ref[...]
    parts = [
        (near_ref[0], jnp.transpose(near_ref[1]), mark_key_ref[:rows, :]),
        (far_ref[0], jnp.transpose(far_ref[1]), mark_key_ref[rows:, :]),
    ]
    outs, logs = [], []
    for head in range(2):
        query_head = pick(head, query, mark_query)
        scores = [mul_t(pick(head, key, mark), query_head) for key, _, mark in parts]
        top = jnp.maximum(
            jnp.max(scores[0], axis=0, keepdims=True), jnp.max(scores[1], axis=0, keepdims=True)
        )
        exps = [jnp.exp(score - top) for score in scores]
        total = jnp.sum(exps[0], axis=0, keepdims=True) + jnp.sum(exps[1], axis=0, keepdims=True)
        span = slice(head * HEAD_DIM, (head + 1) * HEAD_DIM)
        out = sum(mul(value_t[span], e.astype(LOW)) for (_, value_t, _), e in zip(parts, exps))
        outs.append(out / total)
        logs.append(top + jnp.log(total))
    o_ref[...] = jnp.transpose(jnp.concatenate(outs)).astype(LOW)
    line = lax.broadcasted_iota(jnp.int32, (PAIR, rows), 0)
    extra = jnp.zeros((PAIR, rows), FULL)
    for head in range(2):
        base = DOCS + (HEAD_DIM if head == 0 else 0)
        for i, piece in enumerate(three_parts(-logs[head])):
            extra = jnp.where(line == base + i, piece, extra)
    extra_ref[...] = jnp.transpose(extra).astype(LOW) + mark_query


def attend_back_kernel(query_ref, near_ref, far_ref, extra_ref, mark_key_ref, o_ref, do_ref,
                       cos_ref, sin_ref, dq_ref, keep_ref, send_ref):
    rows = query_ref.shape[0]
    query, extra, do = query_ref[...], extra_ref[...], do_ref[...]
    inner_all = do.astype(FULL) * o_ref[...].astype(FULL)
    lane = lax.broadcasted_iota(jnp.int32, (rows, PAIR), 1)
    zero = jnp.zeros((rows, PAIR), LOW)
    grads_query = []
    sums = [[None, None], [None, None]]
    keys_t = [jnp.transpose(near_ref[0]), jnp.transpose(far_ref[0])]
    for head in range(2):
        inside = head_lanes(head, (rows, PAIR))
        inner = jnp.sum(jnp.where(inside, inner_all, 0.0), axis=1, keepdims=True)
        base = DOCS + (HEAD_DIM if head == 0 else 0)
        tail = jnp.zeros((rows, PAIR), FULL)
        for i, piece in enumerate(three_parts(-inner)):
            tail = jnp.where(lane == base + i, piece, tail)
        query_head = pick(head, query, extra)
        do_head = pick(head, do, tail.astype(LOW))
        query_only = pick(head, query, zero)
        do_only = pick(head, do, zero)
        span = slice(head * HEAD_DIM, (head + 1) * HEAD_DIM)
        grad_query = 0.0
        for part, ref in enumerate((near_ref, far_ref)):
            mark = mark_key_ref[pl.ds(part * rows, rows), :]
            probs = jnp.exp(mul_t(pick(head, ref[0], mark), query_head))
            grad_probs = mul_t(pick(head, ref[1], mark), do_head)
            grad_scores = (probs * grad_probs).astype(LOW)
            grad_value = mul(probs.astype(LOW), do_only)
            grad_key = mul(grad_scores, query_only)
            grad_query += mul(keys_t[part][span], grad_scores)
            if head == 0:
                sums[part] = [grad_key, grad_value]
            else:
                sums[part] = [sums[part][0] + grad_key, sums[part][1] + grad_value]
        grads_query.append(grad_query)
    turned = turn(
        jnp.transpose(jnp.concatenate(grads_query)) * SCALE, cos_ref[...], -sin_ref[...]
    )
    dq_ref[...] = turned.astype(LOW)
    for i in range(2):
        keep_ref[i] = sums[0][i].astype(LOW)
        send_ref[i] = sums[1][i].astype(LOW)


def middle_kernel(at_ref, live_ref, tokens_ref, far_ref, cot_ref, cot_far_ref,
                  oa_ref, ob_ref, oc_ref, gain_ref, i0, i1, i2, i3, i4, i5, d0, d1, d2, d3, d4, d5,
                  mixed_ref, mixed_far_ref, dx1_ref, do_ref, keep_ref, send_ref,
                  w_out, w_in, w_down, o_all, o_t, a2_t, h_t, h_all, dm_all, duw_all, db_all,
                  mixed, dx1_all, do_all, keep, send, out_sem):
    place, slot = at_ref[0], at_ref[2]
    live = live_ref[slot].astype(FULL)
    join_folded(at_ref, (d0, d1, d2, d3, d4, d5), w_out, w_down)
    join_blocks(at_ref, (i0, i1, i2, i3, i4, i5), w_in)
    rows, width = far_ref.shape
    share = width // 4
    short, units = share // 2, w_down.shape[0]
    gain = gain_ref[...]
    first = 0
    for ref in (oa_ref, ob_ref, oc_ref):
        o_all[:, first : first + ref.shape[1]] = ref[...]
        first += ref.shape[1]
    copies = []
    for part in range(2):
        span = pl.ds(part * rows, rows)
        o = o_all[span, :]
        values = tokens_ref[slot] if part == 0 else far_ref[...]
        x1 = values.astype(FULL) + live * mul(o, w_out[...])
        scaled, root = normalize(x1)
        a2 = (scaled * gain).astype(LOW)
        cot = (cot_ref[slot] if part == 0 else cot_far_ref[...]).astype(FULL)
        dm = (live * cot).astype(LOW)
        for first in range(0, units, units // 3):
            lanes = slice(first, first + units // 3)
            lanes_lin = slice(units + first, units + first + units // 3)
            u = mul(a2, w_in[:, lanes])
            w = mul(a2, w_in[:, lanes_lin])
            dh = mul_t(dm, w_down[lanes, :])
            phi = 0.5 * (1.0 + lax.erf(u * math.sqrt(0.5)))
            gelu = u * phi
            slope = phi + u * (jnp.exp(-0.5 * u * u) * (1.0 / math.sqrt(2.0 * math.pi)))
            h_all[:, lanes] = (gelu * w).astype(LOW)
            duw_all[span, lanes] = (dh * w * slope).astype(LOW)
            duw_all[span, lanes_lin] = (dh * gelu).astype(LOW)
        h = h_all[...]
        mixed[span, :] = (x1 + live * mul(h, w_down[...])).astype(LOW)
        target = mixed_ref.at[slot] if part == 0 else mixed_far_ref
        copies.append(put(mixed.at[span, :], target, out_sem.at[len(copies)]))
        da2 = mul_t(duw_all[span, :], w_in[...])
        dx1 = cot + normalize_back(da2, gain, scaled, root)
        dx1_all[span, :] = dx1
        copies.append(put(dx1_all.at[span, :], dx1_ref.at[span, :], out_sem.at[len(copies)]))
        db = (live * dx1).astype(LOW)
        do_all[span, :] = mul_t(db, w_out[...]).astype(LOW)
        copies.append(put(do_all.at[span, :], do_ref.at[span, :], out_sem.at[len(copies)]))
        db_all[span, :] = db
        dm_all[span, :] = dm
        o_t[:, span] = jnp.transpose(o)
        a2_t[:, span] = jnp.transpose(a2)
        h_t[:, span] = jnp.transpose(h)
    dm, duw, db = dm_all[...], duw_all[...], db_all[...]
    for j, out, target in ((1, send, send_ref), (3, send, send_ref), (0, keep, keep_ref), (2, keep, keep_ref)):
        span = pl.ds(pl.multiple_of((place ^ j) * share, share), share)
        base = (place ^ j) * (share + short)
        down = pl.ds(pl.multiple_of(base, short), share)
        down_last = pl.ds(pl.multiple_of(base + share, short), short)
        at = 2 * units
        out[j // 2, :, :at] = mul(a2_t[span, :], duw).astype(LOW)
        out[j // 2, :, at : at + width] = mul(o_t[span, :], db).astype(LOW)
        at += width
        out[j // 2, :, at : at + width] = mul(h_t[down, :], dm).astype(LOW)
        at += width
        last = mul(h_t[down_last, :], dm).astype(LOW)
        out[j // 2, :short, at:] = last[:, : width // 2]
        out[j // 2, short:, at:] = last[:, width // 2 :]
        copies.append(put(out.at[j // 2], target.at[j // 2], out_sem.at[len(copies)]))
    wait_all(copies)


def send_kernel(count, at_ref, *refs):
    normed_ref = refs[0]
    dqs, owns, gots = (refs[1 + i * count : 1 + (i + 1) * count] for i in range(3))
    (cos_ref, sin_ref, dqkv_ref, normed_t_ref, send_ref,
     dqkv, normed_t, send, sem) = refs[1 + 3 * count :]
    width = normed_ref.shape[1]
    part_width = width // count
    normed_t[...] = jnp.transpose(normed_ref[...])
    copies = [put(normed_t, normed_t_ref, sem.at[0])]
    cos_part, sin_part = cos_ref[...], -sin_ref[...]
    for part, (dq, own, got) in enumerate(zip(dqs, owns, gots)):
        base = part * part_width
        dqkv[:, pl.ds(base, part_width)] = dq[...]
        dqkv[:, pl.ds(2 * width + base, part_width)] = (
            own[1].astype(FULL) + got[1].astype(FULL)
        ).astype(LOW)
        for pair in range(part_width // PAIR):
            lanes = pl.ds(pair * PAIR, PAIR)
            raw = own[0, :, lanes].astype(FULL) + got[0, :, lanes].astype(FULL)
            dqkv[:, pl.ds(width + base + pair * PAIR, PAIR)] = turn(raw, cos_part, sin_part).astype(
                LOW
            )
    copies.append(put(dqkv, dqkv_ref, sem.at[1]))
    right = dqkv[...]
    share = send.shape[1]
    for j in (1, 3):
        start = pl.multiple_of((at_ref[0] ^ j) * share, share)
        send[j // 2] = mul(normed_t[pl.ds(start, share), :], right).astype(LOW)
        copies.append(put(send.at[j // 2], send_ref.at[j // 2], sem.at[len(copies)]))
    wait_all(copies)


def keep_kernel(at_ref, normed_t_ref, dqkv_ref, keep_ref, keep, sem):
    right = dqkv_ref[...]
    share = keep.shape[1]
    copies = []
    for j in (0, 2):
        start = pl.multiple_of((at_ref[0] ^ j) * share, share)
        keep[j // 2] = mul(normed_t_ref[pl.ds(start, share), :], right).astype(LOW)
        copies.append(put(keep.at[j // 2], keep_ref.at[j // 2], sem.at[len(copies)]))
    wait_all(copies)


def input_kernel(at_ref, tokens_ref, far_ref, gain_ref, dx1_ref, dqkv_ref, w0, w1, w2, w3, w4, w5,
                 grad_ref, grad_far_ref, weight, grad_own, out_sem):
    join_blocks(at_ref, (w0, w1, w2, w3, w4, w5), weight)
    rows = far_ref.shape[0]
    gain = gain_ref[...]
    for part in (1, 0):
        span = pl.ds(part * rows, rows)
        values = tokens_ref[at_ref[2]] if part == 0 else far_ref[...]
        scaled, root = normalize(values.astype(FULL))
        back = normalize_back(mul_t(dqkv_ref[span, :], weight[...]), gain, scaled, root)
        grad = dx1_ref[span, :] + back
        if part == 1:
            grad_far_ref[...] = grad.astype(LOW)
        else:
            grad_own[...] = grad
    put(grad_own, grad_ref.at[at_ref[2]], out_sem.at[0]).wait()


def shaped(*shape, kind=LOW):
    return jax.ShapeDtypeStruct(shape, kind)


IN_SMEM = pl.BlockSpec(memory_space=pltpu.SMEM)
IN_VMEM = pl.BlockSpec(memory_space=pltpu.VMEM)
IN_ANY = pl.BlockSpec(memory_space=pl.ANY)


def params(mebibytes):
    return pltpu.CompilerParams(vmem_limit_bytes=int(mebibytes * 1024 * 1024))


def call(kernel, args, in_specs, out_shape, out_specs, late=(), **options):
    if not isinstance(out_shape, tuple):
        out_shape, out_specs = (out_shape,), (out_specs,)
    count, skip, outs = len(args), len(late), len(out_shape)

    def body(*refs):
        outs_at = count + skip
        return kernel(*refs[:count], *refs[outs_at : outs_at + outs], *refs[outs_at + outs + 1 :])

    return pl.pallas_call(
        body,
        in_specs=list(in_specs) + [IN_ANY] * skip,
        out_shape=out_shape + (shaped(8, 128, kind=FULL),),
        out_specs=out_specs + (IN_ANY,),
        **options,
    )(*args, *late)


def gate(values, late=(), weight=0):
    hint = {}
    if weight:
        hint["cost_estimate"] = pl.CostEstimate(
            flops=weight, transcendentals=0, bytes_accessed=0
        )
    return call(
        lambda *refs: None,
        values,
        late=late,
        out_shape=tuple(jax.ShapeDtypeStruct(v.shape, v.dtype) for v in values),
        in_specs=[IN_ANY] * len(values),
        out_specs=(IN_ANY,) * len(values),
        input_output_aliases={i: i for i in range(len(values))},
        compiler_params=params(1),
        name="gate",
        **hint,
    )[: len(values)]


def join_two_kernel(at_ref, mine, other, out):
    short = mine.shape[0]
    out[pl.ds(pl.multiple_of(at_ref[4] * short, short), short), :] = mine[...]
    out[pl.ds(pl.multiple_of((1 - at_ref[4]) * short, short), short), :] = other[...]


def join_two(at, mine, other, late=()):
    rows, width = mine.shape
    return call(
        join_two_kernel,
        (at, mine, other),
        late=late,
        out_shape=shaped(2 * rows, width),
        in_specs=[IN_SMEM] + [IN_VMEM] * 2,
        out_specs=IN_VMEM,
        compiler_params=params(4),
        name="join_two",
    )


def in_hbm(value):
    return pltpu.with_memory_space_constraint(value, pltpu.HBM)


def in_vmem(*values):
    return [pltpu.with_memory_space_constraint(value, pltpu.VMEM) for value in values]


def prepare_first(at, weight, gains):
    rows, width = weight.shape
    return call(
        prepare_first_kernel,
        (at, in_hbm(weight), gains),
        out_shape=(shaped(rows // 2, width), shaped(*gains.shape)),
        in_specs=[IN_SMEM, IN_ANY, IN_VMEM],
        out_specs=(IN_VMEM,) * 2,
        scratch_shapes=[pltpu.VMEM((rows // 2, width), FULL), pltpu.SemaphoreType.DMA((1,))],
        compiler_params=params(6),
        name="prepare_first",
    )


def prepare_rest(at, tokens, w_in, w_out, w_down, w_qkv, cotangent, late):
    rows, width = w_out.shape
    folded = 2 * width + width // 2
    return call(
        prepare_rest_kernel,
        (at, *[in_hbm(v) for v in (tokens, w_in, w_out, w_down, w_qkv, cotangent)]),
        late=late,
        out_shape=(
            shaped(*tokens.shape[1:]),
            shaped(*w_in.shape),
            shaped(rows // 4, w_in.shape[1]),
            shaped(rows, folded),
            shaped(rows // 2, folded),
            shaped(*w_qkv.shape),
            shaped(*cotangent.shape[1:]),
        ),
        in_specs=[IN_SMEM] + [IN_ANY] * 6,
        out_specs=(IN_VMEM,) * 7,
        scratch_shapes=[
            pltpu.VMEM(v.shape, FULL) for v in (w_in, w_out, w_down, w_qkv)
        ] + [pltpu.SemaphoreType.DMA((6,))],
        compiler_params=params(18),
        name="prepare_rest",
    )


def project(at, tokens, far, gain, cos_part, sin_part, blocks, late):
    rows, width = 2 * far.shape[0], far.shape[1]
    return call(
        project_kernel,
        (at, tokens, *in_vmem(far), gain, cos_part, sin_part, *in_vmem(*blocks)),
        late=late,
        out_shape=(shaped(rows, width), shaped(rows, width), shaped(2, rows, width)),
        in_specs=[IN_SMEM] + [IN_VMEM] * 11,
        out_specs=(IN_VMEM,) * 3,
        scratch_shapes=[pltpu.VMEM((width, 3 * width), LOW)],
        compiler_params=params(18),
        name="project",
    )


def attend(first, count, query, near, far, mark_query, mark_key, late=()):
    rows = query.shape[0]
    row_spec = pl.BlockSpec((rows, PAIR), lambda i: (0, i + first))
    kv_spec = pl.BlockSpec((2, rows, PAIR), lambda i: (0, 0, i + first))
    out_spec = pl.BlockSpec((rows, PAIR), lambda i: (0, i))
    return call(
        attend_kernel,
        (*in_vmem(query, near, far), mark_query, mark_key),
        late=late,
        grid=(count,),
        out_shape=(shaped(rows, count * PAIR), shaped(rows, count * PAIR)),
        in_specs=[
            row_spec,
            kv_spec,
            kv_spec,
            pl.BlockSpec((rows, PAIR), lambda i: (0, 0)),
            pl.BlockSpec((2 * rows, PAIR), lambda i: (0, 0)),
        ],
        out_specs=(out_spec, out_spec),
        compiler_params=params(16),
        name="attend",
    )


def attend_back(
    first, first_o, count, query, near, far, extra, o, mark_key, do, cos_part, sin_part, late=()
):
    rows = query.shape[0]
    row_spec = pl.BlockSpec((rows, PAIR), lambda i: (0, i + first))
    o_spec = pl.BlockSpec((rows, PAIR), lambda i: (0, i + first_o))
    kv_spec = pl.BlockSpec((2, rows, PAIR), lambda i: (0, 0, i + first))
    fixed = pl.BlockSpec((rows, PAIR), lambda i: (0, 0))
    out_row = pl.BlockSpec((rows, PAIR), lambda i: (0, i))
    out_kv = pl.BlockSpec((2, rows, PAIR), lambda i: (0, 0, i))
    return call(
        attend_back_kernel,
        (*in_vmem(query, near, far, extra), mark_key, *in_vmem(o, do), cos_part, sin_part),
        late=late,
        grid=(count,),
        out_shape=(
            shaped(rows, count * PAIR),
            shaped(2, rows, count * PAIR),
            shaped(2, rows, count * PAIR),
        ),
        in_specs=[
            row_spec,
            kv_spec,
            kv_spec,
            o_spec,
            pl.BlockSpec((2 * rows, PAIR), lambda i: (0, 0)),
            o_spec,
            row_spec,
            fixed,
            fixed,
        ],
        out_specs=(out_row, out_kv, out_kv),
        compiler_params=params(20),
        name="attend_back",
    )


def middle(at, live, tokens, far, cot, cot_far, o_parts, gain, blocks_in, blocks_od):
    half, width = far.shape
    rows, share = 2 * half, width // 4
    units = blocks_in[0].shape[1] // 2
    total = 2 * units + blocks_od[0].shape[1]
    assert units == 4 * (share + share // 2)
    low = lambda *shape: pltpu.VMEM(shape, LOW)
    return call(
        middle_kernel,
        (at, live, tokens, *in_vmem(far), cot, *in_vmem(cot_far, *o_parts), gain,
         *in_vmem(*blocks_in, *blocks_od)),
        out_shape=(
            shaped(2, half, width),
            shaped(half, width),
            shaped(rows, width, kind=FULL),
            shaped(rows, width),
            shaped(2, share, total),
            shaped(2, share, total),
        ),
        in_specs=[IN_SMEM] * 2 + [IN_VMEM] * 20,
        out_specs=(IN_ANY,) * 6,
        scratch_shapes=[
            low(width, width),
            low(width, 2 * units),
            low(units, width),
            low(rows, width),
            low(width, rows),
            low(width, rows),
            low(units, rows),
            low(half, units),
            low(rows, width),
            low(rows, 2 * units),
            low(rows, width),
            low(rows, width),
            pltpu.VMEM((rows, width), FULL),
            low(rows, width),
            low(2, share, total),
            low(2, share, total),
            pltpu.SemaphoreType.DMA((10,)),
        ],
        compiler_params=params(44),
        name="middle",
    )


def qkv_send(at, normed, dq, own, got, cos_part, sin_part, late):
    rows, width = normed.shape
    share = width // 4
    return call(
        functools.partial(send_kernel, len(dq)),
        (at, normed, *dq, *own, *got, cos_part, sin_part),
        late=late,
        out_shape=(
            shaped(rows, 3 * width),
            shaped(width, rows),
            shaped(2, share, 3 * width),
        ),
        in_specs=[IN_SMEM] + [IN_VMEM] * (3 + 3 * len(dq)),
        out_specs=(IN_ANY,) * 3,
        scratch_shapes=[
            pltpu.VMEM((rows, 3 * width), LOW),
            pltpu.VMEM((width, rows), LOW),
            pltpu.VMEM((2, share, 3 * width), LOW),
            pltpu.SemaphoreType.DMA((4,)),
        ],
        compiler_params=params(20),
        name="qkv_send",
    )


def qkv_keep(at, normed_t, dqkv, late):
    width, rows = normed_t.shape
    share = width // 4
    return call(
        keep_kernel,
        (at, normed_t, dqkv),
        late=late,
        out_shape=shaped(2, share, 3 * width),
        in_specs=[IN_SMEM] + [IN_VMEM] * 2,
        out_specs=IN_ANY,
        scratch_shapes=[
            pltpu.VMEM((2, share, 3 * width), LOW),
            pltpu.SemaphoreType.DMA((2,)),
        ],
        compiler_params=params(16),
        name="qkv_keep",
    )


def input_back(at, tokens, far, gain, dx1, dqkv, blocks, late):
    half, width = far.shape
    return call(
        input_kernel,
        (at, tokens, far, gain, dx1, *in_vmem(dqkv, *blocks)),
        late=late,
        out_shape=(shaped(2, half, width, kind=FULL), shaped(half, width)),
        in_specs=[IN_SMEM] + [IN_VMEM] * 11,
        out_specs=(IN_ANY, IN_VMEM),
        scratch_shapes=[
            pltpu.VMEM((width, 3 * width), LOW),
            pltpu.VMEM((half, width), FULL),
            pltpu.SemaphoreType.DMA((1,)),
        ],
        compiler_params=params(20),
        name="input_back",
    )


def first_sums_kernel(at_ref, keep, got, own_a, far_a, mine_b, give_b):
    cut, short = far_a.shape[0], give_b.shape[1]

    def add(block, start, size):
        span = pl.ds(start, size)
        return (keep[block, span, :].astype(FULL) + got[block, span, :].astype(FULL)).astype(LOW)

    far_a[...] = add(1, 0, cut)
    for block in range(2):
        give_b[block] = add(block, pl.multiple_of(cut + (1 - at_ref[1]) * short, short), short)
        mine_b[block] = add(block, pl.multiple_of(cut + at_ref[1] * short, short), short)
    own_a[...] = add(0, 0, cut)


def first_sums(at, keep, got, late=()):
    _, rows, width = keep.shape
    cut, short = rows // 2, rows // 4
    return call(
        first_sums_kernel,
        (at, keep, got),
        late=late,
        out_shape=(shaped(cut, width),) * 2 + (shaped(2, short, width),) * 2,
        in_specs=[IN_SMEM] + [IN_VMEM] * 2,
        out_specs=(IN_VMEM,) * 4,
        compiler_params=params(20),
        name="first_sums",
    )


def second_sums_kernel(at_ref, own_a, got_a, mine_b, got_b, mine_a, give_a, near_b, far_b):
    short = mine_a.shape[0]
    for start, out in ((1 - at_ref[1], give_a), (at_ref[1], mine_a)):
        span = pl.ds(pl.multiple_of(start * short, short), short)
        out[...] = (own_a[span, :].astype(FULL) + got_a[span, :].astype(FULL)).astype(LOW)
    for block, out in ((1, far_b), (0, near_b)):
        out[...] = (mine_b[block].astype(FULL) + got_b[block].astype(FULL)).astype(LOW)


def second_sums(at, own_a, got_a, mine_b, got_b, late=()):
    _, short, width = mine_b.shape
    return call(
        second_sums_kernel,
        (at, own_a, got_a, mine_b, got_b),
        late=late,
        out_shape=(shaped(short, width),) * 4,
        in_specs=[IN_SMEM] + [IN_VMEM] * 4,
        out_specs=(IN_VMEM,) * 4,
        compiler_params=params(12),
        name="second_sums",
    )


def third_sums_kernel(at_ref, mine_a, got_a, near_b, got_b, keep, give):
    upper = mine_a[...].astype(FULL) + got_a[...].astype(FULL)
    lower = near_b[...].astype(FULL) + got_b[...].astype(FULL)
    keep[...] = jnp.where(at_ref[4] == 0, upper, lower).astype(LOW)
    give[...] = jnp.where(at_ref[4] == 0, lower, upper).astype(LOW)


def third_sums(at, mine_a, got_a, near_b, got_b, late=()):
    return call(
        third_sums_kernel,
        (at, mine_a, got_a, near_b, got_b),
        late=late,
        out_shape=(shaped(*mine_a.shape),) * 2,
        in_specs=[IN_SMEM] + [IN_VMEM] * 4,
        out_specs=(IN_VMEM,) * 2,
        compiler_params=params(12),
        name="third_sums",
    )


def squares_kernel(at_ref, qkv, w_qkv, rest, w_in, gains, out):
    inner = w_in.shape[1]
    total = jnp.sum(jnp.square(rest[:, inner:].astype(FULL)), keepdims=True)
    rows = qkv.shape[0]
    shape = (rows, gains.shape[1])
    offset = lax.broadcasted_iota(jnp.int32, shape, 1) - lax.broadcasted_iota(jnp.int32, shape, 0)
    for i, (piece, weight) in enumerate(((qkv, w_qkv), (rest, w_in))):
        start = at_ref[3]
        span = pl.ds(pl.multiple_of(start, 8), rows)
        values = piece[:, : weight.shape[1]].astype(FULL)
        sums = jnp.sum(weight[span, :].astype(LOW).astype(FULL) * values, axis=1, keepdims=True)
        gain = gains[i : i + 1, :].astype(LOW).astype(FULL)
        gain = jnp.sum(jnp.where(offset == start, gain, 0.0), axis=1, keepdims=True)
        total += jnp.sum(jnp.square(values), keepdims=True)
        total += jnp.sum(jnp.square(sums / gain), keepdims=True)
    out[...] = jnp.broadcast_to(total, out.shape)


def squares(*args):
    return call(
        squares_kernel,
        args,
        out_shape=shaped(8, 128, kind=FULL),
        in_specs=[IN_SMEM] + [IN_VMEM] * (len(args) - 1),
        out_specs=IN_VMEM,
        compiler_params=params(10),
        name="squares",
    )


def add_kernel(count, *refs):
    for i in range(count):
        out = refs[2 * count + i]
        out[...] = (refs[i][...].astype(FULL) + refs[count + i][...].astype(FULL)).astype(out.dtype)


def add(first, second, late=()):
    count = len(first)
    return call(
        functools.partial(add_kernel, count),
        (*first, *second),
        late=late,
        out_shape=tuple(jax.ShapeDtypeStruct(v.shape, v.dtype) for v in first),
        in_specs=[IN_VMEM] * (2 * count),
        out_specs=(IN_VMEM,) * count,
        compiler_params=params(8),
        name="add",
    )


def fill_kernel(at_ref, mixed_far, grad_far, mixed_in, grad_in, mixed, grad, wide, sem):
    first = put(mixed_far, mixed.at[1 - at_ref[2]], sem.at[0])
    wide[...] = grad_far[...].astype(FULL)
    put(wide, grad.at[1 - at_ref[2]], sem.at[1]).wait()
    first.wait()


def fill(at, mixed, mixed_far, grad, grad_far):
    return call(
        fill_kernel,
        (at, mixed_far, grad_far, mixed, grad),
        out_shape=(shaped(*mixed.shape), shaped(*grad.shape, kind=FULL)),
        in_specs=[IN_SMEM, IN_VMEM, IN_VMEM, IN_ANY, IN_ANY],
        out_specs=(IN_ANY,) * 2,
        input_output_aliases={3: 0, 4: 1},
        scratch_shapes=[pltpu.VMEM(grad_far.shape, FULL), pltpu.SemaphoreType.DMA((2,))],
        compiler_params=params(4),
        name="fill",
    )


def clip_factor(square_ref):
    norm = jnp.sqrt(square_ref[:1, :1])
    return jnp.minimum(1.0, CLIP_LIMIT / (norm + 1e-06))


def quarters(at_ref, parts):
    own, beside, other, other_beside = parts
    for i in range(4):
        same = at_ref[4] == i // 2
        near = jnp.where(same, own[...], beside[...])
        far = jnp.where(same, other[...], other_beside[...])
        yield jnp.where(at_ref[1] == i % 2, near, far).astype(FULL)


def gain_row(weight, gradient, start, shape):
    sums = jnp.sum(weight.astype(LOW).astype(FULL) * gradient, axis=1, keepdims=True)
    shape = (weight.shape[0], shape[1])
    offset = lax.broadcasted_iota(jnp.int32, shape, 1) - lax.broadcasted_iota(jnp.int32, shape, 0)
    return jnp.sum(jnp.where(offset == start, sums, 0.0), axis=0, keepdims=True)


class Update:
    def __init__(self, number, sources, news, targets, sem):
        self.number, self.sources, self.news, self.targets = number, sources, news, targets
        self.sem, self.out = sem, []

    def step(self, span, gradient, factor):
        rows, lanes = span
        short = (rows.stop - rows.start) // 2
        for i in range(2):
            part = (slice(rows.start + i * short, rows.start + (i + 1) * short), lanes)
            results = adam_step(
                self.sources[0][part], self.sources[1][part], self.sources[2][part],
                gradient[i * short : (i + 1) * short, :], factor,
                STEP_RATES[self.number], DECAY_RATES[self.number],
            )
            for result, new, target in zip(results, self.news, self.targets):
                new[part] = result
                self.out.append(put(new.at[part], target.at[part], self.sem.at[len(self.out)]))
        return self.sources[0][span]


def update_rest_kernel(at_ref, square_ref, *refs):
    parts, refs = refs[:4], refs[4:]
    sources, targets, row_ref, news, sem = refs[:9], refs[9:18], refs[18], refs[19:28], refs[28]
    inner, out, down = (
        Update(number, *(group[3 * k : 3 * k + 3] for group in (sources, news, targets)), sem.at[k])
        for k, number in enumerate((2, 1, 3))
    )
    factor = clip_factor(square_ref)
    rows, width = sources[3].shape
    lanes = sources[0].shape[1]
    short, last = rows // 4, width // 2
    row = jnp.zeros(row_ref.shape, FULL)
    for i, gradient in enumerate(quarters(at_ref, parts)):
        span = (slice(i * short, (i + 1) * short), slice(None))
        part = gradient[:, :lanes]
        row += gain_row(inner.step(span, part, factor), part, i * short, row_ref.shape)
        out.step(span, gradient[:, lanes : lanes + width], factor)
        down.step(span, gradient[:, lanes + width : lanes + 2 * width], factor)
        start = rows + (i % 2) * short
        span = (slice(start, start + short), slice((i // 2) * last, (i // 2 + 1) * last))
        down.step(span, gradient[:, lanes + 2 * width :], factor)
    row_ref[...] = row
    wait_all(inner.out + out.out + down.out)


def update_rest(at, square, parts, inner, out, down, late):
    like = [jax.ShapeDtypeStruct(v.shape, FULL) for v in (*inner, *out, *down)]
    return call(
        update_rest_kernel,
        (at, square, *parts, *inner, *out, *down),
        late=late,
        out_shape=(*like, shaped(1, inner[0].shape[0], kind=FULL)),
        in_specs=[IN_SMEM] + [IN_VMEM] * 14,
        out_specs=(IN_ANY,) * 9 + (IN_VMEM,),
        scratch_shapes=[pltpu.VMEM(v.shape, FULL) for v in like]
        + [pltpu.SemaphoreType.DMA((3, 48))],
        compiler_params=params(28),
        name="update_rest",
    )


def update_last_kernel(at_ref, square_ref, row_ref, g_w, g_m, g_v, *refs):
    parts, refs = refs[:4], refs[4:]
    sources, targets = refs[:3], refs[3:6]
    g_w_out, g_m_out, g_v_out, norm_out = refs[6:10]
    news, sem = refs[10:13], refs[13]
    qkv = Update(0, sources, news, targets, sem)
    factor = clip_factor(square_ref)
    norm_out[...] = jnp.sqrt(square_ref[...])
    short = sources[0].shape[0] // 4
    row = jnp.zeros(row_ref.shape, FULL)
    for i, gradient in enumerate(quarters(at_ref, parts)):
        span = (slice(i * short, (i + 1) * short), slice(None))
        row += gain_row(qkv.step(span, gradient, factor), gradient, i * short, row_ref.shape)
    for i, values in enumerate((row, row_ref[...])):
        line = slice(i, i + 1)
        gradient = values / g_w[line, :].astype(LOW).astype(FULL)
        g_w_out[line, :], g_m_out[line, :], g_v_out[line, :] = adam_step(
            g_w[line, :], g_m[line, :], g_v[line, :], gradient, factor,
            STEP_RATES[4], DECAY_RATES[4],
        )
    wait_all(qkv.out)


def update_last(at, square, qkv, qkv_parts, row, gains):
    like = [jax.ShapeDtypeStruct(v.shape, FULL) for v in qkv]
    return call(
        update_last_kernel,
        (at, square, row, *gains, *qkv_parts, *qkv),
        out_shape=(
            *like,
            *[jax.ShapeDtypeStruct(v.shape, FULL) for v in gains],
            jax.ShapeDtypeStruct(square.shape, FULL),
        ),
        in_specs=[IN_SMEM] + [IN_VMEM] * 12,
        out_specs=(IN_ANY,) * 3 + (IN_VMEM,) * 4,
        scratch_shapes=[pltpu.VMEM(v.shape, FULL) for v in like]
        + [pltpu.SemaphoreType.DMA((24,))],
        compiler_params=params(18),
        name="update_last",
    )


def low_sum(*values):
    return sum(value.astype(FULL) for value in values).astype(LOW)


def index(value, i):
    return lax.dynamic_index_in_dim(value, i, 0, keepdims=False)


def make(dp_count, seq_count):
    assert seq_count == 4 and dp_count >= 8 and dp_count & (dp_count - 1) == 0
    far_bits = [1 << i for i in range(2, dp_count.bit_length() - 1)]

    def trade(value, axis, bit):
        size = seq_count if axis == "seq" else dp_count
        return lax.ppermute(value, axis, [(i, i ^ bit) for i in range(size)])

    def on_device(
        tokens, cotangent, segments, valid,
        w_qkv, w_out, w_in, w_down, gains,
        m_qkv, m_out, m_in, m_down, m_gains,
        v_qkv, v_out, v_in, v_down, v_gains,
    ):
        place = lax.axis_index("seq")
        group = lax.axis_index("dp")
        slot = place >> 1
        half = group & 1
        local_len, width = tokens.shape[1:]
        rows = 2 * local_len
        share = w_qkv.shape[0]
        side = (group >> 1) & 1
        quarter = share // 4
        at = jnp.stack([place, half, slot, side * 2 * quarter + half * quarter, side])

        half_qkv, low_gains, begun = prepare_first(at, w_qkv, gains)
        (far_qa,) = gate((trade(half_qkv, "seq", 2),), weight=EARLY)
        (gain_far,) = gate((trade(low_gains, "seq", 2),), weight=2 * EARLY)
        their_tokens, low_in, part_in, low_od, half_od, low_qkv, their_cot, _ = prepare_rest(
            at, tokens, w_in, w_out, w_down, w_qkv, cotangent, (begun,)
        )
        near_q = trade(low_qkv, "seq", 1)
        far = trade(their_tokens, "seq", 2)
        far_qb = trade(far_qa, "dp", 1)
        near_qa = trade(far_qa, "seq", 1)
        near_qb = trade(far_qb, "seq", 1)
        gain_near = trade(jnp.stack([low_gains, gain_far]), "seq", 1)
        gain_stack = jnp.stack([low_gains, gain_near[0], gain_far, gain_near[1]])
        gain_low = jnp.concatenate(
            [index(gain_stack, b ^ place) for b in range(4)], axis=1
        ).astype(FULL)
        blocks_qkv = (low_qkv, near_q, far_qa, far_qb, near_qa, near_qb)
        low_in, low_od, part_in, half_od = gate((low_in, low_od, part_in, half_od), (far_qa,))
        near_i = trade(low_in, "seq", 1)
        near_o = trade(low_od, "seq", 1)
        (come_in,) = gate((trade(part_in, "seq", 2),), weight=EARLY)

        seg = index(segments, slot)
        positions = doc_positions(seg).reshape(4, local_len)
        seg = seg.reshape(4, local_len)
        chunks = [place, place ^ 2, place ^ 1, place ^ 3]
        seg_keys = jnp.concatenate([index(seg, c) for c in chunks])
        pos = jnp.concatenate([index(positions, c) for c in chunks[:2]])
        cos_part, sin_part = rope_tables(pos)
        lane = jnp.arange(PAIR, dtype=jnp.int32)[None] % HEAD_DIM
        same = seg_keys[:, None] == lane
        mark_key = jnp.where(lane < DOCS, 1.0 - same, (lane < DOCS + 3) * 1.0).astype(LOW)
        mark_query = jnp.where((lane < DOCS) & same[:rows], NEG_FILL, 0.0).astype(LOW)

        normed, query, kv, _ = project(
            at, tokens, far, gain_low[:1], cos_part, sin_part, blocks_qkv,
            (come_in, mark_key, mark_query),
        )
        kv_far = trade(kv, "seq", 1)
        (beside_in,) = gate((trade(come_in, "dp", 2),), weight=EARLY)
        far_ia, _ = join_two(at, come_in, beside_in)
        far_ib = trade(far_ia, "dp", 1)
        near_ia = trade(far_ia, "seq", 1)
        pairs = width // PAIR
        two = pairs // 3
        args = (query, kv, kv_far, mark_query, mark_key)
        o_a, extra_a, done_a = attend(0, two, *args)
        (far_oa,) = gate((trade(half_od, "seq", 2),), (done_a,), weight=EARLY)
        near_oa = trade(far_oa, "seq", 1)
        (their_cot,) = gate((their_cot,), (far_oa,))
        (cot_far,) = gate((trade(their_cot, "seq", 2),), weight=WEIGHT)
        far_ob = trade(far_oa, "dp", 1)
        o_b, extra_b, done_b = attend(two, two, *args, late=(done_a, far_oa))
        o_c, extra_c, done_c = attend(2 * two, pairs - 2 * two, *args, late=(done_b, far_ib))
        near_ib = trade(far_ib, "seq", 1)
        (far_ob,) = gate((far_ob,), (done_c,))
        near_ob = trade(far_ob, "seq", 1)
        blocks_in = (low_in, near_i, far_ia, far_ib, near_ia, near_ib)
        blocks_od = (low_od, near_o, far_oa, far_ob, near_oa, near_ob)

        mixed, mixed_far, dx1, do, keep_rest, send_rest, _ = middle(
            at, valid, tokens, far, cotangent, cot_far, (o_a, o_b, o_c), gain_low[1:], blocks_in, blocks_od
        )
        got_rest = trade(send_rest, "seq", 1)
        near_args = (query, kv, kv_far)
        back_args = (mark_key, do, cos_part, sin_part)
        dq0, own0, give0, back0 = attend_back(0, 0, two, *near_args, extra_a, o_a, *back_args)
        *r1, r1_done = first_sums(at, keep_rest, got_rest, late=(back0,))
        got_ra, got_rb = gate(
            (trade(r1[1], "seq", 2), trade(r1[3], "dp", 1)), weight=10 * WEIGHT
        )
        got0 = trade(give0, "seq", 1)
        dq1, own1, give1, back1 = attend_back(
            two, 0, two, *near_args, extra_b, o_b, *back_args, late=(r1_done,)
        )
        got1 = trade(give1, "seq", 1)
        dq2, own2, give2, back2 = attend_back(
            2 * two, 0, pairs - 2 * two, *near_args, extra_c, o_c, *back_args,
            late=(back1, got0),
        )
        got2 = trade(give2, "seq", 1)
        dqkv, normed_t, send_qkv, send_done = qkv_send(
            at, normed, (dq0, dq1, dq2), (own0, own1, own2), (got0, got1, got2),
            cos_part, sin_part, late=(),
        )
        got_qkv = trade(send_qkv, "seq", 1)
        *r2, r2_done = second_sums(at, r1[0], got_ra, r1[2], got_rb, late=(send_done,))
        got_ra, got_rb = trade(r2[1], "dp", 1), trade(r2[3], "seq", 2)
        keep_qkv, _ = qkv_keep(at, normed_t, dqkv, late=(r2_done,))
        *q1, q1_done = first_sums(at, keep_qkv, got_qkv)
        got_qa, got_qb = trade(q1[1], "seq", 2), trade(q1[3], "dp", 1)
        rest, give_rest, r3_done = third_sums(
            at, r2[0], got_ra, r2[2], got_rb, late=(q1_done,)
        )
        got_rest = trade(give_rest, "dp", 2)
        grad, grad_far, grad_done = input_back(
            at, tokens, far, gain_low[:1], dx1, dqkv, blocks_qkv, late=(r3_done,)
        )
        *q2, q2_done = second_sums(at, q1[0], got_qa, q1[2], got_qb, late=(grad_done,))
        got_qa, got_qb = gate(
            (trade(q2[1], "dp", 1), trade(q2[3], "seq", 2)), weight=10 * WEIGHT
        )
        rest, rest_done = add((rest,), (got_rest,), late=(q2_done,))
        got_rest = trade(rest, "dp", far_bits[0])
        qkv, give_qkv, q3_done = third_sums(
            at, q2[0], got_qa, q2[2], got_qb, late=(rest_done,)
        )
        (mixed_far,) = gate((mixed_far,), (q3_done,))
        mixed_far = trade(mixed_far, "seq", 2)
        qkv, qkv_done = add((qkv,), (trade(give_qkv, "dp", 2),))
        got_qkv = trade(qkv, "dp", far_bits[0])
        rest, rest_done = add((rest,), (got_rest,), late=(qkv_done, mixed_far))
        for bit in far_bits[1:]:
            rest, rest_done = add((rest,), (trade(rest, "dp", bit),))
        (grad_far,) = gate((grad_far,), (rest_done,))
        grad_far = trade(grad_far, "seq", 2)

        beside, other = trade(rest, "dp", 2), trade(rest, "dp", 1)
        mixed, grad, fill_done = fill(at, mixed, mixed_far, grad, grad_far)
        qkv, qkv_done = add((qkv,), (got_qkv,), late=(rest_done, grad_far, beside, other))
        for bit in far_bits[1:]:
            qkv, qkv_done = add((qkv,), (trade(qkv, "dp", bit),))
        (beside,) = gate((beside,), (qkv_done,))
        rest_parts = (rest, beside, other, trade(beside, "dp", 1))
        square, _ = squares(at, qkv, w_qkv, rest, w_in, gains)
        square, _ = add((square,), (trade(square, "seq", 2),))
        square, square_done = add((square,), (trade(square, "seq", 1),), late=(rest_parts[3],))
        (qkv,) = gate((qkv,), (square_done,))
        qkv_beside, qkv_other = trade(qkv, "dp", 2), trade(qkv, "dp", 1)
        qkv_parts = (qkv, qkv_beside, qkv_other, trade(qkv_beside, "dp", 1))
        square, _ = add((square,), (trade(square, "dp", 2),))
        square, _ = add((square,), (trade(square, "dp", 1),), late=(qkv_other, fill_done))

        (new_in, first_in, second_in, new_out, first_out, second_out,
         new_down, first_down, second_down, row, _) = update_rest(
            at, square, rest_parts,
            (w_in, m_in, v_in), (w_out, m_out, v_out), (w_down, m_down, v_down), (),
        )
        (new_qkv, first_qkv, second_qkv, new_gains, first_gains, second_gains, norm, _) = (
            update_last(
                at, square, (w_qkv, m_qkv, v_qkv), qkv_parts, row, (gains, m_gains, v_gains)
            )
        )
        return (
            mixed,
            grad,
            norm[0, 0],
            new_qkv, new_out, new_in, new_down, new_gains,
            first_qkv, first_out, first_in, first_down, first_gains,
            second_qkv, second_out, second_in, second_down, second_gains,
        )

    return on_device


def solution(mesh):
    rows, matrix, gain = P("dp", "seq", None), P("seq", None), P(None, "seq")
    weights = (matrix,) * 4 + (gain,)
    return jax.shard_map(
        make(mesh.shape["dp"], mesh.shape["seq"]),
        mesh=mesh,
        in_specs=(rows, rows, P("dp", None), P("dp")) + weights * 3,
        out_specs=(rows, rows, P()) + weights * 3,
        check_vma=False,
    )
```

```python
import functools
import math

import jax
import jax.numpy as jnp
from jax import lax
from jax.experimental import pallas as pl
from jax.experimental.pallas import tpu as pltpu
from jax.sharding import PartitionSpec as P

HEADS = 12
HEAD_DIM = 64
PAIR = 2 * HEAD_DIM
STEP_COUNT = 10
EPS_NORM = 1e-05
ROPE_BASE = 160000.0
NEG_FILL = -1e30
CLIP_LIMIT = 10.0
BETA_FIRST = 0.9
BETA_SECOND = 0.98
EPS_ADAM = 1e-06
STEP_RATES = (0.1, 0.5, 0.1, 0.1, 1.0)
DECAY_RATES = (0.01, 0.01, 0.01, 0.01, 0.0)
DOCS = 5
LOW = jnp.bfloat16
FULL = jnp.float32
SCALE = 1.0 / math.sqrt(HEAD_DIM)
WEIGHT = 20_000_000_000
EARLY = 20_000_000_000


def doc_positions(segment_ids):
    seq_len = segment_ids.shape[-1]
    places = jnp.arange(seq_len, dtype=jnp.int32)
    first_mark = jnp.ones((1,), jnp.bool_)
    change = jnp.concatenate([first_mark, segment_ids[1:] != segment_ids[:-1]])
    starts = lax.cummax(jnp.where(change, places, 0), axis=0)
    return places - starts


def rope_tables(positions):
    half_dim = HEAD_DIM // 2
    exponents = jnp.arange(half_dim, dtype=jnp.float32) * (2.0 / HEAD_DIM)
    inv_freq = ROPE_BASE ** (-exponents)
    angles = positions.astype(jnp.float32)[:, None] * inv_freq
    cos_part, sin_part = jnp.cos(angles), jnp.sin(angles)
    return (
        jnp.concatenate([cos_part] * 4, axis=1),
        jnp.concatenate([-sin_part, sin_part] * 2, axis=1),
    )


def adam_step(weight, first_old, second_old, gradient, factor, step_rate, decay_rate):
    first_new = BETA_FIRST * first_old + ((1.0 - BETA_FIRST) * factor) * gradient
    second_new = BETA_SECOND * second_old + ((1.0 - BETA_SECOND) * factor * factor) * (
        gradient * gradient
    )
    unbias = math.sqrt(1.0 - BETA_SECOND**STEP_COUNT)
    rate = step_rate / (1.0 - BETA_FIRST**STEP_COUNT) * unbias
    step = first_new * rate / (second_new * lax.rsqrt(second_new) + EPS_ADAM * unbias)
    return (weight * (1.0 - step_rate * decay_rate) - step, first_new, second_new)


def mul(left, right):
    return lax.dot_general(left, right, (((1,), (0,)), ((), ())), preferred_element_type=FULL)


def mul_t(left, right):
    return lax.dot_general(left, right, (((1,), (1,)), ((), ())), preferred_element_type=FULL)


def normalize(values):
    centered = values - jnp.mean(values, axis=-1, keepdims=True)
    root = lax.rsqrt(jnp.mean(centered * centered, axis=-1, keepdims=True) + EPS_NORM)
    return centered * root, root


def normalize_back(grad, gain, scaled, root):
    t = grad * gain
    back = root * (
        t
        - jnp.mean(t, axis=-1, keepdims=True)
        - scaled * jnp.mean(t * scaled, axis=-1, keepdims=True)
    )
    return back


def turn(values, cos_part, sin_part):
    lane = lax.broadcasted_iota(jnp.int32, values.shape, 1)
    swapped = jnp.where(
        lane % HEAD_DIM < HEAD_DIM // 2,
        pltpu.roll(values, PAIR - HEAD_DIM // 2, 1),
        pltpu.roll(values, HEAD_DIM // 2, 1),
    )
    return values * cos_part + swapped * sin_part


def three_parts(values):
    high = values.astype(LOW).astype(FULL)
    rest = values - high
    mid = rest.astype(LOW).astype(FULL)
    return high, mid, rest - mid


def wait_all(copies):
    for copy in copies:
        copy.wait()


def put(source, target, sem):
    copy = pltpu.make_async_copy(source, target, sem)
    copy.start()
    return copy


PIECES = ((0, None), (1, None), (2, 0), (2, 1), (3, 0), (3, 1))


def join_blocks(at_ref, blocks, whole):
    rows = blocks[0].shape[0]
    for block, (bits, part) in zip(blocks, PIECES):
        start = (at_ref[0] ^ bits) * rows
        size = rows
        if part is not None:
            size = rows // 2
            start += (at_ref[1] ^ part) * size
        whole[pl.ds(pl.multiple_of(start, size), size), :] = block[...]


def join_folded(at_ref, blocks, w_out, w_down):
    rows, width = blocks[0].shape[0], w_out.shape[1]
    short, last = rows // 2, width // 2
    for block, (bits, part) in zip(blocks, PIECES):
        owner = at_ref[0] ^ bits
        base = owner * (rows + short)
        first = 0 if part is None else (at_ref[1] ^ part) * short
        size = rows if part is None else short
        span = pl.ds(pl.multiple_of(owner * rows + first, short), size)
        w_out[span, :] = block[:, :width]
        span = pl.ds(pl.multiple_of(base + first, short), size)
        w_down[span, :] = block[:, width : 2 * width]
        span = pl.ds(pl.multiple_of(base + rows, short), short)
        if part is None:
            for i in range(2):
                w_down[span, i * last : (i + 1) * last] = block[
                    i * short : (i + 1) * short, 2 * width :
                ]
        else:
            lanes = pl.ds(pl.multiple_of((at_ref[1] ^ part) * last, last), last)
            w_down[span, lanes] = block[:, 2 * width :]


def fold(out, w_out, w_down, first):
    rows, width = w_out.shape
    short, last = rows // 2, width // 2
    out[:, first : first + width] = w_out[...].astype(LOW)
    out[:, first + width : first + 2 * width] = w_down[:rows, :].astype(LOW)
    for i in range(2):
        out[i * short : (i + 1) * short, first + 2 * width :] = w_down[
            rows:, i * last : (i + 1) * last
        ].astype(LOW)


def prepare_first_kernel(at_ref, w_ref, gains_ref, half_ref, gains_out, wide, sem):
    short = half_ref.shape[0]
    span = pl.ds(pl.multiple_of(at_ref[1] * short, short), short)
    copy = put(w_ref.at[span, :], wide, sem.at[0])
    gains_out[...] = gains_ref[...].astype(LOW)
    copy.wait()
    half_ref[...] = wide[...].astype(LOW)


def prepare_rest_kernel(at_ref, tokens_ref, in_ref, out_ref, down_ref, qkv_ref, cot_ref,
                        their_tokens, low_in, part_in, low_od, half_od, low_qkv, their_cot,
                        in_wide, out_wide, down_wide, qkv_wide, sem):
    slot = 1 - at_ref[2]
    copies = [
        put(source, target, sem.at[i])
        for i, (source, target) in enumerate((
            (tokens_ref.at[slot], their_tokens), (in_ref, in_wide), (out_ref, out_wide),
            (down_ref, down_wide), (qkv_ref, qkv_wide), (cot_ref.at[slot], their_cot),
        ))
    ]
    short = part_in.shape[0]
    span = pl.ds(pl.multiple_of((2 * at_ref[1] + at_ref[4]) * short, short), short)
    copies[1].wait()
    part_in[...] = in_wide[span, :].astype(LOW)
    low_in[...] = in_wide[...].astype(LOW)
    copies[2].wait()
    copies[3].wait()
    fold(low_od, out_wide, down_wide, 0)
    short = half_od.shape[0]
    half_od[...] = low_od[pl.ds(pl.multiple_of(at_ref[1] * short, short), short), :]
    copies[4].wait()
    low_qkv[...] = qkv_wide[...].astype(LOW)
    copies[0].wait()
    copies[5].wait()


def project_kernel(at_ref, tokens_ref, far_ref, gain_ref, cos_ref, sin_ref, w0, w1, w2, w3, w4, w5,
                   normed_ref, query_ref, kv_ref, weight):
    join_blocks(at_ref, (w0, w1, w2, w3, w4, w5), weight)
    rows, width = far_ref.shape
    for part in range(2):
        values = tokens_ref[at_ref[2]] if part == 0 else far_ref[...]
        scaled, _ = normalize(values.astype(FULL))
        normed_ref[pl.ds(part * rows, rows), :] = (scaled * gain_ref[...]).astype(LOW)
    for part in range(2):
        span = pl.ds(part * rows, rows)
        normed = normed_ref[span, :]
        cos_part, sin_part = cos_ref[span, :], sin_ref[span, :]
        for pair in range(2 * width // PAIR):
            lanes = pl.ds(pair * PAIR, PAIR)
            if pair % 2 == 0:
                both = mul(normed, weight[:, pl.ds(pair * PAIR, 2 * PAIR)])
            raw = both[:, (pair % 2) * PAIR : (pair % 2 + 1) * PAIR]
            turned = turn(raw, cos_part, sin_part)
            if pair < width // PAIR:
                query_ref[span, lanes] = (turned * SCALE).astype(LOW)
            else:
                kv_ref[0, span, pl.ds(pair * PAIR - width, PAIR)] = turned.astype(LOW)
        kv_ref[1, span, :] = mul(normed, weight[:, 2 * width :]).astype(LOW)


def head_lanes(head, shape):
    lane = lax.broadcasted_iota(jnp.int32, shape, 1)
    return (lane < HEAD_DIM) if head == 0 else (lane >= HEAD_DIM)


def pick(head, inside, outside):
    return jnp.where(head_lanes(head, inside.shape), inside, outside)


def attend_kernel(query_ref, near_ref, far_ref, mark_query_ref, mark_key_ref, o_ref, extra_ref):
    rows = query_ref.shape[0]
    query = query_ref[...]
    mark_query = mark_query_ref[...]
    parts = [
        (near_ref[0], jnp.transpose(near_ref[1]), mark_key_ref[:rows, :]),
        (far_ref[0], jnp.transpose(far_ref[1]), mark_key_ref[rows:, :]),
    ]
    outs, logs = [], []
    for head in range(2):
        query_head = pick(head, query, mark_query)
        scores = [mul_t(pick(head, key, mark), query_head) for key, _, mark in parts]
        top = jnp.maximum(
            jnp.max(scores[0], axis=0, keepdims=True), jnp.max(scores[1], axis=0, keepdims=True)
        )
        exps = [jnp.exp(score - top) for score in scores]
        total = jnp.sum(exps[0], axis=0, keepdims=True) + jnp.sum(exps[1], axis=0, keepdims=True)
        span = slice(head * HEAD_DIM, (head + 1) * HEAD_DIM)
        out = sum(mul(value_t[span], e.astype(LOW)) for (_, value_t, _), e in zip(parts, exps))
        outs.append(out / total)
        logs.append(top + jnp.log(total))
    o_ref[...] = jnp.transpose(jnp.concatenate(outs)).astype(LOW)
    line = lax.broadcasted_iota(jnp.int32, (PAIR, rows), 0)
    extra = jnp.zeros((PAIR, rows), FULL)
    for head in range(2):
        base = DOCS + (HEAD_DIM if head == 0 else 0)
        for i, piece in enumerate(three_parts(-logs[head])):
            extra = jnp.where(line == base + i, piece, extra)
    extra_ref[...] = jnp.transpose(extra).astype(LOW) + mark_query


def attend_back_kernel(query_ref, near_ref, far_ref, extra_ref, mark_key_ref, o_ref, do_ref,
                       cos_ref, sin_ref, dq_ref, keep_ref, send_ref):
    rows = query_ref.shape[0]
    query, extra, do = query_ref[...], extra_ref[...], do_ref[...]
    inner_all = do.astype(FULL) * o_ref[...].astype(FULL)
    lane = lax.broadcasted_iota(jnp.int32, (rows, PAIR), 1)
    zero = jnp.zeros((rows, PAIR), LOW)
    grads_query = []
    sums = [[None, None], [None, None]]
    keys_t = [jnp.transpose(near_ref[0]), jnp.transpose(far_ref[0])]
    for head in range(2):
        inside = head_lanes(head, (rows, PAIR))
        inner = jnp.sum(jnp.where(inside, inner_all, 0.0), axis=1, keepdims=True)
        base = DOCS + (HEAD_DIM if head == 0 else 0)
        tail = jnp.zeros((rows, PAIR), FULL)
        for i, piece in enumerate(three_parts(-inner)):
            tail = jnp.where(lane == base + i, piece, tail)
        query_head = pick(head, query, extra)
        do_head = pick(head, do, tail.astype(LOW))
        query_only = pick(head, query, zero)
        do_only = pick(head, do, zero)
        span = slice(head * HEAD_DIM, (head + 1) * HEAD_DIM)
        grad_query = 0.0
        for part, ref in enumerate((near_ref, far_ref)):
            mark = mark_key_ref[pl.ds(part * rows, rows), :]
            probs = jnp.exp(mul_t(pick(head, ref[0], mark), query_head))
            grad_probs = mul_t(pick(head, ref[1], mark), do_head)
            grad_scores = (probs * grad_probs).astype(LOW)
            grad_value = mul(probs.astype(LOW), do_only)
            grad_key = mul(grad_scores, query_only)
            grad_query += mul(keys_t[part][span], grad_scores)
            if head == 0:
                sums[part] = [grad_key, grad_value]
            else:
                sums[part] = [sums[part][0] + grad_key, sums[part][1] + grad_value]
        grads_query.append(grad_query)
    turned = turn(
        jnp.transpose(jnp.concatenate(grads_query)) * SCALE, cos_ref[...], -sin_ref[...]
    )
    dq_ref[...] = turned.astype(LOW)
    for i in range(2):
        keep_ref[i] = sums[0][i].astype(LOW)
        send_ref[i] = sums[1][i].astype(LOW)


def middle_kernel(at_ref, live_ref, tokens_ref, far_ref, cot_ref, cot_far_ref,
                  oa_ref, ob_ref, oc_ref, gain_ref, i0, i1, i2, i3, i4, i5, d0, d1, d2, d3, d4, d5,
                  mixed_ref, mixed_far_ref, dx1_ref, do_ref, keep_ref, send_ref,
                  w_out, w_in, w_down, o_all, o_t, a2_t, h_t, h_all, dm_all, duw_all, db_all,
                  mixed, dx1_all, do_all, keep, send, out_sem):
    place, slot = at_ref[0], at_ref[2]
    live = live_ref[slot].astype(FULL)
    join_folded(at_ref, (d0, d1, d2, d3, d4, d5), w_out, w_down)
    join_blocks(at_ref, (i0, i1, i2, i3, i4, i5), w_in)
    rows, width = far_ref.shape
    share = width // 4
    short, units = share // 2, w_down.shape[0]
    gain = gain_ref[...]
    first = 0
    for ref in (oa_ref, ob_ref, oc_ref):
        o_all[:, first : first + ref.shape[1]] = ref[...]
        first += ref.shape[1]
    copies = []
    for part in range(2):
        span = pl.ds(part * rows, rows)
        o = o_all[span, :]
        values = tokens_ref[slot] if part == 0 else far_ref[...]
        x1 = values.astype(FULL) + live * mul(o, w_out[...])
        scaled, root = normalize(x1)
        a2 = (scaled * gain).astype(LOW)
        cot = (cot_ref[slot] if part == 0 else cot_far_ref[...]).astype(FULL)
        dm = (live * cot).astype(LOW)
        for first in range(0, units, units // 3):
            lanes = slice(first, first + units // 3)
            lanes_lin = slice(units + first, units + first + units // 3)
            u = mul(a2, w_in[:, lanes])
            w = mul(a2, w_in[:, lanes_lin])
            dh = mul_t(dm, w_down[lanes, :])
            phi = 0.5 * (1.0 + lax.erf(u * math.sqrt(0.5)))
            gelu = u * phi
            slope = phi + u * (jnp.exp(-0.5 * u * u) * (1.0 / math.sqrt(2.0 * math.pi)))
            h_all[:, lanes] = (gelu * w).astype(LOW)
            duw_all[span, lanes] = (dh * w * slope).astype(LOW)
            duw_all[span, lanes_lin] = (dh * gelu).astype(LOW)
        h = h_all[...]
        mixed[span, :] = (x1 + live * mul(h, w_down[...])).astype(LOW)
        target = mixed_ref.at[slot] if part == 0 else mixed_far_ref
        copies.append(put(mixed.at[span, :], target, out_sem.at[len(copies)]))
        da2 = mul_t(duw_all[span, :], w_in[...])
        dx1 = cot + normalize_back(da2, gain, scaled, root)
        dx1_all[span, :] = dx1
        copies.append(put(dx1_all.at[span, :], dx1_ref.at[span, :], out_sem.at[len(copies)]))
        db = (live * dx1).astype(LOW)
        do_all[span, :] = mul_t(db, w_out[...]).astype(LOW)
        copies.append(put(do_all.at[span, :], do_ref.at[span, :], out_sem.at[len(copies)]))
        db_all[span, :] = db
        dm_all[span, :] = dm
        o_t[:, span] = jnp.transpose(o)
        a2_t[:, span] = jnp.transpose(a2)
        h_t[:, span] = jnp.transpose(h)
    dm, duw, db = dm_all[...], duw_all[...], db_all[...]
    for j, out, target in ((1, send, send_ref), (3, send, send_ref), (0, keep, keep_ref), (2, keep, keep_ref)):
        span = pl.ds(pl.multiple_of((place ^ j) * share, share), share)
        base = (place ^ j) * (share + short)
        down = pl.ds(pl.multiple_of(base, short), share)
        down_last = pl.ds(pl.multiple_of(base + share, short), short)
        at = 2 * units
        out[j // 2, :, :at] = mul(a2_t[span, :], duw).astype(LOW)
        out[j // 2, :, at : at + width] = mul(o_t[span, :], db).astype(LOW)
        at += width
        out[j // 2, :, at : at + width] = mul(h_t[down, :], dm).astype(LOW)
        at += width
        last = mul(h_t[down_last, :], dm).astype(LOW)
        out[j // 2, :short, at:] = last[:, : width // 2]
        out[j // 2, short:, at:] = last[:, width // 2 :]
        copies.append(put(out.at[j // 2], target.at[j // 2], out_sem.at[len(copies)]))
    wait_all(copies)


def send_kernel(count, at_ref, *refs):
    normed_ref = refs[0]
    dqs, owns, gots = (refs[1 + i * count : 1 + (i + 1) * count] for i in range(3))
    (cos_ref, sin_ref, dqkv_ref, normed_t_ref, send_ref,
     dqkv, normed_t, send, sem) = refs[1 + 3 * count :]
    width = normed_ref.shape[1]
    part_width = width // count
    normed_t[...] = jnp.transpose(normed_ref[...])
    copies = [put(normed_t, normed_t_ref, sem.at[0])]
    cos_part, sin_part = cos_ref[...], -sin_ref[...]
    for part, (dq, own, got) in enumerate(zip(dqs, owns, gots)):
        base = part * part_width
        dqkv[:, pl.ds(base, part_width)] = dq[...]
        dqkv[:, pl.ds(2 * width + base, part_width)] = (
            own[1].astype(FULL) + got[1].astype(FULL)
        ).astype(LOW)
        for pair in range(part_width // PAIR):
            lanes = pl.ds(pair * PAIR, PAIR)
            raw = own[0, :, lanes].astype(FULL) + got[0, :, lanes].astype(FULL)
            dqkv[:, pl.ds(width + base + pair * PAIR, PAIR)] = turn(raw, cos_part, sin_part).astype(
                LOW
            )
    copies.append(put(dqkv, dqkv_ref, sem.at[1]))
    right = dqkv[...]
    share = send.shape[1]
    for j in (1, 3):
        start = pl.multiple_of((at_ref[0] ^ j) * share, share)
        send[j // 2] = mul(normed_t[pl.ds(start, share), :], right).astype(LOW)
        copies.append(put(send.at[j // 2], send_ref.at[j // 2], sem.at[len(copies)]))
    wait_all(copies)


def keep_kernel(at_ref, normed_t_ref, dqkv_ref, keep_ref, keep, sem):
    right = dqkv_ref[...]
    share = keep.shape[1]
    copies = []
    for j in (0, 2):
        start = pl.multiple_of((at_ref[0] ^ j) * share, share)
        keep[j // 2] = mul(normed_t_ref[pl.ds(start, share), :], right).astype(LOW)
        copies.append(put(keep.at[j // 2], keep_ref.at[j // 2], sem.at[len(copies)]))
    wait_all(copies)


def input_kernel(at_ref, tokens_ref, far_ref, gain_ref, dx1_ref, dqkv_ref, w0, w1, w2, w3, w4, w5,
                 grad_ref, grad_far_ref, weight, grad_own, out_sem):
    join_blocks(at_ref, (w0, w1, w2, w3, w4, w5), weight)
    rows = far_ref.shape[0]
    gain = gain_ref[...]
    for part in (1, 0):
        span = pl.ds(part * rows, rows)
        values = tokens_ref[at_ref[2]] if part == 0 else far_ref[...]
        scaled, root = normalize(values.astype(FULL))
        back = normalize_back(mul_t(dqkv_ref[span, :], weight[...]), gain, scaled, root)
        grad = dx1_ref[span, :] + back
        if part == 1:
            grad_far_ref[...] = grad.astype(LOW)
        else:
            grad_own[...] = grad
    put(grad_own, grad_ref.at[at_ref[2]], out_sem.at[0]).wait()


def shaped(*shape, kind=LOW):
    return jax.ShapeDtypeStruct(shape, kind)


IN_SMEM = pl.BlockSpec(memory_space=pltpu.SMEM)
IN_VMEM = pl.BlockSpec(memory_space=pltpu.VMEM)
IN_ANY = pl.BlockSpec(memory_space=pl.ANY)


def params(mebibytes):
    return pltpu.CompilerParams(vmem_limit_bytes=int(mebibytes * 1024 * 1024))


def call(kernel, args, in_specs, out_shape, out_specs, late=(), **options):
    if not isinstance(out_shape, tuple):
        out_shape, out_specs = (out_shape,), (out_specs,)
    count, skip, outs = len(args), len(late), len(out_shape)

    def body(*refs):
        outs_at = count + skip
        return kernel(*refs[:count], *refs[outs_at : outs_at + outs], *refs[outs_at + outs + 1 :])

    return pl.pallas_call(
        body,
        in_specs=list(in_specs) + [IN_ANY] * skip,
        out_shape=out_shape + (shaped(8, 128, kind=FULL),),
        out_specs=out_specs + (IN_ANY,),
        **options,
    )(*args, *late)


def gate(values, late=(), weight=0):
    hint = {}
    if weight:
        hint["cost_estimate"] = pl.CostEstimate(
            flops=weight, transcendentals=0, bytes_accessed=0
        )
    return call(
        lambda *refs: None,
        values,
        late=late,
        out_shape=tuple(jax.ShapeDtypeStruct(v.shape, v.dtype) for v in values),
        in_specs=[IN_ANY] * len(values),
        out_specs=(IN_ANY,) * len(values),
        input_output_aliases={i: i for i in range(len(values))},
        compiler_params=params(1),
        name="gate",
        **hint,
    )[: len(values)]


def join_two_kernel(at_ref, mine, other, out):
    short = mine.shape[0]
    out[pl.ds(pl.multiple_of(at_ref[4] * short, short), short), :] = mine[...]
    out[pl.ds(pl.multiple_of((1 - at_ref[4]) * short, short), short), :] = other[...]


def join_two(at, mine, other, late=()):
    rows, width = mine.shape
    return call(
        join_two_kernel,
        (at, mine, other),
        late=late,
        out_shape=shaped(2 * rows, width),
        in_specs=[IN_SMEM] + [IN_VMEM] * 2,
        out_specs=IN_VMEM,
        compiler_params=params(4),
        name="join_two",
    )


def in_hbm(value):
    return pltpu.with_memory_space_constraint(value, pltpu.HBM)


def in_vmem(*values):
    return [pltpu.with_memory_space_constraint(value, pltpu.VMEM) for value in values]


def prepare_first(at, weight, gains):
    rows, width = weight.shape
    return call(
        prepare_first_kernel,
        (at, in_hbm(weight), gains),
        out_shape=(shaped(rows // 2, width), shaped(*gains.shape)),
        in_specs=[IN_SMEM, IN_ANY, IN_VMEM],
        out_specs=(IN_VMEM,) * 2,
        scratch_shapes=[pltpu.VMEM((rows // 2, width), FULL), pltpu.SemaphoreType.DMA((1,))],
        compiler_params=params(6),
        name="prepare_first",
    )


def prepare_rest(at, tokens, w_in, w_out, w_down, w_qkv, cotangent, late):
    rows, width = w_out.shape
    folded = 2 * width + width // 2
    return call(
        prepare_rest_kernel,
        (at, *[in_hbm(v) for v in (tokens, w_in, w_out, w_down, w_qkv, cotangent)]),
        late=late,
        out_shape=(
            shaped(*tokens.shape[1:]),
            shaped(*w_in.shape),
            shaped(rows // 4, w_in.shape[1]),
            shaped(rows, folded),
            shaped(rows // 2, folded),
            shaped(*w_qkv.shape),
            shaped(*cotangent.shape[1:]),
        ),
        in_specs=[IN_SMEM] + [IN_ANY] * 6,
        out_specs=(IN_VMEM,) * 7,
        scratch_shapes=[
            pltpu.VMEM(v.shape, FULL) for v in (w_in, w_out, w_down, w_qkv)
        ] + [pltpu.SemaphoreType.DMA((6,))],
        compiler_params=params(18),
        name="prepare_rest",
    )


def project(at, tokens, far, gain, cos_part, sin_part, blocks, late):
    rows, width = 2 * far.shape[0], far.shape[1]
    return call(
        project_kernel,
        (at, tokens, *in_vmem(far), gain, cos_part, sin_part, *in_vmem(*blocks)),
        late=late,
        out_shape=(shaped(rows, width), shaped(rows, width), shaped(2, rows, width)),
        in_specs=[IN_SMEM] + [IN_VMEM] * 11,
        out_specs=(IN_VMEM,) * 3,
        scratch_shapes=[pltpu.VMEM((width, 3 * width), LOW)],
        compiler_params=params(18),
        name="project",
    )


def attend(first, count, query, near, far, mark_query, mark_key, late=()):
    rows = query.shape[0]
    row_spec = pl.BlockSpec((rows, PAIR), lambda i: (0, i + first))
    kv_spec = pl.BlockSpec((2, rows, PAIR), lambda i: (0, 0, i + first))
    out_spec = pl.BlockSpec((rows, PAIR), lambda i: (0, i))
    return call(
        attend_kernel,
        (*in_vmem(query, near, far), mark_query, mark_key),
        late=late,
        grid=(count,),
        out_shape=(shaped(rows, count * PAIR), shaped(rows, count * PAIR)),
        in_specs=[
            row_spec,
            kv_spec,
            kv_spec,
            pl.BlockSpec((rows, PAIR), lambda i: (0, 0)),
            pl.BlockSpec((2 * rows, PAIR), lambda i: (0, 0)),
        ],
        out_specs=(out_spec, out_spec),
        compiler_params=params(16),
        name="attend",
    )


def attend_back(
    first, first_o, count, query, near, far, extra, o, mark_key, do, cos_part, sin_part, late=()
):
    rows = query.shape[0]
    row_spec = pl.BlockSpec((rows, PAIR), lambda i: (0, i + first))
    o_spec = pl.BlockSpec((rows, PAIR), lambda i: (0, i + first_o))
    kv_spec = pl.BlockSpec((2, rows, PAIR), lambda i: (0, 0, i + first))
    fixed = pl.BlockSpec((rows, PAIR), lambda i: (0, 0))
    out_row = pl.BlockSpec((rows, PAIR), lambda i: (0, i))
    out_kv = pl.BlockSpec((2, rows, PAIR), lambda i: (0, 0, i))
    return call(
        attend_back_kernel,
        (*in_vmem(query, near, far, extra), mark_key, *in_vmem(o, do), cos_part, sin_part),
        late=late,
        grid=(count,),
        out_shape=(
            shaped(rows, count * PAIR),
            shaped(2, rows, count * PAIR),
            shaped(2, rows, count * PAIR),
        ),
        in_specs=[
            row_spec,
            kv_spec,
            kv_spec,
            o_spec,
            pl.BlockSpec((2 * rows, PAIR), lambda i: (0, 0)),
            o_spec,
            row_spec,
            fixed,
            fixed,
        ],
        out_specs=(out_row, out_kv, out_kv),
        compiler_params=params(20),
        name="attend_back",
    )


def middle(at, live, tokens, far, cot, cot_far, o_parts, gain, blocks_in, blocks_od):
    half, width = far.shape
    rows, share = 2 * half, width // 4
    units = blocks_in[0].shape[1] // 2
    total = 2 * units + blocks_od[0].shape[1]
    assert units == 4 * (share + share // 2)
    low = lambda *shape: pltpu.VMEM(shape, LOW)
    return call(
        middle_kernel,
        (at, live, tokens, *in_vmem(far), cot, *in_vmem(cot_far, *o_parts), gain,
         *in_vmem(*blocks_in, *blocks_od)),
        out_shape=(
            shaped(2, half, width),
            shaped(half, width),
            shaped(rows, width, kind=FULL),
            shaped(rows, width),
            shaped(2, share, total),
            shaped(2, share, total),
        ),
        in_specs=[IN_SMEM] * 2 + [IN_VMEM] * 20,
        out_specs=(IN_ANY,) * 6,
        scratch_shapes=[
            low(width, width),
            low(width, 2 * units),
            low(units, width),
            low(rows, width),
            low(width, rows),
            low(width, rows),
            low(units, rows),
            low(half, units),
            low(rows, width),
            low(rows, 2 * units),
            low(rows, width),
            low(rows, width),
            pltpu.VMEM((rows, width), FULL),
            low(rows, width),
            low(2, share, total),
            low(2, share, total),
            pltpu.SemaphoreType.DMA((10,)),
        ],
        compiler_params=params(44),
        name="middle",
    )


def qkv_send(at, normed, dq, own, got, cos_part, sin_part, late):
    rows, width = normed.shape
    share = width // 4
    return call(
        functools.partial(send_kernel, len(dq)),
        (at, normed, *dq, *own, *got, cos_part, sin_part),
        late=late,
        out_shape=(
            shaped(rows, 3 * width),
            shaped(width, rows),
            shaped(2, share, 3 * width),
        ),
        in_specs=[IN_SMEM] + [IN_VMEM] * (3 + 3 * len(dq)),
        out_specs=(IN_ANY,) * 3,
        scratch_shapes=[
            pltpu.VMEM((rows, 3 * width), LOW),
            pltpu.VMEM((width, rows), LOW),
            pltpu.VMEM((2, share, 3 * width), LOW),
            pltpu.SemaphoreType.DMA((4,)),
        ],
        compiler_params=params(20),
        name="qkv_send",
    )


def qkv_keep(at, normed_t, dqkv, late):
    width, rows = normed_t.shape
    share = width // 4
    return call(
        keep_kernel,
        (at, normed_t, dqkv),
        late=late,
        out_shape=shaped(2, share, 3 * width),
        in_specs=[IN_SMEM] + [IN_VMEM] * 2,
        out_specs=IN_ANY,
        scratch_shapes=[
            pltpu.VMEM((2, share, 3 * width), LOW),
            pltpu.SemaphoreType.DMA((2,)),
        ],
        compiler_params=params(16),
        name="qkv_keep",
    )


def input_back(at, tokens, far, gain, dx1, dqkv, blocks, late):
    half, width = far.shape
    return call(
        input_kernel,
        (at, tokens, far, gain, dx1, *in_vmem(dqkv, *blocks)),
        late=late,
        out_shape=(shaped(2, half, width, kind=FULL), shaped(half, width)),
        in_specs=[IN_SMEM] + [IN_VMEM] * 11,
        out_specs=(IN_ANY, IN_VMEM),
        scratch_shapes=[
            pltpu.VMEM((width, 3 * width), LOW),
            pltpu.VMEM((half, width), FULL),
            pltpu.SemaphoreType.DMA((1,)),
        ],
        compiler_params=params(20),
        name="input_back",
    )


def first_sums_kernel(at_ref, keep, got, own_a, far_a, mine_b, give_b):
    cut, short = far_a.shape[0], give_b.shape[1]

    def add(block, start, size):
        span = pl.ds(start, size)
        return (keep[block, span, :].astype(FULL) + got[block, span, :].astype(FULL)).astype(LOW)

    far_a[...] = add(1, 0, cut)
    for block in range(2):
        give_b[block] = add(block, pl.multiple_of(cut + (1 - at_ref[1]) * short, short), short)
        mine_b[block] = add(block, pl.multiple_of(cut + at_ref[1] * short, short), short)
    own_a[...] = add(0, 0, cut)


def first_sums(at, keep, got, late=()):
    _, rows, width = keep.shape
    cut, short = rows // 2, rows // 4
    return call(
        first_sums_kernel,
        (at, keep, got),
        late=late,
        out_shape=(shaped(cut, width),) * 2 + (shaped(2, short, width),) * 2,
        in_specs=[IN_SMEM] + [IN_VMEM] * 2,
        out_specs=(IN_VMEM,) * 4,
        compiler_params=params(20),
        name="first_sums",
    )


def second_sums_kernel(at_ref, own_a, got_a, mine_b, got_b, mine_a, give_a, near_b, far_b):
    short = mine_a.shape[0]
    for start, out in ((1 - at_ref[1], give_a), (at_ref[1], mine_a)):
        span = pl.ds(pl.multiple_of(start * short, short), short)
        out[...] = (own_a[span, :].astype(FULL) + got_a[span, :].astype(FULL)).astype(LOW)
    for block, out in ((1, far_b), (0, near_b)):
        out[...] = (mine_b[block].astype(FULL) + got_b[block].astype(FULL)).astype(LOW)


def second_sums(at, own_a, got_a, mine_b, got_b, late=()):
    _, short, width = mine_b.shape
    return call(
        second_sums_kernel,
        (at, own_a, got_a, mine_b, got_b),
        late=late,
        out_shape=(shaped(short, width),) * 4,
        in_specs=[IN_SMEM] + [IN_VMEM] * 4,
        out_specs=(IN_VMEM,) * 4,
        compiler_params=params(12),
        name="second_sums",
    )


def third_sums_kernel(at_ref, mine_a, got_a, near_b, got_b, keep, give):
    upper = mine_a[...].astype(FULL) + got_a[...].astype(FULL)
    lower = near_b[...].astype(FULL) + got_b[...].astype(FULL)
    keep[...] = jnp.where(at_ref[4] == 0, upper, lower).astype(LOW)
    give[...] = jnp.where(at_ref[4] == 0, lower, upper).astype(LOW)


def third_sums(at, mine_a, got_a, near_b, got_b, late=()):
    return call(
        third_sums_kernel,
        (at, mine_a, got_a, near_b, got_b),
        late=late,
        out_shape=(shaped(*mine_a.shape),) * 2,
        in_specs=[IN_SMEM] + [IN_VMEM] * 4,
        out_specs=(IN_VMEM,) * 2,
        compiler_params=params(12),
        name="third_sums",
    )


def squares_kernel(at_ref, qkv, w_qkv, rest, w_in, gains, out):
    inner = w_in.shape[1]
    total = jnp.sum(jnp.square(rest[:, inner:].astype(FULL)), keepdims=True)
    rows = qkv.shape[0]
    shape = (rows, gains.shape[1])
    offset = lax.broadcasted_iota(jnp.int32, shape, 1) - lax.broadcasted_iota(jnp.int32, shape, 0)
    for i, (piece, weight) in enumerate(((qkv, w_qkv), (rest, w_in))):
        start = at_ref[3]
        span = pl.ds(pl.multiple_of(start, 8), rows)
        values = piece[:, : weight.shape[1]].astype(FULL)
        sums = jnp.sum(weight[span, :].astype(LOW).astype(FULL) * values, axis=1, keepdims=True)
        gain = gains[i : i + 1, :].astype(LOW).astype(FULL)
        gain = jnp.sum(jnp.where(offset == start, gain, 0.0), axis=1, keepdims=True)
        total += jnp.sum(jnp.square(values), keepdims=True)
        total += jnp.sum(jnp.square(sums / gain), keepdims=True)
    out[...] = jnp.broadcast_to(total, out.shape)


def squares(*args):
    return call(
        squares_kernel,
        args,
        out_shape=shaped(8, 128, kind=FULL),
        in_specs=[IN_SMEM] + [IN_VMEM] * (len(args) - 1),
        out_specs=IN_VMEM,
        compiler_params=params(10),
        name="squares",
    )


def add_kernel(count, *refs):
    for i in range(count):
        out = refs[2 * count + i]
        out[...] = (refs[i][...].astype(FULL) + refs[count + i][...].astype(FULL)).astype(out.dtype)


def add(first, second, late=()):
    count = len(first)
    return call(
        functools.partial(add_kernel, count),
        (*first, *second),
        late=late,
        out_shape=tuple(jax.ShapeDtypeStruct(v.shape, v.dtype) for v in first),
        in_specs=[IN_VMEM] * (2 * count),
        out_specs=(IN_VMEM,) * count,
        compiler_params=params(8),
        name="add",
    )


def fill_kernel(at_ref, mixed_far, grad_far, mixed_in, grad_in, mixed, grad, wide, sem):
    first = put(mixed_far, mixed.at[1 - at_ref[2]], sem.at[0])
    wide[...] = grad_far[...].astype(FULL)
    put(wide, grad.at[1 - at_ref[2]], sem.at[1]).wait()
    first.wait()


def fill(at, mixed, mixed_far, grad, grad_far):
    return call(
        fill_kernel,
        (at, mixed_far, grad_far, mixed, grad),
        out_shape=(shaped(*mixed.shape), shaped(*grad.shape, kind=FULL)),
        in_specs=[IN_SMEM, IN_VMEM, IN_VMEM, IN_ANY, IN_ANY],
        out_specs=(IN_ANY,) * 2,
        input_output_aliases={3: 0, 4: 1},
        scratch_shapes=[pltpu.VMEM(grad_far.shape, FULL), pltpu.SemaphoreType.DMA((2,))],
        compiler_params=params(4),
        name="fill",
    )


def clip_factor(square_ref):
    norm = jnp.sqrt(square_ref[:1, :1])
    return jnp.minimum(1.0, CLIP_LIMIT / (norm + 1e-06))


def quarters(at_ref, parts):
    own, beside, other, other_beside = parts
    for i in range(4):
        same = at_ref[4] == i // 2
        near = jnp.where(same, own[...], beside[...])
        far = jnp.where(same, other[...], other_beside[...])
        yield jnp.where(at_ref[1] == i % 2, near, far).astype(FULL)


def gain_row(weight, gradient, start, shape):
    sums = jnp.sum(weight.astype(LOW).astype(FULL) * gradient, axis=1, keepdims=True)
    shape = (weight.shape[0], shape[1])
    offset = lax.broadcasted_iota(jnp.int32, shape, 1) - lax.broadcasted_iota(jnp.int32, shape, 0)
    return jnp.sum(jnp.where(offset == start, sums, 0.0), axis=0, keepdims=True)


class Update:
    def __init__(self, number, sources, news, targets, sem):
        self.number, self.sources, self.news, self.targets = number, sources, news, targets
        self.sem, self.out = sem, []

    def step(self, span, gradient, factor):
        rows, lanes = span
        short = (rows.stop - rows.start) // 2
        for i in range(2):
            part = (slice(rows.start + i * short, rows.start + (i + 1) * short), lanes)
            results = adam_step(
                self.sources[0][part], self.sources[1][part], self.sources[2][part],
                gradient[i * short : (i + 1) * short, :], factor,
                STEP_RATES[self.number], DECAY_RATES[self.number],
            )
            for result, new, target in zip(results, self.news, self.targets):
                new[part] = result
                self.out.append(put(new.at[part], target.at[part], self.sem.at[len(self.out)]))
        return self.sources[0][span]


def update_rest_kernel(at_ref, square_ref, *refs):
    parts, refs = refs[:4], refs[4:]
    sources, targets, row_ref, news, sem = refs[:9], refs[9:18], refs[18], refs[19:28], refs[28]
    inner, out, down = (
        Update(number, *(group[3 * k : 3 * k + 3] for group in (sources, news, targets)), sem.at[k])
        for k, number in enumerate((2, 1, 3))
    )
    factor = clip_factor(square_ref)
    rows, width = sources[3].shape
    lanes = sources[0].shape[1]
    short, last = rows // 4, width // 2
    row = jnp.zeros(row_ref.shape, FULL)
    for i, gradient in enumerate(quarters(at_ref, parts)):
        span = (slice(i * short, (i + 1) * short), slice(None))
        part = gradient[:, :lanes]
        row += gain_row(inner.step(span, part, factor), part, i * short, row_ref.shape)
        out.step(span, gradient[:, lanes : lanes + width], factor)
        down.step(span, gradient[:, lanes + width : lanes + 2 * width], factor)
        start = rows + (i % 2) * short
        span = (slice(start, start + short), slice((i // 2) * last, (i // 2 + 1) * last))
        down.step(span, gradient[:, lanes + 2 * width :], factor)
    row_ref[...] = row
    wait_all(inner.out + out.out + down.out)


def update_rest(at, square, parts, inner, out, down, late):
    like = [jax.ShapeDtypeStruct(v.shape, FULL) for v in (*inner, *out, *down)]
    return call(
        update_rest_kernel,
        (at, square, *parts, *inner, *out, *down),
        late=late,
        out_shape=(*like, shaped(1, inner[0].shape[0], kind=FULL)),
        in_specs=[IN_SMEM] + [IN_VMEM] * 14,
        out_specs=(IN_ANY,) * 9 + (IN_VMEM,),
        scratch_shapes=[pltpu.VMEM(v.shape, FULL) for v in like]
        + [pltpu.SemaphoreType.DMA((3, 48))],
        compiler_params=params(28),
        name="update_rest",
    )


def update_last_kernel(at_ref, square_ref, row_ref, g_w, g_m, g_v, *refs):
    parts, refs = refs[:4], refs[4:]
    sources, targets = refs[:3], refs[3:6]
    g_w_out, g_m_out, g_v_out, norm_out = refs[6:10]
    news, sem = refs[10:13], refs[13]
    qkv = Update(0, sources, news, targets, sem)
    factor = clip_factor(square_ref)
    norm_out[...] = jnp.sqrt(square_ref[...])
    short = sources[0].shape[0] // 4
    row = jnp.zeros(row_ref.shape, FULL)
    for i, gradient in enumerate(quarters(at_ref, parts)):
        span = (slice(i * short, (i + 1) * short), slice(None))
        row += gain_row(qkv.step(span, gradient, factor), gradient, i * short, row_ref.shape)
    for i, values in enumerate((row, row_ref[...])):
        line = slice(i, i + 1)
        gradient = values / g_w[line, :].astype(LOW).astype(FULL)
        g_w_out[line, :], g_m_out[line, :], g_v_out[line, :] = adam_step(
            g_w[line, :], g_m[line, :], g_v[line, :], gradient, factor,
            STEP_RATES[4], DECAY_RATES[4],
        )
    wait_all(qkv.out)


def update_last(at, square, qkv, qkv_parts, row, gains):
    like = [jax.ShapeDtypeStruct(v.shape, FULL) for v in qkv]
    return call(
        update_last_kernel,
        (at, square, row, *gains, *qkv_parts, *qkv),
        out_shape=(
            *like,
            *[jax.ShapeDtypeStruct(v.shape, FULL) for v in gains],
            jax.ShapeDtypeStruct(square.shape, FULL),
        ),
        in_specs=[IN_SMEM] + [IN_VMEM] * 12,
        out_specs=(IN_ANY,) * 3 + (IN_VMEM,) * 4,
        scratch_shapes=[pltpu.VMEM(v.shape, FULL) for v in like]
        + [pltpu.SemaphoreType.DMA((24,))],
        compiler_params=params(18),
        name="update_last",
    )


def low_sum(*values):
    return sum(value.astype(FULL) for value in values).astype(LOW)


def index(value, i):
    return lax.dynamic_index_in_dim(value, i, 0, keepdims=False)


def make(dp_count, seq_count):
    assert seq_count == 4 and dp_count >= 8 and dp_count & (dp_count - 1) == 0
    far_bits = [1 << i for i in range(2, dp_count.bit_length() - 1)]

    def trade(value, axis, bit):
        size = seq_count if axis == "seq" else dp_count
        return lax.ppermute(value, axis, [(i, i ^ bit) for i in range(size)])

    def on_device(
        tokens, cotangent, segments, valid,
        w_qkv, w_out, w_in, w_down, gains,
        m_qkv, m_out, m_in, m_down, m_gains,
        v_qkv, v_out, v_in, v_down, v_gains,
    ):
        place = lax.axis_index("seq")
        group = lax.axis_index("dp")
        slot = place >> 1
        half = group & 1
        local_len, width = tokens.shape[1:]
        rows = 2 * local_len
        share = w_qkv.shape[0]
        side = (group >> 1) & 1
        quarter = share // 4
        at = jnp.stack([place, half, slot, side * 2 * quarter + half * quarter, side])

        half_qkv, low_gains, begun = prepare_first(at, w_qkv, gains)
        (far_qa,) = gate((trade(half_qkv, "seq", 2),), weight=EARLY)
        (gain_far,) = gate((trade(low_gains, "seq", 2),), weight=2 * EARLY)
        their_tokens, low_in, part_in, low_od, half_od, low_qkv, their_cot, _ = prepare_rest(
            at, tokens, w_in, w_out, w_down, w_qkv, cotangent, (begun,)
        )
        near_q = trade(low_qkv, "seq", 1)
        far = trade(their_tokens, "seq", 2)
        far_qb = trade(far_qa, "dp", 1)
        near_qa = trade(far_qa, "seq", 1)
        near_qb = trade(far_qb, "seq", 1)
        gain_near = trade(jnp.stack([low_gains, gain_far]), "seq", 1)
        gain_stack = jnp.stack([low_gains, gain_near[0], gain_far, gain_near[1]])
        gain_low = jnp.concatenate(
            [index(gain_stack, b ^ place) for b in range(4)], axis=1
        ).astype(FULL)
        blocks_qkv = (low_qkv, near_q, far_qa, far_qb, near_qa, near_qb)
        low_in, low_od, part_in, half_od = gate((low_in, low_od, part_in, half_od), (far_qa,))
        near_i = trade(low_in, "seq", 1)
        near_o = trade(low_od, "seq", 1)
        (come_in,) = gate((trade(part_in, "seq", 2),), weight=EARLY)

        seg = index(segments, slot)
        positions = doc_positions(seg).reshape(4, local_len)
        seg = seg.reshape(4, local_len)
        chunks = [place, place ^ 2, place ^ 1, place ^ 3]
        seg_keys = jnp.concatenate([index(seg, c) for c in chunks])
        pos = jnp.concatenate([index(positions, c) for c in chunks[:2]])
        cos_part, sin_part = rope_tables(pos)
        lane = jnp.arange(PAIR, dtype=jnp.int32)[None] % HEAD_DIM
        same = seg_keys[:, None] == lane
        mark_key = jnp.where(lane < DOCS, 1.0 - same, (lane < DOCS + 3) * 1.0).astype(LOW)
        mark_query = jnp.where((lane < DOCS) & same[:rows], NEG_FILL, 0.0).astype(LOW)

        normed, query, kv, _ = project(
            at, tokens, far, gain_low[:1], cos_part, sin_part, blocks_qkv,
            (come_in, mark_key, mark_query),
        )
        kv_far = trade(kv, "seq", 1)
        (beside_in,) = gate((trade(come_in, "dp", 2),), weight=EARLY)
        far_ia, _ = join_two(at, come_in, beside_in)
        far_ib = trade(far_ia, "dp", 1)
        near_ia = trade(far_ia, "seq", 1)
        pairs = width // PAIR
        two = pairs // 3
        args = (query, kv, kv_far, mark_query, mark_key)
        o_a, extra_a, done_a = attend(0, two, *args)
        (far_oa,) = gate((trade(half_od, "seq", 2),), (done_a,), weight=EARLY)
        near_oa = trade(far_oa, "seq", 1)
        (their_cot,) = gate((their_cot,), (far_oa,))
        (cot_far,) = gate((trade(their_cot, "seq", 2),), weight=WEIGHT)
        far_ob = trade(far_oa, "dp", 1)
        o_b, extra_b, done_b = attend(two, two, *args, late=(done_a, far_oa))
        o_c, extra_c, done_c = attend(2 * two, pairs - 2 * two, *args, late=(done_b, far_ib))
        near_ib = trade(far_ib, "seq", 1)
        (far_ob,) = gate((far_ob,), (done_c,))
        near_ob = trade(far_ob, "seq", 1)
        blocks_in = (low_in, near_i, far_ia, far_ib, near_ia, near_ib)
        blocks_od = (low_od, near_o, far_oa, far_ob, near_oa, near_ob)

        mixed, mixed_far, dx1, do, keep_rest, send_rest, _ = middle(
            at, valid, tokens, far, cotangent, cot_far, (o_a, o_b, o_c), gain_low[1:], blocks_in, blocks_od
        )
        got_rest = trade(send_rest, "seq", 1)
        near_args = (query, kv, kv_far)
        back_args = (mark_key, do, cos_part, sin_part)
        dq0, own0, give0, back0 = attend_back(0, 0, two, *near_args, extra_a, o_a, *back_args)
        *r1, r1_done = first_sums(at, keep_rest, got_rest, late=(back0,))
        got_ra, got_rb = gate(
            (trade(r1[1], "seq", 2), trade(r1[3], "dp", 1)), weight=10 * WEIGHT
        )
        got0 = trade(give0, "seq", 1)
        dq1, own1, give1, back1 = attend_back(
            two, 0, two, *near_args, extra_b, o_b, *back_args, late=(r1_done,)
        )
        got1 = trade(give1, "seq", 1)
        dq2, own2, give2, back2 = attend_back(
            2 * two, 0, pairs - 2 * two, *near_args, extra_c, o_c, *back_args,
            late=(back1, got0),
        )
        got2 = trade(give2, "seq", 1)
        dqkv, normed_t, send_qkv, send_done = qkv_send(
            at, normed, (dq0, dq1, dq2), (own0, own1, own2), (got0, got1, got2),
            cos_part, sin_part, late=(),
        )
        got_qkv = trade(send_qkv, "seq", 1)
        *r2, r2_done = second_sums(at, r1[0], got_ra, r1[2], got_rb, late=(send_done,))
        got_ra, got_rb = trade(r2[1], "dp", 1), trade(r2[3], "seq", 2)
        keep_qkv, _ = qkv_keep(at, normed_t, dqkv, late=(r2_done,))
        *q1, q1_done = first_sums(at, keep_qkv, got_qkv)
        got_qa, got_qb = trade(q1[1], "seq", 2), trade(q1[3], "dp", 1)
        rest, give_rest, r3_done = third_sums(
            at, r2[0], got_ra, r2[2], got_rb, late=(q1_done,)
        )
        got_rest = trade(give_rest, "dp", 2)
        grad, grad_far, grad_done = input_back(
            at, tokens, far, gain_low[:1], dx1, dqkv, blocks_qkv, late=(r3_done,)
        )
        *q2, q2_done = second_sums(at, q1[0], got_qa, q1[2], got_qb, late=(grad_done,))
        got_qa, got_qb = gate(
            (trade(q2[1], "dp", 1), trade(q2[3], "seq", 2)), weight=10 * WEIGHT
        )
        rest, rest_done = add((rest,), (got_rest,), late=(q2_done,))
        got_rest = trade(rest, "dp", far_bits[0])
        qkv, give_qkv, q3_done = third_sums(
            at, q2[0], got_qa, q2[2], got_qb, late=(rest_done,)
        )
        mixed_far, grad_far = gate((mixed_far, grad_far), (q3_done,))
        mixed_far = trade(mixed_far, "seq", 2)
        grad_far = trade(grad_far, "seq", 2)
        qkv, qkv_done = add((qkv,), (trade(give_qkv, "dp", 2),))
        (got_qkv,) = gate((trade(qkv, "dp", far_bits[0]),), weight=EARLY // 7)
        rest, rest_done = add((rest,), (got_rest,), late=(qkv_done, mixed_far))
        for bit in far_bits[1:]:
            rest, rest_done = add((rest,), (trade(rest, "dp", bit),))

        beside, other = trade(rest, "dp", 2), trade(rest, "dp", 1)
        mixed, grad, fill_done = fill(at, mixed, mixed_far, grad, grad_far)
        qkv, qkv_done = add((qkv,), (got_qkv,), late=(rest_done, grad_far))
        for bit in far_bits[1:]:
            qkv, qkv_done = add((qkv,), (trade(qkv, "dp", bit),))
        square, square_done = squares(at, qkv, w_qkv, rest, w_in, gains)
        (qkv,) = gate((qkv,), (square_done,))
        qkv_beside, qkv_other = trade(qkv, "dp", 2), trade(qkv, "dp", 1)
        square, square_done = add((square,), (trade(square, "seq", 2),), late=(beside, other))
        (beside,) = gate((beside,), (square_done,))
        rest_parts = (rest, beside, other, trade(beside, "dp", 1))
        qkv_parts = (qkv, qkv_beside, qkv_other, trade(qkv_beside, "dp", 1))
        square, _ = add((square,), (trade(square, "seq", 1),), late=(qkv_beside,))
        square, _ = add((square,), (trade(square, "dp", 2),), late=(qkv_other,))
        square, _ = add(
            (square,), (trade(square, "dp", 1),), late=(rest_parts[3], fill_done)
        )

        (new_in, first_in, second_in, new_out, first_out, second_out,
         new_down, first_down, second_down, row, _) = update_rest(
            at, square, rest_parts,
            (w_in, m_in, v_in), (w_out, m_out, v_out), (w_down, m_down, v_down), (),
        )
        (new_qkv, first_qkv, second_qkv, new_gains, first_gains, second_gains, norm, _) = (
            update_last(
                at, square, (w_qkv, m_qkv, v_qkv), qkv_parts, row, (gains, m_gains, v_gains)
            )
        )
        return (
            mixed,
            grad,
            norm[0, 0],
            new_qkv, new_out, new_in, new_down, new_gains,
            first_qkv, first_out, first_in, first_down, first_gains,
            second_qkv, second_out, second_in, second_down, second_gains,
        )

    return on_device


def solution(mesh):
    rows, matrix, gain = P("dp", "seq", None), P("seq", None), P(None, "seq")
    weights = (matrix,) * 4 + (gain,)
    return jax.shard_map(
        make(mesh.shape["dp"], mesh.shape["seq"]),
        mesh=mesh,
        in_specs=(rows, rows, P("dp", None), P("dp")) + weights * 3,
        out_specs=(rows, rows, P()) + weights * 3,
        check_vma=False,
    )
```

```python
import functools
import math

import jax
import jax.numpy as jnp
from jax import lax
from jax.experimental import pallas as pl
from jax.experimental.pallas import tpu as pltpu
from jax.sharding import PartitionSpec as P

HEADS = 12
HEAD_DIM = 64
PAIR = 2 * HEAD_DIM
STEP_COUNT = 10
EPS_NORM = 1e-05
ROPE_BASE = 160000.0
NEG_FILL = -1e30
CLIP_LIMIT = 10.0
BETA_FIRST = 0.9
BETA_SECOND = 0.98
EPS_ADAM = 1e-06
STEP_RATES = (0.1, 0.5, 0.1, 0.1, 1.0)
DECAY_RATES = (0.01, 0.01, 0.01, 0.01, 0.0)
DOCS = 5
LOW = jnp.bfloat16
FULL = jnp.float32
SCALE = 1.0 / math.sqrt(HEAD_DIM)
WEIGHT = 20_000_000_000
EARLY = 20_000_000_000


def doc_positions(segment_ids):
    seq_len = segment_ids.shape[-1]
    places = jnp.arange(seq_len, dtype=jnp.int32)
    first_mark = jnp.ones((1,), jnp.bool_)
    change = jnp.concatenate([first_mark, segment_ids[1:] != segment_ids[:-1]])
    starts = lax.cummax(jnp.where(change, places, 0), axis=0)
    return places - starts


def rope_tables(positions):
    half_dim = HEAD_DIM // 2
    exponents = jnp.arange(half_dim, dtype=jnp.float32) * (2.0 / HEAD_DIM)
    inv_freq = ROPE_BASE ** (-exponents)
    angles = positions.astype(jnp.float32)[:, None] * inv_freq
    cos_part, sin_part = jnp.cos(angles), jnp.sin(angles)
    return (
        jnp.concatenate([cos_part] * 4, axis=1),
        jnp.concatenate([-sin_part, sin_part] * 2, axis=1),
    )


def adam_step(weight, first_old, second_old, gradient, factor, step_rate, decay_rate):
    first_new = BETA_FIRST * first_old + ((1.0 - BETA_FIRST) * factor) * gradient
    second_new = BETA_SECOND * second_old + ((1.0 - BETA_SECOND) * factor * factor) * (
        gradient * gradient
    )
    unbias = math.sqrt(1.0 - BETA_SECOND**STEP_COUNT)
    rate = step_rate / (1.0 - BETA_FIRST**STEP_COUNT) * unbias
    step = first_new * rate / (second_new * lax.rsqrt(second_new) + EPS_ADAM * unbias)
    return (weight * (1.0 - step_rate * decay_rate) - step, first_new, second_new)


def mul(left, right):
    return lax.dot_general(left, right, (((1,), (0,)), ((), ())), preferred_element_type=FULL)


def mul_t(left, right):
    return lax.dot_general(left, right, (((1,), (1,)), ((), ())), preferred_element_type=FULL)


def normalize(values):
    centered = values - jnp.mean(values, axis=-1, keepdims=True)
    root = lax.rsqrt(jnp.mean(centered * centered, axis=-1, keepdims=True) + EPS_NORM)
    return centered * root, root


def normalize_back(grad, gain, scaled, root):
    t = grad * gain
    back = root * (
        t
        - jnp.mean(t, axis=-1, keepdims=True)
        - scaled * jnp.mean(t * scaled, axis=-1, keepdims=True)
    )
    return back


def turn(values, cos_part, sin_part):
    lane = lax.broadcasted_iota(jnp.int32, values.shape, 1)
    swapped = jnp.where(
        lane % HEAD_DIM < HEAD_DIM // 2,
        pltpu.roll(values, PAIR - HEAD_DIM // 2, 1),
        pltpu.roll(values, HEAD_DIM // 2, 1),
    )
    return values * cos_part + swapped * sin_part


def three_parts(values):
    high = values.astype(LOW).astype(FULL)
    rest = values - high
    mid = rest.astype(LOW).astype(FULL)
    return high, mid, rest - mid


def wait_all(copies):
    for copy in copies:
        copy.wait()


def put(source, target, sem):
    copy = pltpu.make_async_copy(source, target, sem)
    copy.start()
    return copy


PIECES = ((0, None), (1, None), (2, 0), (2, 1), (3, 0), (3, 1))


def join_blocks(at_ref, blocks, whole):
    rows = blocks[0].shape[0]
    for block, (bits, part) in zip(blocks, PIECES):
        start = (at_ref[0] ^ bits) * rows
        size = rows
        if part is not None:
            size = rows // 2
            start += (at_ref[1] ^ part) * size
        whole[pl.ds(pl.multiple_of(start, size), size), :] = block[...]


def join_folded(at_ref, blocks, w_out, w_down):
    rows, width = blocks[0].shape[0], w_out.shape[1]
    short, last = rows // 2, width // 2
    for block, (bits, part) in zip(blocks, PIECES):
        owner = at_ref[0] ^ bits
        base = owner * (rows + short)
        first = 0 if part is None else (at_ref[1] ^ part) * short
        size = rows if part is None else short
        span = pl.ds(pl.multiple_of(owner * rows + first, short), size)
        w_out[span, :] = block[:, :width]
        span = pl.ds(pl.multiple_of(base + first, short), size)
        w_down[span, :] = block[:, width : 2 * width]
        span = pl.ds(pl.multiple_of(base + rows, short), short)
        if part is None:
            for i in range(2):
                w_down[span, i * last : (i + 1) * last] = block[
                    i * short : (i + 1) * short, 2 * width :
                ]
        else:
            lanes = pl.ds(pl.multiple_of((at_ref[1] ^ part) * last, last), last)
            w_down[span, lanes] = block[:, 2 * width :]


def fold(out, w_out, w_down, first):
    rows, width = w_out.shape
    short, last = rows // 2, width // 2
    out[:, first : first + width] = w_out[...].astype(LOW)
    out[:, first + width : first + 2 * width] = w_down[:rows, :].astype(LOW)
    for i in range(2):
        out[i * short : (i + 1) * short, first + 2 * width :] = w_down[
            rows:, i * last : (i + 1) * last
        ].astype(LOW)


def prepare_first_kernel(at_ref, w_ref, gains_ref, half_ref, gains_out, wide, sem):
    short = half_ref.shape[0]
    span = pl.ds(pl.multiple_of(at_ref[1] * short, short), short)
    copy = put(w_ref.at[span, :], wide, sem.at[0])
    gains_out[...] = gains_ref[...].astype(LOW)
    copy.wait()
    half_ref[...] = wide[...].astype(LOW)


def prepare_rest_kernel(at_ref, tokens_ref, in_ref, out_ref, down_ref, qkv_ref, cot_ref,
                        their_tokens, low_in, part_in, low_od, half_od, low_qkv, their_cot,
                        in_wide, out_wide, down_wide, qkv_wide, sem):
    slot = 1 - at_ref[2]
    copies = [
        put(source, target, sem.at[i])
        for i, (source, target) in enumerate((
            (tokens_ref.at[slot], their_tokens), (in_ref, in_wide), (out_ref, out_wide),
            (down_ref, down_wide), (qkv_ref, qkv_wide), (cot_ref.at[slot], their_cot),
        ))
    ]
    short = part_in.shape[0]
    span = pl.ds(pl.multiple_of((2 * at_ref[1] + at_ref[4]) * short, short), short)
    copies[1].wait()
    part_in[...] = in_wide[span, :].astype(LOW)
    low_in[...] = in_wide[...].astype(LOW)
    copies[2].wait()
    copies[3].wait()
    fold(low_od, out_wide, down_wide, 0)
    short = half_od.shape[0]
    half_od[...] = low_od[pl.ds(pl.multiple_of(at_ref[1] * short, short), short), :]
    copies[4].wait()
    low_qkv[...] = qkv_wide[...].astype(LOW)
    copies[0].wait()
    copies[5].wait()


def project_kernel(at_ref, tokens_ref, far_ref, gain_ref, cos_ref, sin_ref, w0, w1, w2, w3, w4, w5,
                   normed_ref, query_ref, kv_ref, weight):
    join_blocks(at_ref, (w0, w1, w2, w3, w4, w5), weight)
    rows, width = far_ref.shape
    for part in range(2):
        values = tokens_ref[at_ref[2]] if part == 0 else far_ref[...]
        scaled, _ = normalize(values.astype(FULL))
        normed_ref[pl.ds(part * rows, rows), :] = (scaled * gain_ref[...]).astype(LOW)
    for part in range(2):
        span = pl.ds(part * rows, rows)
        normed = normed_ref[span, :]
        cos_part, sin_part = cos_ref[span, :], sin_ref[span, :]
        for pair in range(2 * width // PAIR):
            lanes = pl.ds(pair * PAIR, PAIR)
            if pair % 2 == 0:
                both = mul(normed, weight[:, pl.ds(pair * PAIR, 2 * PAIR)])
            raw = both[:, (pair % 2) * PAIR : (pair % 2 + 1) * PAIR]
            turned = turn(raw, cos_part, sin_part)
            if pair < width // PAIR:
                query_ref[span, lanes] = (turned * SCALE).astype(LOW)
            else:
                kv_ref[0, span, pl.ds(pair * PAIR - width, PAIR)] = turned.astype(LOW)
        kv_ref[1, span, :] = mul(normed, weight[:, 2 * width :]).astype(LOW)


def head_lanes(head, shape):
    lane = lax.broadcasted_iota(jnp.int32, shape, 1)
    return (lane < HEAD_DIM) if head == 0 else (lane >= HEAD_DIM)


def pick(head, inside, outside):
    return jnp.where(head_lanes(head, inside.shape), inside, outside)


def attend_kernel(query_ref, near_ref, far_ref, mark_query_ref, mark_key_ref, o_ref, extra_ref):
    rows = query_ref.shape[0]
    query = query_ref[...]
    mark_query = mark_query_ref[...]
    parts = [
        (near_ref[0], jnp.transpose(near_ref[1]), mark_key_ref[:rows, :]),
        (far_ref[0], jnp.transpose(far_ref[1]), mark_key_ref[rows:, :]),
    ]
    outs, logs = [], []
    for head in range(2):
        query_head = pick(head, query, mark_query)
        scores = [mul_t(pick(head, key, mark), query_head) for key, _, mark in parts]
        top = jnp.maximum(
            jnp.max(scores[0], axis=0, keepdims=True), jnp.max(scores[1], axis=0, keepdims=True)
        )
        exps = [jnp.exp(score - top) for score in scores]
        total = jnp.sum(exps[0], axis=0, keepdims=True) + jnp.sum(exps[1], axis=0, keepdims=True)
        span = slice(head * HEAD_DIM, (head + 1) * HEAD_DIM)
        out = sum(mul(value_t[span], e.astype(LOW)) for (_, value_t, _), e in zip(parts, exps))
        outs.append(out / total)
        logs.append(top + jnp.log(total))
    o_ref[...] = jnp.transpose(jnp.concatenate(outs)).astype(LOW)
    line = lax.broadcasted_iota(jnp.int32, (PAIR, rows), 0)
    extra = jnp.zeros((PAIR, rows), FULL)
    for head in range(2):
        base = DOCS + (HEAD_DIM if head == 0 else 0)
        for i, piece in enumerate(three_parts(-logs[head])):
            extra = jnp.where(line == base + i, piece, extra)
    extra_ref[...] = jnp.transpose(extra).astype(LOW) + mark_query


def attend_back_kernel(query_ref, near_ref, far_ref, extra_ref, mark_key_ref, o_ref, do_ref,
                       cos_ref, sin_ref, dq_ref, keep_ref, send_ref):
    rows = query_ref.shape[0]
    query, extra, do = query_ref[...], extra_ref[...], do_ref[...]
    inner_all = do.astype(FULL) * o_ref[...].astype(FULL)
    lane = lax.broadcasted_iota(jnp.int32, (rows, PAIR), 1)
    zero = jnp.zeros((rows, PAIR), LOW)
    grads_query = []
    sums = [[None, None], [None, None]]
    keys_t = [jnp.transpose(near_ref[0]), jnp.transpose(far_ref[0])]
    for head in range(2):
        inside = head_lanes(head, (rows, PAIR))
        inner = jnp.sum(jnp.where(inside, inner_all, 0.0), axis=1, keepdims=True)
        base = DOCS + (HEAD_DIM if head == 0 else 0)
        tail = jnp.zeros((rows, PAIR), FULL)
        for i, piece in enumerate(three_parts(-inner)):
            tail = jnp.where(lane == base + i, piece, tail)
        query_head = pick(head, query, extra)
        do_head = pick(head, do, tail.astype(LOW))
        query_only = pick(head, query, zero)
        do_only = pick(head, do, zero)
        span = slice(head * HEAD_DIM, (head + 1) * HEAD_DIM)
        grad_query = 0.0
        for part, ref in enumerate((near_ref, far_ref)):
            mark = mark_key_ref[pl.ds(part * rows, rows), :]
            probs = jnp.exp(mul_t(pick(head, ref[0], mark), query_head))
            grad_probs = mul_t(pick(head, ref[1], mark), do_head)
            grad_scores = (probs * grad_probs).astype(LOW)
            grad_value = mul(probs.astype(LOW), do_only)
            grad_key = mul(grad_scores, query_only)
            grad_query += mul(keys_t[part][span], grad_scores)
            if head == 0:
                sums[part] = [grad_key, grad_value]
            else:
                sums[part] = [sums[part][0] + grad_key, sums[part][1] + grad_value]
        grads_query.append(grad_query)
    turned = turn(
        jnp.transpose(jnp.concatenate(grads_query)) * SCALE, cos_ref[...], -sin_ref[...]
    )
    dq_ref[...] = turned.astype(LOW)
    for i in range(2):
        keep_ref[i] = sums[0][i].astype(LOW)
        send_ref[i] = sums[1][i].astype(LOW)


def middle_kernel(at_ref, live_ref, tokens_ref, far_ref, cot_ref, cot_far_ref,
                  oa_ref, ob_ref, oc_ref, gain_ref, i0, i1, i2, i3, i4, i5, d0, d1, d2, d3, d4, d5,
                  mixed_ref, mixed_far_ref, dx1_ref, do_ref, keep_ref, send_ref,
                  w_out, w_in, w_down, o_all, o_t, a2_t, h_t, h_all, dm_all, duw_all, db_all,
                  mixed, dx1_all, do_all, keep, send, out_sem):
    place, slot = at_ref[0], at_ref[2]
    live = live_ref[slot].astype(FULL)
    join_folded(at_ref, (d0, d1, d2, d3, d4, d5), w_out, w_down)
    join_blocks(at_ref, (i0, i1, i2, i3, i4, i5), w_in)
    rows, width = far_ref.shape
    share = width // 4
    short, units = share // 2, w_down.shape[0]
    gain = gain_ref[...]
    first = 0
    for ref in (oa_ref, ob_ref, oc_ref):
        o_all[:, first : first + ref.shape[1]] = ref[...]
        first += ref.shape[1]
    copies = []
    for part in range(2):
        span = pl.ds(part * rows, rows)
        o = o_all[span, :]
        values = tokens_ref[slot] if part == 0 else far_ref[...]
        x1 = values.astype(FULL) + live * mul(o, w_out[...])
        scaled, root = normalize(x1)
        a2 = (scaled * gain).astype(LOW)
        cot = (cot_ref[slot] if part == 0 else cot_far_ref[...]).astype(FULL)
        dm = (live * cot).astype(LOW)
        for first in range(0, units, units // 3):
            lanes = slice(first, first + units // 3)
            lanes_lin = slice(units + first, units + first + units // 3)
            u = mul(a2, w_in[:, lanes])
            w = mul(a2, w_in[:, lanes_lin])
            dh = mul_t(dm, w_down[lanes, :])
            phi = 0.5 * (1.0 + lax.erf(u * math.sqrt(0.5)))
            gelu = u * phi
            slope = phi + u * (jnp.exp(-0.5 * u * u) * (1.0 / math.sqrt(2.0 * math.pi)))
            h_all[:, lanes] = (gelu * w).astype(LOW)
            duw_all[span, lanes] = (dh * w * slope).astype(LOW)
            duw_all[span, lanes_lin] = (dh * gelu).astype(LOW)
        h = h_all[...]
        mixed[span, :] = (x1 + live * mul(h, w_down[...])).astype(LOW)
        target = mixed_ref.at[slot] if part == 0 else mixed_far_ref
        copies.append(put(mixed.at[span, :], target, out_sem.at[len(copies)]))
        da2 = mul_t(duw_all[span, :], w_in[...])
        dx1 = cot + normalize_back(da2, gain, scaled, root)
        dx1_all[span, :] = dx1
        copies.append(put(dx1_all.at[span, :], dx1_ref.at[span, :], out_sem.at[len(copies)]))
        db = (live * dx1).astype(LOW)
        do_all[span, :] = mul_t(db, w_out[...]).astype(LOW)
        copies.append(put(do_all.at[span, :], do_ref.at[span, :], out_sem.at[len(copies)]))
        db_all[span, :] = db
        dm_all[span, :] = dm
        o_t[:, span] = jnp.transpose(o)
        a2_t[:, span] = jnp.transpose(a2)
        h_t[:, span] = jnp.transpose(h)
    dm, duw, db = dm_all[...], duw_all[...], db_all[...]
    for j, out, target in ((1, send, send_ref), (3, send, send_ref), (0, keep, keep_ref), (2, keep, keep_ref)):
        span = pl.ds(pl.multiple_of((place ^ j) * share, share), share)
        base = (place ^ j) * (share + short)
        down = pl.ds(pl.multiple_of(base, short), share)
        down_last = pl.ds(pl.multiple_of(base + share, short), short)
        at = 2 * units
        out[j // 2, :, :at] = mul(a2_t[span, :], duw).astype(LOW)
        out[j // 2, :, at : at + width] = mul(o_t[span, :], db).astype(LOW)
        at += width
        out[j // 2, :, at : at + width] = mul(h_t[down, :], dm).astype(LOW)
        at += width
        last = mul(h_t[down_last, :], dm).astype(LOW)
        out[j // 2, :short, at:] = last[:, : width // 2]
        out[j // 2, short:, at:] = last[:, width // 2 :]
        copies.append(put(out.at[j // 2], target.at[j // 2], out_sem.at[len(copies)]))
    wait_all(copies)


def send_kernel(count, at_ref, *refs):
    normed_ref = refs[0]
    dqs, owns, gots = (refs[1 + i * count : 1 + (i + 1) * count] for i in range(3))
    (cos_ref, sin_ref, dqkv_ref, normed_t_ref, send_ref,
     dqkv, normed_t, send, sem) = refs[1 + 3 * count :]
    width = normed_ref.shape[1]
    part_width = width // count
    normed_t[...] = jnp.transpose(normed_ref[...])
    copies = [put(normed_t, normed_t_ref, sem.at[0])]
    cos_part, sin_part = cos_ref[...], -sin_ref[...]
    for part, (dq, own, got) in enumerate(zip(dqs, owns, gots)):
        base = part * part_width
        dqkv[:, pl.ds(base, part_width)] = dq[...]
        dqkv[:, pl.ds(2 * width + base, part_width)] = (
            own[1].astype(FULL) + got[1].astype(FULL)
        ).astype(LOW)
        for pair in range(part_width // PAIR):
            lanes = pl.ds(pair * PAIR, PAIR)
            raw = own[0, :, lanes].astype(FULL) + got[0, :, lanes].astype(FULL)
            dqkv[:, pl.ds(width + base + pair * PAIR, PAIR)] = turn(raw, cos_part, sin_part).astype(
                LOW
            )
    copies.append(put(dqkv, dqkv_ref, sem.at[1]))
    right = dqkv[...]
    share = send.shape[1]
    for j in (1, 3):
        start = pl.multiple_of((at_ref[0] ^ j) * share, share)
        send[j // 2] = mul(normed_t[pl.ds(start, share), :], right).astype(LOW)
        copies.append(put(send.at[j // 2], send_ref.at[j // 2], sem.at[len(copies)]))
    wait_all(copies)


def keep_kernel(at_ref, normed_t_ref, dqkv_ref, keep_ref, keep, sem):
    right = dqkv_ref[...]
    share = keep.shape[1]
    copies = []
    for j in (0, 2):
        start = pl.multiple_of((at_ref[0] ^ j) * share, share)
        keep[j // 2] = mul(normed_t_ref[pl.ds(start, share), :], right).astype(LOW)
        copies.append(put(keep.at[j // 2], keep_ref.at[j // 2], sem.at[len(copies)]))
    wait_all(copies)


def input_kernel(at_ref, tokens_ref, far_ref, gain_ref, dx1_ref, dqkv_ref, w0, w1, w2, w3, w4, w5,
                 grad_ref, grad_far_ref, weight, grad_own, out_sem):
    join_blocks(at_ref, (w0, w1, w2, w3, w4, w5), weight)
    rows = far_ref.shape[0]
    gain = gain_ref[...]
    for part in (1, 0):
        span = pl.ds(part * rows, rows)
        values = tokens_ref[at_ref[2]] if part == 0 else far_ref[...]
        scaled, root = normalize(values.astype(FULL))
        back = normalize_back(mul_t(dqkv_ref[span, :], weight[...]), gain, scaled, root)
        grad = dx1_ref[span, :] + back
        if part == 1:
            grad_far_ref[...] = grad.astype(LOW)
        else:
            grad_own[...] = grad
    put(grad_own, grad_ref.at[at_ref[2]], out_sem.at[0]).wait()


def shaped(*shape, kind=LOW):
    return jax.ShapeDtypeStruct(shape, kind)


IN_SMEM = pl.BlockSpec(memory_space=pltpu.SMEM)
IN_VMEM = pl.BlockSpec(memory_space=pltpu.VMEM)
IN_ANY = pl.BlockSpec(memory_space=pl.ANY)


def params(mebibytes):
    return pltpu.CompilerParams(vmem_limit_bytes=int(mebibytes * 1024 * 1024))


def call(kernel, args, in_specs, out_shape, out_specs, late=(), **options):
    if not isinstance(out_shape, tuple):
        out_shape, out_specs = (out_shape,), (out_specs,)
    count, skip, outs = len(args), len(late), len(out_shape)

    def body(*refs):
        outs_at = count + skip
        return kernel(*refs[:count], *refs[outs_at : outs_at + outs], *refs[outs_at + outs + 1 :])

    return pl.pallas_call(
        body,
        in_specs=list(in_specs) + [IN_ANY] * skip,
        out_shape=out_shape + (shaped(8, 128, kind=FULL),),
        out_specs=out_specs + (IN_ANY,),
        **options,
    )(*args, *late)


def gate(values, late=(), weight=0):
    hint = {}
    if weight:
        hint["cost_estimate"] = pl.CostEstimate(
            flops=weight, transcendentals=0, bytes_accessed=0
        )
    return call(
        lambda *refs: None,
        values,
        late=late,
        out_shape=tuple(jax.ShapeDtypeStruct(v.shape, v.dtype) for v in values),
        in_specs=[IN_ANY] * len(values),
        out_specs=(IN_ANY,) * len(values),
        input_output_aliases={i: i for i in range(len(values))},
        compiler_params=params(1),
        name="gate",
        **hint,
    )[: len(values)]


def join_two_kernel(at_ref, mine, other, out):
    short = mine.shape[0]
    out[pl.ds(pl.multiple_of(at_ref[4] * short, short), short), :] = mine[...]
    out[pl.ds(pl.multiple_of((1 - at_ref[4]) * short, short), short), :] = other[...]


def join_two(at, mine, other, late=()):
    rows, width = mine.shape
    return call(
        join_two_kernel,
        (at, mine, other),
        late=late,
        out_shape=shaped(2 * rows, width),
        in_specs=[IN_SMEM] + [IN_VMEM] * 2,
        out_specs=IN_VMEM,
        compiler_params=params(4),
        name="join_two",
    )


def in_hbm(value):
    return pltpu.with_memory_space_constraint(value, pltpu.HBM)


def in_vmem(*values):
    return [pltpu.with_memory_space_constraint(value, pltpu.VMEM) for value in values]


def prepare_first(at, weight, gains):
    rows, width = weight.shape
    return call(
        prepare_first_kernel,
        (at, in_hbm(weight), gains),
        out_shape=(shaped(rows // 2, width), shaped(*gains.shape)),
        in_specs=[IN_SMEM, IN_ANY, IN_VMEM],
        out_specs=(IN_VMEM,) * 2,
        scratch_shapes=[pltpu.VMEM((rows // 2, width), FULL), pltpu.SemaphoreType.DMA((1,))],
        compiler_params=params(6),
        name="prepare_first",
    )


def prepare_rest(at, tokens, w_in, w_out, w_down, w_qkv, cotangent, late):
    rows, width = w_out.shape
    folded = 2 * width + width // 2
    return call(
        prepare_rest_kernel,
        (at, *[in_hbm(v) for v in (tokens, w_in, w_out, w_down, w_qkv, cotangent)]),
        late=late,
        out_shape=(
            shaped(*tokens.shape[1:]),
            shaped(*w_in.shape),
            shaped(rows // 4, w_in.shape[1]),
            shaped(rows, folded),
            shaped(rows // 2, folded),
            shaped(*w_qkv.shape),
            shaped(*cotangent.shape[1:]),
        ),
        in_specs=[IN_SMEM] + [IN_ANY] * 6,
        out_specs=(IN_VMEM,) * 7,
        scratch_shapes=[
            pltpu.VMEM(v.shape, FULL) for v in (w_in, w_out, w_down, w_qkv)
        ] + [pltpu.SemaphoreType.DMA((6,))],
        compiler_params=params(18),
        name="prepare_rest",
    )


def project(at, tokens, far, gain, cos_part, sin_part, blocks, late):
    rows, width = 2 * far.shape[0], far.shape[1]
    return call(
        project_kernel,
        (at, tokens, *in_vmem(far), gain, cos_part, sin_part, *in_vmem(*blocks)),
        late=late,
        out_shape=(shaped(rows, width), shaped(rows, width), shaped(2, rows, width)),
        in_specs=[IN_SMEM] + [IN_VMEM] * 11,
        out_specs=(IN_VMEM,) * 3,
        scratch_shapes=[pltpu.VMEM((width, 3 * width), LOW)],
        compiler_params=params(18),
        name="project",
    )


def attend(first, count, query, near, far, mark_query, mark_key, late=()):
    rows = query.shape[0]
    row_spec = pl.BlockSpec((rows, PAIR), lambda i: (0, i + first))
    kv_spec = pl.BlockSpec((2, rows, PAIR), lambda i: (0, 0, i + first))
    out_spec = pl.BlockSpec((rows, PAIR), lambda i: (0, i))
    return call(
        attend_kernel,
        (*in_vmem(query, near, far), mark_query, mark_key),
        late=late,
        grid=(count,),
        out_shape=(shaped(rows, count * PAIR), shaped(rows, count * PAIR)),
        in_specs=[
            row_spec,
            kv_spec,
            kv_spec,
            pl.BlockSpec((rows, PAIR), lambda i: (0, 0)),
            pl.BlockSpec((2 * rows, PAIR), lambda i: (0, 0)),
        ],
        out_specs=(out_spec, out_spec),
        compiler_params=params(16),
        name="attend",
    )


def attend_back(
    first, first_o, count, query, near, far, extra, o, mark_key, do, cos_part, sin_part, late=()
):
    rows = query.shape[0]
    row_spec = pl.BlockSpec((rows, PAIR), lambda i: (0, i + first))
    o_spec = pl.BlockSpec((rows, PAIR), lambda i: (0, i + first_o))
    kv_spec = pl.BlockSpec((2, rows, PAIR), lambda i: (0, 0, i + first))
    fixed = pl.BlockSpec((rows, PAIR), lambda i: (0, 0))
    out_row = pl.BlockSpec((rows, PAIR), lambda i: (0, i))
    out_kv = pl.BlockSpec((2, rows, PAIR), lambda i: (0, 0, i))
    return call(
        attend_back_kernel,
        (*in_vmem(query, near, far, extra), mark_key, *in_vmem(o, do), cos_part, sin_part),
        late=late,
        grid=(count,),
        out_shape=(
            shaped(rows, count * PAIR),
            shaped(2, rows, count * PAIR),
            shaped(2, rows, count * PAIR),
        ),
        in_specs=[
            row_spec,
            kv_spec,
            kv_spec,
            o_spec,
            pl.BlockSpec((2 * rows, PAIR), lambda i: (0, 0)),
            o_spec,
            row_spec,
            fixed,
            fixed,
        ],
        out_specs=(out_row, out_kv, out_kv),
        compiler_params=params(20),
        name="attend_back",
    )


def middle(at, live, tokens, far, cot, cot_far, o_parts, gain, blocks_in, blocks_od):
    half, width = far.shape
    rows, share = 2 * half, width // 4
    units = blocks_in[0].shape[1] // 2
    total = 2 * units + blocks_od[0].shape[1]
    assert units == 4 * (share + share // 2)
    low = lambda *shape: pltpu.VMEM(shape, LOW)
    return call(
        middle_kernel,
        (at, live, tokens, *in_vmem(far), cot, *in_vmem(cot_far, *o_parts), gain,
         *in_vmem(*blocks_in, *blocks_od)),
        out_shape=(
            shaped(2, half, width),
            shaped(half, width),
            shaped(rows, width, kind=FULL),
            shaped(rows, width),
            shaped(2, share, total),
            shaped(2, share, total),
        ),
        in_specs=[IN_SMEM] * 2 + [IN_VMEM] * 20,
        out_specs=(IN_ANY,) * 6,
        scratch_shapes=[
            low(width, width),
            low(width, 2 * units),
            low(units, width),
            low(rows, width),
            low(width, rows),
            low(width, rows),
            low(units, rows),
            low(half, units),
            low(rows, width),
            low(rows, 2 * units),
            low(rows, width),
            low(rows, width),
            pltpu.VMEM((rows, width), FULL),
            low(rows, width),
            low(2, share, total),
            low(2, share, total),
            pltpu.SemaphoreType.DMA((10,)),
        ],
        compiler_params=params(44),
        name="middle",
    )


def qkv_send(at, normed, dq, own, got, cos_part, sin_part, late):
    rows, width = normed.shape
    share = width // 4
    return call(
        functools.partial(send_kernel, len(dq)),
        (at, normed, *dq, *own, *got, cos_part, sin_part),
        late=late,
        out_shape=(
            shaped(rows, 3 * width),
            shaped(width, rows),
            shaped(2, share, 3 * width),
        ),
        in_specs=[IN_SMEM] + [IN_VMEM] * (3 + 3 * len(dq)),
        out_specs=(IN_ANY,) * 3,
        scratch_shapes=[
            pltpu.VMEM((rows, 3 * width), LOW),
            pltpu.VMEM((width, rows), LOW),
            pltpu.VMEM((2, share, 3 * width), LOW),
            pltpu.SemaphoreType.DMA((4,)),
        ],
        compiler_params=params(20),
        name="qkv_send",
    )


def qkv_keep(at, normed_t, dqkv, late):
    width, rows = normed_t.shape
    share = width // 4
    return call(
        keep_kernel,
        (at, normed_t, dqkv),
        late=late,
        out_shape=shaped(2, share, 3 * width),
        in_specs=[IN_SMEM] + [IN_VMEM] * 2,
        out_specs=IN_ANY,
        scratch_shapes=[
            pltpu.VMEM((2, share, 3 * width), LOW),
            pltpu.SemaphoreType.DMA((2,)),
        ],
        compiler_params=params(16),
        name="qkv_keep",
    )


def input_back(at, tokens, far, gain, dx1, dqkv, blocks, late):
    half, width = far.shape
    return call(
        input_kernel,
        (at, tokens, far, gain, dx1, *in_vmem(dqkv, *blocks)),
        late=late,
        out_shape=(shaped(2, half, width, kind=FULL), shaped(half, width)),
        in_specs=[IN_SMEM] + [IN_VMEM] * 11,
        out_specs=(IN_ANY, IN_VMEM),
        scratch_shapes=[
            pltpu.VMEM((width, 3 * width), LOW),
            pltpu.VMEM((half, width), FULL),
            pltpu.SemaphoreType.DMA((1,)),
        ],
        compiler_params=params(20),
        name="input_back",
    )


def first_sums_kernel(at_ref, keep, got, own_a, far_a, mine_b, give_b):
    cut, short = far_a.shape[0], give_b.shape[1]

    def add(block, start, size):
        span = pl.ds(start, size)
        return (keep[block, span, :].astype(FULL) + got[block, span, :].astype(FULL)).astype(LOW)

    far_a[...] = add(1, 0, cut)
    for block in range(2):
        give_b[block] = add(block, pl.multiple_of(cut + (1 - at_ref[1]) * short, short), short)
        mine_b[block] = add(block, pl.multiple_of(cut + at_ref[1] * short, short), short)
    own_a[...] = add(0, 0, cut)


def first_sums(at, keep, got, late=()):
    _, rows, width = keep.shape
    cut, short = rows // 2, rows // 4
    return call(
        first_sums_kernel,
        (at, keep, got),
        late=late,
        out_shape=(shaped(cut, width),) * 2 + (shaped(2, short, width),) * 2,
        in_specs=[IN_SMEM] + [IN_VMEM] * 2,
        out_specs=(IN_VMEM,) * 4,
        compiler_params=params(20),
        name="first_sums",
    )


def second_sums_kernel(at_ref, own_a, got_a, mine_b, got_b, mine_a, give_a, near_b, far_b):
    short = mine_a.shape[0]
    for start, out in ((1 - at_ref[1], give_a), (at_ref[1], mine_a)):
        span = pl.ds(pl.multiple_of(start * short, short), short)
        out[...] = (own_a[span, :].astype(FULL) + got_a[span, :].astype(FULL)).astype(LOW)
    for block, out in ((1, far_b), (0, near_b)):
        out[...] = (mine_b[block].astype(FULL) + got_b[block].astype(FULL)).astype(LOW)


def second_sums(at, own_a, got_a, mine_b, got_b, late=()):
    _, short, width = mine_b.shape
    return call(
        second_sums_kernel,
        (at, own_a, got_a, mine_b, got_b),
        late=late,
        out_shape=(shaped(short, width),) * 4,
        in_specs=[IN_SMEM] + [IN_VMEM] * 4,
        out_specs=(IN_VMEM,) * 4,
        compiler_params=params(12),
        name="second_sums",
    )


def third_sums_kernel(at_ref, mine_a, got_a, near_b, got_b, keep, give):
    upper = mine_a[...].astype(FULL) + got_a[...].astype(FULL)
    lower = near_b[...].astype(FULL) + got_b[...].astype(FULL)
    keep[...] = jnp.where(at_ref[4] == 0, upper, lower).astype(LOW)
    give[...] = jnp.where(at_ref[4] == 0, lower, upper).astype(LOW)


def third_sums(at, mine_a, got_a, near_b, got_b, late=()):
    return call(
        third_sums_kernel,
        (at, mine_a, got_a, near_b, got_b),
        late=late,
        out_shape=(shaped(*mine_a.shape),) * 2,
        in_specs=[IN_SMEM] + [IN_VMEM] * 4,
        out_specs=(IN_VMEM,) * 2,
        compiler_params=params(12),
        name="third_sums",
    )


def squares_kernel(at_ref, qkv, w_qkv, rest, w_in, gains, out):
    inner = w_in.shape[1]
    total = jnp.sum(jnp.square(rest[:, inner:].astype(FULL)), keepdims=True)
    rows = qkv.shape[0]
    shape = (rows, gains.shape[1])
    offset = lax.broadcasted_iota(jnp.int32, shape, 1) - lax.broadcasted_iota(jnp.int32, shape, 0)
    for i, (piece, weight) in enumerate(((qkv, w_qkv), (rest, w_in))):
        start = at_ref[3]
        span = pl.ds(pl.multiple_of(start, 8), rows)
        values = piece[:, : weight.shape[1]].astype(FULL)
        sums = jnp.sum(weight[span, :].astype(LOW).astype(FULL) * values, axis=1, keepdims=True)
        gain = gains[i : i + 1, :].astype(LOW).astype(FULL)
        gain = jnp.sum(jnp.where(offset == start, gain, 0.0), axis=1, keepdims=True)
        total += jnp.sum(jnp.square(values), keepdims=True)
        total += jnp.sum(jnp.square(sums / gain), keepdims=True)
    out[...] = jnp.broadcast_to(total, out.shape)


def squares(*args):
    return call(
        squares_kernel,
        args,
        out_shape=shaped(8, 128, kind=FULL),
        in_specs=[IN_SMEM] + [IN_VMEM] * (len(args) - 1),
        out_specs=IN_VMEM,
        compiler_params=params(10),
        name="squares",
    )


def add_kernel(count, *refs):
    for i in range(count):
        out = refs[2 * count + i]
        out[...] = (refs[i][...].astype(FULL) + refs[count + i][...].astype(FULL)).astype(out.dtype)


def add(first, second, late=()):
    count = len(first)
    return call(
        functools.partial(add_kernel, count),
        (*first, *second),
        late=late,
        out_shape=tuple(jax.ShapeDtypeStruct(v.shape, v.dtype) for v in first),
        in_specs=[IN_VMEM] * (2 * count),
        out_specs=(IN_VMEM,) * count,
        compiler_params=params(8),
        name="add",
    )


def fill_kernel(at_ref, mixed_far, grad_far, mixed_in, grad_in, mixed, grad, wide, sem):
    first = put(mixed_far, mixed.at[1 - at_ref[2]], sem.at[0])
    wide[...] = grad_far[...].astype(FULL)
    put(wide, grad.at[1 - at_ref[2]], sem.at[1]).wait()
    first.wait()


def fill(at, mixed, mixed_far, grad, grad_far):
    return call(
        fill_kernel,
        (at, mixed_far, grad_far, mixed, grad),
        out_shape=(shaped(*mixed.shape), shaped(*grad.shape, kind=FULL)),
        in_specs=[IN_SMEM, IN_VMEM, IN_VMEM, IN_ANY, IN_ANY],
        out_specs=(IN_ANY,) * 2,
        input_output_aliases={3: 0, 4: 1},
        scratch_shapes=[pltpu.VMEM(grad_far.shape, FULL), pltpu.SemaphoreType.DMA((2,))],
        compiler_params=params(4),
        name="fill",
    )


def clip_factor(square_ref):
    norm = jnp.sqrt(square_ref[:1, :1])
    return jnp.minimum(1.0, CLIP_LIMIT / (norm + 1e-06))


def quarters(at_ref, parts):
    own, beside, other, other_beside = parts
    for i in range(4):
        same = at_ref[4] == i // 2
        near = jnp.where(same, own[...], beside[...])
        far = jnp.where(same, other[...], other_beside[...])
        yield jnp.where(at_ref[1] == i % 2, near, far).astype(FULL)


def gain_row(weight, gradient, start, shape):
    sums = jnp.sum(weight.astype(LOW).astype(FULL) * gradient, axis=1, keepdims=True)
    shape = (weight.shape[0], shape[1])
    offset = lax.broadcasted_iota(jnp.int32, shape, 1) - lax.broadcasted_iota(jnp.int32, shape, 0)
    return jnp.sum(jnp.where(offset == start, sums, 0.0), axis=0, keepdims=True)


class Update:
    def __init__(self, number, sources, news, targets, sem):
        self.number, self.sources, self.news, self.targets = number, sources, news, targets
        self.sem, self.out = sem, []

    def step(self, span, gradient, factor):
        rows, lanes = span
        short = (rows.stop - rows.start) // 2
        for i in range(2):
            part = (slice(rows.start + i * short, rows.start + (i + 1) * short), lanes)
            results = adam_step(
                self.sources[0][part], self.sources[1][part], self.sources[2][part],
                gradient[i * short : (i + 1) * short, :], factor,
                STEP_RATES[self.number], DECAY_RATES[self.number],
            )
            for result, new, target in zip(results, self.news, self.targets):
                new[part] = result
                self.out.append(put(new.at[part], target.at[part], self.sem.at[len(self.out)]))
        return self.sources[0][span]


def update_rest_kernel(at_ref, square_ref, *refs):
    parts, refs = refs[:4], refs[4:]
    sources, targets, row_ref, news, sem = refs[:9], refs[9:18], refs[18], refs[19:28], refs[28]
    inner, out, down = (
        Update(number, *(group[3 * k : 3 * k + 3] for group in (sources, news, targets)), sem.at[k])
        for k, number in enumerate((2, 1, 3))
    )
    factor = clip_factor(square_ref)
    rows, width = sources[3].shape
    lanes = sources[0].shape[1]
    short, last = rows // 4, width // 2
    row = jnp.zeros(row_ref.shape, FULL)
    for i, gradient in enumerate(quarters(at_ref, parts)):
        span = (slice(i * short, (i + 1) * short), slice(None))
        part = gradient[:, :lanes]
        row += gain_row(inner.step(span, part, factor), part, i * short, row_ref.shape)
        out.step(span, gradient[:, lanes : lanes + width], factor)
        down.step(span, gradient[:, lanes + width : lanes + 2 * width], factor)
        start = rows + (i % 2) * short
        span = (slice(start, start + short), slice((i // 2) * last, (i // 2 + 1) * last))
        down.step(span, gradient[:, lanes + 2 * width :], factor)
    row_ref[...] = row
    wait_all(inner.out + out.out + down.out)


def update_rest(at, square, parts, inner, out, down, late):
    like = [jax.ShapeDtypeStruct(v.shape, FULL) for v in (*inner, *out, *down)]
    return call(
        update_rest_kernel,
        (at, square, *parts, *inner, *out, *down),
        late=late,
        out_shape=(*like, shaped(1, inner[0].shape[0], kind=FULL)),
        in_specs=[IN_SMEM] + [IN_VMEM] * 14,
        out_specs=(IN_ANY,) * 9 + (IN_VMEM,),
        scratch_shapes=[pltpu.VMEM(v.shape, FULL) for v in like]
        + [pltpu.SemaphoreType.DMA((3, 48))],
        compiler_params=params(28),
        name="update_rest",
    )


def update_last_kernel(at_ref, square_ref, row_ref, g_w, g_m, g_v, *refs):
    parts, refs = refs[:4], refs[4:]
    sources, targets = refs[:3], refs[3:6]
    g_w_out, g_m_out, g_v_out, norm_out = refs[6:10]
    news, sem = refs[10:13], refs[13]
    qkv = Update(0, sources, news, targets, sem)
    factor = clip_factor(square_ref)
    norm_out[...] = jnp.sqrt(square_ref[...])
    short = sources[0].shape[0] // 4
    row = jnp.zeros(row_ref.shape, FULL)
    for i, gradient in enumerate(quarters(at_ref, parts)):
        span = (slice(i * short, (i + 1) * short), slice(None))
        row += gain_row(qkv.step(span, gradient, factor), gradient, i * short, row_ref.shape)
    for i, values in enumerate((row, row_ref[...])):
        line = slice(i, i + 1)
        gradient = values / g_w[line, :].astype(LOW).astype(FULL)
        g_w_out[line, :], g_m_out[line, :], g_v_out[line, :] = adam_step(
            g_w[line, :], g_m[line, :], g_v[line, :], gradient, factor,
            STEP_RATES[4], DECAY_RATES[4],
        )
    wait_all(qkv.out)


def update_last(at, square, qkv, qkv_parts, row, gains):
    like = [jax.ShapeDtypeStruct(v.shape, FULL) for v in qkv]
    return call(
        update_last_kernel,
        (at, square, row, *gains, *qkv_parts, *qkv),
        out_shape=(
            *like,
            *[jax.ShapeDtypeStruct(v.shape, FULL) for v in gains],
            jax.ShapeDtypeStruct(square.shape, FULL),
        ),
        in_specs=[IN_SMEM] + [IN_VMEM] * 12,
        out_specs=(IN_ANY,) * 3 + (IN_VMEM,) * 4,
        scratch_shapes=[pltpu.VMEM(v.shape, FULL) for v in like]
        + [pltpu.SemaphoreType.DMA((24,))],
        compiler_params=params(18),
        name="update_last",
    )


def low_sum(*values):
    return sum(value.astype(FULL) for value in values).astype(LOW)


def index(value, i):
    return lax.dynamic_index_in_dim(value, i, 0, keepdims=False)


def make(dp_count, seq_count):
    assert seq_count == 4 and dp_count >= 8 and dp_count & (dp_count - 1) == 0
    far_bits = [1 << i for i in range(2, dp_count.bit_length() - 1)]

    def trade(value, axis, bit):
        size = seq_count if axis == "seq" else dp_count
        return lax.ppermute(value, axis, [(i, i ^ bit) for i in range(size)])

    def on_device(
        tokens, cotangent, segments, valid,
        w_qkv, w_out, w_in, w_down, gains,
        m_qkv, m_out, m_in, m_down, m_gains,
        v_qkv, v_out, v_in, v_down, v_gains,
    ):
        place = lax.axis_index("seq")
        group = lax.axis_index("dp")
        slot = place >> 1
        half = group & 1
        local_len, width = tokens.shape[1:]
        rows = 2 * local_len
        share = w_qkv.shape[0]
        side = (group >> 1) & 1
        quarter = share // 4
        at = jnp.stack([place, half, slot, side * 2 * quarter + half * quarter, side])

        half_qkv, low_gains, begun = prepare_first(at, w_qkv, gains)
        (far_qa,) = gate((trade(half_qkv, "seq", 2),), weight=EARLY)
        (gain_far,) = gate((trade(low_gains, "seq", 2),), weight=2 * EARLY)
        their_tokens, low_in, part_in, low_od, half_od, low_qkv, their_cot, _ = prepare_rest(
            at, tokens, w_in, w_out, w_down, w_qkv, cotangent, (begun,)
        )
        near_q = trade(low_qkv, "seq", 1)
        far = trade(their_tokens, "seq", 2)
        far_qb = trade(far_qa, "dp", 1)
        near_qa = trade(far_qa, "seq", 1)
        near_qb = trade(far_qb, "seq", 1)
        gain_near = trade(jnp.stack([low_gains, gain_far]), "seq", 1)
        gain_stack = jnp.stack([low_gains, gain_near[0], gain_far, gain_near[1]])
        gain_low = jnp.concatenate(
            [index(gain_stack, b ^ place) for b in range(4)], axis=1
        ).astype(FULL)
        blocks_qkv = (low_qkv, near_q, far_qa, far_qb, near_qa, near_qb)
        low_in, low_od, part_in, half_od = gate((low_in, low_od, part_in, half_od), (far_qa,))
        near_i = trade(low_in, "seq", 1)
        near_o = trade(low_od, "seq", 1)
        (come_in,) = gate((trade(part_in, "seq", 2),), weight=EARLY)

        seg = index(segments, slot)
        positions = doc_positions(seg).reshape(4, local_len)
        seg = seg.reshape(4, local_len)
        chunks = [place, place ^ 2, place ^ 1, place ^ 3]
        seg_keys = jnp.concatenate([index(seg, c) for c in chunks])
        pos = jnp.concatenate([index(positions, c) for c in chunks[:2]])
        cos_part, sin_part = rope_tables(pos)
        lane = jnp.arange(PAIR, dtype=jnp.int32)[None] % HEAD_DIM
        same = seg_keys[:, None] == lane
        mark_key = jnp.where(lane < DOCS, 1.0 - same, (lane < DOCS + 3) * 1.0).astype(LOW)
        mark_query = jnp.where((lane < DOCS) & same[:rows], NEG_FILL, 0.0).astype(LOW)

        normed, query, kv, _ = project(
            at, tokens, far, gain_low[:1], cos_part, sin_part, blocks_qkv,
            (come_in, mark_key, mark_query),
        )
        kv_far = trade(kv, "seq", 1)
        (beside_in,) = gate((trade(come_in, "dp", 2),), weight=EARLY)
        far_ia, _ = join_two(at, come_in, beside_in)
        far_ib = trade(far_ia, "dp", 1)
        near_ia = trade(far_ia, "seq", 1)
        pairs = width // PAIR
        two = pairs // 3
        args = (query, kv, kv_far, mark_query, mark_key)
        o_a, extra_a, done_a = attend(0, two, *args)
        (far_oa,) = gate((trade(half_od, "seq", 2),), (done_a,), weight=EARLY)
        near_oa = trade(far_oa, "seq", 1)
        (their_cot,) = gate((their_cot,), (far_oa,))
        (cot_far,) = gate((trade(their_cot, "seq", 2),), weight=WEIGHT)
        far_ob = trade(far_oa, "dp", 1)
        o_b, extra_b, done_b = attend(two, two, *args, late=(done_a, far_oa))
        o_c, extra_c, done_c = attend(2 * two, pairs - 2 * two, *args, late=(done_b, far_ib))
        near_ib = trade(far_ib, "seq", 1)
        (far_ob,) = gate((far_ob,), (done_c,))
        near_ob = trade(far_ob, "seq", 1)
        blocks_in = (low_in, near_i, far_ia, far_ib, near_ia, near_ib)
        blocks_od = (low_od, near_o, far_oa, far_ob, near_oa, near_ob)

        mixed, mixed_far, dx1, do, keep_rest, send_rest, _ = middle(
            at, valid, tokens, far, cotangent, cot_far, (o_a, o_b, o_c), gain_low[1:], blocks_in, blocks_od
        )
        got_rest = trade(send_rest, "seq", 1)
        near_args = (query, kv, kv_far)
        back_args = (mark_key, do, cos_part, sin_part)
        dq0, own0, give0, back0 = attend_back(0, 0, two, *near_args, extra_a, o_a, *back_args)
        *r1, r1_done = first_sums(at, keep_rest, got_rest, late=(back0,))
        got_ra, got_rb = gate(
            (trade(r1[1], "seq", 2), trade(r1[3], "dp", 1)), weight=10 * WEIGHT
        )
        got0 = trade(give0, "seq", 1)
        dq1, own1, give1, back1 = attend_back(
            two, 0, two, *near_args, extra_b, o_b, *back_args, late=(r1_done,)
        )
        got1 = trade(give1, "seq", 1)
        dq2, own2, give2, back2 = attend_back(
            2 * two, 0, pairs - 2 * two, *near_args, extra_c, o_c, *back_args,
            late=(back1, got0),
        )
        got2 = trade(give2, "seq", 1)
        dqkv, normed_t, send_qkv, send_done = qkv_send(
            at, normed, (dq0, dq1, dq2), (own0, own1, own2), (got0, got1, got2),
            cos_part, sin_part, late=(),
        )
        got_qkv = trade(send_qkv, "seq", 1)
        *r2, r2_done = second_sums(at, r1[0], got_ra, r1[2], got_rb, late=(send_done,))
        got_ra, got_rb = trade(r2[1], "dp", 1), trade(r2[3], "seq", 2)
        keep_qkv, _ = qkv_keep(at, normed_t, dqkv, late=(r2_done,))
        *q1, q1_done = first_sums(at, keep_qkv, got_qkv)
        got_qa, got_qb = trade(q1[1], "seq", 2), trade(q1[3], "dp", 1)
        rest, give_rest, r3_done = third_sums(
            at, r2[0], got_ra, r2[2], got_rb, late=(q1_done,)
        )
        got_rest = trade(give_rest, "dp", 2)
        grad, grad_far, grad_done = input_back(
            at, tokens, far, gain_low[:1], dx1, dqkv, blocks_qkv, late=(r3_done,)
        )
        *q2, q2_done = second_sums(at, q1[0], got_qa, q1[2], got_qb, late=(grad_done,))
        got_qa, got_qb = gate(
            (trade(q2[1], "dp", 1), trade(q2[3], "seq", 2)), weight=10 * WEIGHT
        )
        rest, rest_done = add((rest,), (got_rest,), late=(q2_done,))
        got_rest = trade(rest, "dp", far_bits[0])
        qkv, give_qkv, q3_done = third_sums(
            at, q2[0], got_qa, q2[2], got_qb, late=(rest_done,)
        )
        mixed_far, grad_far = gate((mixed_far, grad_far), (q3_done,))
        mixed_far = trade(mixed_far, "seq", 2)
        grad_far = trade(grad_far, "seq", 2)
        qkv, qkv_done = add((qkv,), (trade(give_qkv, "dp", 2),))
        (got_qkv,) = gate((trade(qkv, "dp", far_bits[0]),), weight=EARLY // 7)
        rest, rest_done = add((rest,), (got_rest,), late=(qkv_done, mixed_far))
        for bit in far_bits[1:]:
            rest, rest_done = add((rest,), (trade(rest, "dp", bit),))

        beside, other = trade(rest, "dp", 2), trade(rest, "dp", 1)
        mixed, grad, fill_done = fill(at, mixed, mixed_far, grad, grad_far)
        qkv, qkv_done = add((qkv,), (got_qkv,), late=(rest_done, grad_far))
        for bit in far_bits[1:]:
            qkv, qkv_done = add((qkv,), (trade(qkv, "dp", bit),))
        square, square_done = squares(at, qkv, w_qkv, rest, w_in, gains)
        (qkv,) = gate((qkv,), (square_done,))
        qkv_beside, qkv_other = trade(qkv, "dp", 2), trade(qkv, "dp", 1)
        square, _ = add((square,), (trade(square, "seq", 2),))
        square, square_done = add(
            (square,), (trade(square, "seq", 1),), late=(qkv_beside, qkv_other, beside, other)
        )
        (beside,) = gate((beside,), (square_done,))
        rest_parts = (rest, beside, other, trade(beside, "dp", 1))
        qkv_parts = (qkv, qkv_beside, qkv_other, trade(qkv_beside, "dp", 1))
        square, _ = add((square,), (trade(square, "dp", 2),))
        square, _ = add(
            (square,), (trade(square, "dp", 1),), late=(rest_parts[3], fill_done)
        )

        (new_in, first_in, second_in, new_out, first_out, second_out,
         new_down, first_down, second_down, row, _) = update_rest(
            at, square, rest_parts,
            (w_in, m_in, v_in), (w_out, m_out, v_out), (w_down, m_down, v_down), (),
        )
        (new_qkv, first_qkv, second_qkv, new_gains, first_gains, second_gains, norm, _) = (
            update_last(
                at, square, (w_qkv, m_qkv, v_qkv), qkv_parts, row, (gains, m_gains, v_gains)
            )
        )
        return (
            mixed,
            grad,
            norm[0, 0],
            new_qkv, new_out, new_in, new_down, new_gains,
            first_qkv, first_out, first_in, first_down, first_gains,
            second_qkv, second_out, second_in, second_down, second_gains,
        )

    return on_device


def solution(mesh):
    rows, matrix, gain = P("dp", "seq", None), P("seq", None), P(None, "seq")
    weights = (matrix,) * 4 + (gain,)
    return jax.shard_map(
        make(mesh.shape["dp"], mesh.shape["seq"]),
        mesh=mesh,
        in_specs=(rows, rows, P("dp", None), P("dp")) + weights * 3,
        out_specs=(rows, rows, P()) + weights * 3,
        check_vma=False,
    )
```

```python
import functools
import math

import jax
import jax.numpy as jnp
from jax import lax
from jax.experimental import pallas as pl
from jax.experimental.pallas import tpu as pltpu
from jax.sharding import PartitionSpec as P

HEADS = 12
HEAD_DIM = 64
PAIR = 2 * HEAD_DIM
STEP_COUNT = 10
EPS_NORM = 1e-05
ROPE_BASE = 160000.0
NEG_FILL = -1e30
CLIP_LIMIT = 10.0
BETA_FIRST = 0.9
BETA_SECOND = 0.98
EPS_ADAM = 1e-06
STEP_RATES = (0.1, 0.5, 0.1, 0.1, 1.0)
DECAY_RATES = (0.01, 0.01, 0.01, 0.01, 0.0)
DOCS = 5
LOW = jnp.bfloat16
FULL = jnp.float32
SCALE = 1.0 / math.sqrt(HEAD_DIM)
WEIGHT = 20_000_000_000
EARLY = 20_000_000_000


def doc_positions(segment_ids):
    seq_len = segment_ids.shape[-1]
    places = jnp.arange(seq_len, dtype=jnp.int32)
    first_mark = jnp.ones((1,), jnp.bool_)
    change = jnp.concatenate([first_mark, segment_ids[1:] != segment_ids[:-1]])
    starts = lax.cummax(jnp.where(change, places, 0), axis=0)
    return places - starts


def rope_tables(positions):
    half_dim = HEAD_DIM // 2
    exponents = jnp.arange(half_dim, dtype=jnp.float32) * (2.0 / HEAD_DIM)
    inv_freq = ROPE_BASE ** (-exponents)
    angles = positions.astype(jnp.float32)[:, None] * inv_freq
    cos_part, sin_part = jnp.cos(angles), jnp.sin(angles)
    return (
        jnp.concatenate([cos_part] * 4, axis=1),
        jnp.concatenate([-sin_part, sin_part] * 2, axis=1),
    )


def adam_step(weight, first_old, second_old, gradient, factor, step_rate, decay_rate):
    first_new = BETA_FIRST * first_old + ((1.0 - BETA_FIRST) * factor) * gradient
    second_new = BETA_SECOND * second_old + ((1.0 - BETA_SECOND) * factor * factor) * (
        gradient * gradient
    )
    unbias = math.sqrt(1.0 - BETA_SECOND**STEP_COUNT)
    rate = step_rate / (1.0 - BETA_FIRST**STEP_COUNT) * unbias
    inverse = lax.rsqrt(second_new * lax.rsqrt(second_new) + EPS_ADAM * unbias)
    step = first_new * rate * (inverse * inverse)
    return (weight * (1.0 - step_rate * decay_rate) - step, first_new, second_new)


def mul(left, right):
    return lax.dot_general(left, right, (((1,), (0,)), ((), ())), preferred_element_type=FULL)


def mul_t(left, right):
    return lax.dot_general(left, right, (((1,), (1,)), ((), ())), preferred_element_type=FULL)


def normalize(values):
    centered = values - jnp.mean(values, axis=-1, keepdims=True)
    root = lax.rsqrt(jnp.mean(centered * centered, axis=-1, keepdims=True) + EPS_NORM)
    return centered * root, root


def normalize_back(grad, gain, scaled, root):
    t = grad * gain
    back = root * (
        t
        - jnp.mean(t, axis=-1, keepdims=True)
        - scaled * jnp.mean(t * scaled, axis=-1, keepdims=True)
    )
    return back


def turn(values, cos_part, sin_part):
    lane = lax.broadcasted_iota(jnp.int32, values.shape, 1)
    swapped = jnp.where(
        lane % HEAD_DIM < HEAD_DIM // 2,
        pltpu.roll(values, PAIR - HEAD_DIM // 2, 1),
        pltpu.roll(values, HEAD_DIM // 2, 1),
    )
    return values * cos_part + swapped * sin_part


def three_parts(values):
    high = values.astype(LOW).astype(FULL)
    rest = values - high
    mid = rest.astype(LOW).astype(FULL)
    return high, mid, rest - mid


def wait_all(copies):
    for copy in copies:
        copy.wait()


def put(source, target, sem):
    copy = pltpu.make_async_copy(source, target, sem)
    copy.start()
    return copy


PIECES = ((0, None), (1, None), (2, 0), (2, 1), (3, 0), (3, 1))


def join_blocks(at_ref, blocks, whole):
    rows = blocks[0].shape[0]
    for block, (bits, part) in zip(blocks, PIECES):
        start = (at_ref[0] ^ bits) * rows
        size = rows
        if part is not None:
            size = rows // 2
            start += (at_ref[1] ^ part) * size
        whole[pl.ds(pl.multiple_of(start, size), size), :] = block[...]


def join_folded(at_ref, blocks, w_out, w_down):
    rows, width = blocks[0].shape[0], w_out.shape[1]
    short, last = rows // 2, width // 2
    for block, (bits, part) in zip(blocks, PIECES):
        owner = at_ref[0] ^ bits
        base = owner * (rows + short)
        first = 0 if part is None else (at_ref[1] ^ part) * short
        size = rows if part is None else short
        span = pl.ds(pl.multiple_of(owner * rows + first, short), size)
        w_out[span, :] = block[:, :width]
        span = pl.ds(pl.multiple_of(base + first, short), size)
        w_down[span, :] = block[:, width : 2 * width]
        span = pl.ds(pl.multiple_of(base + rows, short), short)
        if part is None:
            for i in range(2):
                w_down[span, i * last : (i + 1) * last] = block[
                    i * short : (i + 1) * short, 2 * width :
                ]
        else:
            lanes = pl.ds(pl.multiple_of((at_ref[1] ^ part) * last, last), last)
            w_down[span, lanes] = block[:, 2 * width :]


def fold(out, w_out, w_down, first):
    rows, width = w_out.shape
    short, last = rows // 2, width // 2
    out[:, first : first + width] = w_out[...].astype(LOW)
    out[:, first + width : first + 2 * width] = w_down[:rows, :].astype(LOW)
    for i in range(2):
        out[i * short : (i + 1) * short, first + 2 * width :] = w_down[
            rows:, i * last : (i + 1) * last
        ].astype(LOW)


def prepare_first_kernel(at_ref, w_ref, gains_ref, half_ref, gains_out, wide, sem):
    short = half_ref.shape[0]
    span = pl.ds(pl.multiple_of(at_ref[1] * short, short), short)
    copy = put(w_ref.at[span, :], wide, sem.at[0])
    gains_out[...] = gains_ref[...].astype(LOW)
    copy.wait()
    half_ref[...] = wide[...].astype(LOW)


def prepare_rest_kernel(at_ref, tokens_ref, in_ref, out_ref, down_ref, qkv_ref, cot_ref,
                        their_tokens, low_in, part_in, low_od, half_od, low_qkv, their_cot,
                        in_wide, out_wide, down_wide, qkv_wide, sem):
    slot = 1 - at_ref[2]
    copies = [
        put(source, target, sem.at[i])
        for i, (source, target) in enumerate((
            (tokens_ref.at[slot], their_tokens), (in_ref, in_wide), (out_ref, out_wide),
            (down_ref, down_wide), (qkv_ref, qkv_wide), (cot_ref.at[slot], their_cot),
        ))
    ]
    short = part_in.shape[0]
    span = pl.ds(pl.multiple_of((2 * at_ref[1] + at_ref[4]) * short, short), short)
    copies[1].wait()
    part_in[...] = in_wide[span, :].astype(LOW)
    low_in[...] = in_wide[...].astype(LOW)
    copies[2].wait()
    copies[3].wait()
    fold(low_od, out_wide, down_wide, 0)
    short = half_od.shape[0]
    half_od[...] = low_od[pl.ds(pl.multiple_of(at_ref[1] * short, short), short), :]
    copies[4].wait()
    low_qkv[...] = qkv_wide[...].astype(LOW)
    copies[0].wait()
    copies[5].wait()


def project_kernel(at_ref, tokens_ref, far_ref, gain_ref, cos_ref, sin_ref, w0, w1, w2, w3, w4, w5,
                   normed_ref, query_ref, kv_ref, weight):
    join_blocks(at_ref, (w0, w1, w2, w3, w4, w5), weight)
    rows, width = far_ref.shape
    for part in range(2):
        values = tokens_ref[at_ref[2]] if part == 0 else far_ref[...]
        scaled, _ = normalize(values.astype(FULL))
        normed_ref[pl.ds(part * rows, rows), :] = (scaled * gain_ref[...]).astype(LOW)
    for part in range(2):
        span = pl.ds(part * rows, rows)
        normed = normed_ref[span, :]
        cos_part, sin_part = cos_ref[span, :], sin_ref[span, :]
        for pair in range(2 * width // PAIR):
            lanes = pl.ds(pair * PAIR, PAIR)
            if pair % 2 == 0:
                both = mul(normed, weight[:, pl.ds(pair * PAIR, 2 * PAIR)])
            raw = both[:, (pair % 2) * PAIR : (pair % 2 + 1) * PAIR]
            turned = turn(raw, cos_part, sin_part)
            if pair < width // PAIR:
                query_ref[span, lanes] = (turned * SCALE).astype(LOW)
            else:
                kv_ref[0, span, pl.ds(pair * PAIR - width, PAIR)] = turned.astype(LOW)
        kv_ref[1, span, :] = mul(normed, weight[:, 2 * width :]).astype(LOW)


def head_lanes(head, shape):
    lane = lax.broadcasted_iota(jnp.int32, shape, 1)
    return (lane < HEAD_DIM) if head == 0 else (lane >= HEAD_DIM)


def pick(head, inside, outside):
    return jnp.where(head_lanes(head, inside.shape), inside, outside)


def attend_kernel(query_ref, near_ref, far_ref, mark_query_ref, mark_key_ref, o_ref, extra_ref):
    rows = query_ref.shape[0]
    query = query_ref[...]
    mark_query = mark_query_ref[...]
    parts = [
        (near_ref[0], jnp.transpose(near_ref[1]), mark_key_ref[:rows, :]),
        (far_ref[0], jnp.transpose(far_ref[1]), mark_key_ref[rows:, :]),
    ]
    outs, logs = [], []
    for head in range(2):
        query_head = pick(head, query, mark_query)
        scores = [mul_t(pick(head, key, mark), query_head) for key, _, mark in parts]
        top = jnp.maximum(
            jnp.max(scores[0], axis=0, keepdims=True), jnp.max(scores[1], axis=0, keepdims=True)
        )
        exps = [jnp.exp(score - top) for score in scores]
        total = jnp.sum(exps[0], axis=0, keepdims=True) + jnp.sum(exps[1], axis=0, keepdims=True)
        span = slice(head * HEAD_DIM, (head + 1) * HEAD_DIM)
        out = sum(mul(value_t[span], e.astype(LOW)) for (_, value_t, _), e in zip(parts, exps))
        outs.append(out / total)
        logs.append(top + jnp.log(total))
    o_ref[...] = jnp.transpose(jnp.concatenate(outs)).astype(LOW)
    line = lax.broadcasted_iota(jnp.int32, (PAIR, rows), 0)
    extra = jnp.zeros((PAIR, rows), FULL)
    for head in range(2):
        base = DOCS + (HEAD_DIM if head == 0 else 0)
        for i, piece in enumerate(three_parts(-logs[head])):
            extra = jnp.where(line == base + i, piece, extra)
    extra_ref[...] = jnp.transpose(extra).astype(LOW) + mark_query


def attend_back_kernel(query_ref, near_ref, far_ref, extra_ref, mark_key_ref, o_ref, do_ref,
                       cos_ref, sin_ref, dq_ref, keep_ref, send_ref):
    rows = query_ref.shape[0]
    query, extra, do = query_ref[...], extra_ref[...], do_ref[...]
    inner_all = do.astype(FULL) * o_ref[...].astype(FULL)
    lane = lax.broadcasted_iota(jnp.int32, (rows, PAIR), 1)
    zero = jnp.zeros((rows, PAIR), LOW)
    grads_query = []
    sums = [[None, None], [None, None]]
    keys_t = [jnp.transpose(near_ref[0]), jnp.transpose(far_ref[0])]
    for head in range(2):
        inside = head_lanes(head, (rows, PAIR))
        inner = jnp.sum(jnp.where(inside, inner_all, 0.0), axis=1, keepdims=True)
        base = DOCS + (HEAD_DIM if head == 0 else 0)
        tail = jnp.zeros((rows, PAIR), FULL)
        for i, piece in enumerate(three_parts(-inner)):
            tail = jnp.where(lane == base + i, piece, tail)
        query_head = pick(head, query, extra)
        do_head = pick(head, do, tail.astype(LOW))
        query_only = pick(head, query, zero)
        do_only = pick(head, do, zero)
        span = slice(head * HEAD_DIM, (head + 1) * HEAD_DIM)
        grad_query = 0.0
        for part, ref in enumerate((near_ref, far_ref)):
            mark = mark_key_ref[pl.ds(part * rows, rows), :]
            probs = jnp.exp(mul_t(pick(head, ref[0], mark), query_head))
            grad_probs = mul_t(pick(head, ref[1], mark), do_head)
            grad_scores = (probs * grad_probs).astype(LOW)
            grad_value = mul(probs.astype(LOW), do_only)
            grad_key = mul(grad_scores, query_only)
            grad_query += mul(keys_t[part][span], grad_scores)
            if head == 0:
                sums[part] = [grad_key, grad_value]
            else:
                sums[part] = [sums[part][0] + grad_key, sums[part][1] + grad_value]
        grads_query.append(grad_query)
    turned = turn(
        jnp.transpose(jnp.concatenate(grads_query)) * SCALE, cos_ref[...], -sin_ref[...]
    )
    dq_ref[...] = turned.astype(LOW)
    for i in range(2):
        keep_ref[i] = sums[0][i].astype(LOW)
        send_ref[i] = sums[1][i].astype(LOW)


def middle_kernel(at_ref, live_ref, tokens_ref, far_ref, cot_ref, cot_far_ref,
                  oa_ref, ob_ref, oc_ref, gain_ref, i0, i1, i2, i3, i4, i5, d0, d1, d2, d3, d4, d5,
                  mixed_ref, mixed_far_ref, dx1_ref, do_ref, keep_ref, send_ref,
                  w_out, w_in, w_down, o_all, o_t, a2_t, h_t, h_all, dm_all, duw_all, db_all,
                  mixed, dx1_all, do_all, keep, send, out_sem):
    place, slot = at_ref[0], at_ref[2]
    live = live_ref[slot].astype(FULL)
    join_folded(at_ref, (d0, d1, d2, d3, d4, d5), w_out, w_down)
    join_blocks(at_ref, (i0, i1, i2, i3, i4, i5), w_in)
    rows, width = far_ref.shape
    share = width // 4
    short, units = share // 2, w_down.shape[0]
    gain = gain_ref[...]
    first = 0
    for ref in (oa_ref, ob_ref, oc_ref):
        o_all[:, first : first + ref.shape[1]] = ref[...]
        first += ref.shape[1]
    copies = []
    for part in range(2):
        span = pl.ds(part * rows, rows)
        o = o_all[span, :]
        values = tokens_ref[slot] if part == 0 else far_ref[...]
        x1 = values.astype(FULL) + live * mul(o, w_out[...])
        scaled, root = normalize(x1)
        a2 = (scaled * gain).astype(LOW)
        cot = (cot_ref[slot] if part == 0 else cot_far_ref[...]).astype(FULL)
        dm = (live * cot).astype(LOW)
        for first in range(0, units, units // 3):
            lanes = slice(first, first + units // 3)
            lanes_lin = slice(units + first, units + first + units // 3)
            u = mul(a2, w_in[:, lanes])
            w = mul(a2, w_in[:, lanes_lin])
            dh = mul_t(dm, w_down[lanes, :])
            phi = 0.5 * (1.0 + lax.erf(u * math.sqrt(0.5)))
            gelu = u * phi
            slope = phi + u * (jnp.exp(-0.5 * u * u) * (1.0 / math.sqrt(2.0 * math.pi)))
            h_all[:, lanes] = (gelu * w).astype(LOW)
            duw_all[span, lanes] = (dh * w * slope).astype(LOW)
            duw_all[span, lanes_lin] = (dh * gelu).astype(LOW)
        h = h_all[...]
        mixed[span, :] = (x1 + live * mul(h, w_down[...])).astype(LOW)
        target = mixed_ref.at[slot] if part == 0 else mixed_far_ref
        copies.append(put(mixed.at[span, :], target, out_sem.at[len(copies)]))
        da2 = mul_t(duw_all[span, :], w_in[...])
        dx1 = cot + normalize_back(da2, gain, scaled, root)
        dx1_all[span, :] = dx1
        copies.append(put(dx1_all.at[span, :], dx1_ref.at[span, :], out_sem.at[len(copies)]))
        db = (live * dx1).astype(LOW)
        do_all[span, :] = mul_t(db, w_out[...]).astype(LOW)
        copies.append(put(do_all.at[span, :], do_ref.at[span, :], out_sem.at[len(copies)]))
        db_all[span, :] = db
        dm_all[span, :] = dm
        o_t[:, span] = jnp.transpose(o)
        a2_t[:, span] = jnp.transpose(a2)
        h_t[:, span] = jnp.transpose(h)
    dm, duw, db = dm_all[...], duw_all[...], db_all[...]
    for j, out, target in ((1, send, send_ref), (3, send, send_ref), (0, keep, keep_ref), (2, keep, keep_ref)):
        span = pl.ds(pl.multiple_of((place ^ j) * share, share), share)
        base = (place ^ j) * (share + short)
        down = pl.ds(pl.multiple_of(base, short), share)
        down_last = pl.ds(pl.multiple_of(base + share, short), short)
        at = 2 * units
        out[j // 2, :, :at] = mul(a2_t[span, :], duw).astype(LOW)
        out[j // 2, :, at : at + width] = mul(o_t[span, :], db).astype(LOW)
        at += width
        out[j // 2, :, at : at + width] = mul(h_t[down, :], dm).astype(LOW)
        at += width
        last = mul(h_t[down_last, :], dm).astype(LOW)
        out[j // 2, :short, at:] = last[:, : width // 2]
        out[j // 2, short:, at:] = last[:, width // 2 :]
        copies.append(put(out.at[j // 2], target.at[j // 2], out_sem.at[len(copies)]))
    wait_all(copies)


def send_kernel(count, at_ref, *refs):
    normed_ref = refs[0]
    dqs, owns, gots = (refs[1 + i * count : 1 + (i + 1) * count] for i in range(3))
    (cos_ref, sin_ref, dqkv_ref, normed_t_ref, send_ref,
     dqkv, normed_t, send, sem) = refs[1 + 3 * count :]
    width = normed_ref.shape[1]
    part_width = width // count
    normed_t[...] = jnp.transpose(normed_ref[...])
    copies = [put(normed_t, normed_t_ref, sem.at[0])]
    cos_part, sin_part = cos_ref[...], -sin_ref[...]
    for part, (dq, own, got) in enumerate(zip(dqs, owns, gots)):
        base = part * part_width
        dqkv[:, pl.ds(base, part_width)] = dq[...]
        dqkv[:, pl.ds(2 * width + base, part_width)] = (
            own[1].astype(FULL) + got[1].astype(FULL)
        ).astype(LOW)
        for pair in range(part_width // PAIR):
            lanes = pl.ds(pair * PAIR, PAIR)
            raw = own[0, :, lanes].astype(FULL) + got[0, :, lanes].astype(FULL)
            dqkv[:, pl.ds(width + base + pair * PAIR, PAIR)] = turn(raw, cos_part, sin_part).astype(
                LOW
            )
    copies.append(put(dqkv, dqkv_ref, sem.at[1]))
    right = dqkv[...]
    share = send.shape[1]
    for j in (1, 3):
        start = pl.multiple_of((at_ref[0] ^ j) * share, share)
        send[j // 2] = mul(normed_t[pl.ds(start, share), :], right).astype(LOW)
        copies.append(put(send.at[j // 2], send_ref.at[j // 2], sem.at[len(copies)]))
    wait_all(copies)


def keep_kernel(at_ref, normed_t_ref, dqkv_ref, keep_ref, keep, sem):
    right = dqkv_ref[...]
    share = keep.shape[1]
    copies = []
    for j in (0, 2):
        start = pl.multiple_of((at_ref[0] ^ j) * share, share)
        keep[j // 2] = mul(normed_t_ref[pl.ds(start, share), :], right).astype(LOW)
        copies.append(put(keep.at[j // 2], keep_ref.at[j // 2], sem.at[len(copies)]))
    wait_all(copies)


def input_kernel(at_ref, tokens_ref, far_ref, gain_ref, dx1_ref, dqkv_ref, w0, w1, w2, w3, w4, w5,
                 grad_ref, grad_far_ref, weight, grad_own, out_sem):
    join_blocks(at_ref, (w0, w1, w2, w3, w4, w5), weight)
    rows = far_ref.shape[0]
    gain = gain_ref[...]
    for part in (1, 0):
        span = pl.ds(part * rows, rows)
        values = tokens_ref[at_ref[2]] if part == 0 else far_ref[...]
        scaled, root = normalize(values.astype(FULL))
        back = normalize_back(mul_t(dqkv_ref[span, :], weight[...]), gain, scaled, root)
        grad = dx1_ref[span, :] + back
        if part == 1:
            grad_far_ref[...] = grad.astype(LOW)
        else:
            grad_own[...] = grad
    put(grad_own, grad_ref.at[at_ref[2]], out_sem.at[0]).wait()


def shaped(*shape, kind=LOW):
    return jax.ShapeDtypeStruct(shape, kind)


IN_SMEM = pl.BlockSpec(memory_space=pltpu.SMEM)
IN_VMEM = pl.BlockSpec(memory_space=pltpu.VMEM)
IN_ANY = pl.BlockSpec(memory_space=pl.ANY)


def params(mebibytes):
    return pltpu.CompilerParams(vmem_limit_bytes=int(mebibytes * 1024 * 1024))


def call(kernel, args, in_specs, out_shape, out_specs, late=(), **options):
    if not isinstance(out_shape, tuple):
        out_shape, out_specs = (out_shape,), (out_specs,)
    count, skip, outs = len(args), len(late), len(out_shape)

    def body(*refs):
        outs_at = count + skip
        return kernel(*refs[:count], *refs[outs_at : outs_at + outs], *refs[outs_at + outs + 1 :])

    return pl.pallas_call(
        body,
        in_specs=list(in_specs) + [IN_ANY] * skip,
        out_shape=out_shape + (shaped(8, 128, kind=FULL),),
        out_specs=out_specs + (IN_ANY,),
        **options,
    )(*args, *late)


def gate(values, late=(), weight=0):
    hint = {}
    if weight:
        hint["cost_estimate"] = pl.CostEstimate(
            flops=weight, transcendentals=0, bytes_accessed=0
        )
    return call(
        lambda *refs: None,
        values,
        late=late,
        out_shape=tuple(jax.ShapeDtypeStruct(v.shape, v.dtype) for v in values),
        in_specs=[IN_ANY] * len(values),
        out_specs=(IN_ANY,) * len(values),
        input_output_aliases={i: i for i in range(len(values))},
        compiler_params=params(1),
        name="gate",
        **hint,
    )[: len(values)]


def join_two_kernel(at_ref, mine, other, out):
    short = mine.shape[0]
    out[pl.ds(pl.multiple_of(at_ref[4] * short, short), short), :] = mine[...]
    out[pl.ds(pl.multiple_of((1 - at_ref[4]) * short, short), short), :] = other[...]


def join_two(at, mine, other, late=()):
    rows, width = mine.shape
    return call(
        join_two_kernel,
        (at, mine, other),
        late=late,
        out_shape=shaped(2 * rows, width),
        in_specs=[IN_SMEM] + [IN_VMEM] * 2,
        out_specs=IN_VMEM,
        compiler_params=params(4),
        name="join_two",
    )


def in_hbm(value):
    return pltpu.with_memory_space_constraint(value, pltpu.HBM)


def in_vmem(*values):
    return [pltpu.with_memory_space_constraint(value, pltpu.VMEM) for value in values]


def prepare_first(at, weight, gains):
    rows, width = weight.shape
    return call(
        prepare_first_kernel,
        (at, in_hbm(weight), gains),
        out_shape=(shaped(rows // 2, width), shaped(*gains.shape)),
        in_specs=[IN_SMEM, IN_ANY, IN_VMEM],
        out_specs=(IN_VMEM,) * 2,
        scratch_shapes=[pltpu.VMEM((rows // 2, width), FULL), pltpu.SemaphoreType.DMA((1,))],
        compiler_params=params(6),
        name="prepare_first",
    )


def prepare_rest(at, tokens, w_in, w_out, w_down, w_qkv, cotangent, late):
    rows, width = w_out.shape
    folded = 2 * width + width // 2
    return call(
        prepare_rest_kernel,
        (at, *[in_hbm(v) for v in (tokens, w_in, w_out, w_down, w_qkv, cotangent)]),
        late=late,
        out_shape=(
            shaped(*tokens.shape[1:]),
            shaped(*w_in.shape),
            shaped(rows // 4, w_in.shape[1]),
            shaped(rows, folded),
            shaped(rows // 2, folded),
            shaped(*w_qkv.shape),
            shaped(*cotangent.shape[1:]),
        ),
        in_specs=[IN_SMEM] + [IN_ANY] * 6,
        out_specs=(IN_VMEM,) * 7,
        scratch_shapes=[
            pltpu.VMEM(v.shape, FULL) for v in (w_in, w_out, w_down, w_qkv)
        ] + [pltpu.SemaphoreType.DMA((6,))],
        compiler_params=params(18),
        name="prepare_rest",
    )


def project(at, tokens, far, gain, cos_part, sin_part, blocks, late):
    rows, width = 2 * far.shape[0], far.shape[1]
    return call(
        project_kernel,
        (at, tokens, *in_vmem(far), gain, cos_part, sin_part, *in_vmem(*blocks)),
        late=late,
        out_shape=(shaped(rows, width), shaped(rows, width), shaped(2, rows, width)),
        in_specs=[IN_SMEM] + [IN_VMEM] * 11,
        out_specs=(IN_VMEM,) * 3,
        scratch_shapes=[pltpu.VMEM((width, 3 * width), LOW)],
        compiler_params=params(18),
        name="project",
    )


def attend(first, count, query, near, far, mark_query, mark_key, late=()):
    rows = query.shape[0]
    row_spec = pl.BlockSpec((rows, PAIR), lambda i: (0, i + first))
    kv_spec = pl.BlockSpec((2, rows, PAIR), lambda i: (0, 0, i + first))
    out_spec = pl.BlockSpec((rows, PAIR), lambda i: (0, i))
    return call(
        attend_kernel,
        (*in_vmem(query, near, far), mark_query, mark_key),
        late=late,
        grid=(count,),
        out_shape=(shaped(rows, count * PAIR), shaped(rows, count * PAIR)),
        in_specs=[
            row_spec,
            kv_spec,
            kv_spec,
            pl.BlockSpec((rows, PAIR), lambda i: (0, 0)),
            pl.BlockSpec((2 * rows, PAIR), lambda i: (0, 0)),
        ],
        out_specs=(out_spec, out_spec),
        compiler_params=params(16),
        name="attend",
    )


def attend_back(
    first, first_o, count, query, near, far, extra, o, mark_key, do, cos_part, sin_part, late=()
):
    rows = query.shape[0]
    row_spec = pl.BlockSpec((rows, PAIR), lambda i: (0, i + first))
    o_spec = pl.BlockSpec((rows, PAIR), lambda i: (0, i + first_o))
    kv_spec = pl.BlockSpec((2, rows, PAIR), lambda i: (0, 0, i + first))
    fixed = pl.BlockSpec((rows, PAIR), lambda i: (0, 0))
    out_row = pl.BlockSpec((rows, PAIR), lambda i: (0, i))
    out_kv = pl.BlockSpec((2, rows, PAIR), lambda i: (0, 0, i))
    return call(
        attend_back_kernel,
        (*in_vmem(query, near, far, extra), mark_key, *in_vmem(o, do), cos_part, sin_part),
        late=late,
        grid=(count,),
        out_shape=(
            shaped(rows, count * PAIR),
            shaped(2, rows, count * PAIR),
            shaped(2, rows, count * PAIR),
        ),
        in_specs=[
            row_spec,
            kv_spec,
            kv_spec,
            o_spec,
            pl.BlockSpec((2 * rows, PAIR), lambda i: (0, 0)),
            o_spec,
            row_spec,
            fixed,
            fixed,
        ],
        out_specs=(out_row, out_kv, out_kv),
        compiler_params=params(20),
        name="attend_back",
    )


def middle(at, live, tokens, far, cot, cot_far, o_parts, gain, blocks_in, blocks_od):
    half, width = far.shape
    rows, share = 2 * half, width // 4
    units = blocks_in[0].shape[1] // 2
    total = 2 * units + blocks_od[0].shape[1]
    assert units == 4 * (share + share // 2)
    low = lambda *shape: pltpu.VMEM(shape, LOW)
    return call(
        middle_kernel,
        (at, live, tokens, *in_vmem(far), cot, *in_vmem(cot_far, *o_parts), gain,
         *in_vmem(*blocks_in, *blocks_od)),
        out_shape=(
            shaped(2, half, width),
            shaped(half, width),
            shaped(rows, width, kind=FULL),
            shaped(rows, width),
            shaped(2, share, total),
            shaped(2, share, total),
        ),
        in_specs=[IN_SMEM] * 2 + [IN_VMEM] * 20,
        out_specs=(IN_ANY,) * 6,
        scratch_shapes=[
            low(width, width),
            low(width, 2 * units),
            low(units, width),
            low(rows, width),
            low(width, rows),
            low(width, rows),
            low(units, rows),
            low(half, units),
            low(rows, width),
            low(rows, 2 * units),
            low(rows, width),
            low(rows, width),
            pltpu.VMEM((rows, width), FULL),
            low(rows, width),
            low(2, share, total),
            low(2, share, total),
            pltpu.SemaphoreType.DMA((10,)),
        ],
        compiler_params=params(44),
        name="middle",
    )


def qkv_send(at, normed, dq, own, got, cos_part, sin_part, late):
    rows, width = normed.shape
    share = width // 4
    return call(
        functools.partial(send_kernel, len(dq)),
        (at, normed, *dq, *own, *got, cos_part, sin_part),
        late=late,
        out_shape=(
            shaped(rows, 3 * width),
            shaped(width, rows),
            shaped(2, share, 3 * width),
        ),
        in_specs=[IN_SMEM] + [IN_VMEM] * (3 + 3 * len(dq)),
        out_specs=(IN_ANY,) * 3,
        scratch_shapes=[
            pltpu.VMEM((rows, 3 * width), LOW),
            pltpu.VMEM((width, rows), LOW),
            pltpu.VMEM((2, share, 3 * width), LOW),
            pltpu.SemaphoreType.DMA((4,)),
        ],
        compiler_params=params(20),
        name="qkv_send",
    )


def qkv_keep(at, normed_t, dqkv, late):
    width, rows = normed_t.shape
    share = width // 4
    return call(
        keep_kernel,
        (at, normed_t, dqkv),
        late=late,
        out_shape=shaped(2, share, 3 * width),
        in_specs=[IN_SMEM] + [IN_VMEM] * 2,
        out_specs=IN_ANY,
        scratch_shapes=[
            pltpu.VMEM((2, share, 3 * width), LOW),
            pltpu.SemaphoreType.DMA((2,)),
        ],
        compiler_params=params(16),
        name="qkv_keep",
    )


def input_back(at, tokens, far, gain, dx1, dqkv, blocks, late):
    half, width = far.shape
    return call(
        input_kernel,
        (at, tokens, far, gain, dx1, *in_vmem(dqkv, *blocks)),
        late=late,
        out_shape=(shaped(2, half, width, kind=FULL), shaped(half, width)),
        in_specs=[IN_SMEM] + [IN_VMEM] * 11,
        out_specs=(IN_ANY, IN_VMEM),
        scratch_shapes=[
            pltpu.VMEM((width, 3 * width), LOW),
            pltpu.VMEM((half, width), FULL),
            pltpu.SemaphoreType.DMA((1,)),
        ],
        compiler_params=params(20),
        name="input_back",
    )


def first_sums_kernel(at_ref, keep, got, own_a, far_a, mine_b, give_b):
    cut, short = far_a.shape[0], give_b.shape[1]

    def add(block, start, size):
        span = pl.ds(start, size)
        return (keep[block, span, :].astype(FULL) + got[block, span, :].astype(FULL)).astype(LOW)

    far_a[...] = add(1, 0, cut)
    for block in range(2):
        give_b[block] = add(block, pl.multiple_of(cut + (1 - at_ref[1]) * short, short), short)
        mine_b[block] = add(block, pl.multiple_of(cut + at_ref[1] * short, short), short)
    own_a[...] = add(0, 0, cut)


def first_sums(at, keep, got, late=()):
    _, rows, width = keep.shape
    cut, short = rows // 2, rows // 4
    return call(
        first_sums_kernel,
        (at, keep, got),
        late=late,
        out_shape=(shaped(cut, width),) * 2 + (shaped(2, short, width),) * 2,
        in_specs=[IN_SMEM] + [IN_VMEM] * 2,
        out_specs=(IN_VMEM,) * 4,
        compiler_params=params(20),
        name="first_sums",
    )


def second_sums_kernel(at_ref, own_a, got_a, mine_b, got_b, mine_a, give_a, near_b, far_b):
    short = mine_a.shape[0]
    for start, out in ((1 - at_ref[1], give_a), (at_ref[1], mine_a)):
        span = pl.ds(pl.multiple_of(start * short, short), short)
        out[...] = (own_a[span, :].astype(FULL) + got_a[span, :].astype(FULL)).astype(LOW)
    for block, out in ((1, far_b), (0, near_b)):
        out[...] = (mine_b[block].astype(FULL) + got_b[block].astype(FULL)).astype(LOW)


def second_sums(at, own_a, got_a, mine_b, got_b, late=()):
    _, short, width = mine_b.shape
    return call(
        second_sums_kernel,
        (at, own_a, got_a, mine_b, got_b),
        late=late,
        out_shape=(shaped(short, width),) * 4,
        in_specs=[IN_SMEM] + [IN_VMEM] * 4,
        out_specs=(IN_VMEM,) * 4,
        compiler_params=params(12),
        name="second_sums",
    )


def third_sums_kernel(at_ref, mine_a, got_a, near_b, got_b, keep, give):
    upper = mine_a[...].astype(FULL) + got_a[...].astype(FULL)
    lower = near_b[...].astype(FULL) + got_b[...].astype(FULL)
    keep[...] = jnp.where(at_ref[4] == 0, upper, lower).astype(LOW)
    give[...] = jnp.where(at_ref[4] == 0, lower, upper).astype(LOW)


def third_sums(at, mine_a, got_a, near_b, got_b, late=()):
    return call(
        third_sums_kernel,
        (at, mine_a, got_a, near_b, got_b),
        late=late,
        out_shape=(shaped(*mine_a.shape),) * 2,
        in_specs=[IN_SMEM] + [IN_VMEM] * 4,
        out_specs=(IN_VMEM,) * 2,
        compiler_params=params(12),
        name="third_sums",
    )


def squares_kernel(at_ref, qkv, w_qkv, rest, w_in, gains, out):
    inner = w_in.shape[1]
    total = jnp.sum(jnp.square(rest[:, inner:].astype(FULL)), keepdims=True)
    rows = qkv.shape[0]
    shape = (rows, gains.shape[1])
    offset = lax.broadcasted_iota(jnp.int32, shape, 1) - lax.broadcasted_iota(jnp.int32, shape, 0)
    for i, (piece, weight) in enumerate(((qkv, w_qkv), (rest, w_in))):
        start = at_ref[3]
        span = pl.ds(pl.multiple_of(start, 8), rows)
        values = piece[:, : weight.shape[1]].astype(FULL)
        sums = jnp.sum(weight[span, :].astype(LOW).astype(FULL) * values, axis=1, keepdims=True)
        gain = gains[i : i + 1, :].astype(LOW).astype(FULL)
        gain = jnp.sum(jnp.where(offset == start, gain, 0.0), axis=1, keepdims=True)
        total += jnp.sum(jnp.square(values), keepdims=True)
        total += jnp.sum(jnp.square(sums / gain), keepdims=True)
    out[...] = jnp.broadcast_to(total, out.shape)


def squares(*args):
    return call(
        squares_kernel,
        args,
        out_shape=shaped(8, 128, kind=FULL),
        in_specs=[IN_SMEM] + [IN_VMEM] * (len(args) - 1),
        out_specs=IN_VMEM,
        compiler_params=params(10),
        name="squares",
    )


def add_kernel(count, *refs):
    for i in range(count):
        out = refs[2 * count + i]
        out[...] = (refs[i][...].astype(FULL) + refs[count + i][...].astype(FULL)).astype(out.dtype)


def add(first, second, late=()):
    count = len(first)
    return call(
        functools.partial(add_kernel, count),
        (*first, *second),
        late=late,
        out_shape=tuple(jax.ShapeDtypeStruct(v.shape, v.dtype) for v in first),
        in_specs=[IN_VMEM] * (2 * count),
        out_specs=(IN_VMEM,) * count,
        compiler_params=params(8),
        name="add",
    )


def fill_kernel(at_ref, mixed_far, grad_far, mixed_in, grad_in, mixed, grad, wide, sem):
    first = put(mixed_far, mixed.at[1 - at_ref[2]], sem.at[0])
    wide[...] = grad_far[...].astype(FULL)
    put(wide, grad.at[1 - at_ref[2]], sem.at[1]).wait()
    first.wait()


def fill(at, mixed, mixed_far, grad, grad_far):
    return call(
        fill_kernel,
        (at, mixed_far, grad_far, mixed, grad),
        out_shape=(shaped(*mixed.shape), shaped(*grad.shape, kind=FULL)),
        in_specs=[IN_SMEM, IN_VMEM, IN_VMEM, IN_ANY, IN_ANY],
        out_specs=(IN_ANY,) * 2,
        input_output_aliases={3: 0, 4: 1},
        scratch_shapes=[pltpu.VMEM(grad_far.shape, FULL), pltpu.SemaphoreType.DMA((2,))],
        compiler_params=params(4),
        name="fill",
    )


def clip_factor(square_ref):
    norm = jnp.sqrt(square_ref[:1, :1])
    return jnp.minimum(1.0, CLIP_LIMIT / (norm + 1e-06))


def quarters(at_ref, parts):
    own, beside, other, other_beside = parts
    for i in range(4):
        same = at_ref[4] == i // 2
        near = jnp.where(same, own[...], beside[...])
        far = jnp.where(same, other[...], other_beside[...])
        yield jnp.where(at_ref[1] == i % 2, near, far).astype(FULL)


def gain_row(weight, gradient, start, shape):
    sums = jnp.sum(weight.astype(LOW).astype(FULL) * gradient, axis=1, keepdims=True)
    shape = (weight.shape[0], shape[1])
    offset = lax.broadcasted_iota(jnp.int32, shape, 1) - lax.broadcasted_iota(jnp.int32, shape, 0)
    return jnp.sum(jnp.where(offset == start, sums, 0.0), axis=0, keepdims=True)


class Update:
    def __init__(self, number, sources, news, targets, sem):
        self.number, self.sources, self.news, self.targets = number, sources, news, targets
        self.sem, self.out = sem, []

    def step(self, span, gradient, factor):
        rows, lanes = span
        short = (rows.stop - rows.start) // 2
        for i in range(2):
            part = (slice(rows.start + i * short, rows.start + (i + 1) * short), lanes)
            results = adam_step(
                self.sources[0][part], self.sources[1][part], self.sources[2][part],
                gradient[i * short : (i + 1) * short, :], factor,
                STEP_RATES[self.number], DECAY_RATES[self.number],
            )
            for result, new, target in zip(results, self.news, self.targets):
                new[part] = result
                self.out.append(put(new.at[part], target.at[part], self.sem.at[len(self.out)]))
        return self.sources[0][span]


def update_rest_kernel(at_ref, square_ref, *refs):
    parts, refs = refs[:4], refs[4:]
    sources, targets, row_ref, news, sem = refs[:9], refs[9:18], refs[18], refs[19:28], refs[28]
    inner, out, down = (
        Update(number, *(group[3 * k : 3 * k + 3] for group in (sources, news, targets)), sem.at[k])
        for k, number in enumerate((2, 1, 3))
    )
    factor = clip_factor(square_ref)
    rows, width = sources[3].shape
    lanes = sources[0].shape[1]
    short, last = rows // 4, width // 2
    row = jnp.zeros(row_ref.shape, FULL)
    for i, gradient in enumerate(quarters(at_ref, parts)):
        span = (slice(i * short, (i + 1) * short), slice(None))
        part = gradient[:, :lanes]
        row += gain_row(inner.step(span, part, factor), part, i * short, row_ref.shape)
        out.step(span, gradient[:, lanes : lanes + width], factor)
        down.step(span, gradient[:, lanes + width : lanes + 2 * width], factor)
        start = rows + (i % 2) * short
        span = (slice(start, start + short), slice((i // 2) * last, (i // 2 + 1) * last))
        down.step(span, gradient[:, lanes + 2 * width :], factor)
    row_ref[...] = row
    wait_all(inner.out + out.out + down.out)


def update_rest(at, square, parts, inner, out, down, late):
    like = [jax.ShapeDtypeStruct(v.shape, FULL) for v in (*inner, *out, *down)]
    return call(
        update_rest_kernel,
        (at, square, *parts, *inner, *out, *down),
        late=late,
        out_shape=(*like, shaped(1, inner[0].shape[0], kind=FULL)),
        in_specs=[IN_SMEM] + [IN_VMEM] * 14,
        out_specs=(IN_ANY,) * 9 + (IN_VMEM,),
        scratch_shapes=[pltpu.VMEM(v.shape, FULL) for v in like]
        + [pltpu.SemaphoreType.DMA((3, 48))],
        compiler_params=params(28),
        name="update_rest",
    )


def update_last_kernel(at_ref, square_ref, row_ref, g_w, g_m, g_v, *refs):
    parts, refs = refs[:4], refs[4:]
    sources, targets = refs[:3], refs[3:6]
    g_w_out, g_m_out, g_v_out, norm_out = refs[6:10]
    news, sem = refs[10:13], refs[13]
    qkv = Update(0, sources, news, targets, sem)
    factor = clip_factor(square_ref)
    norm_out[...] = jnp.sqrt(square_ref[...])
    short = sources[0].shape[0] // 4
    row = jnp.zeros(row_ref.shape, FULL)
    for i, gradient in enumerate(quarters(at_ref, parts)):
        span = (slice(i * short, (i + 1) * short), slice(None))
        row += gain_row(qkv.step(span, gradient, factor), gradient, i * short, row_ref.shape)
    for i, values in enumerate((row, row_ref[...])):
        line = slice(i, i + 1)
        gradient = values / g_w[line, :].astype(LOW).astype(FULL)
        g_w_out[line, :], g_m_out[line, :], g_v_out[line, :] = adam_step(
            g_w[line, :], g_m[line, :], g_v[line, :], gradient, factor,
            STEP_RATES[4], DECAY_RATES[4],
        )
    wait_all(qkv.out)


def update_last(at, square, qkv, qkv_parts, row, gains):
    like = [jax.ShapeDtypeStruct(v.shape, FULL) for v in qkv]
    return call(
        update_last_kernel,
        (at, square, row, *gains, *qkv_parts, *qkv),
        out_shape=(
            *like,
            *[jax.ShapeDtypeStruct(v.shape, FULL) for v in gains],
            jax.ShapeDtypeStruct(square.shape, FULL),
        ),
        in_specs=[IN_SMEM] + [IN_VMEM] * 12,
        out_specs=(IN_ANY,) * 3 + (IN_VMEM,) * 4,
        scratch_shapes=[pltpu.VMEM(v.shape, FULL) for v in like]
        + [pltpu.SemaphoreType.DMA((24,))],
        compiler_params=params(18),
        name="update_last",
    )


def low_sum(*values):
    return sum(value.astype(FULL) for value in values).astype(LOW)


def index(value, i):
    return lax.dynamic_index_in_dim(value, i, 0, keepdims=False)


def make(dp_count, seq_count):
    assert seq_count == 4 and dp_count >= 8 and dp_count & (dp_count - 1) == 0
    far_bits = [1 << i for i in range(2, dp_count.bit_length() - 1)]

    def trade(value, axis, bit):
        size = seq_count if axis == "seq" else dp_count
        return lax.ppermute(value, axis, [(i, i ^ bit) for i in range(size)])

    def on_device(
        tokens, cotangent, segments, valid,
        w_qkv, w_out, w_in, w_down, gains,
        m_qkv, m_out, m_in, m_down, m_gains,
        v_qkv, v_out, v_in, v_down, v_gains,
    ):
        place = lax.axis_index("seq")
        group = lax.axis_index("dp")
        slot = place >> 1
        half = group & 1
        local_len, width = tokens.shape[1:]
        rows = 2 * local_len
        share = w_qkv.shape[0]
        side = (group >> 1) & 1
        quarter = share // 4
        at = jnp.stack([place, half, slot, side * 2 * quarter + half * quarter, side])

        half_qkv, low_gains, begun = prepare_first(at, w_qkv, gains)
        (far_qa,) = gate((trade(half_qkv, "seq", 2),), weight=EARLY)
        (gain_far,) = gate((trade(low_gains, "seq", 2),), weight=2 * EARLY)
        their_tokens, low_in, part_in, low_od, half_od, low_qkv, their_cot, _ = prepare_rest(
            at, tokens, w_in, w_out, w_down, w_qkv, cotangent, (begun,)
        )
        near_q = trade(low_qkv, "seq", 1)
        far = trade(their_tokens, "seq", 2)
        far_qb = trade(far_qa, "dp", 1)
        near_qa = trade(far_qa, "seq", 1)
        near_qb = trade(far_qb, "seq", 1)
        gain_near = trade(jnp.stack([low_gains, gain_far]), "seq", 1)
        gain_stack = jnp.stack([low_gains, gain_near[0], gain_far, gain_near[1]])
        gain_low = jnp.concatenate(
            [index(gain_stack, b ^ place) for b in range(4)], axis=1
        ).astype(FULL)
        blocks_qkv = (low_qkv, near_q, far_qa, far_qb, near_qa, near_qb)
        low_in, low_od, part_in, half_od = gate((low_in, low_od, part_in, half_od), (far_qa,))
        near_i = trade(low_in, "seq", 1)
        near_o = trade(low_od, "seq", 1)
        (come_in,) = gate((trade(part_in, "seq", 2),), weight=EARLY)

        seg = index(segments, slot)
        positions = doc_positions(seg).reshape(4, local_len)
        seg = seg.reshape(4, local_len)
        chunks = [place, place ^ 2, place ^ 1, place ^ 3]
        seg_keys = jnp.concatenate([index(seg, c) for c in chunks])
        pos = jnp.concatenate([index(positions, c) for c in chunks[:2]])
        cos_part, sin_part = rope_tables(pos)
        lane = jnp.arange(PAIR, dtype=jnp.int32)[None] % HEAD_DIM
        same = seg_keys[:, None] == lane
        mark_key = jnp.where(lane < DOCS, 1.0 - same, (lane < DOCS + 3) * 1.0).astype(LOW)
        mark_query = jnp.where((lane < DOCS) & same[:rows], NEG_FILL, 0.0).astype(LOW)

        normed, query, kv, _ = project(
            at, tokens, far, gain_low[:1], cos_part, sin_part, blocks_qkv,
            (come_in, mark_key, mark_query),
        )
        kv_far = trade(kv, "seq", 1)
        (beside_in,) = gate((trade(come_in, "dp", 2),), weight=EARLY)
        far_ia, _ = join_two(at, come_in, beside_in)
        far_ib = trade(far_ia, "dp", 1)
        near_ia = trade(far_ia, "seq", 1)
        pairs = width // PAIR
        two = pairs // 3
        args = (query, kv, kv_far, mark_query, mark_key)
        o_a, extra_a, done_a = attend(0, two, *args)
        (far_oa,) = gate((trade(half_od, "seq", 2),), (done_a,), weight=EARLY)
        near_oa = trade(far_oa, "seq", 1)
        (their_cot,) = gate((their_cot,), (far_oa,))
        (cot_far,) = gate((trade(their_cot, "seq", 2),), weight=WEIGHT)
        far_ob = trade(far_oa, "dp", 1)
        o_b, extra_b, done_b = attend(two, two, *args, late=(done_a, far_oa))
        o_c, extra_c, done_c = attend(2 * two, pairs - 2 * two, *args, late=(done_b, far_ib))
        near_ib = trade(far_ib, "seq", 1)
        (far_ob,) = gate((far_ob,), (done_c,))
        near_ob = trade(far_ob, "seq", 1)
        blocks_in = (low_in, near_i, far_ia, far_ib, near_ia, near_ib)
        blocks_od = (low_od, near_o, far_oa, far_ob, near_oa, near_ob)

        mixed, mixed_far, dx1, do, keep_rest, send_rest, _ = middle(
            at, valid, tokens, far, cotangent, cot_far, (o_a, o_b, o_c), gain_low[1:], blocks_in, blocks_od
        )
        got_rest = trade(send_rest, "seq", 1)
        near_args = (query, kv, kv_far)
        back_args = (mark_key, do, cos_part, sin_part)
        dq0, own0, give0, back0 = attend_back(0, 0, two, *near_args, extra_a, o_a, *back_args)
        *r1, r1_done = first_sums(at, keep_rest, got_rest, late=(back0,))
        got_ra, got_rb = gate(
            (trade(r1[1], "seq", 2), trade(r1[3], "dp", 1)), weight=10 * WEIGHT
        )
        got0 = trade(give0, "seq", 1)
        dq1, own1, give1, back1 = attend_back(
            two, 0, two, *near_args, extra_b, o_b, *back_args, late=(r1_done,)
        )
        got1 = trade(give1, "seq", 1)
        dq2, own2, give2, back2 = attend_back(
            2 * two, 0, pairs - 2 * two, *near_args, extra_c, o_c, *back_args,
            late=(back1, got0),
        )
        got2 = trade(give2, "seq", 1)
        dqkv, normed_t, send_qkv, send_done = qkv_send(
            at, normed, (dq0, dq1, dq2), (own0, own1, own2), (got0, got1, got2),
            cos_part, sin_part, late=(),
        )
        got_qkv = trade(send_qkv, "seq", 1)
        *r2, r2_done = second_sums(at, r1[0], got_ra, r1[2], got_rb, late=(send_done,))
        got_ra, got_rb = trade(r2[1], "dp", 1), trade(r2[3], "seq", 2)
        keep_qkv, _ = qkv_keep(at, normed_t, dqkv, late=(r2_done,))
        *q1, q1_done = first_sums(at, keep_qkv, got_qkv)
        got_qa, got_qb = trade(q1[1], "seq", 2), trade(q1[3], "dp", 1)
        rest, give_rest, r3_done = third_sums(
            at, r2[0], got_ra, r2[2], got_rb, late=(q1_done,)
        )
        got_rest = trade(give_rest, "dp", 2)
        grad, grad_far, grad_done = input_back(
            at, tokens, far, gain_low[:1], dx1, dqkv, blocks_qkv, late=(r3_done,)
        )
        *q2, q2_done = second_sums(at, q1[0], got_qa, q1[2], got_qb, late=(grad_done,))
        got_qa, got_qb = gate(
            (trade(q2[1], "dp", 1), trade(q2[3], "seq", 2)), weight=10 * WEIGHT
        )
        rest, rest_done = add((rest,), (got_rest,), late=(q2_done,))
        got_rest = trade(rest, "dp", far_bits[0])
        qkv, give_qkv, q3_done = third_sums(
            at, q2[0], got_qa, q2[2], got_qb, late=(rest_done,)
        )
        mixed_far, grad_far = gate((mixed_far, grad_far), (q3_done,))
        mixed_far = trade(mixed_far, "seq", 2)
        grad_far = trade(grad_far, "seq", 2)
        qkv, qkv_done = add((qkv,), (trade(give_qkv, "dp", 2),))
        (got_qkv,) = gate((trade(qkv, "dp", far_bits[0]),), weight=WEIGHT // 15)
        rest, rest_done = add((rest,), (got_rest,), late=(qkv_done, mixed_far))
        for bit in far_bits[1:]:
            rest, rest_done = add((rest,), (trade(rest, "dp", bit),))

        beside, other = trade(rest, "dp", 2), trade(rest, "dp", 1)
        mixed, grad, fill_done = fill(at, mixed, mixed_far, grad, grad_far)
        qkv, qkv_done = add((qkv,), (got_qkv,), late=(rest_done, grad_far))
        for bit in far_bits[1:]:
            qkv, qkv_done = add((qkv,), (trade(qkv, "dp", bit),))
        square, square_done = squares(at, qkv, w_qkv, rest, w_in, gains)
        (qkv,) = gate((qkv,), (square_done,))
        qkv_beside, qkv_other = trade(qkv, "dp", 2), trade(qkv, "dp", 1)
        square, _ = add((square,), (trade(square, "seq", 2),))
        square, square_done = add(
            (square,), (trade(square, "seq", 1),), late=(qkv_beside, qkv_other, beside, other)
        )
        (beside,) = gate((beside,), (square_done,))
        rest_parts = (rest, beside, other, trade(beside, "dp", 1))
        qkv_parts = (qkv, qkv_beside, qkv_other, trade(qkv_beside, "dp", 1))
        square, _ = add((square,), (trade(square, "dp", 2),))
        square, _ = add(
            (square,), (trade(square, "dp", 1),), late=(rest_parts[3], fill_done)
        )

        (new_in, first_in, second_in, new_out, first_out, second_out,
         new_down, first_down, second_down, row, _) = update_rest(
            at, square, rest_parts,
            (w_in, m_in, v_in), (w_out, m_out, v_out), (w_down, m_down, v_down), (),
        )
        (new_qkv, first_qkv, second_qkv, new_gains, first_gains, second_gains, norm, _) = (
            update_last(
                at, square, (w_qkv, m_qkv, v_qkv), qkv_parts, row, (gains, m_gains, v_gains)
            )
        )
        return (
            mixed,
            grad,
            norm[0, 0],
            new_qkv, new_out, new_in, new_down, new_gains,
            first_qkv, first_out, first_in, first_down, first_gains,
            second_qkv, second_out, second_in, second_down, second_gains,
        )

    return on_device


def solution(mesh):
    rows, matrix, gain = P("dp", "seq", None), P("seq", None), P(None, "seq")
    weights = (matrix,) * 4 + (gain,)
    return jax.shard_map(
        make(mesh.shape["dp"], mesh.shape["seq"]),
        mesh=mesh,
        in_specs=(rows, rows, P("dp", None), P("dp")) + weights * 3,
        out_specs=(rows, rows, P()) + weights * 3,
        check_vma=False,
    )
```

```python
import functools
import math

import jax
import jax.numpy as jnp
from jax import lax
from jax.experimental import pallas as pl
from jax.experimental.pallas import tpu as pltpu
from jax.sharding import PartitionSpec as P

HEADS = 12
HEAD_DIM = 64
PAIR = 2 * HEAD_DIM
STEP_COUNT = 10
EPS_NORM = 1e-05
ROPE_BASE = 160000.0
NEG_FILL = -1e30
CLIP_LIMIT = 10.0
BETA_FIRST = 0.9
BETA_SECOND = 0.98
EPS_ADAM = 1e-06
STEP_RATES = (0.1, 0.5, 0.1, 0.1, 1.0)
DECAY_RATES = (0.01, 0.01, 0.01, 0.01, 0.0)
DOCS = 5
LOW = jnp.bfloat16
FULL = jnp.float32
SCALE = 1.0 / math.sqrt(HEAD_DIM)
WEIGHT = 20_000_000_000
EARLY = 20_000_000_000


def doc_positions(segment_ids):
    seq_len = segment_ids.shape[-1]
    places = jnp.arange(seq_len, dtype=jnp.int32)
    first_mark = jnp.ones((1,), jnp.bool_)
    change = jnp.concatenate([first_mark, segment_ids[1:] != segment_ids[:-1]])
    starts = lax.cummax(jnp.where(change, places, 0), axis=0)
    return places - starts


def rope_tables(positions):
    half_dim = HEAD_DIM // 2
    exponents = jnp.arange(half_dim, dtype=jnp.float32) * (2.0 / HEAD_DIM)
    inv_freq = ROPE_BASE ** (-exponents)
    angles = positions.astype(jnp.float32)[:, None] * inv_freq
    cos_part, sin_part = jnp.cos(angles), jnp.sin(angles)
    return (
        jnp.concatenate([cos_part] * 4, axis=1),
        jnp.concatenate([-sin_part, sin_part] * 2, axis=1),
    )


def adam_step(weight, first_old, second_old, gradient, factor, step_rate, decay_rate):
    first_new = BETA_FIRST * first_old + ((1.0 - BETA_FIRST) * factor) * gradient
    second_new = BETA_SECOND * second_old + ((1.0 - BETA_SECOND) * factor * factor) * (
        gradient * gradient
    )
    unbias = math.sqrt(1.0 - BETA_SECOND**STEP_COUNT)
    rate = step_rate / (1.0 - BETA_FIRST**STEP_COUNT) * unbias
    inverse = lax.rsqrt(second_new * lax.rsqrt(second_new) + EPS_ADAM * unbias)
    step = first_new * rate * (inverse * inverse)
    return (weight * (1.0 - step_rate * decay_rate) - step, first_new, second_new)


def mul(left, right):
    return lax.dot_general(left, right, (((1,), (0,)), ((), ())), preferred_element_type=FULL)


def mul_t(left, right):
    return lax.dot_general(left, right, (((1,), (1,)), ((), ())), preferred_element_type=FULL)


def normalize(values):
    centered = values - jnp.mean(values, axis=-1, keepdims=True)
    root = lax.rsqrt(jnp.mean(centered * centered, axis=-1, keepdims=True) + EPS_NORM)
    return centered * root, root


def normalize_back(grad, gain, scaled, root):
    t = grad * gain
    back = root * (
        t
        - jnp.mean(t, axis=-1, keepdims=True)
        - scaled * jnp.mean(t * scaled, axis=-1, keepdims=True)
    )
    return back


def turn(values, cos_part, sin_part):
    lane = lax.broadcasted_iota(jnp.int32, values.shape, 1)
    swapped = jnp.where(
        lane % HEAD_DIM < HEAD_DIM // 2,
        pltpu.roll(values, PAIR - HEAD_DIM // 2, 1),
        pltpu.roll(values, HEAD_DIM // 2, 1),
    )
    return values * cos_part + swapped * sin_part


def three_parts(values):
    high = values.astype(LOW).astype(FULL)
    rest = values - high
    mid = rest.astype(LOW).astype(FULL)
    return high, mid, rest - mid


def wait_all(copies):
    for copy in copies:
        copy.wait()


def put(source, target, sem):
    copy = pltpu.make_async_copy(source, target, sem)
    copy.start()
    return copy


PIECES = ((0, None), (1, None), (2, 0), (2, 1), (3, 0), (3, 1))


def join_blocks(at_ref, blocks, whole):
    rows = blocks[0].shape[0]
    for block, (bits, part) in zip(blocks, PIECES):
        start = (at_ref[0] ^ bits) * rows
        size = rows
        if part is not None:
            size = rows // 2
            start += (at_ref[1] ^ part) * size
        whole[pl.ds(pl.multiple_of(start, size), size), :] = block[...]


def join_folded(at_ref, blocks, w_out, w_down):
    rows, width = blocks[0].shape[0], w_out.shape[1]
    short, last = rows // 2, width // 2
    for block, (bits, part) in zip(blocks, PIECES):
        owner = at_ref[0] ^ bits
        base = owner * (rows + short)
        first = 0 if part is None else (at_ref[1] ^ part) * short
        size = rows if part is None else short
        span = pl.ds(pl.multiple_of(owner * rows + first, short), size)
        w_out[span, :] = block[:, :width]
        span = pl.ds(pl.multiple_of(base + first, short), size)
        w_down[span, :] = block[:, width : 2 * width]
        span = pl.ds(pl.multiple_of(base + rows, short), short)
        if part is None:
            for i in range(2):
                w_down[span, i * last : (i + 1) * last] = block[
                    i * short : (i + 1) * short, 2 * width :
                ]
        else:
            lanes = pl.ds(pl.multiple_of((at_ref[1] ^ part) * last, last), last)
            w_down[span, lanes] = block[:, 2 * width :]


def fold(out, w_out, w_down, first):
    rows, width = w_out.shape
    short, last = rows // 2, width // 2
    out[:, first : first + width] = w_out[...].astype(LOW)
    out[:, first + width : first + 2 * width] = w_down[:rows, :].astype(LOW)
    for i in range(2):
        out[i * short : (i + 1) * short, first + 2 * width :] = w_down[
            rows:, i * last : (i + 1) * last
        ].astype(LOW)


def prepare_first_kernel(at_ref, w_ref, gains_ref, half_ref, gains_out, wide, sem):
    short = half_ref.shape[0]
    span = pl.ds(pl.multiple_of(at_ref[1] * short, short), short)
    copy = put(w_ref.at[span, :], wide, sem.at[0])
    gains_out[...] = gains_ref[...].astype(LOW)
    copy.wait()
    half_ref[...] = wide[...].astype(LOW)


def prepare_rest_kernel(at_ref, tokens_ref, in_ref, out_ref, down_ref, qkv_ref, cot_ref,
                        their_tokens, low_in, part_in, low_od, half_od, low_qkv, their_cot,
                        in_wide, out_wide, down_wide, qkv_wide, sem):
    slot = 1 - at_ref[2]
    copies = [
        put(source, target, sem.at[i])
        for i, (source, target) in enumerate((
            (tokens_ref.at[slot], their_tokens), (in_ref, in_wide), (out_ref, out_wide),
            (down_ref, down_wide), (qkv_ref, qkv_wide), (cot_ref.at[slot], their_cot),
        ))
    ]
    short = part_in.shape[0]
    span = pl.ds(pl.multiple_of((2 * at_ref[1] + at_ref[4]) * short, short), short)
    copies[1].wait()
    part_in[...] = in_wide[span, :].astype(LOW)
    low_in[...] = in_wide[...].astype(LOW)
    copies[2].wait()
    copies[3].wait()
    fold(low_od, out_wide, down_wide, 0)
    short = half_od.shape[0]
    half_od[...] = low_od[pl.ds(pl.multiple_of(at_ref[1] * short, short), short), :]
    copies[4].wait()
    low_qkv[...] = qkv_wide[...].astype(LOW)
    copies[0].wait()
    copies[5].wait()


def project_kernel(at_ref, tokens_ref, far_ref, gain_ref, cos_ref, sin_ref, w0, w1, w2, w3, w4, w5,
                   normed_ref, query_ref, kv_ref, weight):
    join_blocks(at_ref, (w0, w1, w2, w3, w4, w5), weight)
    rows, width = far_ref.shape
    for part in range(2):
        values = tokens_ref[at_ref[2]] if part == 0 else far_ref[...]
        scaled, _ = normalize(values.astype(FULL))
        normed_ref[pl.ds(part * rows, rows), :] = (scaled * gain_ref[...]).astype(LOW)
    for part in range(2):
        span = pl.ds(part * rows, rows)
        normed = normed_ref[span, :]
        cos_part, sin_part = cos_ref[span, :], sin_ref[span, :]
        for pair in range(2 * width // PAIR):
            lanes = pl.ds(pair * PAIR, PAIR)
            if pair % 2 == 0:
                both = mul(normed, weight[:, pl.ds(pair * PAIR, 2 * PAIR)])
            raw = both[:, (pair % 2) * PAIR : (pair % 2 + 1) * PAIR]
            turned = turn(raw, cos_part, sin_part)
            if pair < width // PAIR:
                query_ref[span, lanes] = (turned * SCALE).astype(LOW)
            else:
                kv_ref[0, span, pl.ds(pair * PAIR - width, PAIR)] = turned.astype(LOW)
        kv_ref[1, span, :] = mul(normed, weight[:, 2 * width :]).astype(LOW)


def head_lanes(head, shape):
    lane = lax.broadcasted_iota(jnp.int32, shape, 1)
    return (lane < HEAD_DIM) if head == 0 else (lane >= HEAD_DIM)


def pick(head, inside, outside):
    return jnp.where(head_lanes(head, inside.shape), inside, outside)


def attend_kernel(query_ref, near_ref, far_ref, mark_query_ref, mark_key_ref, o_ref, extra_ref):
    rows = query_ref.shape[0]
    query = query_ref[...]
    mark_query = mark_query_ref[...]
    parts = [
        (near_ref[0], jnp.transpose(near_ref[1]), mark_key_ref[:rows, :]),
        (far_ref[0], jnp.transpose(far_ref[1]), mark_key_ref[rows:, :]),
    ]
    outs, logs = [], []
    for head in range(2):
        query_head = pick(head, query, mark_query)
        scores = [mul_t(pick(head, key, mark), query_head) for key, _, mark in parts]
        top = jnp.maximum(
            jnp.max(scores[0], axis=0, keepdims=True), jnp.max(scores[1], axis=0, keepdims=True)
        )
        exps = [jnp.exp(score - top) for score in scores]
        total = jnp.sum(exps[0], axis=0, keepdims=True) + jnp.sum(exps[1], axis=0, keepdims=True)
        span = slice(head * HEAD_DIM, (head + 1) * HEAD_DIM)
        out = sum(mul(value_t[span], e.astype(LOW)) for (_, value_t, _), e in zip(parts, exps))
        outs.append(out / total)
        logs.append(top + jnp.log(total))
    o_ref[...] = jnp.transpose(jnp.concatenate(outs)).astype(LOW)
    line = lax.broadcasted_iota(jnp.int32, (PAIR, rows), 0)
    extra = jnp.zeros((PAIR, rows), FULL)
    for head in range(2):
        base = DOCS + (HEAD_DIM if head == 0 else 0)
        for i, piece in enumerate(three_parts(-logs[head])):
            extra = jnp.where(line == base + i, piece, extra)
    extra_ref[...] = jnp.transpose(extra).astype(LOW) + mark_query


def attend_back_kernel(query_ref, near_ref, far_ref, extra_ref, mark_key_ref, o_ref, do_ref,
                       cos_ref, sin_ref, dq_ref, keep_ref, send_ref):
    rows = query_ref.shape[0]
    query, extra, do = query_ref[...], extra_ref[...], do_ref[...]
    inner_all = do.astype(FULL) * o_ref[...].astype(FULL)
    lane = lax.broadcasted_iota(jnp.int32, (rows, PAIR), 1)
    zero = jnp.zeros((rows, PAIR), LOW)
    grads_query = []
    sums = [[None, None], [None, None]]
    keys_t = [jnp.transpose(near_ref[0]), jnp.transpose(far_ref[0])]
    for head in range(2):
        inside = head_lanes(head, (rows, PAIR))
        inner = jnp.sum(jnp.where(inside, inner_all, 0.0), axis=1, keepdims=True)
        base = DOCS + (HEAD_DIM if head == 0 else 0)
        tail = jnp.zeros((rows, PAIR), FULL)
        for i, piece in enumerate(three_parts(-inner)):
            tail = jnp.where(lane == base + i, piece, tail)
        query_head = pick(head, query, extra)
        do_head = pick(head, do, tail.astype(LOW))
        query_only = pick(head, query, zero)
        do_only = pick(head, do, zero)
        span = slice(head * HEAD_DIM, (head + 1) * HEAD_DIM)
        grad_query = 0.0
        for part, ref in enumerate((near_ref, far_ref)):
            mark = mark_key_ref[pl.ds(part * rows, rows), :]
            probs = jnp.exp(mul_t(pick(head, ref[0], mark), query_head))
            grad_probs = mul_t(pick(head, ref[1], mark), do_head)
            grad_scores = (probs * grad_probs).astype(LOW)
            grad_value = mul(probs.astype(LOW), do_only)
            grad_key = mul(grad_scores, query_only)
            grad_query += mul(keys_t[part][span], grad_scores)
            if head == 0:
                sums[part] = [grad_key, grad_value]
            else:
                sums[part] = [sums[part][0] + grad_key, sums[part][1] + grad_value]
        grads_query.append(grad_query)
    turned = turn(
        jnp.transpose(jnp.concatenate(grads_query)) * SCALE, cos_ref[...], -sin_ref[...]
    )
    dq_ref[...] = turned.astype(LOW)
    for i in range(2):
        keep_ref[i] = sums[0][i].astype(LOW)
        send_ref[i] = sums[1][i].astype(LOW)


def middle_kernel(at_ref, live_ref, tokens_ref, far_ref, cot_ref, cot_far_ref,
                  oa_ref, ob_ref, oc_ref, gain_ref, i0, i1, i2, i3, i4, i5, d0, d1, d2, d3, d4, d5,
                  mixed_ref, mixed_far_ref, dx1_ref, do_ref, keep_ref, send_ref,
                  w_out, w_in, w_down, o_all, o_t, a2_t, h_t, h_all, dm_all, duw_all, db_all,
                  mixed, dx1_all, do_all, keep, send, out_sem):
    place, slot = at_ref[0], at_ref[2]
    live = live_ref[slot].astype(FULL)
    join_folded(at_ref, (d0, d1, d2, d3, d4, d5), w_out, w_down)
    join_blocks(at_ref, (i0, i1, i2, i3, i4, i5), w_in)
    rows, width = far_ref.shape
    share = width // 4
    short, units = share // 2, w_down.shape[0]
    gain = gain_ref[...]
    first = 0
    for ref in (oa_ref, ob_ref, oc_ref):
        o_all[:, first : first + ref.shape[1]] = ref[...]
        first += ref.shape[1]
    copies = []
    for part in range(2):
        span = pl.ds(part * rows, rows)
        o = o_all[span, :]
        values = tokens_ref[slot] if part == 0 else far_ref[...]
        x1 = values.astype(FULL) + live * mul(o, w_out[...])
        scaled, root = normalize(x1)
        a2 = (scaled * gain).astype(LOW)
        cot = (cot_ref[slot] if part == 0 else cot_far_ref[...]).astype(FULL)
        dm = (live * cot).astype(LOW)
        for first in range(0, units, units // 3):
            lanes = slice(first, first + units // 3)
            lanes_lin = slice(units + first, units + first + units // 3)
            u = mul(a2, w_in[:, lanes])
            w = mul(a2, w_in[:, lanes_lin])
            dh = mul_t(dm, w_down[lanes, :])
            phi = 0.5 * (1.0 + lax.erf(u * math.sqrt(0.5)))
            gelu = u * phi
            slope = phi + u * (jnp.exp(-0.5 * u * u) * (1.0 / math.sqrt(2.0 * math.pi)))
            h_all[:, lanes] = (gelu * w).astype(LOW)
            duw_all[span, lanes] = (dh * w * slope).astype(LOW)
            duw_all[span, lanes_lin] = (dh * gelu).astype(LOW)
        h = h_all[...]
        mixed[span, :] = (x1 + live * mul(h, w_down[...])).astype(LOW)
        target = mixed_ref.at[slot] if part == 0 else mixed_far_ref
        copies.append(put(mixed.at[span, :], target, out_sem.at[len(copies)]))
        da2 = mul_t(duw_all[span, :], w_in[...])
        dx1 = cot + normalize_back(da2, gain, scaled, root)
        dx1_all[span, :] = dx1
        copies.append(put(dx1_all.at[span, :], dx1_ref.at[span, :], out_sem.at[len(copies)]))
        db = (live * dx1).astype(LOW)
        do_all[span, :] = mul_t(db, w_out[...]).astype(LOW)
        copies.append(put(do_all.at[span, :], do_ref.at[span, :], out_sem.at[len(copies)]))
        db_all[span, :] = db
        dm_all[span, :] = dm
        o_t[:, span] = jnp.transpose(o)
        a2_t[:, span] = jnp.transpose(a2)
        h_t[:, span] = jnp.transpose(h)
    dm, duw, db = dm_all[...], duw_all[...], db_all[...]
    for j, out, target in ((1, send, send_ref), (3, send, send_ref), (0, keep, keep_ref), (2, keep, keep_ref)):
        span = pl.ds(pl.multiple_of((place ^ j) * share, share), share)
        base = (place ^ j) * (share + short)
        down = pl.ds(pl.multiple_of(base, short), share)
        down_last = pl.ds(pl.multiple_of(base + share, short), short)
        at = 2 * units
        out[j // 2, :, :at] = mul(a2_t[span, :], duw).astype(LOW)
        out[j // 2, :, at : at + width] = mul(o_t[span, :], db).astype(LOW)
        at += width
        out[j // 2, :, at : at + width] = mul(h_t[down, :], dm).astype(LOW)
        at += width
        last = mul(h_t[down_last, :], dm).astype(LOW)
        out[j // 2, :short, at:] = last[:, : width // 2]
        out[j // 2, short:, at:] = last[:, width // 2 :]
        copies.append(put(out.at[j // 2], target.at[j // 2], out_sem.at[len(copies)]))
    wait_all(copies)


def send_kernel(count, at_ref, *refs):
    normed_ref = refs[0]
    dqs, owns, gots = (refs[1 + i * count : 1 + (i + 1) * count] for i in range(3))
    (cos_ref, sin_ref, dqkv_ref, normed_t_ref, send_ref,
     dqkv, normed_t, send, sem) = refs[1 + 3 * count :]
    width = normed_ref.shape[1]
    part_width = width // count
    normed_t[...] = jnp.transpose(normed_ref[...])
    copies = [put(normed_t, normed_t_ref, sem.at[0])]
    cos_part, sin_part = cos_ref[...], -sin_ref[...]
    for part, (dq, own, got) in enumerate(zip(dqs, owns, gots)):
        base = part * part_width
        dqkv[:, pl.ds(base, part_width)] = dq[...]
        dqkv[:, pl.ds(2 * width + base, part_width)] = (
            own[1].astype(FULL) + got[1].astype(FULL)
        ).astype(LOW)
        for pair in range(part_width // PAIR):
            lanes = pl.ds(pair * PAIR, PAIR)
            raw = own[0, :, lanes].astype(FULL) + got[0, :, lanes].astype(FULL)
            dqkv[:, pl.ds(width + base + pair * PAIR, PAIR)] = turn(raw, cos_part, sin_part).astype(
                LOW
            )
    copies.append(put(dqkv, dqkv_ref, sem.at[1]))
    right = dqkv[...]
    share = send.shape[1]
    for j in (1, 3):
        start = pl.multiple_of((at_ref[0] ^ j) * share, share)
        send[j // 2] = mul(normed_t[pl.ds(start, share), :], right).astype(LOW)
        copies.append(put(send.at[j // 2], send_ref.at[j // 2], sem.at[len(copies)]))
    wait_all(copies)


def keep_kernel(at_ref, normed_t_ref, dqkv_ref, keep_ref, keep, sem):
    right = dqkv_ref[...]
    share = keep.shape[1]
    copies = []
    for j in (0, 2):
        start = pl.multiple_of((at_ref[0] ^ j) * share, share)
        keep[j // 2] = mul(normed_t_ref[pl.ds(start, share), :], right).astype(LOW)
        copies.append(put(keep.at[j // 2], keep_ref.at[j // 2], sem.at[len(copies)]))
    wait_all(copies)


def input_kernel(at_ref, tokens_ref, far_ref, gain_ref, dx1_ref, dqkv_ref, w0, w1, w2, w3, w4, w5,
                 grad_ref, grad_far_ref, weight, grad_own, out_sem):
    join_blocks(at_ref, (w0, w1, w2, w3, w4, w5), weight)
    rows = far_ref.shape[0]
    gain = gain_ref[...]
    for part in (1, 0):
        span = pl.ds(part * rows, rows)
        values = tokens_ref[at_ref[2]] if part == 0 else far_ref[...]
        scaled, root = normalize(values.astype(FULL))
        back = normalize_back(mul_t(dqkv_ref[span, :], weight[...]), gain, scaled, root)
        grad = dx1_ref[span, :] + back
        if part == 1:
            grad_far_ref[...] = grad.astype(LOW)
        else:
            grad_own[...] = grad
    put(grad_own, grad_ref.at[at_ref[2]], out_sem.at[0]).wait()


def shaped(*shape, kind=LOW):
    return jax.ShapeDtypeStruct(shape, kind)


IN_SMEM = pl.BlockSpec(memory_space=pltpu.SMEM)
IN_VMEM = pl.BlockSpec(memory_space=pltpu.VMEM)
IN_ANY = pl.BlockSpec(memory_space=pl.ANY)


def params(mebibytes):
    return pltpu.CompilerParams(vmem_limit_bytes=int(mebibytes * 1024 * 1024))


def call(kernel, args, in_specs, out_shape, out_specs, late=(), **options):
    if not isinstance(out_shape, tuple):
        out_shape, out_specs = (out_shape,), (out_specs,)
    count, skip, outs = len(args), len(late), len(out_shape)

    def body(*refs):
        outs_at = count + skip
        return kernel(*refs[:count], *refs[outs_at : outs_at + outs], *refs[outs_at + outs + 1 :])

    return pl.pallas_call(
        body,
        in_specs=list(in_specs) + [IN_ANY] * skip,
        out_shape=out_shape + (shaped(8, 128, kind=FULL),),
        out_specs=out_specs + (IN_ANY,),
        **options,
    )(*args, *late)


def gate(values, late=(), weight=0):
    hint = {}
    if weight:
        hint["cost_estimate"] = pl.CostEstimate(
            flops=weight, transcendentals=0, bytes_accessed=0
        )
    return call(
        lambda *refs: None,
        values,
        late=late,
        out_shape=tuple(jax.ShapeDtypeStruct(v.shape, v.dtype) for v in values),
        in_specs=[IN_ANY] * len(values),
        out_specs=(IN_ANY,) * len(values),
        input_output_aliases={i: i for i in range(len(values))},
        compiler_params=params(1),
        name="gate",
        **hint,
    )[: len(values)]


def join_two_kernel(at_ref, mine, other, out):
    short = mine.shape[0]
    out[pl.ds(pl.multiple_of(at_ref[4] * short, short), short), :] = mine[...]
    out[pl.ds(pl.multiple_of((1 - at_ref[4]) * short, short), short), :] = other[...]


def join_two(at, mine, other, late=()):
    rows, width = mine.shape
    return call(
        join_two_kernel,
        (at, mine, other),
        late=late,
        out_shape=shaped(2 * rows, width),
        in_specs=[IN_SMEM] + [IN_VMEM] * 2,
        out_specs=IN_VMEM,
        compiler_params=params(4),
        name="join_two",
    )


def in_hbm(value):
    return pltpu.with_memory_space_constraint(value, pltpu.HBM)


def in_vmem(*values):
    return [pltpu.with_memory_space_constraint(value, pltpu.VMEM) for value in values]


def prepare_first(at, weight, gains):
    rows, width = weight.shape
    return call(
        prepare_first_kernel,
        (at, in_hbm(weight), gains),
        out_shape=(shaped(rows // 2, width), shaped(*gains.shape)),
        in_specs=[IN_SMEM, IN_ANY, IN_VMEM],
        out_specs=(IN_VMEM,) * 2,
        scratch_shapes=[pltpu.VMEM((rows // 2, width), FULL), pltpu.SemaphoreType.DMA((1,))],
        compiler_params=params(6),
        name="prepare_first",
    )


def prepare_rest(at, tokens, w_in, w_out, w_down, w_qkv, cotangent, late):
    rows, width = w_out.shape
    folded = 2 * width + width // 2
    return call(
        prepare_rest_kernel,
        (at, *[in_hbm(v) for v in (tokens, w_in, w_out, w_down, w_qkv, cotangent)]),
        late=late,
        out_shape=(
            shaped(*tokens.shape[1:]),
            shaped(*w_in.shape),
            shaped(rows // 4, w_in.shape[1]),
            shaped(rows, folded),
            shaped(rows // 2, folded),
            shaped(*w_qkv.shape),
            shaped(*cotangent.shape[1:]),
        ),
        in_specs=[IN_SMEM] + [IN_ANY] * 6,
        out_specs=(IN_VMEM,) * 7,
        scratch_shapes=[
            pltpu.VMEM(v.shape, FULL) for v in (w_in, w_out, w_down, w_qkv)
        ] + [pltpu.SemaphoreType.DMA((6,))],
        compiler_params=params(18),
        name="prepare_rest",
    )


def project(at, tokens, far, gain, cos_part, sin_part, blocks, late):
    rows, width = 2 * far.shape[0], far.shape[1]
    return call(
        project_kernel,
        (at, tokens, *in_vmem(far), gain, cos_part, sin_part, *in_vmem(*blocks)),
        late=late,
        out_shape=(shaped(rows, width), shaped(rows, width), shaped(2, rows, width)),
        in_specs=[IN_SMEM] + [IN_VMEM] * 11,
        out_specs=(IN_VMEM,) * 3,
        scratch_shapes=[pltpu.VMEM((width, 3 * width), LOW)],
        compiler_params=params(18),
        name="project",
    )


def attend(first, count, query, near, far, mark_query, mark_key, late=()):
    rows = query.shape[0]
    row_spec = pl.BlockSpec((rows, PAIR), lambda i: (0, i + first))
    kv_spec = pl.BlockSpec((2, rows, PAIR), lambda i: (0, 0, i + first))
    out_spec = pl.BlockSpec((rows, PAIR), lambda i: (0, i))
    return call(
        attend_kernel,
        (*in_vmem(query, near, far), mark_query, mark_key),
        late=late,
        grid=(count,),
        out_shape=(shaped(rows, count * PAIR), shaped(rows, count * PAIR)),
        in_specs=[
            row_spec,
            kv_spec,
            kv_spec,
            pl.BlockSpec((rows, PAIR), lambda i: (0, 0)),
            pl.BlockSpec((2 * rows, PAIR), lambda i: (0, 0)),
        ],
        out_specs=(out_spec, out_spec),
        compiler_params=params(16),
        name="attend",
    )


def attend_back(
    first, first_o, count, query, near, far, extra, o, mark_key, do, cos_part, sin_part, late=()
):
    rows = query.shape[0]
    row_spec = pl.BlockSpec((rows, PAIR), lambda i: (0, i + first))
    o_spec = pl.BlockSpec((rows, PAIR), lambda i: (0, i + first_o))
    kv_spec = pl.BlockSpec((2, rows, PAIR), lambda i: (0, 0, i + first))
    fixed = pl.BlockSpec((rows, PAIR), lambda i: (0, 0))
    out_row = pl.BlockSpec((rows, PAIR), lambda i: (0, i))
    out_kv = pl.BlockSpec((2, rows, PAIR), lambda i: (0, 0, i))
    return call(
        attend_back_kernel,
        (*in_vmem(query, near, far, extra), mark_key, *in_vmem(o, do), cos_part, sin_part),
        late=late,
        grid=(count,),
        out_shape=(
            shaped(rows, count * PAIR),
            shaped(2, rows, count * PAIR),
            shaped(2, rows, count * PAIR),
        ),
        in_specs=[
            row_spec,
            kv_spec,
            kv_spec,
            o_spec,
            pl.BlockSpec((2 * rows, PAIR), lambda i: (0, 0)),
            o_spec,
            row_spec,
            fixed,
            fixed,
        ],
        out_specs=(out_row, out_kv, out_kv),
        compiler_params=params(20),
        name="attend_back",
    )


def middle(at, live, tokens, far, cot, cot_far, o_parts, gain, blocks_in, blocks_od):
    half, width = far.shape
    rows, share = 2 * half, width // 4
    units = blocks_in[0].shape[1] // 2
    total = 2 * units + blocks_od[0].shape[1]
    assert units == 4 * (share + share // 2)
    low = lambda *shape: pltpu.VMEM(shape, LOW)
    return call(
        middle_kernel,
        (at, live, tokens, *in_vmem(far), cot, *in_vmem(cot_far, *o_parts), gain,
         *in_vmem(*blocks_in, *blocks_od)),
        out_shape=(
            shaped(2, half, width),
            shaped(half, width),
            shaped(rows, width, kind=FULL),
            shaped(rows, width),
            shaped(2, share, total),
            shaped(2, share, total),
        ),
        in_specs=[IN_SMEM] * 2 + [IN_VMEM] * 20,
        out_specs=(IN_ANY,) * 6,
        scratch_shapes=[
            low(width, width),
            low(width, 2 * units),
            low(units, width),
            low(rows, width),
            low(width, rows),
            low(width, rows),
            low(units, rows),
            low(half, units),
            low(rows, width),
            low(rows, 2 * units),
            low(rows, width),
            low(rows, width),
            pltpu.VMEM((rows, width), FULL),
            low(rows, width),
            low(2, share, total),
            low(2, share, total),
            pltpu.SemaphoreType.DMA((10,)),
        ],
        compiler_params=params(44),
        name="middle",
    )


def qkv_send(at, normed, dq, own, got, cos_part, sin_part, late):
    rows, width = normed.shape
    share = width // 4
    return call(
        functools.partial(send_kernel, len(dq)),
        (at, normed, *dq, *own, *got, cos_part, sin_part),
        late=late,
        out_shape=(
            shaped(rows, 3 * width),
            shaped(width, rows),
            shaped(2, share, 3 * width),
        ),
        in_specs=[IN_SMEM] + [IN_VMEM] * (3 + 3 * len(dq)),
        out_specs=(IN_ANY,) * 3,
        scratch_shapes=[
            pltpu.VMEM((rows, 3 * width), LOW),
            pltpu.VMEM((width, rows), LOW),
            pltpu.VMEM((2, share, 3 * width), LOW),
            pltpu.SemaphoreType.DMA((4,)),
        ],
        compiler_params=params(20),
        name="qkv_send",
    )


def qkv_keep(at, normed_t, dqkv, late):
    width, rows = normed_t.shape
    share = width // 4
    return call(
        keep_kernel,
        (at, normed_t, dqkv),
        late=late,
        out_shape=shaped(2, share, 3 * width),
        in_specs=[IN_SMEM] + [IN_VMEM] * 2,
        out_specs=IN_ANY,
        scratch_shapes=[
            pltpu.VMEM((2, share, 3 * width), LOW),
            pltpu.SemaphoreType.DMA((2,)),
        ],
        compiler_params=params(16),
        name="qkv_keep",
    )


def input_back(at, tokens, far, gain, dx1, dqkv, blocks, late):
    half, width = far.shape
    return call(
        input_kernel,
        (at, tokens, far, gain, dx1, *in_vmem(dqkv, *blocks)),
        late=late,
        out_shape=(shaped(2, half, width, kind=FULL), shaped(half, width)),
        in_specs=[IN_SMEM] + [IN_VMEM] * 11,
        out_specs=(IN_ANY, IN_VMEM),
        scratch_shapes=[
            pltpu.VMEM((width, 3 * width), LOW),
            pltpu.VMEM((half, width), FULL),
            pltpu.SemaphoreType.DMA((1,)),
        ],
        compiler_params=params(20),
        name="input_back",
    )


def first_sums_kernel(at_ref, keep, got, own_a, far_a, mine_b, give_b):
    cut, short = far_a.shape[0], give_b.shape[1]

    def add(block, start, size):
        span = pl.ds(start, size)
        return (keep[block, span, :].astype(FULL) + got[block, span, :].astype(FULL)).astype(LOW)

    far_a[...] = add(1, 0, cut)
    for block in range(2):
        give_b[block] = add(block, pl.multiple_of(cut + (1 - at_ref[1]) * short, short), short)
        mine_b[block] = add(block, pl.multiple_of(cut + at_ref[1] * short, short), short)
    own_a[...] = add(0, 0, cut)


def first_sums(at, keep, got, late=()):
    _, rows, width = keep.shape
    cut, short = rows // 2, rows // 4
    return call(
        first_sums_kernel,
        (at, keep, got),
        late=late,
        out_shape=(shaped(cut, width),) * 2 + (shaped(2, short, width),) * 2,
        in_specs=[IN_SMEM] + [IN_VMEM] * 2,
        out_specs=(IN_VMEM,) * 4,
        compiler_params=params(20),
        name="first_sums",
    )


def second_sums_kernel(at_ref, own_a, got_a, mine_b, got_b, mine_a, give_a, near_b, far_b):
    short = mine_a.shape[0]
    for start, out in ((1 - at_ref[1], give_a), (at_ref[1], mine_a)):
        span = pl.ds(pl.multiple_of(start * short, short), short)
        out[...] = (own_a[span, :].astype(FULL) + got_a[span, :].astype(FULL)).astype(LOW)
    for block, out in ((1, far_b), (0, near_b)):
        out[...] = (mine_b[block].astype(FULL) + got_b[block].astype(FULL)).astype(LOW)


def second_sums(at, own_a, got_a, mine_b, got_b, late=()):
    _, short, width = mine_b.shape
    return call(
        second_sums_kernel,
        (at, own_a, got_a, mine_b, got_b),
        late=late,
        out_shape=(shaped(short, width),) * 4,
        in_specs=[IN_SMEM] + [IN_VMEM] * 4,
        out_specs=(IN_VMEM,) * 4,
        compiler_params=params(12),
        name="second_sums",
    )


def third_sums_kernel(at_ref, mine_a, got_a, near_b, got_b, keep, give):
    upper = mine_a[...].astype(FULL) + got_a[...].astype(FULL)
    lower = near_b[...].astype(FULL) + got_b[...].astype(FULL)
    keep[...] = jnp.where(at_ref[4] == 0, upper, lower).astype(LOW)
    give[...] = jnp.where(at_ref[4] == 0, lower, upper).astype(LOW)


def third_sums(at, mine_a, got_a, near_b, got_b, late=()):
    return call(
        third_sums_kernel,
        (at, mine_a, got_a, near_b, got_b),
        late=late,
        out_shape=(shaped(*mine_a.shape),) * 2,
        in_specs=[IN_SMEM] + [IN_VMEM] * 4,
        out_specs=(IN_VMEM,) * 2,
        compiler_params=params(12),
        name="third_sums",
    )


def squares_kernel(at_ref, qkv, w_qkv, rest, w_in, gains, out):
    inner = w_in.shape[1]
    total = jnp.sum(jnp.square(rest[:, inner:].astype(FULL)), keepdims=True)
    rows = qkv.shape[0]
    shape = (rows, gains.shape[1])
    offset = lax.broadcasted_iota(jnp.int32, shape, 1) - lax.broadcasted_iota(jnp.int32, shape, 0)
    for i, (piece, weight) in enumerate(((qkv, w_qkv), (rest, w_in))):
        start = at_ref[3]
        span = pl.ds(pl.multiple_of(start, 8), rows)
        values = piece[:, : weight.shape[1]].astype(FULL)
        sums = jnp.sum(weight[span, :].astype(LOW).astype(FULL) * values, axis=1, keepdims=True)
        gain = gains[i : i + 1, :].astype(LOW).astype(FULL)
        gain = jnp.sum(jnp.where(offset == start, gain, 0.0), axis=1, keepdims=True)
        total += jnp.sum(jnp.square(values), keepdims=True)
        total += jnp.sum(jnp.square(sums / gain), keepdims=True)
    out[...] = jnp.broadcast_to(total, out.shape)


def squares(*args):
    return call(
        squares_kernel,
        args,
        out_shape=shaped(8, 128, kind=FULL),
        in_specs=[IN_SMEM] + [IN_VMEM] * (len(args) - 1),
        out_specs=IN_VMEM,
        compiler_params=params(10),
        name="squares",
    )


def add_kernel(count, *refs):
    for i in range(count):
        out = refs[2 * count + i]
        out[...] = (refs[i][...].astype(FULL) + refs[count + i][...].astype(FULL)).astype(out.dtype)


def add(first, second, late=()):
    count = len(first)
    return call(
        functools.partial(add_kernel, count),
        (*first, *second),
        late=late,
        out_shape=tuple(jax.ShapeDtypeStruct(v.shape, v.dtype) for v in first),
        in_specs=[IN_VMEM] * (2 * count),
        out_specs=(IN_VMEM,) * count,
        compiler_params=params(8),
        name="add",
    )


def fill_kernel(at_ref, mixed_far, grad_far, mixed_in, grad_in, mixed, grad, wide, sem):
    first = put(mixed_far, mixed.at[1 - at_ref[2]], sem.at[0])
    wide[...] = grad_far[...].astype(FULL)
    put(wide, grad.at[1 - at_ref[2]], sem.at[1]).wait()
    first.wait()


def fill(at, mixed, mixed_far, grad, grad_far):
    return call(
        fill_kernel,
        (at, mixed_far, grad_far, mixed, grad),
        out_shape=(shaped(*mixed.shape), shaped(*grad.shape, kind=FULL)),
        in_specs=[IN_SMEM, IN_VMEM, IN_VMEM, IN_ANY, IN_ANY],
        out_specs=(IN_ANY,) * 2,
        input_output_aliases={3: 0, 4: 1},
        scratch_shapes=[pltpu.VMEM(grad_far.shape, FULL), pltpu.SemaphoreType.DMA((2,))],
        compiler_params=params(4),
        name="fill",
    )


def clip_factor(square_ref):
    norm = jnp.sqrt(square_ref[:1, :1])
    return jnp.minimum(1.0, CLIP_LIMIT / (norm + 1e-06))


def quarters(at_ref, parts):
    own, beside, other, other_beside = parts
    for i in range(4):
        same = at_ref[4] == i // 2
        near = jnp.where(same, own[...], beside[...])
        far = jnp.where(same, other[...], other_beside[...])
        yield jnp.where(at_ref[1] == i % 2, near, far).astype(FULL)


def gain_row(weight, gradient, start, shape):
    sums = jnp.sum(weight.astype(LOW).astype(FULL) * gradient, axis=1, keepdims=True)
    shape = (weight.shape[0], shape[1])
    offset = lax.broadcasted_iota(jnp.int32, shape, 1) - lax.broadcasted_iota(jnp.int32, shape, 0)
    return jnp.sum(jnp.where(offset == start, sums, 0.0), axis=0, keepdims=True)


class Update:
    def __init__(self, number, sources, news, targets, sem):
        self.number, self.sources, self.news, self.targets = number, sources, news, targets
        self.sem, self.out = sem, []

    def step(self, span, gradient, factor):
        rows, lanes = span
        short = (rows.stop - rows.start) // 2
        for i in range(2):
            part = (slice(rows.start + i * short, rows.start + (i + 1) * short), lanes)
            results = adam_step(
                self.sources[0][part], self.sources[1][part], self.sources[2][part],
                gradient[i * short : (i + 1) * short, :], factor,
                STEP_RATES[self.number], DECAY_RATES[self.number],
            )
            for result, new, target in zip(results, self.news, self.targets):
                new[part] = result
                self.out.append(put(new.at[part], target.at[part], self.sem.at[len(self.out)]))
        return self.sources[0][span]


def update_rest_kernel(at_ref, square_ref, *refs):
    parts, refs = refs[:4], refs[4:]
    sources, targets, row_ref, news, sem = refs[:9], refs[9:18], refs[18], refs[19:28], refs[28]
    inner, out, down = (
        Update(number, *(group[3 * k : 3 * k + 3] for group in (sources, news, targets)), sem.at[k])
        for k, number in enumerate((2, 1, 3))
    )
    factor = clip_factor(square_ref)
    rows, width = sources[3].shape
    lanes = sources[0].shape[1]
    short, last = rows // 4, width // 2
    row = jnp.zeros(row_ref.shape, FULL)
    for i, gradient in enumerate(quarters(at_ref, parts)):
        span = (slice(i * short, (i + 1) * short), slice(None))
        part = gradient[:, :lanes]
        row += gain_row(inner.step(span, part, factor), part, i * short, row_ref.shape)
        out.step(span, gradient[:, lanes : lanes + width], factor)
        down.step(span, gradient[:, lanes + width : lanes + 2 * width], factor)
        start = rows + (i % 2) * short
        span = (slice(start, start + short), slice((i // 2) * last, (i // 2 + 1) * last))
        down.step(span, gradient[:, lanes + 2 * width :], factor)
    row_ref[...] = row
    wait_all(inner.out + out.out + down.out)


def update_rest(at, square, parts, inner, out, down, late):
    like = [jax.ShapeDtypeStruct(v.shape, FULL) for v in (*inner, *out, *down)]
    return call(
        update_rest_kernel,
        (at, square, *parts, *inner, *out, *down),
        late=late,
        out_shape=(*like, shaped(1, inner[0].shape[0], kind=FULL)),
        in_specs=[IN_SMEM] + [IN_VMEM] * 14,
        out_specs=(IN_ANY,) * 9 + (IN_VMEM,),
        scratch_shapes=[pltpu.VMEM(v.shape, FULL) for v in like]
        + [pltpu.SemaphoreType.DMA((3, 48))],
        compiler_params=params(28),
        name="update_rest",
    )


def update_last_kernel(at_ref, square_ref, row_ref, g_w, g_m, g_v, *refs):
    parts, refs = refs[:4], refs[4:]
    sources, targets = refs[:3], refs[3:6]
    g_w_out, g_m_out, g_v_out, norm_out = refs[6:10]
    news, sem = refs[10:13], refs[13]
    qkv = Update(0, sources, news, targets, sem)
    factor = clip_factor(square_ref)
    norm_out[...] = jnp.sqrt(square_ref[...])
    short = sources[0].shape[0] // 4
    row = jnp.zeros(row_ref.shape, FULL)
    for i, gradient in enumerate(quarters(at_ref, parts)):
        span = (slice(i * short, (i + 1) * short), slice(None))
        row += gain_row(qkv.step(span, gradient, factor), gradient, i * short, row_ref.shape)
    for i, values in enumerate((row, row_ref[...])):
        line = slice(i, i + 1)
        gradient = values / g_w[line, :].astype(LOW).astype(FULL)
        g_w_out[line, :], g_m_out[line, :], g_v_out[line, :] = adam_step(
            g_w[line, :], g_m[line, :], g_v[line, :], gradient, factor,
            STEP_RATES[4], DECAY_RATES[4],
        )
    wait_all(qkv.out)


def update_last(at, square, qkv, qkv_parts, row, gains):
    like = [jax.ShapeDtypeStruct(v.shape, FULL) for v in qkv]
    return call(
        update_last_kernel,
        (at, square, row, *gains, *qkv_parts, *qkv),
        out_shape=(
            *like,
            *[jax.ShapeDtypeStruct(v.shape, FULL) for v in gains],
            jax.ShapeDtypeStruct(square.shape, FULL),
        ),
        in_specs=[IN_SMEM] + [IN_VMEM] * 12,
        out_specs=(IN_ANY,) * 3 + (IN_VMEM,) * 4,
        scratch_shapes=[pltpu.VMEM(v.shape, FULL) for v in like]
        + [pltpu.SemaphoreType.DMA((24,))],
        compiler_params=params(18),
        name="update_last",
    )


def low_sum(*values):
    return sum(value.astype(FULL) for value in values).astype(LOW)


def index(value, i):
    return lax.dynamic_index_in_dim(value, i, 0, keepdims=False)


def make(dp_count, seq_count):
    assert seq_count == 4 and dp_count >= 8 and dp_count & (dp_count - 1) == 0
    far_bits = [1 << i for i in range(2, dp_count.bit_length() - 1)]

    def trade(value, axis, bit):
        size = seq_count if axis == "seq" else dp_count
        return lax.ppermute(value, axis, [(i, i ^ bit) for i in range(size)])

    def on_device(
        tokens, cotangent, segments, valid,
        w_qkv, w_out, w_in, w_down, gains,
        m_qkv, m_out, m_in, m_down, m_gains,
        v_qkv, v_out, v_in, v_down, v_gains,
    ):
        place = lax.axis_index("seq")
        group = lax.axis_index("dp")
        slot = place >> 1
        half = group & 1
        local_len, width = tokens.shape[1:]
        rows = 2 * local_len
        share = w_qkv.shape[0]
        side = (group >> 1) & 1
        quarter = share // 4
        at = jnp.stack([place, half, slot, side * 2 * quarter + half * quarter, side])

        half_qkv, low_gains, begun = prepare_first(at, w_qkv, gains)
        (far_qa,) = gate((trade(half_qkv, "seq", 2),), weight=EARLY)
        (gain_far,) = gate((trade(low_gains, "seq", 2),), weight=2 * EARLY)
        their_tokens, low_in, part_in, low_od, half_od, low_qkv, their_cot, _ = prepare_rest(
            at, tokens, w_in, w_out, w_down, w_qkv, cotangent, (begun,)
        )
        near_q = trade(low_qkv, "seq", 1)
        far = trade(their_tokens, "seq", 2)
        far_qb = trade(far_qa, "dp", 1)
        near_qa = trade(far_qa, "seq", 1)
        near_qb = trade(far_qb, "seq", 1)
        gain_near = trade(jnp.stack([low_gains, gain_far]), "seq", 1)
        gain_stack = jnp.stack([low_gains, gain_near[0], gain_far, gain_near[1]])
        gain_low = jnp.concatenate(
            [index(gain_stack, b ^ place) for b in range(4)], axis=1
        ).astype(FULL)
        blocks_qkv = (low_qkv, near_q, far_qa, far_qb, near_qa, near_qb)
        low_in, low_od, part_in, half_od = gate((low_in, low_od, part_in, half_od), (far_qa,))
        near_i = trade(low_in, "seq", 1)
        near_o = trade(low_od, "seq", 1)
        (come_in,) = gate((trade(part_in, "seq", 2),), weight=EARLY)

        seg = index(segments, slot)
        positions = doc_positions(seg).reshape(4, local_len)
        seg = seg.reshape(4, local_len)
        chunks = [place, place ^ 2, place ^ 1, place ^ 3]
        seg_keys = jnp.concatenate([index(seg, c) for c in chunks])
        pos = jnp.concatenate([index(positions, c) for c in chunks[:2]])
        cos_part, sin_part = rope_tables(pos)
        lane = jnp.arange(PAIR, dtype=jnp.int32)[None] % HEAD_DIM
        same = seg_keys[:, None] == lane
        mark_key = jnp.where(lane < DOCS, 1.0 - same, (lane < DOCS + 3) * 1.0).astype(LOW)
        mark_query = jnp.where((lane < DOCS) & same[:rows], NEG_FILL, 0.0).astype(LOW)

        normed, query, kv, _ = project(
            at, tokens, far, gain_low[:1], cos_part, sin_part, blocks_qkv,
            (come_in, mark_key, mark_query),
        )
        kv_far = trade(kv, "seq", 1)
        (beside_in,) = gate((trade(come_in, "dp", 2),), weight=EARLY)
        far_ia, _ = join_two(at, come_in, beside_in)
        far_ib = trade(far_ia, "dp", 1)
        near_ia = trade(far_ia, "seq", 1)
        pairs = width // PAIR
        two = pairs // 3
        args = (query, kv, kv_far, mark_query, mark_key)
        o_a, extra_a, done_a = attend(0, two, *args)
        (far_oa,) = gate((trade(half_od, "seq", 2),), (done_a,), weight=EARLY)
        near_oa = trade(far_oa, "seq", 1)
        (their_cot,) = gate((their_cot,), (far_oa,))
        (cot_far,) = gate((trade(their_cot, "seq", 2),), weight=WEIGHT)
        far_ob = trade(far_oa, "dp", 1)
        o_b, extra_b, done_b = attend(two, two, *args, late=(done_a, far_oa))
        o_c, extra_c, done_c = attend(2 * two, pairs - 2 * two, *args, late=(done_b, far_ib))
        near_ib = trade(far_ib, "seq", 1)
        (far_ob,) = gate((far_ob,), (done_c,))
        near_ob = trade(far_ob, "seq", 1)
        blocks_in = (low_in, near_i, far_ia, far_ib, near_ia, near_ib)
        blocks_od = (low_od, near_o, far_oa, far_ob, near_oa, near_ob)

        mixed, mixed_far, dx1, do, keep_rest, send_rest, _ = middle(
            at, valid, tokens, far, cotangent, cot_far, (o_a, o_b, o_c), gain_low[1:], blocks_in, blocks_od
        )
        got_rest = trade(send_rest, "seq", 1)
        near_args = (query, kv, kv_far)
        back_args = (mark_key, do, cos_part, sin_part)
        dq0, own0, give0, back0 = attend_back(0, 0, two, *near_args, extra_a, o_a, *back_args)
        *r1, r1_done = first_sums(at, keep_rest, got_rest, late=(back0,))
        got_ra, got_rb = gate(
            (trade(r1[1], "seq", 2), trade(r1[3], "dp", 1)), weight=10 * WEIGHT
        )
        got0 = trade(give0, "seq", 1)
        dq1, own1, give1, back1 = attend_back(
            two, 0, two, *near_args, extra_b, o_b, *back_args, late=(r1_done,)
        )
        got1 = trade(give1, "seq", 1)
        dq2, own2, give2, back2 = attend_back(
            2 * two, 0, pairs - 2 * two, *near_args, extra_c, o_c, *back_args,
            late=(back1, got0),
        )
        got2 = trade(give2, "seq", 1)
        dqkv, normed_t, send_qkv, send_done = qkv_send(
            at, normed, (dq0, dq1, dq2), (own0, own1, own2), (got0, got1, got2),
            cos_part, sin_part, late=(),
        )
        got_qkv = trade(send_qkv, "seq", 1)
        *r2, r2_done = second_sums(at, r1[0], got_ra, r1[2], got_rb, late=(send_done,))
        got_ra, got_rb = trade(r2[1], "dp", 1), trade(r2[3], "seq", 2)
        keep_qkv, _ = qkv_keep(at, normed_t, dqkv, late=(r2_done,))
        *q1, q1_done = first_sums(at, keep_qkv, got_qkv)
        got_qa, got_qb = trade(q1[1], "seq", 2), trade(q1[3], "dp", 1)
        rest, give_rest, r3_done = third_sums(
            at, r2[0], got_ra, r2[2], got_rb, late=(q1_done,)
        )
        got_rest = trade(give_rest, "dp", 2)
        grad, grad_far, grad_done = input_back(
            at, tokens, far, gain_low[:1], dx1, dqkv, blocks_qkv, late=(r3_done,)
        )
        *q2, q2_done = second_sums(at, q1[0], got_qa, q1[2], got_qb, late=(grad_done,))
        got_qa, got_qb = gate(
            (trade(q2[1], "dp", 1), trade(q2[3], "seq", 2)), weight=10 * WEIGHT
        )
        rest, rest_done = add((rest,), (got_rest,), late=(q2_done,))
        got_rest = trade(rest, "dp", far_bits[0])
        qkv, give_qkv, q3_done = third_sums(
            at, q2[0], got_qa, q2[2], got_qb, late=(rest_done,)
        )
        mixed_far, grad_far = gate((mixed_far, grad_far), (q3_done,))
        mixed_far = trade(mixed_far, "seq", 2)
        grad_far = trade(grad_far, "seq", 2)
        qkv, qkv_done = add((qkv,), (trade(give_qkv, "dp", 2),))
        (got_qkv,) = gate((trade(qkv, "dp", far_bits[0]),), weight=WEIGHT // 15)
        rest, rest_done = add((rest,), (got_rest,), late=(qkv_done, mixed_far))
        for bit in far_bits[1:]:
            rest, rest_done = add((rest,), (trade(rest, "dp", bit),))

        beside, other = trade(rest, "dp", 2), trade(rest, "dp", 1)
        mixed, grad, fill_done = fill(at, mixed, mixed_far, grad, grad_far)
        qkv, qkv_done = add((qkv,), (got_qkv,), late=(rest_done, grad_far))
        for bit in far_bits[1:]:
            qkv, qkv_done = add((qkv,), (trade(qkv, "dp", bit),))
        square, square_done = squares(at, qkv, w_qkv, rest, w_in, gains)
        (qkv,) = gate((qkv,), (square_done,))
        qkv_beside, qkv_other = trade(qkv, "dp", 2), trade(qkv, "dp", 1)
        square, _ = add((square,), (trade(square, "seq", 2),))
        square, square_done = add(
            (square,), (trade(square, "seq", 1),), late=(qkv_beside, qkv_other, beside, other)
        )
        (beside,) = gate((beside,), (square_done,))
        rest_parts = (rest, beside, other, trade(beside, "dp", 1))
        square, _ = add((square,), (trade(square, "dp", 2),))
        square, _ = add(
            (square,), (trade(square, "dp", 1),), late=(rest_parts[3], fill_done)
        )
        (qkv_beside,) = gate((qkv_beside,), (square,))
        qkv_parts = (qkv, qkv_beside, qkv_other, trade(qkv_beside, "dp", 1))

        (new_in, first_in, second_in, new_out, first_out, second_out,
         new_down, first_down, second_down, row, _) = update_rest(
            at, square, rest_parts,
            (w_in, m_in, v_in), (w_out, m_out, v_out), (w_down, m_down, v_down), (),
        )
        (new_qkv, first_qkv, second_qkv, new_gains, first_gains, second_gains, norm, _) = (
            update_last(
                at, square, (w_qkv, m_qkv, v_qkv), qkv_parts, row, (gains, m_gains, v_gains)
            )
        )
        return (
            mixed,
            grad,
            norm[0, 0],
            new_qkv, new_out, new_in, new_down, new_gains,
            first_qkv, first_out, first_in, first_down, first_gains,
            second_qkv, second_out, second_in, second_down, second_gains,
        )

    return on_device


def solution(mesh):
    rows, matrix, gain = P("dp", "seq", None), P("seq", None), P(None, "seq")
    weights = (matrix,) * 4 + (gain,)
    return jax.shard_map(
        make(mesh.shape["dp"], mesh.shape["seq"]),
        mesh=mesh,
        in_specs=(rows, rows, P("dp", None), P("dp")) + weights * 3,
        out_specs=(rows, rows, P()) + weights * 3,
        check_vma=False,
    )
```
